32 devices in a mesh: gx: 8 (over z, x), gy: 4 (over y, core).
Axes of the slice: x: 2, y: 2, z: 4, core: 2. Of those that a mesh axis runs over, the one named last changes fastest.
Arguments:
- thermal_state: float32 [4, 512, 2048], P(None, 'gx', 'gy'), may hold values from 0 to 1
- baseline_thermal_coefficient: float32 [4, 512, 2048], P(None, 'gx', 'gy'), may hold values from 0.5 to 2
- stirrer_grid_locations: int32 [64], replicated, may hold values from 0 to 1048575
- stirrer_energy_supply: float32 [64], replicated, may hold values from 13107 to 131072
Outputs:
- new_temperature: float32 [4, 512, 2048], P(None, 'gx', 'gy')
The draws below stay inside these ranges and needn't reach their ends.
Inputs may be any that keep to these rules, and one draw needn't show every extreme that they name: `stirrer_grid_locations`: each entry is a plate cell x * 2048 + y.
All inputs are finite; a program needn't handle non-finite values.
Results may differ from the reference program's by a relative error of at most 0.0023.
Values sent between devices are 32-bit elements; how exact they have to be, the bound alone decides.
No kernel may reach another device: no remote copies, remote signals or barrier semaphores. Data moves between devices by JAX's collectives and lax.ppermute only.
A program may use at most 64 MiB of HBM per device.

```python
import math
import jax
import jax.numpy as jnp
from jax import lax

DEPTH_SHEETS = 4
SUBSTEPS = 64
GRID_WIDTHWISE = 512
GRID_LENGTHWISE = 2048


def touch_ends(array, stream_key, least, largest):
    extent = array.shape
    spot = [jax.random.randint(jax.random.fold_in(stream_key, axis), (), 0, extent[axis]) for axis in range(len(extent))]
    array = array.at[tuple(spot)].set(least)
    longest = extent.index(max(extent))
    spot[longest] = (spot[longest] + 1) % extent[longest]
    return array.at[tuple(spot)].set(largest)


def steps_of(key, dims, shards, low, top_value):
    factor_of, own = 1.0, jax.random.fold_in(key, 6)
    for position, blocks in shards:
        heights = jnp.exp(jax.random.uniform(jax.random.fold_in(own, position), (blocks,), jnp.float32, low / len(shards), top_value / len(shards)))
        factor_of = factor_of * jnp.repeat(heights, dims[position] // blocks).reshape([-1 if axis == position else 1 for axis in range(len(dims))])
    return factor_of


def setup_inputs(seed: int = 0) -> dict:
    keys = jax.random.split(jax.random.key(seed), 5)
    thermal_state = jnp.clip(1.0 * jax.random.uniform(keys[0], (DEPTH_SHEETS, GRID_WIDTHWISE, GRID_LENGTHWISE), jnp.float32) ** steps_of(keys[0], (DEPTH_SHEETS, GRID_WIDTHWISE, GRID_LENGTHWISE), ((1, 8), (2, 4)), -0.2, 0.2), 0.0, 1.0)
    baseline_thermal_coefficient = jnp.clip(jnp.exp(math.log(2.0) - 1.3862944 * jax.random.uniform(keys[1], (DEPTH_SHEETS, GRID_WIDTHWISE, GRID_LENGTHWISE), jnp.float32) ** steps_of(keys[1], (DEPTH_SHEETS, GRID_WIDTHWISE, GRID_LENGTHWISE), ((1, 8), (2, 4)), -0.2, 0.2)), 0.5, 2.0)
    stirrer_grid_locations = touch_ends(jax.random.randint(keys[2], (SUBSTEPS,), 0, GRID_WIDTHWISE * GRID_LENGTHWISE), jax.random.fold_in(keys[2], 1), 0, (GRID_WIDTHWISE * GRID_LENGTHWISE) - 1).astype(jnp.int32)
    stirrer_energy_supply = jnp.clip(jnp.exp(jax.random.uniform(keys[3], (SUBSTEPS,), jnp.float32, math.log(13107.0), math.log(131072.0))), 13107.0, 131072.0)
    return {"thermal_state": thermal_state, "baseline_thermal_coefficient": baseline_thermal_coefficient, "stirrer_grid_locations": stirrer_grid_locations, "stirrer_energy_supply": stirrer_energy_supply}


RATE = 2000.0
THERMAL_GROWTH = 0.8

def ghost_margin(values, traversal_orientation):
    widths = [(0, 0)] * values.ndim
    widths[traversal_orientation] = (1, 1)
    return jnp.pad(values, widths)

def three_rows(padded, traversal_orientation):
    length = padded.shape[traversal_orientation] - 2
    west_cells = lax.slice_in_dim(padded, 0, length, axis=traversal_orientation)
    centre = lax.slice_in_dim(padded, 1, length + 1, axis=traversal_orientation)
    east_cells = lax.slice_in_dim(padded, 2, length + 2, axis=traversal_orientation)
    return (west_cells, centre, east_cells)

def conductances(padded, traversal_orientation):
    west_cells, centre, east_cells = three_rows(padded, traversal_orientation)
    bottom_interface_transfer = jnp.where(jnp.minimum(west_cells, centre) > 0.0, 0.5 * (west_cells + centre), 0.0)
    top_interface_transfer = jnp.where(jnp.minimum(centre, east_cells) > 0.0, 0.5 * (centre + east_cells), 0.0)
    return (bottom_interface_transfer, top_interface_transfer)

def diffusion_stencil(padded, bottom_interface_transfer, top_interface_transfer, traversal_orientation):
    west_cells, centre, east_cells = three_rows(padded, traversal_orientation)
    return top_interface_transfer * (east_cells - centre) - bottom_interface_transfer * (centre - west_cells)

def solve_lines(lower_band, pivot, upper_band, target, traversal_orientation):
    moved = [jnp.moveaxis(item, traversal_orientation, -1) for item in (lower_band, pivot, upper_band, target)]
    solution = lax.linalg.tridiagonal_solve(moved[0], moved[1], moved[2], moved[3][..., None])[..., 0]
    return jnp.moveaxis(solution, -1, traversal_orientation)

def sweep(thermal_coefficient_of, target, traversal_orientation):
    bottom_interface_transfer, top_interface_transfer = conductances(ghost_margin(thermal_coefficient_of, traversal_orientation), traversal_orientation)
    pivot = 1.0 + RATE * (bottom_interface_transfer + top_interface_transfer)
    lower_band = -RATE * bottom_interface_transfer
    upper_band = -RATE * top_interface_transfer
    if traversal_orientation == 0:
        return solve_lines(lower_band, pivot, upper_band, target, 0)
    return lax.map(lambda group: solve_lines(group[0], group[1], group[2], group[3], traversal_orientation - 1), (lower_band, pivot, upper_band, target))

def reference(thermal_state, baseline_thermal_coefficient, stirrer_grid_locations, stirrer_energy_supply):
    thermal_coefficient_of = baseline_thermal_coefficient * (1.0 + THERMAL_GROWTH * thermal_state)
    forward_euler_advance = jnp.zeros_like(thermal_state)
    for traversal_orientation in (0, 1, 2):
        bottom_interface_transfer, top_interface_transfer = conductances(ghost_margin(thermal_coefficient_of, traversal_orientation), traversal_orientation)
        forward_euler_advance = forward_euler_advance + diffusion_stencil(ghost_margin(thermal_state, traversal_orientation), bottom_interface_transfer, top_interface_transfer, traversal_orientation)
    sheet_extent_horizontal = (stirrer_grid_locations // GRID_LENGTHWISE).astype(jnp.int32)
    sheet_extent_vertical = (stirrer_grid_locations % GRID_LENGTHWISE).astype(jnp.int32)
    energy_injection = jnp.zeros_like(thermal_state).at[0, sheet_extent_horizontal, sheet_extent_vertical].add(stirrer_energy_supply)
    target = RATE * forward_euler_advance + energy_injection
    first_pass = sweep(thermal_coefficient_of, target, 1)
    second_pass = sweep(thermal_coefficient_of, first_pass, 2)
    closing_traversal = sweep(thermal_coefficient_of, second_pass, 0)
    return thermal_state + closing_traversal
```

```python
import functools

import jax
import jax.numpy as jnp
from jax import lax
from jax.experimental import pallas as pl
from jax.experimental.pallas import tpu as pltpu
from jax.sharding import PartitionSpec as P

RATE = 2000.0
THERMAL_GROWTH = 0.8
LANES = 128
SUBLANES = 8
F32 = jnp.float32
VMEM_LIMIT = 40 * 1024 * 1024


def half_conduct(base, temperature):
    return base * (0.5 * RATE + (0.5 * RATE * THERMAL_GROWTH) * temperature)


def join(a, b, face):
    a00, a0l, all_, a_first, a_last = a
    b00, b0l, bll, b_first, b_last = b
    inv = 1.0 / (1.0 / face + all_ + b00)
    left = a0l * inv
    right = b0l * inv
    jump = b_first - a_last
    joined = (
        a00 - left * a0l,
        left * b0l,
        bll - right * b0l,
        a_first + left * jump,
        b_last - right * jump,
    )
    return joined, (jump * inv, right, left)


def eliminate(cond, target, steps):
    kept = []
    here = cond(0)
    rhs = target(0)
    one = jnp.ones_like(here)
    ground, path, first, first_first = one, one, None, None
    for k in range(steps - 1):
        following = cond(k + 1)
        face = here + following
        inv = 1.0 / (ground + face)
        w = face * inv
        h = rhs * inv
        p = path * inv
        kept.append((w, h, p))
        first = path * h if first is None else first + path * h
        first_first = path * p if first_first is None else first_first + path * p
        path = path * w
        rhs = target(k + 1) + w * rhs
        ground = 1.0 + w * ground
        here = following
    inv = 1.0 / ground
    last = rhs * inv
    first_last = path * inv
    kept.append((inv, last, first_last))
    block = (
        first_first + path * first_last,
        first_last,
        inv,
        first + path * last,
        last,
    )
    return block, kept


def edges_kernel(tlo, thi, blo, bhi, lo, hi):
    sheets, rows, _ = tlo.shape
    lane = lax.broadcasted_iota(jnp.int32, (rows, LANES), 1)
    for t_ref, b_ref, out, source in ((tlo, blo, lo, 0), (thi, bhi, hi, LANES - 1)):
        packed = jnp.zeros((rows, LANES), F32)
        for z in range(sheets):
            t = t_ref[z]
            c = half_conduct(b_ref[z], t)
            packed = jnp.where(lane == z, t[:, source : source + 1], packed)
            packed = jnp.where(lane == sheets + z, c[:, source : source + 1], packed)
        out[...] = packed


def pack_edges(temperature, base):
    sheets, rows, columns = temperature.shape
    last = columns // LANES - 1
    first_block = pl.BlockSpec((sheets, rows, LANES), lambda i: (0, 0, 0))
    last_block = pl.BlockSpec((sheets, rows, LANES), lambda i: (0, 0, last))
    whole = pl.BlockSpec((rows, LANES), lambda i: (0, 0))
    shape = jax.ShapeDtypeStruct((rows, LANES), F32)
    return pl.pallas_call(
        edges_kernel,
        grid=(1,),
        in_specs=[first_block, last_block, first_block, last_block],
        out_specs=[whole, whole],
        out_shape=[shape, shape],
        compiler_params=pltpu.CompilerParams(vmem_limit_bytes=VMEM_LIMIT),
    )(temperature, temperature, base, base)


def x_forward_kernel(
    chips, per, plate, loc, energy, t_ref, b_ref, before, after, w_ref, h_ref, p_ref, chain, send,
    t_s, c_s, q_s, m_s,
):
    sheets, rows, columns = t_ref.shape
    chunks = columns // LANES
    steps = rows // SUBLANES
    x0 = lax.axis_index("gx") * rows
    y0 = lax.axis_index("gy") * columns

    place = loc[...]
    local_x = place // plate - x0
    local_y = place % plate - y0
    count = place.shape[1]
    by_x = jnp.where(
        lax.broadcasted_iota(jnp.int32, (rows, count), 0) == local_x, energy[...], 0.0
    )
    by_y = jnp.where(
        lax.broadcasted_iota(jnp.int32, (columns, count), 0) == local_y, 1.0, 0.0
    ).astype(F32)
    plane = lax.dot_general(
        by_x,
        by_y,
        (((1,), (1,)), ((), ())),
        precision=lax.Precision.HIGHEST,
        preferred_element_type=F32,
    )

    lane = lax.broadcasted_iota(jnp.int32, (SUBLANES, columns), 1)
    for r in range(steps):
        at = slice(r * SUBLANES, (r + 1) * SUBLANES)
        lo = before[at, :]
        hi = after[at, :]
        ts = [t_ref[z, at, :] for z in range(sheets)]
        cs = [half_conduct(b_ref[z, at, :], ts[z]) for z in range(sheets)]
        flux = [(cs[z] + cs[z + 1]) * (ts[z + 1] - ts[z]) for z in range(sheets - 1)]
        for z in range(sheets):
            t, c = ts[z], cs[z]
            t_lo, t_hi = lo[:, z : z + 1], hi[:, z : z + 1]
            c_lo, c_hi = lo[:, sheets + z : sheets + z + 1], hi[:, sheets + z : sheets + z + 1]
            t_next = jnp.where(lane == columns - 1, t_hi, pltpu.roll(t, columns - 1, 1))
            c_next = jnp.where(lane == columns - 1, c_hi, pltpu.roll(c, columns - 1, 1))
            face = jnp.where(c_next > 0.0, c + c_next, 0.0)
            out_flux = face * (t_next - t)
            face_lo = jnp.where(c_lo > 0.0, c[:, :1] + c_lo, 0.0)
            in_flux = jnp.where(lane == 0, face_lo * (t[:, :1] - t_lo), pltpu.roll(out_flux, 1, 1))
            total = t + (out_flux - in_flux)
            if z < sheets - 1:
                total = total + flux[z]
            if z > 0:
                total = total - flux[z - 1]
            if z == 0:
                total = total + plane[at, :]
            for y in range(chunks):
                part = slice(y * LANES, (y + 1) * LANES)
                t_s[z * chunks + y, at, :] = total[:, part]
                c_s[z * chunks + y, at, :] = c[:, part]

    for y in range(chunks):

        def cells(ref):
            return lambda k: jnp.stack(
                [ref[z * chunks + y, pl.ds(k, SUBLANES, stride=steps), :] for z in range(sheets)], 0
            )

        block, kept = eliminate(cells(c_s), cells(t_s), steps)
        for k, (w, h, p) in enumerate(kept):
            w_ref[y, k] = w
            h_ref[y, k] = h
            p_ref[y, k] = p
        views = block + (cells(c_s)(0), cells(c_s)(steps - 1))
        for q, value in enumerate(views):
            for z in range(sheets):
                first = (z * chunks + y) * SUBLANES
                q_s[q, first : first + SUBLANES, :] = value[z]

    lines = sheets * chunks

    def segment(s):
        return [q_s[q, pl.ds(s, lines, stride=SUBLANES), :] for q in range(7)]

    total = segment(0)
    c_first, c_last = total[5], total[6]
    total = tuple(total[:5])
    for s in range(1, SUBLANES):
        item = segment(s)
        total, links = join(total, tuple(item[:5]), c_last + item[5])
        c_last = item[6]
        for q in range(3):
            chain[q, s - 1] = links[q]
    for q, value in enumerate(total + (c_first, c_last)):
        m_s[q] = value
    send[...] = jnp.zeros_like(send)
    for d in range(min(chips, lines // per)):
        for q in range(7):
            send[d, q * per : (q + 1) * per, :] = m_s[q, d * per : (d + 1) * per, :]


def x_forward(temperature, base, before, after, loc, energy, chips, per, plate):
    sheets, rows, columns = temperature.shape
    chunks = columns // LANES
    lines = sheets * chunks
    steps = rows // SUBLANES
    stored = jax.ShapeDtypeStruct((chunks, steps, sheets, SUBLANES, LANES), F32)
    return pl.pallas_call(
        functools.partial(x_forward_kernel, chips, per, plate),
        out_shape=[
            stored,
            stored,
            stored,
            jax.ShapeDtypeStruct((3, SUBLANES - 1, lines, LANES), F32),
            jax.ShapeDtypeStruct((chips, padded(7 * per), LANES), F32),
        ],
        scratch_shapes=[
            pltpu.VMEM((lines, rows, LANES), F32),
            pltpu.VMEM((lines, rows, LANES), F32),
            pltpu.VMEM((7, lines * SUBLANES, LANES), F32),
            pltpu.VMEM((7, lines, LANES), F32),
        ],
        compiler_params=pltpu.CompilerParams(vmem_limit_bytes=VMEM_LIMIT),
    )(loc, energy, temperature, base, before, after)


def padded(rows):
    return -(-rows // SUBLANES) * SUBLANES


def chain_fluxes(item, count):
    _, _, last_last, _, last, _, c_last = item(0)
    links = []
    for k in range(1, count):
        b00, b0l, bll, b_first, b_last, c_first, c_end = item(k)
        inv = 1.0 / (1.0 / (c_last + c_first) + last_last + b00)
        right = b0l * inv
        jump = b_first - last
        links.append((jump * inv, right))
        last = b_last - right * jump
        last_last = bll - right * b0l
        c_last = c_end
    fluxes = [None] * (count - 1)
    flux = None
    for k in range(count - 2, -1, -1):
        own, right = links[k]
        flux = own if flux is None else own + right * flux
        fluxes[k] = flux
    return fluxes


def x_interface_kernel(per, got, send):
    count = got.shape[0]

    def item(k):
        return [got[k, q * per : (q + 1) * per, :] for q in range(7)]

    fluxes = chain_fluxes(item, count)
    zero = jnp.zeros((per, LANES), F32)
    send[...] = jnp.zeros_like(send)
    for k in range(count):
        send[k, 0:per, :] = -fluxes[k - 1] if k > 0 else zero
        send[k, per : 2 * per, :] = fluxes[k] if k < count - 1 else zero


def x_interface(got, per):
    return pl.pallas_call(
        functools.partial(x_interface_kernel, per),
        out_shape=jax.ShapeDtypeStruct((got.shape[0], padded(2 * per), LANES), F32),
        compiler_params=pltpu.CompilerParams(vmem_limit_bytes=VMEM_LIMIT),
    )(got)


Y_PARTS = 4


def y_forward_kernel(
    per, got, chain, xw, xh, xp, t_ref, b_ref, w_ref, h_ref, p_ref, inner, outer, send,
    e_s, f_s, g_s, c_s, q_s,
):
    sheets, rows, columns = t_ref.shape
    chunks = columns // LANES
    lines = sheets * chunks
    x_steps = rows // SUBLANES

    for d in range(lines // per):
        e_s[0, d * per : (d + 1) * per, :] = got[d, 0:per, :]
        e_s[1, d * per : (d + 1) * per, :] = got[d, per : 2 * per, :]
    low = e_s[0]
    flux = e_s[1]
    for s in range(SUBLANES - 1, -1, -1):
        f_s[1, pl.ds(s, lines, stride=SUBLANES), :] = flux
        if s > 0:
            flux = chain[0, s - 1] + chain[1, s - 1] * flux - chain[2, s - 1] * low
            f_s[0, pl.ds(s, lines, stride=SUBLANES), :] = -flux
        else:
            f_s[0, pl.ds(s, lines, stride=SUBLANES), :] = low
    for y in range(chunks):
        ends = [
            jnp.stack(
                [
                    f_s[i, (z * chunks + y) * SUBLANES : (z * chunks + y + 1) * SUBLANES, :]
                    for z in range(sheets)
                ],
                0,
            )
            for i in range(2)
        ]
        value = ends[1]
        for k in range(x_steps - 1, -1, -1):
            value = xw[y, k] * value + (xh[y, k] + xp[y, k] * ends[0])
            for z in range(sheets):
                g_s[z * chunks + y, pl.ds(k, SUBLANES, stride=x_steps), :] = value[z]

    pairs = sheets * rows // LANES
    each = sheets // pairs
    for m in range(pairs):
        for y in range(chunks):
            part = slice(y * LANES, (y + 1) * LANES)
            field, cond = [], []
            for z in range(m * each, (m + 1) * each):
                t = t_ref[z, :, part]
                field.append(g_s[z * chunks + y] - t)
                cond.append(half_conduct(b_ref[z, :, part], t))
            e_y = jnp.concatenate(field, 0).T
            c_y = jnp.concatenate(cond, 0).T
            q_s[0, m, part, :] = e_y
            c_s[m, part, :] = c_y

    span = columns // SUBLANES
    steps = span // Y_PARTS

    def cells(pick):
        return lambda k: jnp.stack(
            [
                jnp.stack([pick(m)[pl.ds(j * steps + k, SUBLANES, stride=span), :] for j in range(Y_PARTS)], 0)
                for m in range(pairs)
            ],
            0,
        )

    cond_of = cells(lambda m: c_s.at[m])
    block, kept = eliminate(cond_of, cells(lambda m: q_s.at[0, m]), steps)
    for k, (w, h, p) in enumerate(kept):
        w_ref[k] = w
        h_ref[k] = h
        p_ref[k] = p
    firsts, lasts = cond_of(0), cond_of(steps - 1)
    total = tuple(v[:, 0] for v in block)
    for j in range(1, Y_PARTS):
        total, links = join(total, tuple(v[:, j] for v in block), lasts[:, j - 1] + firsts[:, j])
        for q in range(3):
            inner[q, j - 1] = links[q]
    views = total + (firsts[:, 0], lasts[:, Y_PARTS - 1])
    for q, value in enumerate(views):
        for m in range(pairs):
            e_s[q, m * SUBLANES : (m + 1) * SUBLANES, :] = value[m]

    def segment(s):
        return [e_s[q, pl.ds(s, pairs, stride=SUBLANES), :] for q in range(7)]

    total = segment(0)
    c_first, c_last = total[5], total[6]
    total = tuple(total[:5])
    for s in range(1, SUBLANES):
        item = segment(s)
        total, links = join(total, tuple(item[:5]), c_last + item[5])
        c_last = item[6]
        for q in range(3):
            outer[q, s - 1] = links[q]
    send[...] = jnp.zeros_like(send)
    for q, value in enumerate(total + (c_first, c_last)):
        for d in range(send.shape[0]):
            send[d, q * pairs : (q + 1) * pairs, :] = value


def y_forward(got, chain, xw, xh, xp, temperature, base, per, gy):
    sheets, rows, columns = temperature.shape
    chunks = columns // LANES
    lines = sheets * chunks
    pairs = sheets * rows // LANES
    steps = columns // SUBLANES // Y_PARTS
    stored = jax.ShapeDtypeStruct((steps, pairs, Y_PARTS, SUBLANES, LANES), F32)
    return pl.pallas_call(
        functools.partial(y_forward_kernel, per),
        out_shape=[
            stored,
            stored,
            stored,
            jax.ShapeDtypeStruct((3, Y_PARTS - 1, pairs, SUBLANES, LANES), F32),
            jax.ShapeDtypeStruct((3, SUBLANES - 1, pairs, LANES), F32),
            jax.ShapeDtypeStruct((gy, padded(7 * pairs), LANES), F32),
        ],
        scratch_shapes=[
            pltpu.VMEM((7, max(lines, pairs * SUBLANES), LANES), F32),
            pltpu.VMEM((2, lines * SUBLANES, LANES), F32),
            pltpu.VMEM((lines, rows, LANES), F32),
            pltpu.VMEM((pairs, columns, LANES), F32),
            pltpu.VMEM((1, pairs, columns, LANES), F32),
        ],
        compiler_params=pltpu.CompilerParams(vmem_limit_bytes=VMEM_LIMIT),
    )(got, chain, xw, xh, xp, temperature, base)


def finish_kernel(got, inner, outer, yw, yh, yp, t_ref, b_ref, out, e_s, u_s):
    sheets, rows, columns = t_ref.shape
    chunks = columns // LANES
    pairs = sheets * rows // LANES
    each = sheets // pairs
    steps = yw.shape[0]
    span = columns // SUBLANES
    count = got.shape[0]
    me = lax.axis_index("gy")

    def item(k):
        return [got[k, q * pairs : (q + 1) * pairs, :] for q in range(7)]

    fluxes = chain_fluxes(item, count)
    low = jnp.zeros((pairs, LANES), F32)
    flux = low
    for k in range(count - 1):
        low = jnp.where(me == k + 1, -fluxes[k], low)
        flux = jnp.where(me == k, fluxes[k], flux)
    for s in range(SUBLANES - 1, -1, -1):
        e_s[1, pl.ds(s, pairs, stride=SUBLANES), :] = flux
        if s > 0:
            flux = outer[0, s - 1] + outer[1, s - 1] * flux - outer[2, s - 1] * low
            e_s[0, pl.ds(s, pairs, stride=SUBLANES), :] = -flux
        else:
            e_s[0, pl.ds(s, pairs, stride=SUBLANES), :] = low
    ends = [
        jnp.stack([e_s[i, m * SUBLANES : (m + 1) * SUBLANES, :] for m in range(pairs)], 0)
        for i in range(2)
    ]
    lows, highs = [None] * Y_PARTS, [None] * Y_PARTS
    flux = ends[1]
    for j in range(Y_PARTS - 1, -1, -1):
        highs[j] = flux
        if j > 0:
            flux = inner[0, j - 1] + inner[1, j - 1] * flux - inner[2, j - 1] * ends[0]
            lows[j] = -flux
        else:
            lows[j] = ends[0]
    low = jnp.stack(lows, 1)
    value = jnp.stack(highs, 1)
    for k in range(steps - 1, -1, -1):
        value = yw[k] * value + (yh[k] + yp[k] * low)
        for m in range(pairs):
            for j in range(Y_PARTS):
                u_s[m, pl.ds(j * steps + k, SUBLANES, stride=span), :] = value[m, j]

    for y in range(chunks):
        part = slice(y * LANES, (y + 1) * LANES)
        turned = [u_s[m, part, :].T for m in range(pairs)]
        for r in range(rows // SUBLANES):
            at = slice(r * SUBLANES, (r + 1) * SUBLANES)
            ts = [t_ref[z, at, part] for z in range(sheets)]
            cs = [half_conduct(b_ref[z, at, part], ts[z]) for z in range(sheets)]
            ground, rhs, kept = None, None, []
            for z in range(sheets):
                first = (z % each) * rows + r * SUBLANES
                own = turned[z // each][first : first + SUBLANES, :]
                if z == 0:
                    rhs = own
                else:
                    face = cs[z - 1] + cs[z]
                    before = 1.0 if ground is None else ground
                    inv = 1.0 / (before + face)
                    w = face * inv
                    kept.append((w, rhs * inv))
                    rhs = own + w * rhs
                    ground = 1.0 + w * before
            value = rhs / ground
            out[sheets - 1, at, part] = ts[sheets - 1] + value
            for z in range(sheets - 2, -1, -1):
                w, h = kept[z]
                value = w * value + h
                out[z, at, part] = ts[z] + value


def finish(got, inner, outer, yw, yh, yp, temperature, base):
    sheets, rows, columns = temperature.shape
    pairs = sheets * rows // LANES
    return pl.pallas_call(
        finish_kernel,
        out_shape=jax.ShapeDtypeStruct(temperature.shape, F32),
        scratch_shapes=[
            pltpu.VMEM((2, pairs * SUBLANES, LANES), F32),
            pltpu.VMEM((pairs, columns, LANES), F32),
        ],
        compiler_params=pltpu.CompilerParams(vmem_limit_bytes=VMEM_LIMIT),
    )(got, inner, outer, yw, yh, yp, temperature, base)


def per_device(temperature, base, locations, energy):
    sheets, rows, columns = temperature.shape
    gx, gy = lax.axis_size("gx"), lax.axis_size("gy")
    lines = sheets * columns // LANES
    per = max(1, lines // gx)
    low_edge, high_edge = pack_edges(temperature, base)
    before = lax.ppermute(high_edge, "gy", [(i, i + 1) for i in range(gy - 1)])
    after = lax.ppermute(low_edge, "gy", [(i + 1, i) for i in range(gy - 1)])
    xw, xh, xp, chain, send = x_forward(
        temperature, base, before, after, locations[None], energy[None], gx, per, columns * gy
    )
    got = lax.all_to_all(send, "gx", split_axis=0, concat_axis=0, tiled=True)
    fluxes = lax.all_to_all(x_interface(got, per), "gx", split_axis=0, concat_axis=0, tiled=True)
    yw, yh, yp, inner, outer, send = y_forward(
        fluxes, chain, xw, xh, xp, temperature, base, per, gy
    )
    got = lax.all_to_all(send, "gy", split_axis=0, concat_axis=0, tiled=True)
    return finish(got, inner, outer, yw, yh, yp, temperature, base)


def solution(mesh):
    in_specs = (P(None, "gx", "gy"), P(None, "gx", "gy"), P(), P())
    out_specs = P(None, "gx", "gy")
    return jax.shard_map(
        per_device, mesh=mesh, in_specs=in_specs, out_specs=out_specs, check_vma=False
    )
```

```python
import functools

import jax
import jax.numpy as jnp
from jax import lax
from jax.experimental import pallas as pl
from jax.experimental.pallas import tpu as pltpu
from jax.sharding import PartitionSpec as P

RATE = 2000.0
THERMAL_GROWTH = 0.8
LANES = 128
SUBLANES = 8
Y_PARTS = 4
F32 = jnp.float32
MIB = 1024 * 1024
ANYWHERE = pl.BlockSpec(memory_space=pl.ANY)
IN_HBM = pl.BlockSpec(memory_space=pltpu.HBM)
IN_VMEM = pl.BlockSpec(memory_space=pltpu.VMEM)

R00, R0L, RLL, FIRST, LAST, C0, CL = range(7)
COEFS = (R00, R0L, RLL, C0, CL)


def params(limit=40):
    return pltpu.CompilerParams(vmem_limit_bytes=limit * MIB)


def shape_of(*sizes):
    return jax.ShapeDtypeStruct(sizes, F32)


def half_conduct(base, temperature):
    return base * (0.5 * RATE + (0.5 * RATE * THERMAL_GROWTH) * temperature)


def inverse(x):
    guess = pl.reciprocal(x, approx=True)
    return guess * (2.0 - x * guess)


def join_coefs(a, b):
    face = a[CL] + b[C0]
    inv = face * inverse(1.0 + face * (a[RLL] + b[R00]))
    left = a[R0L] * inv
    right = b[R0L] * inv
    joined = {
        R00: a[R00] - left * a[R0L],
        R0L: left * b[R0L],
        RLL: b[RLL] - right * b[R0L],
        C0: a[C0],
        CL: b[CL],
    }
    return joined, (inv, right, left)


def join_targets(a, b, links):
    inv, right, left = links
    jump = b[0] - a[1]
    return (a[0] + left * jump, b[1] - right * jump), jump * inv


def between(own, right, left, low, high):
    return own + right * high - left * low


def tree(items, join):
    levels = []
    while len(items) > 1:
        pairs = [join(items[i], items[i + 1]) for i in range(0, len(items), 2)]
        items = [p[0] for p in pairs]
        levels.append([p[1] for p in pairs])
    return items[0], levels


def descend(levels, low, high):
    ends = [(low, high)]
    for level in reversed(levels):
        below = []
        for (lo, hi), (own, right, left) in zip(ends, level):
            flux = between(own, right, left, lo, hi)
            below += [(lo, flux), (-flux, hi)]
        ends = below
    return ends


def node_offsets(leaves):
    offsets, at, count = [], 0, leaves // 2
    while count:
        offsets.append((at, count))
        at += count
        count //= 2
    return offsets


def factor(cond, steps, keep):
    here = cond(0)
    c_first = here
    one = jnp.ones_like(here)
    ground, path, first_first = one, one, None
    for k in range(steps - 1):
        following = cond(k + 1)
        face = here + following
        inv = inverse(ground + face)
        w = face * inv
        p = path * inv
        keep(k, w, inv, p)
        step = path * p
        first_first = step if first_first is None else first_first + step
        path = path * w
        ground = 1.0 + w * ground
        here = following
    inv = inverse(ground)
    p = path * inv
    keep(steps - 1, inv, inv, p)
    return {R00: first_first + path * p, R0L: p, RLL: inv, C0: c_first, CL: here}


def eliminate(target, steps, w, inv, p, keep):
    rhs = target(0)
    first = None
    for k in range(steps):
        h = rhs * inv(k)
        keep(k, h)
        step = rhs * p(k)
        first = step if first is None else first + step
        if k < steps - 1:
            rhs = target(k + 1) + w(k) * rhs
    return first, h


def load_kernel(t_hbm, b_hbm, loc_hbm, energy_hbm, t_out, b_out, loc, energy, lo, hi, sems):
    chunks, sheets, rows, _ = t_out.shape
    order = [0, chunks - 1] + list(range(1, chunks - 1))
    copies = {}
    for y in order:
        part = pl.ds(y * LANES, LANES)
        copies[y] = [
            pltpu.make_async_copy(src.at[:, :, part], dst.at[y], sems.at[i, y])
            for i, (src, dst) in enumerate(((t_hbm, t_out), (b_hbm, b_out)))
        ]
        for copy in copies[y]:
            copy.start()
    small = [
        pltpu.make_async_copy(loc_hbm, loc, sems.at[2, 0]),
        pltpu.make_async_copy(energy_hbm, energy, sems.at[2, 1]),
    ]
    for copy in small:
        copy.start()
    lane = lax.broadcasted_iota(jnp.int32, (rows, LANES), 1)
    for y, out, source in ((0, lo, 0), (chunks - 1, hi, LANES - 1)):
        for copy in copies[y]:
            copy.wait()
        packed = jnp.zeros((rows, LANES), F32)
        for z in range(sheets):
            t = t_out[y, z]
            c = half_conduct(b_out[y, z], t)
            packed = jnp.where(lane == z, t[:, source : source + 1], packed)
            packed = jnp.where(lane == sheets + z, c[:, source : source + 1], packed)
        out[...] = packed
    for y in range(1, chunks - 1):
        for copy in copies[y]:
            copy.wait()
    for copy in small:
        copy.wait()


def load(temperature, base, locations, energy):
    sheets, rows, columns = temperature.shape
    chunks = columns // LANES
    field = shape_of(chunks, sheets, rows, LANES)
    return pl.pallas_call(
        load_kernel,
        in_specs=[IN_HBM] * 4,
        out_shape=[
            field,
            field,
            jax.ShapeDtypeStruct(locations.shape, jnp.int32),
            jax.ShapeDtypeStruct(energy.shape, F32),
            shape_of(rows, LANES),
            shape_of(rows, LANES),
        ],
        scratch_shapes=[pltpu.SemaphoreType.DMA((3, max(2, chunks)))],
        compiler_params=params(55),
    )(temperature, base, locations, energy)


def source_plane(loc, energy, rows, columns, plate):
    place = loc[...]
    count = place.shape[1]
    local_x = place // plate - lax.axis_index("gx") * rows
    local_y = place % plate - lax.axis_index("gy") * columns
    in_x = lax.broadcasted_iota(jnp.int32, (rows, count), 0) == local_x
    in_y = lax.broadcasted_iota(jnp.int32, (columns, count), 0) == local_y
    by_y = jnp.where(in_y, 1.0, 0.0).astype(jnp.bfloat16)
    left = energy[...]
    plane = None
    for _ in range(3):
        part = left.astype(jnp.bfloat16).astype(F32)
        left = left - part
        term = lax.dot_general(
            jnp.where(in_x, part, 0.0).astype(jnp.bfloat16),
            by_y,
            (((1,), (1,)), ((), ())),
            preferred_element_type=F32,
        )
        plane = term if plane is None else plane + term
    return plane


def x_factor_kernel(plate, loc, energy, t_ref, b_ref, c_ref, total_ref, w_ref, i_ref, p_ref, links, view, q_s):
    chunks, sheets, rows, _ = t_ref.shape
    lines = chunks * sheets
    steps = rows // SUBLANES
    plane = source_plane(loc, energy, rows, chunks * LANES, plate)

    lane = lax.broadcasted_iota(jnp.int32, (SUBLANES, LANES), 1)
    is_first, is_last = lane == 0, lane == LANES - 1
    for r in range(steps):
        at = slice(r * SUBLANES, (r + 1) * SUBLANES)
        before_t, before_c = None, None
        for z in range(sheets):
            ts = [t_ref[y, z, at, :] for y in range(chunks)]
            cs = [half_conduct(b_ref[y, z, at, :], ts[y]) for y in range(chunks)]
            t_turned = [pltpu.roll(v, LANES - 1, 1) for v in ts]
            c_turned = [pltpu.roll(v, LANES - 1, 1) for v in cs]
            flux = []
            for y in range(chunks):
                if y < chunks - 1:
                    t_next = jnp.where(is_last, t_turned[y + 1], t_turned[y])
                    c_next = jnp.where(is_last, c_turned[y + 1], c_turned[y])
                    flux.append((cs[y] + c_next) * (t_next - ts[y]))
                else:
                    inside = (cs[y] + c_turned[y]) * (t_turned[y] - ts[y])
                    flux.append(jnp.where(is_last, 0.0, inside))
            turned = [pltpu.roll(v, 1, 1) for v in flux]
            for y in range(chunks):
                from_low = jnp.where(is_first, turned[y - 1] if y else 0.0, turned[y])
                total = ts[y] + (flux[y] - from_low)
                if z == 0:
                    total = total + plane[at, y * LANES : (y + 1) * LANES]
                else:
                    across = (before_c[y] + cs[y]) * (ts[y] - before_t[y])
                    total = total - across
                    total_ref[y, z - 1, at, :] += across
                total_ref[y, z, at, :] = total
                c_ref[y, z, at, :] = cs[y]
            before_t, before_c = ts, cs

    group = max(1, 8 // sheets)
    for y in range(0, chunks, group):
        members = [(y + i, z) for i in range(group) for z in range(sheets)]
        at = slice(y * sheets, (y + group) * sheets)

        def cond(k):
            return jnp.stack([c_ref[i, z, pl.ds(k, SUBLANES, stride=steps), :] for i, z in members], 0)

        def keep(k, w, inv, p):
            w_ref[k, at] = w
            i_ref[k, at] = inv
            p_ref[k, at] = p

        block = factor(cond, steps, keep)
        for n, q in enumerate(COEFS):
            for i in range(len(members)):
                first = (y * sheets + i) * SUBLANES
                q_s[n, first : first + SUBLANES, :] = block[q][i]

    segments = [
        {q: q_s[n, pl.ds(s, lines, stride=SUBLANES), :] for n, q in enumerate(COEFS)}
        for s in range(SUBLANES)
    ]
    whole, levels = tree(segments, join_coefs)
    for (offset, _), level in zip(node_offsets(SUBLANES), levels):
        for n, values in enumerate(level):
            for i in range(3):
                links[offset + n, i] = values[i]
    for n, q in enumerate(COEFS):
        view[n] = whole[q]


def x_factor(loc, energy, t, b, plate):
    chunks, sheets, rows, _ = t.shape
    lines = chunks * sheets
    steps = rows // SUBLANES
    field = shape_of(*t.shape)
    stored = shape_of(steps, lines, SUBLANES, LANES)
    return pl.pallas_call(
        functools.partial(x_factor_kernel, plate),
        out_shape=[
            field,
            field,
            stored,
            stored,
            stored,
            shape_of(SUBLANES - 1, 3, lines, LANES),
            shape_of(len(COEFS), lines, LANES),
        ],
        scratch_shapes=[pltpu.VMEM((len(COEFS), lines * SUBLANES, LANES), F32)],
        compiler_params=params(),
        cost_estimate=pl.CostEstimate(flops=40 * t.size, bytes_accessed=28 * t.size, transcendentals=0),
    )(loc, energy, t, b)


def x_target_kernel(t_ref, c_ref, total_ref, before, after, w_ref, i_ref, p_ref, links, view, h_ref, own, send, e_s, q_s):
    chunks, sheets, rows, _ = t_ref.shape
    lines = chunks * sheets
    steps = rows // SUBLANES

    lane = lax.broadcasted_iota(jnp.int32, (rows, LANES), 1)
    for y, halo, edge, place in ((0, before, 0, 0), (chunks - 1, after, LANES - 1, 1)):
        for z in range(sheets):
            c_next = halo[:, sheets + z : sheets + z + 1]
            t_next = halo[:, z : z + 1]
            face = jnp.where(c_next > 0.0, c_ref[y, z] + c_next, 0.0)
            flux = jnp.where(lane == edge, face * (t_next - t_ref[y, z]), 0.0)
            base = total_ref[y, z] if place == 0 or chunks > 1 else e_s[0, z]
            e_s[place, z] = base + flux

    def field(y, z):
        if y == chunks - 1:
            return e_s.at[1, z]
        return e_s.at[0, z] if y == 0 else total_ref.at[y, z]

    group = max(1, 8 // sheets)
    for y in range(0, chunks, group):
        members = [(y + i, z) for i in range(group) for z in range(sheets)]
        at = slice(y * sheets, (y + group) * sheets)

        def target(k):
            return jnp.stack([field(i, z)[pl.ds(k, SUBLANES, stride=steps), :] for i, z in members], 0)

        def keep(k, h):
            h_ref[k, at] = h

        ends = eliminate(
            target, steps, lambda k: w_ref[k, at], lambda k: i_ref[k, at], lambda k: p_ref[k, at], keep
        )
        for q in range(2):
            for i in range(len(members)):
                first = (y * sheets + i) * SUBLANES
                q_s[q, first : first + SUBLANES, :] = ends[q][i]
    items = [
        tuple(q_s[q, pl.ds(s, lines, stride=SUBLANES), :] for q in range(2)) for s in range(SUBLANES)
    ]
    for offset, count in node_offsets(SUBLANES):
        joined = []
        for n in range(count):
            ties = tuple(links[offset + n, i] for i in range(3))
            both, flux = join_targets(items[2 * n], items[2 * n + 1], ties)
            own[offset + n] = flux
            joined.append(both)
        items = joined
    for n, q in enumerate(COEFS):
        send[q] = view[n]
    send[FIRST], send[LAST] = items[0]


def x_target(t, c, total, before, after, w, inv, p, links, view):
    chunks, sheets, rows, _ = t.shape
    lines = chunks * sheets
    steps = rows // SUBLANES
    return pl.pallas_call(
        x_target_kernel,
        out_shape=[
            shape_of(steps, lines, SUBLANES, LANES),
            shape_of(SUBLANES - 1, lines, LANES),
            shape_of(7, lines, LANES),
        ],
        scratch_shapes=[
            pltpu.VMEM((2, sheets, rows, LANES), F32),
            pltpu.VMEM((2, lines * SUBLANES, LANES), F32),
        ],
        compiler_params=params(),
    )(t, c, total, before, after, w, inv, p, links, view)


def stages_of(axis):
    return lax.axis_size(axis).bit_length() - 1


def swap(value, axis, stage):
    count = lax.axis_size(axis)
    return lax.ppermute(value, axis, [(i, i ^ (1 << stage)) for i in range(count)])


def on_right(axis, stage):
    return (lax.axis_index(axis) >> stage) % 2 == 1


def toward(right, block):
    return (
        jnp.where(right, block[R00], block[RLL]),
        jnp.where(right, block[FIRST], block[LAST]),
        jnp.where(right, block[C0], block[CL]),
    )


def join_kernel(axis, stage, last, own, got, *refs):
    send, links = refs[-2:]
    right = on_right(axis, stage)
    a = {q: jnp.where(right, got[q], own[q]) for q in range(7)}
    b = {q: jnp.where(right, own[q], got[q]) for q in range(7)}
    joined, ties = join_coefs(a, b)
    (joined[FIRST], joined[LAST]), flux = join_targets((a[FIRST], a[LAST]), (b[FIRST], b[LAST]), ties)
    links[0], links[1], links[2] = flux, ties[1], ties[2]
    if last:
        for n, value in enumerate(toward(on_right(axis, stage + 1), joined)):
            send[n] = value
    else:
        for q in range(7):
            send[q] = joined[q]


def join_stage(own, got, axis, stage, last, after):
    lines = own.shape[1]
    return pl.pallas_call(
        functools.partial(join_kernel, axis, stage, last),
        in_specs=[IN_VMEM] * 2 + [ANYWHERE] * len(after),
        out_shape=[shape_of(3 if last else 7, lines, LANES), shape_of(3, lines, LANES)],
        compiler_params=params(),
    )(own, got, *after)


def gather_line(view, axis, meanwhile=()):
    stages = stages_of(axis)
    links = []
    for stage in range(stages - 1):
        got = swap(view, axis, stage)
        view, tie = join_stage(view, got, axis, stage, stage == stages - 2, meanwhile[stage : stage + 1])
        links.append(tie)
    return view, swap(view, axis, stages - 1), links


def block_ends(axis, own, got, links):
    top = len(links)
    right = on_right(axis, top)
    face = own[2] + got[2]
    jump = jnp.where(right, own[1] - got[1], got[1] - own[1])
    flux = jump * face * inverse(1.0 + face * (own[0] + got[0]))
    low = jnp.where(right, -flux, 0.0)
    high = jnp.where(right, 0.0, flux)
    for stage in range(top - 1, -1, -1):
        tie = links[stage]
        right = on_right(axis, stage)
        flux = between(tie[0], tie[1], tie[2], low, high)
        low, high = jnp.where(right, -flux, low), jnp.where(right, high, flux)
    return low, high


def y_factor_kernel(c_ref, after, w_ref, i_ref, p_ref, inner, outer, view, c_s, q_s):
    chunks, sheets, rows, _ = c_ref.shape
    each = LANES // rows
    pairs = sheets // each
    span = chunks * LANES // SUBLANES
    steps = span // Y_PARTS
    for m in range(pairs):
        for y in range(chunks):
            block = jnp.concatenate([c_ref[y, m * each + i] for i in range(each)], 0)
            c_s[m, y * LANES : (y + 1) * LANES, :] = block.T

    members = [(j, m) for j in range(Y_PARTS) for m in range(pairs)]

    def cond(k):
        return jnp.stack([c_s[m, pl.ds(j * steps + k, SUBLANES, stride=span), :] for j, m in members], 0)

    def keep(k, w, inv, p):
        w_ref[k] = w
        i_ref[k] = inv
        p_ref[k] = p

    block = factor(cond, steps, keep)
    parts = [{q: block[q][j * pairs : (j + 1) * pairs] for q in COEFS} for j in range(Y_PARTS)]
    whole, levels = tree(parts, join_coefs)
    for (offset, _), level in zip(node_offsets(Y_PARTS), levels):
        for n, values in enumerate(level):
            for i in range(3):
                inner[offset + n, i] = values[i]
    for n, q in enumerate(COEFS):
        for m in range(pairs):
            q_s[n, m * SUBLANES : (m + 1) * SUBLANES, :] = whole[q][m]
    segments = [
        {q: q_s[n, pl.ds(s, pairs, stride=SUBLANES), :] for n, q in enumerate(COEFS)}
        for s in range(SUBLANES)
    ]
    whole, levels = tree(segments, join_coefs)
    for (offset, _), level in zip(node_offsets(SUBLANES), levels):
        for n, values in enumerate(level):
            for i in range(3):
                outer[offset + n, i] = values[i]
    for n, q in enumerate(COEFS):
        view[n] = whole[q]


def y_factor(c, after):
    chunks, sheets, rows, _ = c.shape
    pairs = sheets * rows // LANES
    steps = chunks * LANES // SUBLANES // Y_PARTS
    stored = shape_of(steps, Y_PARTS * pairs, SUBLANES, LANES)
    return pl.pallas_call(
        y_factor_kernel,
        in_specs=[IN_VMEM, ANYWHERE],
        out_shape=[
            stored,
            stored,
            stored,
            shape_of(Y_PARTS - 1, 3, pairs, SUBLANES, LANES),
            shape_of(SUBLANES - 1, 3, pairs, LANES),
            shape_of(len(COEFS), pairs, LANES),
        ],
        scratch_shapes=[
            pltpu.VMEM((pairs, chunks * LANES, LANES), F32),
            pltpu.VMEM((len(COEFS), pairs * SUBLANES, LANES), F32),
        ],
        compiler_params=params(),
        cost_estimate=pl.CostEstimate(flops=20 * c.size, bytes_accessed=16 * c.size, transcendentals=0),
    )(c, after)


def z_factor_kernel(c_ref, after, w_ref, i_ref):
    sheets = c_ref.shape[1]
    ground = 1.0
    for z in range(sheets - 1):
        face = c_ref[:, z] + c_ref[:, z + 1]
        inv = inverse(ground + face)
        w = face * inv
        i_ref[z] = inv
        w_ref[z] = w
        ground = 1.0 + w * ground
    i_ref[sheets - 1] = inverse(ground)


def z_factor(c, after):
    chunks, sheets, rows, _ = c.shape
    return pl.pallas_call(
        z_factor_kernel,
        in_specs=[IN_VMEM, ANYWHERE],
        out_shape=[
            shape_of(sheets - 1, chunks, rows, LANES),
            shape_of(sheets, chunks, rows, LANES),
        ],
        compiler_params=params(),
        cost_estimate=pl.CostEstimate(flops=10 * c.size, bytes_accessed=12 * c.size, transcendentals=0),
    )(c, after)


def y_target_kernel(stages, *refs):
    own, got = refs[:2]
    ties = refs[2 : 1 + stages]
    xw, xh, xp, x_links, x_own, t_ref, yw, yi, yp, inner, outer, view = refs[1 + stages : 13 + stages]
    h_ref, inner_own, outer_own, send = refs[13 + stages : 17 + stages]
    f_s, g_s, y_s, q_s = refs[17 + stages :]
    chunks, sheets, rows, _ = t_ref.shape
    lines = chunks * sheets
    x_steps = rows // SUBLANES

    low, high = block_ends("gx", own, got, ties)
    levels = [
        [(x_own[o + n], x_links[o + n, 1], x_links[o + n, 2]) for n in range(count)]
        for o, count in node_offsets(SUBLANES)
    ]
    for s, ends in enumerate(descend(levels, low, high)):
        for i in range(2):
            f_s[i, pl.ds(s, lines, stride=SUBLANES), :] = ends[i]
    group = max(1, 8 // sheets)
    for y in range(0, chunks, group):
        members = [(y + i, z) for i in range(group) for z in range(sheets)]
        at = slice(y * sheets, (y + group) * sheets)
        low, value = (
            jnp.stack(
                [
                    f_s[i, (y * sheets + n) * SUBLANES : (y * sheets + n + 1) * SUBLANES, :]
                    for n in range(len(members))
                ],
                0,
            )
            for i in range(2)
        )
        for k in range(x_steps - 1, -1, -1):
            value = xw[k, at] * value + (xh[k, at] + xp[k, at] * low)
            for n, (i, z) in enumerate(members):
                g_s[i, z, pl.ds(k, SUBLANES, stride=x_steps), :] = value[n]

    each = LANES // rows
    pairs = sheets // each
    span = chunks * LANES // SUBLANES
    steps = span // Y_PARTS
    for m in range(pairs):
        for y in range(chunks):
            block = jnp.concatenate(
                [g_s[y, m * each + i] - t_ref[y, m * each + i] for i in range(each)], 0
            )
            y_s[m, y * LANES : (y + 1) * LANES, :] = block.T
    members = [(j, m) for j in range(Y_PARTS) for m in range(pairs)]

    def target(k):
        return jnp.stack([y_s[m, pl.ds(j * steps + k, SUBLANES, stride=span), :] for j, m in members], 0)

    def keep(k, h):
        h_ref[k] = h

    ends = eliminate(target, steps, lambda k: yw[k], lambda k: yi[k], lambda k: yp[k], keep)
    items = [tuple(v[j * pairs : (j + 1) * pairs] for v in ends) for j in range(Y_PARTS)]
    for offset, count in node_offsets(Y_PARTS):
        joined = []
        for n in range(count):
            tie = tuple(inner[offset + n, i] for i in range(3))
            both, flux = join_targets(items[2 * n], items[2 * n + 1], tie)
            inner_own[offset + n] = flux
            joined.append(both)
        items = joined
    for q in range(2):
        for m in range(pairs):
            q_s[q, m * SUBLANES : (m + 1) * SUBLANES, :] = items[0][q][m]
    items = [
        tuple(q_s[q, pl.ds(s, pairs, stride=SUBLANES), :] for q in range(2)) for s in range(SUBLANES)
    ]
    for offset, count in node_offsets(SUBLANES):
        joined = []
        for n in range(count):
            tie = tuple(outer[offset + n, i] for i in range(3))
            both, flux = join_targets(items[2 * n], items[2 * n + 1], tie)
            outer_own[offset + n] = flux
            joined.append(both)
        items = joined
    for n, q in enumerate(COEFS):
        send[q] = view[n]
    send[FIRST], send[LAST] = items[0]


def y_target(own, got, ties, xw, xh, xp, x_links, x_own, t, yw, yi, yp, inner, outer, view):
    chunks, sheets, rows, _ = t.shape
    lines = chunks * sheets
    pairs = sheets * rows // LANES
    return pl.pallas_call(
        functools.partial(y_target_kernel, len(ties) + 1),
        out_shape=[
            shape_of(*yw.shape),
            shape_of(Y_PARTS - 1, pairs, SUBLANES, LANES),
            shape_of(SUBLANES - 1, pairs, LANES),
            shape_of(7, pairs, LANES),
        ],
        scratch_shapes=[
            pltpu.VMEM((2, lines * SUBLANES, LANES), F32),
            pltpu.VMEM((chunks, sheets, rows, LANES), F32),
            pltpu.VMEM((pairs, chunks * LANES, LANES), F32),
            pltpu.VMEM((2, pairs * SUBLANES, LANES), F32),
        ],
        compiler_params=params(),
    )(own, got, *ties, xw, xh, xp, x_links, x_own, t, yw, yi, yp, inner, outer, view)


def finish_kernel(stages, *refs):
    own, got = refs[:2]
    ties = refs[2 : 1 + stages]
    yw, yh, yp, inner, inner_own, outer, outer_own, zw, zi, t_ref = refs[1 + stages : 11 + stages]
    out, e_s, u_s, o_s, sems = refs[11 + stages :]
    chunks, sheets, rows, _ = t_ref.shape
    each = LANES // rows
    pairs = sheets // each
    steps = yw.shape[0]
    span = chunks * LANES // SUBLANES

    low, high = block_ends("gy", own, got, ties)
    levels = [
        [(outer_own[o + n], outer[o + n, 1], outer[o + n, 2]) for n in range(count)]
        for o, count in node_offsets(SUBLANES)
    ]
    for s, ends in enumerate(descend(levels, low, high)):
        for i in range(2):
            e_s[i, pl.ds(s, pairs, stride=SUBLANES), :] = ends[i]
    low, high = (
        jnp.stack([e_s[i, m * SUBLANES : (m + 1) * SUBLANES, :] for m in range(pairs)], 0)
        for i in range(2)
    )
    levels = [
        [(inner_own[o + n], inner[o + n, 1], inner[o + n, 2]) for n in range(count)]
        for o, count in node_offsets(Y_PARTS)
    ]
    ends = descend(levels, low, high)
    low = jnp.concatenate([e[0] for e in ends], 0)
    value = jnp.concatenate([e[1] for e in ends], 0)
    members = [(j, m) for j in range(Y_PARTS) for m in range(pairs)]
    for k in range(steps - 1, -1, -1):
        value = yw[k] * value + (yh[k] + yp[k] * low)
        for n, (j, m) in enumerate(members):
            u_s[m, pl.ds(j * steps + k, SUBLANES, stride=span), :] = value[n]

    copies = []
    for y in range(chunks):
        part = slice(y * LANES, (y + 1) * LANES)
        turned = [u_s[m, part, :].T for m in range(pairs)]
        rhs, kept = None, []
        for z in range(sheets):
            first = (z % each) * rows
            own_rhs = turned[z // each][first : first + rows, :]
            rhs = own_rhs if z == 0 else own_rhs + zw[z - 1, y] * rhs
            kept.append(rhs * zi[z, y])
        value = kept[-1]
        o_s[y, sheets - 1] = t_ref[y, sheets - 1] + value
        for z in range(sheets - 2, -1, -1):
            value = zw[z, y] * value + kept[z]
            o_s[y, z] = t_ref[y, z] + value
        copy = pltpu.make_async_copy(o_s.at[y], out.at[:, :, pl.ds(y * LANES, LANES)], sems.at[y])
        copy.start()
        copies.append(copy)
    for copy in copies:
        copy.wait()


def finish(own, got, ties, yw, yh, yp, inner, inner_own, outer, outer_own, zw, zi, t):
    chunks, sheets, rows, _ = t.shape
    pairs = sheets * rows // LANES
    return pl.pallas_call(
        functools.partial(finish_kernel, len(ties) + 1),
        out_shape=shape_of(sheets, rows, chunks * LANES),
        out_specs=ANYWHERE,
        scratch_shapes=[
            pltpu.VMEM((2, pairs * SUBLANES, LANES), F32),
            pltpu.VMEM((pairs, chunks * LANES, LANES), F32),
            pltpu.VMEM(t.shape, F32),
            pltpu.SemaphoreType.DMA((chunks,)),
        ],
        compiler_params=params(),
    )(own, got, *ties, yw, yh, yp, inner, inner_own, outer, outer_own, zw, zi, t)


def per_device(temperature, base, locations, energy):
    columns = temperature.shape[2]
    gy = lax.axis_size("gy")
    t, b, loc, heat, low_edge, high_edge = load(temperature, base, locations[None], energy[None])
    before = lax.ppermute(high_edge, "gy", [(i, i + 1) for i in range(gy - 1)])
    after = lax.ppermute(low_edge, "gy", [(i + 1, i) for i in range(gy - 1)])
    c, total, xw, xi, xp, x_links, x_view = x_factor(loc, heat, t, b, columns * gy)
    xh, x_own, view = x_target(t, c, total, before, after, xw, xi, xp, x_links, x_view)
    yw, yi, yp, inner, outer, y_view = y_factor(c, view)
    zw, zi = z_factor(c, view)
    own, got, ties = gather_line(view, "gx", (y_view, zw))
    yh, inner_own, outer_own, view = y_target(
        own, got, ties, xw, xh, xp, x_links, x_own, t, yw, yi, yp, inner, outer, y_view
    )
    own, got, ties = gather_line(view, "gy")
    return finish(own, got, ties, yw, yh, yp, inner, inner_own, outer, outer_own, zw, zi, t)


def solution(mesh):
    in_specs = (P(None, "gx", "gy"), P(None, "gx", "gy"), P(), P())
    out_specs = P(None, "gx", "gy")
    return jax.shard_map(
        per_device, mesh=mesh, in_specs=in_specs, out_specs=out_specs, check_vma=False
    )
```

```python
import functools

import jax
import jax.numpy as jnp
from jax import lax
from jax.experimental import pallas as pl
from jax.experimental.pallas import tpu as pltpu
from jax.sharding import PartitionSpec as P

RATE = 2000.0
THERMAL_GROWTH = 0.8
LANES = 128
SUBLANES = 8
Y_PARTS = 4
F32 = jnp.float32
MIB = 1024 * 1024
ANYWHERE = pl.BlockSpec(memory_space=pl.ANY)
IN_HBM = pl.BlockSpec(memory_space=pltpu.HBM)
IN_VMEM = pl.BlockSpec(memory_space=pltpu.VMEM)

R00, R0L, RLL, FIRST, LAST, C0, CL = range(7)
COEFS = (R00, R0L, RLL, C0, CL)


def params(limit=40):
    return pltpu.CompilerParams(vmem_limit_bytes=limit * MIB)


def shape_of(*sizes):
    return jax.ShapeDtypeStruct(sizes, F32)


def half_conduct(base, temperature):
    return base * (0.5 * RATE + (0.5 * RATE * THERMAL_GROWTH) * temperature)


def inverse(x):
    guess = pl.reciprocal(x, approx=True)
    return guess * (2.0 - x * guess)


def join_coefs(a, b):
    face = a[CL] + b[C0]
    inv = face * inverse(1.0 + face * (a[RLL] + b[R00]))
    left = a[R0L] * inv
    right = b[R0L] * inv
    joined = {
        R00: a[R00] - left * a[R0L],
        R0L: left * b[R0L],
        RLL: b[RLL] - right * b[R0L],
        C0: a[C0],
        CL: b[CL],
    }
    return joined, (inv, right, left)


def join_targets(a, b, links):
    inv, right, left = links
    jump = b[0] - a[1]
    return (a[0] + left * jump, b[1] - right * jump), jump * inv


def between(own, right, left, low, high):
    return own + right * high - left * low


def tree(items, join):
    levels = []
    while len(items) > 1:
        pairs = [join(items[i], items[i + 1]) for i in range(0, len(items), 2)]
        items = [p[0] for p in pairs]
        levels.append([p[1] for p in pairs])
    return items[0], levels


def descend(levels, low, high):
    ends = [(low, high)]
    for level in reversed(levels):
        below = []
        for (lo, hi), (own, right, left) in zip(ends, level):
            flux = between(own, right, left, lo, hi)
            below += [(lo, flux), (-flux, hi)]
        ends = below
    return ends


def node_offsets(leaves):
    offsets, at, count = [], 0, leaves // 2
    while count:
        offsets.append((at, count))
        at += count
        count //= 2
    return offsets


def factor(cond, steps, keep):
    here = cond(0)
    c_first = here
    one = jnp.ones_like(here)
    ground, path, first_first = one, one, None
    for k in range(steps - 1):
        following = cond(k + 1)
        face = here + following
        inv = inverse(ground + face)
        w = face * inv
        p = path * inv
        keep(k, w, inv, p)
        step = path * p
        first_first = step if first_first is None else first_first + step
        path = path * w
        ground = 1.0 + w * ground
        here = following
    inv = inverse(ground)
    p = path * inv
    keep(steps - 1, inv, inv, p)
    return {R00: first_first + path * p, R0L: p, RLL: inv, C0: c_first, CL: here}


def eliminate(target, steps, w, inv, p, keep):
    rhs = target(0)
    first = None
    for k in range(steps):
        h = rhs * inv(k)
        keep(k, h)
        step = rhs * p(k)
        first = step if first is None else first + step
        if k < steps - 1:
            rhs = target(k + 1) + w(k) * rhs
    return first, h


def is_odd(axis):
    return lax.axis_index(axis) % 2 == 1


def load_kernel(t_hbm, b_hbm, loc_hbm, energy_hbm, t_out, b_out, loc, energy, near, far, sems):
    chunks, sheets, rows, _ = t_out.shape
    order = [0, chunks - 1] + list(range(1, chunks - 1))
    copies = {}
    for y in order:
        part = pl.ds(y * LANES, LANES)
        copies[y] = [
            pltpu.make_async_copy(src.at[:, :, part], dst.at[y], sems.at[i, y])
            for i, (src, dst) in enumerate(((t_hbm, t_out), (b_hbm, b_out)))
        ]
        for copy in copies[y]:
            copy.start()
    small = [
        pltpu.make_async_copy(loc_hbm, loc, sems.at[2, 0]),
        pltpu.make_async_copy(energy_hbm, energy, sems.at[2, 1]),
    ]
    for copy in small:
        copy.start()
    lane = lax.broadcasted_iota(jnp.int32, (rows, LANES), 1)
    edges = []
    for y, source in ((0, 0), (chunks - 1, LANES - 1)):
        for copy in copies[y] if y or not edges else ():
            copy.wait()
        packed = jnp.zeros((rows, LANES), F32)
        for z in range(sheets):
            t = t_out[y, z]
            c = half_conduct(b_out[y, z], t)
            packed = jnp.where(lane == z, t[:, source : source + 1], packed)
            packed = jnp.where(lane == sheets + z, c[:, source : source + 1], packed)
        edges.append(packed)
    near[...] = jnp.where(is_odd("gy"), edges[0], edges[1])
    far[...] = jnp.where(is_odd("gy"), edges[1], edges[0])
    for y in range(1, chunks - 1):
        for copy in copies[y]:
            copy.wait()
    for copy in small:
        copy.wait()


def load(temperature, base, locations, energy):
    sheets, rows, columns = temperature.shape
    chunks = columns // LANES
    field = pltpu.VMEM((chunks, sheets, rows, LANES), F32)
    return pl.pallas_call(
        load_kernel,
        in_specs=[IN_HBM] * 4,
        out_shape=[
            field,
            field,
            pltpu.VMEM(locations.shape, jnp.int32),
            pltpu.VMEM(energy.shape, F32),
            pltpu.VMEM((rows, LANES), F32),
            pltpu.VMEM((rows, LANES), F32),
        ],
        scratch_shapes=[pltpu.SemaphoreType.DMA((3, max(2, chunks)))],
        compiler_params=params(),
    )(*[pltpu.with_memory_space_constraint(v, pltpu.HBM) for v in (temperature, base, locations, energy)])


def source_plane(loc, energy, rows, columns, plate):
    place = loc[...]
    count = place.shape[1]
    local_x = place // plate - lax.axis_index("gx") * rows
    local_y = place % plate - lax.axis_index("gy") * columns
    in_x = lax.broadcasted_iota(jnp.int32, (rows, count), 0) == local_x
    in_y = lax.broadcasted_iota(jnp.int32, (columns, count), 0) == local_y
    by_y = jnp.where(in_y, 1.0, 0.0).astype(jnp.bfloat16)
    left = energy[...]
    plane = None
    for _ in range(3):
        part = left.astype(jnp.bfloat16).astype(F32)
        left = left - part
        term = lax.dot_general(
            jnp.where(in_x, part, 0.0).astype(jnp.bfloat16),
            by_y,
            (((1,), (1,)), ((), ())),
            preferred_element_type=F32,
        )
        plane = term if plane is None else plane + term
    return plane


def x_factor_kernel(plate, loc, energy, t_ref, b_ref, c_ref, total_ref, w_ref, i_ref, p_ref, links, view, q_s):
    chunks, sheets, rows, _ = t_ref.shape
    lines = chunks * sheets
    steps = rows // SUBLANES
    plane = source_plane(loc, energy, rows, chunks * LANES, plate)

    lane = lax.broadcasted_iota(jnp.int32, (SUBLANES, LANES), 1)
    is_first, is_last = lane == 0, lane == LANES - 1
    for r in range(steps):
        at = slice(r * SUBLANES, (r + 1) * SUBLANES)
        before_t, before_c = None, None
        for z in range(sheets):
            ts = [t_ref[y, z, at, :] for y in range(chunks)]
            cs = [half_conduct(b_ref[y, z, at, :], ts[y]) for y in range(chunks)]
            t_turned = [pltpu.roll(v, LANES - 1, 1) for v in ts]
            c_turned = [pltpu.roll(v, LANES - 1, 1) for v in cs]
            flux = []
            for y in range(chunks):
                if y < chunks - 1:
                    t_next = jnp.where(is_last, t_turned[y + 1], t_turned[y])
                    c_next = jnp.where(is_last, c_turned[y + 1], c_turned[y])
                    flux.append((cs[y] + c_next) * (t_next - ts[y]))
                else:
                    inside = (cs[y] + c_turned[y]) * (t_turned[y] - ts[y])
                    flux.append(jnp.where(is_last, 0.0, inside))
            turned = [pltpu.roll(v, 1, 1) for v in flux]
            for y in range(chunks):
                from_low = jnp.where(is_first, turned[y - 1] if y else 0.0, turned[y])
                total = ts[y] + (flux[y] - from_low)
                if z == 0:
                    total = total + plane[at, y * LANES : (y + 1) * LANES]
                else:
                    across = (before_c[y] + cs[y]) * (ts[y] - before_t[y])
                    total = total - across
                    total_ref[y, z - 1, at, :] += across
                total_ref[y, z, at, :] = total
                c_ref[y, z, at, :] = cs[y]
            before_t, before_c = ts, cs

    group = max(1, 8 // sheets)
    for y in range(0, chunks, group):
        members = [(y + i, z) for i in range(group) for z in range(sheets)]
        at = slice(y * sheets, (y + group) * sheets)

        def cond(k):
            return jnp.stack([c_ref[i, z, pl.ds(k, SUBLANES, stride=steps), :] for i, z in members], 0)

        def keep(k, w, inv, p):
            w_ref[k, at] = w
            i_ref[k, at] = inv
            p_ref[k, at] = p

        block = factor(cond, steps, keep)
        for n, q in enumerate(COEFS):
            for i in range(len(members)):
                first = (y * sheets + i) * SUBLANES
                q_s[n, first : first + SUBLANES, :] = block[q][i]

    segments = [
        {q: q_s[n, pl.ds(s, lines, stride=SUBLANES), :] for n, q in enumerate(COEFS)}
        for s in range(SUBLANES)
    ]
    whole, levels = tree(segments, join_coefs)
    for (offset, _), level in zip(node_offsets(SUBLANES), levels):
        for n, values in enumerate(level):
            for i in range(3):
                links[offset + n, i] = values[i]
    for n, q in enumerate(COEFS):
        view[n] = whole[q]


def x_factor(loc, energy, t, b, plate):
    chunks, sheets, rows, _ = t.shape
    lines = chunks * sheets
    steps = rows // SUBLANES
    field = shape_of(*t.shape)
    stored = shape_of(steps, lines, SUBLANES, LANES)
    return pl.pallas_call(
        functools.partial(x_factor_kernel, plate),
        out_shape=[
            field,
            field,
            stored,
            stored,
            stored,
            shape_of(SUBLANES - 1, 3, lines, LANES),
            shape_of(len(COEFS), lines, LANES),
        ],
        scratch_shapes=[pltpu.VMEM((len(COEFS), lines * SUBLANES, LANES), F32)],
        compiler_params=params(),
        cost_estimate=pl.CostEstimate(flops=40 * t.size, bytes_accessed=28 * t.size, transcendentals=0),
    )(loc, energy, t, b)


def x_target_kernel(t_ref, c_ref, total_ref, near, far, w_ref, i_ref, p_ref, links, view, h_ref, own, send, e_s, q_s):
    chunks, sheets, rows, _ = t_ref.shape
    lines = chunks * sheets
    steps = rows // SUBLANES

    before = jnp.where(is_odd("gy"), near[...], far[...])
    after = jnp.where(is_odd("gy"), far[...], near[...])
    lane = lax.broadcasted_iota(jnp.int32, (rows, LANES), 1)
    for y, halo, edge, place in ((0, before, 0, 0), (chunks - 1, after, LANES - 1, 1)):
        for z in range(sheets):
            c_next = halo[:, sheets + z : sheets + z + 1]
            t_next = halo[:, z : z + 1]
            face = jnp.where(c_next > 0.0, c_ref[y, z] + c_next, 0.0)
            flux = jnp.where(lane == edge, face * (t_next - t_ref[y, z]), 0.0)
            base = total_ref[y, z] if place == 0 or chunks > 1 else e_s[0, z]
            e_s[place, z] = base + flux

    def field(y, z):
        if y == chunks - 1:
            return e_s.at[1, z]
        return e_s.at[0, z] if y == 0 else total_ref.at[y, z]

    group = max(1, 8 // sheets)
    for y in range(0, chunks, group):
        members = [(y + i, z) for i in range(group) for z in range(sheets)]
        at = slice(y * sheets, (y + group) * sheets)

        def target(k):
            return jnp.stack([field(i, z)[pl.ds(k, SUBLANES, stride=steps), :] for i, z in members], 0)

        def keep(k, h):
            h_ref[k, at] = h

        ends = eliminate(
            target, steps, lambda k: w_ref[k, at], lambda k: i_ref[k, at], lambda k: p_ref[k, at], keep
        )
        for q in range(2):
            for i in range(len(members)):
                first = (y * sheets + i) * SUBLANES
                q_s[q, first : first + SUBLANES, :] = ends[q][i]
    items = [
        tuple(q_s[q, pl.ds(s, lines, stride=SUBLANES), :] for q in range(2)) for s in range(SUBLANES)
    ]
    for offset, count in node_offsets(SUBLANES):
        joined = []
        for n in range(count):
            ties = tuple(links[offset + n, i] for i in range(3))
            both, flux = join_targets(items[2 * n], items[2 * n + 1], ties)
            own[offset + n] = flux
            joined.append(both)
        items = joined
    for n, q in enumerate(COEFS):
        send[q] = view[n]
    send[FIRST], send[LAST] = items[0]


def x_target(t, c, total, near, far, w, inv, p, links, view):
    chunks, sheets, rows, _ = t.shape
    lines = chunks * sheets
    steps = rows // SUBLANES
    return pl.pallas_call(
        x_target_kernel,
        out_shape=[
            shape_of(steps, lines, SUBLANES, LANES),
            shape_of(SUBLANES - 1, lines, LANES),
            shape_of(7, lines, LANES),
        ],
        scratch_shapes=[
            pltpu.VMEM((2, sheets, rows, LANES), F32),
            pltpu.VMEM((2, lines * SUBLANES, LANES), F32),
        ],
        compiler_params=params(),
    )(t, c, total, near, far, w, inv, p, links, view)


def stages_of(axis):
    return lax.axis_size(axis).bit_length() - 1


def swap(value, axis, stage):
    count = lax.axis_size(axis)
    return lax.ppermute(value, axis, [(i, i ^ (1 << stage)) for i in range(count)])


def on_right(axis, stage):
    return (lax.axis_index(axis) >> stage) % 2 == 1


def toward(right, block):
    return (
        jnp.where(right, block[R00], block[RLL]),
        jnp.where(right, block[FIRST], block[LAST]),
        jnp.where(right, block[C0], block[CL]),
    )


def join_kernel(axis, stage, last, own, got, *refs):
    send, links = refs[-2:]
    right = on_right(axis, stage)
    a = {q: jnp.where(right, got[q], own[q]) for q in range(7)}
    b = {q: jnp.where(right, own[q], got[q]) for q in range(7)}
    joined, ties = join_coefs(a, b)
    (joined[FIRST], joined[LAST]), flux = join_targets((a[FIRST], a[LAST]), (b[FIRST], b[LAST]), ties)
    links[0], links[1], links[2] = flux, ties[1], ties[2]
    if last:
        for n, value in enumerate(toward(on_right(axis, stage + 1), joined)):
            send[n] = value
    else:
        for q in range(7):
            send[q] = joined[q]


def join_stage(own, got, axis, stage, last, after):
    lines = own.shape[1]
    return pl.pallas_call(
        functools.partial(join_kernel, axis, stage, last),
        in_specs=[IN_VMEM] * 2 + [ANYWHERE] * len(after),
        out_shape=[shape_of(3 if last else 7, lines, LANES), shape_of(3, lines, LANES)],
        compiler_params=params(),
    )(own, got, *after)


def gather_line(view, axis, meanwhile=()):
    stages = stages_of(axis)
    links = []
    for stage in range(stages - 1):
        got = swap(view, axis, stage)
        view, tie = join_stage(view, got, axis, stage, stage == stages - 2, meanwhile[stage : stage + 1])
        links.append(tie)
    return view, swap(view, axis, stages - 1), links


def block_ends(axis, own, got, links):
    top = len(links)
    right = on_right(axis, top)
    face = own[2] + got[2]
    jump = jnp.where(right, own[1] - got[1], got[1] - own[1])
    flux = jump * face * inverse(1.0 + face * (own[0] + got[0]))
    low = jnp.where(right, -flux, 0.0)
    high = jnp.where(right, 0.0, flux)
    for stage in range(top - 1, -1, -1):
        tie = links[stage]
        right = on_right(axis, stage)
        flux = between(tie[0], tie[1], tie[2], low, high)
        low, high = jnp.where(right, -flux, low), jnp.where(right, high, flux)
    return low, high


def y_factor_kernel(c_ref, after, w_ref, i_ref, p_ref, inner, outer, view, c_s, q_s):
    chunks, sheets, rows, _ = c_ref.shape
    each = LANES // rows
    pairs = sheets // each
    span = chunks * LANES // SUBLANES
    steps = span // Y_PARTS
    for m in range(pairs):
        for y in range(chunks):
            block = jnp.concatenate([c_ref[y, m * each + i] for i in range(each)], 0)
            c_s[m, y * LANES : (y + 1) * LANES, :] = block.T

    members = [(j, m) for j in range(Y_PARTS) for m in range(pairs)]

    def cond(k):
        return jnp.stack([c_s[m, pl.ds(j * steps + k, SUBLANES, stride=span), :] for j, m in members], 0)

    def keep(k, w, inv, p):
        w_ref[k] = w
        i_ref[k] = inv
        p_ref[k] = p

    block = factor(cond, steps, keep)
    parts = [{q: block[q][j * pairs : (j + 1) * pairs] for q in COEFS} for j in range(Y_PARTS)]
    whole, levels = tree(parts, join_coefs)
    for (offset, _), level in zip(node_offsets(Y_PARTS), levels):
        for n, values in enumerate(level):
            for i in range(3):
                inner[offset + n, i] = values[i]
    for n, q in enumerate(COEFS):
        for m in range(pairs):
            q_s[n, m * SUBLANES : (m + 1) * SUBLANES, :] = whole[q][m]
    segments = [
        {q: q_s[n, pl.ds(s, pairs, stride=SUBLANES), :] for n, q in enumerate(COEFS)}
        for s in range(SUBLANES)
    ]
    whole, levels = tree(segments, join_coefs)
    for (offset, _), level in zip(node_offsets(SUBLANES), levels):
        for n, values in enumerate(level):
            for i in range(3):
                outer[offset + n, i] = values[i]
    for n, q in enumerate(COEFS):
        view[n] = whole[q]


def y_factor(c, after):
    chunks, sheets, rows, _ = c.shape
    pairs = sheets * rows // LANES
    steps = chunks * LANES // SUBLANES // Y_PARTS
    stored = shape_of(steps, Y_PARTS * pairs, SUBLANES, LANES)
    return pl.pallas_call(
        y_factor_kernel,
        in_specs=[IN_VMEM, ANYWHERE],
        out_shape=[
            stored,
            stored,
            stored,
            shape_of(Y_PARTS - 1, 3, pairs, SUBLANES, LANES),
            shape_of(SUBLANES - 1, 3, pairs, LANES),
            shape_of(len(COEFS), pairs, LANES),
        ],
        scratch_shapes=[
            pltpu.VMEM((pairs, chunks * LANES, LANES), F32),
            pltpu.VMEM((len(COEFS), pairs * SUBLANES, LANES), F32),
        ],
        compiler_params=params(),
        cost_estimate=pl.CostEstimate(flops=20 * c.size, bytes_accessed=16 * c.size, transcendentals=0),
    )(c, after)


def z_factor_kernel(c_ref, after, w_ref, i_ref):
    sheets = c_ref.shape[1]
    ground = 1.0
    for z in range(sheets - 1):
        face = c_ref[:, z] + c_ref[:, z + 1]
        inv = inverse(ground + face)
        w = face * inv
        i_ref[z] = inv
        w_ref[z] = w
        ground = 1.0 + w * ground
    i_ref[sheets - 1] = inverse(ground)


def z_factor(c, after):
    chunks, sheets, rows, _ = c.shape
    return pl.pallas_call(
        z_factor_kernel,
        in_specs=[IN_VMEM, ANYWHERE],
        out_shape=[
            shape_of(sheets - 1, chunks, rows, LANES),
            shape_of(sheets, chunks, rows, LANES),
        ],
        compiler_params=params(),
        cost_estimate=pl.CostEstimate(flops=10 * c.size, bytes_accessed=12 * c.size, transcendentals=0),
    )(c, after)


def y_target_kernel(stages, *refs):
    own, got = refs[:2]
    ties = refs[2 : 1 + stages]
    xw, xh, xp, x_links, x_own, t_ref, yw, yi, yp, inner, outer, view = refs[1 + stages : 13 + stages]
    h_ref, inner_own, outer_own, send = refs[13 + stages : 17 + stages]
    f_s, g_s, y_s, q_s = refs[17 + stages :]
    chunks, sheets, rows, _ = t_ref.shape
    lines = chunks * sheets
    x_steps = rows // SUBLANES

    low, high = block_ends("gx", own, got, ties)
    levels = [
        [(x_own[o + n], x_links[o + n, 1], x_links[o + n, 2]) for n in range(count)]
        for o, count in node_offsets(SUBLANES)
    ]
    for s, ends in enumerate(descend(levels, low, high)):
        for i in range(2):
            f_s[i, pl.ds(s, lines, stride=SUBLANES), :] = ends[i]
    group = max(1, 8 // sheets)
    for y in range(0, chunks, group):
        members = [(y + i, z) for i in range(group) for z in range(sheets)]
        at = slice(y * sheets, (y + group) * sheets)
        low, value = (
            jnp.stack(
                [
                    f_s[i, (y * sheets + n) * SUBLANES : (y * sheets + n + 1) * SUBLANES, :]
                    for n in range(len(members))
                ],
                0,
            )
            for i in range(2)
        )
        for k in range(x_steps - 1, -1, -1):
            value = xw[k, at] * value + (xh[k, at] + xp[k, at] * low)
            for n, (i, z) in enumerate(members):
                g_s[i, z, pl.ds(k, SUBLANES, stride=x_steps), :] = value[n]

    each = LANES // rows
    pairs = sheets // each
    span = chunks * LANES // SUBLANES
    steps = span // Y_PARTS
    for m in range(pairs):
        for y in range(chunks):
            block = jnp.concatenate(
                [g_s[y, m * each + i] - t_ref[y, m * each + i] for i in range(each)], 0
            )
            y_s[m, y * LANES : (y + 1) * LANES, :] = block.T
    members = [(j, m) for j in range(Y_PARTS) for m in range(pairs)]

    def target(k):
        return jnp.stack([y_s[m, pl.ds(j * steps + k, SUBLANES, stride=span), :] for j, m in members], 0)

    def keep(k, h):
        h_ref[k] = h

    ends = eliminate(target, steps, lambda k: yw[k], lambda k: yi[k], lambda k: yp[k], keep)
    items = [tuple(v[j * pairs : (j + 1) * pairs] for v in ends) for j in range(Y_PARTS)]
    for offset, count in node_offsets(Y_PARTS):
        joined = []
        for n in range(count):
            tie = tuple(inner[offset + n, i] for i in range(3))
            both, flux = join_targets(items[2 * n], items[2 * n + 1], tie)
            inner_own[offset + n] = flux
            joined.append(both)
        items = joined
    for q in range(2):
        for m in range(pairs):
            q_s[q, m * SUBLANES : (m + 1) * SUBLANES, :] = items[0][q][m]
    items = [
        tuple(q_s[q, pl.ds(s, pairs, stride=SUBLANES), :] for q in range(2)) for s in range(SUBLANES)
    ]
    for offset, count in node_offsets(SUBLANES):
        joined = []
        for n in range(count):
            tie = tuple(outer[offset + n, i] for i in range(3))
            both, flux = join_targets(items[2 * n], items[2 * n + 1], tie)
            outer_own[offset + n] = flux
            joined.append(both)
        items = joined
    for n, q in enumerate(COEFS):
        send[q] = view[n]
    send[FIRST], send[LAST] = items[0]


def y_target(own, got, ties, xw, xh, xp, x_links, x_own, t, yw, yi, yp, inner, outer, view):
    chunks, sheets, rows, _ = t.shape
    lines = chunks * sheets
    pairs = sheets * rows // LANES
    return pl.pallas_call(
        functools.partial(y_target_kernel, len(ties) + 1),
        out_shape=[
            shape_of(*yw.shape),
            shape_of(Y_PARTS - 1, pairs, SUBLANES, LANES),
            shape_of(SUBLANES - 1, pairs, LANES),
            shape_of(7, pairs, LANES),
        ],
        scratch_shapes=[
            pltpu.VMEM((2, lines * SUBLANES, LANES), F32),
            pltpu.VMEM((chunks, sheets, rows, LANES), F32),
            pltpu.VMEM((pairs, chunks * LANES, LANES), F32),
            pltpu.VMEM((2, pairs * SUBLANES, LANES), F32),
        ],
        compiler_params=params(),
    )(own, got, *ties, xw, xh, xp, x_links, x_own, t, yw, yi, yp, inner, outer, view)


def finish_kernel(stages, *refs):
    own, got = refs[:2]
    ties = refs[2 : 1 + stages]
    yw, yh, yp, inner, inner_own, outer, outer_own, zw, zi, t_ref = refs[1 + stages : 11 + stages]
    out, e_s, u_s, o_s, sems = refs[11 + stages :]
    chunks, sheets, rows, _ = t_ref.shape
    each = LANES // rows
    pairs = sheets // each
    steps = yw.shape[0]
    span = chunks * LANES // SUBLANES

    low, high = block_ends("gy", own, got, ties)
    levels = [
        [(outer_own[o + n], outer[o + n, 1], outer[o + n, 2]) for n in range(count)]
        for o, count in node_offsets(SUBLANES)
    ]
    for s, ends in enumerate(descend(levels, low, high)):
        for i in range(2):
            e_s[i, pl.ds(s, pairs, stride=SUBLANES), :] = ends[i]
    low, high = (
        jnp.stack([e_s[i, m * SUBLANES : (m + 1) * SUBLANES, :] for m in range(pairs)], 0)
        for i in range(2)
    )
    levels = [
        [(inner_own[o + n], inner[o + n, 1], inner[o + n, 2]) for n in range(count)]
        for o, count in node_offsets(Y_PARTS)
    ]
    ends = descend(levels, low, high)
    low = jnp.concatenate([e[0] for e in ends], 0)
    value = jnp.concatenate([e[1] for e in ends], 0)
    members = [(j, m) for j in range(Y_PARTS) for m in range(pairs)]
    for k in range(steps - 1, -1, -1):
        value = yw[k] * value + (yh[k] + yp[k] * low)
        for n, (j, m) in enumerate(members):
            u_s[m, pl.ds(j * steps + k, SUBLANES, stride=span), :] = value[n]

    copies = []
    for y in range(chunks):
        part = slice(y * LANES, (y + 1) * LANES)
        turned = [u_s[m, part, :].T for m in range(pairs)]
        rhs, kept = None, []
        for z in range(sheets):
            first = (z % each) * rows
            own_rhs = turned[z // each][first : first + rows, :]
            rhs = own_rhs if z == 0 else own_rhs + zw[z - 1, y] * rhs
            kept.append(rhs * zi[z, y])
        value = kept[-1]
        o_s[y, sheets - 1] = t_ref[y, sheets - 1] + value
        for z in range(sheets - 2, -1, -1):
            value = zw[z, y] * value + kept[z]
            o_s[y, z] = t_ref[y, z] + value
        copy = pltpu.make_async_copy(o_s.at[y], out.at[:, :, pl.ds(y * LANES, LANES)], sems.at[y])
        copy.start()
        copies.append(copy)
    for copy in copies:
        copy.wait()


def finish(own, got, ties, yw, yh, yp, inner, inner_own, outer, outer_own, zw, zi, t):
    chunks, sheets, rows, _ = t.shape
    pairs = sheets * rows // LANES
    return pl.pallas_call(
        functools.partial(finish_kernel, len(ties) + 1),
        out_shape=shape_of(sheets, rows, chunks * LANES),
        out_specs=ANYWHERE,
        scratch_shapes=[
            pltpu.VMEM((2, pairs * SUBLANES, LANES), F32),
            pltpu.VMEM((pairs, chunks * LANES, LANES), F32),
            pltpu.VMEM(t.shape, F32),
            pltpu.SemaphoreType.DMA((chunks,)),
        ],
        compiler_params=params(),
    )(own, got, *ties, yw, yh, yp, inner, inner_own, outer, outer_own, zw, zi, t)


def per_device(temperature, base, locations, energy):
    columns = temperature.shape[2]
    gy = lax.axis_size("gy")
    t, b, loc, heat, near_edge, far_edge = load(temperature, base, locations[None], energy[None])
    near = lax.ppermute(near_edge, "gy", [(i, i ^ 1) for i in range(gy)])
    far = lax.ppermute(far_edge, "gy", [(i, (i + 1 ^ 1) - 1) for i in range(1, gy - 1)])
    c, total, xw, xi, xp, x_links, x_view = x_factor(loc, heat, t, b, columns * gy)
    xh, x_own, view = x_target(t, c, total, near, far, xw, xi, xp, x_links, x_view)
    yw, yi, yp, inner, outer, y_view = y_factor(c, view)
    zw, zi = z_factor(c, view)
    own, got, ties = gather_line(view, "gx", (y_view, zw))
    yh, inner_own, outer_own, view = y_target(
        own, got, ties, xw, xh, xp, x_links, x_own, t, yw, yi, yp, inner, outer, y_view
    )
    own, got, ties = gather_line(view, "gy")
    return finish(own, got, ties, yw, yh, yp, inner, inner_own, outer, outer_own, zw, zi, t)


def solution(mesh):
    in_specs = (P(None, "gx", "gy"), P(None, "gx", "gy"), P(), P())
    out_specs = P(None, "gx", "gy")
    return jax.shard_map(
        per_device, mesh=mesh, in_specs=in_specs, out_specs=out_specs, check_vma=False
    )
```

```python
import functools

import jax
import jax.numpy as jnp
from jax import lax
from jax.experimental import pallas as pl
from jax.experimental.pallas import tpu as pltpu
from jax.sharding import PartitionSpec as P

RATE = 2000.0
THERMAL_GROWTH = 0.8
LANES = 128
SUBLANES = 8
Y_PARTS = 4
F32 = jnp.float32
MIB = 1024 * 1024
ANYWHERE = pl.BlockSpec(memory_space=pl.ANY)
IN_HBM = pl.BlockSpec(memory_space=pltpu.HBM)
IN_VMEM = pl.BlockSpec(memory_space=pltpu.VMEM)

R00, R0L, RLL, FIRST, LAST, C0, CL = range(7)
COEFS = (R00, R0L, RLL, C0, CL)


def params(limit=40):
    return pltpu.CompilerParams(vmem_limit_bytes=limit * MIB)


def shape_of(*sizes):
    return jax.ShapeDtypeStruct(sizes, F32)


def half_conduct(base, temperature):
    return base * (0.5 * RATE + (0.5 * RATE * THERMAL_GROWTH) * temperature)


def inverse(x):
    guess = pl.reciprocal(x, approx=True)
    return guess * (2.0 - x * guess)


def join_coefs(a, b):
    face = a[CL] + b[C0]
    inv = face * inverse(1.0 + face * (a[RLL] + b[R00]))
    left = a[R0L] * inv
    right = b[R0L] * inv
    joined = {
        R00: a[R00] - left * a[R0L],
        R0L: left * b[R0L],
        RLL: b[RLL] - right * b[R0L],
        C0: a[C0],
        CL: b[CL],
    }
    return joined, (inv, right, left)


def join_targets(a, b, links):
    inv, right, left = links
    jump = b[0] - a[1]
    return (a[0] + left * jump, b[1] - right * jump), jump * inv


def between(own, right, left, low, high):
    return own + right * high - left * low


def tree(items, join):
    levels = []
    while len(items) > 1:
        pairs = [join(items[i], items[i + 1]) for i in range(0, len(items), 2)]
        items = [p[0] for p in pairs]
        levels.append([p[1] for p in pairs])
    return items[0], levels


def descend(levels, low, high):
    ends = [(low, high)]
    for level in reversed(levels):
        below = []
        for (lo, hi), (own, right, left) in zip(ends, level):
            flux = between(own, right, left, lo, hi)
            below += [(lo, flux), (-flux, hi)]
        ends = below
    return ends


def node_offsets(leaves):
    offsets, at, count = [], 0, leaves // 2
    while count:
        offsets.append((at, count))
        at += count
        count //= 2
    return offsets


def factor(cond, steps, keep):
    here = cond(0)
    c_first = here
    one = jnp.ones_like(here)
    ground, path, first_first = one, one, None
    for k in range(steps - 1):
        following = cond(k + 1)
        face = here + following
        inv = inverse(ground + face)
        w = face * inv
        p = path * inv
        keep(k, w, inv, p)
        step = path * p
        first_first = step if first_first is None else first_first + step
        path = path * w
        ground = 1.0 + w * ground
        here = following
    inv = inverse(ground)
    p = path * inv
    keep(steps - 1, inv, inv, p)
    return {R00: first_first + path * p, R0L: p, RLL: inv, C0: c_first, CL: here}


def eliminate(target, steps, w, inv, p, keep):
    rhs = target(0)
    first = None
    for k in range(steps):
        h = rhs * inv(k)
        keep(k, h)
        step = rhs * p(k)
        first = step if first is None else first + step
        if k < steps - 1:
            rhs = target(k + 1) + w(k) * rhs
    return first, h


def is_odd(axis):
    return lax.axis_index(axis) % 2 == 1


def edges_kernel(t_hbm, b_hbm, loc_hbm, energy_hbm, loc, energy, packed, t_s, b_s, sems):
    sheets, rows, columns = t_hbm.shape
    copies = [
        pltpu.make_async_copy(loc_hbm, loc, sems.at[2, 0]),
        pltpu.make_async_copy(energy_hbm, energy, sems.at[2, 1]),
    ]
    for side, start in enumerate((0, columns - LANES)):
        for i, (src, dst) in enumerate(((t_hbm, t_s), (b_hbm, b_s))):
            part = src.at[:, :, pl.ds(start, LANES)]
            copies.append(pltpu.make_async_copy(part, dst.at[side], sems.at[i, side]))
    for copy in copies:
        copy.start()
    for copy in copies:
        copy.wait()
    lane = lax.broadcasted_iota(jnp.int32, (rows, LANES), 1)
    total = jnp.zeros((rows, LANES), F32)
    for side, source in enumerate((0, LANES - 1)):
        for z in range(sheets):
            t = t_s[side, z]
            c = half_conduct(b_s[side, z], t)
            place = 2 * sheets * side + z
            total = jnp.where(lane == place, t[:, source : source + 1], total)
            total = jnp.where(lane == place + sheets, c[:, source : source + 1], total)
    packed[...] = total


def edges(temperature, base, locations, energy):
    sheets, rows, _ = temperature.shape
    operands = (temperature, base, locations, energy)
    return pl.pallas_call(
        edges_kernel,
        in_specs=[IN_HBM] * 4,
        out_shape=[
            pltpu.VMEM(locations.shape, jnp.int32),
            pltpu.VMEM(energy.shape, F32),
            pltpu.VMEM((rows, LANES), F32),
        ],
        scratch_shapes=[
            pltpu.VMEM((2, sheets, rows, LANES), F32),
            pltpu.VMEM((2, sheets, rows, LANES), F32),
            pltpu.SemaphoreType.DMA((3, 2)),
        ],
        compiler_params=params(),
    )(*[pltpu.with_memory_space_constraint(v, pltpu.HBM) for v in operands])


def source_plane(loc, energy, rows, columns, plate):
    place = loc[...]
    count = place.shape[1]
    local_x = place // plate - lax.axis_index("gx") * rows
    local_y = place % plate - lax.axis_index("gy") * columns
    in_x = lax.broadcasted_iota(jnp.int32, (rows, count), 0) == local_x
    in_y = lax.broadcasted_iota(jnp.int32, (columns, count), 0) == local_y
    by_y = jnp.where(in_y, 1.0, 0.0).astype(jnp.bfloat16)
    left = energy[...]
    plane = None
    for _ in range(3):
        part = left.astype(jnp.bfloat16).astype(F32)
        left = left - part
        term = lax.dot_general(
            jnp.where(in_x, part, 0.0).astype(jnp.bfloat16),
            by_y,
            (((1,), (1,)), ((), ())),
            preferred_element_type=F32,
        )
        plane = term if plane is None else plane + term
    return plane


def part_of(y):
    return slice(y * LANES, (y + 1) * LANES)


def x_factor_kernel(plate, loc, energy, t_ref, b_ref, after, *refs):
    c_ref, total_ref, w_ref, i_ref, p_ref, links, view, q_s = refs
    chunks, sheets, rows, _ = c_ref.shape
    lines = chunks * sheets
    steps = rows // SUBLANES
    plane = source_plane(loc, energy, rows, chunks * LANES, plate)

    lane = lax.broadcasted_iota(jnp.int32, (SUBLANES, LANES), 1)
    is_first, is_last = lane == 0, lane == LANES - 1
    for r in range(steps):
        at = slice(r * SUBLANES, (r + 1) * SUBLANES)
        before_t, before_c = None, None
        for z in range(sheets):
            ts = [t_ref[z, at, part_of(y)] for y in range(chunks)]
            cs = [half_conduct(b_ref[z, at, part_of(y)], ts[y]) for y in range(chunks)]
            t_turned = [pltpu.roll(v, LANES - 1, 1) for v in ts]
            c_turned = [pltpu.roll(v, LANES - 1, 1) for v in cs]
            flux = []
            for y in range(chunks):
                if y < chunks - 1:
                    t_next = jnp.where(is_last, t_turned[y + 1], t_turned[y])
                    c_next = jnp.where(is_last, c_turned[y + 1], c_turned[y])
                    flux.append((cs[y] + c_next) * (t_next - ts[y]))
                else:
                    inside = (cs[y] + c_turned[y]) * (t_turned[y] - ts[y])
                    flux.append(jnp.where(is_last, 0.0, inside))
            turned = [pltpu.roll(v, 1, 1) for v in flux]
            for y in range(chunks):
                from_low = jnp.where(is_first, turned[y - 1] if y else 0.0, turned[y])
                total = ts[y] + (flux[y] - from_low)
                if z == 0:
                    total = total + plane[at, part_of(y)]
                else:
                    across = (before_c[y] + cs[y]) * (ts[y] - before_t[y])
                    total = total - across
                    total_ref[y, z - 1, at, :] += across
                total_ref[y, z, at, :] = total
                c_ref[y, z, at, :] = cs[y]
            before_t, before_c = ts, cs

    group = max(1, 8 // sheets)
    for y in range(0, chunks, group):
        members = [(y + i, z) for i in range(group) for z in range(sheets)]
        at = slice(y * sheets, (y + group) * sheets)

        def cond(k):
            return jnp.stack([c_ref[i, z, pl.ds(k, SUBLANES, stride=steps), :] for i, z in members], 0)

        def keep(k, w, inv, p):
            w_ref[k, at] = w
            i_ref[k, at] = inv
            p_ref[k, at] = p

        block = factor(cond, steps, keep)
        for n, q in enumerate(COEFS):
            for i in range(len(members)):
                first = (y * sheets + i) * SUBLANES
                q_s[n, first : first + SUBLANES, :] = block[q][i]

    segments = [
        {q: q_s[n, pl.ds(s, lines, stride=SUBLANES), :] for n, q in enumerate(COEFS)}
        for s in range(SUBLANES)
    ]
    whole, levels = tree(segments, join_coefs)
    for (offset, _), level in zip(node_offsets(SUBLANES), levels):
        for n, values in enumerate(level):
            for i in range(3):
                links[offset + n, i] = values[i]
    for n, q in enumerate(COEFS):
        view[n] = whole[q]


def x_factor(loc, energy, t, b, plate, after):
    sheets, rows, columns = t.shape
    chunks = columns // LANES
    lines = chunks * sheets
    steps = rows // SUBLANES
    field = shape_of(chunks, sheets, rows, LANES)
    stored = shape_of(steps, lines, SUBLANES, LANES)
    return pl.pallas_call(
        functools.partial(x_factor_kernel, plate),
        in_specs=[IN_VMEM] * 4 + [ANYWHERE],
        out_shape=[
            field,
            field,
            stored,
            stored,
            stored,
            shape_of(SUBLANES - 1, 3, lines, LANES),
            shape_of(len(COEFS), lines, LANES),
        ],
        scratch_shapes=[pltpu.VMEM((len(COEFS), lines * SUBLANES, LANES), F32)],
        compiler_params=params(),
        cost_estimate=pl.CostEstimate(flops=40 * t.size, bytes_accessed=28 * t.size, transcendentals=0),
    )(loc, energy, t, b, after)


def x_target_kernel(t_ref, c_ref, total_ref, near, far, w_ref, i_ref, p_ref, links, view, h_ref, own, send, e_s, q_s):
    chunks, sheets, rows, _ = c_ref.shape
    lines = chunks * sheets
    steps = rows // SUBLANES

    before = jnp.where(is_odd("gy"), near[...], far[...])
    after = jnp.where(is_odd("gy"), far[...], near[...])
    lane = lax.broadcasted_iota(jnp.int32, (rows, LANES), 1)
    for y, halo, edge, place in ((0, before, 0, 0), (chunks - 1, after, LANES - 1, 1)):
        for z in range(sheets):
            at = z if place else 2 * sheets + z
            t_next = halo[:, at : at + 1]
            c_next = halo[:, at + sheets : at + sheets + 1]
            face = jnp.where(c_next > 0.0, c_ref[y, z] + c_next, 0.0)
            flux = jnp.where(lane == edge, face * (t_next - t_ref[z, :, part_of(y)]), 0.0)
            base = total_ref[y, z] if place == 0 or chunks > 1 else e_s[0, z]
            e_s[place, z] = base + flux

    def field(y, z):
        if y == chunks - 1:
            return e_s.at[1, z]
        return e_s.at[0, z] if y == 0 else total_ref.at[y, z]

    group = max(1, 8 // sheets)
    for y in range(0, chunks, group):
        members = [(y + i, z) for i in range(group) for z in range(sheets)]
        at = slice(y * sheets, (y + group) * sheets)

        def target(k):
            return jnp.stack([field(i, z)[pl.ds(k, SUBLANES, stride=steps), :] for i, z in members], 0)

        def keep(k, h):
            h_ref[k, at] = h

        ends = eliminate(
            target, steps, lambda k: w_ref[k, at], lambda k: i_ref[k, at], lambda k: p_ref[k, at], keep
        )
        for q in range(2):
            for i in range(len(members)):
                first = (y * sheets + i) * SUBLANES
                q_s[q, first : first + SUBLANES, :] = ends[q][i]
    items = [
        tuple(q_s[q, pl.ds(s, lines, stride=SUBLANES), :] for q in range(2)) for s in range(SUBLANES)
    ]
    for offset, count in node_offsets(SUBLANES):
        joined = []
        for n in range(count):
            ties = tuple(links[offset + n, i] for i in range(3))
            both, flux = join_targets(items[2 * n], items[2 * n + 1], ties)
            own[offset + n] = flux
            joined.append(both)
        items = joined
    for n, q in enumerate(COEFS):
        send[q] = view[n]
    send[FIRST], send[LAST] = items[0]


def x_target(t, c, total, near, far, w, inv, p, links, view):
    chunks, sheets, rows, _ = c.shape
    lines = chunks * sheets
    steps = rows // SUBLANES
    return pl.pallas_call(
        x_target_kernel,
        out_shape=[
            shape_of(steps, lines, SUBLANES, LANES),
            shape_of(SUBLANES - 1, lines, LANES),
            shape_of(7, lines, LANES),
        ],
        scratch_shapes=[
            pltpu.VMEM((2, sheets, rows, LANES), F32),
            pltpu.VMEM((2, lines * SUBLANES, LANES), F32),
        ],
        compiler_params=params(),
    )(t, c, total, near, far, w, inv, p, links, view)


def stages_of(axis):
    return lax.axis_size(axis).bit_length() - 1


def swap(value, axis, flip):
    count = lax.axis_size(axis)
    return lax.ppermute(value, axis, [(i, i ^ flip) for i in range(count)])


def on_right(axis, stage):
    return (lax.axis_index(axis) >> stage) % 2 == 1


def toward(right, block):
    return (
        jnp.where(right, block[R00], block[RLL]),
        jnp.where(right, block[FIRST], block[LAST]),
        jnp.where(right, block[C0], block[CL]),
    )


def join(a, b):
    joined, ties = join_coefs(a, b)
    (joined[FIRST], joined[LAST]), flux = join_targets((a[FIRST], a[LAST]), (b[FIRST], b[LAST]), ties)
    return joined, (flux, ties[1], ties[2])


def ordered(right, own, other):
    first = [jnp.where(right, theirs, mine) for mine, theirs in zip(own, other)]
    second = [jnp.where(right, mine, theirs) for mine, theirs in zip(own, other)]
    return first, second


def join_kernel(axis, stage, width, last, *refs):
    blocks = [[refs[i][q] for q in range(7)] for i in range(1 << width)]
    send = refs[-1 - width]
    links = refs[-width:]
    for bit in range(width):
        right = on_right(axis, stage + bit)
        for i in range(1 << width):
            if not i >> bit & 1:
                j = i | 1 << bit
                blocks[i], blocks[j] = ordered(right, blocks[i], blocks[j])
    for bit in range(width):
        pairs = [join(blocks[i], blocks[i + 1]) for i in range(0, len(blocks), 2)]
        blocks = [p[0] for p in pairs]
        ties = [p[1] for p in pairs]
        for upper in range(bit + 1, width):
            right = on_right(axis, stage + upper)
            ties = [
                tuple(jnp.where(right, v, u) for u, v in zip(ties[i], ties[i + 1]))
                for i in range(0, len(ties), 2)
            ]
        for i in range(3):
            links[bit][i] = ties[0][i]
    (whole,) = blocks
    if last:
        for n, value in enumerate(toward(on_right(axis, stage + width), whole)):
            send[n] = value
    else:
        for q in range(7):
            send[q] = whole[q]


def join_stage(own, got, axis, stage, width, last, after):
    lines = own.shape[1]
    return pl.pallas_call(
        functools.partial(join_kernel, axis, stage, width, last),
        in_specs=[IN_VMEM] * (1 + len(got)) + [ANYWHERE] * len(after),
        out_shape=[shape_of(3 if last else 7, lines, LANES)] + [shape_of(3, lines, LANES)] * width,
        compiler_params=params(),
    )(own, *got, *after)


def gather_line(view, axis, widest=1, meanwhile=()):
    stages = stages_of(axis)
    links, stage = [], 0
    while stage < stages - 1:
        width = min(widest, stages - 1 - stage)
        got = [swap(view, axis, flip << stage) for flip in range(1, 1 << width)]
        last = stage + width == stages - 1
        view, *ties = join_stage(view, got, axis, stage, width, last, meanwhile)
        links += ties
        stage += width
        meanwhile = ()
    return view, swap(view, axis, 1 << stage), links


def block_ends(axis, own, got, links):
    top = len(links)
    right = on_right(axis, top)
    face = own[2] + got[2]
    jump = jnp.where(right, own[1] - got[1], got[1] - own[1])
    flux = jump * face * inverse(1.0 + face * (own[0] + got[0]))
    low = jnp.where(right, -flux, 0.0)
    high = jnp.where(right, 0.0, flux)
    for stage in range(top - 1, -1, -1):
        tie = links[stage]
        right = on_right(axis, stage)
        flux = between(tie[0], tie[1], tie[2], low, high)
        low, high = jnp.where(right, -flux, low), jnp.where(right, high, flux)
    return low, high


def y_factor_kernel(c_ref, after, w_ref, i_ref, p_ref, inner, outer, view, c_s, q_s):
    chunks, sheets, rows, _ = c_ref.shape
    each = LANES // rows
    pairs = sheets // each
    span = chunks * LANES // SUBLANES
    steps = span // Y_PARTS
    for m in range(pairs):
        for y in range(chunks):
            block = jnp.concatenate([c_ref[y, m * each + i] for i in range(each)], 0)
            c_s[m, y * LANES : (y + 1) * LANES, :] = block.T

    members = [(j, m) for j in range(Y_PARTS) for m in range(pairs)]

    def cond(k):
        return jnp.stack([c_s[m, pl.ds(j * steps + k, SUBLANES, stride=span), :] for j, m in members], 0)

    def keep(k, w, inv, p):
        w_ref[k] = w
        i_ref[k] = inv
        p_ref[k] = p

    block = factor(cond, steps, keep)
    parts = [{q: block[q][j * pairs : (j + 1) * pairs] for q in COEFS} for j in range(Y_PARTS)]
    whole, levels = tree(parts, join_coefs)
    for (offset, _), level in zip(node_offsets(Y_PARTS), levels):
        for n, values in enumerate(level):
            for i in range(3):
                inner[offset + n, i] = values[i]
    for n, q in enumerate(COEFS):
        for m in range(pairs):
            q_s[n, m * SUBLANES : (m + 1) * SUBLANES, :] = whole[q][m]
    segments = [
        {q: q_s[n, pl.ds(s, pairs, stride=SUBLANES), :] for n, q in enumerate(COEFS)}
        for s in range(SUBLANES)
    ]
    whole, levels = tree(segments, join_coefs)
    for (offset, _), level in zip(node_offsets(SUBLANES), levels):
        for n, values in enumerate(level):
            for i in range(3):
                outer[offset + n, i] = values[i]
    for n, q in enumerate(COEFS):
        view[n] = whole[q]


def y_factor(c, after):
    chunks, sheets, rows, _ = c.shape
    pairs = sheets * rows // LANES
    steps = chunks * LANES // SUBLANES // Y_PARTS
    stored = shape_of(steps, Y_PARTS * pairs, SUBLANES, LANES)
    return pl.pallas_call(
        y_factor_kernel,
        in_specs=[IN_VMEM, ANYWHERE],
        out_shape=[
            stored,
            stored,
            stored,
            shape_of(Y_PARTS - 1, 3, pairs, SUBLANES, LANES),
            shape_of(SUBLANES - 1, 3, pairs, LANES),
            shape_of(len(COEFS), pairs, LANES),
        ],
        scratch_shapes=[
            pltpu.VMEM((pairs, chunks * LANES, LANES), F32),
            pltpu.VMEM((len(COEFS), pairs * SUBLANES, LANES), F32),
        ],
        compiler_params=params(),
        cost_estimate=pl.CostEstimate(flops=20 * c.size, bytes_accessed=16 * c.size, transcendentals=0),
    )(c, after)


def z_factor_kernel(c_ref, after, w_ref, i_ref):
    sheets = c_ref.shape[1]
    ground = 1.0
    for z in range(sheets - 1):
        face = c_ref[:, z] + c_ref[:, z + 1]
        inv = inverse(ground + face)
        w = face * inv
        i_ref[z] = inv
        w_ref[z] = w
        ground = 1.0 + w * ground
    i_ref[sheets - 1] = inverse(ground)


def z_factor(c, after):
    chunks, sheets, rows, _ = c.shape
    return pl.pallas_call(
        z_factor_kernel,
        in_specs=[IN_VMEM, ANYWHERE],
        out_shape=[
            shape_of(sheets - 1, chunks, rows, LANES),
            shape_of(sheets, chunks, rows, LANES),
        ],
        compiler_params=params(),
        cost_estimate=pl.CostEstimate(flops=10 * c.size, bytes_accessed=12 * c.size, transcendentals=0),
    )(c, after)


def y_target_kernel(stages, *refs):
    own, got = refs[:2]
    ties = refs[2 : 1 + stages]
    xw, xh, xp, x_links, x_own, t_ref, yw, yi, yp, inner, outer, view = refs[1 + stages : 13 + stages]
    h_ref, inner_own, outer_own, send = refs[13 + stages : 17 + stages]
    f_s, g_s, y_s, q_s = refs[17 + stages :]
    chunks, sheets, rows, _ = g_s.shape
    lines = chunks * sheets
    x_steps = rows // SUBLANES

    low, high = block_ends("gx", own, got, ties)
    levels = [
        [(x_own[o + n], x_links[o + n, 1], x_links[o + n, 2]) for n in range(count)]
        for o, count in node_offsets(SUBLANES)
    ]
    for s, ends in enumerate(descend(levels, low, high)):
        for i in range(2):
            f_s[i, pl.ds(s, lines, stride=SUBLANES), :] = ends[i]
    group = max(1, 8 // sheets)
    for y in range(0, chunks, group):
        members = [(y + i, z) for i in range(group) for z in range(sheets)]
        at = slice(y * sheets, (y + group) * sheets)
        low, value = (
            jnp.stack(
                [
                    f_s[i, (y * sheets + n) * SUBLANES : (y * sheets + n + 1) * SUBLANES, :]
                    for n in range(len(members))
                ],
                0,
            )
            for i in range(2)
        )
        for k in range(x_steps - 1, -1, -1):
            value = xw[k, at] * value + (xh[k, at] + xp[k, at] * low)
            for n, (i, z) in enumerate(members):
                g_s[i, z, pl.ds(k, SUBLANES, stride=x_steps), :] = value[n]

    each = LANES // rows
    pairs = sheets // each
    span = chunks * LANES // SUBLANES
    steps = span // Y_PARTS
    for m in range(pairs):
        for y in range(chunks):
            block = jnp.concatenate(
                [g_s[y, m * each + i] - t_ref[m * each + i, :, part_of(y)] for i in range(each)], 0
            )
            y_s[m, y * LANES : (y + 1) * LANES, :] = block.T
    members = [(j, m) for j in range(Y_PARTS) for m in range(pairs)]

    def target(k):
        return jnp.stack([y_s[m, pl.ds(j * steps + k, SUBLANES, stride=span), :] for j, m in members], 0)

    def keep(k, h):
        h_ref[k] = h

    ends = eliminate(target, steps, lambda k: yw[k], lambda k: yi[k], lambda k: yp[k], keep)
    items = [tuple(v[j * pairs : (j + 1) * pairs] for v in ends) for j in range(Y_PARTS)]
    for offset, count in node_offsets(Y_PARTS):
        joined = []
        for n in range(count):
            tie = tuple(inner[offset + n, i] for i in range(3))
            both, flux = join_targets(items[2 * n], items[2 * n + 1], tie)
            inner_own[offset + n] = flux
            joined.append(both)
        items = joined
    for q in range(2):
        for m in range(pairs):
            q_s[q, m * SUBLANES : (m + 1) * SUBLANES, :] = items[0][q][m]
    items = [
        tuple(q_s[q, pl.ds(s, pairs, stride=SUBLANES), :] for q in range(2)) for s in range(SUBLANES)
    ]
    for offset, count in node_offsets(SUBLANES):
        joined = []
        for n in range(count):
            tie = tuple(outer[offset + n, i] for i in range(3))
            both, flux = join_targets(items[2 * n], items[2 * n + 1], tie)
            outer_own[offset + n] = flux
            joined.append(both)
        items = joined
    for n, q in enumerate(COEFS):
        send[q] = view[n]
    send[FIRST], send[LAST] = items[0]


def y_target(own, got, ties, xw, xh, xp, x_links, x_own, t, yw, yi, yp, inner, outer, view):
    sheets, rows, columns = t.shape
    chunks = columns // LANES
    lines = chunks * sheets
    pairs = sheets * rows // LANES
    return pl.pallas_call(
        functools.partial(y_target_kernel, len(ties) + 1),
        out_shape=[
            shape_of(*yw.shape),
            shape_of(Y_PARTS - 1, pairs, SUBLANES, LANES),
            shape_of(SUBLANES - 1, pairs, LANES),
            shape_of(7, pairs, LANES),
        ],
        scratch_shapes=[
            pltpu.VMEM((2, lines * SUBLANES, LANES), F32),
            pltpu.VMEM((chunks, sheets, rows, LANES), F32),
            pltpu.VMEM((pairs, chunks * LANES, LANES), F32),
            pltpu.VMEM((2, pairs * SUBLANES, LANES), F32),
        ],
        compiler_params=params(),
    )(own, got, *ties, xw, xh, xp, x_links, x_own, t, yw, yi, yp, inner, outer, view)


def finish_kernel(stages, *refs):
    own, got = refs[:2]
    ties = refs[2 : 1 + stages]
    yw, yh, yp, inner, inner_own, outer, outer_own, zw, zi, t_ref = refs[1 + stages : 11 + stages]
    out, e_s, u_s, o_s, sems = refs[11 + stages :]
    chunks, sheets, rows, _ = o_s.shape
    each = LANES // rows
    pairs = sheets // each
    steps = yw.shape[0]
    span = chunks * LANES // SUBLANES

    low, high = block_ends("gy", own, got, ties)
    levels = [
        [(outer_own[o + n], outer[o + n, 1], outer[o + n, 2]) for n in range(count)]
        for o, count in node_offsets(SUBLANES)
    ]
    for s, ends in enumerate(descend(levels, low, high)):
        for i in range(2):
            e_s[i, pl.ds(s, pairs, stride=SUBLANES), :] = ends[i]
    low, high = (
        jnp.stack([e_s[i, m * SUBLANES : (m + 1) * SUBLANES, :] for m in range(pairs)], 0)
        for i in range(2)
    )
    levels = [
        [(inner_own[o + n], inner[o + n, 1], inner[o + n, 2]) for n in range(count)]
        for o, count in node_offsets(Y_PARTS)
    ]
    ends = descend(levels, low, high)
    low = jnp.concatenate([e[0] for e in ends], 0)
    value = jnp.concatenate([e[1] for e in ends], 0)
    members = [(j, m) for j in range(Y_PARTS) for m in range(pairs)]
    for k in range(steps - 1, -1, -1):
        value = yw[k] * value + (yh[k] + yp[k] * low)
        for n, (j, m) in enumerate(members):
            u_s[m, pl.ds(j * steps + k, SUBLANES, stride=span), :] = value[n]

    copies = []
    for y in range(chunks):
        part = part_of(y)
        turned = [u_s[m, part, :].T for m in range(pairs)]
        rhs, kept = None, []
        for z in range(sheets):
            first = (z % each) * rows
            own_rhs = turned[z // each][first : first + rows, :]
            rhs = own_rhs if z == 0 else own_rhs + zw[z - 1, y] * rhs
            kept.append(rhs * zi[z, y])
        value = kept[-1]
        o_s[y, sheets - 1] = t_ref[sheets - 1, :, part] + value
        for z in range(sheets - 2, -1, -1):
            value = zw[z, y] * value + kept[z]
            o_s[y, z] = t_ref[z, :, part] + value
        copy = pltpu.make_async_copy(o_s.at[y], out.at[:, :, pl.ds(y * LANES, LANES)], sems.at[y])
        copy.start()
        copies.append(copy)
    for copy in copies:
        copy.wait()


def finish(own, got, ties, yw, yh, yp, inner, inner_own, outer, outer_own, zw, zi, t):
    sheets, rows, columns = t.shape
    chunks = columns // LANES
    pairs = sheets * rows // LANES
    return pl.pallas_call(
        functools.partial(finish_kernel, len(ties) + 1),
        out_shape=shape_of(sheets, rows, chunks * LANES),
        out_specs=ANYWHERE,
        scratch_shapes=[
            pltpu.VMEM((2, pairs * SUBLANES, LANES), F32),
            pltpu.VMEM((pairs, chunks * LANES, LANES), F32),
            pltpu.VMEM((chunks, sheets, rows, LANES), F32),
            pltpu.SemaphoreType.DMA((chunks,)),
        ],
        compiler_params=params(),
    )(own, got, *ties, yw, yh, yp, inner, inner_own, outer, outer_own, zw, zi, t)


def per_device(temperature, base, locations, energy):
    columns = temperature.shape[2]
    gy = lax.axis_size("gy")
    loc, heat, packed = edges(temperature, base, locations[None], energy[None])
    near = swap(packed, "gy", 1)
    far = lax.ppermute(
        near, "gy", [(i, i + 2) for i in range(0, gy - 2, 2)] + [(i, i - 2) for i in range(3, gy, 2)]
    )
    t, b = (pltpu.with_memory_space_constraint(v, pltpu.VMEM) for v in (temperature, base))
    c, total, xw, xi, xp, x_links, x_view = x_factor(loc, heat, t, b, columns * gy, near)
    xh, x_own, view = x_target(t, c, total, near, far, xw, xi, xp, x_links, x_view)
    yw, yi, yp, inner, outer, y_view = y_factor(c, x_view)
    zw, zi = z_factor(c, view)
    own, got, ties = gather_line(view, "gx", 2, (y_view, zw))
    yh, inner_own, outer_own, view = y_target(
        own, got, ties, xw, xh, xp, x_links, x_own, t, yw, yi, yp, inner, outer, y_view
    )
    own, got, ties = gather_line(view, "gy")
    return finish(own, got, ties, yw, yh, yp, inner, inner_own, outer, outer_own, zw, zi, t)


def solution(mesh):
    in_specs = (P(None, "gx", "gy"), P(None, "gx", "gy"), P(), P())
    out_specs = P(None, "gx", "gy")
    return jax.shard_map(
        per_device, mesh=mesh, in_specs=in_specs, out_specs=out_specs, check_vma=False
    )
```

```python
import functools

import jax
import jax.numpy as jnp
from jax import lax
from jax.experimental import pallas as pl
from jax.experimental.pallas import tpu as pltpu
from jax.sharding import PartitionSpec as P

RATE = 2000.0
THERMAL_GROWTH = 0.8
LANES = 128
SUBLANES = 8
Y_PARTS = 4
F32 = jnp.float32
MIB = 1024 * 1024
ANYWHERE = pl.BlockSpec(memory_space=pl.ANY)
IN_HBM = pl.BlockSpec(memory_space=pltpu.HBM)
IN_VMEM = pl.BlockSpec(memory_space=pltpu.VMEM)

R00, R0L, RLL, FIRST, LAST, C0, CL = range(7)
COEFS = (R00, R0L, RLL, C0, CL)


def params(limit=40):
    return pltpu.CompilerParams(vmem_limit_bytes=limit * MIB)


def shape_of(*sizes):
    return jax.ShapeDtypeStruct(sizes, F32)


def half_conduct(base, temperature):
    return base * (0.5 * RATE + (0.5 * RATE * THERMAL_GROWTH) * temperature)


def inverse(x):
    guess = pl.reciprocal(x, approx=True)
    return guess * (2.0 - x * guess)


def join_coefs(a, b):
    face = a[CL] + b[C0]
    inv = face * inverse(1.0 + face * (a[RLL] + b[R00]))
    left = a[R0L] * inv
    right = b[R0L] * inv
    joined = {
        R00: a[R00] - left * a[R0L],
        R0L: left * b[R0L],
        RLL: b[RLL] - right * b[R0L],
        C0: a[C0],
        CL: b[CL],
    }
    return joined, (inv, right, left)


def join_targets(a, b, links):
    inv, right, left = links
    jump = b[0] - a[1]
    return (a[0] + left * jump, b[1] - right * jump), jump * inv


def between(own, right, left, low, high):
    return own + right * high - left * low


def tree(items, join):
    levels = []
    while len(items) > 1:
        pairs = [join(items[i], items[i + 1]) for i in range(0, len(items), 2)]
        items = [p[0] for p in pairs]
        levels.append([p[1] for p in pairs])
    return items[0], levels


def descend(levels, low, high):
    ends = [(low, high)]
    for level in reversed(levels):
        below = []
        for (lo, hi), (own, right, left) in zip(ends, level):
            flux = between(own, right, left, lo, hi)
            below += [(lo, flux), (-flux, hi)]
        ends = below
    return ends


def node_offsets(leaves):
    offsets, at, count = [], 0, leaves // 2
    while count:
        offsets.append((at, count))
        at += count
        count //= 2
    return offsets


def factor(cond, steps, keep):
    here = cond(0)
    c_first = here
    one = jnp.ones_like(here)
    ground, path, first_first = one, one, None
    for k in range(steps - 1):
        following = cond(k + 1)
        face = here + following
        inv = inverse(ground + face)
        w = face * inv
        p = path * inv
        keep(k, w, inv, p)
        step = path * p
        first_first = step if first_first is None else first_first + step
        path = path * w
        ground = 1.0 + w * ground
        here = following
    inv = inverse(ground)
    p = path * inv
    keep(steps - 1, inv, inv, p)
    return {R00: first_first + path * p, R0L: p, RLL: inv, C0: c_first, CL: here}


def eliminate(target, steps, w, inv, p, keep):
    rhs = target(0)
    first = None
    for k in range(steps):
        h = rhs * inv(k)
        keep(k, h)
        step = rhs * p(k)
        first = step if first is None else first + step
        if k < steps - 1:
            rhs = target(k + 1) + w(k) * rhs
    return first, h


def is_odd(axis):
    return lax.axis_index(axis) % 2 == 1


def edges_kernel(t_hbm, b_hbm, loc_hbm, energy_hbm, loc, energy, packed, t_s, b_s, sems):
    sheets, rows, columns = t_hbm.shape
    copies = [
        pltpu.make_async_copy(loc_hbm, loc, sems.at[2, 0]),
        pltpu.make_async_copy(energy_hbm, energy, sems.at[2, 1]),
    ]
    for side, start in enumerate((0, columns - LANES)):
        for i, (src, dst) in enumerate(((t_hbm, t_s), (b_hbm, b_s))):
            part = src.at[:, :, pl.ds(start, LANES)]
            copies.append(pltpu.make_async_copy(part, dst.at[side], sems.at[i, side]))
    for copy in copies:
        copy.start()
    for copy in copies:
        copy.wait()
    lane = lax.broadcasted_iota(jnp.int32, (rows, LANES), 1)
    total = jnp.zeros((rows, LANES), F32)
    for side, source in enumerate((0, LANES - 1)):
        for z in range(sheets):
            t = t_s[side, z]
            c = half_conduct(b_s[side, z], t)
            place = 2 * sheets * side + z
            total = jnp.where(lane == place, t[:, source : source + 1], total)
            total = jnp.where(lane == place + sheets, c[:, source : source + 1], total)
    packed[...] = total


def edges(temperature, base, locations, energy):
    sheets, rows, _ = temperature.shape
    operands = (temperature, base, locations, energy)
    return pl.pallas_call(
        edges_kernel,
        in_specs=[IN_HBM] * 4,
        out_shape=[
            pltpu.VMEM(locations.shape, jnp.int32),
            pltpu.VMEM(energy.shape, F32),
            pltpu.VMEM((rows, LANES), F32),
        ],
        scratch_shapes=[
            pltpu.VMEM((2, sheets, rows, LANES), F32),
            pltpu.VMEM((2, sheets, rows, LANES), F32),
            pltpu.SemaphoreType.DMA((3, 2)),
        ],
        compiler_params=params(),
    )(*[pltpu.with_memory_space_constraint(v, pltpu.HBM) for v in operands])


def source_plane(loc, energy, rows, columns, plate):
    place = loc[...]
    count = place.shape[1]
    local_x = place // plate - lax.axis_index("gx") * rows
    local_y = place % plate - lax.axis_index("gy") * columns
    in_x = lax.broadcasted_iota(jnp.int32, (rows, count), 0) == local_x
    in_y = lax.broadcasted_iota(jnp.int32, (columns, count), 0) == local_y
    by_y = jnp.where(in_y, 1.0, 0.0).astype(jnp.bfloat16)
    left = energy[...]
    plane = None
    for _ in range(3):
        part = left.astype(jnp.bfloat16).astype(F32)
        left = left - part
        term = lax.dot_general(
            jnp.where(in_x, part, 0.0).astype(jnp.bfloat16),
            by_y,
            (((1,), (1,)), ((), ())),
            preferred_element_type=F32,
        )
        plane = term if plane is None else plane + term
    return plane


def part_of(y):
    return slice(y * LANES, (y + 1) * LANES)


def x_factor_kernel(plate, loc, energy, t_ref, b_ref, after, *refs):
    c_ref, total_ref, w_ref, i_ref, p_ref, links, view, q_s = refs
    chunks, sheets, rows, _ = c_ref.shape
    lines = chunks * sheets
    steps = rows // SUBLANES
    plane = source_plane(loc, energy, rows, chunks * LANES, plate)

    lane = lax.broadcasted_iota(jnp.int32, (SUBLANES, LANES), 1)
    is_first, is_last = lane == 0, lane == LANES - 1
    for r in range(steps):
        at = slice(r * SUBLANES, (r + 1) * SUBLANES)
        before_t, before_c = None, None
        for z in range(sheets):
            ts = [t_ref[z, at, part_of(y)] for y in range(chunks)]
            cs = [half_conduct(b_ref[z, at, part_of(y)], ts[y]) for y in range(chunks)]
            t_turned = [pltpu.roll(v, LANES - 1, 1) for v in ts]
            c_turned = [pltpu.roll(v, LANES - 1, 1) for v in cs]
            flux = []
            for y in range(chunks):
                if y < chunks - 1:
                    t_next = jnp.where(is_last, t_turned[y + 1], t_turned[y])
                    c_next = jnp.where(is_last, c_turned[y + 1], c_turned[y])
                    flux.append((cs[y] + c_next) * (t_next - ts[y]))
                else:
                    inside = (cs[y] + c_turned[y]) * (t_turned[y] - ts[y])
                    flux.append(jnp.where(is_last, 0.0, inside))
            turned = [pltpu.roll(v, 1, 1) for v in flux]
            for y in range(chunks):
                from_low = jnp.where(is_first, turned[y - 1] if y else 0.0, turned[y])
                total = ts[y] + (flux[y] - from_low)
                if z == 0:
                    total = total + plane[at, part_of(y)]
                else:
                    across = (before_c[y] + cs[y]) * (ts[y] - before_t[y])
                    total = total - across
                    total_ref[y, z - 1, at, :] += across
                total_ref[y, z, at, :] = total
                c_ref[y, z, at, :] = cs[y]
            before_t, before_c = ts, cs

    group = max(1, 8 // sheets)
    for y in range(0, chunks, group):
        members = [(y + i, z) for i in range(group) for z in range(sheets)]
        at = slice(y * sheets, (y + group) * sheets)

        def cond(k):
            return jnp.stack([c_ref[i, z, pl.ds(k, SUBLANES, stride=steps), :] for i, z in members], 0)

        def keep(k, w, inv, p):
            w_ref[k, at] = w
            i_ref[k, at] = inv
            p_ref[k, at] = p

        block = factor(cond, steps, keep)
        for n, q in enumerate(COEFS):
            for i in range(len(members)):
                first = (y * sheets + i) * SUBLANES
                q_s[n, first : first + SUBLANES, :] = block[q][i]

    segments = [
        {q: q_s[n, pl.ds(s, lines, stride=SUBLANES), :] for n, q in enumerate(COEFS)}
        for s in range(SUBLANES)
    ]
    whole, levels = tree(segments, join_coefs)
    for (offset, _), level in zip(node_offsets(SUBLANES), levels):
        for n, values in enumerate(level):
            for i in range(3):
                links[offset + n, i] = values[i]
    for n, q in enumerate(COEFS):
        view[n] = whole[q]


def x_factor(loc, energy, t, b, plate, after):
    sheets, rows, columns = t.shape
    chunks = columns // LANES
    lines = chunks * sheets
    steps = rows // SUBLANES
    field = shape_of(chunks, sheets, rows, LANES)
    stored = shape_of(steps, lines, SUBLANES, LANES)
    return pl.pallas_call(
        functools.partial(x_factor_kernel, plate),
        in_specs=[IN_VMEM] * 4 + [ANYWHERE],
        out_shape=[
            field,
            field,
            stored,
            stored,
            stored,
            shape_of(SUBLANES - 1, 3, lines, LANES),
            shape_of(len(COEFS), lines, LANES),
        ],
        scratch_shapes=[pltpu.VMEM((len(COEFS), lines * SUBLANES, LANES), F32)],
        compiler_params=params(),
        cost_estimate=pl.CostEstimate(flops=40 * t.size, bytes_accessed=28 * t.size, transcendentals=0),
    )(loc, energy, t, b, after)


def far_side(sources):
    place = lax.axis_index("gy")
    paired = (place >> 1) % 2 != place % 2
    nothing = jnp.zeros(sources[0].shape, F32)
    by_pair = sources[1][...] if len(sources) > 1 else nothing
    other = sources[2][...] if len(sources) > 2 else nothing
    return jnp.where(paired, by_pair, other)


def x_target_kernel(count, t_ref, c_ref, total_ref, *refs):
    w_ref, i_ref, p_ref, links, view, h_ref, own, send, e_s, q_s = refs[count:]
    chunks, sheets, rows, _ = c_ref.shape
    lines = chunks * sheets
    steps = rows // SUBLANES

    near, far = refs[0][...], far_side(refs[:count])
    before = jnp.where(is_odd("gy"), near, far)
    after = jnp.where(is_odd("gy"), far, near)
    lane = lax.broadcasted_iota(jnp.int32, (rows, LANES), 1)
    for y, halo, edge, place in ((0, before, 0, 0), (chunks - 1, after, LANES - 1, 1)):
        for z in range(sheets):
            at = z if place else 2 * sheets + z
            t_next = halo[:, at : at + 1]
            c_next = halo[:, at + sheets : at + sheets + 1]
            face = jnp.where(c_next > 0.0, c_ref[y, z] + c_next, 0.0)
            flux = jnp.where(lane == edge, face * (t_next - t_ref[z, :, part_of(y)]), 0.0)
            base = total_ref[y, z] if place == 0 or chunks > 1 else e_s[0, z]
            e_s[place, z] = base + flux

    def field(y, z):
        if y == chunks - 1:
            return e_s.at[1, z]
        return e_s.at[0, z] if y == 0 else total_ref.at[y, z]

    group = max(1, 8 // sheets)
    for y in range(0, chunks, group):
        members = [(y + i, z) for i in range(group) for z in range(sheets)]
        at = slice(y * sheets, (y + group) * sheets)

        def target(k):
            return jnp.stack([field(i, z)[pl.ds(k, SUBLANES, stride=steps), :] for i, z in members], 0)

        def keep(k, h):
            h_ref[k, at] = h

        ends = eliminate(
            target, steps, lambda k: w_ref[k, at], lambda k: i_ref[k, at], lambda k: p_ref[k, at], keep
        )
        for q in range(2):
            for i in range(len(members)):
                first = (y * sheets + i) * SUBLANES
                q_s[q, first : first + SUBLANES, :] = ends[q][i]
    items = [
        tuple(q_s[q, pl.ds(s, lines, stride=SUBLANES), :] for q in range(2)) for s in range(SUBLANES)
    ]
    for offset, count in node_offsets(SUBLANES):
        joined = []
        for n in range(count):
            ties = tuple(links[offset + n, i] for i in range(3))
            both, flux = join_targets(items[2 * n], items[2 * n + 1], ties)
            own[offset + n] = flux
            joined.append(both)
        items = joined
    for n, q in enumerate(COEFS):
        send[q] = view[n]
    send[FIRST], send[LAST] = items[0]


def x_target(t, c, total, edge_cells, w, inv, p, links, view):
    chunks, sheets, rows, _ = c.shape
    lines = chunks * sheets
    steps = rows // SUBLANES
    return pl.pallas_call(
        functools.partial(x_target_kernel, len(edge_cells)),
        out_shape=[
            shape_of(steps, lines, SUBLANES, LANES),
            shape_of(SUBLANES - 1, lines, LANES),
            shape_of(7, lines, LANES),
        ],
        scratch_shapes=[
            pltpu.VMEM((2, sheets, rows, LANES), F32),
            pltpu.VMEM((2, lines * SUBLANES, LANES), F32),
        ],
        compiler_params=params(),
    )(t, c, total, *edge_cells, w, inv, p, links, view)


def stages_of(axis):
    return lax.axis_size(axis).bit_length() - 1


def swap(value, axis, flip):
    count = lax.axis_size(axis)
    return lax.ppermute(value, axis, [(i, i ^ flip) for i in range(count)])


def on_right(axis, stage):
    return (lax.axis_index(axis) >> stage) % 2 == 1


def toward(right, block):
    return (
        jnp.where(right, block[R00], block[RLL]),
        jnp.where(right, block[FIRST], block[LAST]),
        jnp.where(right, block[C0], block[CL]),
    )


def join(a, b):
    joined, ties = join_coefs(a, b)
    (joined[FIRST], joined[LAST]), flux = join_targets((a[FIRST], a[LAST]), (b[FIRST], b[LAST]), ties)
    return joined, (flux, ties[1], ties[2])


def ordered(right, own, other):
    first = [jnp.where(right, theirs, mine) for mine, theirs in zip(own, other)]
    second = [jnp.where(right, mine, theirs) for mine, theirs in zip(own, other)]
    return first, second


def join_kernel(axis, stage, width, last, *refs):
    count = 1 << width
    blocks = [[refs[-i % count][q] for q in range(7)] for i in range(count)]
    send = refs[-1 - width]
    links = refs[-width:]
    for bit in range(width):
        right = on_right(axis, stage + bit)
        for i in range(count):
            if not i >> bit & 1:
                j = i | 1 << bit
                blocks[i], blocks[j] = ordered(right, blocks[i], blocks[j])
    for bit in range(width):
        pairs = [join(blocks[i], blocks[i + 1]) for i in range(0, len(blocks), 2)]
        blocks = [p[0] for p in pairs]
        ties = [p[1] for p in pairs]
        for upper in range(bit + 1, width):
            right = on_right(axis, stage + upper)
            ties = [
                tuple(jnp.where(right, v, u) for u, v in zip(ties[i], ties[i + 1]))
                for i in range(0, len(ties), 2)
            ]
        for i in range(3):
            links[bit][i] = ties[0][i]
    (whole,) = blocks
    if last:
        for n, value in enumerate(toward(on_right(axis, stage + width), whole)):
            send[n] = value
    else:
        for q in range(7):
            send[q] = whole[q]


def join_stage(own, got, axis, stage, width, last, after):
    lines = own.shape[1]
    return pl.pallas_call(
        functools.partial(join_kernel, axis, stage, width, last),
        in_specs=[IN_VMEM] * (1 + len(got)) + [ANYWHERE] * len(after),
        out_shape=[shape_of(3 if last else 7, lines, LANES)] + [shape_of(3, lines, LANES)] * width,
        compiler_params=params(),
    )(own, *got, *after)


def gather_line(view, axis, widest=1, meanwhile=()):
    stages = stages_of(axis)
    links, stage = [], 0
    while stage < stages - 1:
        width = min(widest, stages - 1 - stage)
        got = [swap(view, axis, flip << stage) for flip in range((1 << width) - 1, 0, -1)]
        last = stage + width == stages - 1
        view, *ties = join_stage(view, got, axis, stage, width, last, meanwhile)
        links += ties
        stage += width
        meanwhile = ()
    return view, swap(view, axis, 1 << stage), links


def block_ends(axis, own, got, links):
    top = len(links)
    right = on_right(axis, top)
    face = own[2] + got[2]
    jump = jnp.where(right, own[1] - got[1], got[1] - own[1])
    flux = jump * face * inverse(1.0 + face * (own[0] + got[0]))
    low = jnp.where(right, -flux, 0.0)
    high = jnp.where(right, 0.0, flux)
    for stage in range(top - 1, -1, -1):
        tie = links[stage]
        right = on_right(axis, stage)
        flux = between(tie[0], tie[1], tie[2], low, high)
        low, high = jnp.where(right, -flux, low), jnp.where(right, high, flux)
    return low, high


def y_factor_kernel(c_ref, after, w_ref, i_ref, p_ref, inner, outer, view, c_s, q_s):
    chunks, sheets, rows, _ = c_ref.shape
    each = LANES // rows
    pairs = sheets // each
    span = chunks * LANES // SUBLANES
    steps = span // Y_PARTS
    for m in range(pairs):
        for y in range(chunks):
            block = jnp.concatenate([c_ref[y, m * each + i] for i in range(each)], 0)
            c_s[m, y * LANES : (y + 1) * LANES, :] = block.T

    members = [(j, m) for j in range(Y_PARTS) for m in range(pairs)]

    def cond(k):
        return jnp.stack([c_s[m, pl.ds(j * steps + k, SUBLANES, stride=span), :] for j, m in members], 0)

    def keep(k, w, inv, p):
        w_ref[k] = w
        i_ref[k] = inv
        p_ref[k] = p

    block = factor(cond, steps, keep)
    parts = [{q: block[q][j * pairs : (j + 1) * pairs] for q in COEFS} for j in range(Y_PARTS)]
    whole, levels = tree(parts, join_coefs)
    for (offset, _), level in zip(node_offsets(Y_PARTS), levels):
        for n, values in enumerate(level):
            for i in range(3):
                inner[offset + n, i] = values[i]
    for n, q in enumerate(COEFS):
        for m in range(pairs):
            q_s[n, m * SUBLANES : (m + 1) * SUBLANES, :] = whole[q][m]
    segments = [
        {q: q_s[n, pl.ds(s, pairs, stride=SUBLANES), :] for n, q in enumerate(COEFS)}
        for s in range(SUBLANES)
    ]
    whole, levels = tree(segments, join_coefs)
    for (offset, _), level in zip(node_offsets(SUBLANES), levels):
        for n, values in enumerate(level):
            for i in range(3):
                outer[offset + n, i] = values[i]
    for n, q in enumerate(COEFS):
        view[n] = whole[q]


def y_factor(c, after):
    chunks, sheets, rows, _ = c.shape
    pairs = sheets * rows // LANES
    steps = chunks * LANES // SUBLANES // Y_PARTS
    stored = shape_of(steps, Y_PARTS * pairs, SUBLANES, LANES)
    return pl.pallas_call(
        y_factor_kernel,
        in_specs=[IN_VMEM, ANYWHERE],
        out_shape=[
            stored,
            stored,
            stored,
            shape_of(Y_PARTS - 1, 3, pairs, SUBLANES, LANES),
            shape_of(SUBLANES - 1, 3, pairs, LANES),
            shape_of(len(COEFS), pairs, LANES),
        ],
        scratch_shapes=[
            pltpu.VMEM((pairs, chunks * LANES, LANES), F32),
            pltpu.VMEM((len(COEFS), pairs * SUBLANES, LANES), F32),
        ],
        compiler_params=params(),
        cost_estimate=pl.CostEstimate(flops=20 * c.size, bytes_accessed=16 * c.size, transcendentals=0),
    )(c, after)


def z_factor_kernel(c_ref, after, w_ref, i_ref):
    sheets = c_ref.shape[1]
    ground = 1.0
    for z in range(sheets - 1):
        face = c_ref[:, z] + c_ref[:, z + 1]
        inv = inverse(ground + face)
        w = face * inv
        i_ref[z] = inv
        w_ref[z] = w
        ground = 1.0 + w * ground
    i_ref[sheets - 1] = inverse(ground)


def z_factor(c, after):
    chunks, sheets, rows, _ = c.shape
    return pl.pallas_call(
        z_factor_kernel,
        in_specs=[IN_VMEM, ANYWHERE],
        out_shape=[
            shape_of(sheets - 1, chunks, rows, LANES),
            shape_of(sheets, chunks, rows, LANES),
        ],
        compiler_params=params(),
        cost_estimate=pl.CostEstimate(flops=10 * c.size, bytes_accessed=12 * c.size, transcendentals=0),
    )(c, after)


def y_target_kernel(stages, *refs):
    own, got = refs[:2]
    ties = refs[2 : 1 + stages]
    xw, xh, xp, x_links, x_own, t_ref, yw, yi, yp, inner, outer, view = refs[1 + stages : 13 + stages]
    h_ref, inner_own, outer_own, send = refs[13 + stages : 17 + stages]
    f_s, g_s, y_s, q_s = refs[17 + stages :]
    chunks, sheets, rows, _ = g_s.shape
    lines = chunks * sheets
    x_steps = rows // SUBLANES

    low, high = block_ends("gx", own, got, ties)
    levels = [
        [(x_own[o + n], x_links[o + n, 1], x_links[o + n, 2]) for n in range(count)]
        for o, count in node_offsets(SUBLANES)
    ]
    for s, ends in enumerate(descend(levels, low, high)):
        for i in range(2):
            f_s[i, pl.ds(s, lines, stride=SUBLANES), :] = ends[i]
    group = max(1, 8 // sheets)
    for y in range(0, chunks, group):
        members = [(y + i, z) for i in range(group) for z in range(sheets)]
        at = slice(y * sheets, (y + group) * sheets)
        low, value = (
            jnp.stack(
                [
                    f_s[i, (y * sheets + n) * SUBLANES : (y * sheets + n + 1) * SUBLANES, :]
                    for n in range(len(members))
                ],
                0,
            )
            for i in range(2)
        )
        for k in range(x_steps - 1, -1, -1):
            value = xw[k, at] * value + (xh[k, at] + xp[k, at] * low)
            for n, (i, z) in enumerate(members):
                g_s[i, z, pl.ds(k, SUBLANES, stride=x_steps), :] = value[n]

    each = LANES // rows
    pairs = sheets // each
    span = chunks * LANES // SUBLANES
    steps = span // Y_PARTS
    for m in range(pairs):
        for y in range(chunks):
            block = jnp.concatenate(
                [g_s[y, m * each + i] - t_ref[m * each + i, :, part_of(y)] for i in range(each)], 0
            )
            y_s[m, y * LANES : (y + 1) * LANES, :] = block.T
    members = [(j, m) for j in range(Y_PARTS) for m in range(pairs)]

    def target(k):
        return jnp.stack([y_s[m, pl.ds(j * steps + k, SUBLANES, stride=span), :] for j, m in members], 0)

    def keep(k, h):
        h_ref[k] = h

    ends = eliminate(target, steps, lambda k: yw[k], lambda k: yi[k], lambda k: yp[k], keep)
    items = [tuple(v[j * pairs : (j + 1) * pairs] for v in ends) for j in range(Y_PARTS)]
    for offset, count in node_offsets(Y_PARTS):
        joined = []
        for n in range(count):
            tie = tuple(inner[offset + n, i] for i in range(3))
            both, flux = join_targets(items[2 * n], items[2 * n + 1], tie)
            inner_own[offset + n] = flux
            joined.append(both)
        items = joined
    for q in range(2):
        for m in range(pairs):
            q_s[q, m * SUBLANES : (m + 1) * SUBLANES, :] = items[0][q][m]
    items = [
        tuple(q_s[q, pl.ds(s, pairs, stride=SUBLANES), :] for q in range(2)) for s in range(SUBLANES)
    ]
    for offset, count in node_offsets(SUBLANES):
        joined = []
        for n in range(count):
            tie = tuple(outer[offset + n, i] for i in range(3))
            both, flux = join_targets(items[2 * n], items[2 * n + 1], tie)
            outer_own[offset + n] = flux
            joined.append(both)
        items = joined
    for n, q in enumerate(COEFS):
        send[q] = view[n]
    send[FIRST], send[LAST] = items[0]


def y_target(own, got, ties, xw, xh, xp, x_links, x_own, t, yw, yi, yp, inner, outer, view):
    sheets, rows, columns = t.shape
    chunks = columns // LANES
    lines = chunks * sheets
    pairs = sheets * rows // LANES
    return pl.pallas_call(
        functools.partial(y_target_kernel, len(ties) + 1),
        out_shape=[
            shape_of(*yw.shape),
            shape_of(Y_PARTS - 1, pairs, SUBLANES, LANES),
            shape_of(SUBLANES - 1, pairs, LANES),
            shape_of(7, pairs, LANES),
        ],
        scratch_shapes=[
            pltpu.VMEM((2, lines * SUBLANES, LANES), F32),
            pltpu.VMEM((chunks, sheets, rows, LANES), F32),
            pltpu.VMEM((pairs, chunks * LANES, LANES), F32),
            pltpu.VMEM((2, pairs * SUBLANES, LANES), F32),
        ],
        compiler_params=params(),
    )(own, got, *ties, xw, xh, xp, x_links, x_own, t, yw, yi, yp, inner, outer, view)


def finish_kernel(stages, *refs):
    own, got = refs[:2]
    ties = refs[2 : 1 + stages]
    yw, yh, yp, inner, inner_own, outer, outer_own, zw, zi, t_ref = refs[1 + stages : 11 + stages]
    out, e_s, u_s, o_s, sems = refs[11 + stages :]
    chunks, sheets, rows, _ = o_s.shape
    each = LANES // rows
    pairs = sheets // each
    steps = yw.shape[0]
    span = chunks * LANES // SUBLANES

    low, high = block_ends("gy", own, got, ties)
    levels = [
        [(outer_own[o + n], outer[o + n, 1], outer[o + n, 2]) for n in range(count)]
        for o, count in node_offsets(SUBLANES)
    ]
    for s, ends in enumerate(descend(levels, low, high)):
        for i in range(2):
            e_s[i, pl.ds(s, pairs, stride=SUBLANES), :] = ends[i]
    low, high = (
        jnp.stack([e_s[i, m * SUBLANES : (m + 1) * SUBLANES, :] for m in range(pairs)], 0)
        for i in range(2)
    )
    levels = [
        [(inner_own[o + n], inner[o + n, 1], inner[o + n, 2]) for n in range(count)]
        for o, count in node_offsets(Y_PARTS)
    ]
    ends = descend(levels, low, high)
    low = jnp.concatenate([e[0] for e in ends], 0)
    value = jnp.concatenate([e[1] for e in ends], 0)
    members = [(j, m) for j in range(Y_PARTS) for m in range(pairs)]
    for k in range(steps - 1, -1, -1):
        value = yw[k] * value + (yh[k] + yp[k] * low)
        for n, (j, m) in enumerate(members):
            u_s[m, pl.ds(j * steps + k, SUBLANES, stride=span), :] = value[n]

    copies = []
    for y in range(chunks):
        part = part_of(y)
        turned = [u_s[m, part, :].T for m in range(pairs)]
        rhs, kept = None, []
        for z in range(sheets):
            first = (z % each) * rows
            own_rhs = turned[z // each][first : first + rows, :]
            rhs = own_rhs if z == 0 else own_rhs + zw[z - 1, y] * rhs
            kept.append(rhs * zi[z, y])
        value = kept[-1]
        o_s[y, sheets - 1] = t_ref[sheets - 1, :, part] + value
        for z in range(sheets - 2, -1, -1):
            value = zw[z, y] * value + kept[z]
            o_s[y, z] = t_ref[z, :, part] + value
        copy = pltpu.make_async_copy(o_s.at[y], out.at[:, :, pl.ds(y * LANES, LANES)], sems.at[y])
        copy.start()
        copies.append(copy)
    for copy in copies:
        copy.wait()


def finish(own, got, ties, yw, yh, yp, inner, inner_own, outer, outer_own, zw, zi, t):
    sheets, rows, columns = t.shape
    chunks = columns // LANES
    pairs = sheets * rows // LANES
    return pl.pallas_call(
        functools.partial(finish_kernel, len(ties) + 1),
        out_shape=shape_of(sheets, rows, chunks * LANES),
        out_specs=ANYWHERE,
        scratch_shapes=[
            pltpu.VMEM((2, pairs * SUBLANES, LANES), F32),
            pltpu.VMEM((pairs, chunks * LANES, LANES), F32),
            pltpu.VMEM((chunks, sheets, rows, LANES), F32),
            pltpu.SemaphoreType.DMA((chunks,)),
        ],
        compiler_params=params(),
    )(own, got, *ties, yw, yh, yp, inner, inner_own, outer, outer_own, zw, zi, t)


def per_device(temperature, base, locations, energy):
    columns = temperature.shape[2]
    gy = lax.axis_size("gy")
    loc, heat, packed = edges(temperature, base, locations[None], energy[None])
    near = swap(packed, "gy", 1)
    far = [swap(near, "gy", 2)] if gy > 2 else []
    if gy > 4:
        far.append(lax.ppermute(near, "gy", [(i, (i + 2 ^ 2) - 2) for i in range(2, gy - 2)]))
    t, b = (pltpu.with_memory_space_constraint(v, pltpu.VMEM) for v in (temperature, base))
    c, total, xw, xi, xp, x_links, x_view = x_factor(loc, heat, t, b, columns * gy, near)
    xh, x_own, view = x_target(t, c, total, [near] + far, xw, xi, xp, x_links, x_view)
    yw, yi, yp, inner, outer, y_view = y_factor(c, x_view)
    zw, zi = z_factor(c, view)
    own, got, ties = gather_line(view, "gx", 2, (y_view, zw))
    yh, inner_own, outer_own, view = y_target(
        own, got, ties, xw, xh, xp, x_links, x_own, t, yw, yi, yp, inner, outer, y_view
    )
    own, got, ties = gather_line(view, "gy")
    return finish(own, got, ties, yw, yh, yp, inner, inner_own, outer, outer_own, zw, zi, t)


def solution(mesh):
    in_specs = (P(None, "gx", "gy"), P(None, "gx", "gy"), P(), P())
    out_specs = P(None, "gx", "gy")
    return jax.shard_map(
        per_device, mesh=mesh, in_specs=in_specs, out_specs=out_specs, check_vma=False
    )
```

```python
import functools

import jax
import jax.numpy as jnp
from jax import lax
from jax.experimental import pallas as pl
from jax.experimental.pallas import tpu as pltpu
from jax.sharding import PartitionSpec as P

RATE = 2000.0
THERMAL_GROWTH = 0.8
LANES = 128
SUBLANES = 8
Y_PARTS = 4
F32 = jnp.float32
MIB = 1024 * 1024
ANYWHERE = pl.BlockSpec(memory_space=pl.ANY)
IN_HBM = pl.BlockSpec(memory_space=pltpu.HBM)
IN_VMEM = pl.BlockSpec(memory_space=pltpu.VMEM)

R00, R0L, RLL, FIRST, LAST, C0, CL = range(7)
COEFS = (R00, R0L, RLL, C0, CL)


def params(limit=40):
    return pltpu.CompilerParams(vmem_limit_bytes=limit * MIB)


def shape_of(*sizes):
    return jax.ShapeDtypeStruct(sizes, F32)


def half_conduct(base, temperature):
    return base * (0.5 * RATE + (0.5 * RATE * THERMAL_GROWTH) * temperature)


def inverse(x):
    guess = pl.reciprocal(x, approx=True)
    return guess * (2.0 - x * guess)


def join_coefs(a, b):
    face = a[CL] + b[C0]
    inv = face * inverse(1.0 + face * (a[RLL] + b[R00]))
    left = a[R0L] * inv
    right = b[R0L] * inv
    joined = {
        R00: a[R00] - left * a[R0L],
        R0L: left * b[R0L],
        RLL: b[RLL] - right * b[R0L],
        C0: a[C0],
        CL: b[CL],
    }
    return joined, (inv, right, left)


def join_targets(a, b, links):
    inv, right, left = links
    jump = b[0] - a[1]
    return (a[0] + left * jump, b[1] - right * jump), jump * inv


def between(own, right, left, low, high):
    return own + right * high - left * low


def tree(items, join):
    levels = []
    while len(items) > 1:
        pairs = [join(items[i], items[i + 1]) for i in range(0, len(items), 2)]
        items = [p[0] for p in pairs]
        levels.append([p[1] for p in pairs])
    return items[0], levels


def descend(levels, low, high):
    ends = [(low, high)]
    for level in reversed(levels):
        below = []
        for (lo, hi), (own, right, left) in zip(ends, level):
            flux = between(own, right, left, lo, hi)
            below += [(lo, flux), (-flux, hi)]
        ends = below
    return ends


def node_offsets(leaves):
    offsets, at, count = [], 0, leaves // 2
    while count:
        offsets.append((at, count))
        at += count
        count //= 2
    return offsets


def factor(cond, steps, keep):
    here = cond(0)
    c_first = here
    one = jnp.ones_like(here)
    ground, path, first_first = one, one, None
    for k in range(steps - 1):
        following = cond(k + 1)
        face = here + following
        inv = inverse(ground + face)
        w = face * inv
        p = path * inv
        keep(k, w, inv, p)
        step = path * p
        first_first = step if first_first is None else first_first + step
        path = path * w
        ground = 1.0 + w * ground
        here = following
    inv = inverse(ground)
    p = path * inv
    keep(steps - 1, inv, inv, p)
    return {R00: first_first + path * p, R0L: p, RLL: inv, C0: c_first, CL: here}


def eliminate(target, steps, w, inv, p, keep):
    rhs = target(0)
    first = None
    for k in range(steps):
        h = rhs * inv(k)
        keep(k, h)
        step = rhs * p(k)
        first = step if first is None else first + step
        if k < steps - 1:
            rhs = target(k + 1) + w(k) * rhs
    return first, h


def is_odd(axis):
    return lax.axis_index(axis) % 2 == 1


def edges_kernel(t_hbm, b_hbm, loc_hbm, energy_hbm, loc, energy, packed, t_s, b_s, sems):
    sheets, rows, columns = t_hbm.shape
    copies = [
        pltpu.make_async_copy(loc_hbm, loc, sems.at[2, 0]),
        pltpu.make_async_copy(energy_hbm, energy, sems.at[2, 1]),
    ]
    for side, start in enumerate((0, columns - LANES)):
        for i, (src, dst) in enumerate(((t_hbm, t_s), (b_hbm, b_s))):
            for z in range(sheets):
                part = src.at[z, :, pl.ds(start, LANES)]
                place = side * sheets + z
                copies.append(pltpu.make_async_copy(part, dst.at[side, z], sems.at[i, place]))
    for copy in copies:
        copy.start()
    for copy in copies:
        copy.wait()
    lane = lax.broadcasted_iota(jnp.int32, (rows, LANES), 1)
    total = jnp.zeros((rows, LANES), F32)
    for side, source in enumerate((0, LANES - 1)):
        for z in range(sheets):
            t = t_s[side, z]
            c = half_conduct(b_s[side, z], t)
            place = 2 * sheets * side + z
            total = jnp.where(lane == place, t[:, source : source + 1], total)
            total = jnp.where(lane == place + sheets, c[:, source : source + 1], total)
    packed[...] = total


def edges(temperature, base, locations, energy):
    sheets, rows, _ = temperature.shape
    operands = (temperature, base, locations, energy)
    return pl.pallas_call(
        edges_kernel,
        in_specs=[IN_HBM] * 4,
        out_shape=[
            pltpu.VMEM(locations.shape, jnp.int32),
            pltpu.VMEM(energy.shape, F32),
            pltpu.VMEM((rows, LANES), F32),
        ],
        scratch_shapes=[
            pltpu.VMEM((2, sheets, rows, LANES), F32),
            pltpu.VMEM((2, sheets, rows, LANES), F32),
            pltpu.SemaphoreType.DMA((3, 2 * sheets)),
        ],
        compiler_params=params(),
    )(*[pltpu.with_memory_space_constraint(v, pltpu.HBM) for v in operands])


def load_kernel(t_hbm, b_hbm, after, t_out, b_out, sems):
    sheets = t_hbm.shape[0]
    copies = []
    for i, (src, dst) in enumerate(((t_hbm, t_out), (b_hbm, b_out))):
        for z in range(sheets):
            copies.append(pltpu.make_async_copy(src.at[z], dst.at[z], sems.at[i, z]))
    for copy in copies:
        copy.start()
    for copy in copies:
        copy.wait()


def load(temperature, base, after):
    fields = [pltpu.with_memory_space_constraint(v, pltpu.HBM) for v in (temperature, base)]
    return pl.pallas_call(
        load_kernel,
        in_specs=[IN_HBM] * 2 + [ANYWHERE],
        out_shape=[pltpu.VMEM(temperature.shape, F32)] * 2,
        scratch_shapes=[pltpu.SemaphoreType.DMA((2, temperature.shape[0]))],
        compiler_params=params(),
        cost_estimate=pl.CostEstimate(flops=0, bytes_accessed=16 * temperature.size, transcendentals=0),
    )(*fields, after)


def source_plane(loc, energy, rows, columns, plate):
    place = loc[...]
    count = place.shape[1]
    local_x = place // plate - lax.axis_index("gx") * rows
    local_y = place % plate - lax.axis_index("gy") * columns
    in_x = lax.broadcasted_iota(jnp.int32, (rows, count), 0) == local_x
    in_y = lax.broadcasted_iota(jnp.int32, (columns, count), 0) == local_y
    by_y = jnp.where(in_y, 1.0, 0.0).astype(jnp.bfloat16)
    left = energy[...]
    plane = None
    for _ in range(3):
        part = left.astype(jnp.bfloat16).astype(F32)
        left = left - part
        term = lax.dot_general(
            jnp.where(in_x, part, 0.0).astype(jnp.bfloat16),
            by_y,
            (((1,), (1,)), ((), ())),
            preferred_element_type=F32,
        )
        plane = term if plane is None else plane + term
    return plane


def part_of(y):
    return slice(y * LANES, (y + 1) * LANES)


def line_groups(chunks, sheets):
    order = [0, chunks - 1] + list(range(1, chunks - 1))
    return [[(y, z) for y in order[i : i + 2] for z in range(sheets)] for i in range(0, chunks, 2)]


def x_eliminate(field, members, first_line, w_ref, i_ref, p_ref, h_ref, h_line, q_s):
    steps = w_ref.shape[0]
    at = slice(first_line, first_line + len(members))
    kept_at = slice(h_line, h_line + len(members))

    def target(k):
        return jnp.stack([field(y, z)[pl.ds(k, SUBLANES, stride=steps), :] for y, z in members], 0)

    def keep(k, h):
        h_ref[k, kept_at] = h

    ends = eliminate(
        target, steps, lambda k: w_ref[k, at], lambda k: i_ref[k, at], lambda k: p_ref[k, at], keep
    )
    for q in range(2):
        for i in range(len(members)):
            first = (first_line + i) * SUBLANES
            q_s[q, first : first + SUBLANES, :] = ends[q][i]


def x_factor_kernel(plate, loc, energy, t_ref, b_ref, after, *refs):
    c_ref, total_ref, w_ref, i_ref, p_ref, links, view, h_ref, ends_ref, q_s = refs
    chunks, sheets, rows, _ = c_ref.shape
    lines = chunks * sheets
    steps = rows // SUBLANES
    plane = source_plane(loc, energy, rows, chunks * LANES, plate)

    lane = lax.broadcasted_iota(jnp.int32, (SUBLANES, LANES), 1)
    is_first, is_last = lane == 0, lane == LANES - 1
    for r in range(steps):
        at = slice(r * SUBLANES, (r + 1) * SUBLANES)
        before_t, before_c = None, None
        for z in range(sheets):
            ts = [t_ref[z, at, part_of(y)] for y in range(chunks)]
            cs = [half_conduct(b_ref[z, at, part_of(y)], ts[y]) for y in range(chunks)]
            t_turned = [pltpu.roll(v, LANES - 1, 1) for v in ts]
            c_turned = [pltpu.roll(v, LANES - 1, 1) for v in cs]
            flux = []
            for y in range(chunks):
                if y < chunks - 1:
                    t_next = jnp.where(is_last, t_turned[y + 1], t_turned[y])
                    c_next = jnp.where(is_last, c_turned[y + 1], c_turned[y])
                    flux.append((cs[y] + c_next) * (t_next - ts[y]))
                else:
                    inside = (cs[y] + c_turned[y]) * (t_turned[y] - ts[y])
                    flux.append(jnp.where(is_last, 0.0, inside))
            turned = [pltpu.roll(v, 1, 1) for v in flux]
            for y in range(chunks):
                from_low = jnp.where(is_first, turned[y - 1] if y else 0.0, turned[y])
                total = ts[y] + (flux[y] - from_low)
                if z == 0:
                    total = total + plane[at, part_of(y)]
                else:
                    across = (before_c[y] + cs[y]) * (ts[y] - before_t[y])
                    total = total - across
                    total_ref[y, z - 1, at, :] += across
                total_ref[y, z, at, :] = total
                c_ref[y, z, at, :] = cs[y]
            before_t, before_c = ts, cs

    at = 0
    for n, members in enumerate(line_groups(chunks, sheets)):

        def cond(k):
            return jnp.stack([c_ref[y, z, pl.ds(k, SUBLANES, stride=steps), :] for y, z in members], 0)

        def keep(k, w, inv, p):
            w_ref[k, at : at + len(members)] = w
            i_ref[k, at : at + len(members)] = inv
            p_ref[k, at : at + len(members)] = p

        block = factor(cond, steps, keep)
        for i, q in enumerate(COEFS):
            for j in range(len(members)):
                first = (at + j) * SUBLANES
                q_s[i, first : first + SUBLANES, :] = block[q][j]
        if n > 0:
            x_eliminate(
                lambda y, z: total_ref.at[y, z], members, at, w_ref, i_ref, p_ref, h_ref,
                at - 2 * sheets, ends_ref,
            )
        at += len(members)

    segments = [
        {q: q_s[n, pl.ds(s, lines, stride=SUBLANES), :] for n, q in enumerate(COEFS)}
        for s in range(SUBLANES)
    ]
    whole, levels = tree(segments, join_coefs)
    for (offset, _), level in zip(node_offsets(SUBLANES), levels):
        for n, values in enumerate(level):
            for i in range(3):
                links[offset + n, i] = values[i]
    for n, q in enumerate(COEFS):
        view[n] = whole[q]


def x_factor(loc, energy, t, b, plate, after):
    sheets, rows, columns = t.shape
    chunks = columns // LANES
    lines = chunks * sheets
    steps = rows // SUBLANES
    field = shape_of(chunks, sheets, rows, LANES)
    stored = shape_of(steps, lines, SUBLANES, LANES)
    return pl.pallas_call(
        functools.partial(x_factor_kernel, plate),
        in_specs=[IN_VMEM] * 4 + [ANYWHERE],
        out_shape=[
            field,
            field,
            stored,
            stored,
            stored,
            shape_of(SUBLANES - 1, 3, lines, LANES),
            shape_of(len(COEFS), lines, LANES),
            shape_of(steps, max(1, lines - 2 * sheets), SUBLANES, LANES),
            shape_of(2, lines * SUBLANES, LANES),
        ],
        scratch_shapes=[pltpu.VMEM((len(COEFS), lines * SUBLANES, LANES), F32)],
        compiler_params=params(),
        cost_estimate=pl.CostEstimate(flops=40 * t.size, bytes_accessed=28 * t.size, transcendentals=0),
    )(loc, energy, t, b, after)


def far_side(sources):
    place = lax.axis_index("gy")
    paired = (place >> 1) % 2 != place % 2
    nothing = jnp.zeros(sources[0].shape, F32)
    by_pair = sources[1][...] if len(sources) > 1 else nothing
    other = sources[2][...] if len(sources) > 2 else nothing
    return jnp.where(paired, by_pair, other)


def x_target_kernel(count, own_cells, t_ref, total_ref, *refs):
    w_ref, i_ref, p_ref, links, view, ends_ref, h_ref, own, send, e_s, q_s = refs[count:]
    chunks, sheets, rows, _ = total_ref.shape
    lines = chunks * sheets

    near, far = refs[0][...], far_side(refs[:count])
    before = jnp.where(is_odd("gy"), near, far)
    after = jnp.where(is_odd("gy"), far, near)
    lane = lax.broadcasted_iota(jnp.int32, (rows, LANES), 1)
    side = 2 * sheets
    beyond = jnp.where(lane < side, pltpu.roll(before, LANES - side, 1), pltpu.roll(after, side, 1))
    mine = own_cells[...]
    face = jnp.where(beyond > 0.0, mine + beyond, 0.0)
    flux = pltpu.roll(face, LANES - sheets, 1) * (beyond - mine)
    for n, (y, edge) in enumerate(((0, 0), (chunks - 1, LANES - 1))):
        for z in range(sheets):
            at = n * side + z
            e_s[n, z] = total_ref[y, z] + jnp.where(lane == edge, flux[:, at : at + 1], 0.0)

    members = line_groups(chunks, sheets)[0]
    x_eliminate(
        lambda y, z: e_s.at[0 if y == 0 else 1, z], members, 0, w_ref, i_ref, p_ref, h_ref, 0, q_s
    )
    split = len(members)
    items = [
        tuple(
            jnp.concatenate(
                [
                    q_s[q, pl.ds(s, split, stride=SUBLANES), :],
                    ends_ref[q, pl.ds(split * SUBLANES + s, lines - split, stride=SUBLANES), :],
                ],
                0,
            )
            for q in range(2)
        )
        for s in range(SUBLANES)
    ]
    for offset, count in node_offsets(SUBLANES):
        joined = []
        for n in range(count):
            ties = tuple(links[offset + n, i] for i in range(3))
            both, flux = join_targets(items[2 * n], items[2 * n + 1], ties)
            own[offset + n] = flux
            joined.append(both)
        items = joined
    for n, q in enumerate(COEFS):
        send[q] = view[n]
    send[FIRST], send[LAST] = items[0]


def x_target(own_cells, t, total, edge_cells, w, inv, p, links, view, ends):
    chunks, sheets, rows, _ = total.shape
    lines = chunks * sheets
    steps = rows // SUBLANES
    return pl.pallas_call(
        functools.partial(x_target_kernel, len(edge_cells)),
        out_shape=[
            shape_of(steps, 2 * sheets, SUBLANES, LANES),
            shape_of(SUBLANES - 1, lines, LANES),
            shape_of(7, lines, LANES),
        ],
        scratch_shapes=[
            pltpu.VMEM((2, sheets, rows, LANES), F32),
            pltpu.VMEM((2, 2 * sheets * SUBLANES, LANES), F32),
        ],
        compiler_params=params(),
    )(own_cells, t, total, *edge_cells, w, inv, p, links, view, ends)


def stages_of(axis):
    return lax.axis_size(axis).bit_length() - 1


def swap(value, axis, flip):
    count = lax.axis_size(axis)
    return lax.ppermute(value, axis, [(i, i ^ flip) for i in range(count)])


def on_right(axis, stage):
    return (lax.axis_index(axis) >> stage) % 2 == 1


def toward(right, block):
    return (
        jnp.where(right, block[R00], block[RLL]),
        jnp.where(right, block[FIRST], block[LAST]),
        jnp.where(right, block[C0], block[CL]),
    )


def join(a, b):
    joined, ties = join_coefs(a, b)
    (joined[FIRST], joined[LAST]), flux = join_targets((a[FIRST], a[LAST]), (b[FIRST], b[LAST]), ties)
    return joined, (flux, ties[1], ties[2])


def ordered(right, own, other):
    first = [jnp.where(right, theirs, mine) for mine, theirs in zip(own, other)]
    second = [jnp.where(right, mine, theirs) for mine, theirs in zip(own, other)]
    return first, second


def join_kernel(axis, stage, width, last, *refs):
    count = 1 << width
    blocks = [[refs[-i % count][q] for q in range(7)] for i in range(count)]
    send = refs[-1 - width]
    links = refs[-width:]
    for bit in range(width):
        right = on_right(axis, stage + bit)
        for i in range(count):
            if not i >> bit & 1:
                j = i | 1 << bit
                blocks[i], blocks[j] = ordered(right, blocks[i], blocks[j])
    for bit in range(width):
        pairs = [join(blocks[i], blocks[i + 1]) for i in range(0, len(blocks), 2)]
        blocks = [p[0] for p in pairs]
        ties = [p[1] for p in pairs]
        for upper in range(bit + 1, width):
            right = on_right(axis, stage + upper)
            ties = [
                tuple(jnp.where(right, v, u) for u, v in zip(ties[i], ties[i + 1]))
                for i in range(0, len(ties), 2)
            ]
        for i in range(3):
            links[bit][i] = ties[0][i]
    (whole,) = blocks
    if last:
        for n, value in enumerate(toward(on_right(axis, stage + width), whole)):
            send[n] = value
    else:
        for q in range(7):
            send[q] = whole[q]


def join_stage(own, got, axis, stage, width, last, after):
    lines = own.shape[1]
    return pl.pallas_call(
        functools.partial(join_kernel, axis, stage, width, last),
        in_specs=[IN_VMEM] * (1 + len(got)) + [ANYWHERE] * len(after),
        out_shape=[shape_of(3 if last else 7, lines, LANES)] + [shape_of(3, lines, LANES)] * width,
        compiler_params=params(),
    )(own, *got, *after)


def gather_line(view, axis, widest=1, meanwhile=()):
    stages = stages_of(axis)
    links, stage = [], 0
    while stage < stages - 1:
        width = min(widest, stages - 1 - stage)
        got = [swap(view, axis, flip << stage) for flip in range((1 << width) - 1, 0, -1)]
        last = stage + width == stages - 1
        view, *ties = join_stage(view, got, axis, stage, width, last, meanwhile)
        links += ties
        stage += width
        meanwhile = ()
    return view, swap(view, axis, 1 << stage), links


def block_ends(axis, own, got, links):
    top = len(links)
    right = on_right(axis, top)
    face = own[2] + got[2]
    jump = jnp.where(right, own[1] - got[1], got[1] - own[1])
    flux = jump * face * inverse(1.0 + face * (own[0] + got[0]))
    low = jnp.where(right, -flux, 0.0)
    high = jnp.where(right, 0.0, flux)
    for stage in range(top - 1, -1, -1):
        tie = links[stage]
        right = on_right(axis, stage)
        flux = between(tie[0], tie[1], tie[2], low, high)
        low, high = jnp.where(right, -flux, low), jnp.where(right, high, flux)
    return low, high


def y_factor_kernel(c_ref, after, w_ref, i_ref, p_ref, inner, outer, view, c_s, q_s):
    chunks, sheets, rows, _ = c_ref.shape
    each = LANES // rows
    pairs = sheets // each
    span = chunks * LANES // SUBLANES
    steps = span // Y_PARTS
    for m in range(pairs):
        for y in range(chunks):
            block = jnp.concatenate([c_ref[y, m * each + i] for i in range(each)], 0)
            c_s[m, y * LANES : (y + 1) * LANES, :] = block.T

    members = [(j, m) for j in range(Y_PARTS) for m in range(pairs)]

    def cond(k):
        return jnp.stack([c_s[m, pl.ds(j * steps + k, SUBLANES, stride=span), :] for j, m in members], 0)

    def keep(k, w, inv, p):
        w_ref[k] = w
        i_ref[k] = inv
        p_ref[k] = p

    block = factor(cond, steps, keep)
    parts = [{q: block[q][j * pairs : (j + 1) * pairs] for q in COEFS} for j in range(Y_PARTS)]
    whole, levels = tree(parts, join_coefs)
    for (offset, _), level in zip(node_offsets(Y_PARTS), levels):
        for n, values in enumerate(level):
            for i in range(3):
                inner[offset + n, i] = values[i]
    for n, q in enumerate(COEFS):
        for m in range(pairs):
            q_s[n, m * SUBLANES : (m + 1) * SUBLANES, :] = whole[q][m]
    segments = [
        {q: q_s[n, pl.ds(s, pairs, stride=SUBLANES), :] for n, q in enumerate(COEFS)}
        for s in range(SUBLANES)
    ]
    whole, levels = tree(segments, join_coefs)
    for (offset, _), level in zip(node_offsets(SUBLANES), levels):
        for n, values in enumerate(level):
            for i in range(3):
                outer[offset + n, i] = values[i]
    for n, q in enumerate(COEFS):
        view[n] = whole[q]


def y_factor(c, after):
    chunks, sheets, rows, _ = c.shape
    pairs = sheets * rows // LANES
    steps = chunks * LANES // SUBLANES // Y_PARTS
    stored = shape_of(steps, Y_PARTS * pairs, SUBLANES, LANES)
    return pl.pallas_call(
        y_factor_kernel,
        in_specs=[IN_VMEM, ANYWHERE],
        out_shape=[
            stored,
            stored,
            stored,
            shape_of(Y_PARTS - 1, 3, pairs, SUBLANES, LANES),
            shape_of(SUBLANES - 1, 3, pairs, LANES),
            shape_of(len(COEFS), pairs, LANES),
        ],
        scratch_shapes=[
            pltpu.VMEM((pairs, chunks * LANES, LANES), F32),
            pltpu.VMEM((len(COEFS), pairs * SUBLANES, LANES), F32),
        ],
        compiler_params=params(),
        cost_estimate=pl.CostEstimate(flops=20 * c.size, bytes_accessed=16 * c.size, transcendentals=0),
    )(c, after)


def z_factor_kernel(c_ref, after, w_ref, i_ref):
    sheets = c_ref.shape[1]
    ground = 1.0
    for z in range(sheets - 1):
        face = c_ref[:, z] + c_ref[:, z + 1]
        inv = inverse(ground + face)
        w = face * inv
        i_ref[z] = inv
        w_ref[z] = w
        ground = 1.0 + w * ground
    i_ref[sheets - 1] = inverse(ground)


def z_factor(c, after):
    chunks, sheets, rows, _ = c.shape
    return pl.pallas_call(
        z_factor_kernel,
        in_specs=[IN_VMEM, ANYWHERE],
        out_shape=[
            shape_of(sheets - 1, chunks, rows, LANES),
            shape_of(sheets, chunks, rows, LANES),
        ],
        compiler_params=params(),
        cost_estimate=pl.CostEstimate(flops=10 * c.size, bytes_accessed=12 * c.size, transcendentals=0),
    )(c, after)


def y_target_kernel(stages, *refs):
    own, got = refs[:2]
    ties = refs[2 : 1 + stages]
    xw, xh, xm, xp, x_links, x_own, t_ref, yw, yi, yp, inner, outer, view = refs[1 + stages : 14 + stages]
    h_ref, inner_own, outer_own, send = refs[14 + stages : 18 + stages]
    f_s, g_s, y_s, q_s = refs[18 + stages :]
    chunks, sheets, rows, _ = g_s.shape
    lines = chunks * sheets
    x_steps = rows // SUBLANES

    low, high = block_ends("gx", own, got, ties)
    levels = [
        [(x_own[o + n], x_links[o + n, 1], x_links[o + n, 2]) for n in range(count)]
        for o, count in node_offsets(SUBLANES)
    ]
    for s, ends in enumerate(descend(levels, low, high)):
        for i in range(2):
            f_s[i, pl.ds(s, lines, stride=SUBLANES), :] = ends[i]
    first = 0
    for n, members in enumerate(line_groups(chunks, sheets)):
        at = slice(first, first + len(members))
        h_ref_of, h_at = (xh, at) if n == 0 else (xm, slice(first - 2 * sheets, at.stop - 2 * sheets))
        low, value = (
            jnp.stack(
                [f_s[i, j * SUBLANES : (j + 1) * SUBLANES, :] for j in range(at.start, at.stop)], 0
            )
            for i in range(2)
        )
        for k in range(x_steps - 1, -1, -1):
            value = xw[k, at] * value + (h_ref_of[k, h_at] + xp[k, at] * low)
            for j, (y, z) in enumerate(members):
                g_s[y, z, pl.ds(k, SUBLANES, stride=x_steps), :] = value[j]
        first = at.stop

    each = LANES // rows
    pairs = sheets // each
    span = chunks * LANES // SUBLANES
    steps = span // Y_PARTS
    for m in range(pairs):
        for y in range(chunks):
            block = jnp.concatenate(
                [g_s[y, m * each + i] - t_ref[m * each + i, :, part_of(y)] for i in range(each)], 0
            )
            y_s[m, y * LANES : (y + 1) * LANES, :] = block.T
    members = [(j, m) for j in range(Y_PARTS) for m in range(pairs)]

    def target(k):
        return jnp.stack([y_s[m, pl.ds(j * steps + k, SUBLANES, stride=span), :] for j, m in members], 0)

    def keep(k, h):
        h_ref[k] = h

    ends = eliminate(target, steps, lambda k: yw[k], lambda k: yi[k], lambda k: yp[k], keep)
    items = [tuple(v[j * pairs : (j + 1) * pairs] for v in ends) for j in range(Y_PARTS)]
    for offset, count in node_offsets(Y_PARTS):
        joined = []
        for n in range(count):
            tie = tuple(inner[offset + n, i] for i in range(3))
            both, flux = join_targets(items[2 * n], items[2 * n + 1], tie)
            inner_own[offset + n] = flux
            joined.append(both)
        items = joined
    for q in range(2):
        for m in range(pairs):
            q_s[q, m * SUBLANES : (m + 1) * SUBLANES, :] = items[0][q][m]
    items = [
        tuple(q_s[q, pl.ds(s, pairs, stride=SUBLANES), :] for q in range(2)) for s in range(SUBLANES)
    ]
    for offset, count in node_offsets(SUBLANES):
        joined = []
        for n in range(count):
            tie = tuple(outer[offset + n, i] for i in range(3))
            both, flux = join_targets(items[2 * n], items[2 * n + 1], tie)
            outer_own[offset + n] = flux
            joined.append(both)
        items = joined
    for n, q in enumerate(COEFS):
        send[q] = view[n]
    send[FIRST], send[LAST] = items[0]


def y_target(own, got, ties, xw, xh, xm, xp, x_links, x_own, t, yw, yi, yp, inner, outer, view):
    sheets, rows, columns = t.shape
    chunks = columns // LANES
    lines = chunks * sheets
    pairs = sheets * rows // LANES
    return pl.pallas_call(
        functools.partial(y_target_kernel, len(ties) + 1),
        out_shape=[
            shape_of(*yw.shape),
            shape_of(Y_PARTS - 1, pairs, SUBLANES, LANES),
            shape_of(SUBLANES - 1, pairs, LANES),
            shape_of(7, pairs, LANES),
        ],
        scratch_shapes=[
            pltpu.VMEM((2, lines * SUBLANES, LANES), F32),
            pltpu.VMEM((chunks, sheets, rows, LANES), F32),
            pltpu.VMEM((pairs, chunks * LANES, LANES), F32),
            pltpu.VMEM((2, pairs * SUBLANES, LANES), F32),
        ],
        compiler_params=params(),
    )(own, got, *ties, xw, xh, xm, xp, x_links, x_own, t, yw, yi, yp, inner, outer, view)


def finish_kernel(stages, *refs):
    own, got = refs[:2]
    ties = refs[2 : 1 + stages]
    yw, yh, yp, inner, inner_own, outer, outer_own, zw, zi, t_ref = refs[1 + stages : 11 + stages]
    out, e_s, u_s, o_s, sems = refs[11 + stages :]
    chunks, sheets, rows, _ = o_s.shape
    each = LANES // rows
    pairs = sheets // each
    steps = yw.shape[0]
    span = chunks * LANES // SUBLANES

    low, high = block_ends("gy", own, got, ties)
    levels = [
        [(outer_own[o + n], outer[o + n, 1], outer[o + n, 2]) for n in range(count)]
        for o, count in node_offsets(SUBLANES)
    ]
    for s, ends in enumerate(descend(levels, low, high)):
        for i in range(2):
            e_s[i, pl.ds(s, pairs, stride=SUBLANES), :] = ends[i]
    low, high = (
        jnp.stack([e_s[i, m * SUBLANES : (m + 1) * SUBLANES, :] for m in range(pairs)], 0)
        for i in range(2)
    )
    levels = [
        [(inner_own[o + n], inner[o + n, 1], inner[o + n, 2]) for n in range(count)]
        for o, count in node_offsets(Y_PARTS)
    ]
    ends = descend(levels, low, high)
    low = jnp.concatenate([e[0] for e in ends], 0)
    value = jnp.concatenate([e[1] for e in ends], 0)
    members = [(j, m) for j in range(Y_PARTS) for m in range(pairs)]
    for k in range(steps - 1, -1, -1):
        value = yw[k] * value + (yh[k] + yp[k] * low)
        for n, (j, m) in enumerate(members):
            u_s[m, pl.ds(j * steps + k, SUBLANES, stride=span), :] = value[n]

    copies = []
    for y in range(chunks):
        part = part_of(y)
        turned = [u_s[m, part, :].T for m in range(pairs)]
        for half in range(2):
            at = slice(half * rows // 2, (half + 1) * rows // 2)
            rhs, kept = None, []
            for z in range(sheets):
                first = (z % each) * rows + at.start
                own_rhs = turned[z // each][first : first + rows // 2, :]
                rhs = own_rhs if z == 0 else own_rhs + zw[z - 1, y, at, :] * rhs
                kept.append(rhs * zi[z, y, at, :])
            value = kept[-1]
            o_s[y, sheets - 1, at, :] = t_ref[sheets - 1, at, part] + value
            for z in range(sheets - 2, -1, -1):
                value = zw[z, y, at, :] * value + kept[z]
                o_s[y, z, at, :] = t_ref[z, at, part] + value
            strip = pl.ds(at.start, rows // 2)
            copy = pltpu.make_async_copy(
                o_s.at[y, :, strip, :], out.at[:, strip, pl.ds(y * LANES, LANES)], sems.at[y, half]
            )
            copy.start()
            copies.append(copy)
    for copy in copies:
        copy.wait()


def finish(own, got, ties, yw, yh, yp, inner, inner_own, outer, outer_own, zw, zi, t):
    sheets, rows, columns = t.shape
    chunks = columns // LANES
    pairs = sheets * rows // LANES
    return pl.pallas_call(
        functools.partial(finish_kernel, len(ties) + 1),
        out_shape=shape_of(sheets, rows, chunks * LANES),
        out_specs=ANYWHERE,
        scratch_shapes=[
            pltpu.VMEM((2, pairs * SUBLANES, LANES), F32),
            pltpu.VMEM((pairs, chunks * LANES, LANES), F32),
            pltpu.VMEM((chunks, sheets, rows, LANES), F32),
            pltpu.SemaphoreType.DMA((chunks, 2)),
        ],
        compiler_params=params(),
    )(own, got, *ties, yw, yh, yp, inner, inner_own, outer, outer_own, zw, zi, t)


def per_device(temperature, base, locations, energy):
    columns = temperature.shape[2]
    gy = lax.axis_size("gy")
    loc, heat, packed = edges(temperature, base, locations[None], energy[None])
    near = swap(packed, "gy", 1)
    t, b = load(temperature, base, packed)
    near, t, b = lax.optimization_barrier((near, t, b))
    far = [swap(near, "gy", 2)] if gy > 2 else []
    if gy > 4:
        far.append(lax.ppermute(near, "gy", [(i, (i + 2 ^ 2) - 2) for i in range(2, gy - 2)]))
    c, total, xw, xi, xp, x_links, x_view, xm, ends = x_factor(loc, heat, t, b, columns * gy, near)
    xh, x_own, view = x_target(packed, t, total, [near] + far, xw, xi, xp, x_links, x_view, ends)
    yw, yi, yp, inner, outer, y_view = y_factor(c, x_view)
    zw, zi = z_factor(c, view)
    own, got, ties = gather_line(view, "gx", 2, (y_view, zw))
    yh, inner_own, outer_own, view = y_target(
        own, got, ties, xw, xh, xm, xp, x_links, x_own, t, yw, yi, yp, inner, outer, y_view
    )
    own, got, ties = gather_line(view, "gy")
    return finish(own, got, ties, yw, yh, yp, inner, inner_own, outer, outer_own, zw, zi, t)


def solution(mesh):
    in_specs = (P(None, "gx", "gy"), P(None, "gx", "gy"), P(), P())
    out_specs = P(None, "gx", "gy")
    return jax.shard_map(
        per_device, mesh=mesh, in_specs=in_specs, out_specs=out_specs, check_vma=False
    )
```

```python
import functools

import jax
import jax.numpy as jnp
from jax import lax
from jax.experimental import pallas as pl
from jax.experimental.pallas import tpu as pltpu
from jax.sharding import PartitionSpec as P

RATE = 2000.0
THERMAL_GROWTH = 0.8
LANES = 128
SUBLANES = 8
Y_PARTS = 4
OUT_COPIES = 4
F32 = jnp.float32
MIB = 1024 * 1024
ANYWHERE = pl.BlockSpec(memory_space=pl.ANY)
IN_HBM = pl.BlockSpec(memory_space=pltpu.HBM)
IN_VMEM = pl.BlockSpec(memory_space=pltpu.VMEM)

R00, R0L, RLL, FIRST, LAST, C0, CL = range(7)
COEFS = (R00, R0L, RLL, C0, CL)


def params(limit=40):
    return pltpu.CompilerParams(vmem_limit_bytes=limit * MIB)


def shape_of(*sizes):
    return jax.ShapeDtypeStruct(sizes, F32)


def half_conduct(base, temperature):
    return base * (0.5 * RATE + (0.5 * RATE * THERMAL_GROWTH) * temperature)


def inverse(x):
    guess = pl.reciprocal(x, approx=True)
    return guess * (2.0 - x * guess)


def join_coefs(a, b):
    face = a[CL] + b[C0]
    inv = face * inverse(1.0 + face * (a[RLL] + b[R00]))
    left = a[R0L] * inv
    right = b[R0L] * inv
    joined = {
        R00: a[R00] - left * a[R0L],
        R0L: left * b[R0L],
        RLL: b[RLL] - right * b[R0L],
        C0: a[C0],
        CL: b[CL],
    }
    return joined, (inv, right, left)


def join_targets(a, b, links):
    inv, right, left = links
    jump = b[0] - a[1]
    return (a[0] + left * jump, b[1] - right * jump), jump * inv


def between(own, right, left, low, high):
    return own + right * high - left * low


def tree(items, join):
    levels = []
    while len(items) > 1:
        pairs = [join(items[i], items[i + 1]) for i in range(0, len(items), 2)]
        items = [p[0] for p in pairs]
        levels.append([p[1] for p in pairs])
    return items[0], levels


def descend(levels, low, high):
    ends = [(low, high)]
    for level in reversed(levels):
        below = []
        for (lo, hi), (own, right, left) in zip(ends, level):
            flux = between(own, right, left, lo, hi)
            below += [(lo, flux), (-flux, hi)]
        ends = below
    return ends


def node_offsets(leaves):
    offsets, at, count = [], 0, leaves // 2
    while count:
        offsets.append((at, count))
        at += count
        count //= 2
    return offsets


def factor(cond, steps, keep):
    here = cond(0)
    c_first = here
    one = jnp.ones_like(here)
    ground, path, first_first = one, one, None
    for k in range(steps - 1):
        following = cond(k + 1)
        face = here + following
        inv = inverse(ground + face)
        w = face * inv
        p = path * inv
        keep(k, w, inv, p)
        step = path * p
        first_first = step if first_first is None else first_first + step
        path = path * w
        ground = 1.0 + w * ground
        here = following
    inv = inverse(ground)
    p = path * inv
    keep(steps - 1, inv, inv, p)
    return {R00: first_first + path * p, R0L: p, RLL: inv, C0: c_first, CL: here}


def eliminate(target, steps, w, inv, p, keep):
    rhs = target(0)
    first = None
    for k in range(steps):
        h = rhs * inv(k)
        keep(k, h)
        step = rhs * p(k)
        first = step if first is None else first + step
        if k < steps - 1:
            rhs = target(k + 1) + w(k) * rhs
    return first, h


def is_odd(axis):
    return lax.axis_index(axis) % 2 == 1


def edges_kernel(t_hbm, b_hbm, packed, t_s, b_s, sems):
    sheets, rows, columns = t_hbm.shape
    sides = []
    for side, start in enumerate((0, columns - LANES)):
        sides.append(
            [
                pltpu.make_async_copy(src.at[:, :, pl.ds(start, LANES)], dst.at[side], sems.at[i, side])
                for i, (src, dst) in enumerate(((t_hbm, t_s), (b_hbm, b_s)))
            ]
        )
        for copy in sides[-1]:
            copy.start()
    lane = lax.broadcasted_iota(jnp.int32, (rows, LANES), 1)
    total = jnp.zeros((rows, LANES), F32)
    for side, source in enumerate((0, LANES - 1)):
        for copy in sides[side]:
            copy.wait()
        for z in range(sheets):
            t = t_s[side, z]
            c = half_conduct(b_s[side, z], t)
            place = 2 * sheets * side + z
            total = jnp.where(lane == place, t[:, source : source + 1], total)
            total = jnp.where(lane == place + sheets, c[:, source : source + 1], total)
    packed[...] = total


def edges(temperature, base):
    sheets, rows, _ = temperature.shape
    return pl.pallas_call(
        edges_kernel,
        in_specs=[IN_HBM] * 2,
        out_shape=pltpu.VMEM((rows, LANES), F32),
        scratch_shapes=[
            pltpu.VMEM((2, sheets, rows, LANES), F32),
            pltpu.VMEM((2, sheets, rows, LANES), F32),
            pltpu.SemaphoreType.DMA((2, 2)),
        ],
        compiler_params=params(),
    )(*[pltpu.with_memory_space_constraint(v, pltpu.HBM) for v in (temperature, base)])


def load_kernel(*refs):
    count = len(refs) // 2 - 1
    sems = refs[-1]
    copies = [
        pltpu.make_async_copy(refs[i], refs[count + 1 + i], sems.at[i]) for i in range(count)
    ]
    for copy in copies:
        copy.start()
    for copy in copies:
        copy.wait()


def load(values, after):
    return pl.pallas_call(
        load_kernel,
        in_specs=[IN_HBM] * len(values) + [ANYWHERE],
        out_shape=[pltpu.VMEM(v.shape, v.dtype) for v in values],
        scratch_shapes=[pltpu.SemaphoreType.DMA((len(values),))],
        compiler_params=params(),
        cost_estimate=pl.CostEstimate(
            flops=0, bytes_accessed=16 * values[0].size, transcendentals=0
        ),
    )(*[pltpu.with_memory_space_constraint(v, pltpu.HBM) for v in values], after)


def source_plane(loc, energy, rows, columns, plate):
    place = loc[...]
    count = place.shape[1]
    local_x = place // plate - lax.axis_index("gx") * rows
    local_y = place % plate - lax.axis_index("gy") * columns
    in_x = lax.broadcasted_iota(jnp.int32, (rows, count), 0) == local_x
    in_y = lax.broadcasted_iota(jnp.int32, (columns, count), 0) == local_y
    by_y = jnp.where(in_y, 1.0, 0.0).astype(jnp.bfloat16)
    left = energy[...]
    plane = None
    for _ in range(3):
        part = left.astype(jnp.bfloat16).astype(F32)
        left = left - part
        term = lax.dot_general(
            jnp.where(in_x, part, 0.0).astype(jnp.bfloat16),
            by_y,
            (((1,), (1,)), ((), ())),
            preferred_element_type=F32,
        )
        plane = term if plane is None else plane + term
    return plane


def part_of(y):
    return slice(y * LANES, (y + 1) * LANES)


def line_groups(chunks, sheets):
    order = [0, chunks - 1] + list(range(1, chunks - 1))
    return [[(y, z) for y in order[i : i + 2] for z in range(sheets)] for i in range(0, chunks, 2)]


def x_eliminate(field, members, first_line, w_ref, i_ref, p_ref, h_ref, h_line, q_s):
    steps = w_ref.shape[0]
    at = slice(first_line, first_line + len(members))
    kept_at = slice(h_line, h_line + len(members))

    def target(k):
        return jnp.stack([field(y, z)[pl.ds(k, SUBLANES, stride=steps), :] for y, z in members], 0)

    def keep(k, h):
        h_ref[k, kept_at] = h

    ends = eliminate(
        target, steps, lambda k: w_ref[k, at], lambda k: i_ref[k, at], lambda k: p_ref[k, at], keep
    )
    for q in range(2):
        for i in range(len(members)):
            first = (first_line + i) * SUBLANES
            q_s[q, first : first + SUBLANES, :] = ends[q][i]


def x_factor_kernel(plate, loc, energy, t_ref, b_ref, after, *refs):
    c_ref, total_ref, w_ref, i_ref, p_ref, links, view, h_ref, ends_ref, q_s = refs
    chunks, sheets, rows, _ = c_ref.shape
    lines = chunks * sheets
    steps = rows // SUBLANES
    plane = source_plane(loc, energy, rows, chunks * LANES, plate)

    lane = lax.broadcasted_iota(jnp.int32, (SUBLANES, LANES), 1)
    is_first, is_last = lane == 0, lane == LANES - 1
    for r in range(steps):
        at = slice(r * SUBLANES, (r + 1) * SUBLANES)
        before_t, before_c = None, None
        for z in range(sheets):
            ts = [t_ref[z, at, part_of(y)] for y in range(chunks)]
            cs = [half_conduct(b_ref[z, at, part_of(y)], ts[y]) for y in range(chunks)]
            t_turned = [pltpu.roll(v, LANES - 1, 1) for v in ts]
            c_turned = [pltpu.roll(v, LANES - 1, 1) for v in cs]
            flux = []
            for y in range(chunks):
                if y < chunks - 1:
                    t_next = jnp.where(is_last, t_turned[y + 1], t_turned[y])
                    c_next = jnp.where(is_last, c_turned[y + 1], c_turned[y])
                    flux.append((cs[y] + c_next) * (t_next - ts[y]))
                else:
                    inside = (cs[y] + c_turned[y]) * (t_turned[y] - ts[y])
                    flux.append(jnp.where(is_last, 0.0, inside))
            turned = [pltpu.roll(v, 1, 1) for v in flux]
            for y in range(chunks):
                from_low = jnp.where(is_first, turned[y - 1] if y else 0.0, turned[y])
                total = ts[y] + (flux[y] - from_low)
                if z == 0:
                    total = total + plane[at, part_of(y)]
                else:
                    across = (before_c[y] + cs[y]) * (ts[y] - before_t[y])
                    total = total - across
                    total_ref[y, z - 1, at, :] += across
                total_ref[y, z, at, :] = total
                c_ref[y, z, at, :] = cs[y]
            before_t, before_c = ts, cs

    at = 0
    for n, members in enumerate(line_groups(chunks, sheets)):

        def cond(k):
            return jnp.stack([c_ref[y, z, pl.ds(k, SUBLANES, stride=steps), :] for y, z in members], 0)

        def keep(k, w, inv, p):
            w_ref[k, at : at + len(members)] = w
            i_ref[k, at : at + len(members)] = inv
            p_ref[k, at : at + len(members)] = p

        block = factor(cond, steps, keep)
        for i, q in enumerate(COEFS):
            for j in range(len(members)):
                first = (at + j) * SUBLANES
                q_s[i, first : first + SUBLANES, :] = block[q][j]
        if n > 0:
            x_eliminate(
                lambda y, z: total_ref.at[y, z], members, at, w_ref, i_ref, p_ref, h_ref,
                at - 2 * sheets, ends_ref,
            )
        at += len(members)

    segments = [
        {q: q_s[n, pl.ds(s, lines, stride=SUBLANES), :] for n, q in enumerate(COEFS)}
        for s in range(SUBLANES)
    ]
    whole, levels = tree(segments, join_coefs)
    for (offset, _), level in zip(node_offsets(SUBLANES), levels):
        for n, values in enumerate(level):
            for i in range(3):
                links[offset + n, i] = values[i]
    for n, q in enumerate(COEFS):
        view[n] = whole[q]


def x_factor(loc, energy, t, b, plate, after):
    sheets, rows, columns = t.shape
    chunks = columns // LANES
    lines = chunks * sheets
    steps = rows // SUBLANES
    field = shape_of(chunks, sheets, rows, LANES)
    stored = shape_of(steps, lines, SUBLANES, LANES)
    return pl.pallas_call(
        functools.partial(x_factor_kernel, plate),
        in_specs=[IN_VMEM] * 4 + [ANYWHERE],
        out_shape=[
            field,
            field,
            stored,
            stored,
            stored,
            shape_of(SUBLANES - 1, 3, lines, LANES),
            shape_of(len(COEFS), lines, LANES),
            shape_of(steps, max(1, lines - 2 * sheets), SUBLANES, LANES),
            shape_of(2, lines * SUBLANES, LANES),
        ],
        scratch_shapes=[pltpu.VMEM((len(COEFS), lines * SUBLANES, LANES), F32)],
        compiler_params=params(),
        cost_estimate=pl.CostEstimate(flops=40 * t.size, bytes_accessed=28 * t.size, transcendentals=0),
    )(loc, energy, t, b, after)


def far_side(sources):
    place = lax.axis_index("gy")
    paired = (place >> 1) % 2 != place % 2
    nothing = jnp.zeros(sources[0].shape, F32)
    by_pair = sources[1][...] if len(sources) > 1 else nothing
    other = sources[2][...] if len(sources) > 2 else nothing
    return jnp.where(paired, by_pair, other)


def x_target_kernel(count, own_cells, t_ref, total_ref, *refs):
    w_ref, i_ref, p_ref, links, view, ends_ref, h_ref, own, send, e_s, q_s = refs[count:]
    chunks, sheets, rows, _ = total_ref.shape
    lines = chunks * sheets

    near, far = refs[0][...], far_side(refs[:count])
    before = jnp.where(is_odd("gy"), near, far)
    after = jnp.where(is_odd("gy"), far, near)
    lane = lax.broadcasted_iota(jnp.int32, (rows, LANES), 1)
    side = 2 * sheets
    beyond = jnp.where(lane < side, pltpu.roll(before, LANES - side, 1), pltpu.roll(after, side, 1))
    mine = own_cells[...]
    face = jnp.where(beyond > 0.0, mine + beyond, 0.0)
    flux = pltpu.roll(face, LANES - sheets, 1) * (beyond - mine)
    for n, (y, edge) in enumerate(((0, 0), (chunks - 1, LANES - 1))):
        for z in range(sheets):
            at = n * side + z
            e_s[n, z] = total_ref[y, z] + jnp.where(lane == edge, flux[:, at : at + 1], 0.0)

    members = line_groups(chunks, sheets)[0]
    x_eliminate(
        lambda y, z: e_s.at[0 if y == 0 else 1, z], members, 0, w_ref, i_ref, p_ref, h_ref, 0, q_s
    )
    split = len(members)
    items = [
        tuple(
            jnp.concatenate(
                [
                    q_s[q, pl.ds(s, split, stride=SUBLANES), :],
                    ends_ref[q, pl.ds(split * SUBLANES + s, lines - split, stride=SUBLANES), :],
                ],
                0,
            )
            for q in range(2)
        )
        for s in range(SUBLANES)
    ]
    for offset, count in node_offsets(SUBLANES):
        joined = []
        for n in range(count):
            ties = tuple(links[offset + n, i] for i in range(3))
            both, flux = join_targets(items[2 * n], items[2 * n + 1], ties)
            own[offset + n] = flux
            joined.append(both)
        items = joined
    for n, q in enumerate(COEFS):
        send[q] = view[n]
    send[FIRST], send[LAST] = items[0]


def x_target(own_cells, t, total, edge_cells, w, inv, p, links, view, ends):
    chunks, sheets, rows, _ = total.shape
    lines = chunks * sheets
    steps = rows // SUBLANES
    return pl.pallas_call(
        functools.partial(x_target_kernel, len(edge_cells)),
        out_shape=[
            shape_of(steps, 2 * sheets, SUBLANES, LANES),
            shape_of(SUBLANES - 1, lines, LANES),
            shape_of(7, lines, LANES),
        ],
        scratch_shapes=[
            pltpu.VMEM((2, sheets, rows, LANES), F32),
            pltpu.VMEM((2, 2 * sheets * SUBLANES, LANES), F32),
        ],
        compiler_params=params(),
    )(own_cells, t, total, *edge_cells, w, inv, p, links, view, ends)


def stages_of(axis):
    return lax.axis_size(axis).bit_length() - 1


def swap(value, axis, flip):
    count = lax.axis_size(axis)
    return lax.ppermute(value, axis, [(i, i ^ flip) for i in range(count)])


def on_right(axis, stage):
    return (lax.axis_index(axis) >> stage) % 2 == 1


def toward(right, block):
    return (
        jnp.where(right, block[R00], block[RLL]),
        jnp.where(right, block[FIRST], block[LAST]),
        jnp.where(right, block[C0], block[CL]),
    )


def join(a, b):
    joined, ties = join_coefs(a, b)
    (joined[FIRST], joined[LAST]), flux = join_targets((a[FIRST], a[LAST]), (b[FIRST], b[LAST]), ties)
    return joined, (flux, ties[1], ties[2])


def ordered(right, own, other):
    first = [jnp.where(right, theirs, mine) for mine, theirs in zip(own, other)]
    second = [jnp.where(right, mine, theirs) for mine, theirs in zip(own, other)]
    return first, second


def join_kernel(axis, stage, width, last, *refs):
    count = 1 << width
    blocks = [[refs[-i % count][q] for q in range(7)] for i in range(count)]
    send = refs[-1 - width]
    links = refs[-width:]
    for bit in range(width):
        right = on_right(axis, stage + bit)
        for i in range(count):
            if not i >> bit & 1:
                j = i | 1 << bit
                blocks[i], blocks[j] = ordered(right, blocks[i], blocks[j])
    for bit in range(width):
        pairs = [join(blocks[i], blocks[i + 1]) for i in range(0, len(blocks), 2)]
        blocks = [p[0] for p in pairs]
        ties = [p[1] for p in pairs]
        for upper in range(bit + 1, width):
            right = on_right(axis, stage + upper)
            ties = [
                tuple(jnp.where(right, v, u) for u, v in zip(ties[i], ties[i + 1]))
                for i in range(0, len(ties), 2)
            ]
        for i in range(3):
            links[bit][i] = ties[0][i]
    (whole,) = blocks
    if last:
        for n, value in enumerate(toward(on_right(axis, stage + width), whole)):
            send[n] = value
    else:
        for q in range(7):
            send[q] = whole[q]


def join_stage(own, got, axis, stage, width, last, after):
    lines = own.shape[1]
    return pl.pallas_call(
        functools.partial(join_kernel, axis, stage, width, last),
        in_specs=[IN_VMEM] * (1 + len(got)) + [ANYWHERE] * len(after),
        out_shape=[shape_of(3 if last else 7, lines, LANES)] + [shape_of(3, lines, LANES)] * width,
        compiler_params=params(),
    )(own, *got, *after)


def gather_line(view, axis, widest=1, meanwhile=()):
    stages = stages_of(axis)
    links, stage = [], 0
    while stage < stages - 1:
        width = min(widest, stages - 1 - stage)
        got = [swap(view, axis, flip << stage) for flip in range((1 << width) - 1, 0, -1)]
        last = stage + width == stages - 1
        view, *ties = join_stage(view, got, axis, stage, width, last, meanwhile)
        links += ties
        stage += width
        meanwhile = ()
    return view, swap(view, axis, 1 << stage), links


def block_ends(axis, own, got, links):
    top = len(links)
    right = on_right(axis, top)
    face = own[2] + got[2]
    jump = jnp.where(right, own[1] - got[1], got[1] - own[1])
    flux = jump * face * inverse(1.0 + face * (own[0] + got[0]))
    low = jnp.where(right, -flux, 0.0)
    high = jnp.where(right, 0.0, flux)
    for stage in range(top - 1, -1, -1):
        tie = links[stage]
        right = on_right(axis, stage)
        flux = between(tie[0], tie[1], tie[2], low, high)
        low, high = jnp.where(right, -flux, low), jnp.where(right, high, flux)
    return low, high


def y_factor_kernel(c_ref, after, w_ref, i_ref, p_ref, inner, outer, view, c_s, q_s):
    chunks, sheets, rows, _ = c_ref.shape
    each = LANES // rows
    pairs = sheets // each
    span = chunks * LANES // SUBLANES
    steps = span // Y_PARTS
    for m in range(pairs):
        for y in range(chunks):
            block = jnp.concatenate([c_ref[y, m * each + i] for i in range(each)], 0)
            c_s[m, y * LANES : (y + 1) * LANES, :] = block.T

    members = [(j, m) for j in range(Y_PARTS) for m in range(pairs)]

    def cond(k):
        return jnp.stack([c_s[m, pl.ds(j * steps + k, SUBLANES, stride=span), :] for j, m in members], 0)

    def keep(k, w, inv, p):
        w_ref[k] = w
        i_ref[k] = inv
        p_ref[k] = p

    block = factor(cond, steps, keep)
    parts = [{q: block[q][j * pairs : (j + 1) * pairs] for q in COEFS} for j in range(Y_PARTS)]
    whole, levels = tree(parts, join_coefs)
    for (offset, _), level in zip(node_offsets(Y_PARTS), levels):
        for n, values in enumerate(level):
            for i in range(3):
                inner[offset + n, i] = values[i]
    for n, q in enumerate(COEFS):
        for m in range(pairs):
            q_s[n, m * SUBLANES : (m + 1) * SUBLANES, :] = whole[q][m]
    segments = [
        {q: q_s[n, pl.ds(s, pairs, stride=SUBLANES), :] for n, q in enumerate(COEFS)}
        for s in range(SUBLANES)
    ]
    whole, levels = tree(segments, join_coefs)
    for (offset, _), level in zip(node_offsets(SUBLANES), levels):
        for n, values in enumerate(level):
            for i in range(3):
                outer[offset + n, i] = values[i]
    for n, q in enumerate(COEFS):
        view[n] = whole[q]


def y_factor(c, after):
    chunks, sheets, rows, _ = c.shape
    pairs = sheets * rows // LANES
    steps = chunks * LANES // SUBLANES // Y_PARTS
    stored = shape_of(steps, Y_PARTS * pairs, SUBLANES, LANES)
    return pl.pallas_call(
        y_factor_kernel,
        in_specs=[IN_VMEM, ANYWHERE],
        out_shape=[
            stored,
            stored,
            stored,
            shape_of(Y_PARTS - 1, 3, pairs, SUBLANES, LANES),
            shape_of(SUBLANES - 1, 3, pairs, LANES),
            shape_of(len(COEFS), pairs, LANES),
        ],
        scratch_shapes=[
            pltpu.VMEM((pairs, chunks * LANES, LANES), F32),
            pltpu.VMEM((len(COEFS), pairs * SUBLANES, LANES), F32),
        ],
        compiler_params=params(),
        cost_estimate=pl.CostEstimate(flops=20 * c.size, bytes_accessed=16 * c.size, transcendentals=0),
    )(c, after)


def z_factor_kernel(c_ref, after, w_ref, i_ref):
    sheets = c_ref.shape[1]
    ground = 1.0
    for z in range(sheets - 1):
        face = c_ref[:, z] + c_ref[:, z + 1]
        inv = inverse(ground + face)
        w = face * inv
        i_ref[z] = inv
        w_ref[z] = w
        ground = 1.0 + w * ground
    i_ref[sheets - 1] = inverse(ground)


def z_factor(c, after):
    chunks, sheets, rows, _ = c.shape
    return pl.pallas_call(
        z_factor_kernel,
        in_specs=[IN_VMEM, ANYWHERE],
        out_shape=[
            shape_of(sheets - 1, chunks, rows, LANES),
            shape_of(sheets, chunks, rows, LANES),
        ],
        compiler_params=params(),
        cost_estimate=pl.CostEstimate(flops=10 * c.size, bytes_accessed=12 * c.size, transcendentals=0),
    )(c, after)


def y_target_kernel(stages, *refs):
    own, got = refs[:2]
    ties = refs[2 : 1 + stages]
    xw, xh, xm, xp, x_links, x_own, t_ref, yw, yi, yp, inner, outer, view = refs[1 + stages : 14 + stages]
    h_ref, inner_own, outer_own, send = refs[14 + stages : 18 + stages]
    f_s, g_s, y_s, q_s = refs[18 + stages :]
    chunks, sheets, rows, _ = g_s.shape
    lines = chunks * sheets
    x_steps = rows // SUBLANES

    low, high = block_ends("gx", own, got, ties)
    levels = [
        [(x_own[o + n], x_links[o + n, 1], x_links[o + n, 2]) for n in range(count)]
        for o, count in node_offsets(SUBLANES)
    ]
    for s, ends in enumerate(descend(levels, low, high)):
        for i in range(2):
            f_s[i, pl.ds(s, lines, stride=SUBLANES), :] = ends[i]
    first = 0
    for n, members in enumerate(line_groups(chunks, sheets)):
        at = slice(first, first + len(members))
        h_ref_of, h_at = (xh, at) if n == 0 else (xm, slice(first - 2 * sheets, at.stop - 2 * sheets))
        low, value = (
            jnp.stack(
                [f_s[i, j * SUBLANES : (j + 1) * SUBLANES, :] for j in range(at.start, at.stop)], 0
            )
            for i in range(2)
        )
        for k in range(x_steps - 1, -1, -1):
            value = xw[k, at] * value + (h_ref_of[k, h_at] + xp[k, at] * low)
            for j, (y, z) in enumerate(members):
                g_s[y, z, pl.ds(k, SUBLANES, stride=x_steps), :] = value[j]
        first = at.stop

    each = LANES // rows
    pairs = sheets // each
    span = chunks * LANES // SUBLANES
    steps = span // Y_PARTS
    for m in range(pairs):
        for y in range(chunks):
            block = jnp.concatenate(
                [g_s[y, m * each + i] - t_ref[m * each + i, :, part_of(y)] for i in range(each)], 0
            )
            y_s[m, y * LANES : (y + 1) * LANES, :] = block.T
    members = [(j, m) for j in range(Y_PARTS) for m in range(pairs)]

    def target(k):
        return jnp.stack([y_s[m, pl.ds(j * steps + k, SUBLANES, stride=span), :] for j, m in members], 0)

    def keep(k, h):
        h_ref[k] = h

    ends = eliminate(target, steps, lambda k: yw[k], lambda k: yi[k], lambda k: yp[k], keep)
    items = [tuple(v[j * pairs : (j + 1) * pairs] for v in ends) for j in range(Y_PARTS)]
    for offset, count in node_offsets(Y_PARTS):
        joined = []
        for n in range(count):
            tie = tuple(inner[offset + n, i] for i in range(3))
            both, flux = join_targets(items[2 * n], items[2 * n + 1], tie)
            inner_own[offset + n] = flux
            joined.append(both)
        items = joined
    for q in range(2):
        for m in range(pairs):
            q_s[q, m * SUBLANES : (m + 1) * SUBLANES, :] = items[0][q][m]
    items = [
        tuple(q_s[q, pl.ds(s, pairs, stride=SUBLANES), :] for q in range(2)) for s in range(SUBLANES)
    ]
    for offset, count in node_offsets(SUBLANES):
        joined = []
        for n in range(count):
            tie = tuple(outer[offset + n, i] for i in range(3))
            both, flux = join_targets(items[2 * n], items[2 * n + 1], tie)
            outer_own[offset + n] = flux
            joined.append(both)
        items = joined
    for n, q in enumerate(COEFS):
        send[q] = view[n]
    send[FIRST], send[LAST] = items[0]


def y_target(own, got, ties, xw, xh, xm, xp, x_links, x_own, t, yw, yi, yp, inner, outer, view):
    sheets, rows, columns = t.shape
    chunks = columns // LANES
    lines = chunks * sheets
    pairs = sheets * rows // LANES
    return pl.pallas_call(
        functools.partial(y_target_kernel, len(ties) + 1),
        out_shape=[
            shape_of(*yw.shape),
            shape_of(Y_PARTS - 1, pairs, SUBLANES, LANES),
            shape_of(SUBLANES - 1, pairs, LANES),
            shape_of(7, pairs, LANES),
        ],
        scratch_shapes=[
            pltpu.VMEM((2, lines * SUBLANES, LANES), F32),
            pltpu.VMEM((chunks, sheets, rows, LANES), F32),
            pltpu.VMEM((pairs, chunks * LANES, LANES), F32),
            pltpu.VMEM((2, pairs * SUBLANES, LANES), F32),
        ],
        compiler_params=params(),
    )(own, got, *ties, xw, xh, xm, xp, x_links, x_own, t, yw, yi, yp, inner, outer, view)


def finish_kernel(stages, *refs):
    own, got = refs[:2]
    ties = refs[2 : 1 + stages]
    yw, yh, yp, inner, inner_own, outer, outer_own, zw, zi, t_ref = refs[1 + stages : 11 + stages]
    out, e_s, u_s, n_s, o_s, sems = refs[11 + stages :]
    sheets, rows, columns = o_s.shape
    chunks = columns // LANES
    each = LANES // rows
    pairs = sheets // each
    steps = yw.shape[0]
    span = chunks * LANES // SUBLANES

    low, high = block_ends("gy", own, got, ties)
    levels = [
        [(outer_own[o + n], outer[o + n, 1], outer[o + n, 2]) for n in range(count)]
        for o, count in node_offsets(SUBLANES)
    ]
    for s, ends in enumerate(descend(levels, low, high)):
        for i in range(2):
            e_s[i, pl.ds(s, pairs, stride=SUBLANES), :] = ends[i]
    low, high = (
        jnp.stack([e_s[i, m * SUBLANES : (m + 1) * SUBLANES, :] for m in range(pairs)], 0)
        for i in range(2)
    )
    levels = [
        [(inner_own[o + n], inner[o + n, 1], inner[o + n, 2]) for n in range(count)]
        for o, count in node_offsets(Y_PARTS)
    ]
    ends = descend(levels, low, high)
    low = jnp.concatenate([e[0] for e in ends], 0)
    value = jnp.concatenate([e[1] for e in ends], 0)
    members = [(j, m) for j in range(Y_PARTS) for m in range(pairs)]
    for k in range(steps - 1, -1, -1):
        value = yw[k] * value + (yh[k] + yp[k] * low)
        for n, (j, m) in enumerate(members):
            u_s[m, pl.ds(j * steps + k, SUBLANES, stride=span), :] = value[n]

    for y in range(chunks):
        for m in range(pairs):
            turned = u_s[m, part_of(y), :].T
            for i in range(each):
                n_s[m * each + i, :, part_of(y)] = turned[i * rows : (i + 1) * rows, :]
    copies = []
    block = rows // OUT_COPIES
    for n in range(OUT_COPIES):
        at = slice(n * block, (n + 1) * block)
        for y in range(chunks):
            part = part_of(y)
            rhs, kept = None, []
            for z in range(sheets):
                own_rhs = n_s[z, at, part]
                rhs = own_rhs if z == 0 else own_rhs + zw[z - 1, y, at, :] * rhs
                kept.append(rhs * zi[z, y, at, :])
            value = kept[-1]
            o_s[sheets - 1, at, part] = t_ref[sheets - 1, at, part] + value
            for z in range(sheets - 2, -1, -1):
                value = zw[z, y, at, :] * value + kept[z]
                o_s[z, at, part] = t_ref[z, at, part] + value
        strip = pl.ds(at.start, block)
        copy = pltpu.make_async_copy(o_s.at[:, strip, :], out.at[:, strip, :], sems.at[n])
        copy.start()
        copies.append(copy)
    for copy in copies:
        copy.wait()


def finish(own, got, ties, yw, yh, yp, inner, inner_own, outer, outer_own, zw, zi, t):
    sheets, rows, columns = t.shape
    chunks = columns // LANES
    pairs = sheets * rows // LANES
    return pl.pallas_call(
        functools.partial(finish_kernel, len(ties) + 1),
        out_shape=shape_of(sheets, rows, chunks * LANES),
        out_specs=ANYWHERE,
        scratch_shapes=[
            pltpu.VMEM((2, pairs * SUBLANES, LANES), F32),
            pltpu.VMEM((pairs, chunks * LANES, LANES), F32),
            pltpu.VMEM(t.shape, F32),
            pltpu.VMEM(t.shape, F32),
            pltpu.SemaphoreType.DMA((OUT_COPIES,)),
        ],
        compiler_params=params(),
    )(own, got, *ties, yw, yh, yp, inner, inner_own, outer, outer_own, zw, zi, t)


def per_device(temperature, base, locations, energy):
    columns = temperature.shape[2]
    gy = lax.axis_size("gy")
    packed = edges(temperature, base)
    near = swap(packed, "gy", 1)
    t, b, loc, heat = load((temperature, base, locations[None], energy[None]), packed)
    near, t, b = lax.optimization_barrier((near, t, b))
    far = [swap(near, "gy", 2)] if gy > 2 else []
    if gy > 4:
        far.append(lax.ppermute(near, "gy", [(i, (i + 2 ^ 2) - 2) for i in range(2, gy - 2)]))
    c, total, xw, xi, xp, x_links, x_view, xm, ends = x_factor(loc, heat, t, b, columns * gy, near)
    xh, x_own, view = x_target(packed, t, total, [near] + far, xw, xi, xp, x_links, x_view, ends)
    yw, yi, yp, inner, outer, y_view = y_factor(c, x_view)
    zw, zi = z_factor(c, view)
    own, got, ties = gather_line(view, "gx", 2, (y_view, zw))
    yh, inner_own, outer_own, view = y_target(
        own, got, ties, xw, xh, xm, xp, x_links, x_own, t, yw, yi, yp, inner, outer, y_view
    )
    own, got, ties = gather_line(view, "gy")
    return finish(own, got, ties, yw, yh, yp, inner, inner_own, outer, outer_own, zw, zi, t)


def solution(mesh):
    in_specs = (P(None, "gx", "gy"), P(None, "gx", "gy"), P(), P())
    out_specs = P(None, "gx", "gy")
    return jax.shard_map(
        per_device, mesh=mesh, in_specs=in_specs, out_specs=out_specs, check_vma=False
    )
```

```python
import functools

import jax
import jax.numpy as jnp
from jax import lax
from jax.experimental import pallas as pl
from jax.experimental.pallas import tpu as pltpu
from jax.sharding import PartitionSpec as P

RATE = 2000.0
THERMAL_GROWTH = 0.8
LANES = 128
SUBLANES = 8
F32 = jnp.float32
MIB = 1024 * 1024
ANYWHERE = pl.BlockSpec(memory_space=pl.ANY)
IN_HBM = pl.BlockSpec(memory_space=pltpu.HBM)
IN_VMEM = pl.BlockSpec(memory_space=pltpu.VMEM)

R00, R0L, RLL, FIRST, LAST, C0, CL = range(7)
COEFS = (R00, R0L, RLL, C0, CL)


def params(limit=40):
    return pltpu.CompilerParams(vmem_limit_bytes=limit * MIB)


def shape_of(*sizes):
    return jax.ShapeDtypeStruct(sizes, F32)


def half_conduct(base, temperature):
    return base * (0.5 * RATE + (0.5 * RATE * THERMAL_GROWTH) * temperature)


def inverse(x):
    guess = pl.reciprocal(x, approx=True)
    return guess * (2.0 - x * guess)


def join_coefs(a, b):
    face = a[CL] + b[C0]
    inv = face * inverse(1.0 + face * (a[RLL] + b[R00]))
    left = a[R0L] * inv
    right = b[R0L] * inv
    joined = {
        R00: a[R00] - left * a[R0L],
        R0L: left * b[R0L],
        RLL: b[RLL] - right * b[R0L],
        C0: a[C0],
        CL: b[CL],
    }
    return joined, (inv, right, left)


def join_targets(a, b, links):
    inv, right, left = links
    jump = b[0] - a[1]
    return (a[0] + left * jump, b[1] - right * jump), jump * inv


def between(own, right, left, low, high):
    return own + right * high - left * low


def tree(items, join):
    levels = []
    while len(items) > 1:
        pairs = [join(items[i], items[i + 1]) for i in range(0, len(items), 2)]
        items = [p[0] for p in pairs]
        levels.append([p[1] for p in pairs])
    return items[0], levels


def descend(levels, low, high):
    ends = [(low, high)]
    for level in reversed(levels):
        below = []
        for (lo, hi), (own, right, left) in zip(ends, level):
            flux = between(own, right, left, lo, hi)
            below += [(lo, flux), (-flux, hi)]
        ends = below
    return ends


def node_offsets(leaves):
    offsets, at, count = [], 0, leaves // 2
    while count:
        offsets.append((at, count))
        at += count
        count //= 2
    return offsets


def factor(cond, steps, keep):
    here = cond(0)
    c_first = here
    one = jnp.ones_like(here)
    ground, path, first_first = one, one, None
    for k in range(steps - 1):
        following = cond(k + 1)
        face = here + following
        inv = inverse(ground + face)
        w = face * inv
        p = path * inv
        keep(k, w, inv, p)
        step = path * p
        first_first = step if first_first is None else first_first + step
        path = path * w
        ground = 1.0 + w * ground
        here = following
    inv = inverse(ground)
    p = path * inv
    keep(steps - 1, inv, inv, p)
    return {R00: first_first + path * p, R0L: p, RLL: inv, C0: c_first, CL: here}


def eliminate(target, steps, w, inv, p, keep):
    rhs = target(0)
    first = None
    for k in range(steps):
        h = rhs * inv(k)
        keep(k, h)
        step = rhs * p(k)
        first = step if first is None else first + step
        if k < steps - 1:
            rhs = target(k + 1) + w(k) * rhs
    return first, h


def is_odd(axis):
    return lax.axis_index(axis) % 2 == 1


def edges_kernel(t_hbm, b_hbm, packed, t_s, b_s, sems):
    sheets, rows, columns = t_hbm.shape
    sides = []
    for side, start in enumerate((0, columns - LANES)):
        sides.append(
            [
                pltpu.make_async_copy(src.at[:, :, pl.ds(start, LANES)], dst.at[side], sems.at[i, side])
                for i, (src, dst) in enumerate(((t_hbm, t_s), (b_hbm, b_s)))
            ]
        )
        for copy in sides[-1]:
            copy.start()
    lane = lax.broadcasted_iota(jnp.int32, (rows, LANES), 1)
    total = jnp.zeros((rows, LANES), F32)
    for side, source in enumerate((0, LANES - 1)):
        for copy in sides[side]:
            copy.wait()
        for z in range(sheets):
            t = t_s[side, z]
            c = half_conduct(b_s[side, z], t)
            place = 2 * sheets * side + z
            total = jnp.where(lane == place, t[:, source : source + 1], total)
            total = jnp.where(lane == place + sheets, c[:, source : source + 1], total)
    packed[...] = total


def edges(temperature, base):
    sheets, rows, _ = temperature.shape
    return pl.pallas_call(
        edges_kernel,
        in_specs=[IN_HBM] * 2,
        out_shape=pltpu.VMEM((rows, LANES), F32),
        scratch_shapes=[
            pltpu.VMEM((2, sheets, rows, LANES), F32),
            pltpu.VMEM((2, sheets, rows, LANES), F32),
            pltpu.SemaphoreType.DMA((2, 2)),
        ],
        compiler_params=params(),
    )(*[pltpu.with_memory_space_constraint(v, pltpu.HBM) for v in (temperature, base)])


def load_kernel(*refs):
    count = len(refs) // 2 - 1
    sems = refs[-1]
    copies = [
        pltpu.make_async_copy(refs[i], refs[count + 1 + i], sems.at[i]) for i in range(count)
    ]
    for copy in copies:
        copy.start()
    for copy in copies:
        copy.wait()


def load(values, after):
    return pl.pallas_call(
        load_kernel,
        in_specs=[IN_HBM] * len(values) + [ANYWHERE],
        out_shape=[pltpu.VMEM(v.shape, v.dtype) for v in values],
        scratch_shapes=[pltpu.SemaphoreType.DMA((len(values),))],
        compiler_params=params(),
        cost_estimate=pl.CostEstimate(
            flops=0, bytes_accessed=16 * values[0].size, transcendentals=0
        ),
    )(*[pltpu.with_memory_space_constraint(v, pltpu.HBM) for v in values], after)


def source_plane(loc, energy, rows, columns, plate):
    place = loc[...]
    count = place.shape[1]
    local_x = place // plate - lax.axis_index("gx") * rows
    local_y = place % plate - lax.axis_index("gy") * columns
    in_x = lax.broadcasted_iota(jnp.int32, (rows, count), 0) == local_x
    in_y = lax.broadcasted_iota(jnp.int32, (columns, count), 0) == local_y
    by_y = jnp.where(in_y, 1.0, 0.0).astype(jnp.bfloat16)
    left = energy[...]
    plane = None
    for _ in range(3):
        part = left.astype(jnp.bfloat16).astype(F32)
        left = left - part
        term = lax.dot_general(
            jnp.where(in_x, part, 0.0).astype(jnp.bfloat16),
            by_y,
            (((1,), (1,)), ((), ())),
            preferred_element_type=F32,
        )
        plane = term if plane is None else plane + term
    return plane


def part_of(y):
    return slice(y * LANES, (y + 1) * LANES)


def line_groups(chunks, sheets):
    order = [0, chunks - 1] + list(range(1, chunks - 1))
    return [[(y, z) for y in order[i : i + 2] for z in range(sheets)] for i in range(0, chunks, 2)]


def x_eliminate(field, members, first_line, w_ref, i_ref, p_ref, h_ref, h_line, q_s):
    steps = w_ref.shape[0]
    at = slice(first_line, first_line + len(members))
    kept_at = slice(h_line, h_line + len(members))

    def target(k):
        return jnp.stack([field(y, z)[pl.ds(k, SUBLANES, stride=steps), :] for y, z in members], 0)

    def keep(k, h):
        h_ref[k, kept_at] = h

    ends = eliminate(
        target, steps, lambda k: w_ref[k, at], lambda k: i_ref[k, at], lambda k: p_ref[k, at], keep
    )
    for q in range(2):
        for i in range(len(members)):
            first = (first_line + i) * SUBLANES
            q_s[q, first : first + SUBLANES, :] = ends[q][i]


def x_factor_kernel(plate, loc, energy, t_ref, b_ref, after, *refs):
    c_ref, total_ref, w_ref, i_ref, p_ref, links, view, h_ref, ends_ref, t_out, q_s, t_s = refs
    chunks, sheets, rows, _ = c_ref.shape
    lines = chunks * sheets
    steps = rows // SUBLANES
    plane = source_plane(loc, energy, rows, chunks * LANES, plate)

    lane = lax.broadcasted_iota(jnp.int32, (SUBLANES, LANES), 1)
    is_first, is_last = lane == 0, lane == LANES - 1
    for r in range(steps):
        at = slice(r * SUBLANES, (r + 1) * SUBLANES)
        before_t, before_c = None, None
        for z in range(sheets):
            ts = [t_ref[z, at, part_of(y)] for y in range(chunks)]
            cs = [half_conduct(b_ref[z, at, part_of(y)], ts[y]) for y in range(chunks)]
            t_turned = [pltpu.roll(v, LANES - 1, 1) for v in ts]
            c_turned = [pltpu.roll(v, LANES - 1, 1) for v in cs]
            flux = []
            for y in range(chunks):
                if y < chunks - 1:
                    t_next = jnp.where(is_last, t_turned[y + 1], t_turned[y])
                    c_next = jnp.where(is_last, c_turned[y + 1], c_turned[y])
                    flux.append((cs[y] + c_next) * (t_next - ts[y]))
                else:
                    inside = (cs[y] + c_turned[y]) * (t_turned[y] - ts[y])
                    flux.append(jnp.where(is_last, 0.0, inside))
            turned = [pltpu.roll(v, 1, 1) for v in flux]
            for y in range(chunks):
                from_low = jnp.where(is_first, turned[y - 1] if y else 0.0, turned[y])
                total = ts[y] + (flux[y] - from_low)
                if z == 0:
                    total = total + plane[at, part_of(y)]
                else:
                    across = (before_c[y] + cs[y]) * (ts[y] - before_t[y])
                    total = total - across
                    total_ref[y, z - 1, at, :] += across
                total_ref[y, z, at, :] = total
                c_ref[y, z, at, :] = cs[y]
                t_s[y, z, at, :] = ts[y]
            before_t, before_c = ts, cs

    at = 0
    for n, members in enumerate(line_groups(chunks, sheets)):

        def cond(k):
            return jnp.stack([c_ref[y, z, pl.ds(k, SUBLANES, stride=steps), :] for y, z in members], 0)

        def keep(k, w, inv, p):
            w_ref[k, at : at + len(members)] = w
            i_ref[k, at : at + len(members)] = inv
            p_ref[k, at : at + len(members)] = p

        block = factor(cond, steps, keep)
        for i, q in enumerate(COEFS):
            for j in range(len(members)):
                first = (at + j) * SUBLANES
                q_s[i, first : first + SUBLANES, :] = block[q][j]
        if n > 0:
            x_eliminate(
                lambda y, z: total_ref.at[y, z], members, at, w_ref, i_ref, p_ref, h_ref,
                at - 2 * sheets, ends_ref,
            )
        for k in range(steps):
            for i, (y, z) in enumerate(members):
                t_out[k, at + i] = t_s[y, z, pl.ds(k, SUBLANES, stride=steps), :]
        at += len(members)

    segments = [
        {q: q_s[n, pl.ds(s, lines, stride=SUBLANES), :] for n, q in enumerate(COEFS)}
        for s in range(SUBLANES)
    ]
    whole, levels = tree(segments, join_coefs)
    for (offset, _), level in zip(node_offsets(SUBLANES), levels):
        for n, values in enumerate(level):
            for i in range(3):
                links[offset + n, i] = values[i]
    for n, q in enumerate(COEFS):
        view[n] = whole[q]


def x_factor(loc, energy, t, b, plate, after):
    sheets, rows, columns = t.shape
    chunks = columns // LANES
    lines = chunks * sheets
    steps = rows // SUBLANES
    field = shape_of(chunks, sheets, rows, LANES)
    stored = shape_of(steps, lines, SUBLANES, LANES)
    return pl.pallas_call(
        functools.partial(x_factor_kernel, plate),
        in_specs=[IN_VMEM] * 4 + [ANYWHERE],
        out_shape=[
            field,
            field,
            stored,
            stored,
            stored,
            shape_of(SUBLANES - 1, 3, lines, LANES),
            shape_of(len(COEFS), lines, LANES),
            shape_of(steps, max(1, lines - 2 * sheets), SUBLANES, LANES),
            shape_of(2, lines * SUBLANES, LANES),
            stored,
        ],
        scratch_shapes=[
            pltpu.VMEM((len(COEFS), lines * SUBLANES, LANES), F32),
            pltpu.VMEM((chunks, sheets, rows, LANES), F32),
        ],
        compiler_params=params(),
        cost_estimate=pl.CostEstimate(flops=40 * t.size, bytes_accessed=28 * t.size, transcendentals=0),
    )(loc, energy, t, b, after)


def far_side(sources):
    place = lax.axis_index("gy")
    paired = (place >> 1) % 2 != place % 2
    nothing = jnp.zeros(sources[0].shape, F32)
    by_pair = sources[1][...] if len(sources) > 1 else nothing
    other = sources[2][...] if len(sources) > 2 else nothing
    return jnp.where(paired, by_pair, other)


def x_target_kernel(count, own_cells, t_ref, total_ref, *refs):
    w_ref, i_ref, p_ref, links, view, ends_ref, h_ref, own, send, e_s, q_s = refs[count:]
    chunks, sheets, rows, _ = total_ref.shape
    lines = chunks * sheets

    near, far = refs[0][...], far_side(refs[:count])
    before = jnp.where(is_odd("gy"), near, far)
    after = jnp.where(is_odd("gy"), far, near)
    lane = lax.broadcasted_iota(jnp.int32, (rows, LANES), 1)
    side = 2 * sheets
    beyond = jnp.where(lane < side, pltpu.roll(before, LANES - side, 1), pltpu.roll(after, side, 1))
    mine = own_cells[...]
    face = jnp.where(beyond > 0.0, mine + beyond, 0.0)
    flux = pltpu.roll(face, LANES - sheets, 1) * (beyond - mine)
    for n, (y, edge) in enumerate(((0, 0), (chunks - 1, LANES - 1))):
        for z in range(sheets):
            at = n * side + z
            e_s[n, z] = total_ref[y, z] + jnp.where(lane == edge, flux[:, at : at + 1], 0.0)

    members = line_groups(chunks, sheets)[0]
    x_eliminate(
        lambda y, z: e_s.at[0 if y == 0 else 1, z], members, 0, w_ref, i_ref, p_ref, h_ref, 0, q_s
    )
    split = len(members)
    items = [
        tuple(
            jnp.concatenate(
                [
                    q_s[q, pl.ds(s, split, stride=SUBLANES), :],
                    ends_ref[q, pl.ds(split * SUBLANES + s, lines - split, stride=SUBLANES), :],
                ],
                0,
            )
            for q in range(2)
        )
        for s in range(SUBLANES)
    ]
    for offset, count in node_offsets(SUBLANES):
        joined = []
        for n in range(count):
            ties = tuple(links[offset + n, i] for i in range(3))
            both, flux = join_targets(items[2 * n], items[2 * n + 1], ties)
            own[offset + n] = flux
            joined.append(both)
        items = joined
    for n, q in enumerate(COEFS):
        send[q] = view[n]
    send[FIRST], send[LAST] = items[0]


def x_target(own_cells, t, total, edge_cells, w, inv, p, links, view, ends):
    chunks, sheets, rows, _ = total.shape
    lines = chunks * sheets
    steps = rows // SUBLANES
    return pl.pallas_call(
        functools.partial(x_target_kernel, len(edge_cells)),
        out_shape=[
            shape_of(steps, 2 * sheets, SUBLANES, LANES),
            shape_of(SUBLANES - 1, lines, LANES),
            shape_of(7, lines, LANES),
        ],
        scratch_shapes=[
            pltpu.VMEM((2, sheets, rows, LANES), F32),
            pltpu.VMEM((2, 2 * sheets * SUBLANES, LANES), F32),
        ],
        compiler_params=params(),
    )(own_cells, t, total, *edge_cells, w, inv, p, links, view, ends)


def stages_of(axis):
    return lax.axis_size(axis).bit_length() - 1


def swap(value, axis, flip):
    count = lax.axis_size(axis)
    return lax.ppermute(value, axis, [(i, i ^ flip) for i in range(count)])


def on_right(axis, stage):
    return (lax.axis_index(axis) >> stage) % 2 == 1


def toward(right, block):
    return (
        jnp.where(right, block[R00], block[RLL]),
        jnp.where(right, block[FIRST], block[LAST]),
        jnp.where(right, block[C0], block[CL]),
    )


def join(a, b):
    joined, ties = join_coefs(a, b)
    (joined[FIRST], joined[LAST]), flux = join_targets((a[FIRST], a[LAST]), (b[FIRST], b[LAST]), ties)
    return joined, (flux, ties[1], ties[2])


def ordered(right, own, other):
    first = [jnp.where(right, theirs, mine) for mine, theirs in zip(own, other)]
    second = [jnp.where(right, mine, theirs) for mine, theirs in zip(own, other)]
    return first, second


def join_kernel(axis, stage, width, last, *refs):
    count = 1 << width
    blocks = [[refs[-i % count][q] for q in range(7)] for i in range(count)]
    send = refs[-1 - width]
    links = refs[-width:]
    for bit in range(width):
        right = on_right(axis, stage + bit)
        for i in range(count):
            if not i >> bit & 1:
                j = i | 1 << bit
                blocks[i], blocks[j] = ordered(right, blocks[i], blocks[j])
    for bit in range(width):
        pairs = [join(blocks[i], blocks[i + 1]) for i in range(0, len(blocks), 2)]
        blocks = [p[0] for p in pairs]
        ties = [p[1] for p in pairs]
        for upper in range(bit + 1, width):
            right = on_right(axis, stage + upper)
            ties = [
                tuple(jnp.where(right, v, u) for u, v in zip(ties[i], ties[i + 1]))
                for i in range(0, len(ties), 2)
            ]
        for i in range(3):
            links[bit][i] = ties[0][i]
    (whole,) = blocks
    if last:
        for n, value in enumerate(toward(on_right(axis, stage + width), whole)):
            send[n] = value
    else:
        for q in range(7):
            send[q] = whole[q]


def join_stage(own, got, axis, stage, width, last, after):
    lines = own.shape[1]
    return pl.pallas_call(
        functools.partial(join_kernel, axis, stage, width, last),
        in_specs=[IN_VMEM] * (1 + len(got)) + [ANYWHERE] * len(after),
        out_shape=[shape_of(3 if last else 7, lines, LANES)] + [shape_of(3, lines, LANES)] * width,
        compiler_params=params(),
    )(own, *got, *after)


def gather_line(view, axis, widest=1, meanwhile=()):
    stages = stages_of(axis)
    links, stage = [], 0
    while stage < stages - 1:
        width = min(widest, stages - 1 - stage)
        got = [swap(view, axis, flip << stage) for flip in range((1 << width) - 1, 0, -1)]
        last = stage + width == stages - 1
        view, *ties = join_stage(view, got, axis, stage, width, last, meanwhile)
        links += ties
        stage += width
        meanwhile = ()
    return view, swap(view, axis, 1 << stage), links


def block_ends(axis, own, got, links):
    top = len(links)
    right = on_right(axis, top)
    face = own[2] + got[2]
    jump = jnp.where(right, own[1] - got[1], got[1] - own[1])
    flux = jump * face * inverse(1.0 + face * (own[0] + got[0]))
    low = jnp.where(right, -flux, 0.0)
    high = jnp.where(right, 0.0, flux)
    for stage in range(top - 1, -1, -1):
        tie = links[stage]
        right = on_right(axis, stage)
        flux = between(tie[0], tie[1], tie[2], low, high)
        low, high = jnp.where(right, -flux, low), jnp.where(right, high, flux)
    return low, high


def natural(index, parts):
    span = SUBLANES * parts
    local = index % span
    return index - local + local % SUBLANES * parts + local // SUBLANES


def turn_matrix(shape, from_natural, parts):
    row = lax.broadcasted_iota(jnp.int32, shape, 0)
    column = lax.broadcasted_iota(jnp.int32, shape, 1) % LANES
    hit = natural(row, parts) == column if from_natural else row == natural(column, parts)
    return jnp.where(hit, 1.0, 0.0).astype(jnp.bfloat16)


def turned(matrix, field):
    high = field.astype(jnp.bfloat16)
    low = (field - high.astype(F32)).astype(jnp.bfloat16)
    both = jnp.concatenate([high, low], 1)
    return lax.dot_general(
        matrix, both, (((1,), (1,)), ((), ())), preferred_element_type=F32
    )


def y_factor_kernel(c_ref, after, w_ref, i_ref, p_ref, inner, outer, view, to_y, to_x, c_s, q_s, r_s):
    chunks, sheets, rows, _ = c_ref.shape
    each = LANES // rows
    pairs = sheets // each
    x_steps = rows // SUBLANES
    steps = LANES // SUBLANES
    to_y[...] = turn_matrix(to_y.shape, True, steps)
    to_x[...] = turn_matrix(to_x.shape, False, x_steps)
    for m in range(pairs):
        for y in range(chunks):
            block = jnp.concatenate(
                [
                    c_ref[y, m * each + i, pl.ds(k, SUBLANES, stride=x_steps), :]
                    for i in range(each)
                    for k in range(x_steps)
                ],
                0,
            )
            c_s[m, part_of(y), :] = block.T

    members = [(y, m) for y in range(chunks) for m in range(pairs)]
    lines = len(members)

    def cond(k):
        return jnp.stack([c_s[m, pl.ds(y * LANES + k, SUBLANES, stride=steps), :] for y, m in members], 0)

    def keep(k, w, inv, p):
        w_ref[k] = w
        i_ref[k] = inv
        p_ref[k] = p

    block = factor(cond, steps, keep)
    for n, q in enumerate(COEFS):
        for i in range(lines):
            q_s[n, i * SUBLANES : (i + 1) * SUBLANES, :] = block[q][i]
    segments = [
        {q: q_s[n, pl.ds(s, lines, stride=SUBLANES), :] for n, q in enumerate(COEFS)}
        for s in range(SUBLANES)
    ]
    whole, levels = tree(segments, join_coefs)
    for (offset, _), level in zip(node_offsets(SUBLANES), levels):
        for n, values in enumerate(level):
            for i in range(3):
                inner[offset + n, i] = values[i]
    for n, q in enumerate(COEFS):
        r_s[n] = whole[q]
    parts = [
        {q: r_s[n, y * pairs : (y + 1) * pairs, :] for n, q in enumerate(COEFS)} for y in range(chunks)
    ]
    whole, levels = tree(parts, join_coefs)
    for (offset, _), level in zip(node_offsets(chunks), levels):
        for n, values in enumerate(level):
            for i in range(3):
                outer[offset + n, i] = values[i]
    for n, q in enumerate(COEFS):
        view[n] = whole[q]


def y_factor(c, after):
    chunks, sheets, rows, _ = c.shape
    pairs = sheets * rows // LANES
    lines = chunks * pairs
    stored = shape_of(LANES // SUBLANES, lines, SUBLANES, LANES)
    matrix = jax.ShapeDtypeStruct((LANES, 2 * LANES), jnp.bfloat16)
    return pl.pallas_call(
        y_factor_kernel,
        in_specs=[IN_VMEM, ANYWHERE],
        out_shape=[
            stored,
            stored,
            stored,
            shape_of(SUBLANES - 1, 3, lines, LANES),
            shape_of(chunks - 1, 3, pairs, LANES),
            shape_of(len(COEFS), pairs, LANES),
            matrix,
            matrix,
        ],
        scratch_shapes=[
            pltpu.VMEM((pairs, chunks * LANES, LANES), F32),
            pltpu.VMEM((len(COEFS), lines * SUBLANES, LANES), F32),
            pltpu.VMEM((len(COEFS), lines, LANES), F32),
        ],
        compiler_params=params(),
        cost_estimate=pl.CostEstimate(flops=20 * c.size, bytes_accessed=16 * c.size, transcendentals=0),
    )(c, after)


def z_factor_kernel(c_ref, after, w_ref, i_ref):
    sheets = c_ref.shape[1]
    ground = 1.0
    for z in range(sheets - 1):
        face = c_ref[:, z] + c_ref[:, z + 1]
        inv = inverse(ground + face)
        w = face * inv
        i_ref[z] = inv
        w_ref[z] = w
        ground = 1.0 + w * ground
    i_ref[sheets - 1] = inverse(ground)


def z_factor(c, after):
    chunks, sheets, rows, _ = c.shape
    return pl.pallas_call(
        z_factor_kernel,
        in_specs=[IN_VMEM, ANYWHERE],
        out_shape=[
            shape_of(sheets - 1, chunks, rows, LANES),
            shape_of(sheets, chunks, rows, LANES),
        ],
        compiler_params=params(),
        cost_estimate=pl.CostEstimate(flops=10 * c.size, bytes_accessed=12 * c.size, transcendentals=0),
    )(c, after)


def join_tree(items, links, own):
    for offset, count in node_offsets(len(items)):
        joined = []
        for n in range(count):
            tie = tuple(links[offset + n, i] for i in range(3))
            both, flux = join_targets(items[2 * n], items[2 * n + 1], tie)
            own[offset + n] = flux
            joined.append(both)
        items = joined
    return items[0]


def tree_ends(leaves, links, own, low, high):
    levels = [
        [(own[offset + n], links[offset + n, 1], links[offset + n, 2]) for n in range(count)]
        for offset, count in node_offsets(leaves)
    ]
    return descend(levels, low, high)


def y_target_kernel(stages, *refs):
    own, got = refs[:2]
    ties = refs[2 : 1 + stages]
    xw, xh, xm, xp, x_links, x_own, t_ref, yw, yi, yp, inner, outer, view, to_y = refs[1 + stages : 15 + stages]
    h_ref, inner_own, outer_own, send = refs[15 + stages : 19 + stages]
    f_s, g_s, q_s, r_s = refs[19 + stages :]
    x_steps, lines = xw.shape[:2]
    chunks = g_s.shape[0]
    sheets = lines // chunks
    rows = x_steps * SUBLANES
    pairs = sheets * rows // LANES
    steps = yw.shape[0]

    low, high = block_ends("gx", own, got, ties)
    for s, ends in enumerate(tree_ends(SUBLANES, x_links, x_own, low, high)):
        for i in range(2):
            f_s[i, pl.ds(s, lines, stride=SUBLANES), :] = ends[i]
    first = 0
    for n, members in enumerate(line_groups(chunks, sheets)):
        at = slice(first, first + len(members))
        h_ref_of, h_at = (xh, at) if n == 0 else (xm, slice(first - 2 * sheets, at.stop - 2 * sheets))
        low, value = (
            jnp.stack(
                [f_s[i, j * SUBLANES : (j + 1) * SUBLANES, :] for j in range(at.start, at.stop)], 0
            )
            for i in range(2)
        )
        for k in range(x_steps - 1, -1, -1):
            value = xw[k, at] * value + (h_ref_of[k, h_at] + xp[k, at] * low)
            field = value - t_ref[k, at]
            for j, (y, z) in enumerate(members):
                place = z * rows + k * SUBLANES
                g_s[y, place : place + SUBLANES, :] = field[j]
        first = at.stop

    fields = [turned(to_y[...], g_s[y]) for y in range(chunks)]

    def target(k):
        at = slice(k * SUBLANES, (k + 1) * SUBLANES)
        return jnp.stack(
            [fields[y][at, m * LANES : (m + 1) * LANES] for y in range(chunks) for m in range(pairs)], 0
        )

    def keep(k, h):
        h_ref[k] = h

    ends = eliminate(target, steps, lambda k: yw[k], lambda k: yi[k], lambda k: yp[k], keep)
    for q in range(2):
        for i in range(chunks * pairs):
            q_s[q, i * SUBLANES : (i + 1) * SUBLANES, :] = ends[q][i]
    items = [
        tuple(q_s[q, pl.ds(s, chunks * pairs, stride=SUBLANES), :] for q in range(2))
        for s in range(SUBLANES)
    ]
    r_s[0], r_s[1] = join_tree(items, inner, inner_own)
    items = [tuple(r_s[q, y * pairs : (y + 1) * pairs, :] for q in range(2)) for y in range(chunks)]
    for n, q in enumerate(COEFS):
        send[q] = view[n]
    send[FIRST], send[LAST] = join_tree(items, outer, outer_own)


def y_target(own, got, ties, xw, xh, xm, xp, x_links, x_own, t, yw, yi, yp, inner, outer, view, to_y):
    x_steps, lines = xw.shape[:2]
    y_lines = yw.shape[1]
    pairs = view.shape[1]
    chunks = y_lines // pairs
    return pl.pallas_call(
        functools.partial(y_target_kernel, len(ties) + 1),
        out_shape=[
            shape_of(*yw.shape),
            shape_of(SUBLANES - 1, y_lines, LANES),
            shape_of(chunks - 1, pairs, LANES),
            shape_of(7, pairs, LANES),
        ],
        scratch_shapes=[
            pltpu.VMEM((2, lines * SUBLANES, LANES), F32),
            pltpu.VMEM((chunks, pairs * LANES, LANES), F32),
            pltpu.VMEM((2, y_lines * SUBLANES, LANES), F32),
            pltpu.VMEM((2, y_lines, LANES), F32),
        ],
        compiler_params=params(),
    )(own, got, *ties, xw, xh, xm, xp, x_links, x_own, t, yw, yi, yp, inner, outer, view, to_y)


def finish_kernel(stages, *refs):
    own, got = refs[:2]
    ties = refs[2 : 1 + stages]
    yw, yh, yp, inner, inner_own, outer, outer_own, zw, zi, t_ref, to_x = refs[1 + stages : 12 + stages]
    out, r_s, e_s, u_s, o_s, sems = refs[12 + stages :]
    chunks, sheets, rows, _ = o_s.shape
    each = LANES // rows
    pairs = sheets // each
    steps = yw.shape[0]
    lines = chunks * pairs

    low, high = block_ends("gy", own, got, ties)
    for y, ends in enumerate(tree_ends(chunks, outer, outer_own, low, high)):
        for i in range(2):
            r_s[i, y * pairs : (y + 1) * pairs, :] = ends[i]
    for s, ends in enumerate(tree_ends(SUBLANES, inner, inner_own, r_s[0], r_s[1])):
        for i in range(2):
            e_s[i, pl.ds(s, lines, stride=SUBLANES), :] = ends[i]
    low, value = (
        jnp.stack([e_s[i, n * SUBLANES : (n + 1) * SUBLANES, :] for n in range(lines)], 0)
        for i in range(2)
    )
    for k in range(steps - 1, -1, -1):
        value = yw[k] * value + (yh[k] + yp[k] * low)
        for y in range(chunks):
            for m in range(pairs):
                u_s[m, pl.ds(y * LANES + k, SUBLANES, stride=steps), :] = value[y * pairs + m]

    copies = []
    for first in range(0, chunks, 2):
        both = slice(first * LANES, (first + 2) * LANES)
        fields = [turned(to_x[...], u_s[m, both, :]) for m in range(pairs)]
        for y in range(first, first + 2):
            part = part_of(y)
            rhs, kept = None, []
            for z in range(sheets):
                at = z % each * rows
                own_rhs = fields[z // each][at : at + rows, part_of(y - first)]
                rhs = own_rhs if z == 0 else own_rhs + zw[z - 1, y] * rhs
                kept.append(rhs * zi[z, y])
            value = kept[-1]
            o_s[y, sheets - 1] = t_ref[sheets - 1, :, part] + value
            for z in range(sheets - 2, -1, -1):
                value = zw[z, y] * value + kept[z]
                o_s[y, z] = t_ref[z, :, part] + value
            copy = pltpu.make_async_copy(o_s.at[y], out.at[:, :, pl.ds(y * LANES, LANES)], sems.at[y])
            copy.start()
            copies.append(copy)
    for copy in copies:
        copy.wait()


def finish(own, got, ties, yw, yh, yp, inner, inner_own, outer, outer_own, zw, zi, t, to_x):
    sheets, rows, columns = t.shape
    chunks = columns // LANES
    pairs = sheets * rows // LANES
    lines = chunks * pairs
    return pl.pallas_call(
        functools.partial(finish_kernel, len(ties) + 1),
        out_shape=shape_of(sheets, rows, columns),
        out_specs=ANYWHERE,
        scratch_shapes=[
            pltpu.VMEM((2, lines, LANES), F32),
            pltpu.VMEM((2, lines * SUBLANES, LANES), F32),
            pltpu.VMEM((pairs, columns, LANES), F32),
            pltpu.VMEM((chunks, sheets, rows, LANES), F32),
            pltpu.SemaphoreType.DMA((chunks,)),
        ],
        compiler_params=params(),
    )(own, got, *ties, yw, yh, yp, inner, inner_own, outer, outer_own, zw, zi, t, to_x)


def per_device(temperature, base, locations, energy):
    columns = temperature.shape[2]
    gy = lax.axis_size("gy")
    packed = edges(temperature, base)
    near = swap(packed, "gy", 1)
    t, b, loc, heat = load((temperature, base, locations[None], energy[None]), packed)
    near, t, b = lax.optimization_barrier((near, t, b))
    far = [swap(near, "gy", 2)] if gy > 2 else []
    if gy > 4:
        far.append(lax.ppermute(near, "gy", [(i, (i + 2 ^ 2) - 2) for i in range(2, gy - 2)]))
    c, total, xw, xi, xp, x_links, x_view, xm, ends, t_steps = x_factor(loc, heat, t, b, columns * gy, near)
    xh, x_own, view = x_target(packed, t, total, [near] + far, xw, xi, xp, x_links, x_view, ends)
    yw, yi, yp, inner, outer, y_view, to_y, to_x = y_factor(c, x_view)
    zw, zi = z_factor(c, view)
    own, got, ties = gather_line(view, "gx", 2, (y_view, zw))
    yh, inner_own, outer_own, view = y_target(
        own, got, ties, xw, xh, xm, xp, x_links, x_own, t_steps, yw, yi, yp, inner, outer, y_view, to_y
    )
    own, got, ties = gather_line(view, "gy")
    return finish(own, got, ties, yw, yh, yp, inner, inner_own, outer, outer_own, zw, zi, t, to_x)


def solution(mesh):
    in_specs = (P(None, "gx", "gy"), P(None, "gx", "gy"), P(), P())
    out_specs = P(None, "gx", "gy")
    return jax.shard_map(
        per_device, mesh=mesh, in_specs=in_specs, out_specs=out_specs, check_vma=False
    )
```

```python
import functools

import jax
import jax.numpy as jnp
from jax import lax
from jax.experimental import pallas as pl
from jax.experimental.pallas import tpu as pltpu
from jax.sharding import PartitionSpec as P

RATE = 2000.0
THERMAL_GROWTH = 0.8
LANES = 128
SUBLANES = 8
F32 = jnp.float32
MIB = 1024 * 1024
ANYWHERE = pl.BlockSpec(memory_space=pl.ANY)
IN_HBM = pl.BlockSpec(memory_space=pltpu.HBM)
IN_VMEM = pl.BlockSpec(memory_space=pltpu.VMEM)

R00, R0L, RLL, FIRST, LAST, C0, CL = range(7)
COEFS = (R00, R0L, RLL, C0, CL)


def params(limit=40):
    return pltpu.CompilerParams(vmem_limit_bytes=limit * MIB)


def shape_of(*sizes):
    return jax.ShapeDtypeStruct(sizes, F32)


def half_conduct(base, temperature):
    return base * (0.5 * RATE + (0.5 * RATE * THERMAL_GROWTH) * temperature)


def inverse(x):
    guess = pl.reciprocal(x, approx=True)
    return guess * (2.0 - x * guess)


def join_coefs(a, b):
    face = a[CL] + b[C0]
    inv = face * inverse(1.0 + face * (a[RLL] + b[R00]))
    left = a[R0L] * inv
    right = b[R0L] * inv
    joined = {
        R00: a[R00] - left * a[R0L],
        R0L: left * b[R0L],
        RLL: b[RLL] - right * b[R0L],
        C0: a[C0],
        CL: b[CL],
    }
    return joined, (inv, right, left)


def join_targets(a, b, links):
    inv, right, left = links
    jump = b[0] - a[1]
    return (a[0] + left * jump, b[1] - right * jump), jump * inv


def between(own, right, left, low, high):
    return own + right * high - left * low


def tree(items, join):
    levels = []
    while len(items) > 1:
        pairs = [join(items[i], items[i + 1]) for i in range(0, len(items), 2)]
        items = [p[0] for p in pairs]
        levels.append([p[1] for p in pairs])
    return items[0], levels


def descend(levels, low, high):
    ends = [(low, high)]
    for level in reversed(levels):
        below = []
        for (lo, hi), (own, right, left) in zip(ends, level):
            flux = between(own, right, left, lo, hi)
            below += [(lo, flux), (-flux, hi)]
        ends = below
    return ends


def node_offsets(leaves):
    offsets, at, count = [], 0, leaves // 2
    while count:
        offsets.append((at, count))
        at += count
        count //= 2
    return offsets


def factor(cond, steps, keep):
    here = cond(0)
    c_first = here
    one = jnp.ones_like(here)
    ground, path, first_first = one, one, None
    for k in range(steps - 1):
        following = cond(k + 1)
        face = here + following
        inv = inverse(ground + face)
        w = face * inv
        p = path * inv
        keep(k, w, inv, p)
        step = path * p
        first_first = step if first_first is None else first_first + step
        path = path * w
        ground = 1.0 + w * ground
        here = following
    inv = inverse(ground)
    p = path * inv
    keep(steps - 1, inv, inv, p)
    return {R00: first_first + path * p, R0L: p, RLL: inv, C0: c_first, CL: here}


def eliminate(target, steps, w, inv, p, keep):
    rhs = target(0)
    first = None
    for k in range(steps):
        h = rhs * inv(k)
        keep(k, h)
        step = rhs * p(k)
        first = step if first is None else first + step
        if k < steps - 1:
            rhs = target(k + 1) + w(k) * rhs
    return first, h


def is_odd(axis):
    return lax.axis_index(axis) % 2 == 1


def edges_kernel(t_hbm, b_hbm, packed, t_s, b_s, sems):
    sheets, rows, columns = t_hbm.shape
    sides = []
    for side, start in enumerate((0, columns - LANES)):
        sides.append(
            [
                pltpu.make_async_copy(src.at[:, :, pl.ds(start, LANES)], dst.at[side], sems.at[i, side])
                for i, (src, dst) in enumerate(((t_hbm, t_s), (b_hbm, b_s)))
            ]
        )
        for copy in sides[-1]:
            copy.start()
    lane = lax.broadcasted_iota(jnp.int32, (rows, LANES), 1)
    total = jnp.zeros((rows, LANES), F32)
    for side, source in enumerate((0, LANES - 1)):
        for copy in sides[side]:
            copy.wait()
        for z in range(sheets):
            t = t_s[side, z]
            c = half_conduct(b_s[side, z], t)
            place = 2 * sheets * side + z
            total = jnp.where(lane == place, t[:, source : source + 1], total)
            total = jnp.where(lane == place + sheets, c[:, source : source + 1], total)
    packed[...] = total


def edges(temperature, base):
    sheets, rows, _ = temperature.shape
    return pl.pallas_call(
        edges_kernel,
        in_specs=[IN_HBM] * 2,
        out_shape=pltpu.VMEM((rows, LANES), F32),
        scratch_shapes=[
            pltpu.VMEM((2, sheets, rows, LANES), F32),
            pltpu.VMEM((2, sheets, rows, LANES), F32),
            pltpu.SemaphoreType.DMA((2, 2)),
        ],
        compiler_params=params(),
    )(*[pltpu.with_memory_space_constraint(v, pltpu.HBM) for v in (temperature, base)])


def load_kernel(*refs):
    count = len(refs) // 2 - 1
    sems = refs[-1]
    copies = [
        pltpu.make_async_copy(refs[i], refs[count + 1 + i], sems.at[i]) for i in range(count)
    ]
    for copy in copies:
        copy.start()
    for copy in copies:
        copy.wait()


def load(values, after):
    return pl.pallas_call(
        load_kernel,
        in_specs=[IN_HBM] * len(values) + [ANYWHERE],
        out_shape=[pltpu.VMEM(v.shape, v.dtype) for v in values],
        scratch_shapes=[pltpu.SemaphoreType.DMA((len(values),))],
        compiler_params=params(),
        cost_estimate=pl.CostEstimate(
            flops=0, bytes_accessed=16 * values[0].size, transcendentals=0
        ),
    )(*[pltpu.with_memory_space_constraint(v, pltpu.HBM) for v in values], after)


def source_plane(loc, energy, rows, columns, plate):
    place = loc[...]
    count = place.shape[1]
    local_x = place // plate - lax.axis_index("gx") * rows
    local_y = place % plate - lax.axis_index("gy") * columns
    in_x = lax.broadcasted_iota(jnp.int32, (rows, count), 0) == local_x
    in_y = lax.broadcasted_iota(jnp.int32, (columns, count), 0) == local_y
    by_y = jnp.where(in_y, 1.0, 0.0).astype(jnp.bfloat16)
    left = energy[...]
    plane = None
    for _ in range(3):
        part = left.astype(jnp.bfloat16).astype(F32)
        left = left - part
        term = lax.dot_general(
            jnp.where(in_x, part, 0.0).astype(jnp.bfloat16),
            by_y,
            (((1,), (1,)), ((), ())),
            preferred_element_type=F32,
        )
        plane = term if plane is None else plane + term
    return plane


def part_of(y):
    return slice(y * LANES, (y + 1) * LANES)


def line_groups(chunks, sheets):
    order = [0, chunks - 1] + list(range(1, chunks - 1))
    return [[(y, z) for y in order[i : i + 2] for z in range(sheets)] for i in range(0, chunks, 2)]


def x_eliminate(field, members, first_line, w_ref, i_ref, p_ref, h_ref, h_line, q_s):
    steps = w_ref.shape[0]
    at = slice(first_line, first_line + len(members))
    kept_at = slice(h_line, h_line + len(members))

    def target(k):
        return jnp.stack([field(y, z)[pl.ds(k, SUBLANES, stride=steps), :] for y, z in members], 0)

    def keep(k, h):
        h_ref[k, kept_at] = h

    ends = eliminate(
        target, steps, lambda k: w_ref[k, at], lambda k: i_ref[k, at], lambda k: p_ref[k, at], keep
    )
    for q in range(2):
        for i in range(len(members)):
            first = (first_line + i) * SUBLANES
            q_s[q, first : first + SUBLANES, :] = ends[q][i]


def x_factor_kernel(plate, loc, energy, t_ref, b_ref, after, *refs):
    c_ref, total_ref, w_ref, i_ref, p_ref, links, view, h_ref, ends_ref, t_out, q_s, t_s = refs
    chunks, sheets, rows, _ = c_ref.shape
    lines = chunks * sheets
    steps = rows // SUBLANES
    plane = source_plane(loc, energy, rows, chunks * LANES, plate)

    lane = lax.broadcasted_iota(jnp.int32, (SUBLANES, LANES), 1)
    is_first, is_last = lane == 0, lane == LANES - 1
    for r in range(steps):
        at = slice(r * SUBLANES, (r + 1) * SUBLANES)
        before_t, before_c = None, None
        for z in range(sheets):
            ts = [t_ref[z, at, part_of(y)] for y in range(chunks)]
            cs = [half_conduct(b_ref[z, at, part_of(y)], ts[y]) for y in range(chunks)]
            t_turned = [pltpu.roll(v, LANES - 1, 1) for v in ts]
            c_turned = [pltpu.roll(v, LANES - 1, 1) for v in cs]
            flux = []
            for y in range(chunks):
                if y < chunks - 1:
                    t_next = jnp.where(is_last, t_turned[y + 1], t_turned[y])
                    c_next = jnp.where(is_last, c_turned[y + 1], c_turned[y])
                    flux.append((cs[y] + c_next) * (t_next - ts[y]))
                else:
                    inside = (cs[y] + c_turned[y]) * (t_turned[y] - ts[y])
                    flux.append(jnp.where(is_last, 0.0, inside))
            turned = [pltpu.roll(v, 1, 1) for v in flux]
            for y in range(chunks):
                from_low = jnp.where(is_first, turned[y - 1] if y else 0.0, turned[y])
                total = ts[y] + (flux[y] - from_low)
                if z == 0:
                    total = total + plane[at, part_of(y)]
                else:
                    across = (before_c[y] + cs[y]) * (ts[y] - before_t[y])
                    total = total - across
                    total_ref[y, z - 1, at, :] += across
                total_ref[y, z, at, :] = total
                c_ref[y, z, at, :] = cs[y]
                t_s[y, z, at, :] = ts[y]
            before_t, before_c = ts, cs

    at = 0
    for n, members in enumerate(line_groups(chunks, sheets)):

        def cond(k):
            return jnp.stack([c_ref[y, z, pl.ds(k, SUBLANES, stride=steps), :] for y, z in members], 0)

        def keep(k, w, inv, p):
            w_ref[k, at : at + len(members)] = w
            i_ref[k, at : at + len(members)] = inv
            p_ref[k, at : at + len(members)] = p

        block = factor(cond, steps, keep)
        for i, q in enumerate(COEFS):
            for j in range(len(members)):
                first = (at + j) * SUBLANES
                q_s[i, first : first + SUBLANES, :] = block[q][j]
        if n > 0:
            x_eliminate(
                lambda y, z: total_ref.at[y, z], members, at, w_ref, i_ref, p_ref, h_ref,
                at - 2 * sheets, ends_ref,
            )
        for k in range(steps):
            for i, (y, z) in enumerate(members):
                t_out[k, at + i] = t_s[y, z, pl.ds(k, SUBLANES, stride=steps), :]
        at += len(members)

    segments = [
        {q: q_s[n, pl.ds(s, lines, stride=SUBLANES), :] for n, q in enumerate(COEFS)}
        for s in range(SUBLANES)
    ]
    whole, levels = tree(segments, join_coefs)
    for (offset, _), level in zip(node_offsets(SUBLANES), levels):
        for n, values in enumerate(level):
            for i in range(3):
                links[offset + n, i] = values[i]
    for n, q in enumerate(COEFS):
        view[n] = whole[q]


def x_factor(loc, energy, t, b, plate, after):
    sheets, rows, columns = t.shape
    chunks = columns // LANES
    lines = chunks * sheets
    steps = rows // SUBLANES
    field = shape_of(chunks, sheets, rows, LANES)
    stored = shape_of(steps, lines, SUBLANES, LANES)
    return pl.pallas_call(
        functools.partial(x_factor_kernel, plate),
        in_specs=[IN_VMEM] * 4 + [ANYWHERE],
        out_shape=[
            field,
            field,
            stored,
            stored,
            stored,
            shape_of(SUBLANES - 1, 3, lines, LANES),
            shape_of(len(COEFS), lines, LANES),
            shape_of(steps, max(1, lines - 2 * sheets), SUBLANES, LANES),
            shape_of(2, lines * SUBLANES, LANES),
            stored,
        ],
        scratch_shapes=[
            pltpu.VMEM((len(COEFS), lines * SUBLANES, LANES), F32),
            pltpu.VMEM((chunks, sheets, rows, LANES), F32),
        ],
        compiler_params=params(),
        cost_estimate=pl.CostEstimate(flops=40 * t.size, bytes_accessed=28 * t.size, transcendentals=0),
    )(loc, energy, t, b, after)


def far_side(sources):
    place = lax.axis_index("gy")
    paired = (place >> 1) % 2 != place % 2
    nothing = jnp.zeros(sources[0].shape, F32)
    by_pair = sources[1][...] if len(sources) > 1 else nothing
    other = sources[2][...] if len(sources) > 2 else nothing
    return jnp.where(paired, by_pair, other)


def x_target_kernel(count, own_cells, t_ref, total_ref, *refs):
    w_ref, i_ref, p_ref, links, view, ends_ref, h_ref, own, send, e_s, q_s = refs[count:]
    chunks, sheets, rows, _ = total_ref.shape
    lines = chunks * sheets

    near, far = refs[0][...], far_side(refs[:count])
    before = jnp.where(is_odd("gy"), near, far)
    after = jnp.where(is_odd("gy"), far, near)
    lane = lax.broadcasted_iota(jnp.int32, (rows, LANES), 1)
    side = 2 * sheets
    beyond = jnp.where(lane < side, pltpu.roll(before, LANES - side, 1), pltpu.roll(after, side, 1))
    mine = own_cells[...]
    face = jnp.where(beyond > 0.0, mine + beyond, 0.0)
    flux = pltpu.roll(face, LANES - sheets, 1) * (beyond - mine)
    for n, (y, edge) in enumerate(((0, 0), (chunks - 1, LANES - 1))):
        for z in range(sheets):
            at = n * side + z
            e_s[n, z] = total_ref[y, z] + jnp.where(lane == edge, flux[:, at : at + 1], 0.0)

    members = line_groups(chunks, sheets)[0]
    x_eliminate(
        lambda y, z: e_s.at[0 if y == 0 else 1, z], members, 0, w_ref, i_ref, p_ref, h_ref, 0, q_s
    )
    split = len(members)
    items = [
        tuple(
            jnp.concatenate(
                [
                    q_s[q, pl.ds(s, split, stride=SUBLANES), :],
                    ends_ref[q, pl.ds(split * SUBLANES + s, lines - split, stride=SUBLANES), :],
                ],
                0,
            )
            for q in range(2)
        )
        for s in range(SUBLANES)
    ]
    for offset, count in node_offsets(SUBLANES):
        joined = []
        for n in range(count):
            ties = tuple(links[offset + n, i] for i in range(3))
            both, flux = join_targets(items[2 * n], items[2 * n + 1], ties)
            own[offset + n] = flux
            joined.append(both)
        items = joined
    for n, q in enumerate(COEFS):
        send[q] = view[n]
    send[FIRST], send[LAST] = items[0]


def x_target(own_cells, t, total, edge_cells, w, inv, p, links, view, ends):
    chunks, sheets, rows, _ = total.shape
    lines = chunks * sheets
    steps = rows // SUBLANES
    return pl.pallas_call(
        functools.partial(x_target_kernel, len(edge_cells)),
        out_shape=[
            shape_of(steps, 2 * sheets, SUBLANES, LANES),
            shape_of(SUBLANES - 1, lines, LANES),
            shape_of(7, lines, LANES),
        ],
        scratch_shapes=[
            pltpu.VMEM((2, sheets, rows, LANES), F32),
            pltpu.VMEM((2, 2 * sheets * SUBLANES, LANES), F32),
        ],
        compiler_params=params(),
    )(own_cells, t, total, *edge_cells, w, inv, p, links, view, ends)


def stages_of(axis):
    return lax.axis_size(axis).bit_length() - 1


def swap(value, axis, flip):
    count = lax.axis_size(axis)
    return lax.ppermute(value, axis, [(i, i ^ flip) for i in range(count)])


def on_right(axis, stage):
    return (lax.axis_index(axis) >> stage) % 2 == 1


def toward(right, block):
    return (
        jnp.where(right, block[R00], block[RLL]),
        jnp.where(right, block[FIRST], block[LAST]),
        jnp.where(right, block[C0], block[CL]),
    )


def join(a, b):
    joined, ties = join_coefs(a, b)
    (joined[FIRST], joined[LAST]), flux = join_targets((a[FIRST], a[LAST]), (b[FIRST], b[LAST]), ties)
    return joined, (flux, ties[1], ties[2])


def ordered(right, own, other):
    first = [jnp.where(right, theirs, mine) for mine, theirs in zip(own, other)]
    second = [jnp.where(right, mine, theirs) for mine, theirs in zip(own, other)]
    return first, second


def join_kernel(axis, stage, width, last, *refs):
    count = 1 << width
    blocks = [[refs[-i % count][q] for q in range(7)] for i in range(count)]
    send = refs[-1 - width]
    links = refs[-width:]
    for bit in range(width):
        right = on_right(axis, stage + bit)
        for i in range(count):
            if not i >> bit & 1:
                j = i | 1 << bit
                blocks[i], blocks[j] = ordered(right, blocks[i], blocks[j])
    for bit in range(width):
        pairs = [join(blocks[i], blocks[i + 1]) for i in range(0, len(blocks), 2)]
        blocks = [p[0] for p in pairs]
        ties = [p[1] for p in pairs]
        for upper in range(bit + 1, width):
            right = on_right(axis, stage + upper)
            ties = [
                tuple(jnp.where(right, v, u) for u, v in zip(ties[i], ties[i + 1]))
                for i in range(0, len(ties), 2)
            ]
        for i in range(3):
            links[bit][i] = ties[0][i]
    (whole,) = blocks
    if last:
        for n, value in enumerate(toward(on_right(axis, stage + width), whole)):
            send[n] = value
    else:
        for q in range(7):
            send[q] = whole[q]


def join_stage(own, got, axis, stage, width, last, after):
    lines = own.shape[1]
    return pl.pallas_call(
        functools.partial(join_kernel, axis, stage, width, last),
        in_specs=[IN_VMEM] * (1 + len(got)) + [ANYWHERE] * len(after),
        out_shape=[shape_of(3 if last else 7, lines, LANES)] + [shape_of(3, lines, LANES)] * width,
        compiler_params=params(),
    )(own, *got, *after)


def gather_line(view, axis, widest=1, meanwhile=()):
    stages = stages_of(axis)
    links, stage = [], 0
    while stage < stages - 1:
        width = min(widest, stages - 1 - stage)
        got = [swap(view, axis, flip << stage) for flip in range((1 << width) - 1, 0, -1)]
        last = stage + width == stages - 1
        view, *ties = join_stage(view, got, axis, stage, width, last, meanwhile)
        links += ties
        stage += width
        meanwhile = ()
    return view, swap(view, axis, 1 << stage), links


def top_flux(axis, stages, own, got):
    right = on_right(axis, stages - 1)
    face = own[2] + got[2]
    jump = jnp.where(right, own[1] - got[1], got[1] - own[1])
    return jump * face * inverse(1.0 + face * (own[0] + got[0]))


def block_ends(axis, stages, links):
    shape = links[0].shape[1:] if links else None
    right = on_right(axis, stages - 1)
    zero = jnp.zeros(shape, F32)
    low, high = zero, zero
    unit_low = zero + jnp.where(right, -1.0, 0.0)
    unit_high = zero + jnp.where(right, 0.0, 1.0)
    for stage in range(stages - 2, -1, -1):
        tie = links[stage]
        right = on_right(axis, stage)
        flux = between(tie[0], tie[1], tie[2], low, high)
        unit = between(0.0, tie[1], tie[2], unit_low, unit_high)
        low, high = jnp.where(right, -flux, low), jnp.where(right, high, flux)
        unit_low, unit_high = jnp.where(right, -unit, unit_low), jnp.where(right, unit_high, unit)
    return (low, high), (unit_low, unit_high)


def natural(index, parts):
    span = SUBLANES * parts
    local = index % span
    return index - local + local % SUBLANES * parts + local // SUBLANES


def turn_matrix(shape, from_natural, parts):
    row = lax.broadcasted_iota(jnp.int32, shape, 0)
    column = lax.broadcasted_iota(jnp.int32, shape, 1) % LANES
    hit = natural(row, parts) == column if from_natural else row == natural(column, parts)
    return jnp.where(hit, 1.0, 0.0).astype(jnp.bfloat16)


def turned(matrix, field):
    high = field.astype(jnp.bfloat16)
    low = (field - high.astype(F32)).astype(jnp.bfloat16)
    both = jnp.concatenate([high, low], 1)
    return lax.dot_general(
        matrix, both, (((1,), (1,)), ((), ())), preferred_element_type=F32
    )


def y_factor_kernel(c_ref, after, w_ref, i_ref, p_ref, inner, outer, view, to_y, to_x, c_s, q_s, r_s):
    chunks, sheets, rows, _ = c_ref.shape
    each = LANES // rows
    pairs = sheets // each
    x_steps = rows // SUBLANES
    steps = LANES // SUBLANES
    to_y[...] = turn_matrix(to_y.shape, True, steps)
    to_x[...] = turn_matrix(to_x.shape, False, x_steps)
    for m in range(pairs):
        for y in range(chunks):
            block = jnp.concatenate(
                [
                    c_ref[y, m * each + i, pl.ds(k, SUBLANES, stride=x_steps), :]
                    for i in range(each)
                    for k in range(x_steps)
                ],
                0,
            )
            c_s[m, part_of(y), :] = block.T

    members = [(y, m) for y in range(chunks) for m in range(pairs)]
    lines = len(members)

    def cond(k):
        return jnp.stack([c_s[m, pl.ds(y * LANES + k, SUBLANES, stride=steps), :] for y, m in members], 0)

    def keep(k, w, inv, p):
        w_ref[k] = w
        i_ref[k] = inv
        p_ref[k] = p

    block = factor(cond, steps, keep)
    for n, q in enumerate(COEFS):
        for i in range(lines):
            q_s[n, i * SUBLANES : (i + 1) * SUBLANES, :] = block[q][i]
    segments = [
        {q: q_s[n, pl.ds(s, lines, stride=SUBLANES), :] for n, q in enumerate(COEFS)}
        for s in range(SUBLANES)
    ]
    whole, levels = tree(segments, join_coefs)
    for (offset, _), level in zip(node_offsets(SUBLANES), levels):
        for n, values in enumerate(level):
            for i in range(3):
                inner[offset + n, i] = values[i]
    for n, q in enumerate(COEFS):
        r_s[n] = whole[q]
    parts = [
        {q: r_s[n, y * pairs : (y + 1) * pairs, :] for n, q in enumerate(COEFS)} for y in range(chunks)
    ]
    whole, levels = tree(parts, join_coefs)
    for (offset, _), level in zip(node_offsets(chunks), levels):
        for n, values in enumerate(level):
            for i in range(3):
                outer[offset + n, i] = values[i]
    for n, q in enumerate(COEFS):
        view[n] = whole[q]


def y_factor(c, after):
    chunks, sheets, rows, _ = c.shape
    pairs = sheets * rows // LANES
    lines = chunks * pairs
    stored = shape_of(LANES // SUBLANES, lines, SUBLANES, LANES)
    matrix = jax.ShapeDtypeStruct((LANES, 2 * LANES), jnp.bfloat16)
    return pl.pallas_call(
        y_factor_kernel,
        in_specs=[IN_VMEM, ANYWHERE],
        out_shape=[
            stored,
            stored,
            stored,
            shape_of(SUBLANES - 1, 3, lines, LANES),
            shape_of(chunks - 1, 3, pairs, LANES),
            shape_of(len(COEFS), pairs, LANES),
            matrix,
            matrix,
        ],
        scratch_shapes=[
            pltpu.VMEM((pairs, chunks * LANES, LANES), F32),
            pltpu.VMEM((len(COEFS), lines * SUBLANES, LANES), F32),
            pltpu.VMEM((len(COEFS), lines, LANES), F32),
        ],
        compiler_params=params(),
        cost_estimate=pl.CostEstimate(flops=20 * c.size, bytes_accessed=16 * c.size, transcendentals=0),
    )(c, after)


def z_factor_kernel(c_ref, after, w_ref, i_ref):
    sheets = c_ref.shape[1]
    ground = 1.0
    for z in range(sheets - 1):
        face = c_ref[:, z] + c_ref[:, z + 1]
        inv = inverse(ground + face)
        w = face * inv
        i_ref[z] = inv
        w_ref[z] = w
        ground = 1.0 + w * ground
    i_ref[sheets - 1] = inverse(ground)


def z_factor(c, after):
    chunks, sheets, rows, _ = c.shape
    return pl.pallas_call(
        z_factor_kernel,
        in_specs=[IN_VMEM, ANYWHERE],
        out_shape=[
            shape_of(sheets - 1, chunks, rows, LANES),
            shape_of(sheets, chunks, rows, LANES),
        ],
        compiler_params=params(),
        cost_estimate=pl.CostEstimate(flops=10 * c.size, bytes_accessed=12 * c.size, transcendentals=0),
    )(c, after)


def join_tree(items, links, own):
    for offset, count in node_offsets(len(items)):
        joined = []
        for n in range(count):
            tie = tuple(links[offset + n, i] for i in range(3))
            both, flux = join_targets(items[2 * n], items[2 * n + 1], tie)
            own[offset + n] = flux
            joined.append(both)
        items = joined
    return items[0]


def tree_ends(leaves, links, own, low, high):
    levels = [
        [(own(offset + n), links[offset + n, 1], links[offset + n, 2]) for n in range(count)]
        for offset, count in node_offsets(leaves)
    ]
    return descend(levels, low, high)


def nothing(node):
    return 0.0


def y_prepare_kernel(stages, *refs):
    ties = refs[: stages - 1]
    xw, xh, xm, xp, x_links, x_own, t_ref, to_y = refs[stages - 1 : stages + 7]
    base, response, f_s, g_s = refs[stages + 7 :]
    x_steps, lines = xw.shape[:2]
    chunks = base.shape[0]
    sheets = lines // chunks
    rows = x_steps * SUBLANES

    ends, units = block_ends("gx", stages, ties)
    for n, (own, (low, high)) in enumerate(((lambda i: x_own[i], ends), (nothing, units))):
        for s, pair in enumerate(tree_ends(SUBLANES, x_links, own, low, high)):
            for i in range(2):
                f_s[n, i, pl.ds(s, lines, stride=SUBLANES), :] = pair[i]
    first = 0
    for n, members in enumerate(line_groups(chunks, sheets)):
        at = slice(first, first + len(members))
        h_ref_of, h_at = (xh, at) if n == 0 else (xm, slice(first - 2 * sheets, at.stop - 2 * sheets))
        (low, value), (unit_low, unit) = (
            [
                jnp.stack(
                    [f_s[q, i, j * SUBLANES : (j + 1) * SUBLANES, :] for j in range(at.start, at.stop)], 0
                )
                for i in range(2)
            ]
            for q in range(2)
        )
        for k in range(x_steps - 1, -1, -1):
            w, p = xw[k, at], xp[k, at]
            value = w * value + (h_ref_of[k, h_at] + p * low)
            unit = w * unit + p * unit_low
            field = value - t_ref[k, at]
            for j, (y, z) in enumerate(members):
                place = z * rows + k * SUBLANES
                g_s[0, y, place : place + SUBLANES, :] = field[j]
                g_s[1, y, place : place + SUBLANES, :] = unit[j]
        first = at.stop

    for y in range(chunks):
        base[y] = turned(to_y[...], g_s[0, y])
        response[y] = turned(to_y[...], g_s[1, y])


def y_prepare(ties, xw, xh, xm, xp, x_links, x_own, t, to_y, chunks):
    x_steps, lines = xw.shape[:2]
    width = lines // chunks * x_steps * SUBLANES
    field = shape_of(chunks, LANES, width)
    return pl.pallas_call(
        functools.partial(y_prepare_kernel, len(ties) + 1),
        out_shape=[field, field],
        scratch_shapes=[
            pltpu.VMEM((2, 2, lines * SUBLANES, LANES), F32),
            pltpu.VMEM((2, chunks, width, LANES), F32),
        ],
        compiler_params=params(),
        cost_estimate=pl.CostEstimate(flops=8 * t.size, bytes_accessed=16 * t.size, transcendentals=0),
    )(*ties, xw, xh, xm, xp, x_links, x_own, t, to_y)


def y_target_kernel(stages, own, got, base, response, yw, yi, yp, inner, outer, view, to_y, *refs):
    h_ref, inner_own, outer_own, send, q_s, r_s = refs
    chunks, _, width = base.shape
    pairs = width // LANES
    sheets = own.shape[1] // chunks
    rows = width // sheets
    steps = yw.shape[0]

    flux = top_flux("gx", stages, own, got)
    line_of = {member: n for n, member in enumerate(sum(line_groups(chunks, sheets), []))}
    fields = []
    for y in range(chunks):
        spread = jnp.concatenate(
            [
                jnp.broadcast_to(flux[line_of[y, z] : line_of[y, z] + 1, :], (rows, LANES))
                for z in range(sheets)
            ],
            0,
        )
        fields.append(base[y] + response[y] * turned(to_y[...], spread))

    def target(k):
        at = slice(k * SUBLANES, (k + 1) * SUBLANES)
        return jnp.stack(
            [fields[y][at, m * LANES : (m + 1) * LANES] for y in range(chunks) for m in range(pairs)], 0
        )

    def keep(k, h):
        h_ref[k] = h

    ends = eliminate(target, steps, lambda k: yw[k], lambda k: yi[k], lambda k: yp[k], keep)
    for q in range(2):
        for i in range(chunks * pairs):
            q_s[q, i * SUBLANES : (i + 1) * SUBLANES, :] = ends[q][i]
    items = [
        tuple(q_s[q, pl.ds(s, chunks * pairs, stride=SUBLANES), :] for q in range(2))
        for s in range(SUBLANES)
    ]
    r_s[0], r_s[1] = join_tree(items, inner, inner_own)
    items = [tuple(r_s[q, y * pairs : (y + 1) * pairs, :] for q in range(2)) for y in range(chunks)]
    for n, q in enumerate(COEFS):
        send[q] = view[n]
    send[FIRST], send[LAST] = join_tree(items, outer, outer_own)


def y_target(own, got, base, response, yw, yi, yp, inner, outer, view, to_y):
    y_lines = yw.shape[1]
    pairs = view.shape[1]
    chunks = y_lines // pairs
    return pl.pallas_call(
        functools.partial(y_target_kernel, stages_of("gx")),
        out_shape=[
            shape_of(*yw.shape),
            shape_of(SUBLANES - 1, y_lines, LANES),
            shape_of(chunks - 1, pairs, LANES),
            shape_of(7, pairs, LANES),
        ],
        scratch_shapes=[
            pltpu.VMEM((2, y_lines * SUBLANES, LANES), F32),
            pltpu.VMEM((2, y_lines, LANES), F32),
        ],
        compiler_params=params(),
    )(own, got, base, response, yw, yi, yp, inner, outer, view, to_y)


def z_solve(zw, zi, field, at, keep):
    sheets = zi.shape[0]
    rhs, kept = None, []
    for z in range(sheets):
        rhs = field(z) if z == 0 else field(z) + zw[z - 1, at] * rhs
        kept.append(rhs * zi[z, at])
    value = kept[-1]
    keep(sheets - 1, value)
    for z in range(sheets - 2, -1, -1):
        value = zw[z, at] * value + kept[z]
        keep(z, value)


def finish_prepare_kernel(stages, *refs):
    ties = refs[: stages - 1]
    yw, yh, yp, inner, inner_own, outer, outer_own, zw, zi, t_ref, to_x = refs[stages - 1 : stages + 10]
    base, response, r_s, e_s, u_s = refs[stages + 10 :]
    chunks, sheets, rows, _ = base.shape
    each = LANES // rows
    pairs = sheets // each
    steps = yw.shape[0]
    lines = chunks * pairs

    ends, units = block_ends("gy", stages, ties)
    both = (
        (lambda i: outer_own[i], lambda i: inner_own[i], ends),
        (nothing, nothing, units),
    )
    for n, (upper, lower, (low, high)) in enumerate(both):
        for y, pair in enumerate(tree_ends(chunks, outer, upper, low, high)):
            for i in range(2):
                r_s[n, i, y * pairs : (y + 1) * pairs, :] = pair[i]
        for s, pair in enumerate(tree_ends(SUBLANES, inner, lower, r_s[n, 0], r_s[n, 1])):
            for i in range(2):
                e_s[n, i, pl.ds(s, lines, stride=SUBLANES), :] = pair[i]
    (low, value), (unit_low, unit) = (
        [
            jnp.stack([e_s[q, i, n * SUBLANES : (n + 1) * SUBLANES, :] for n in range(lines)], 0)
            for i in range(2)
        ]
        for q in range(2)
    )
    for k in range(steps - 1, -1, -1):
        w, p = yw[k], yp[k]
        value = w * value + (yh[k] + p * low)
        unit = w * unit + p * unit_low
        for y in range(chunks):
            for m in range(pairs):
                place = pl.ds(y * LANES + k, SUBLANES, stride=steps)
                u_s[0, m, place, :] = value[y * pairs + m]
                u_s[1, m, place, :] = unit[y * pairs + m]

    for y in range(chunks):
        part = part_of(y)
        fields = [turned(to_x[...], u_s[0, m, part, :]) for m in range(pairs)]

        def field(z):
            at = z % each * rows
            return fields[z // each][at : at + rows, :]

        def keep(z, value):
            base[y, z] = t_ref[z, :, part] + value

        z_solve(zw, zi, field, y, keep)
        for m in range(pairs):
            units = turned(to_x[...], u_s[1, m, part, :])
            for i in range(each):
                response[y, m * each + i] = units[i * rows : (i + 1) * rows, :]


def finish_prepare(ties, yw, yh, yp, inner, inner_own, outer, outer_own, zw, zi, t, to_x):
    sheets, rows, columns = t.shape
    chunks = columns // LANES
    pairs = sheets * rows // LANES
    lines = chunks * pairs
    field = shape_of(chunks, sheets, rows, LANES)
    return pl.pallas_call(
        functools.partial(finish_prepare_kernel, len(ties) + 1),
        out_shape=[field, field],
        scratch_shapes=[
            pltpu.VMEM((2, 2, lines, LANES), F32),
            pltpu.VMEM((2, 2, lines * SUBLANES, LANES), F32),
            pltpu.VMEM((2, pairs, columns, LANES), F32),
        ],
        compiler_params=params(),
        cost_estimate=pl.CostEstimate(flops=12 * t.size, bytes_accessed=20 * t.size, transcendentals=0),
    )(*ties, yw, yh, yp, inner, inner_own, outer, outer_own, zw, zi, t, to_x)


def finish_kernel(stages, own, got, base, response, zw, zi, to_x, out, o_s, sems):
    chunks, sheets, rows, _ = base.shape
    each = LANES // rows
    pairs = sheets // each
    copies, _, _, wide = o_s.shape

    flux = top_flux("gy", stages, own, got)
    spread = [
        turned(to_x[...], jnp.broadcast_to(flux[m : m + 1, :], (LANES, LANES))) for m in range(pairs)
    ]
    started = []
    for n in range(copies):
        for y in range(n * chunks // copies, (n + 1) * chunks // copies):
            part = part_of(y - n * chunks // copies)

            def field(z):
                at = z % each * rows
                return response[y, z] * spread[z // each][at : at + rows, :]

            def keep(z, value):
                o_s[n, z, :, part] = base[y, z] + value

            z_solve(zw, zi, field, y, keep)
        copy = pltpu.make_async_copy(o_s.at[n], out.at[:, :, pl.ds(n * wide, wide)], sems.at[n])
        copy.start()
        started.append(copy)
    for copy in started:
        copy.wait()


def finish(own, got, base, response, zw, zi, to_x):
    chunks, sheets, rows, _ = base.shape
    copies = 2
    return pl.pallas_call(
        functools.partial(finish_kernel, stages_of("gy")),
        out_shape=shape_of(sheets, rows, chunks * LANES),
        out_specs=ANYWHERE,
        scratch_shapes=[
            pltpu.VMEM((copies, sheets, rows, chunks * LANES // copies), F32),
            pltpu.SemaphoreType.DMA((copies,)),
        ],
        compiler_params=params(),
    )(own, got, base, response, zw, zi, to_x)


def per_device(temperature, base, locations, energy):
    columns = temperature.shape[2]
    gy = lax.axis_size("gy")
    packed = edges(temperature, base)
    near = swap(packed, "gy", 1)
    t, b, loc, heat = load((temperature, base, locations[None], energy[None]), packed)
    near, t, b = lax.optimization_barrier((near, t, b))
    far = [swap(near, "gy", 2)] if gy > 2 else []
    if gy > 4:
        far.append(lax.ppermute(near, "gy", [(i, (i + 2 ^ 2) - 2) for i in range(2, gy - 2)]))
    c, total, xw, xi, xp, x_links, x_view, xm, ends, t_steps = x_factor(loc, heat, t, b, columns * gy, near)
    xh, x_own, view = x_target(packed, t, total, [near] + far, xw, xi, xp, x_links, x_view, ends)
    yw, yi, yp, inner, outer, y_view, to_y, to_x = y_factor(c, x_view)
    zw, zi = z_factor(c, view)
    own, got, ties = gather_line(view, "gx", 2, (y_view, zw))
    base, response = y_prepare(
        ties, xw, xh, xm, xp, x_links, x_own, t_steps, to_y, columns // LANES
    )
    yh, inner_own, outer_own, view = y_target(
        own, got, base, response, yw, yi, yp, inner, outer, y_view, to_y
    )
    own, got, ties = gather_line(view, "gy")
    base, response = finish_prepare(
        ties, yw, yh, yp, inner, inner_own, outer, outer_own, zw, zi, t, to_x
    )
    return finish(own, got, base, response, zw, zi, to_x)


def solution(mesh):
    in_specs = (P(None, "gx", "gy"), P(None, "gx", "gy"), P(), P())
    out_specs = P(None, "gx", "gy")
    return jax.shard_map(
        per_device, mesh=mesh, in_specs=in_specs, out_specs=out_specs, check_vma=False
    )
```

```python
import functools

import jax
import jax.numpy as jnp
from jax import lax
from jax.experimental import pallas as pl
from jax.experimental.pallas import tpu as pltpu
from jax.sharding import PartitionSpec as P

RATE = 2000.0
THERMAL_GROWTH = 0.8
LANES = 128
SUBLANES = 8
F32 = jnp.float32
MIB = 1024 * 1024
ANYWHERE = pl.BlockSpec(memory_space=pl.ANY)
IN_HBM = pl.BlockSpec(memory_space=pltpu.HBM)
IN_VMEM = pl.BlockSpec(memory_space=pltpu.VMEM)

R00, R0L, RLL, FIRST, LAST, C0, CL = range(7)
COEFS = (R00, R0L, RLL, C0, CL)


def params(limit=40):
    return pltpu.CompilerParams(vmem_limit_bytes=limit * MIB)


def shape_of(*sizes):
    return jax.ShapeDtypeStruct(sizes, F32)


def half_conduct(base, temperature):
    return base * (0.5 * RATE + (0.5 * RATE * THERMAL_GROWTH) * temperature)


def inverse(x):
    guess = pl.reciprocal(x, approx=True)
    return guess * (2.0 - x * guess)


def join_coefs(a, b):
    face = a[CL] + b[C0]
    inv = face * inverse(1.0 + face * (a[RLL] + b[R00]))
    left = a[R0L] * inv
    right = b[R0L] * inv
    joined = {
        R00: a[R00] - left * a[R0L],
        R0L: left * b[R0L],
        RLL: b[RLL] - right * b[R0L],
        C0: a[C0],
        CL: b[CL],
    }
    return joined, (inv, right, left)


def join_targets(a, b, links):
    inv, right, left = links
    jump = b[0] - a[1]
    return (a[0] + left * jump, b[1] - right * jump), jump * inv


def between(own, right, left, low, high):
    return own + right * high - left * low


def tree(items, join):
    levels = []
    while len(items) > 1:
        pairs = [join(items[i], items[i + 1]) for i in range(0, len(items), 2)]
        items = [p[0] for p in pairs]
        levels.append([p[1] for p in pairs])
    return items[0], levels


def descend(levels, low, high):
    ends = [(low, high)]
    for level in reversed(levels):
        below = []
        for (lo, hi), (own, right, left) in zip(ends, level):
            flux = between(own, right, left, lo, hi)
            below += [(lo, flux), (-flux, hi)]
        ends = below
    return ends


def node_offsets(leaves):
    offsets, at, count = [], 0, leaves // 2
    while count:
        offsets.append((at, count))
        at += count
        count //= 2
    return offsets


def factor(cond, steps, keep):
    here = cond(0)
    c_first = here
    one = jnp.ones_like(here)
    ground, path, first_first = one, one, None
    for k in range(steps - 1):
        following = cond(k + 1)
        face = here + following
        inv = inverse(ground + face)
        w = face * inv
        p = path * inv
        keep(k, w, inv, p)
        step = path * p
        first_first = step if first_first is None else first_first + step
        path = path * w
        ground = 1.0 + w * ground
        here = following
    inv = inverse(ground)
    p = path * inv
    keep(steps - 1, inv, inv, p)
    return {R00: first_first + path * p, R0L: p, RLL: inv, C0: c_first, CL: here}


def eliminate(target, steps, w, inv, p, keep):
    rhs = target(0)
    first = None
    for k in range(steps):
        h = rhs * inv(k)
        keep(k, h)
        step = rhs * p(k)
        first = step if first is None else first + step
        if k < steps - 1:
            rhs = target(k + 1) + w(k) * rhs
    return first, h


def is_odd(axis):
    return lax.axis_index(axis) % 2 == 1


def fold(cells, used):
    total = cells[:SUBLANES]
    lane = lax.broadcasted_iota(jnp.int32, total.shape, 1)
    for n in range(1, cells.shape[0] // SUBLANES):
        part = pltpu.roll(cells[n * SUBLANES : (n + 1) * SUBLANES], n * used, 1)
        total = jnp.where(lane // used == n, part, total)
    return total


def unfold(cells, used, rows):
    parts = [cells] + [
        pltpu.roll(cells, LANES - n * used, 1) for n in range(1, rows // SUBLANES)
    ]
    return jnp.concatenate(parts, 0)


def edges_kernel(t_hbm, b_hbm, packed, t_s, b_s, sems):
    sheets, rows, columns = t_hbm.shape
    sides = []
    for side, start in enumerate((0, columns - LANES)):
        sides.append(
            [
                pltpu.make_async_copy(src.at[:, :, pl.ds(start, LANES)], dst.at[side], sems.at[i, side])
                for i, (src, dst) in enumerate(((t_hbm, t_s), (b_hbm, b_s)))
            ]
        )
        for copy in sides[-1]:
            copy.start()
    lane = lax.broadcasted_iota(jnp.int32, (rows, LANES), 1)
    total = jnp.zeros((rows, LANES), F32)
    for side, source in enumerate((0, LANES - 1)):
        for copy in sides[side]:
            copy.wait()
        for z in range(sheets):
            t = t_s[side, z]
            c = half_conduct(b_s[side, z], t)
            place = 2 * sheets * side + z
            total = jnp.where(lane == place, t[:, source : source + 1], total)
            total = jnp.where(lane == place + sheets, c[:, source : source + 1], total)
    packed[...] = fold(total, 4 * sheets)


def edges(temperature, base):
    sheets, rows, _ = temperature.shape
    assert rows // SUBLANES * 4 * sheets <= LANES
    return pl.pallas_call(
        edges_kernel,
        in_specs=[IN_HBM] * 2,
        out_shape=pltpu.VMEM((SUBLANES, LANES), F32),
        scratch_shapes=[
            pltpu.VMEM((2, sheets, rows, LANES), F32),
            pltpu.VMEM((2, sheets, rows, LANES), F32),
            pltpu.SemaphoreType.DMA((2, 2)),
        ],
        compiler_params=params(),
    )(*[pltpu.with_memory_space_constraint(v, pltpu.HBM) for v in (temperature, base)])


def load_kernel(*refs):
    count = len(refs) // 2 - 1
    sems = refs[-1]
    copies = [
        pltpu.make_async_copy(refs[i], refs[count + 1 + i], sems.at[i]) for i in range(count)
    ]
    for copy in copies:
        copy.start()
    for copy in copies:
        copy.wait()


def load(values, after):
    return pl.pallas_call(
        load_kernel,
        in_specs=[IN_HBM] * len(values) + [ANYWHERE],
        out_shape=[pltpu.VMEM(v.shape, v.dtype) for v in values],
        scratch_shapes=[pltpu.SemaphoreType.DMA((len(values),))],
        compiler_params=params(),
        cost_estimate=pl.CostEstimate(
            flops=0, bytes_accessed=16 * values[0].size, transcendentals=0
        ),
    )(*[pltpu.with_memory_space_constraint(v, pltpu.HBM) for v in values], after)


def source_plane(loc, energy, rows, columns, plate):
    place = loc[...]
    count = place.shape[1]
    local_x = place // plate - lax.axis_index("gx") * rows
    local_y = place % plate - lax.axis_index("gy") * columns
    in_x = lax.broadcasted_iota(jnp.int32, (rows, count), 0) == local_x
    in_y = lax.broadcasted_iota(jnp.int32, (columns, count), 0) == local_y
    by_y = jnp.where(in_y, 1.0, 0.0).astype(jnp.bfloat16)
    left = energy[...]
    plane = None
    for _ in range(3):
        part = left.astype(jnp.bfloat16).astype(F32)
        left = left - part
        term = lax.dot_general(
            jnp.where(in_x, part, 0.0).astype(jnp.bfloat16),
            by_y,
            (((1,), (1,)), ((), ())),
            preferred_element_type=F32,
        )
        plane = term if plane is None else plane + term
    return plane


def part_of(y):
    return slice(y * LANES, (y + 1) * LANES)


def line_groups(chunks, sheets):
    order = [0, chunks - 1] + list(range(1, chunks - 1))
    return [[(y, z) for y in order[i : i + 2] for z in range(sheets)] for i in range(0, chunks, 2)]


def x_eliminate(field, members, first_line, w_ref, i_ref, p_ref, h_ref, h_line, q_s):
    steps = w_ref.shape[0]
    at = slice(first_line, first_line + len(members))
    kept_at = slice(h_line, h_line + len(members))

    def target(k):
        return jnp.stack([field(y, z)[pl.ds(k, SUBLANES, stride=steps), :] for y, z in members], 0)

    def keep(k, h):
        h_ref[k, kept_at] = h

    ends = eliminate(
        target, steps, lambda k: w_ref[k, at], lambda k: i_ref[k, at], lambda k: p_ref[k, at], keep
    )
    for q in range(2):
        for i in range(len(members)):
            first = (first_line + i) * SUBLANES
            q_s[q, first : first + SUBLANES, :] = ends[q][i]


def x_factor_kernel(plate, loc, energy, t_ref, b_ref, after, *refs):
    c_ref, total_ref, w_ref, i_ref, p_ref, links, view, h_ref, ends_ref, t_out, q_s, t_s = refs
    chunks, sheets, rows, _ = c_ref.shape
    lines = chunks * sheets
    steps = rows // SUBLANES
    plane = source_plane(loc, energy, rows, chunks * LANES, plate)

    lane = lax.broadcasted_iota(jnp.int32, (SUBLANES, LANES), 1)
    is_first, is_last = lane == 0, lane == LANES - 1
    for r in range(steps):
        at = slice(r * SUBLANES, (r + 1) * SUBLANES)
        before_t, before_c = None, None
        for z in range(sheets):
            ts = [t_ref[z, at, part_of(y)] for y in range(chunks)]
            cs = [half_conduct(b_ref[z, at, part_of(y)], ts[y]) for y in range(chunks)]
            t_turned = [pltpu.roll(v, LANES - 1, 1) for v in ts]
            c_turned = [pltpu.roll(v, LANES - 1, 1) for v in cs]
            flux = []
            for y in range(chunks):
                if y < chunks - 1:
                    t_next = jnp.where(is_last, t_turned[y + 1], t_turned[y])
                    c_next = jnp.where(is_last, c_turned[y + 1], c_turned[y])
                    flux.append((cs[y] + c_next) * (t_next - ts[y]))
                else:
                    inside = (cs[y] + c_turned[y]) * (t_turned[y] - ts[y])
                    flux.append(jnp.where(is_last, 0.0, inside))
            turned = [pltpu.roll(v, 1, 1) for v in flux]
            for y in range(chunks):
                from_low = jnp.where(is_first, turned[y - 1] if y else 0.0, turned[y])
                total = ts[y] + (flux[y] - from_low)
                if z == 0:
                    total = total + plane[at, part_of(y)]
                else:
                    across = (before_c[y] + cs[y]) * (ts[y] - before_t[y])
                    total = total - across
                    total_ref[y, z - 1, at, :] += across
                total_ref[y, z, at, :] = total
                c_ref[y, z, at, :] = cs[y]
                t_s[y, z, at, :] = ts[y]
            before_t, before_c = ts, cs

    at = 0
    for n, members in enumerate(line_groups(chunks, sheets)):

        def cond(k):
            return jnp.stack([c_ref[y, z, pl.ds(k, SUBLANES, stride=steps), :] for y, z in members], 0)

        def keep(k, w, inv, p):
            w_ref[k, at : at + len(members)] = w
            i_ref[k, at : at + len(members)] = inv
            p_ref[k, at : at + len(members)] = p

        block = factor(cond, steps, keep)
        for i, q in enumerate(COEFS):
            for j in range(len(members)):
                first = (at + j) * SUBLANES
                q_s[i, first : first + SUBLANES, :] = block[q][j]
        if n > 0:
            x_eliminate(
                lambda y, z: total_ref.at[y, z], members, at, w_ref, i_ref, p_ref, h_ref,
                at - 2 * sheets, ends_ref,
            )
        for k in range(steps):
            for i, (y, z) in enumerate(members):
                t_out[k, at + i] = t_s[y, z, pl.ds(k, SUBLANES, stride=steps), :]
        at += len(members)

    segments = [
        {q: q_s[n, pl.ds(s, lines, stride=SUBLANES), :] for n, q in enumerate(COEFS)}
        for s in range(SUBLANES)
    ]
    whole, levels = tree(segments, join_coefs)
    for (offset, _), level in zip(node_offsets(SUBLANES), levels):
        for n, values in enumerate(level):
            for i in range(3):
                links[offset + n, i] = values[i]
    for n, q in enumerate(COEFS):
        view[n] = whole[q]


def x_factor(loc, energy, t, b, plate, after):
    sheets, rows, columns = t.shape
    chunks = columns // LANES
    lines = chunks * sheets
    steps = rows // SUBLANES
    field = shape_of(chunks, sheets, rows, LANES)
    stored = shape_of(steps, lines, SUBLANES, LANES)
    return pl.pallas_call(
        functools.partial(x_factor_kernel, plate),
        in_specs=[IN_VMEM] * 4 + [ANYWHERE],
        out_shape=[
            field,
            field,
            stored,
            stored,
            stored,
            shape_of(SUBLANES - 1, 3, lines, LANES),
            shape_of(len(COEFS), lines, LANES),
            shape_of(steps, max(1, lines - 2 * sheets), SUBLANES, LANES),
            shape_of(2, lines * SUBLANES, LANES),
            stored,
        ],
        scratch_shapes=[
            pltpu.VMEM((len(COEFS), lines * SUBLANES, LANES), F32),
            pltpu.VMEM((chunks, sheets, rows, LANES), F32),
        ],
        compiler_params=params(),
        cost_estimate=pl.CostEstimate(flops=40 * t.size, bytes_accessed=28 * t.size, transcendentals=0),
    )(loc, energy, t, b, after)


def far_side(sources):
    place = lax.axis_index("gy")
    paired = (place >> 1) % 2 != place % 2
    nothing = jnp.zeros(sources[0].shape, F32)
    by_pair = sources[1][...] if len(sources) > 1 else nothing
    other = sources[2][...] if len(sources) > 2 else nothing
    return jnp.where(paired, by_pair, other)


def x_target_kernel(count, own_cells, t_ref, total_ref, *refs):
    w_ref, i_ref, p_ref, links, view, ends_ref, h_ref, own, send, e_s, q_s = refs[count:]
    chunks, sheets, rows, _ = total_ref.shape
    lines = chunks * sheets

    lane = lax.broadcasted_iota(jnp.int32, (rows, LANES), 1)
    side = 2 * sheets
    near, far = (unfold(v, 2 * side, rows) for v in (refs[0][...], far_side(refs[:count])))
    before = jnp.where(is_odd("gy"), near, far)
    after = jnp.where(is_odd("gy"), far, near)
    beyond = jnp.where(lane < side, pltpu.roll(before, LANES - side, 1), pltpu.roll(after, side, 1))
    mine = unfold(own_cells[...], 2 * side, rows)
    face = jnp.where(beyond > 0.0, mine + beyond, 0.0)
    flux = pltpu.roll(face, LANES - sheets, 1) * (beyond - mine)
    for n, (y, edge) in enumerate(((0, 0), (chunks - 1, LANES - 1))):
        for z in range(sheets):
            at = n * side + z
            e_s[n, z] = total_ref[y, z] + jnp.where(lane == edge, flux[:, at : at + 1], 0.0)

    members = line_groups(chunks, sheets)[0]
    x_eliminate(
        lambda y, z: e_s.at[0 if y == 0 else 1, z], members, 0, w_ref, i_ref, p_ref, h_ref, 0, q_s
    )
    split = len(members)
    items = [
        tuple(
            jnp.concatenate(
                [
                    q_s[q, pl.ds(s, split, stride=SUBLANES), :],
                    ends_ref[q, pl.ds(split * SUBLANES + s, lines - split, stride=SUBLANES), :],
                ],
                0,
            )
            for q in range(2)
        )
        for s in range(SUBLANES)
    ]
    for offset, count in node_offsets(SUBLANES):
        joined = []
        for n in range(count):
            ties = tuple(links[offset + n, i] for i in range(3))
            both, flux = join_targets(items[2 * n], items[2 * n + 1], ties)
            own[offset + n] = flux
            joined.append(both)
        items = joined
    for n, q in enumerate(COEFS):
        send[q] = view[n]
    send[FIRST], send[LAST] = items[0]


def x_target(own_cells, t, total, edge_cells, w, inv, p, links, view, ends):
    chunks, sheets, rows, _ = total.shape
    lines = chunks * sheets
    steps = rows // SUBLANES
    return pl.pallas_call(
        functools.partial(x_target_kernel, len(edge_cells)),
        out_shape=[
            shape_of(steps, 2 * sheets, SUBLANES, LANES),
            shape_of(SUBLANES - 1, lines, LANES),
            shape_of(7, lines, LANES),
        ],
        scratch_shapes=[
            pltpu.VMEM((2, sheets, rows, LANES), F32),
            pltpu.VMEM((2, 2 * sheets * SUBLANES, LANES), F32),
        ],
        compiler_params=params(),
    )(own_cells, t, total, *edge_cells, w, inv, p, links, view, ends)


def stages_of(axis):
    return lax.axis_size(axis).bit_length() - 1


def swap(value, axis, flip):
    count = lax.axis_size(axis)
    return lax.ppermute(value, axis, [(i, i ^ flip) for i in range(count)])


def on_right(axis, stage):
    return (lax.axis_index(axis) >> stage) % 2 == 1


def toward(right, block):
    return (
        jnp.where(right, block[R00], block[RLL]),
        jnp.where(right, block[FIRST], block[LAST]),
        jnp.where(right, block[C0], block[CL]),
    )


def join(a, b):
    joined, ties = join_coefs(a, b)
    (joined[FIRST], joined[LAST]), flux = join_targets((a[FIRST], a[LAST]), (b[FIRST], b[LAST]), ties)
    return joined, (flux, ties[1], ties[2])


def ordered(right, own, other):
    first = [jnp.where(right, theirs, mine) for mine, theirs in zip(own, other)]
    second = [jnp.where(right, mine, theirs) for mine, theirs in zip(own, other)]
    return first, second


def join_kernel(axis, stage, width, last, *refs):
    count = 1 << width
    blocks = [[refs[i][q] for q in range(7)] for i in range(count)]
    send = refs[-1 - width]
    links = refs[-width:]
    for bit in range(width):
        right = on_right(axis, stage + bit)
        for i in range(count):
            if not i >> bit & 1:
                j = i | 1 << bit
                blocks[i], blocks[j] = ordered(right, blocks[i], blocks[j])
    for bit in range(width):
        pairs = [join(blocks[i], blocks[i + 1]) for i in range(0, len(blocks), 2)]
        blocks = [p[0] for p in pairs]
        ties = [p[1] for p in pairs]
        for upper in range(bit + 1, width):
            right = on_right(axis, stage + upper)
            ties = [
                tuple(jnp.where(right, v, u) for u, v in zip(ties[i], ties[i + 1]))
                for i in range(0, len(ties), 2)
            ]
        for i in range(3):
            links[bit][i] = ties[0][i]
    (whole,) = blocks
    if last:
        for n, value in enumerate(toward(on_right(axis, stage + width), whole)):
            send[n] = value
    else:
        for q in range(7):
            send[q] = whole[q]


def join_stage(own, got, axis, stage, width, last, after):
    lines = own.shape[1]
    return pl.pallas_call(
        functools.partial(join_kernel, axis, stage, width, last),
        in_specs=[IN_VMEM] * (1 + len(got)) + [ANYWHERE] * len(after),
        out_shape=[shape_of(3 if last else 7, lines, LANES)] + [shape_of(3, lines, LANES)] * width,
        compiler_params=params(),
    )(own, *got, *after)


def gather_line(view, axis, widest=1, meanwhile=()):
    stages = stages_of(axis)
    links, stage = [], 0
    while stage < stages - 1:
        width = min(widest, stages - 1 - stage)
        got = [swap(view, axis, flip << stage) for flip in range(1, 1 << width)]
        last = stage + width == stages - 1
        view, *ties = join_stage(view, got, axis, stage, width, last, meanwhile)
        links += ties
        stage += width
        meanwhile = ()
    return view, swap(view, axis, 1 << stage), links


def top_flux(axis, stages, own, got):
    right = on_right(axis, stages - 1)
    face = own[2] + got[2]
    jump = jnp.where(right, own[1] - got[1], got[1] - own[1])
    return jump * face * inverse(1.0 + face * (own[0] + got[0]))


def block_ends(axis, stages, links):
    shape = links[0].shape[1:] if links else None
    right = on_right(axis, stages - 1)
    zero = jnp.zeros(shape, F32)
    low, high = zero, zero
    unit_low = zero + jnp.where(right, -1.0, 0.0)
    unit_high = zero + jnp.where(right, 0.0, 1.0)
    for stage in range(stages - 2, -1, -1):
        tie = links[stage]
        right = on_right(axis, stage)
        flux = between(tie[0], tie[1], tie[2], low, high)
        unit = between(0.0, tie[1], tie[2], unit_low, unit_high)
        low, high = jnp.where(right, -flux, low), jnp.where(right, high, flux)
        unit_low, unit_high = jnp.where(right, -unit, unit_low), jnp.where(right, unit_high, unit)
    return (low, high), (unit_low, unit_high)


def natural(index, parts):
    span = SUBLANES * parts
    local = index % span
    return index - local + local % SUBLANES * parts + local // SUBLANES


def turn_matrix(shape, from_natural, parts):
    row = lax.broadcasted_iota(jnp.int32, shape, 0)
    column = lax.broadcasted_iota(jnp.int32, shape, 1) % LANES
    hit = natural(row, parts) == column if from_natural else row == natural(column, parts)
    return jnp.where(hit, 1.0, 0.0).astype(jnp.bfloat16)


def turned(matrix, field):
    high = field.astype(jnp.bfloat16)
    low = (field - high.astype(F32)).astype(jnp.bfloat16)
    both = jnp.concatenate([high, low], 1)
    return lax.dot_general(
        matrix, both, (((1,), (1,)), ((), ())), preferred_element_type=F32
    )


def y_factor_kernel(c_ref, after, w_ref, i_ref, p_ref, inner, outer, view, to_y, to_x, c_s, q_s, r_s):
    chunks, sheets, rows, _ = c_ref.shape
    each = LANES // rows
    pairs = sheets // each
    x_steps = rows // SUBLANES
    steps = LANES // SUBLANES
    to_y[...] = turn_matrix(to_y.shape, True, steps)
    to_x[...] = turn_matrix(to_x.shape, False, x_steps)
    for m in range(pairs):
        for y in range(chunks):
            block = jnp.concatenate(
                [
                    c_ref[y, m * each + i, pl.ds(k, SUBLANES, stride=x_steps), :]
                    for i in range(each)
                    for k in range(x_steps)
                ],
                0,
            )
            c_s[m, part_of(y), :] = block.T

    members = [(y, m) for y in range(chunks) for m in range(pairs)]
    lines = len(members)

    def cond(k):
        return jnp.stack([c_s[m, pl.ds(y * LANES + k, SUBLANES, stride=steps), :] for y, m in members], 0)

    def keep(k, w, inv, p):
        w_ref[k] = w
        i_ref[k] = inv
        p_ref[k] = p

    block = factor(cond, steps, keep)
    for n, q in enumerate(COEFS):
        for i in range(lines):
            q_s[n, i * SUBLANES : (i + 1) * SUBLANES, :] = block[q][i]
    segments = [
        {q: q_s[n, pl.ds(s, lines, stride=SUBLANES), :] for n, q in enumerate(COEFS)}
        for s in range(SUBLANES)
    ]
    whole, levels = tree(segments, join_coefs)
    for (offset, _), level in zip(node_offsets(SUBLANES), levels):
        for n, values in enumerate(level):
            for i in range(3):
                inner[offset + n, i] = values[i]
    for n, q in enumerate(COEFS):
        r_s[n] = whole[q]
    parts = [
        {q: r_s[n, y * pairs : (y + 1) * pairs, :] for n, q in enumerate(COEFS)} for y in range(chunks)
    ]
    whole, levels = tree(parts, join_coefs)
    for (offset, _), level in zip(node_offsets(chunks), levels):
        for n, values in enumerate(level):
            for i in range(3):
                outer[offset + n, i] = values[i]
    for n, q in enumerate(COEFS):
        view[n] = whole[q]


def y_factor(c, after):
    chunks, sheets, rows, _ = c.shape
    pairs = sheets * rows // LANES
    lines = chunks * pairs
    stored = shape_of(LANES // SUBLANES, lines, SUBLANES, LANES)
    matrix = jax.ShapeDtypeStruct((LANES, 2 * LANES), jnp.bfloat16)
    return pl.pallas_call(
        y_factor_kernel,
        in_specs=[IN_VMEM, ANYWHERE],
        out_shape=[
            stored,
            stored,
            stored,
            shape_of(SUBLANES - 1, 3, lines, LANES),
            shape_of(chunks - 1, 3, pairs, LANES),
            shape_of(len(COEFS), pairs, LANES),
            matrix,
            matrix,
        ],
        scratch_shapes=[
            pltpu.VMEM((pairs, chunks * LANES, LANES), F32),
            pltpu.VMEM((len(COEFS), lines * SUBLANES, LANES), F32),
            pltpu.VMEM((len(COEFS), lines, LANES), F32),
        ],
        compiler_params=params(),
        cost_estimate=pl.CostEstimate(flops=20 * c.size, bytes_accessed=16 * c.size, transcendentals=0),
    )(c, after)


def z_factor_kernel(c_ref, after, w_ref, i_ref):
    sheets = c_ref.shape[1]
    ground = 1.0
    for z in range(sheets - 1):
        face = c_ref[:, z] + c_ref[:, z + 1]
        inv = inverse(ground + face)
        w = face * inv
        i_ref[z] = inv
        w_ref[z] = w
        ground = 1.0 + w * ground
    i_ref[sheets - 1] = inverse(ground)


def z_factor(c, after):
    chunks, sheets, rows, _ = c.shape
    return pl.pallas_call(
        z_factor_kernel,
        in_specs=[IN_VMEM, ANYWHERE],
        out_shape=[
            shape_of(sheets - 1, chunks, rows, LANES),
            shape_of(sheets, chunks, rows, LANES),
        ],
        compiler_params=params(),
        cost_estimate=pl.CostEstimate(flops=10 * c.size, bytes_accessed=12 * c.size, transcendentals=0),
    )(c, after)


def join_tree(items, links, own):
    for offset, count in node_offsets(len(items)):
        joined = []
        for n in range(count):
            tie = tuple(links[offset + n, i] for i in range(3))
            both, flux = join_targets(items[2 * n], items[2 * n + 1], tie)
            own[offset + n] = flux
            joined.append(both)
        items = joined
    return items[0]


def tree_ends(leaves, links, own, low, high):
    levels = [
        [(own(offset + n), links[offset + n, 1], links[offset + n, 2]) for n in range(count)]
        for offset, count in node_offsets(leaves)
    ]
    return descend(levels, low, high)


def nothing(node):
    return 0.0


def y_prepare_kernel(stages, *refs):
    ties = refs[: stages - 1]
    xw, xh, xm, xp, x_links, x_own, t_ref, to_y = refs[stages - 1 : stages + 7]
    base, response, f_s, g_s = refs[stages + 7 :]
    x_steps, lines = xw.shape[:2]
    chunks = base.shape[0]
    sheets = lines // chunks
    rows = x_steps * SUBLANES

    ends, units = block_ends("gx", stages, ties)
    for n, (own, (low, high)) in enumerate(((lambda i: x_own[i], ends), (nothing, units))):
        for s, pair in enumerate(tree_ends(SUBLANES, x_links, own, low, high)):
            for i in range(2):
                f_s[n, i, pl.ds(s, lines, stride=SUBLANES), :] = pair[i]
    first = 0
    for n, members in enumerate(line_groups(chunks, sheets)):
        at = slice(first, first + len(members))
        h_ref_of, h_at = (xh, at) if n == 0 else (xm, slice(first - 2 * sheets, at.stop - 2 * sheets))
        (low, value), (unit_low, unit) = (
            [
                jnp.stack(
                    [f_s[q, i, j * SUBLANES : (j + 1) * SUBLANES, :] for j in range(at.start, at.stop)], 0
                )
                for i in range(2)
            ]
            for q in range(2)
        )
        for k in range(x_steps - 1, -1, -1):
            w, p = xw[k, at], xp[k, at]
            value = w * value + (h_ref_of[k, h_at] + p * low)
            unit = w * unit + p * unit_low
            field = value - t_ref[k, at]
            for j, (y, z) in enumerate(members):
                place = z * rows + k * SUBLANES
                g_s[0, y, place : place + SUBLANES, :] = field[j]
                g_s[1, y, place : place + SUBLANES, :] = unit[j]
        first = at.stop

    for y in range(chunks):
        base[y] = turned(to_y[...], g_s[0, y])
        response[y] = turned(to_y[...], g_s[1, y])


def y_prepare(ties, xw, xh, xm, xp, x_links, x_own, t, to_y, chunks):
    x_steps, lines = xw.shape[:2]
    width = lines // chunks * x_steps * SUBLANES
    field = shape_of(chunks, LANES, width)
    return pl.pallas_call(
        functools.partial(y_prepare_kernel, len(ties) + 1),
        out_shape=[field, field],
        scratch_shapes=[
            pltpu.VMEM((2, 2, lines * SUBLANES, LANES), F32),
            pltpu.VMEM((2, chunks, width, LANES), F32),
        ],
        compiler_params=params(),
        cost_estimate=pl.CostEstimate(flops=8 * t.size, bytes_accessed=16 * t.size, transcendentals=0),
    )(*ties, xw, xh, xm, xp, x_links, x_own, t, to_y)


def y_target_kernel(stages, own, got, base, response, yw, yi, yp, inner, outer, view, to_y, *refs):
    h_ref, inner_own, outer_own, send, q_s, r_s = refs
    chunks, _, width = base.shape
    pairs = width // LANES
    sheets = own.shape[1] // chunks
    rows = width // sheets
    steps = yw.shape[0]

    flux = top_flux("gx", stages, own, got)
    line_of = {member: n for n, member in enumerate(sum(line_groups(chunks, sheets), []))}
    fields = []
    for y in range(chunks):
        spread = jnp.concatenate(
            [
                jnp.broadcast_to(flux[line_of[y, z] : line_of[y, z] + 1, :], (rows, LANES))
                for z in range(sheets)
            ],
            0,
        )
        fields.append(base[y] + response[y] * turned(to_y[...], spread))

    def target(k):
        at = slice(k * SUBLANES, (k + 1) * SUBLANES)
        return jnp.stack(
            [fields[y][at, m * LANES : (m + 1) * LANES] for y in range(chunks) for m in range(pairs)], 0
        )

    def keep(k, h):
        h_ref[k] = h

    ends = eliminate(target, steps, lambda k: yw[k], lambda k: yi[k], lambda k: yp[k], keep)
    for q in range(2):
        for i in range(chunks * pairs):
            q_s[q, i * SUBLANES : (i + 1) * SUBLANES, :] = ends[q][i]
    items = [
        tuple(q_s[q, pl.ds(s, chunks * pairs, stride=SUBLANES), :] for q in range(2))
        for s in range(SUBLANES)
    ]
    r_s[0], r_s[1] = join_tree(items, inner, inner_own)
    items = [tuple(r_s[q, y * pairs : (y + 1) * pairs, :] for q in range(2)) for y in range(chunks)]
    for n, q in enumerate(COEFS):
        send[q] = view[n]
    send[FIRST], send[LAST] = join_tree(items, outer, outer_own)


def y_target(own, got, base, response, yw, yi, yp, inner, outer, view, to_y):
    y_lines = yw.shape[1]
    pairs = view.shape[1]
    chunks = y_lines // pairs
    return pl.pallas_call(
        functools.partial(y_target_kernel, stages_of("gx")),
        out_shape=[
            shape_of(*yw.shape),
            shape_of(SUBLANES - 1, y_lines, LANES),
            shape_of(chunks - 1, pairs, LANES),
            shape_of(7, pairs, LANES),
        ],
        scratch_shapes=[
            pltpu.VMEM((2, y_lines * SUBLANES, LANES), F32),
            pltpu.VMEM((2, y_lines, LANES), F32),
        ],
        compiler_params=params(),
    )(own, got, base, response, yw, yi, yp, inner, outer, view, to_y)


def z_solve(zw, zi, field, at, keep):
    sheets = zi.shape[0]
    rhs, kept = None, []
    for z in range(sheets):
        rhs = field(z) if z == 0 else field(z) + zw[z - 1, at] * rhs
        kept.append(rhs * zi[z, at])
    value = kept[-1]
    keep(sheets - 1, value)
    for z in range(sheets - 2, -1, -1):
        value = zw[z, at] * value + kept[z]
        keep(z, value)


def finish_prepare_kernel(stages, *refs):
    ties = refs[: stages - 1]
    yw, yh, yp, inner, inner_own, outer, outer_own, zw, zi, t_ref, to_x = refs[stages - 1 : stages + 10]
    base, response, r_s, e_s, u_s = refs[stages + 10 :]
    chunks, sheets, rows, _ = base.shape
    each = LANES // rows
    pairs = sheets // each
    steps = yw.shape[0]
    lines = chunks * pairs

    ends, units = block_ends("gy", stages, ties)
    both = (
        (lambda i: outer_own[i], lambda i: inner_own[i], ends),
        (nothing, nothing, units),
    )
    for n, (upper, lower, (low, high)) in enumerate(both):
        for y, pair in enumerate(tree_ends(chunks, outer, upper, low, high)):
            for i in range(2):
                r_s[n, i, y * pairs : (y + 1) * pairs, :] = pair[i]
        for s, pair in enumerate(tree_ends(SUBLANES, inner, lower, r_s[n, 0], r_s[n, 1])):
            for i in range(2):
                e_s[n, i, pl.ds(s, lines, stride=SUBLANES), :] = pair[i]
    (low, value), (unit_low, unit) = (
        [
            jnp.stack([e_s[q, i, n * SUBLANES : (n + 1) * SUBLANES, :] for n in range(lines)], 0)
            for i in range(2)
        ]
        for q in range(2)
    )
    for k in range(steps - 1, -1, -1):
        w, p = yw[k], yp[k]
        value = w * value + (yh[k] + p * low)
        unit = w * unit + p * unit_low
        for y in range(chunks):
            for m in range(pairs):
                place = pl.ds(y * LANES + k, SUBLANES, stride=steps)
                u_s[0, m, place, :] = value[y * pairs + m]
                u_s[1, m, place, :] = unit[y * pairs + m]

    for y in range(chunks):
        part = part_of(y)
        fields = [turned(to_x[...], u_s[0, m, part, :]) for m in range(pairs)]

        def field(z):
            at = z % each * rows
            return fields[z // each][at : at + rows, :]

        def keep(z, value):
            base[y, z] = t_ref[z, :, part] + value

        z_solve(zw, zi, field, y, keep)
        for m in range(pairs):
            units = turned(to_x[...], u_s[1, m, part, :])
            for i in range(each):
                response[y, m * each + i] = units[i * rows : (i + 1) * rows, :]


def finish_prepare(ties, yw, yh, yp, inner, inner_own, outer, outer_own, zw, zi, t, to_x):
    sheets, rows, columns = t.shape
    chunks = columns // LANES
    pairs = sheets * rows // LANES
    lines = chunks * pairs
    field = shape_of(chunks, sheets, rows, LANES)
    return pl.pallas_call(
        functools.partial(finish_prepare_kernel, len(ties) + 1),
        out_shape=[field, field],
        scratch_shapes=[
            pltpu.VMEM((2, 2, lines, LANES), F32),
            pltpu.VMEM((2, 2, lines * SUBLANES, LANES), F32),
            pltpu.VMEM((2, pairs, columns, LANES), F32),
        ],
        compiler_params=params(),
        cost_estimate=pl.CostEstimate(flops=12 * t.size, bytes_accessed=20 * t.size, transcendentals=0),
    )(*ties, yw, yh, yp, inner, inner_own, outer, outer_own, zw, zi, t, to_x)


def finish_kernel(stages, own, got, base, response, zw, zi, to_x, out, o_s, sems):
    chunks, sheets, rows, _ = base.shape
    each = LANES // rows
    pairs = sheets // each
    copies, _, _, wide = o_s.shape

    flux = top_flux("gy", stages, own, got)
    spread = [
        turned(to_x[...], jnp.broadcast_to(flux[m : m + 1, :], (LANES, LANES))) for m in range(pairs)
    ]
    started = []
    for n in range(copies):
        for y in range(n * chunks // copies, (n + 1) * chunks // copies):
            part = part_of(y - n * chunks // copies)

            def field(z):
                at = z % each * rows
                return response[y, z] * spread[z // each][at : at + rows, :]

            def keep(z, value):
                o_s[n, z, :, part] = base[y, z] + value

            z_solve(zw, zi, field, y, keep)
        copy = pltpu.make_async_copy(o_s.at[n], out.at[:, :, pl.ds(n * wide, wide)], sems.at[n])
        copy.start()
        started.append(copy)
    for copy in started:
        copy.wait()


def finish(own, got, base, response, zw, zi, to_x):
    chunks, sheets, rows, _ = base.shape
    copies = chunks
    return pl.pallas_call(
        functools.partial(finish_kernel, stages_of("gy")),
        out_shape=shape_of(sheets, rows, chunks * LANES),
        out_specs=ANYWHERE,
        scratch_shapes=[
            pltpu.VMEM((copies, sheets, rows, chunks * LANES // copies), F32),
            pltpu.SemaphoreType.DMA((copies,)),
        ],
        compiler_params=params(),
    )(own, got, base, response, zw, zi, to_x)


def per_device(temperature, base, locations, energy):
    columns = temperature.shape[2]
    gy = lax.axis_size("gy")
    packed = edges(temperature, base)
    near = swap(packed, "gy", 1)
    t, b, loc, heat = load((temperature, base, locations[None], energy[None]), packed)
    near, t, b = lax.optimization_barrier((near, t, b))
    far = [swap(near, "gy", 2)] if gy > 2 else []
    if gy > 4:
        far.append(lax.ppermute(near, "gy", [(i, (i + 2 ^ 2) - 2) for i in range(2, gy - 2)]))
    c, total, xw, xi, xp, x_links, x_view, xm, ends, t_steps = x_factor(loc, heat, t, b, columns * gy, near)
    xh, x_own, view = x_target(packed, t, total, [near] + far, xw, xi, xp, x_links, x_view, ends)
    yw, yi, yp, inner, outer, y_view, to_y, to_x = y_factor(c, x_view)
    zw, zi = z_factor(c, view)
    own, got, ties = gather_line(view, "gx", 2, (y_view, zw))
    base, response = y_prepare(
        ties, xw, xh, xm, xp, x_links, x_own, t_steps, to_y, columns // LANES
    )
    yh, inner_own, outer_own, view = y_target(
        own, got, base, response, yw, yi, yp, inner, outer, y_view, to_y
    )
    own, got, ties = gather_line(view, "gy")
    base, response = finish_prepare(
        ties, yw, yh, yp, inner, inner_own, outer, outer_own, zw, zi, t, to_x
    )
    return finish(own, got, base, response, zw, zi, to_x)


def solution(mesh):
    in_specs = (P(None, "gx", "gy"), P(None, "gx", "gy"), P(), P())
    out_specs = P(None, "gx", "gy")
    return jax.shard_map(
        per_device, mesh=mesh, in_specs=in_specs, out_specs=out_specs, check_vma=False
    )
```

```python
import functools

import jax
import jax.numpy as jnp
from jax import lax
from jax.experimental import pallas as pl
from jax.experimental.pallas import tpu as pltpu
from jax.sharding import PartitionSpec as P

RATE = 2000.0
THERMAL_GROWTH = 0.8
LANES = 128
SUBLANES = 8
F32 = jnp.float32
MIB = 1024 * 1024
ANYWHERE = pl.BlockSpec(memory_space=pl.ANY)
IN_HBM = pl.BlockSpec(memory_space=pltpu.HBM)
IN_VMEM = pl.BlockSpec(memory_space=pltpu.VMEM)

R00, R0L, RLL, FIRST, LAST, C0, CL = range(7)
COEFS = (R00, R0L, RLL, C0, CL)


def params(limit=40):
    return pltpu.CompilerParams(vmem_limit_bytes=limit * MIB)


def shape_of(*sizes):
    return jax.ShapeDtypeStruct(sizes, F32)


def half_conduct(base, temperature):
    return base * (0.5 * RATE + (0.5 * RATE * THERMAL_GROWTH) * temperature)


def inverse(x):
    guess = pl.reciprocal(x, approx=True)
    return guess * (2.0 - x * guess)


def join_coefs(a, b):
    face = a[CL] + b[C0]
    inv = face * inverse(1.0 + face * (a[RLL] + b[R00]))
    left = a[R0L] * inv
    right = b[R0L] * inv
    joined = {
        R00: a[R00] - left * a[R0L],
        R0L: left * b[R0L],
        RLL: b[RLL] - right * b[R0L],
        C0: a[C0],
        CL: b[CL],
    }
    return joined, (inv, right, left)


def join_targets(a, b, links):
    inv, right, left = links
    jump = b[0] - a[1]
    return (a[0] + left * jump, b[1] - right * jump), jump * inv


def between(own, right, left, low, high):
    return own + right * high - left * low


def tree(items, join):
    levels = []
    while len(items) > 1:
        pairs = [join(items[i], items[i + 1]) for i in range(0, len(items), 2)]
        items = [p[0] for p in pairs]
        levels.append([p[1] for p in pairs])
    return items[0], levels


def descend(levels, low, high):
    ends = [(low, high)]
    for level in reversed(levels):
        below = []
        for (lo, hi), (own, right, left) in zip(ends, level):
            flux = between(own, right, left, lo, hi)
            below += [(lo, flux), (-flux, hi)]
        ends = below
    return ends


def node_offsets(leaves):
    offsets, at, count = [], 0, leaves // 2
    while count:
        offsets.append((at, count))
        at += count
        count //= 2
    return offsets


def factor(cond, steps, keep):
    here = cond(0)
    c_first = here
    one = jnp.ones_like(here)
    ground, path, first_first = one, one, None
    for k in range(steps - 1):
        following = cond(k + 1)
        face = here + following
        inv = inverse(ground + face)
        w = face * inv
        p = path * inv
        keep(k, w, inv, p)
        step = path * p
        first_first = step if first_first is None else first_first + step
        path = path * w
        ground = 1.0 + w * ground
        here = following
    inv = inverse(ground)
    p = path * inv
    keep(steps - 1, inv, inv, p)
    return {R00: first_first + path * p, R0L: p, RLL: inv, C0: c_first, CL: here}


def eliminate(target, steps, w, inv, p, keep):
    rhs = target(0)
    first = None
    for k in range(steps):
        h = rhs * inv(k)
        keep(k, h)
        step = rhs * p(k)
        first = step if first is None else first + step
        if k < steps - 1:
            rhs = target(k + 1) + w(k) * rhs
    return first, h


def is_odd(axis):
    return lax.axis_index(axis) % 2 == 1


def fold(cells, used):
    total = cells[:SUBLANES]
    lane = lax.broadcasted_iota(jnp.int32, total.shape, 1)
    for n in range(1, cells.shape[0] // SUBLANES):
        part = pltpu.roll(cells[n * SUBLANES : (n + 1) * SUBLANES], n * used, 1)
        total = jnp.where(lane // used == n, part, total)
    return total


def unfold(cells, used, rows):
    parts = [cells] + [
        pltpu.roll(cells, LANES - n * used, 1) for n in range(1, rows // SUBLANES)
    ]
    return jnp.concatenate(parts, 0)


def edges_kernel(t_hbm, b_hbm, packed, t_s, b_s, sems):
    sheets, rows, columns = t_hbm.shape
    sides = []
    for side, start in enumerate((0, columns - LANES)):
        sides.append(
            [
                pltpu.make_async_copy(src.at[:, :, pl.ds(start, LANES)], dst.at[side], sems.at[i, side])
                for i, (src, dst) in enumerate(((t_hbm, t_s), (b_hbm, b_s)))
            ]
        )
        for copy in sides[-1]:
            copy.start()
    lane = lax.broadcasted_iota(jnp.int32, (rows, LANES), 1)
    total = jnp.zeros((rows, LANES), F32)
    for side, source in enumerate((0, LANES - 1)):
        for copy in sides[side]:
            copy.wait()
        for z in range(sheets):
            t = t_s[side, z]
            c = half_conduct(b_s[side, z], t)
            place = 2 * sheets * side + z
            total = jnp.where(lane == place, t[:, source : source + 1], total)
            total = jnp.where(lane == place + sheets, c[:, source : source + 1], total)
    packed[...] = fold(total, 4 * sheets)


def edges(temperature, base):
    sheets, rows, _ = temperature.shape
    assert rows // SUBLANES * 4 * sheets <= LANES
    return pl.pallas_call(
        edges_kernel,
        in_specs=[IN_HBM] * 2,
        out_shape=pltpu.VMEM((SUBLANES, LANES), F32),
        scratch_shapes=[
            pltpu.VMEM((2, sheets, rows, LANES), F32),
            pltpu.VMEM((2, sheets, rows, LANES), F32),
            pltpu.SemaphoreType.DMA((2, 2)),
        ],
        compiler_params=params(),
    )(*[pltpu.with_memory_space_constraint(v, pltpu.HBM) for v in (temperature, base)])


def load_kernel(*refs):
    count = len(refs) // 2 - 1
    sems = refs[-1]
    copies = [
        pltpu.make_async_copy(refs[i], refs[count + 1 + i], sems.at[i]) for i in range(count)
    ]
    for copy in copies:
        copy.start()
    for copy in copies:
        copy.wait()


def load(values, after):
    return pl.pallas_call(
        load_kernel,
        in_specs=[IN_HBM] * len(values) + [ANYWHERE],
        out_shape=[pltpu.VMEM(v.shape, v.dtype) for v in values],
        scratch_shapes=[pltpu.SemaphoreType.DMA((len(values),))],
        compiler_params=params(),
        cost_estimate=pl.CostEstimate(
            flops=0, bytes_accessed=16 * values[0].size, transcendentals=0
        ),
    )(*[pltpu.with_memory_space_constraint(v, pltpu.HBM) for v in values], after)


def source_plane(loc, energy, rows, columns, plate):
    place = loc[...]
    count = place.shape[1]
    local_x = place // plate - lax.axis_index("gx") * rows
    local_y = place % plate - lax.axis_index("gy") * columns
    in_x = lax.broadcasted_iota(jnp.int32, (rows, count), 0) == local_x
    in_y = lax.broadcasted_iota(jnp.int32, (columns, count), 0) == local_y
    by_y = jnp.where(in_y, 1.0, 0.0).astype(jnp.bfloat16)
    left = energy[...]
    plane = None
    for _ in range(3):
        part = left.astype(jnp.bfloat16).astype(F32)
        left = left - part
        term = lax.dot_general(
            jnp.where(in_x, part, 0.0).astype(jnp.bfloat16),
            by_y,
            (((1,), (1,)), ((), ())),
            preferred_element_type=F32,
        )
        plane = term if plane is None else plane + term
    return plane


def part_of(y):
    return slice(y * LANES, (y + 1) * LANES)


def line_groups(chunks, sheets):
    order = [0, chunks - 1] + list(range(1, chunks - 1))
    return [[(y, z) for y in order[i : i + 2] for z in range(sheets)] for i in range(0, chunks, 2)]


def x_eliminate(field, members, first_line, w_ref, i_ref, p_ref, h_ref, h_line, q_s):
    steps = w_ref.shape[0]
    at = slice(first_line, first_line + len(members))
    kept_at = slice(h_line, h_line + len(members))

    def target(k):
        return jnp.stack([field(y, z)[pl.ds(k, SUBLANES, stride=steps), :] for y, z in members], 0)

    def keep(k, h):
        h_ref[k, kept_at] = h

    ends = eliminate(
        target, steps, lambda k: w_ref[k, at], lambda k: i_ref[k, at], lambda k: p_ref[k, at], keep
    )
    for q in range(2):
        for i in range(len(members)):
            first = (first_line + i) * SUBLANES
            q_s[q, first : first + SUBLANES, :] = ends[q][i]


def x_factor_kernel(plate, loc, energy, t_ref, b_ref, after, *refs):
    c_ref, total_ref, w_ref, i_ref, p_ref, links, view, h_ref, ends_ref, t_out, q_s, t_s = refs
    chunks, sheets, rows, _ = c_ref.shape
    lines = chunks * sheets
    steps = rows // SUBLANES
    plane = source_plane(loc, energy, rows, chunks * LANES, plate)

    lane = lax.broadcasted_iota(jnp.int32, (SUBLANES, LANES), 1)
    is_first, is_last = lane == 0, lane == LANES - 1
    for r in range(steps):
        at = slice(r * SUBLANES, (r + 1) * SUBLANES)
        before_t, before_c = None, None
        for z in range(sheets):
            ts = [t_ref[z, at, part_of(y)] for y in range(chunks)]
            cs = [half_conduct(b_ref[z, at, part_of(y)], ts[y]) for y in range(chunks)]
            t_turned = [pltpu.roll(v, LANES - 1, 1) for v in ts]
            c_turned = [pltpu.roll(v, LANES - 1, 1) for v in cs]
            flux = []
            for y in range(chunks):
                if y < chunks - 1:
                    t_next = jnp.where(is_last, t_turned[y + 1], t_turned[y])
                    c_next = jnp.where(is_last, c_turned[y + 1], c_turned[y])
                    flux.append((cs[y] + c_next) * (t_next - ts[y]))
                else:
                    inside = (cs[y] + c_turned[y]) * (t_turned[y] - ts[y])
                    flux.append(jnp.where(is_last, 0.0, inside))
            turned = [pltpu.roll(v, 1, 1) for v in flux]
            for y in range(chunks):
                from_low = jnp.where(is_first, turned[y - 1] if y else 0.0, turned[y])
                total = ts[y] + (flux[y] - from_low)
                if z == 0:
                    total = total + plane[at, part_of(y)]
                else:
                    across = (before_c[y] + cs[y]) * (ts[y] - before_t[y])
                    total = total - across
                    total_ref[y, z - 1, at, :] += across
                total_ref[y, z, at, :] = total
                c_ref[y, z, at, :] = cs[y]
                t_s[y, z, at, :] = ts[y]
            before_t, before_c = ts, cs

    at = 0
    for n, members in enumerate(line_groups(chunks, sheets)):

        def cond(k):
            return jnp.stack([c_ref[y, z, pl.ds(k, SUBLANES, stride=steps), :] for y, z in members], 0)

        def keep(k, w, inv, p):
            w_ref[k, at : at + len(members)] = w
            i_ref[k, at : at + len(members)] = inv
            p_ref[k, at : at + len(members)] = p

        block = factor(cond, steps, keep)
        for i, q in enumerate(COEFS):
            for j in range(len(members)):
                first = (at + j) * SUBLANES
                q_s[i, first : first + SUBLANES, :] = block[q][j]
        if n > 0:
            x_eliminate(
                lambda y, z: total_ref.at[y, z], members, at, w_ref, i_ref, p_ref, h_ref,
                at - 2 * sheets, ends_ref,
            )
        for k in range(steps):
            for i, (y, z) in enumerate(members):
                t_out[k, at + i] = t_s[y, z, pl.ds(k, SUBLANES, stride=steps), :]
        at += len(members)

    segments = [
        {q: q_s[n, pl.ds(s, lines, stride=SUBLANES), :] for n, q in enumerate(COEFS)}
        for s in range(SUBLANES)
    ]
    whole, levels = tree(segments, join_coefs)
    for (offset, _), level in zip(node_offsets(SUBLANES), levels):
        for n, values in enumerate(level):
            for i in range(3):
                links[offset + n, i] = values[i]
    for n, q in enumerate(COEFS):
        view[n] = whole[q]


def x_factor(loc, energy, t, b, plate, after):
    sheets, rows, columns = t.shape
    chunks = columns // LANES
    lines = chunks * sheets
    steps = rows // SUBLANES
    field = shape_of(chunks, sheets, rows, LANES)
    stored = shape_of(steps, lines, SUBLANES, LANES)
    return pl.pallas_call(
        functools.partial(x_factor_kernel, plate),
        in_specs=[IN_VMEM] * 4 + [ANYWHERE],
        out_shape=[
            field,
            field,
            stored,
            stored,
            stored,
            shape_of(SUBLANES - 1, 3, lines, LANES),
            shape_of(len(COEFS), lines, LANES),
            shape_of(steps, max(1, lines - 2 * sheets), SUBLANES, LANES),
            shape_of(2, lines * SUBLANES, LANES),
            stored,
        ],
        scratch_shapes=[
            pltpu.VMEM((len(COEFS), lines * SUBLANES, LANES), F32),
            pltpu.VMEM((chunks, sheets, rows, LANES), F32),
        ],
        compiler_params=params(),
        cost_estimate=pl.CostEstimate(flops=40 * t.size, bytes_accessed=28 * t.size, transcendentals=0),
    )(loc, energy, t, b, after)


def far_side(sources):
    place = lax.axis_index("gy")
    paired = (place >> 1) % 2 != place % 2
    nothing = jnp.zeros(sources[0].shape, F32)
    by_pair = sources[1][...] if len(sources) > 1 else nothing
    other = sources[2][...] if len(sources) > 2 else nothing
    return jnp.where(paired, by_pair, other)


def x_target_kernel(count, own_cells, t_ref, total_ref, *refs):
    w_ref, i_ref, p_ref, links, view, ends_ref, h_ref, own, send, e_s, q_s = refs[count:]
    chunks, sheets, rows, _ = total_ref.shape
    lines = chunks * sheets

    lane = lax.broadcasted_iota(jnp.int32, (rows, LANES), 1)
    side = 2 * sheets
    near, far = (unfold(v, 2 * side, rows) for v in (refs[0][...], far_side(refs[:count])))
    before = jnp.where(is_odd("gy"), near, far)
    after = jnp.where(is_odd("gy"), far, near)
    beyond = jnp.where(lane < side, pltpu.roll(before, LANES - side, 1), pltpu.roll(after, side, 1))
    mine = unfold(own_cells[...], 2 * side, rows)
    face = jnp.where(beyond > 0.0, mine + beyond, 0.0)
    flux = pltpu.roll(face, LANES - sheets, 1) * (beyond - mine)
    for n, (y, edge) in enumerate(((0, 0), (chunks - 1, LANES - 1))):
        for z in range(sheets):
            at = n * side + z
            e_s[n, z] = total_ref[y, z] + jnp.where(lane == edge, flux[:, at : at + 1], 0.0)

    members = line_groups(chunks, sheets)[0]
    x_eliminate(
        lambda y, z: e_s.at[0 if y == 0 else 1, z], members, 0, w_ref, i_ref, p_ref, h_ref, 0, q_s
    )
    split = len(members)
    items = [
        tuple(
            jnp.concatenate(
                [
                    q_s[q, pl.ds(s, split, stride=SUBLANES), :],
                    ends_ref[q, pl.ds(split * SUBLANES + s, lines - split, stride=SUBLANES), :],
                ],
                0,
            )
            for q in range(2)
        )
        for s in range(SUBLANES)
    ]
    for offset, count in node_offsets(SUBLANES):
        joined = []
        for n in range(count):
            ties = tuple(links[offset + n, i] for i in range(3))
            both, flux = join_targets(items[2 * n], items[2 * n + 1], ties)
            own[offset + n] = flux
            joined.append(both)
        items = joined
    for d in range(send.shape[0]):
        for n, q in enumerate(COEFS):
            send[d, q] = view[n]
        send[d, FIRST], send[d, LAST] = items[0]


def x_target(own_cells, t, total, edge_cells, w, inv, p, links, view, ends):
    chunks, sheets, rows, _ = total.shape
    lines = chunks * sheets
    steps = rows // SUBLANES
    return pl.pallas_call(
        functools.partial(x_target_kernel, len(edge_cells)),
        out_shape=[
            shape_of(steps, 2 * sheets, SUBLANES, LANES),
            shape_of(SUBLANES - 1, lines, LANES),
            shape_of(4, 7, lines, LANES),
        ],
        scratch_shapes=[
            pltpu.VMEM((2, sheets, rows, LANES), F32),
            pltpu.VMEM((2, 2 * sheets * SUBLANES, LANES), F32),
        ],
        compiler_params=params(),
    )(own_cells, t, total, *edge_cells, w, inv, p, links, view, ends)


def stages_of(axis):
    return lax.axis_size(axis).bit_length() - 1


def swap(value, axis, flip):
    count = lax.axis_size(axis)
    return lax.ppermute(value, axis, [(i, i ^ flip) for i in range(count)])


def on_right(axis, stage):
    return (lax.axis_index(axis) >> stage) % 2 == 1


def toward(right, block):
    return (
        jnp.where(right, block[R00], block[RLL]),
        jnp.where(right, block[FIRST], block[LAST]),
        jnp.where(right, block[C0], block[CL]),
    )


def join(a, b):
    joined, ties = join_coefs(a, b)
    (joined[FIRST], joined[LAST]), flux = join_targets((a[FIRST], a[LAST]), (b[FIRST], b[LAST]), ties)
    return joined, (flux, ties[1], ties[2])


def ordered(right, own, other):
    first = [jnp.where(right, theirs, mine) for mine, theirs in zip(own, other)]
    second = [jnp.where(right, mine, theirs) for mine, theirs in zip(own, other)]
    return first, second


def join_kernel(axis, stage, width, last, *refs):
    count = 1 << width
    send = refs[-1 - width]
    links = refs[-width:]
    if width > 1:
        blocks = [[refs[0][i, q] for q in range(7)] for i in range(count)]
    else:
        blocks = list(ordered(on_right(axis, stage), *([ref[q] for q in range(7)] for ref in refs[:2])))
    for bit in range(width):
        pairs = [join(blocks[i], blocks[i + 1]) for i in range(0, len(blocks), 2)]
        blocks = [p[0] for p in pairs]
        ties = [p[1] for p in pairs]
        for upper in range(bit + 1, width):
            right = on_right(axis, stage + upper)
            ties = [
                tuple(jnp.where(right, v, u) for u, v in zip(ties[i], ties[i + 1]))
                for i in range(0, len(ties), 2)
            ]
        for i in range(3):
            links[bit][i] = ties[0][i]
    (whole,) = blocks
    if last:
        for n, value in enumerate(toward(on_right(axis, stage + width), whole)):
            send[n] = value
    else:
        for q in range(7):
            send[q] = whole[q]


def join_stage(got, axis, stage, width, last):
    lines = got[0].shape[-2]
    return pl.pallas_call(
        functools.partial(join_kernel, axis, stage, width, last),
        out_shape=[shape_of(3 if last else 7, lines, LANES)] + [shape_of(3, lines, LANES)] * width,
        compiler_params=params(),
    )(*got)


def gather_line(view, axis, first_width=1):
    stages = stages_of(axis)
    links, stage = [], 0
    while stage < stages - 1:
        width = 1 if stage else first_width
        last = stage + width == stages - 1
        if width > 1:
            size = 1 << width
            groups = [list(range(i, i + size)) for i in range(0, 1 << stages, size)]
            got = [lax.all_to_all(view, axis, 0, 0, axis_index_groups=groups, tiled=True)]
        else:
            got = [view, swap(view, axis, 1 << stage)]
        view, *ties = join_stage(got, axis, stage, width, last)
        links += ties
        stage += width
    return view, swap(view, axis, 1 << stage), links


def top_flux(axis, stages, own, got):
    right = on_right(axis, stages - 1)
    face = own[2] + got[2]
    jump = jnp.where(right, own[1] - got[1], got[1] - own[1])
    return jump * face * inverse(1.0 + face * (own[0] + got[0]))


def block_ends(axis, stages, links):
    shape = links[0].shape[1:] if links else None
    right = on_right(axis, stages - 1)
    zero = jnp.zeros(shape, F32)
    low, high = zero, zero
    unit_low = zero + jnp.where(right, -1.0, 0.0)
    unit_high = zero + jnp.where(right, 0.0, 1.0)
    for stage in range(stages - 2, -1, -1):
        tie = links[stage]
        right = on_right(axis, stage)
        flux = between(tie[0], tie[1], tie[2], low, high)
        unit = between(0.0, tie[1], tie[2], unit_low, unit_high)
        low, high = jnp.where(right, -flux, low), jnp.where(right, high, flux)
        unit_low, unit_high = jnp.where(right, -unit, unit_low), jnp.where(right, unit_high, unit)
    return (low, high), (unit_low, unit_high)


def natural(index, parts):
    span = SUBLANES * parts
    local = index % span
    return index - local + local % SUBLANES * parts + local // SUBLANES


def turn_matrix(shape, from_natural, parts):
    row = lax.broadcasted_iota(jnp.int32, shape, 0)
    column = lax.broadcasted_iota(jnp.int32, shape, 1) % LANES
    hit = natural(row, parts) == column if from_natural else row == natural(column, parts)
    return jnp.where(hit, 1.0, 0.0).astype(jnp.bfloat16)


def turned(matrix, field):
    high = field.astype(jnp.bfloat16)
    low = (field - high.astype(F32)).astype(jnp.bfloat16)
    both = jnp.concatenate([high, low], 1)
    return lax.dot_general(
        matrix, both, (((1,), (1,)), ((), ())), preferred_element_type=F32
    )


def y_factor_kernel(c_ref, after, w_ref, i_ref, p_ref, inner, outer, view, to_y, to_x, c_s, q_s, r_s):
    chunks, sheets, rows, _ = c_ref.shape
    each = LANES // rows
    pairs = sheets // each
    x_steps = rows // SUBLANES
    steps = LANES // SUBLANES
    to_y[...] = turn_matrix(to_y.shape, True, steps)
    to_x[...] = turn_matrix(to_x.shape, False, x_steps)
    for m in range(pairs):
        for y in range(chunks):
            block = jnp.concatenate(
                [
                    c_ref[y, m * each + i, pl.ds(k, SUBLANES, stride=x_steps), :]
                    for i in range(each)
                    for k in range(x_steps)
                ],
                0,
            )
            c_s[m, part_of(y), :] = block.T

    members = [(y, m) for y in range(chunks) for m in range(pairs)]
    lines = len(members)

    def cond(k):
        return jnp.stack([c_s[m, pl.ds(y * LANES + k, SUBLANES, stride=steps), :] for y, m in members], 0)

    def keep(k, w, inv, p):
        w_ref[k] = w
        i_ref[k] = inv
        p_ref[k] = p

    block = factor(cond, steps, keep)
    for n, q in enumerate(COEFS):
        for i in range(lines):
            q_s[n, i * SUBLANES : (i + 1) * SUBLANES, :] = block[q][i]
    segments = [
        {q: q_s[n, pl.ds(s, lines, stride=SUBLANES), :] for n, q in enumerate(COEFS)}
        for s in range(SUBLANES)
    ]
    whole, levels = tree(segments, join_coefs)
    for (offset, _), level in zip(node_offsets(SUBLANES), levels):
        for n, values in enumerate(level):
            for i in range(3):
                inner[offset + n, i] = values[i]
    for n, q in enumerate(COEFS):
        r_s[n] = whole[q]
    parts = [
        {q: r_s[n, y * pairs : (y + 1) * pairs, :] for n, q in enumerate(COEFS)} for y in range(chunks)
    ]
    whole, levels = tree(parts, join_coefs)
    for (offset, _), level in zip(node_offsets(chunks), levels):
        for n, values in enumerate(level):
            for i in range(3):
                outer[offset + n, i] = values[i]
    for n, q in enumerate(COEFS):
        view[n] = whole[q]


def y_factor(c, after):
    chunks, sheets, rows, _ = c.shape
    pairs = sheets * rows // LANES
    lines = chunks * pairs
    stored = shape_of(LANES // SUBLANES, lines, SUBLANES, LANES)
    matrix = jax.ShapeDtypeStruct((LANES, 2 * LANES), jnp.bfloat16)
    return pl.pallas_call(
        y_factor_kernel,
        in_specs=[IN_VMEM, ANYWHERE],
        out_shape=[
            stored,
            stored,
            stored,
            shape_of(SUBLANES - 1, 3, lines, LANES),
            shape_of(chunks - 1, 3, pairs, LANES),
            shape_of(len(COEFS), pairs, LANES),
            matrix,
            matrix,
        ],
        scratch_shapes=[
            pltpu.VMEM((pairs, chunks * LANES, LANES), F32),
            pltpu.VMEM((len(COEFS), lines * SUBLANES, LANES), F32),
            pltpu.VMEM((len(COEFS), lines, LANES), F32),
        ],
        compiler_params=params(),
        cost_estimate=pl.CostEstimate(flops=20 * c.size, bytes_accessed=16 * c.size, transcendentals=0),
    )(c, after)


def z_factor_kernel(c_ref, after, w_ref, i_ref):
    sheets = c_ref.shape[1]
    ground = 1.0
    for z in range(sheets - 1):
        face = c_ref[:, z] + c_ref[:, z + 1]
        inv = inverse(ground + face)
        w = face * inv
        i_ref[z] = inv
        w_ref[z] = w
        ground = 1.0 + w * ground
    i_ref[sheets - 1] = inverse(ground)


def z_factor(c, after):
    chunks, sheets, rows, _ = c.shape
    return pl.pallas_call(
        z_factor_kernel,
        in_specs=[IN_VMEM, ANYWHERE],
        out_shape=[
            shape_of(sheets - 1, chunks, rows, LANES),
            shape_of(sheets, chunks, rows, LANES),
        ],
        compiler_params=params(),
        cost_estimate=pl.CostEstimate(flops=10 * c.size, bytes_accessed=12 * c.size, transcendentals=0),
    )(c, after)


def join_tree(items, links, own):
    for offset, count in node_offsets(len(items)):
        joined = []
        for n in range(count):
            tie = tuple(links[offset + n, i] for i in range(3))
            both, flux = join_targets(items[2 * n], items[2 * n + 1], tie)
            own[offset + n] = flux
            joined.append(both)
        items = joined
    return items[0]


def tree_ends(leaves, links, own, low, high):
    levels = [
        [(own(offset + n), links[offset + n, 1], links[offset + n, 2]) for n in range(count)]
        for offset, count in node_offsets(leaves)
    ]
    return descend(levels, low, high)


def nothing(node):
    return 0.0


def y_prepare_kernel(stages, *refs):
    ties = refs[: stages - 1]
    xw, xh, xm, xp, x_links, x_own, t_ref, to_y = refs[stages - 1 : stages + 7]
    base, response, f_s, g_s = refs[stages + 7 :]
    x_steps, lines = xw.shape[:2]
    chunks = base.shape[0]
    sheets = lines // chunks
    rows = x_steps * SUBLANES

    ends, units = block_ends("gx", stages, ties)
    for n, (own, (low, high)) in enumerate(((lambda i: x_own[i], ends), (nothing, units))):
        for s, pair in enumerate(tree_ends(SUBLANES, x_links, own, low, high)):
            for i in range(2):
                f_s[n, i, pl.ds(s, lines, stride=SUBLANES), :] = pair[i]
    first = 0
    for n, members in enumerate(line_groups(chunks, sheets)):
        at = slice(first, first + len(members))
        h_ref_of, h_at = (xh, at) if n == 0 else (xm, slice(first - 2 * sheets, at.stop - 2 * sheets))
        (low, value), (unit_low, unit) = (
            [
                jnp.stack(
                    [f_s[q, i, j * SUBLANES : (j + 1) * SUBLANES, :] for j in range(at.start, at.stop)], 0
                )
                for i in range(2)
            ]
            for q in range(2)
        )
        for k in range(x_steps - 1, -1, -1):
            w, p = xw[k, at], xp[k, at]
            value = w * value + (h_ref_of[k, h_at] + p * low)
            unit = w * unit + p * unit_low
            field = value - t_ref[k, at]
            for j, (y, z) in enumerate(members):
                place = z * rows + k * SUBLANES
                g_s[0, y, place : place + SUBLANES, :] = field[j]
                g_s[1, y, place : place + SUBLANES, :] = unit[j]
        first = at.stop

    for y in range(chunks):
        base[y] = turned(to_y[...], g_s[0, y])
        response[y] = turned(to_y[...], g_s[1, y])


def y_prepare(ties, xw, xh, xm, xp, x_links, x_own, t, to_y, chunks):
    x_steps, lines = xw.shape[:2]
    width = lines // chunks * x_steps * SUBLANES
    field = shape_of(chunks, LANES, width)
    return pl.pallas_call(
        functools.partial(y_prepare_kernel, len(ties) + 1),
        out_shape=[field, field],
        scratch_shapes=[
            pltpu.VMEM((2, 2, lines * SUBLANES, LANES), F32),
            pltpu.VMEM((2, chunks, width, LANES), F32),
        ],
        compiler_params=params(),
        cost_estimate=pl.CostEstimate(flops=8 * t.size, bytes_accessed=16 * t.size, transcendentals=0),
    )(*ties, xw, xh, xm, xp, x_links, x_own, t, to_y)


def y_target_kernel(stages, own, got, base, response, yw, yi, yp, inner, outer, view, to_y, *refs):
    h_ref, inner_own, outer_own, send, q_s, r_s = refs
    chunks, _, width = base.shape
    pairs = width // LANES
    sheets = own.shape[1] // chunks
    rows = width // sheets
    steps = yw.shape[0]

    flux = top_flux("gx", stages, own, got)
    line_of = {member: n for n, member in enumerate(sum(line_groups(chunks, sheets), []))}
    fields = []
    for y in range(chunks):
        spread = jnp.concatenate(
            [
                jnp.broadcast_to(flux[line_of[y, z] : line_of[y, z] + 1, :], (rows, LANES))
                for z in range(sheets)
            ],
            0,
        )
        fields.append(base[y] + response[y] * turned(to_y[...], spread))

    def target(k):
        at = slice(k * SUBLANES, (k + 1) * SUBLANES)
        return jnp.stack(
            [fields[y][at, m * LANES : (m + 1) * LANES] for y in range(chunks) for m in range(pairs)], 0
        )

    def keep(k, h):
        h_ref[k] = h

    ends = eliminate(target, steps, lambda k: yw[k], lambda k: yi[k], lambda k: yp[k], keep)
    for q in range(2):
        for i in range(chunks * pairs):
            q_s[q, i * SUBLANES : (i + 1) * SUBLANES, :] = ends[q][i]
    items = [
        tuple(q_s[q, pl.ds(s, chunks * pairs, stride=SUBLANES), :] for q in range(2))
        for s in range(SUBLANES)
    ]
    r_s[0], r_s[1] = join_tree(items, inner, inner_own)
    items = [tuple(r_s[q, y * pairs : (y + 1) * pairs, :] for q in range(2)) for y in range(chunks)]
    for n, q in enumerate(COEFS):
        send[q] = view[n]
    send[FIRST], send[LAST] = join_tree(items, outer, outer_own)


def y_target(own, got, base, response, yw, yi, yp, inner, outer, view, to_y):
    y_lines = yw.shape[1]
    pairs = view.shape[1]
    chunks = y_lines // pairs
    return pl.pallas_call(
        functools.partial(y_target_kernel, stages_of("gx")),
        out_shape=[
            shape_of(*yw.shape),
            shape_of(SUBLANES - 1, y_lines, LANES),
            shape_of(chunks - 1, pairs, LANES),
            shape_of(7, pairs, LANES),
        ],
        scratch_shapes=[
            pltpu.VMEM((2, y_lines * SUBLANES, LANES), F32),
            pltpu.VMEM((2, y_lines, LANES), F32),
        ],
        compiler_params=params(),
    )(own, got, base, response, yw, yi, yp, inner, outer, view, to_y)


def z_solve(zw, zi, field, at, keep):
    sheets = zi.shape[0]
    rhs, kept = None, []
    for z in range(sheets):
        rhs = field(z) if z == 0 else field(z) + zw[z - 1, at] * rhs
        kept.append(rhs * zi[z, at])
    value = kept[-1]
    keep(sheets - 1, value)
    for z in range(sheets - 2, -1, -1):
        value = zw[z, at] * value + kept[z]
        keep(z, value)


def finish_prepare_kernel(stages, *refs):
    ties = refs[: stages - 1]
    yw, yh, yp, inner, inner_own, outer, outer_own, zw, zi, t_ref, to_x = refs[stages - 1 : stages + 10]
    base, response, r_s, e_s, u_s = refs[stages + 10 :]
    chunks, sheets, rows, _ = base.shape
    each = LANES // rows
    pairs = sheets // each
    steps = yw.shape[0]
    lines = chunks * pairs

    ends, units = block_ends("gy", stages, ties)
    both = (
        (lambda i: outer_own[i], lambda i: inner_own[i], ends),
        (nothing, nothing, units),
    )
    for n, (upper, lower, (low, high)) in enumerate(both):
        for y, pair in enumerate(tree_ends(chunks, outer, upper, low, high)):
            for i in range(2):
                r_s[n, i, y * pairs : (y + 1) * pairs, :] = pair[i]
        for s, pair in enumerate(tree_ends(SUBLANES, inner, lower, r_s[n, 0], r_s[n, 1])):
            for i in range(2):
                e_s[n, i, pl.ds(s, lines, stride=SUBLANES), :] = pair[i]
    (low, value), (unit_low, unit) = (
        [
            jnp.stack([e_s[q, i, n * SUBLANES : (n + 1) * SUBLANES, :] for n in range(lines)], 0)
            for i in range(2)
        ]
        for q in range(2)
    )
    for k in range(steps - 1, -1, -1):
        w, p = yw[k], yp[k]
        value = w * value + (yh[k] + p * low)
        unit = w * unit + p * unit_low
        for y in range(chunks):
            for m in range(pairs):
                place = pl.ds(y * LANES + k, SUBLANES, stride=steps)
                u_s[0, m, place, :] = value[y * pairs + m]
                u_s[1, m, place, :] = unit[y * pairs + m]

    for y in range(chunks):
        part = part_of(y)
        fields = [turned(to_x[...], u_s[0, m, part, :]) for m in range(pairs)]

        def field(z):
            at = z % each * rows
            return fields[z // each][at : at + rows, :]

        def keep(z, value):
            base[y, z] = t_ref[z, :, part] + value

        z_solve(zw, zi, field, y, keep)
        for m in range(pairs):
            units = turned(to_x[...], u_s[1, m, part, :])
            for i in range(each):
                response[y, m * each + i] = units[i * rows : (i + 1) * rows, :]


def finish_prepare(ties, yw, yh, yp, inner, inner_own, outer, outer_own, zw, zi, t, to_x):
    sheets, rows, columns = t.shape
    chunks = columns // LANES
    pairs = sheets * rows // LANES
    lines = chunks * pairs
    field = shape_of(chunks, sheets, rows, LANES)
    return pl.pallas_call(
        functools.partial(finish_prepare_kernel, len(ties) + 1),
        out_shape=[field, field],
        scratch_shapes=[
            pltpu.VMEM((2, 2, lines, LANES), F32),
            pltpu.VMEM((2, 2, lines * SUBLANES, LANES), F32),
            pltpu.VMEM((2, pairs, columns, LANES), F32),
        ],
        compiler_params=params(),
        cost_estimate=pl.CostEstimate(flops=12 * t.size, bytes_accessed=20 * t.size, transcendentals=0),
    )(*ties, yw, yh, yp, inner, inner_own, outer, outer_own, zw, zi, t, to_x)


def finish_kernel(stages, own, got, base, response, zw, zi, to_x, out, o_s, sems):
    chunks, sheets, rows, _ = base.shape
    each = LANES // rows
    pairs = sheets // each
    copies, _, _, wide = o_s.shape

    flux = top_flux("gy", stages, own, got)
    spread = [
        turned(to_x[...], jnp.broadcast_to(flux[m : m + 1, :], (LANES, LANES))) for m in range(pairs)
    ]
    started = []
    for n in range(copies):
        for y in range(n * chunks // copies, (n + 1) * chunks // copies):
            part = part_of(y - n * chunks // copies)

            def field(z):
                at = z % each * rows
                return response[y, z] * spread[z // each][at : at + rows, :]

            def keep(z, value):
                o_s[n, z, :, part] = base[y, z] + value

            z_solve(zw, zi, field, y, keep)
        copy = pltpu.make_async_copy(o_s.at[n], out.at[:, :, pl.ds(n * wide, wide)], sems.at[n])
        copy.start()
        started.append(copy)
    for copy in started:
        copy.wait()


def finish(own, got, base, response, zw, zi, to_x):
    chunks, sheets, rows, _ = base.shape
    copies = chunks
    return pl.pallas_call(
        functools.partial(finish_kernel, stages_of("gy")),
        out_shape=shape_of(sheets, rows, chunks * LANES),
        out_specs=ANYWHERE,
        scratch_shapes=[
            pltpu.VMEM((copies, sheets, rows, chunks * LANES // copies), F32),
            pltpu.SemaphoreType.DMA((copies,)),
        ],
        compiler_params=params(),
    )(own, got, base, response, zw, zi, to_x)


def per_device(temperature, base, locations, energy):
    columns = temperature.shape[2]
    gy = lax.axis_size("gy")
    packed = edges(temperature, base)
    near = swap(packed, "gy", 1)
    t, b, loc, heat = load((temperature, base, locations[None], energy[None]), packed)
    near, t, b = lax.optimization_barrier((near, t, b))
    far = [swap(near, "gy", 2)] if gy > 2 else []
    if gy > 4:
        far.append(lax.ppermute(near, "gy", [(i, (i + 2 ^ 2) - 2) for i in range(2, gy - 2)]))
    c, total, xw, xi, xp, x_links, x_view, xm, ends, t_steps = x_factor(loc, heat, t, b, columns * gy, near)
    xh, x_own, view = x_target(packed, t, total, [near] + far, xw, xi, xp, x_links, x_view, ends)
    yw, yi, yp, inner, outer, y_view, to_y, to_x = y_factor(c, x_view)
    zw, zi = z_factor(c, view)
    own, got, ties = gather_line(view, "gx", 2)
    base, response = y_prepare(
        ties, xw, xh, xm, xp, x_links, x_own, t_steps, to_y, columns // LANES
    )
    yh, inner_own, outer_own, view = y_target(
        own, got, base, response, yw, yi, yp, inner, outer, y_view, to_y
    )
    own, got, ties = gather_line(view, "gy")
    base, response = finish_prepare(
        ties, yw, yh, yp, inner, inner_own, outer, outer_own, zw, zi, t, to_x
    )
    return finish(own, got, base, response, zw, zi, to_x)


def solution(mesh):
    in_specs = (P(None, "gx", "gy"), P(None, "gx", "gy"), P(), P())
    out_specs = P(None, "gx", "gy")
    return jax.shard_map(
        per_device, mesh=mesh, in_specs=in_specs, out_specs=out_specs, check_vma=False
    )
```

```python
import functools

import jax
import jax.numpy as jnp
from jax import lax
from jax.experimental import pallas as pl
from jax.experimental.pallas import tpu as pltpu
from jax.sharding import PartitionSpec as P

RATE = 2000.0
THERMAL_GROWTH = 0.8
LANES = 128
SUBLANES = 8
F32 = jnp.float32
MIB = 1024 * 1024
ANYWHERE = pl.BlockSpec(memory_space=pl.ANY)
IN_HBM = pl.BlockSpec(memory_space=pltpu.HBM)
IN_VMEM = pl.BlockSpec(memory_space=pltpu.VMEM)

R00, R0L, RLL, FIRST, LAST, C0, CL = range(7)
COEFS = (R00, R0L, RLL, C0, CL)


def params(limit=40):
    return pltpu.CompilerParams(vmem_limit_bytes=limit * MIB)


def shape_of(*sizes):
    return jax.ShapeDtypeStruct(sizes, F32)


def half_conduct(base, temperature):
    return base * (0.5 * RATE + (0.5 * RATE * THERMAL_GROWTH) * temperature)


def inverse(x):
    guess = pl.reciprocal(x, approx=True)
    return guess * (2.0 - x * guess)


def join_coefs(a, b):
    face = a[CL] + b[C0]
    inv = face * inverse(1.0 + face * (a[RLL] + b[R00]))
    left = a[R0L] * inv
    right = b[R0L] * inv
    joined = {
        R00: a[R00] - left * a[R0L],
        R0L: left * b[R0L],
        RLL: b[RLL] - right * b[R0L],
        C0: a[C0],
        CL: b[CL],
    }
    return joined, (inv, right, left)


def join_targets(a, b, links):
    inv, right, left = links
    jump = b[0] - a[1]
    return (a[0] + left * jump, b[1] - right * jump), jump * inv


def between(own, right, left, low, high):
    return own + right * high - left * low


def tree(items, join):
    levels = []
    while len(items) > 1:
        pairs = [join(items[i], items[i + 1]) for i in range(0, len(items), 2)]
        items = [p[0] for p in pairs]
        levels.append([p[1] for p in pairs])
    return items[0], levels


def descend(levels, low, high):
    ends = [(low, high)]
    for level in reversed(levels):
        below = []
        for (lo, hi), (own, right, left) in zip(ends, level):
            flux = between(own, right, left, lo, hi)
            below += [(lo, flux), (-flux, hi)]
        ends = below
    return ends


def node_offsets(leaves):
    offsets, at, count = [], 0, leaves // 2
    while count:
        offsets.append((at, count))
        at += count
        count //= 2
    return offsets


def factor(cond, steps, keep):
    here = cond(0)
    c_first = here
    one = jnp.ones_like(here)
    ground, path, first_first = one, one, None
    for k in range(steps - 1):
        following = cond(k + 1)
        face = here + following
        inv = inverse(ground + face)
        w = face * inv
        p = path * inv
        keep(k, w, inv, p)
        step = path * p
        first_first = step if first_first is None else first_first + step
        path = path * w
        ground = 1.0 + w * ground
        here = following
    inv = inverse(ground)
    p = path * inv
    keep(steps - 1, inv, inv, p)
    return {R00: first_first + path * p, R0L: p, RLL: inv, C0: c_first, CL: here}


def eliminate(target, steps, w, inv, p, keep):
    rhs = target(0)
    first = None
    for k in range(steps):
        h = rhs * inv(k)
        keep(k, h)
        step = rhs * p(k)
        first = step if first is None else first + step
        if k < steps - 1:
            rhs = target(k + 1) + w(k) * rhs
    return first, h


def is_odd(axis):
    return lax.axis_index(axis) % 2 == 1


def fold(cells, used):
    total = cells[:SUBLANES]
    lane = lax.broadcasted_iota(jnp.int32, total.shape, 1)
    for n in range(1, cells.shape[0] // SUBLANES):
        part = pltpu.roll(cells[n * SUBLANES : (n + 1) * SUBLANES], n * used, 1)
        total = jnp.where(lane // used == n, part, total)
    return total


def unfold(cells, used, rows):
    parts = [cells] + [
        pltpu.roll(cells, LANES - n * used, 1) for n in range(1, rows // SUBLANES)
    ]
    return jnp.concatenate(parts, 0)


def edges_kernel(sheets, t_hbm, b_hbm, packed, t_s, b_s, sems):
    columns = t_hbm.shape[1]
    rows = t_hbm.shape[0] // sheets
    sides = []
    for side, start in enumerate((0, columns - LANES)):
        sides.append(
            [
                pltpu.make_async_copy(src.at[:, pl.ds(start, LANES)], dst.at[side], sems.at[i, side])
                for i, (src, dst) in enumerate(((t_hbm, t_s), (b_hbm, b_s)))
            ]
        )
        for copy in sides[-1]:
            copy.start()
    lane = lax.broadcasted_iota(jnp.int32, (rows, LANES), 1)
    total = jnp.zeros((rows, LANES), F32)
    for side, source in enumerate((0, LANES - 1)):
        for copy in sides[side]:
            copy.wait()
        for z in range(sheets):
            t = t_s[side, z * rows : (z + 1) * rows, :]
            c = half_conduct(b_s[side, z * rows : (z + 1) * rows, :], t)
            place = 2 * sheets * side + z
            total = jnp.where(lane == place, t[:, source : source + 1], total)
            total = jnp.where(lane == place + sheets, c[:, source : source + 1], total)
    packed[...] = fold(total, 4 * sheets)


def edges(temperature, base):
    sheets, rows, _ = temperature.shape
    assert rows // SUBLANES * 4 * sheets <= LANES
    columns = temperature.shape[2]
    fields = [
        pltpu.with_memory_space_constraint(v.reshape(sheets * rows, columns), pltpu.HBM)
        for v in (temperature, base)
    ]
    return pl.pallas_call(
        functools.partial(edges_kernel, sheets),
        in_specs=[IN_HBM] * 2,
        out_shape=pltpu.VMEM((SUBLANES, LANES), F32),
        scratch_shapes=[
            pltpu.VMEM((2, sheets * rows, LANES), F32),
            pltpu.VMEM((2, sheets * rows, LANES), F32),
            pltpu.SemaphoreType.DMA((2, 2)),
        ],
        compiler_params=params(),
    )(*fields)


def load_kernel(*refs):
    count = len(refs) // 2 - 1
    sems = refs[-1]
    copies = [
        pltpu.make_async_copy(refs[i], refs[count + 1 + i], sems.at[i]) for i in range(count)
    ]
    for copy in copies:
        copy.start()
    for copy in copies:
        copy.wait()


def load(values, after):
    return pl.pallas_call(
        load_kernel,
        in_specs=[IN_HBM] * len(values) + [ANYWHERE],
        out_shape=[pltpu.VMEM(v.shape, v.dtype) for v in values],
        scratch_shapes=[pltpu.SemaphoreType.DMA((len(values),))],
        compiler_params=params(),
        cost_estimate=pl.CostEstimate(
            flops=0, bytes_accessed=16 * values[0].size, transcendentals=0
        ),
    )(*[pltpu.with_memory_space_constraint(v, pltpu.HBM) for v in values], after)


def source_plane(loc, energy, rows, columns, plate):
    place = loc[...]
    count = place.shape[1]
    local_x = place // plate - lax.axis_index("gx") * rows
    local_y = place % plate - lax.axis_index("gy") * columns
    in_x = lax.broadcasted_iota(jnp.int32, (rows, count), 0) == local_x
    in_y = lax.broadcasted_iota(jnp.int32, (columns, count), 0) == local_y
    by_y = jnp.where(in_y, 1.0, 0.0).astype(jnp.bfloat16)
    left = energy[...]
    plane = None
    for _ in range(3):
        part = left.astype(jnp.bfloat16).astype(F32)
        left = left - part
        term = lax.dot_general(
            jnp.where(in_x, part, 0.0).astype(jnp.bfloat16),
            by_y,
            (((1,), (1,)), ((), ())),
            preferred_element_type=F32,
        )
        plane = term if plane is None else plane + term
    return plane


def part_of(y):
    return slice(y * LANES, (y + 1) * LANES)


def line_groups(chunks, sheets):
    order = [0, chunks - 1] + list(range(1, chunks - 1))
    return [[(y, z) for y in order[i : i + 2] for z in range(sheets)] for i in range(0, chunks, 2)]


def x_eliminate(field, members, first_line, w_ref, i_ref, p_ref, h_ref, h_line, q_s):
    steps = w_ref.shape[0]
    at = slice(first_line, first_line + len(members))
    kept_at = slice(h_line, h_line + len(members))

    def target(k):
        return jnp.stack([field(y, z)[pl.ds(k, SUBLANES, stride=steps), :] for y, z in members], 0)

    def keep(k, h):
        h_ref[k, kept_at] = h

    ends = eliminate(
        target, steps, lambda k: w_ref[k, at], lambda k: i_ref[k, at], lambda k: p_ref[k, at], keep
    )
    for q in range(2):
        for i in range(len(members)):
            first = (first_line + i) * SUBLANES
            q_s[q, first : first + SUBLANES, :] = ends[q][i]


def x_factor_kernel(plate, loc, energy, t_ref, b_ref, after, *refs):
    c_ref, total_ref, w_ref, i_ref, p_ref, links, view, h_ref, ends_ref, t_out, q_s, t_s = refs
    chunks, sheets, rows, _ = c_ref.shape
    lines = chunks * sheets
    steps = rows // SUBLANES
    plane = source_plane(loc, energy, rows, chunks * LANES, plate)

    lane = lax.broadcasted_iota(jnp.int32, (SUBLANES, LANES), 1)
    is_first, is_last = lane == 0, lane == LANES - 1
    for r in range(steps):
        at = slice(r * SUBLANES, (r + 1) * SUBLANES)
        before_t, before_c = None, None
        for z in range(sheets):
            ts = [t_ref[z, at, part_of(y)] for y in range(chunks)]
            cs = [half_conduct(b_ref[z, at, part_of(y)], ts[y]) for y in range(chunks)]
            t_turned = [pltpu.roll(v, LANES - 1, 1) for v in ts]
            c_turned = [pltpu.roll(v, LANES - 1, 1) for v in cs]
            flux = []
            for y in range(chunks):
                if y < chunks - 1:
                    t_next = jnp.where(is_last, t_turned[y + 1], t_turned[y])
                    c_next = jnp.where(is_last, c_turned[y + 1], c_turned[y])
                    flux.append((cs[y] + c_next) * (t_next - ts[y]))
                else:
                    inside = (cs[y] + c_turned[y]) * (t_turned[y] - ts[y])
                    flux.append(jnp.where(is_last, 0.0, inside))
            turned = [pltpu.roll(v, 1, 1) for v in flux]
            for y in range(chunks):
                from_low = jnp.where(is_first, turned[y - 1] if y else 0.0, turned[y])
                total = ts[y] + (flux[y] - from_low)
                if z == 0:
                    total = total + plane[at, part_of(y)]
                else:
                    across = (before_c[y] + cs[y]) * (ts[y] - before_t[y])
                    total = total - across
                    total_ref[y, z - 1, at, :] += across
                total_ref[y, z, at, :] = total
                c_ref[y, z, at, :] = cs[y]
                t_s[y, z, at, :] = ts[y]
            before_t, before_c = ts, cs

    at = 0
    for n, members in enumerate(line_groups(chunks, sheets)):

        def cond(k):
            return jnp.stack([c_ref[y, z, pl.ds(k, SUBLANES, stride=steps), :] for y, z in members], 0)

        def keep(k, w, inv, p):
            w_ref[k, at : at + len(members)] = w
            i_ref[k, at : at + len(members)] = inv
            p_ref[k, at : at + len(members)] = p

        block = factor(cond, steps, keep)
        for i, q in enumerate(COEFS):
            for j in range(len(members)):
                first = (at + j) * SUBLANES
                q_s[i, first : first + SUBLANES, :] = block[q][j]
        if n > 0:
            x_eliminate(
                lambda y, z: total_ref.at[y, z], members, at, w_ref, i_ref, p_ref, h_ref,
                at - 2 * sheets, ends_ref,
            )
        for k in range(steps):
            for i, (y, z) in enumerate(members):
                t_out[k, at + i] = t_s[y, z, pl.ds(k, SUBLANES, stride=steps), :]
        at += len(members)

    segments = [
        {q: q_s[n, pl.ds(s, lines, stride=SUBLANES), :] for n, q in enumerate(COEFS)}
        for s in range(SUBLANES)
    ]
    whole, levels = tree(segments, join_coefs)
    for (offset, _), level in zip(node_offsets(SUBLANES), levels):
        for n, values in enumerate(level):
            for i in range(3):
                links[offset + n, i] = values[i]
    for n, q in enumerate(COEFS):
        view[n] = whole[q]


def x_factor(loc, energy, t, b, plate, after):
    sheets, rows, columns = t.shape
    chunks = columns // LANES
    lines = chunks * sheets
    steps = rows // SUBLANES
    field = shape_of(chunks, sheets, rows, LANES)
    stored = shape_of(steps, lines, SUBLANES, LANES)
    return pl.pallas_call(
        functools.partial(x_factor_kernel, plate),
        in_specs=[IN_VMEM] * 4 + [ANYWHERE],
        out_shape=[
            field,
            field,
            stored,
            stored,
            stored,
            shape_of(SUBLANES - 1, 3, lines, LANES),
            shape_of(len(COEFS), lines, LANES),
            shape_of(steps, max(1, lines - 2 * sheets), SUBLANES, LANES),
            shape_of(2, lines * SUBLANES, LANES),
            stored,
        ],
        scratch_shapes=[
            pltpu.VMEM((len(COEFS), lines * SUBLANES, LANES), F32),
            pltpu.VMEM((chunks, sheets, rows, LANES), F32),
        ],
        compiler_params=params(),
        cost_estimate=pl.CostEstimate(flops=40 * t.size, bytes_accessed=28 * t.size, transcendentals=0),
    )(loc, energy, t, b, after)


def far_side(sources):
    place = lax.axis_index("gy")
    paired = (place >> 1) % 2 != place % 2
    nothing = jnp.zeros(sources[0].shape, F32)
    by_pair = sources[1][...] if len(sources) > 1 else nothing
    other = sources[2][...] if len(sources) > 2 else nothing
    return jnp.where(paired, by_pair, other)


def x_target_kernel(count, own_cells, t_ref, total_ref, *refs):
    w_ref, i_ref, p_ref, links, view, ends_ref, h_ref, own, send, e_s, q_s = refs[count:]
    chunks, sheets, rows, _ = total_ref.shape
    lines = chunks * sheets

    lane = lax.broadcasted_iota(jnp.int32, (rows, LANES), 1)
    side = 2 * sheets
    near, far = (unfold(v, 2 * side, rows) for v in (refs[0][...], far_side(refs[:count])))
    before = jnp.where(is_odd("gy"), near, far)
    after = jnp.where(is_odd("gy"), far, near)
    beyond = jnp.where(lane < side, pltpu.roll(before, LANES - side, 1), pltpu.roll(after, side, 1))
    mine = unfold(own_cells[...], 2 * side, rows)
    face = jnp.where(beyond > 0.0, mine + beyond, 0.0)
    flux = pltpu.roll(face, LANES - sheets, 1) * (beyond - mine)
    for n, (y, edge) in enumerate(((0, 0), (chunks - 1, LANES - 1))):
        for z in range(sheets):
            at = n * side + z
            e_s[n, z] = total_ref[y, z] + jnp.where(lane == edge, flux[:, at : at + 1], 0.0)

    members = line_groups(chunks, sheets)[0]
    x_eliminate(
        lambda y, z: e_s.at[0 if y == 0 else 1, z], members, 0, w_ref, i_ref, p_ref, h_ref, 0, q_s
    )
    split = len(members)
    items = [
        tuple(
            jnp.concatenate(
                [
                    q_s[q, pl.ds(s, split, stride=SUBLANES), :],
                    ends_ref[q, pl.ds(split * SUBLANES + s, lines - split, stride=SUBLANES), :],
                ],
                0,
            )
            for q in range(2)
        )
        for s in range(SUBLANES)
    ]
    for offset, count in node_offsets(SUBLANES):
        joined = []
        for n in range(count):
            ties = tuple(links[offset + n, i] for i in range(3))
            both, flux = join_targets(items[2 * n], items[2 * n + 1], ties)
            own[offset + n] = flux
            joined.append(both)
        items = joined
    for n, q in enumerate(COEFS):
        send[q] = view[n]
    send[FIRST], send[LAST] = items[0]


def x_target(own_cells, t, total, edge_cells, w, inv, p, links, view, ends):
    chunks, sheets, rows, _ = total.shape
    lines = chunks * sheets
    steps = rows // SUBLANES
    return pl.pallas_call(
        functools.partial(x_target_kernel, len(edge_cells)),
        out_shape=[
            shape_of(steps, 2 * sheets, SUBLANES, LANES),
            shape_of(SUBLANES - 1, lines, LANES),
            shape_of(7, lines, LANES),
        ],
        scratch_shapes=[
            pltpu.VMEM((2, sheets, rows, LANES), F32),
            pltpu.VMEM((2, 2 * sheets * SUBLANES, LANES), F32),
        ],
        compiler_params=params(),
    )(own_cells, t, total, *edge_cells, w, inv, p, links, view, ends)


def stages_of(axis):
    return lax.axis_size(axis).bit_length() - 1


def swap(value, axis, flip):
    count = lax.axis_size(axis)
    return lax.ppermute(value, axis, [(i, i ^ flip) for i in range(count)])


def on_right(axis, stage):
    return (lax.axis_index(axis) >> stage) % 2 == 1


def toward(right, block):
    return (
        jnp.where(right, block[R00], block[RLL]),
        jnp.where(right, block[FIRST], block[LAST]),
        jnp.where(right, block[C0], block[CL]),
    )


def join(a, b):
    joined, ties = join_coefs(a, b)
    (joined[FIRST], joined[LAST]), flux = join_targets((a[FIRST], a[LAST]), (b[FIRST], b[LAST]), ties)
    return joined, (flux, ties[1], ties[2])


def ordered(right, own, other):
    first = [jnp.where(right, theirs, mine) for mine, theirs in zip(own, other)]
    second = [jnp.where(right, mine, theirs) for mine, theirs in zip(own, other)]
    return first, second


def join_kernel(axis, stage, width, last, *refs):
    count = 1 << width
    blocks = [[refs[i][q] for q in range(7)] for i in range(count)]
    send = refs[-1 - width]
    links = refs[-width:]
    for bit in range(width):
        right = on_right(axis, stage + bit)
        for i in range(count):
            if not i >> bit & 1:
                j = i | 1 << bit
                blocks[i], blocks[j] = ordered(right, blocks[i], blocks[j])
    for bit in range(width):
        pairs = [join(blocks[i], blocks[i + 1]) for i in range(0, len(blocks), 2)]
        blocks = [p[0] for p in pairs]
        ties = [p[1] for p in pairs]
        for upper in range(bit + 1, width):
            right = on_right(axis, stage + upper)
            ties = [
                tuple(jnp.where(right, v, u) for u, v in zip(ties[i], ties[i + 1]))
                for i in range(0, len(ties), 2)
            ]
        for i in range(3):
            links[bit][i] = ties[0][i]
    (whole,) = blocks
    if last:
        for n, value in enumerate(toward(on_right(axis, stage + width), whole)):
            send[n] = value
    else:
        for q in range(7):
            send[q] = whole[q]


def join_stage(own, got, axis, stage, width, last, after):
    lines = own.shape[1]
    return pl.pallas_call(
        functools.partial(join_kernel, axis, stage, width, last),
        in_specs=[IN_VMEM] * (1 + len(got)) + [ANYWHERE] * len(after),
        out_shape=[shape_of(3 if last else 7, lines, LANES)] + [shape_of(3, lines, LANES)] * width,
        compiler_params=params(),
    )(own, *got, *after)


def gather_line(view, axis, widest=1, meanwhile=()):
    stages = stages_of(axis)
    links, stage = [], 0
    while stage < stages - 1:
        width = min(widest, stages - 1 - stage)
        got = [swap(view, axis, flip << stage) for flip in range(1, 1 << width)]
        last = stage + width == stages - 1
        view, *ties = join_stage(view, got, axis, stage, width, last, meanwhile)
        links += ties
        stage += width
        meanwhile = ()
    return view, swap(view, axis, 1 << stage), links


def top_flux(axis, stages, own, got):
    right = on_right(axis, stages - 1)
    face = own[2] + got[2]
    jump = jnp.where(right, own[1] - got[1], got[1] - own[1])
    return jump * face * inverse(1.0 + face * (own[0] + got[0]))


def block_ends(axis, stages, links):
    shape = links[0].shape[1:] if links else None
    right = on_right(axis, stages - 1)
    zero = jnp.zeros(shape, F32)
    low, high = zero, zero
    unit_low = zero + jnp.where(right, -1.0, 0.0)
    unit_high = zero + jnp.where(right, 0.0, 1.0)
    for stage in range(stages - 2, -1, -1):
        tie = links[stage]
        right = on_right(axis, stage)
        flux = between(tie[0], tie[1], tie[2], low, high)
        unit = between(0.0, tie[1], tie[2], unit_low, unit_high)
        low, high = jnp.where(right, -flux, low), jnp.where(right, high, flux)
        unit_low, unit_high = jnp.where(right, -unit, unit_low), jnp.where(right, unit_high, unit)
    return (low, high), (unit_low, unit_high)


def natural(index, parts):
    span = SUBLANES * parts
    local = index % span
    return index - local + local % SUBLANES * parts + local // SUBLANES


def turn_matrix(shape, from_natural, parts):
    row = lax.broadcasted_iota(jnp.int32, shape, 0)
    column = lax.broadcasted_iota(jnp.int32, shape, 1) % LANES
    hit = natural(row, parts) == column if from_natural else row == natural(column, parts)
    return jnp.where(hit, 1.0, 0.0).astype(jnp.bfloat16)


def turned(matrix, field):
    high = field.astype(jnp.bfloat16)
    low = (field - high.astype(F32)).astype(jnp.bfloat16)
    both = jnp.concatenate([high, low], 1)
    return lax.dot_general(
        matrix, both, (((1,), (1,)), ((), ())), preferred_element_type=F32
    )


def y_factor_kernel(c_ref, after, w_ref, i_ref, p_ref, inner, outer, view, to_y, to_x, c_s, q_s, r_s):
    chunks, sheets, rows, _ = c_ref.shape
    each = LANES // rows
    pairs = sheets // each
    x_steps = rows // SUBLANES
    steps = LANES // SUBLANES
    to_y[...] = turn_matrix(to_y.shape, True, steps)
    to_x[...] = turn_matrix(to_x.shape, False, x_steps)
    for m in range(pairs):
        for y in range(chunks):
            block = jnp.concatenate(
                [
                    c_ref[y, m * each + i, pl.ds(k, SUBLANES, stride=x_steps), :]
                    for i in range(each)
                    for k in range(x_steps)
                ],
                0,
            )
            c_s[m, part_of(y), :] = block.T

    members = [(y, m) for y in range(chunks) for m in range(pairs)]
    lines = len(members)

    def cond(k):
        return jnp.stack([c_s[m, pl.ds(y * LANES + k, SUBLANES, stride=steps), :] for y, m in members], 0)

    def keep(k, w, inv, p):
        w_ref[k] = w
        i_ref[k] = inv
        p_ref[k] = p

    block = factor(cond, steps, keep)
    for n, q in enumerate(COEFS):
        for i in range(lines):
            q_s[n, i * SUBLANES : (i + 1) * SUBLANES, :] = block[q][i]
    segments = [
        {q: q_s[n, pl.ds(s, lines, stride=SUBLANES), :] for n, q in enumerate(COEFS)}
        for s in range(SUBLANES)
    ]
    whole, levels = tree(segments, join_coefs)
    for (offset, _), level in zip(node_offsets(SUBLANES), levels):
        for n, values in enumerate(level):
            for i in range(3):
                inner[offset + n, i] = values[i]
    for n, q in enumerate(COEFS):
        r_s[n] = whole[q]
    parts = [
        {q: r_s[n, y * pairs : (y + 1) * pairs, :] for n, q in enumerate(COEFS)} for y in range(chunks)
    ]
    whole, levels = tree(parts, join_coefs)
    for (offset, _), level in zip(node_offsets(chunks), levels):
        for n, values in enumerate(level):
            for i in range(3):
                outer[offset + n, i] = values[i]
    for n, q in enumerate(COEFS):
        view[n] = whole[q]


def y_factor(c, after):
    chunks, sheets, rows, _ = c.shape
    pairs = sheets * rows // LANES
    lines = chunks * pairs
    stored = shape_of(LANES // SUBLANES, lines, SUBLANES, LANES)
    matrix = jax.ShapeDtypeStruct((LANES, 2 * LANES), jnp.bfloat16)
    return pl.pallas_call(
        y_factor_kernel,
        in_specs=[IN_VMEM, ANYWHERE],
        out_shape=[
            stored,
            stored,
            stored,
            shape_of(SUBLANES - 1, 3, lines, LANES),
            shape_of(chunks - 1, 3, pairs, LANES),
            shape_of(len(COEFS), pairs, LANES),
            matrix,
            matrix,
        ],
        scratch_shapes=[
            pltpu.VMEM((pairs, chunks * LANES, LANES), F32),
            pltpu.VMEM((len(COEFS), lines * SUBLANES, LANES), F32),
            pltpu.VMEM((len(COEFS), lines, LANES), F32),
        ],
        compiler_params=params(),
        cost_estimate=pl.CostEstimate(flops=20 * c.size, bytes_accessed=16 * c.size, transcendentals=0),
    )(c, after)


def z_factor_kernel(c_ref, after, w_ref, i_ref):
    sheets = c_ref.shape[1]
    ground = 1.0
    for z in range(sheets - 1):
        face = c_ref[:, z] + c_ref[:, z + 1]
        inv = inverse(ground + face)
        w = face * inv
        i_ref[z] = inv
        w_ref[z] = w
        ground = 1.0 + w * ground
    i_ref[sheets - 1] = inverse(ground)


def z_factor(c, after):
    chunks, sheets, rows, _ = c.shape
    return pl.pallas_call(
        z_factor_kernel,
        in_specs=[IN_VMEM, ANYWHERE],
        out_shape=[
            shape_of(sheets - 1, chunks, rows, LANES),
            shape_of(sheets, chunks, rows, LANES),
        ],
        compiler_params=params(),
        cost_estimate=pl.CostEstimate(flops=10 * c.size, bytes_accessed=12 * c.size, transcendentals=0),
    )(c, after)


def join_tree(items, links, own):
    for offset, count in node_offsets(len(items)):
        joined = []
        for n in range(count):
            tie = tuple(links[offset + n, i] for i in range(3))
            both, flux = join_targets(items[2 * n], items[2 * n + 1], tie)
            own[offset + n] = flux
            joined.append(both)
        items = joined
    return items[0]


def tree_ends(leaves, links, own, low, high):
    levels = [
        [(own(offset + n), links[offset + n, 1], links[offset + n, 2]) for n in range(count)]
        for offset, count in node_offsets(leaves)
    ]
    return descend(levels, low, high)


def nothing(node):
    return 0.0


def y_prepare_kernel(stages, *refs):
    ties = refs[: stages - 1]
    xw, xh, xm, xp, x_links, x_own, t_ref, to_y = refs[stages - 1 : stages + 7]
    base, response, f_s, g_s = refs[stages + 7 :]
    x_steps, lines = xw.shape[:2]
    chunks = base.shape[0]
    sheets = lines // chunks
    rows = x_steps * SUBLANES

    ends, units = block_ends("gx", stages, ties)
    for n, (own, (low, high)) in enumerate(((lambda i: x_own[i], ends), (nothing, units))):
        for s, pair in enumerate(tree_ends(SUBLANES, x_links, own, low, high)):
            for i in range(2):
                f_s[n, i, pl.ds(s, lines, stride=SUBLANES), :] = pair[i]
    first = 0
    for n, members in enumerate(line_groups(chunks, sheets)):
        at = slice(first, first + len(members))
        h_ref_of, h_at = (xh, at) if n == 0 else (xm, slice(first - 2 * sheets, at.stop - 2 * sheets))
        (low, value), (unit_low, unit) = (
            [
                jnp.stack(
                    [f_s[q, i, j * SUBLANES : (j + 1) * SUBLANES, :] for j in range(at.start, at.stop)], 0
                )
                for i in range(2)
            ]
            for q in range(2)
        )
        for k in range(x_steps - 1, -1, -1):
            w, p = xw[k, at], xp[k, at]
            value = w * value + (h_ref_of[k, h_at] + p * low)
            unit = w * unit + p * unit_low
            field = value - t_ref[k, at]
            for j, (y, z) in enumerate(members):
                place = z * rows + k * SUBLANES
                g_s[0, y, place : place + SUBLANES, :] = field[j]
                g_s[1, y, place : place + SUBLANES, :] = unit[j]
        first = at.stop

    for y in range(chunks):
        base[y] = turned(to_y[...], g_s[0, y])
        response[y] = turned(to_y[...], g_s[1, y])


def y_prepare(ties, xw, xh, xm, xp, x_links, x_own, t, to_y, chunks):
    x_steps, lines = xw.shape[:2]
    width = lines // chunks * x_steps * SUBLANES
    field = shape_of(chunks, LANES, width)
    return pl.pallas_call(
        functools.partial(y_prepare_kernel, len(ties) + 1),
        out_shape=[field, field],
        scratch_shapes=[
            pltpu.VMEM((2, 2, lines * SUBLANES, LANES), F32),
            pltpu.VMEM((2, chunks, width, LANES), F32),
        ],
        compiler_params=params(),
        cost_estimate=pl.CostEstimate(flops=8 * t.size, bytes_accessed=16 * t.size, transcendentals=0),
    )(*ties, xw, xh, xm, xp, x_links, x_own, t, to_y)


def y_target_kernel(stages, own, got, base, response, yw, yi, yp, inner, outer, view, to_y, *refs):
    h_ref, inner_own, outer_own, send, q_s, r_s = refs
    chunks, _, width = base.shape
    pairs = width // LANES
    sheets = own.shape[1] // chunks
    rows = width // sheets
    steps = yw.shape[0]

    flux = top_flux("gx", stages, own, got)
    line_of = {member: n for n, member in enumerate(sum(line_groups(chunks, sheets), []))}
    fields = []
    for y in range(chunks):
        spread = jnp.concatenate(
            [
                jnp.broadcast_to(flux[line_of[y, z] : line_of[y, z] + 1, :], (rows, LANES))
                for z in range(sheets)
            ],
            0,
        )
        fields.append(base[y] + response[y] * turned(to_y[...], spread))

    def target(k):
        at = slice(k * SUBLANES, (k + 1) * SUBLANES)
        return jnp.stack(
            [fields[y][at, m * LANES : (m + 1) * LANES] for y in range(chunks) for m in range(pairs)], 0
        )

    def keep(k, h):
        h_ref[k] = h

    ends = eliminate(target, steps, lambda k: yw[k], lambda k: yi[k], lambda k: yp[k], keep)
    for q in range(2):
        for i in range(chunks * pairs):
            q_s[q, i * SUBLANES : (i + 1) * SUBLANES, :] = ends[q][i]
    items = [
        tuple(q_s[q, pl.ds(s, chunks * pairs, stride=SUBLANES), :] for q in range(2))
        for s in range(SUBLANES)
    ]
    r_s[0], r_s[1] = join_tree(items, inner, inner_own)
    items = [tuple(r_s[q, y * pairs : (y + 1) * pairs, :] for q in range(2)) for y in range(chunks)]
    for n, q in enumerate(COEFS):
        send[q] = view[n]
    send[FIRST], send[LAST] = join_tree(items, outer, outer_own)


def y_target(own, got, base, response, yw, yi, yp, inner, outer, view, to_y):
    y_lines = yw.shape[1]
    pairs = view.shape[1]
    chunks = y_lines // pairs
    return pl.pallas_call(
        functools.partial(y_target_kernel, stages_of("gx")),
        out_shape=[
            shape_of(*yw.shape),
            shape_of(SUBLANES - 1, y_lines, LANES),
            shape_of(chunks - 1, pairs, LANES),
            shape_of(7, pairs, LANES),
        ],
        scratch_shapes=[
            pltpu.VMEM((2, y_lines * SUBLANES, LANES), F32),
            pltpu.VMEM((2, y_lines, LANES), F32),
        ],
        compiler_params=params(),
    )(own, got, base, response, yw, yi, yp, inner, outer, view, to_y)


def z_solve(zw, zi, field, at, keep):
    sheets = zi.shape[0]
    rhs, kept = None, []
    for z in range(sheets):
        rhs = field(z) if z == 0 else field(z) + zw[z - 1, at] * rhs
        kept.append(rhs * zi[z, at])
    value = kept[-1]
    keep(sheets - 1, value)
    for z in range(sheets - 2, -1, -1):
        value = zw[z, at] * value + kept[z]
        keep(z, value)


def finish_prepare_kernel(stages, *refs):
    ties = refs[: stages - 1]
    yw, yh, yp, inner, inner_own, outer, outer_own, zw, zi, t_ref, to_x = refs[stages - 1 : stages + 10]
    base, response, r_s, e_s, u_s = refs[stages + 10 :]
    chunks, sheets, rows, _ = base.shape
    each = LANES // rows
    pairs = sheets // each
    steps = yw.shape[0]
    lines = chunks * pairs

    ends, units = block_ends("gy", stages, ties)
    both = (
        (lambda i: outer_own[i], lambda i: inner_own[i], ends),
        (nothing, nothing, units),
    )
    for n, (upper, lower, (low, high)) in enumerate(both):
        for y, pair in enumerate(tree_ends(chunks, outer, upper, low, high)):
            for i in range(2):
                r_s[n, i, y * pairs : (y + 1) * pairs, :] = pair[i]
        for s, pair in enumerate(tree_ends(SUBLANES, inner, lower, r_s[n, 0], r_s[n, 1])):
            for i in range(2):
                e_s[n, i, pl.ds(s, lines, stride=SUBLANES), :] = pair[i]
    (low, value), (unit_low, unit) = (
        [
            jnp.stack([e_s[q, i, n * SUBLANES : (n + 1) * SUBLANES, :] for n in range(lines)], 0)
            for i in range(2)
        ]
        for q in range(2)
    )
    for k in range(steps - 1, -1, -1):
        w, p = yw[k], yp[k]
        value = w * value + (yh[k] + p * low)
        unit = w * unit + p * unit_low
        for y in range(chunks):
            for m in range(pairs):
                place = pl.ds(y * LANES + k, SUBLANES, stride=steps)
                u_s[0, m, place, :] = value[y * pairs + m]
                u_s[1, m, place, :] = unit[y * pairs + m]

    for y in range(chunks):
        part = part_of(y)
        fields = [turned(to_x[...], u_s[0, m, part, :]) for m in range(pairs)]

        def field(z):
            at = z % each * rows
            return fields[z // each][at : at + rows, :]

        def keep(z, value):
            base[y, z] = t_ref[z, :, part] + value

        z_solve(zw, zi, field, y, keep)
        for m in range(pairs):
            units = turned(to_x[...], u_s[1, m, part, :])
            for i in range(each):
                response[y, m * each + i] = units[i * rows : (i + 1) * rows, :]


def finish_prepare(ties, yw, yh, yp, inner, inner_own, outer, outer_own, zw, zi, t, to_x):
    sheets, rows, columns = t.shape
    chunks = columns // LANES
    pairs = sheets * rows // LANES
    lines = chunks * pairs
    field = shape_of(chunks, sheets, rows, LANES)
    return pl.pallas_call(
        functools.partial(finish_prepare_kernel, len(ties) + 1),
        out_shape=[field, field],
        scratch_shapes=[
            pltpu.VMEM((2, 2, lines, LANES), F32),
            pltpu.VMEM((2, 2, lines * SUBLANES, LANES), F32),
            pltpu.VMEM((2, pairs, columns, LANES), F32),
        ],
        compiler_params=params(),
        cost_estimate=pl.CostEstimate(flops=12 * t.size, bytes_accessed=20 * t.size, transcendentals=0),
    )(*ties, yw, yh, yp, inner, inner_own, outer, outer_own, zw, zi, t, to_x)


def finish_kernel(stages, own, got, base, response, zw, zi, to_x, out, o_s, sems):
    chunks, sheets, rows, _ = base.shape
    each = LANES // rows
    pairs = sheets // each
    copies, _, wide = o_s.shape

    flux = top_flux("gy", stages, own, got)
    spread = [
        turned(to_x[...], jnp.broadcast_to(flux[m : m + 1, :], (LANES, LANES))) for m in range(pairs)
    ]
    started = []
    for n in range(copies):
        for y in range(n * chunks // copies, (n + 1) * chunks // copies):
            part = part_of(y - n * chunks // copies)

            def field(z):
                at = z % each * rows
                return response[y, z] * spread[z // each][at : at + rows, :]

            def keep(z, value):
                o_s[n, z * rows : (z + 1) * rows, part] = base[y, z] + value

            z_solve(zw, zi, field, y, keep)
        copy = pltpu.make_async_copy(o_s.at[n], out.at[:, pl.ds(n * wide, wide)], sems.at[n])
        copy.start()
        started.append(copy)
    for copy in started:
        copy.wait()


def finish(own, got, base, response, zw, zi, to_x):
    chunks, sheets, rows, _ = base.shape
    copies = chunks
    return pl.pallas_call(
        functools.partial(finish_kernel, stages_of("gy")),
        out_shape=shape_of(sheets * rows, chunks * LANES),
        out_specs=ANYWHERE,
        scratch_shapes=[
            pltpu.VMEM((copies, sheets * rows, chunks * LANES // copies), F32),
            pltpu.SemaphoreType.DMA((copies,)),
        ],
        compiler_params=params(),
    )(own, got, base, response, zw, zi, to_x).reshape(sheets, rows, chunks * LANES)


def per_device(temperature, base, locations, energy):
    columns = temperature.shape[2]
    gy = lax.axis_size("gy")
    packed = edges(temperature, base)
    near = swap(packed, "gy", 1)
    t, b, loc, heat = load((temperature, base, locations[None], energy[None]), packed)
    near, t, b = lax.optimization_barrier((near, t, b))
    far = [swap(near, "gy", 2)] if gy > 2 else []
    if gy > 4:
        far.append(lax.ppermute(near, "gy", [(i, (i + 2 ^ 2) - 2) for i in range(2, gy - 2)]))
    c, total, xw, xi, xp, x_links, x_view, xm, ends, t_steps = x_factor(loc, heat, t, b, columns * gy, near)
    xh, x_own, view = x_target(packed, t, total, [near] + far, xw, xi, xp, x_links, x_view, ends)
    yw, yi, yp, inner, outer, y_view, to_y, to_x = y_factor(c, x_view)
    zw, zi = z_factor(c, view)
    own, got, ties = gather_line(view, "gx", 2, (y_view, zw))
    base, response = y_prepare(
        ties, xw, xh, xm, xp, x_links, x_own, t_steps, to_y, columns // LANES
    )
    yh, inner_own, outer_own, view = y_target(
        own, got, base, response, yw, yi, yp, inner, outer, y_view, to_y
    )
    own, got, ties = gather_line(view, "gy")
    base, response = finish_prepare(
        ties, yw, yh, yp, inner, inner_own, outer, outer_own, zw, zi, t, to_x
    )
    return finish(own, got, base, response, zw, zi, to_x)


def solution(mesh):
    in_specs = (P(None, "gx", "gy"), P(None, "gx", "gy"), P(), P())
    out_specs = P(None, "gx", "gy")
    return jax.shard_map(
        per_device, mesh=mesh, in_specs=in_specs, out_specs=out_specs, check_vma=False
    )
```

```python
import functools

import jax
import jax.numpy as jnp
from jax import lax
from jax.experimental import pallas as pl
from jax.experimental.pallas import tpu as pltpu
from jax.sharding import PartitionSpec as P

RATE = 2000.0
THERMAL_GROWTH = 0.8
LANES = 128
SUBLANES = 8
F32 = jnp.float32
MIB = 1024 * 1024
ANYWHERE = pl.BlockSpec(memory_space=pl.ANY)
IN_HBM = pl.BlockSpec(memory_space=pltpu.HBM)
IN_VMEM = pl.BlockSpec(memory_space=pltpu.VMEM)

R00, R0L, RLL, FIRST, LAST, C0, CL = range(7)
COEFS = (R00, R0L, RLL, C0, CL)


def params(limit=40):
    return pltpu.CompilerParams(vmem_limit_bytes=limit * MIB)


def shape_of(*sizes):
    return jax.ShapeDtypeStruct(sizes, F32)


def half_conduct(base, temperature):
    return base * (0.5 * RATE + (0.5 * RATE * THERMAL_GROWTH) * temperature)


def inverse(x):
    guess = pl.reciprocal(x, approx=True)
    return guess * (2.0 - x * guess)


def join_coefs(a, b):
    face = a[CL] + b[C0]
    inv = face * inverse(1.0 + face * (a[RLL] + b[R00]))
    left = a[R0L] * inv
    right = b[R0L] * inv
    joined = {
        R00: a[R00] - left * a[R0L],
        R0L: left * b[R0L],
        RLL: b[RLL] - right * b[R0L],
        C0: a[C0],
        CL: b[CL],
    }
    return joined, (inv, right, left)


def join_targets(a, b, links):
    inv, right, left = links
    jump = b[0] - a[1]
    return (a[0] + left * jump, b[1] - right * jump), jump * inv


def between(own, right, left, low, high):
    return own + right * high - left * low


def tree(items, join):
    levels = []
    while len(items) > 1:
        pairs = [join(items[i], items[i + 1]) for i in range(0, len(items), 2)]
        items = [p[0] for p in pairs]
        levels.append([p[1] for p in pairs])
    return items[0], levels


def descend(levels, low, high):
    ends = [(low, high)]
    for level in reversed(levels):
        below = []
        for (lo, hi), (own, right, left) in zip(ends, level):
            flux = between(own, right, left, lo, hi)
            below += [(lo, flux), (-flux, hi)]
        ends = below
    return ends


def node_offsets(leaves):
    offsets, at, count = [], 0, leaves // 2
    while count:
        offsets.append((at, count))
        at += count
        count //= 2
    return offsets


def factor(cond, steps, keep):
    here = cond(0)
    c_first = here
    one = jnp.ones_like(here)
    ground, path, first_first = one, one, None
    for k in range(steps - 1):
        following = cond(k + 1)
        face = here + following
        inv = inverse(ground + face)
        w = face * inv
        p = path * inv
        keep(k, w, inv, p)
        step = path * p
        first_first = step if first_first is None else first_first + step
        path = path * w
        ground = 1.0 + w * ground
        here = following
    inv = inverse(ground)
    p = path * inv
    keep(steps - 1, inv, inv, p)
    return {R00: first_first + path * p, R0L: p, RLL: inv, C0: c_first, CL: here}


def eliminate(target, steps, w, inv, p, keep):
    rhs = target(0)
    first = None
    for k in range(steps):
        h = rhs * inv(k)
        keep(k, h)
        step = rhs * p(k)
        first = step if first is None else first + step
        if k < steps - 1:
            rhs = target(k + 1) + w(k) * rhs
    return first, h


def is_odd(axis):
    return lax.axis_index(axis) % 2 == 1


def fold(cells, used):
    total = cells[:SUBLANES]
    lane = lax.broadcasted_iota(jnp.int32, total.shape, 1)
    for n in range(1, cells.shape[0] // SUBLANES):
        part = pltpu.roll(cells[n * SUBLANES : (n + 1) * SUBLANES], n * used, 1)
        total = jnp.where(lane // used == n, part, total)
    return total


def unfold(cells, used, rows):
    parts = [cells] + [
        pltpu.roll(cells, LANES - n * used, 1) for n in range(1, rows // SUBLANES)
    ]
    return jnp.concatenate(parts, 0)


def edges_kernel(sheets, t_hbm, b_hbm, packed, t_s, b_s, sems):
    columns = t_hbm.shape[1]
    rows = t_hbm.shape[0] // sheets
    sides = []
    for side, start in enumerate((0, columns - LANES)):
        sides.append(
            [
                pltpu.make_async_copy(src.at[:, pl.ds(start, LANES)], dst.at[side], sems.at[i, side])
                for i, (src, dst) in enumerate(((t_hbm, t_s), (b_hbm, b_s)))
            ]
        )
        for copy in sides[-1]:
            copy.start()
    lane = lax.broadcasted_iota(jnp.int32, (rows, LANES), 1)
    total = jnp.zeros((rows, LANES), F32)
    for side, source in enumerate((0, LANES - 1)):
        for copy in sides[side]:
            copy.wait()
        for z in range(sheets):
            t = t_s[side, z * rows : (z + 1) * rows, :]
            c = half_conduct(b_s[side, z * rows : (z + 1) * rows, :], t)
            place = 2 * sheets * side + z
            total = jnp.where(lane == place, t[:, source : source + 1], total)
            total = jnp.where(lane == place + sheets, c[:, source : source + 1], total)
    packed[...] = fold(total, 4 * sheets)


def edges(temperature, base):
    sheets, rows, _ = temperature.shape
    assert rows // SUBLANES * 4 * sheets <= LANES
    columns = temperature.shape[2]
    fields = [
        pltpu.with_memory_space_constraint(v.reshape(sheets * rows, columns), pltpu.HBM)
        for v in (temperature, base)
    ]
    return pl.pallas_call(
        functools.partial(edges_kernel, sheets),
        in_specs=[IN_HBM] * 2,
        out_shape=pltpu.VMEM((SUBLANES, LANES), F32),
        scratch_shapes=[
            pltpu.VMEM((2, sheets * rows, LANES), F32),
            pltpu.VMEM((2, sheets * rows, LANES), F32),
            pltpu.SemaphoreType.DMA((2, 2)),
        ],
        compiler_params=params(),
    )(*fields)


def load_kernel(*refs):
    count = len(refs) // 2 - 1
    sems = refs[-1]
    copies = [
        pltpu.make_async_copy(refs[i], refs[count + 1 + i], sems.at[i]) for i in range(count)
    ]
    for copy in copies:
        copy.start()
    for copy in copies:
        copy.wait()


def load(values, after):
    return pl.pallas_call(
        load_kernel,
        in_specs=[IN_HBM] * len(values) + [ANYWHERE],
        out_shape=[pltpu.VMEM(v.shape, v.dtype) for v in values],
        scratch_shapes=[pltpu.SemaphoreType.DMA((len(values),))],
        compiler_params=params(),
        cost_estimate=pl.CostEstimate(
            flops=0, bytes_accessed=16 * values[0].size, transcendentals=0
        ),
    )(*[pltpu.with_memory_space_constraint(v, pltpu.HBM) for v in values], after)


def source_plane(loc, energy, rows, columns, plate):
    place = loc[...]
    count = place.shape[1]
    local_x = place // plate - lax.axis_index("gx") * rows
    local_y = place % plate - lax.axis_index("gy") * columns
    in_x = lax.broadcasted_iota(jnp.int32, (rows, count), 0) == local_x
    in_y = lax.broadcasted_iota(jnp.int32, (columns, count), 0) == local_y
    by_y = jnp.where(in_y, 1.0, 0.0).astype(jnp.bfloat16)
    left = energy[...]
    plane = None
    for _ in range(3):
        part = left.astype(jnp.bfloat16).astype(F32)
        left = left - part
        term = lax.dot_general(
            jnp.where(in_x, part, 0.0).astype(jnp.bfloat16),
            by_y,
            (((1,), (1,)), ((), ())),
            preferred_element_type=F32,
        )
        plane = term if plane is None else plane + term
    return plane


def part_of(y):
    return slice(y * LANES, (y + 1) * LANES)


def line_groups(chunks, sheets):
    order = [0, chunks - 1] + list(range(1, chunks - 1))
    return [[(y, z) for y in order[i : i + 2] for z in range(sheets)] for i in range(0, chunks, 2)]


def x_eliminate(field, members, first_line, w_ref, i_ref, p_ref, h_ref, h_line, q_s):
    steps = w_ref.shape[0]
    at = slice(first_line, first_line + len(members))
    kept_at = slice(h_line, h_line + len(members))

    def target(k):
        return jnp.stack([field(y, z)[pl.ds(k, SUBLANES, stride=steps), :] for y, z in members], 0)

    def keep(k, h):
        h_ref[k, kept_at] = h

    ends = eliminate(
        target, steps, lambda k: w_ref[k, at], lambda k: i_ref[k, at], lambda k: p_ref[k, at], keep
    )
    for q in range(2):
        for i in range(len(members)):
            first = (first_line + i) * SUBLANES
            q_s[q, first : first + SUBLANES, :] = ends[q][i]


def x_factor_kernel(plate, loc, energy, t_ref, b_ref, after, *refs):
    c_ref, total_ref, w_ref, i_ref, p_ref, links, view, h_ref, ends_ref, t_out, q_s, t_s = refs
    chunks, sheets, rows, _ = c_ref.shape
    lines = chunks * sheets
    steps = rows // SUBLANES
    plane = source_plane(loc, energy, rows, chunks * LANES, plate)

    lane = lax.broadcasted_iota(jnp.int32, (SUBLANES, LANES), 1)
    is_first, is_last = lane == 0, lane == LANES - 1
    for r in range(steps):
        at = slice(r * SUBLANES, (r + 1) * SUBLANES)
        before_t, before_c = None, None
        for z in range(sheets):
            ts = [t_ref[z, at, part_of(y)] for y in range(chunks)]
            cs = [half_conduct(b_ref[z, at, part_of(y)], ts[y]) for y in range(chunks)]
            t_turned = [pltpu.roll(v, LANES - 1, 1) for v in ts]
            c_turned = [pltpu.roll(v, LANES - 1, 1) for v in cs]
            flux = []
            for y in range(chunks):
                if y < chunks - 1:
                    t_next = jnp.where(is_last, t_turned[y + 1], t_turned[y])
                    c_next = jnp.where(is_last, c_turned[y + 1], c_turned[y])
                    flux.append((cs[y] + c_next) * (t_next - ts[y]))
                else:
                    inside = (cs[y] + c_turned[y]) * (t_turned[y] - ts[y])
                    flux.append(jnp.where(is_last, 0.0, inside))
            turned = [pltpu.roll(v, 1, 1) for v in flux]
            for y in range(chunks):
                from_low = jnp.where(is_first, turned[y - 1] if y else 0.0, turned[y])
                total = ts[y] + (flux[y] - from_low)
                if z == 0:
                    total = total + plane[at, part_of(y)]
                else:
                    across = (before_c[y] + cs[y]) * (ts[y] - before_t[y])
                    total = total - across
                    total_ref[y, z - 1, at, :] += across
                total_ref[y, z, at, :] = total
                c_ref[y, z, at, :] = cs[y]
                t_s[y, z, at, :] = ts[y]
            before_t, before_c = ts, cs

    at = 0
    for n, members in enumerate(line_groups(chunks, sheets)):

        def cond(k):
            return jnp.stack([c_ref[y, z, pl.ds(k, SUBLANES, stride=steps), :] for y, z in members], 0)

        def keep(k, w, inv, p):
            w_ref[k, at : at + len(members)] = w
            i_ref[k, at : at + len(members)] = inv
            p_ref[k, at : at + len(members)] = p

        block = factor(cond, steps, keep)
        for i, q in enumerate(COEFS):
            for j in range(len(members)):
                first = (at + j) * SUBLANES
                q_s[i, first : first + SUBLANES, :] = block[q][j]
        if n > 0:
            x_eliminate(
                lambda y, z: total_ref.at[y, z], members, at, w_ref, i_ref, p_ref, h_ref,
                at - 2 * sheets, ends_ref,
            )
        for k in range(steps):
            for i, (y, z) in enumerate(members):
                t_out[k, at + i] = t_s[y, z, pl.ds(k, SUBLANES, stride=steps), :]
        at += len(members)

    segments = [
        {q: q_s[n, pl.ds(s, lines, stride=SUBLANES), :] for n, q in enumerate(COEFS)}
        for s in range(SUBLANES)
    ]
    whole, levels = tree(segments, join_coefs)
    for (offset, _), level in zip(node_offsets(SUBLANES), levels):
        for n, values in enumerate(level):
            for i in range(3):
                links[offset + n, i] = values[i]
    for n, q in enumerate(COEFS):
        view[n] = whole[q]


def x_factor(loc, energy, t, b, plate, after):
    sheets, rows, columns = t.shape
    chunks = columns // LANES
    lines = chunks * sheets
    steps = rows // SUBLANES
    field = shape_of(chunks, sheets, rows, LANES)
    stored = shape_of(steps, lines, SUBLANES, LANES)
    return pl.pallas_call(
        functools.partial(x_factor_kernel, plate),
        in_specs=[IN_VMEM] * 4 + [ANYWHERE],
        out_shape=[
            field,
            field,
            stored,
            stored,
            stored,
            shape_of(SUBLANES - 1, 3, lines, LANES),
            shape_of(len(COEFS), lines, LANES),
            shape_of(steps, max(1, lines - 2 * sheets), SUBLANES, LANES),
            shape_of(2, lines * SUBLANES, LANES),
            stored,
        ],
        scratch_shapes=[
            pltpu.VMEM((len(COEFS), lines * SUBLANES, LANES), F32),
            pltpu.VMEM((chunks, sheets, rows, LANES), F32),
        ],
        compiler_params=params(),
        cost_estimate=pl.CostEstimate(flops=40 * t.size, bytes_accessed=28 * t.size, transcendentals=0),
    )(loc, energy, t, b, after)


def far_side(sources):
    place = lax.axis_index("gy")
    paired = (place >> 1) % 2 != place % 2
    nothing = jnp.zeros(sources[0].shape, F32)
    by_pair = sources[1][...] if len(sources) > 1 else nothing
    other = sources[2][...] if len(sources) > 2 else nothing
    return jnp.where(paired, by_pair, other)


def x_target_kernel(count, own_cells, t_ref, total_ref, *refs):
    w_ref, i_ref, p_ref, links, view, ends_ref, h_ref, own, send, e_s, q_s = refs[count:]
    chunks, sheets, rows, _ = total_ref.shape
    lines = chunks * sheets

    lane = lax.broadcasted_iota(jnp.int32, (rows, LANES), 1)
    side = 2 * sheets
    near, far = (unfold(v, 2 * side, rows) for v in (refs[0][...], far_side(refs[:count])))
    before = jnp.where(is_odd("gy"), near, far)
    after = jnp.where(is_odd("gy"), far, near)
    beyond = jnp.where(lane < side, pltpu.roll(before, LANES - side, 1), pltpu.roll(after, side, 1))
    mine = unfold(own_cells[...], 2 * side, rows)
    face = jnp.where(beyond > 0.0, mine + beyond, 0.0)
    flux = pltpu.roll(face, LANES - sheets, 1) * (beyond - mine)
    for n, (y, edge) in enumerate(((0, 0), (chunks - 1, LANES - 1))):
        for z in range(sheets):
            at = n * side + z
            e_s[n, z] = total_ref[y, z] + jnp.where(lane == edge, flux[:, at : at + 1], 0.0)

    members = line_groups(chunks, sheets)[0]
    x_eliminate(
        lambda y, z: e_s.at[0 if y == 0 else 1, z], members, 0, w_ref, i_ref, p_ref, h_ref, 0, q_s
    )
    split = len(members)
    items = [
        tuple(
            jnp.concatenate(
                [
                    q_s[q, pl.ds(s, split, stride=SUBLANES), :],
                    ends_ref[q, pl.ds(split * SUBLANES + s, lines - split, stride=SUBLANES), :],
                ],
                0,
            )
            for q in range(2)
        )
        for s in range(SUBLANES)
    ]
    for offset, count in node_offsets(SUBLANES):
        joined = []
        for n in range(count):
            ties = tuple(links[offset + n, i] for i in range(3))
            both, flux = join_targets(items[2 * n], items[2 * n + 1], ties)
            own[offset + n] = flux
            joined.append(both)
        items = joined
    for n, q in enumerate(COEFS):
        send[q] = view[n]
    send[FIRST], send[LAST] = items[0]


def x_target(own_cells, t, total, edge_cells, w, inv, p, links, view, ends):
    chunks, sheets, rows, _ = total.shape
    lines = chunks * sheets
    steps = rows // SUBLANES
    return pl.pallas_call(
        functools.partial(x_target_kernel, len(edge_cells)),
        out_shape=[
            shape_of(steps, 2 * sheets, SUBLANES, LANES),
            shape_of(SUBLANES - 1, lines, LANES),
            shape_of(7, lines, LANES),
        ],
        scratch_shapes=[
            pltpu.VMEM((2, sheets, rows, LANES), F32),
            pltpu.VMEM((2, 2 * sheets * SUBLANES, LANES), F32),
        ],
        compiler_params=params(),
    )(own_cells, t, total, *edge_cells, w, inv, p, links, view, ends)


def stages_of(axis):
    return lax.axis_size(axis).bit_length() - 1


def swap(value, axis, flip):
    count = lax.axis_size(axis)
    return lax.ppermute(value, axis, [(i, i ^ flip) for i in range(count)])


def on_right(axis, stage):
    return (lax.axis_index(axis) >> stage) % 2 == 1


def toward(right, block):
    return (
        jnp.where(right, block[R00], block[RLL]),
        jnp.where(right, block[FIRST], block[LAST]),
        jnp.where(right, block[C0], block[CL]),
    )


def join(a, b):
    joined, ties = join_coefs(a, b)
    (joined[FIRST], joined[LAST]), flux = join_targets((a[FIRST], a[LAST]), (b[FIRST], b[LAST]), ties)
    return joined, (flux, ties[1], ties[2])


def ordered(right, own, other):
    first = [jnp.where(right, theirs, mine) for mine, theirs in zip(own, other)]
    second = [jnp.where(right, mine, theirs) for mine, theirs in zip(own, other)]
    return first, second


def join_kernel(axis, stage, width, last, *refs):
    count = 1 << width
    blocks = [[refs[i][q] for q in range(7)] for i in range(count)]
    send = refs[-1 - width]
    links = refs[-width:]
    for bit in range(width):
        right = on_right(axis, stage + bit)
        for i in range(count):
            if not i >> bit & 1:
                j = i | 1 << bit
                blocks[i], blocks[j] = ordered(right, blocks[i], blocks[j])
    for bit in range(width):
        pairs = [join(blocks[i], blocks[i + 1]) for i in range(0, len(blocks), 2)]
        blocks = [p[0] for p in pairs]
        ties = [p[1] for p in pairs]
        for upper in range(bit + 1, width):
            right = on_right(axis, stage + upper)
            ties = [
                tuple(jnp.where(right, v, u) for u, v in zip(ties[i], ties[i + 1]))
                for i in range(0, len(ties), 2)
            ]
        for i in range(3):
            links[bit][i] = ties[0][i]
    (whole,) = blocks
    if last:
        for n, value in enumerate(toward(on_right(axis, stage + width), whole)):
            send[n] = value
    else:
        for q in range(7):
            send[q] = whole[q]


def join_stage(own, got, axis, stage, width, last, after):
    lines = own.shape[1]
    return pl.pallas_call(
        functools.partial(join_kernel, axis, stage, width, last),
        in_specs=[IN_VMEM] * (1 + len(got)) + [ANYWHERE] * len(after),
        out_shape=[shape_of(3 if last else 7, lines, LANES)] + [shape_of(3, lines, LANES)] * width,
        compiler_params=params(),
    )(own, *got, *after)


def gather_line(view, axis, widest=1, meanwhile=(), one_core=False):
    stages = stages_of(axis)
    links, stage = [], 0
    while stage < stages - 1:
        width = min(widest, stages - 1 - stage)
        got = [swap(view, axis, flip << stage) for flip in range(1, 1 << width)]
        last = stage + width == stages - 1
        view, *ties = join_stage(view, got, axis, stage, width, last, meanwhile)
        links += ties
        stage += width
        meanwhile = ()
    if one_core and stage:
        pairs = [(i, i ^ 1 << stage) for i in range(1, 1 << stages, 2)]
        got = lax.ppermute(view, axis, pairs)
        return view, (got, swap(got, axis, 1)), links
    return view, swap(view, axis, 1 << stage), links


def top_flux(axis, stages, own, got):
    right = on_right(axis, stages - 1)
    face = own[2] + got[2]
    jump = jnp.where(right, own[1] - got[1], got[1] - own[1])
    return jump * face * inverse(1.0 + face * (own[0] + got[0]))


def block_ends(axis, stages, links):
    shape = links[0].shape[1:] if links else None
    right = on_right(axis, stages - 1)
    zero = jnp.zeros(shape, F32)
    low, high = zero, zero
    unit_low = zero + jnp.where(right, -1.0, 0.0)
    unit_high = zero + jnp.where(right, 0.0, 1.0)
    for stage in range(stages - 2, -1, -1):
        tie = links[stage]
        right = on_right(axis, stage)
        flux = between(tie[0], tie[1], tie[2], low, high)
        unit = between(0.0, tie[1], tie[2], unit_low, unit_high)
        low, high = jnp.where(right, -flux, low), jnp.where(right, high, flux)
        unit_low, unit_high = jnp.where(right, -unit, unit_low), jnp.where(right, unit_high, unit)
    return (low, high), (unit_low, unit_high)


def natural(index, parts):
    span = SUBLANES * parts
    local = index % span
    return index - local + local % SUBLANES * parts + local // SUBLANES


def turn_matrix(shape, from_natural, parts):
    row = lax.broadcasted_iota(jnp.int32, shape, 0)
    column = lax.broadcasted_iota(jnp.int32, shape, 1) % LANES
    hit = natural(row, parts) == column if from_natural else row == natural(column, parts)
    return jnp.where(hit, 1.0, 0.0).astype(jnp.bfloat16)


def turned(matrix, field):
    high = field.astype(jnp.bfloat16)
    low = (field - high.astype(F32)).astype(jnp.bfloat16)
    both = jnp.concatenate([high, low], 1)
    return lax.dot_general(
        matrix, both, (((1,), (1,)), ((), ())), preferred_element_type=F32
    )


def y_factor_kernel(c_ref, after, w_ref, i_ref, p_ref, inner, outer, view, to_y, to_x, c_s, q_s, r_s):
    chunks, sheets, rows, _ = c_ref.shape
    each = LANES // rows
    pairs = sheets // each
    x_steps = rows // SUBLANES
    steps = LANES // SUBLANES
    to_y[...] = turn_matrix(to_y.shape, True, steps)
    to_x[...] = turn_matrix(to_x.shape, False, x_steps)
    for m in range(pairs):
        for y in range(chunks):
            block = jnp.concatenate(
                [
                    c_ref[y, m * each + i, pl.ds(k, SUBLANES, stride=x_steps), :]
                    for i in range(each)
                    for k in range(x_steps)
                ],
                0,
            )
            c_s[m, part_of(y), :] = block.T

    members = [(y, m) for y in range(chunks) for m in range(pairs)]
    lines = len(members)

    def cond(k):
        return jnp.stack([c_s[m, pl.ds(y * LANES + k, SUBLANES, stride=steps), :] for y, m in members], 0)

    def keep(k, w, inv, p):
        w_ref[k] = w
        i_ref[k] = inv
        p_ref[k] = p

    block = factor(cond, steps, keep)
    for n, q in enumerate(COEFS):
        for i in range(lines):
            q_s[n, i * SUBLANES : (i + 1) * SUBLANES, :] = block[q][i]
    segments = [
        {q: q_s[n, pl.ds(s, lines, stride=SUBLANES), :] for n, q in enumerate(COEFS)}
        for s in range(SUBLANES)
    ]
    whole, levels = tree(segments, join_coefs)
    for (offset, _), level in zip(node_offsets(SUBLANES), levels):
        for n, values in enumerate(level):
            for i in range(3):
                inner[offset + n, i] = values[i]
    for n, q in enumerate(COEFS):
        r_s[n] = whole[q]
    parts = [
        {q: r_s[n, y * pairs : (y + 1) * pairs, :] for n, q in enumerate(COEFS)} for y in range(chunks)
    ]
    whole, levels = tree(parts, join_coefs)
    for (offset, _), level in zip(node_offsets(chunks), levels):
        for n, values in enumerate(level):
            for i in range(3):
                outer[offset + n, i] = values[i]
    for n, q in enumerate(COEFS):
        view[n] = whole[q]


def y_factor(c, after):
    chunks, sheets, rows, _ = c.shape
    pairs = sheets * rows // LANES
    lines = chunks * pairs
    stored = shape_of(LANES // SUBLANES, lines, SUBLANES, LANES)
    matrix = jax.ShapeDtypeStruct((LANES, 2 * LANES), jnp.bfloat16)
    return pl.pallas_call(
        y_factor_kernel,
        in_specs=[IN_VMEM, ANYWHERE],
        out_shape=[
            stored,
            stored,
            stored,
            shape_of(SUBLANES - 1, 3, lines, LANES),
            shape_of(chunks - 1, 3, pairs, LANES),
            shape_of(len(COEFS), pairs, LANES),
            matrix,
            matrix,
        ],
        scratch_shapes=[
            pltpu.VMEM((pairs, chunks * LANES, LANES), F32),
            pltpu.VMEM((len(COEFS), lines * SUBLANES, LANES), F32),
            pltpu.VMEM((len(COEFS), lines, LANES), F32),
        ],
        compiler_params=params(),
        cost_estimate=pl.CostEstimate(flops=20 * c.size, bytes_accessed=16 * c.size, transcendentals=0),
    )(c, after)


def z_factor_kernel(c_ref, after, w_ref, i_ref):
    sheets = c_ref.shape[1]
    ground = 1.0
    for z in range(sheets - 1):
        face = c_ref[:, z] + c_ref[:, z + 1]
        inv = inverse(ground + face)
        w = face * inv
        i_ref[z] = inv
        w_ref[z] = w
        ground = 1.0 + w * ground
    i_ref[sheets - 1] = inverse(ground)


def z_factor(c, after):
    chunks, sheets, rows, _ = c.shape
    return pl.pallas_call(
        z_factor_kernel,
        in_specs=[IN_VMEM, ANYWHERE],
        out_shape=[
            shape_of(sheets - 1, chunks, rows, LANES),
            shape_of(sheets, chunks, rows, LANES),
        ],
        compiler_params=params(),
        cost_estimate=pl.CostEstimate(flops=10 * c.size, bytes_accessed=12 * c.size, transcendentals=0),
    )(c, after)


def join_tree(items, links, own):
    for offset, count in node_offsets(len(items)):
        joined = []
        for n in range(count):
            tie = tuple(links[offset + n, i] for i in range(3))
            both, flux = join_targets(items[2 * n], items[2 * n + 1], tie)
            own[offset + n] = flux
            joined.append(both)
        items = joined
    return items[0]


def tree_ends(leaves, links, own, low, high):
    levels = [
        [(own(offset + n), links[offset + n, 1], links[offset + n, 2]) for n in range(count)]
        for offset, count in node_offsets(leaves)
    ]
    return descend(levels, low, high)


def nothing(node):
    return 0.0


def y_prepare_kernel(stages, *refs):
    ties = refs[: stages - 1]
    xw, xh, xm, xp, x_links, x_own, t_ref, to_y = refs[stages - 1 : stages + 7]
    base, response, f_s, g_s = refs[stages + 7 :]
    x_steps, lines = xw.shape[:2]
    chunks = base.shape[0]
    sheets = lines // chunks
    rows = x_steps * SUBLANES

    ends, units = block_ends("gx", stages, ties)
    for n, (own, (low, high)) in enumerate(((lambda i: x_own[i], ends), (nothing, units))):
        for s, pair in enumerate(tree_ends(SUBLANES, x_links, own, low, high)):
            for i in range(2):
                f_s[n, i, pl.ds(s, lines, stride=SUBLANES), :] = pair[i]
    first = 0
    for n, members in enumerate(line_groups(chunks, sheets)):
        at = slice(first, first + len(members))
        h_ref_of, h_at = (xh, at) if n == 0 else (xm, slice(first - 2 * sheets, at.stop - 2 * sheets))
        (low, value), (unit_low, unit) = (
            [
                jnp.stack(
                    [f_s[q, i, j * SUBLANES : (j + 1) * SUBLANES, :] for j in range(at.start, at.stop)], 0
                )
                for i in range(2)
            ]
            for q in range(2)
        )
        for k in range(x_steps - 1, -1, -1):
            w, p = xw[k, at], xp[k, at]
            value = w * value + (h_ref_of[k, h_at] + p * low)
            unit = w * unit + p * unit_low
            field = value - t_ref[k, at]
            for j, (y, z) in enumerate(members):
                place = z * rows + k * SUBLANES
                g_s[0, y, place : place + SUBLANES, :] = field[j]
                g_s[1, y, place : place + SUBLANES, :] = unit[j]
        first = at.stop

    for y in range(chunks):
        base[y] = turned(to_y[...], g_s[0, y])
        response[y] = turned(to_y[...], g_s[1, y])


def y_prepare(ties, xw, xh, xm, xp, x_links, x_own, t, to_y, chunks):
    x_steps, lines = xw.shape[:2]
    width = lines // chunks * x_steps * SUBLANES
    field = shape_of(chunks, LANES, width)
    return pl.pallas_call(
        functools.partial(y_prepare_kernel, len(ties) + 1),
        out_shape=[field, field],
        scratch_shapes=[
            pltpu.VMEM((2, 2, lines * SUBLANES, LANES), F32),
            pltpu.VMEM((2, chunks, width, LANES), F32),
        ],
        compiler_params=params(),
        cost_estimate=pl.CostEstimate(flops=8 * t.size, bytes_accessed=16 * t.size, transcendentals=0),
    )(*ties, xw, xh, xm, xp, x_links, x_own, t, to_y)


def y_target_kernel(stages, own, got, base, response, yw, yi, yp, inner, outer, view, to_y, *refs):
    h_ref, inner_own, outer_own, send, q_s, r_s = refs
    chunks, _, width = base.shape
    pairs = width // LANES
    sheets = own.shape[1] // chunks
    rows = width // sheets
    steps = yw.shape[0]

    flux = top_flux("gx", stages, own, got)
    line_of = {member: n for n, member in enumerate(sum(line_groups(chunks, sheets), []))}
    fields = []
    for y in range(chunks):
        spread = jnp.concatenate(
            [
                jnp.broadcast_to(flux[line_of[y, z] : line_of[y, z] + 1, :], (rows, LANES))
                for z in range(sheets)
            ],
            0,
        )
        fields.append(base[y] + response[y] * turned(to_y[...], spread))

    def target(k):
        at = slice(k * SUBLANES, (k + 1) * SUBLANES)
        return jnp.stack(
            [fields[y][at, m * LANES : (m + 1) * LANES] for y in range(chunks) for m in range(pairs)], 0
        )

    def keep(k, h):
        h_ref[k] = h

    ends = eliminate(target, steps, lambda k: yw[k], lambda k: yi[k], lambda k: yp[k], keep)
    for q in range(2):
        for i in range(chunks * pairs):
            q_s[q, i * SUBLANES : (i + 1) * SUBLANES, :] = ends[q][i]
    items = [
        tuple(q_s[q, pl.ds(s, chunks * pairs, stride=SUBLANES), :] for q in range(2))
        for s in range(SUBLANES)
    ]
    r_s[0], r_s[1] = join_tree(items, inner, inner_own)
    items = [tuple(r_s[q, y * pairs : (y + 1) * pairs, :] for q in range(2)) for y in range(chunks)]
    for n, q in enumerate(COEFS):
        send[q] = view[n]
    send[FIRST], send[LAST] = join_tree(items, outer, outer_own)


def y_target(own, got, base, response, yw, yi, yp, inner, outer, view, to_y):
    y_lines = yw.shape[1]
    pairs = view.shape[1]
    chunks = y_lines // pairs
    return pl.pallas_call(
        functools.partial(y_target_kernel, stages_of("gx")),
        out_shape=[
            shape_of(*yw.shape),
            shape_of(SUBLANES - 1, y_lines, LANES),
            shape_of(chunks - 1, pairs, LANES),
            shape_of(7, pairs, LANES),
        ],
        scratch_shapes=[
            pltpu.VMEM((2, y_lines * SUBLANES, LANES), F32),
            pltpu.VMEM((2, y_lines, LANES), F32),
        ],
        compiler_params=params(),
    )(own, got, base, response, yw, yi, yp, inner, outer, view, to_y)


def z_solve(zw, zi, field, at, keep):
    sheets = zi.shape[0]
    rhs, kept = None, []
    for z in range(sheets):
        rhs = field(z) if z == 0 else field(z) + zw[z - 1, at] * rhs
        kept.append(rhs * zi[z, at])
    value = kept[-1]
    keep(sheets - 1, value)
    for z in range(sheets - 2, -1, -1):
        value = zw[z, at] * value + kept[z]
        keep(z, value)


def finish_prepare_kernel(stages, *refs):
    ties = refs[: stages - 1]
    yw, yh, yp, inner, inner_own, outer, outer_own, zw, zi, t_ref, to_x = refs[stages - 1 : stages + 10]
    base, response, r_s, e_s, u_s = refs[stages + 10 :]
    chunks, sheets, rows, _ = base.shape
    each = LANES // rows
    pairs = sheets // each
    steps = yw.shape[0]
    lines = chunks * pairs

    ends, units = block_ends("gy", stages, ties)
    both = (
        (lambda i: outer_own[i], lambda i: inner_own[i], ends),
        (nothing, nothing, units),
    )
    for n, (upper, lower, (low, high)) in enumerate(both):
        for y, pair in enumerate(tree_ends(chunks, outer, upper, low, high)):
            for i in range(2):
                r_s[n, i, y * pairs : (y + 1) * pairs, :] = pair[i]
        for s, pair in enumerate(tree_ends(SUBLANES, inner, lower, r_s[n, 0], r_s[n, 1])):
            for i in range(2):
                e_s[n, i, pl.ds(s, lines, stride=SUBLANES), :] = pair[i]
    (low, value), (unit_low, unit) = (
        [
            jnp.stack([e_s[q, i, n * SUBLANES : (n + 1) * SUBLANES, :] for n in range(lines)], 0)
            for i in range(2)
        ]
        for q in range(2)
    )
    for k in range(steps - 1, -1, -1):
        w, p = yw[k], yp[k]
        value = w * value + (yh[k] + p * low)
        unit = w * unit + p * unit_low
        for y in range(chunks):
            for m in range(pairs):
                place = pl.ds(y * LANES + k, SUBLANES, stride=steps)
                u_s[0, m, place, :] = value[y * pairs + m]
                u_s[1, m, place, :] = unit[y * pairs + m]

    for y in range(chunks):
        part = part_of(y)
        fields = [turned(to_x[...], u_s[0, m, part, :]) for m in range(pairs)]

        def field(z):
            at = z % each * rows
            return fields[z // each][at : at + rows, :]

        def keep(z, value):
            base[y, z] = t_ref[z, :, part] + value

        z_solve(zw, zi, field, y, keep)
        for m in range(pairs):
            units = turned(to_x[...], u_s[1, m, part, :])
            for i in range(each):
                response[y, m * each + i] = units[i * rows : (i + 1) * rows, :]


def finish_prepare(ties, yw, yh, yp, inner, inner_own, outer, outer_own, zw, zi, t, to_x):
    sheets, rows, columns = t.shape
    chunks = columns // LANES
    pairs = sheets * rows // LANES
    lines = chunks * pairs
    field = shape_of(chunks, sheets, rows, LANES)
    return pl.pallas_call(
        functools.partial(finish_prepare_kernel, len(ties) + 1),
        out_shape=[field, field],
        scratch_shapes=[
            pltpu.VMEM((2, 2, lines, LANES), F32),
            pltpu.VMEM((2, 2, lines * SUBLANES, LANES), F32),
            pltpu.VMEM((2, pairs, columns, LANES), F32),
        ],
        compiler_params=params(),
        cost_estimate=pl.CostEstimate(flops=12 * t.size, bytes_accessed=20 * t.size, transcendentals=0),
    )(*ties, yw, yh, yp, inner, inner_own, outer, outer_own, zw, zi, t, to_x)


def finish_kernel(stages, own, *refs):
    *parts, base, response, zw, zi, to_x, out, o_s, sems = refs
    chunks, sheets, rows, _ = base.shape
    each = LANES // rows
    pairs = sheets // each
    copies, _, wide = o_s.shape

    got = [jnp.where(is_odd("gy"), parts[0][q], parts[-1][q]) for q in range(3)]
    flux = top_flux("gy", stages, own, got)
    spread = [
        turned(to_x[...], jnp.broadcast_to(flux[m : m + 1, :], (LANES, LANES))) for m in range(pairs)
    ]
    started = []
    for n in range(copies):
        for y in range(n * chunks // copies, (n + 1) * chunks // copies):
            part = part_of(y - n * chunks // copies)

            def field(z):
                at = z % each * rows
                return response[y, z] * spread[z // each][at : at + rows, :]

            def keep(z, value):
                o_s[n, z * rows : (z + 1) * rows, part] = base[y, z] + value

            z_solve(zw, zi, field, y, keep)
        copy = pltpu.make_async_copy(o_s.at[n], out.at[:, pl.ds(n * wide, wide)], sems.at[n])
        copy.start()
        started.append(copy)
    for copy in started:
        copy.wait()


def finish(own, got, base, response, zw, zi, to_x):
    chunks, sheets, rows, _ = base.shape
    copies = chunks
    return pl.pallas_call(
        functools.partial(finish_kernel, stages_of("gy")),
        out_shape=shape_of(sheets * rows, chunks * LANES),
        out_specs=ANYWHERE,
        scratch_shapes=[
            pltpu.VMEM((copies, sheets * rows, chunks * LANES // copies), F32),
            pltpu.SemaphoreType.DMA((copies,)),
        ],
        compiler_params=params(),
    )(own, *got, base, response, zw, zi, to_x).reshape(sheets, rows, chunks * LANES)


def per_device(temperature, base, locations, energy):
    columns = temperature.shape[2]
    gy = lax.axis_size("gy")
    packed = edges(temperature, base)
    near = swap(packed, "gy", 1)
    t, b, loc, heat = load((temperature, base, locations[None], energy[None]), packed)
    near, t, b = lax.optimization_barrier((near, t, b))
    far = [swap(near, "gy", 2)] if gy > 2 else []
    if gy > 4:
        far.append(lax.ppermute(near, "gy", [(i, (i + 2 ^ 2) - 2) for i in range(2, gy - 2)]))
    c, total, xw, xi, xp, x_links, x_view, xm, ends, t_steps = x_factor(loc, heat, t, b, columns * gy, near)
    xh, x_own, view = x_target(packed, t, total, [near] + far, xw, xi, xp, x_links, x_view, ends)
    yw, yi, yp, inner, outer, y_view, to_y, to_x = y_factor(c, x_view)
    zw, zi = z_factor(c, view)
    own, got, ties = gather_line(view, "gx", 2, (y_view, zw))
    base, response = y_prepare(
        ties, xw, xh, xm, xp, x_links, x_own, t_steps, to_y, columns // LANES
    )
    yh, inner_own, outer_own, view = y_target(
        own, got, base, response, yw, yi, yp, inner, outer, y_view, to_y
    )
    own, got, ties = gather_line(view, "gy", one_core=True)
    base, response = finish_prepare(
        ties, yw, yh, yp, inner, inner_own, outer, outer_own, zw, zi, t, to_x
    )
    return finish(own, got, base, response, zw, zi, to_x)


def solution(mesh):
    in_specs = (P(None, "gx", "gy"), P(None, "gx", "gy"), P(), P())
    out_specs = P(None, "gx", "gy")
    return jax.shard_map(
        per_device, mesh=mesh, in_specs=in_specs, out_specs=out_specs, check_vma=False
    )
```

```python
import functools

import jax
import jax.numpy as jnp
from jax import lax
from jax.experimental import pallas as pl
from jax.experimental.pallas import tpu as pltpu
from jax.sharding import PartitionSpec as P

RATE = 2000.0
THERMAL_GROWTH = 0.8
LANES = 128
SUBLANES = 8
F32 = jnp.float32
MIB = 1024 * 1024
ANYWHERE = pl.BlockSpec(memory_space=pl.ANY)
IN_HBM = pl.BlockSpec(memory_space=pltpu.HBM)
IN_VMEM = pl.BlockSpec(memory_space=pltpu.VMEM)

R00, R0L, RLL, FIRST, LAST, C0, CL = range(7)
COEFS = (R00, R0L, RLL, C0, CL)


def params(limit=40):
    return pltpu.CompilerParams(vmem_limit_bytes=limit * MIB)


def shape_of(*sizes):
    return jax.ShapeDtypeStruct(sizes, F32)


def half_conduct(base, temperature):
    return base * (0.5 * RATE + (0.5 * RATE * THERMAL_GROWTH) * temperature)


def inverse(x):
    guess = pl.reciprocal(x, approx=True)
    return guess * (2.0 - x * guess)


def join_coefs(a, b):
    face = a[CL] + b[C0]
    inv = face * inverse(1.0 + face * (a[RLL] + b[R00]))
    left = a[R0L] * inv
    right = b[R0L] * inv
    joined = {
        R00: a[R00] - left * a[R0L],
        R0L: left * b[R0L],
        RLL: b[RLL] - right * b[R0L],
        C0: a[C0],
        CL: b[CL],
    }
    return joined, (inv, right, left)


def join_targets(a, b, links):
    inv, right, left = links
    jump = b[0] - a[1]
    return (a[0] + left * jump, b[1] - right * jump), jump * inv


def between(own, right, left, low, high):
    return own + right * high - left * low


def tree(items, join):
    levels = []
    while len(items) > 1:
        pairs = [join(items[i], items[i + 1]) for i in range(0, len(items), 2)]
        items = [p[0] for p in pairs]
        levels.append([p[1] for p in pairs])
    return items[0], levels


def descend(levels, low, high):
    ends = [(low, high)]
    for level in reversed(levels):
        below = []
        for (lo, hi), (own, right, left) in zip(ends, level):
            flux = between(own, right, left, lo, hi)
            below += [(lo, flux), (-flux, hi)]
        ends = below
    return ends


def node_offsets(leaves):
    offsets, at, count = [], 0, leaves // 2
    while count:
        offsets.append((at, count))
        at += count
        count //= 2
    return offsets


def factor(cond, steps, keep):
    here = cond(0)
    c_first = here
    one = jnp.ones_like(here)
    ground, path, first_first = one, one, None
    for k in range(steps - 1):
        following = cond(k + 1)
        face = here + following
        inv = inverse(ground + face)
        w = face * inv
        p = path * inv
        keep(k, w, inv, p)
        step = path * p
        first_first = step if first_first is None else first_first + step
        path = path * w
        ground = 1.0 + w * ground
        here = following
    inv = inverse(ground)
    p = path * inv
    keep(steps - 1, inv, inv, p)
    return {R00: first_first + path * p, R0L: p, RLL: inv, C0: c_first, CL: here}


def eliminate(target, steps, w, inv, p, keep):
    rhs = target(0)
    first = None
    for k in range(steps):
        h = rhs * inv(k)
        keep(k, h)
        step = rhs * p(k)
        first = step if first is None else first + step
        if k < steps - 1:
            rhs = target(k + 1) + w(k) * rhs
    return first, h


def is_odd(axis):
    return lax.axis_index(axis) % 2 == 1


def fold(cells, used):
    total = cells[:SUBLANES]
    lane = lax.broadcasted_iota(jnp.int32, total.shape, 1)
    for n in range(1, cells.shape[0] // SUBLANES):
        part = pltpu.roll(cells[n * SUBLANES : (n + 1) * SUBLANES], n * used, 1)
        total = jnp.where(lane // used == n, part, total)
    return total


def unfold(cells, used, rows):
    parts = [cells] + [
        pltpu.roll(cells, LANES - n * used, 1) for n in range(1, rows // SUBLANES)
    ]
    return jnp.concatenate(parts, 0)


def edges_kernel(sheets, t_hbm, b_hbm, packed, t_s, b_s, sems):
    columns = t_hbm.shape[1]
    rows = t_hbm.shape[0] // sheets
    sides = []
    for side, start in enumerate((0, columns - LANES)):
        sides.append(
            [
                pltpu.make_async_copy(src.at[:, pl.ds(start, LANES)], dst.at[side], sems.at[i, side])
                for i, (src, dst) in enumerate(((t_hbm, t_s), (b_hbm, b_s)))
            ]
        )
        for copy in sides[-1]:
            copy.start()
    lane = lax.broadcasted_iota(jnp.int32, (rows, LANES), 1)
    total = jnp.zeros((rows, LANES), F32)
    for side, source in enumerate((0, LANES - 1)):
        for copy in sides[side]:
            copy.wait()
        for z in range(sheets):
            t = t_s[side, z * rows : (z + 1) * rows, :]
            c = half_conduct(b_s[side, z * rows : (z + 1) * rows, :], t)
            place = 2 * sheets * side + z
            total = jnp.where(lane == place, t[:, source : source + 1], total)
            total = jnp.where(lane == place + sheets, c[:, source : source + 1], total)
    packed[...] = fold(total, 4 * sheets)


def edges(temperature, base):
    sheets, rows, _ = temperature.shape
    assert rows // SUBLANES * 4 * sheets <= LANES
    columns = temperature.shape[2]
    fields = [
        pltpu.with_memory_space_constraint(v.reshape(sheets * rows, columns), pltpu.HBM)
        for v in (temperature, base)
    ]
    return pl.pallas_call(
        functools.partial(edges_kernel, sheets),
        in_specs=[IN_HBM] * 2,
        out_shape=pltpu.VMEM((SUBLANES, LANES), F32),
        scratch_shapes=[
            pltpu.VMEM((2, sheets * rows, LANES), F32),
            pltpu.VMEM((2, sheets * rows, LANES), F32),
            pltpu.SemaphoreType.DMA((2, 2)),
        ],
        compiler_params=params(),
    )(*fields)


def load_kernel(*refs):
    count = len(refs) // 2 - 1
    sems = refs[-1]
    copies = [
        pltpu.make_async_copy(refs[i], refs[count + 1 + i], sems.at[i]) for i in range(count)
    ]
    for copy in copies:
        copy.start()
    for copy in copies:
        copy.wait()


def load(values, after):
    return pl.pallas_call(
        load_kernel,
        in_specs=[IN_HBM] * len(values) + [ANYWHERE],
        out_shape=[pltpu.VMEM(v.shape, v.dtype) for v in values],
        scratch_shapes=[pltpu.SemaphoreType.DMA((len(values),))],
        compiler_params=params(),
        cost_estimate=pl.CostEstimate(
            flops=0, bytes_accessed=16 * values[0].size, transcendentals=0
        ),
    )(*[pltpu.with_memory_space_constraint(v, pltpu.HBM) for v in values], after)


def source_plane(loc, energy, rows, columns, plate):
    place = loc[...]
    count = place.shape[1]
    local_x = place // plate - lax.axis_index("gx") * rows
    local_y = place % plate - lax.axis_index("gy") * columns
    in_x = lax.broadcasted_iota(jnp.int32, (rows, count), 0) == local_x
    in_y = lax.broadcasted_iota(jnp.int32, (columns, count), 0) == local_y
    by_y = jnp.where(in_y, 1.0, 0.0).astype(jnp.bfloat16)
    left = energy[...]
    plane = None
    for _ in range(3):
        part = left.astype(jnp.bfloat16).astype(F32)
        left = left - part
        term = lax.dot_general(
            jnp.where(in_x, part, 0.0).astype(jnp.bfloat16),
            by_y,
            (((1,), (1,)), ((), ())),
            preferred_element_type=F32,
        )
        plane = term if plane is None else plane + term
    return plane


def part_of(y):
    return slice(y * LANES, (y + 1) * LANES)


def line_groups(chunks, sheets):
    order = [0, chunks - 1] + list(range(1, chunks - 1))
    return [[(y, z) for y in order[i : i + 2] for z in range(sheets)] for i in range(0, chunks, 2)]


def x_eliminate(field, members, first_line, w_ref, i_ref, p_ref, h_ref, h_line, q_s):
    steps = w_ref.shape[0]
    at = slice(first_line, first_line + len(members))
    kept_at = slice(h_line, h_line + len(members))

    def target(k):
        return jnp.stack([field(y, z)[pl.ds(k, SUBLANES, stride=steps), :] for y, z in members], 0)

    def keep(k, h):
        h_ref[k, kept_at] = h

    ends = eliminate(
        target, steps, lambda k: w_ref[k, at], lambda k: i_ref[k, at], lambda k: p_ref[k, at], keep
    )
    for q in range(2):
        for i in range(len(members)):
            first = (first_line + i) * SUBLANES
            q_s[q, first : first + SUBLANES, :] = ends[q][i]


def x_factor_kernel(plate, loc, energy, t_ref, b_ref, after, *refs):
    c_ref, total_ref, w_ref, i_ref, p_ref, links, view, h_ref, ends_ref, t_out, q_s, t_s = refs
    chunks, sheets, rows, _ = c_ref.shape
    lines = chunks * sheets
    steps = rows // SUBLANES
    plane = source_plane(loc, energy, rows, chunks * LANES, plate)

    lane = lax.broadcasted_iota(jnp.int32, (SUBLANES, LANES), 1)
    is_first, is_last = lane == 0, lane == LANES - 1
    for r in range(steps):
        at = slice(r * SUBLANES, (r + 1) * SUBLANES)
        before_t, before_c = None, None
        for z in range(sheets):
            ts = [t_ref[z, at, part_of(y)] for y in range(chunks)]
            cs = [half_conduct(b_ref[z, at, part_of(y)], ts[y]) for y in range(chunks)]
            t_turned = [pltpu.roll(v, LANES - 1, 1) for v in ts]
            c_turned = [pltpu.roll(v, LANES - 1, 1) for v in cs]
            flux = []
            for y in range(chunks):
                if y < chunks - 1:
                    t_next = jnp.where(is_last, t_turned[y + 1], t_turned[y])
                    c_next = jnp.where(is_last, c_turned[y + 1], c_turned[y])
                    flux.append((cs[y] + c_next) * (t_next - ts[y]))
                else:
                    inside = (cs[y] + c_turned[y]) * (t_turned[y] - ts[y])
                    flux.append(jnp.where(is_last, 0.0, inside))
            turned = [pltpu.roll(v, 1, 1) for v in flux]
            for y in range(chunks):
                from_low = jnp.where(is_first, turned[y - 1] if y else 0.0, turned[y])
                total = ts[y] + (flux[y] - from_low)
                if z == 0:
                    total = total + plane[at, part_of(y)]
                else:
                    across = (before_c[y] + cs[y]) * (ts[y] - before_t[y])
                    total = total - across
                    total_ref[y, z - 1, at, :] += across
                total_ref[y, z, at, :] = total
                c_ref[y, z, at, :] = cs[y]
                t_s[y, z, at, :] = ts[y]
            before_t, before_c = ts, cs

    at = 0
    for n, members in enumerate(line_groups(chunks, sheets)):

        def cond(k):
            return jnp.stack([c_ref[y, z, pl.ds(k, SUBLANES, stride=steps), :] for y, z in members], 0)

        def keep(k, w, inv, p):
            w_ref[k, at : at + len(members)] = w
            i_ref[k, at : at + len(members)] = inv
            p_ref[k, at : at + len(members)] = p

        block = factor(cond, steps, keep)
        for i, q in enumerate(COEFS):
            for j in range(len(members)):
                first = (at + j) * SUBLANES
                q_s[i, first : first + SUBLANES, :] = block[q][j]
        if n > 0:
            x_eliminate(
                lambda y, z: total_ref.at[y, z], members, at, w_ref, i_ref, p_ref, h_ref,
                at - 2 * sheets, ends_ref,
            )
        for k in range(steps):
            for i, (y, z) in enumerate(members):
                t_out[k, at + i] = t_s[y, z, pl.ds(k, SUBLANES, stride=steps), :]
        at += len(members)

    segments = [
        {q: q_s[n, pl.ds(s, lines, stride=SUBLANES), :] for n, q in enumerate(COEFS)}
        for s in range(SUBLANES)
    ]
    whole, levels = tree(segments, join_coefs)
    for (offset, _), level in zip(node_offsets(SUBLANES), levels):
        for n, values in enumerate(level):
            for i in range(3):
                links[offset + n, i] = values[i]
    for n, q in enumerate(COEFS):
        view[n] = whole[q]


def x_factor(loc, energy, t, b, plate, after):
    sheets, rows, columns = t.shape
    chunks = columns // LANES
    lines = chunks * sheets
    steps = rows // SUBLANES
    field = shape_of(chunks, sheets, rows, LANES)
    stored = shape_of(steps, lines, SUBLANES, LANES)
    return pl.pallas_call(
        functools.partial(x_factor_kernel, plate),
        in_specs=[IN_VMEM] * 4 + [ANYWHERE],
        out_shape=[
            field,
            field,
            stored,
            stored,
            stored,
            shape_of(SUBLANES - 1, 3, lines, LANES),
            shape_of(len(COEFS), lines, LANES),
            shape_of(steps, max(1, lines - 2 * sheets), SUBLANES, LANES),
            shape_of(2, lines * SUBLANES, LANES),
            stored,
        ],
        scratch_shapes=[
            pltpu.VMEM((len(COEFS), lines * SUBLANES, LANES), F32),
            pltpu.VMEM((chunks, sheets, rows, LANES), F32),
        ],
        compiler_params=params(),
        cost_estimate=pl.CostEstimate(flops=40 * t.size, bytes_accessed=28 * t.size, transcendentals=0),
    )(loc, energy, t, b, after)


def x_target_kernel(own_cells, t_ref, total_ref, near_ref, far_ref, *refs):
    w_ref, i_ref, p_ref, links, view, ends_ref, h_ref, own, send, e_s, q_s = refs
    chunks, sheets, rows, _ = total_ref.shape
    lines = chunks * sheets

    lane = lax.broadcasted_iota(jnp.int32, (rows, LANES), 1)
    side = 2 * sheets
    place = lax.axis_index("gy")
    inner = (place > 0) & (place < lax.axis_size("gy") - 1)
    near, far = near_ref[...], jnp.where(inner, far_ref[...], 0.0)
    before = unfold(jnp.where(is_odd("gy"), near, far), 2 * side, rows)
    after = unfold(jnp.where(is_odd("gy"), far, near), 2 * side, rows)
    beyond = jnp.where(lane < side, pltpu.roll(before, LANES - side, 1), pltpu.roll(after, side, 1))
    mine = unfold(own_cells[...], 2 * side, rows)
    face = jnp.where(beyond > 0.0, mine + beyond, 0.0)
    flux = pltpu.roll(face, LANES - sheets, 1) * (beyond - mine)
    for n, (y, edge) in enumerate(((0, 0), (chunks - 1, LANES - 1))):
        for z in range(sheets):
            at = n * side + z
            e_s[n, z] = total_ref[y, z] + jnp.where(lane == edge, flux[:, at : at + 1], 0.0)

    members = line_groups(chunks, sheets)[0]
    x_eliminate(
        lambda y, z: e_s.at[0 if y == 0 else 1, z], members, 0, w_ref, i_ref, p_ref, h_ref, 0, q_s
    )
    split = len(members)
    items = [
        tuple(
            jnp.concatenate(
                [
                    q_s[q, pl.ds(s, split, stride=SUBLANES), :],
                    ends_ref[q, pl.ds(split * SUBLANES + s, lines - split, stride=SUBLANES), :],
                ],
                0,
            )
            for q in range(2)
        )
        for s in range(SUBLANES)
    ]
    for offset, count in node_offsets(SUBLANES):
        joined = []
        for n in range(count):
            ties = tuple(links[offset + n, i] for i in range(3))
            both, flux = join_targets(items[2 * n], items[2 * n + 1], ties)
            own[offset + n] = flux
            joined.append(both)
        items = joined
    for n, q in enumerate(COEFS):
        send[q] = view[n]
    send[FIRST], send[LAST] = items[0]


def x_target(own_cells, t, total, near, far, w, inv, p, links, view, ends):
    chunks, sheets, rows, _ = total.shape
    lines = chunks * sheets
    steps = rows // SUBLANES
    return pl.pallas_call(
        x_target_kernel,
        out_shape=[
            shape_of(steps, 2 * sheets, SUBLANES, LANES),
            shape_of(SUBLANES - 1, lines, LANES),
            shape_of(7, lines, LANES),
        ],
        scratch_shapes=[
            pltpu.VMEM((2, sheets, rows, LANES), F32),
            pltpu.VMEM((2, 2 * sheets * SUBLANES, LANES), F32),
        ],
        compiler_params=params(),
    )(own_cells, t, total, near, far, w, inv, p, links, view, ends)


def stages_of(axis):
    return lax.axis_size(axis).bit_length() - 1


def swap(value, axis, flip):
    count = lax.axis_size(axis)
    return lax.ppermute(value, axis, [(i, i ^ flip) for i in range(count)])


def on_right(axis, stage):
    return (lax.axis_index(axis) >> stage) % 2 == 1


def toward(right, block):
    return (
        jnp.where(right, block[R00], block[RLL]),
        jnp.where(right, block[FIRST], block[LAST]),
        jnp.where(right, block[C0], block[CL]),
    )


def join(a, b):
    joined, ties = join_coefs(a, b)
    (joined[FIRST], joined[LAST]), flux = join_targets((a[FIRST], a[LAST]), (b[FIRST], b[LAST]), ties)
    return joined, (flux, ties[1], ties[2])


def ordered(right, own, other):
    first = [jnp.where(right, theirs, mine) for mine, theirs in zip(own, other)]
    second = [jnp.where(right, mine, theirs) for mine, theirs in zip(own, other)]
    return first, second


def join_kernel(axis, stage, width, last, *refs):
    count = 1 << width
    blocks = [[refs[i][q] for q in range(7)] for i in range(count)]
    send = refs[-1 - width]
    links = refs[-width:]
    for bit in range(width):
        right = on_right(axis, stage + bit)
        for i in range(count):
            if not i >> bit & 1:
                j = i | 1 << bit
                blocks[i], blocks[j] = ordered(right, blocks[i], blocks[j])
    for bit in range(width):
        pairs = [join(blocks[i], blocks[i + 1]) for i in range(0, len(blocks), 2)]
        blocks = [p[0] for p in pairs]
        ties = [p[1] for p in pairs]
        for upper in range(bit + 1, width):
            right = on_right(axis, stage + upper)
            ties = [
                tuple(jnp.where(right, v, u) for u, v in zip(ties[i], ties[i + 1]))
                for i in range(0, len(ties), 2)
            ]
        for i in range(3):
            links[bit][i] = ties[0][i]
    (whole,) = blocks
    if last:
        for n, value in enumerate(toward(on_right(axis, stage + width), whole)):
            send[n] = value
    else:
        for q in range(7):
            send[q] = whole[q]


def join_stage(own, got, axis, stage, width, last, after):
    lines = own.shape[1]
    return pl.pallas_call(
        functools.partial(join_kernel, axis, stage, width, last),
        in_specs=[IN_VMEM] * (1 + len(got)) + [ANYWHERE] * len(after),
        out_shape=[shape_of(3 if last else 7, lines, LANES)] + [shape_of(3, lines, LANES)] * width,
        compiler_params=params(),
    )(own, *got, *after)


def gather_line(view, axis, widest=1, meanwhile=(), one_core=False):
    stages = stages_of(axis)
    links, stage = [], 0
    while stage < stages - 1:
        width = min(widest, stages - 1 - stage)
        got = [swap(view, axis, flip << stage) for flip in range(1, 1 << width)]
        last = stage + width == stages - 1
        view, *ties = join_stage(view, got, axis, stage, width, last, meanwhile)
        links += ties
        stage += width
        meanwhile = ()
    if one_core and stage:
        pairs = [(i, i ^ 1 << stage if i % 2 else i) for i in range(1 << stages)]
        got = lax.ppermute(view, axis, pairs)
        return view, (got, swap(got, axis, 1)), links
    return view, swap(view, axis, 1 << stage), links


def top_flux(axis, stages, own, got):
    right = on_right(axis, stages - 1)
    face = own[2] + got[2]
    jump = jnp.where(right, own[1] - got[1], got[1] - own[1])
    return jump * face * inverse(1.0 + face * (own[0] + got[0]))


def block_ends(axis, stages, links):
    shape = links[0].shape[1:] if links else None
    right = on_right(axis, stages - 1)
    zero = jnp.zeros(shape, F32)
    low, high = zero, zero
    unit_low = zero + jnp.where(right, -1.0, 0.0)
    unit_high = zero + jnp.where(right, 0.0, 1.0)
    for stage in range(stages - 2, -1, -1):
        tie = links[stage]
        right = on_right(axis, stage)
        flux = between(tie[0], tie[1], tie[2], low, high)
        unit = between(0.0, tie[1], tie[2], unit_low, unit_high)
        low, high = jnp.where(right, -flux, low), jnp.where(right, high, flux)
        unit_low, unit_high = jnp.where(right, -unit, unit_low), jnp.where(right, unit_high, unit)
    return (low, high), (unit_low, unit_high)


def natural(index, parts):
    span = SUBLANES * parts
    local = index % span
    return index - local + local % SUBLANES * parts + local // SUBLANES


def turn_matrix(shape, from_natural, parts):
    row = lax.broadcasted_iota(jnp.int32, shape, 0)
    column = lax.broadcasted_iota(jnp.int32, shape, 1) % LANES
    hit = natural(row, parts) == column if from_natural else row == natural(column, parts)
    return jnp.where(hit, 1.0, 0.0).astype(jnp.bfloat16)


def turned(matrix, field):
    high = field.astype(jnp.bfloat16)
    low = (field - high.astype(F32)).astype(jnp.bfloat16)
    both = jnp.concatenate([high, low], 1)
    return lax.dot_general(
        matrix, both, (((1,), (1,)), ((), ())), preferred_element_type=F32
    )


def y_factor_kernel(c_ref, after, w_ref, i_ref, p_ref, inner, outer, view, to_y, to_x, c_s, q_s, r_s):
    chunks, sheets, rows, _ = c_ref.shape
    each = LANES // rows
    pairs = sheets // each
    x_steps = rows // SUBLANES
    steps = LANES // SUBLANES
    to_y[...] = turn_matrix(to_y.shape, True, steps)
    to_x[...] = turn_matrix(to_x.shape, False, x_steps)
    for m in range(pairs):
        for y in range(chunks):
            block = jnp.concatenate(
                [
                    c_ref[y, m * each + i, pl.ds(k, SUBLANES, stride=x_steps), :]
                    for i in range(each)
                    for k in range(x_steps)
                ],
                0,
            )
            c_s[m, part_of(y), :] = block.T

    members = [(y, m) for y in range(chunks) for m in range(pairs)]
    lines = len(members)

    def cond(k):
        return jnp.stack([c_s[m, pl.ds(y * LANES + k, SUBLANES, stride=steps), :] for y, m in members], 0)

    def keep(k, w, inv, p):
        w_ref[k] = w
        i_ref[k] = inv
        p_ref[k] = p

    block = factor(cond, steps, keep)
    for n, q in enumerate(COEFS):
        for i in range(lines):
            q_s[n, i * SUBLANES : (i + 1) * SUBLANES, :] = block[q][i]
    segments = [
        {q: q_s[n, pl.ds(s, lines, stride=SUBLANES), :] for n, q in enumerate(COEFS)}
        for s in range(SUBLANES)
    ]
    whole, levels = tree(segments, join_coefs)
    for (offset, _), level in zip(node_offsets(SUBLANES), levels):
        for n, values in enumerate(level):
            for i in range(3):
                inner[offset + n, i] = values[i]
    for n, q in enumerate(COEFS):
        r_s[n] = whole[q]
    parts = [
        {q: r_s[n, y * pairs : (y + 1) * pairs, :] for n, q in enumerate(COEFS)} for y in range(chunks)
    ]
    whole, levels = tree(parts, join_coefs)
    for (offset, _), level in zip(node_offsets(chunks), levels):
        for n, values in enumerate(level):
            for i in range(3):
                outer[offset + n, i] = values[i]
    for n, q in enumerate(COEFS):
        view[n] = whole[q]


def y_factor(c, after):
    chunks, sheets, rows, _ = c.shape
    pairs = sheets * rows // LANES
    lines = chunks * pairs
    stored = shape_of(LANES // SUBLANES, lines, SUBLANES, LANES)
    matrix = jax.ShapeDtypeStruct((LANES, 2 * LANES), jnp.bfloat16)
    return pl.pallas_call(
        y_factor_kernel,
        in_specs=[IN_VMEM, ANYWHERE],
        out_shape=[
            stored,
            stored,
            stored,
            shape_of(SUBLANES - 1, 3, lines, LANES),
            shape_of(chunks - 1, 3, pairs, LANES),
            shape_of(len(COEFS), pairs, LANES),
            matrix,
            matrix,
        ],
        scratch_shapes=[
            pltpu.VMEM((pairs, chunks * LANES, LANES), F32),
            pltpu.VMEM((len(COEFS), lines * SUBLANES, LANES), F32),
            pltpu.VMEM((len(COEFS), lines, LANES), F32),
        ],
        compiler_params=params(),
        cost_estimate=pl.CostEstimate(flops=20 * c.size, bytes_accessed=16 * c.size, transcendentals=0),
    )(c, after)


def z_factor_kernel(c_ref, after, w_ref, i_ref):
    sheets = c_ref.shape[1]
    ground = 1.0
    for z in range(sheets - 1):
        face = c_ref[:, z] + c_ref[:, z + 1]
        inv = inverse(ground + face)
        w = face * inv
        i_ref[z] = inv
        w_ref[z] = w
        ground = 1.0 + w * ground
    i_ref[sheets - 1] = inverse(ground)


def z_factor(c, after):
    chunks, sheets, rows, _ = c.shape
    return pl.pallas_call(
        z_factor_kernel,
        in_specs=[IN_VMEM, ANYWHERE],
        out_shape=[
            shape_of(sheets - 1, chunks, rows, LANES),
            shape_of(sheets, chunks, rows, LANES),
        ],
        compiler_params=params(),
        cost_estimate=pl.CostEstimate(flops=10 * c.size, bytes_accessed=12 * c.size, transcendentals=0),
    )(c, after)


def join_tree(items, links, own):
    for offset, count in node_offsets(len(items)):
        joined = []
        for n in range(count):
            tie = tuple(links[offset + n, i] for i in range(3))
            both, flux = join_targets(items[2 * n], items[2 * n + 1], tie)
            own[offset + n] = flux
            joined.append(both)
        items = joined
    return items[0]


def tree_ends(leaves, links, own, low, high):
    levels = [
        [(own(offset + n), links[offset + n, 1], links[offset + n, 2]) for n in range(count)]
        for offset, count in node_offsets(leaves)
    ]
    return descend(levels, low, high)


def nothing(node):
    return 0.0


def y_prepare_kernel(stages, *refs):
    ties = refs[: stages - 1]
    xw, xh, xm, xp, x_links, x_own, t_ref, to_y = refs[stages - 1 : stages + 7]
    base, response, f_s, g_s = refs[stages + 7 :]
    x_steps, lines = xw.shape[:2]
    chunks = base.shape[0]
    sheets = lines // chunks
    rows = x_steps * SUBLANES

    ends, units = block_ends("gx", stages, ties)
    for n, (own, (low, high)) in enumerate(((lambda i: x_own[i], ends), (nothing, units))):
        for s, pair in enumerate(tree_ends(SUBLANES, x_links, own, low, high)):
            for i in range(2):
                f_s[n, i, pl.ds(s, lines, stride=SUBLANES), :] = pair[i]
    first = 0
    for n, members in enumerate(line_groups(chunks, sheets)):
        at = slice(first, first + len(members))
        h_ref_of, h_at = (xh, at) if n == 0 else (xm, slice(first - 2 * sheets, at.stop - 2 * sheets))
        (low, value), (unit_low, unit) = (
            [
                jnp.stack(
                    [f_s[q, i, j * SUBLANES : (j + 1) * SUBLANES, :] for j in range(at.start, at.stop)], 0
                )
                for i in range(2)
            ]
            for q in range(2)
        )
        for k in range(x_steps - 1, -1, -1):
            w, p = xw[k, at], xp[k, at]
            value = w * value + (h_ref_of[k, h_at] + p * low)
            unit = w * unit + p * unit_low
            field = value - t_ref[k, at]
            for j, (y, z) in enumerate(members):
                place = z * rows + k * SUBLANES
                g_s[0, y, place : place + SUBLANES, :] = field[j]
                g_s[1, y, place : place + SUBLANES, :] = unit[j]
        first = at.stop

    for y in range(chunks):
        base[y] = turned(to_y[...], g_s[0, y])
        response[y] = turned(to_y[...], g_s[1, y])


def y_prepare(ties, xw, xh, xm, xp, x_links, x_own, t, to_y, chunks):
    x_steps, lines = xw.shape[:2]
    width = lines // chunks * x_steps * SUBLANES
    field = shape_of(chunks, LANES, width)
    return pl.pallas_call(
        functools.partial(y_prepare_kernel, len(ties) + 1),
        out_shape=[field, field],
        scratch_shapes=[
            pltpu.VMEM((2, 2, lines * SUBLANES, LANES), F32),
            pltpu.VMEM((2, chunks, width, LANES), F32),
        ],
        compiler_params=params(),
        cost_estimate=pl.CostEstimate(flops=8 * t.size, bytes_accessed=16 * t.size, transcendentals=0),
    )(*ties, xw, xh, xm, xp, x_links, x_own, t, to_y)


def y_target_kernel(stages, own, got, base, response, yw, yi, yp, inner, outer, view, to_y, *refs):
    h_ref, inner_own, outer_own, send, q_s, r_s = refs
    chunks, _, width = base.shape
    pairs = width // LANES
    sheets = own.shape[1] // chunks
    rows = width // sheets
    steps = yw.shape[0]

    flux = top_flux("gx", stages, own, got)
    line_of = {member: n for n, member in enumerate(sum(line_groups(chunks, sheets), []))}
    fields = []
    for y in range(chunks):
        spread = jnp.concatenate(
            [
                jnp.broadcast_to(flux[line_of[y, z] : line_of[y, z] + 1, :], (rows, LANES))
                for z in range(sheets)
            ],
            0,
        )
        fields.append(base[y] + response[y] * turned(to_y[...], spread))

    def target(k):
        at = slice(k * SUBLANES, (k + 1) * SUBLANES)
        return jnp.stack(
            [fields[y][at, m * LANES : (m + 1) * LANES] for y in range(chunks) for m in range(pairs)], 0
        )

    def keep(k, h):
        h_ref[k] = h

    ends = eliminate(target, steps, lambda k: yw[k], lambda k: yi[k], lambda k: yp[k], keep)
    for q in range(2):
        for i in range(chunks * pairs):
            q_s[q, i * SUBLANES : (i + 1) * SUBLANES, :] = ends[q][i]
    items = [
        tuple(q_s[q, pl.ds(s, chunks * pairs, stride=SUBLANES), :] for q in range(2))
        for s in range(SUBLANES)
    ]
    r_s[0], r_s[1] = join_tree(items, inner, inner_own)
    items = [tuple(r_s[q, y * pairs : (y + 1) * pairs, :] for q in range(2)) for y in range(chunks)]
    for n, q in enumerate(COEFS):
        send[q] = view[n]
    send[FIRST], send[LAST] = join_tree(items, outer, outer_own)


def y_target(own, got, base, response, yw, yi, yp, inner, outer, view, to_y):
    y_lines = yw.shape[1]
    pairs = view.shape[1]
    chunks = y_lines // pairs
    return pl.pallas_call(
        functools.partial(y_target_kernel, stages_of("gx")),
        out_shape=[
            shape_of(*yw.shape),
            shape_of(SUBLANES - 1, y_lines, LANES),
            shape_of(chunks - 1, pairs, LANES),
            shape_of(7, pairs, LANES),
        ],
        scratch_shapes=[
            pltpu.VMEM((2, y_lines * SUBLANES, LANES), F32),
            pltpu.VMEM((2, y_lines, LANES), F32),
        ],
        compiler_params=params(),
    )(own, got, base, response, yw, yi, yp, inner, outer, view, to_y)


def z_solve(zw, zi, field, at, keep):
    sheets = zi.shape[0]
    rhs, kept = None, []
    for z in range(sheets):
        rhs = field(z) if z == 0 else field(z) + zw[z - 1, at] * rhs
        kept.append(rhs * zi[z, at])
    value = kept[-1]
    keep(sheets - 1, value)
    for z in range(sheets - 2, -1, -1):
        value = zw[z, at] * value + kept[z]
        keep(z, value)


def finish_prepare_kernel(stages, *refs):
    ties = refs[: stages - 1]
    yw, yh, yp, inner, inner_own, outer, outer_own, zw, zi, t_ref, to_x = refs[stages - 1 : stages + 10]
    base, response, r_s, e_s, u_s = refs[stages + 10 :]
    chunks, sheets, rows, _ = base.shape
    each = LANES // rows
    pairs = sheets // each
    steps = yw.shape[0]
    lines = chunks * pairs

    ends, units = block_ends("gy", stages, ties)
    both = (
        (lambda i: outer_own[i], lambda i: inner_own[i], ends),
        (nothing, nothing, units),
    )
    for n, (upper, lower, (low, high)) in enumerate(both):
        for y, pair in enumerate(tree_ends(chunks, outer, upper, low, high)):
            for i in range(2):
                r_s[n, i, y * pairs : (y + 1) * pairs, :] = pair[i]
        for s, pair in enumerate(tree_ends(SUBLANES, inner, lower, r_s[n, 0], r_s[n, 1])):
            for i in range(2):
                e_s[n, i, pl.ds(s, lines, stride=SUBLANES), :] = pair[i]
    (low, value), (unit_low, unit) = (
        [
            jnp.stack([e_s[q, i, n * SUBLANES : (n + 1) * SUBLANES, :] for n in range(lines)], 0)
            for i in range(2)
        ]
        for q in range(2)
    )
    for k in range(steps - 1, -1, -1):
        w, p = yw[k], yp[k]
        value = w * value + (yh[k] + p * low)
        unit = w * unit + p * unit_low
        for y in range(chunks):
            for m in range(pairs):
                place = pl.ds(y * LANES + k, SUBLANES, stride=steps)
                u_s[0, m, place, :] = value[y * pairs + m]
                u_s[1, m, place, :] = unit[y * pairs + m]

    for y in range(chunks):
        part = part_of(y)
        fields = [turned(to_x[...], u_s[0, m, part, :]) for m in range(pairs)]

        def field(z):
            at = z % each * rows
            return fields[z // each][at : at + rows, :]

        def keep(z, value):
            base[y, z] = t_ref[z, :, part] + value

        z_solve(zw, zi, field, y, keep)
        for m in range(pairs):
            units = turned(to_x[...], u_s[1, m, part, :])
            for i in range(each):
                response[y, m * each + i] = units[i * rows : (i + 1) * rows, :]


def finish_prepare(ties, yw, yh, yp, inner, inner_own, outer, outer_own, zw, zi, t, to_x):
    sheets, rows, columns = t.shape
    chunks = columns // LANES
    pairs = sheets * rows // LANES
    lines = chunks * pairs
    field = shape_of(chunks, sheets, rows, LANES)
    return pl.pallas_call(
        functools.partial(finish_prepare_kernel, len(ties) + 1),
        out_shape=[field, field],
        scratch_shapes=[
            pltpu.VMEM((2, 2, lines, LANES), F32),
            pltpu.VMEM((2, 2, lines * SUBLANES, LANES), F32),
            pltpu.VMEM((2, pairs, columns, LANES), F32),
        ],
        compiler_params=params(),
        cost_estimate=pl.CostEstimate(flops=12 * t.size, bytes_accessed=20 * t.size, transcendentals=0),
    )(*ties, yw, yh, yp, inner, inner_own, outer, outer_own, zw, zi, t, to_x)


def finish_kernel(stages, own, *refs):
    *parts, base, response, zw, zi, to_x, out, o_s, sems = refs
    chunks, sheets, rows, _ = base.shape
    each = LANES // rows
    pairs = sheets // each
    copies, _, wide = o_s.shape

    got = [jnp.where(is_odd("gy"), parts[0][q], parts[-1][q]) for q in range(3)]
    flux = top_flux("gy", stages, own, got)
    spread = [
        turned(to_x[...], jnp.broadcast_to(flux[m : m + 1, :], (LANES, LANES))) for m in range(pairs)
    ]
    started = []
    for n in range(copies):
        for y in range(n * chunks // copies, (n + 1) * chunks // copies):
            part = part_of(y - n * chunks // copies)

            def field(z):
                at = z % each * rows
                return response[y, z] * spread[z // each][at : at + rows, :]

            def keep(z, value):
                o_s[n, z * rows : (z + 1) * rows, part] = base[y, z] + value

            z_solve(zw, zi, field, y, keep)
        copy = pltpu.make_async_copy(o_s.at[n], out.at[:, pl.ds(n * wide, wide)], sems.at[n])
        copy.start()
        started.append(copy)
    for copy in started:
        copy.wait()


def finish(own, got, base, response, zw, zi, to_x):
    chunks, sheets, rows, _ = base.shape
    copies = chunks
    return pl.pallas_call(
        functools.partial(finish_kernel, stages_of("gy")),
        out_shape=shape_of(sheets * rows, chunks * LANES),
        out_specs=ANYWHERE,
        scratch_shapes=[
            pltpu.VMEM((copies, sheets * rows, chunks * LANES // copies), F32),
            pltpu.SemaphoreType.DMA((copies,)),
        ],
        compiler_params=params(),
    )(own, *got, base, response, zw, zi, to_x).reshape(sheets, rows, chunks * LANES)


def per_device(temperature, base, locations, energy):
    columns = temperature.shape[2]
    gy = lax.axis_size("gy")
    packed = edges(temperature, base)
    near = swap(packed, "gy", 1)
    far = lax.ppermute(packed, "gy", [(i, ((i + 1) % gy ^ 1) - 1 if i else gy - 1) for i in range(gy)])
    t, b, loc, heat = load((temperature, base, locations[None], energy[None]), packed)
    c, total, xw, xi, xp, x_links, x_view, xm, ends, t_steps = x_factor(loc, heat, t, b, columns * gy, packed)
    xh, x_own, view = x_target(packed, t, total, near, far, xw, xi, xp, x_links, x_view, ends)
    yw, yi, yp, inner, outer, y_view, to_y, to_x = y_factor(c, x_view)
    zw, zi = z_factor(c, view)
    own, got, ties = gather_line(view, "gx", 2, (y_view, zw))
    base, response = y_prepare(
        ties, xw, xh, xm, xp, x_links, x_own, t_steps, to_y, columns // LANES
    )
    yh, inner_own, outer_own, view = y_target(
        own, got, base, response, yw, yi, yp, inner, outer, y_view, to_y
    )
    own, got, ties = gather_line(view, "gy", one_core=True)
    base, response = finish_prepare(
        ties, yw, yh, yp, inner, inner_own, outer, outer_own, zw, zi, t, to_x
    )
    return finish(own, got, base, response, zw, zi, to_x)


def solution(mesh):
    in_specs = (P(None, "gx", "gy"), P(None, "gx", "gy"), P(), P())
    out_specs = P(None, "gx", "gy")
    return jax.shard_map(
        per_device, mesh=mesh, in_specs=in_specs, out_specs=out_specs, check_vma=False
    )
```

```python
import functools

import jax
import jax.numpy as jnp
from jax import lax
from jax.experimental import pallas as pl
from jax.experimental.pallas import tpu as pltpu
from jax.sharding import PartitionSpec as P

RATE = 2000.0
THERMAL_GROWTH = 0.8
LANES = 128
SUBLANES = 8
F32 = jnp.float32
MIB = 1024 * 1024
ANYWHERE = pl.BlockSpec(memory_space=pl.ANY)
IN_HBM = pl.BlockSpec(memory_space=pltpu.HBM)
IN_VMEM = pl.BlockSpec(memory_space=pltpu.VMEM)

R00, R0L, RLL, FIRST, LAST, C0, CL = range(7)
COEFS = (R00, R0L, RLL, C0, CL)


def params(limit=40):
    return pltpu.CompilerParams(vmem_limit_bytes=limit * MIB)


def shape_of(*sizes):
    return jax.ShapeDtypeStruct(sizes, F32)


def half_conduct(base, temperature):
    return base * (0.5 * RATE + (0.5 * RATE * THERMAL_GROWTH) * temperature)


def inverse(x):
    guess = pl.reciprocal(x, approx=True)
    return guess * (2.0 - x * guess)


def join_coefs(a, b):
    face = a[CL] + b[C0]
    inv = face * inverse(1.0 + face * (a[RLL] + b[R00]))
    left = a[R0L] * inv
    right = b[R0L] * inv
    joined = {
        R00: a[R00] - left * a[R0L],
        R0L: left * b[R0L],
        RLL: b[RLL] - right * b[R0L],
        C0: a[C0],
        CL: b[CL],
    }
    return joined, (inv, right, left)


def join_targets(a, b, links):
    inv, right, left = links
    jump = b[0] - a[1]
    return (a[0] + left * jump, b[1] - right * jump), jump * inv


def between(own, right, left, low, high):
    return own + right * high - left * low


def tree(items, join):
    levels = []
    while len(items) > 1:
        pairs = [join(items[i], items[i + 1]) for i in range(0, len(items), 2)]
        items = [p[0] for p in pairs]
        levels.append([p[1] for p in pairs])
    return items[0], levels


def descend(levels, low, high):
    ends = [(low, high)]
    for level in reversed(levels):
        below = []
        for (lo, hi), (own, right, left) in zip(ends, level):
            flux = between(own, right, left, lo, hi)
            below += [(lo, flux), (-flux, hi)]
        ends = below
    return ends


def node_offsets(leaves):
    offsets, at, count = [], 0, leaves // 2
    while count:
        offsets.append((at, count))
        at += count
        count //= 2
    return offsets


def factor(cond, steps, keep):
    here = cond(0)
    c_first = here
    one = jnp.ones_like(here)
    ground, path, first_first = one, one, None
    for k in range(steps - 1):
        following = cond(k + 1)
        face = here + following
        inv = inverse(ground + face)
        w = face * inv
        p = path * inv
        keep(k, w, inv, p)
        step = path * p
        first_first = step if first_first is None else first_first + step
        path = path * w
        ground = 1.0 + w * ground
        here = following
    inv = inverse(ground)
    p = path * inv
    keep(steps - 1, inv, inv, p)
    return {R00: first_first + path * p, R0L: p, RLL: inv, C0: c_first, CL: here}


def eliminate(target, steps, w, inv, p, keep):
    rhs = target(0)
    first = None
    for k in range(steps):
        h = rhs * inv(k)
        keep(k, h)
        step = rhs * p(k)
        first = step if first is None else first + step
        if k < steps - 1:
            rhs = target(k + 1) + w(k) * rhs
    return first, h


def is_odd(axis):
    return lax.axis_index(axis) % 2 == 1


def fold(cells, used):
    total = cells[:SUBLANES]
    lane = lax.broadcasted_iota(jnp.int32, total.shape, 1)
    for n in range(1, cells.shape[0] // SUBLANES):
        part = pltpu.roll(cells[n * SUBLANES : (n + 1) * SUBLANES], n * used, 1)
        total = jnp.where(lane // used == n, part, total)
    return total


def unfold(cells, used, rows):
    parts = [cells] + [
        pltpu.roll(cells, LANES - n * used, 1) for n in range(1, rows // SUBLANES)
    ]
    return jnp.concatenate(parts, 0)


def load_kernel(t_hbm, b_hbm, loc_hbm, energy_hbm, t_out, b_out, loc, energy, packed, sems):
    sheets, rows, columns = t_hbm.shape
    parts = [(0, LANES), (columns - LANES, LANES), (LANES, columns - 2 * LANES)]
    copies = []
    for n, (start, size) in enumerate(parts):
        part = pl.ds(start, size)
        for i, (src, dst) in enumerate(((t_hbm, t_out), (b_hbm, b_out))):
            copies.append(
                pltpu.make_async_copy(src.at[:, :, part], dst.at[:, :, part], sems.at[i, n])
            )
    copies.append(pltpu.make_async_copy(loc_hbm, loc, sems.at[2, 0]))
    copies.append(pltpu.make_async_copy(energy_hbm, energy, sems.at[2, 1]))
    for copy in copies:
        copy.start()
    lane = lax.broadcasted_iota(jnp.int32, (rows, LANES), 1)
    total = jnp.zeros((rows, LANES), F32)
    for side, source in enumerate((0, LANES - 1)):
        for copy in copies[2 * side : 2 * side + 2]:
            copy.wait()
        part = slice(parts[side][0], parts[side][0] + LANES)
        for z in range(sheets):
            t = t_out[z, :, part]
            c = half_conduct(b_out[z, :, part], t)
            place = 2 * sheets * side + z
            total = jnp.where(lane == place, t[:, source : source + 1], total)
            total = jnp.where(lane == place + sheets, c[:, source : source + 1], total)
    packed[...] = fold(total, 4 * sheets)
    for copy in copies[4:]:
        copy.wait()


def load(temperature, base, locations, energy):
    sheets, rows, columns = temperature.shape
    assert rows // SUBLANES * 4 * sheets <= LANES and columns > 2 * LANES
    operands = (temperature, base, locations, energy)
    return pl.pallas_call(
        load_kernel,
        in_specs=[IN_HBM] * 4,
        out_shape=[pltpu.VMEM(v.shape, v.dtype) for v in operands]
        + [pltpu.VMEM((SUBLANES, LANES), F32)],
        scratch_shapes=[pltpu.SemaphoreType.DMA((3, 3))],
        compiler_params=params(),
    )(*[pltpu.with_memory_space_constraint(v, pltpu.HBM) for v in operands])


def source_plane(loc, energy, rows, columns, plate):
    place = loc[...]
    count = place.shape[1]
    local_x = place // plate - lax.axis_index("gx") * rows
    local_y = place % plate - lax.axis_index("gy") * columns
    in_x = lax.broadcasted_iota(jnp.int32, (rows, count), 0) == local_x
    in_y = lax.broadcasted_iota(jnp.int32, (columns, count), 0) == local_y
    by_y = jnp.where(in_y, 1.0, 0.0).astype(jnp.bfloat16)
    left = energy[...]
    plane = None
    for _ in range(3):
        part = left.astype(jnp.bfloat16).astype(F32)
        left = left - part
        term = lax.dot_general(
            jnp.where(in_x, part, 0.0).astype(jnp.bfloat16),
            by_y,
            (((1,), (1,)), ((), ())),
            preferred_element_type=F32,
        )
        plane = term if plane is None else plane + term
    return plane


def part_of(y):
    return slice(y * LANES, (y + 1) * LANES)


def line_groups(chunks, sheets):
    order = [0, chunks - 1] + list(range(1, chunks - 1))
    return [[(y, z) for y in order[i : i + 2] for z in range(sheets)] for i in range(0, chunks, 2)]


def x_eliminate(field, members, first_line, w_ref, i_ref, p_ref, h_ref, h_line, q_s):
    steps = w_ref.shape[0]
    at = slice(first_line, first_line + len(members))
    kept_at = slice(h_line, h_line + len(members))

    def target(k):
        return jnp.stack([field(y, z)[pl.ds(k, SUBLANES, stride=steps), :] for y, z in members], 0)

    def keep(k, h):
        h_ref[k, kept_at] = h

    ends = eliminate(
        target, steps, lambda k: w_ref[k, at], lambda k: i_ref[k, at], lambda k: p_ref[k, at], keep
    )
    for q in range(2):
        for i in range(len(members)):
            first = (first_line + i) * SUBLANES
            q_s[q, first : first + SUBLANES, :] = ends[q][i]


def x_factor_kernel(plate, loc, energy, t_ref, b_ref, after, *refs):
    c_ref, total_ref, w_ref, i_ref, p_ref, links, view, h_ref, ends_ref, t_out, q_s, t_s = refs
    chunks, sheets, rows, _ = c_ref.shape
    lines = chunks * sheets
    steps = rows // SUBLANES
    plane = source_plane(loc, energy, rows, chunks * LANES, plate)

    lane = lax.broadcasted_iota(jnp.int32, (SUBLANES, LANES), 1)
    is_first, is_last = lane == 0, lane == LANES - 1
    for r in range(steps):
        at = slice(r * SUBLANES, (r + 1) * SUBLANES)
        before_t, before_c = None, None
        for z in range(sheets):
            ts = [t_ref[z, at, part_of(y)] for y in range(chunks)]
            cs = [half_conduct(b_ref[z, at, part_of(y)], ts[y]) for y in range(chunks)]
            t_turned = [pltpu.roll(v, LANES - 1, 1) for v in ts]
            c_turned = [pltpu.roll(v, LANES - 1, 1) for v in cs]
            flux = []
            for y in range(chunks):
                if y < chunks - 1:
                    t_next = jnp.where(is_last, t_turned[y + 1], t_turned[y])
                    c_next = jnp.where(is_last, c_turned[y + 1], c_turned[y])
                    flux.append((cs[y] + c_next) * (t_next - ts[y]))
                else:
                    inside = (cs[y] + c_turned[y]) * (t_turned[y] - ts[y])
                    flux.append(jnp.where(is_last, 0.0, inside))
            turned = [pltpu.roll(v, 1, 1) for v in flux]
            for y in range(chunks):
                from_low = jnp.where(is_first, turned[y - 1] if y else 0.0, turned[y])
                total = ts[y] + (flux[y] - from_low)
                if z == 0:
                    total = total + plane[at, part_of(y)]
                else:
                    across = (before_c[y] + cs[y]) * (ts[y] - before_t[y])
                    total = total - across
                    total_ref[y, z - 1, at, :] += across
                total_ref[y, z, at, :] = total
                c_ref[y, z, at, :] = cs[y]
                t_s[y, z, at, :] = ts[y]
            before_t, before_c = ts, cs

    at = 0
    for n, members in enumerate(line_groups(chunks, sheets)):

        def cond(k):
            return jnp.stack([c_ref[y, z, pl.ds(k, SUBLANES, stride=steps), :] for y, z in members], 0)

        def keep(k, w, inv, p):
            w_ref[k, at : at + len(members)] = w
            i_ref[k, at : at + len(members)] = inv
            p_ref[k, at : at + len(members)] = p

        block = factor(cond, steps, keep)
        for i, q in enumerate(COEFS):
            for j in range(len(members)):
                first = (at + j) * SUBLANES
                q_s[i, first : first + SUBLANES, :] = block[q][j]
        if n > 0:
            x_eliminate(
                lambda y, z: total_ref.at[y, z], members, at, w_ref, i_ref, p_ref, h_ref,
                at - 2 * sheets, ends_ref,
            )
        for k in range(steps):
            for i, (y, z) in enumerate(members):
                t_out[k, at + i] = t_s[y, z, pl.ds(k, SUBLANES, stride=steps), :]
        at += len(members)

    segments = [
        {q: q_s[n, pl.ds(s, lines, stride=SUBLANES), :] for n, q in enumerate(COEFS)}
        for s in range(SUBLANES)
    ]
    whole, levels = tree(segments, join_coefs)
    for (offset, _), level in zip(node_offsets(SUBLANES), levels):
        for n, values in enumerate(level):
            for i in range(3):
                links[offset + n, i] = values[i]
    for n, q in enumerate(COEFS):
        view[n] = whole[q]


def x_factor(loc, energy, t, b, plate, after):
    sheets, rows, columns = t.shape
    chunks = columns // LANES
    lines = chunks * sheets
    steps = rows // SUBLANES
    field = shape_of(chunks, sheets, rows, LANES)
    stored = shape_of(steps, lines, SUBLANES, LANES)
    return pl.pallas_call(
        functools.partial(x_factor_kernel, plate),
        in_specs=[IN_VMEM] * 4 + [ANYWHERE],
        out_shape=[
            field,
            field,
            stored,
            stored,
            stored,
            shape_of(SUBLANES - 1, 3, lines, LANES),
            shape_of(len(COEFS), lines, LANES),
            shape_of(steps, max(1, lines - 2 * sheets), SUBLANES, LANES),
            shape_of(2, lines * SUBLANES, LANES),
            stored,
        ],
        scratch_shapes=[
            pltpu.VMEM((len(COEFS), lines * SUBLANES, LANES), F32),
            pltpu.VMEM((chunks, sheets, rows, LANES), F32),
        ],
        compiler_params=params(),
        cost_estimate=pl.CostEstimate(flops=40 * t.size, bytes_accessed=28 * t.size, transcendentals=0),
    )(loc, energy, t, b, after)


def x_target_kernel(own_cells, t_ref, total_ref, near_ref, far_ref, *refs):
    w_ref, i_ref, p_ref, links, view, ends_ref, h_ref, own, send, e_s, q_s = refs
    chunks, sheets, rows, _ = total_ref.shape
    lines = chunks * sheets

    lane = lax.broadcasted_iota(jnp.int32, (rows, LANES), 1)
    side = 2 * sheets
    place = lax.axis_index("gy")
    inner = (place > 0) & (place < lax.axis_size("gy") - 1)
    near, far = near_ref[...], jnp.where(inner, far_ref[...], 0.0)
    before = unfold(jnp.where(is_odd("gy"), near, far), 2 * side, rows)
    after = unfold(jnp.where(is_odd("gy"), far, near), 2 * side, rows)
    beyond = jnp.where(lane < side, pltpu.roll(before, LANES - side, 1), pltpu.roll(after, side, 1))
    mine = unfold(own_cells[...], 2 * side, rows)
    face = jnp.where(beyond > 0.0, mine + beyond, 0.0)
    flux = pltpu.roll(face, LANES - sheets, 1) * (beyond - mine)
    for n, (y, edge) in enumerate(((0, 0), (chunks - 1, LANES - 1))):
        for z in range(sheets):
            at = n * side + z
            e_s[n, z] = total_ref[y, z] + jnp.where(lane == edge, flux[:, at : at + 1], 0.0)

    members = line_groups(chunks, sheets)[0]
    x_eliminate(
        lambda y, z: e_s.at[0 if y == 0 else 1, z], members, 0, w_ref, i_ref, p_ref, h_ref, 0, q_s
    )
    split = len(members)
    items = [
        tuple(
            jnp.concatenate(
                [
                    q_s[q, pl.ds(s, split, stride=SUBLANES), :],
                    ends_ref[q, pl.ds(split * SUBLANES + s, lines - split, stride=SUBLANES), :],
                ],
                0,
            )
            for q in range(2)
        )
        for s in range(SUBLANES)
    ]
    for offset, count in node_offsets(SUBLANES):
        joined = []
        for n in range(count):
            ties = tuple(links[offset + n, i] for i in range(3))
            both, flux = join_targets(items[2 * n], items[2 * n + 1], ties)
            own[offset + n] = flux
            joined.append(both)
        items = joined
    for n, q in enumerate(COEFS):
        send[q] = view[n]
    send[FIRST], send[LAST] = items[0]


def x_target(own_cells, t, total, near, far, w, inv, p, links, view, ends):
    chunks, sheets, rows, _ = total.shape
    lines = chunks * sheets
    steps = rows // SUBLANES
    return pl.pallas_call(
        x_target_kernel,
        out_shape=[
            shape_of(steps, 2 * sheets, SUBLANES, LANES),
            shape_of(SUBLANES - 1, lines, LANES),
            shape_of(7, lines, LANES),
        ],
        scratch_shapes=[
            pltpu.VMEM((2, sheets, rows, LANES), F32),
            pltpu.VMEM((2, 2 * sheets * SUBLANES, LANES), F32),
        ],
        compiler_params=params(),
    )(own_cells, t, total, near, far, w, inv, p, links, view, ends)


def stages_of(axis):
    return lax.axis_size(axis).bit_length() - 1


def swap(value, axis, flip):
    count = lax.axis_size(axis)
    return lax.ppermute(value, axis, [(i, i ^ flip) for i in range(count)])


def on_right(axis, stage):
    return (lax.axis_index(axis) >> stage) % 2 == 1


def toward(right, block):
    return (
        jnp.where(right, block[R00], block[RLL]),
        jnp.where(right, block[FIRST], block[LAST]),
        jnp.where(right, block[C0], block[CL]),
    )


def join(a, b):
    joined, ties = join_coefs(a, b)
    (joined[FIRST], joined[LAST]), flux = join_targets((a[FIRST], a[LAST]), (b[FIRST], b[LAST]), ties)
    return joined, (flux, ties[1], ties[2])


def ordered(right, own, other):
    first = [jnp.where(right, theirs, mine) for mine, theirs in zip(own, other)]
    second = [jnp.where(right, mine, theirs) for mine, theirs in zip(own, other)]
    return first, second


def join_kernel(axis, stage, width, last, *refs):
    count = 1 << width
    blocks = [[refs[i][q] for q in range(7)] for i in range(count)]
    send = refs[-1 - width]
    links = refs[-width:]
    for bit in range(width):
        right = on_right(axis, stage + bit)
        for i in range(count):
            if not i >> bit & 1:
                j = i | 1 << bit
                blocks[i], blocks[j] = ordered(right, blocks[i], blocks[j])
    for bit in range(width):
        pairs = [join(blocks[i], blocks[i + 1]) for i in range(0, len(blocks), 2)]
        blocks = [p[0] for p in pairs]
        ties = [p[1] for p in pairs]
        for upper in range(bit + 1, width):
            right = on_right(axis, stage + upper)
            ties = [
                tuple(jnp.where(right, v, u) for u, v in zip(ties[i], ties[i + 1]))
                for i in range(0, len(ties), 2)
            ]
        for i in range(3):
            links[bit][i] = ties[0][i]
    (whole,) = blocks
    if last:
        for n, value in enumerate(toward(on_right(axis, stage + width), whole)):
            send[n] = value
    else:
        for q in range(7):
            send[q] = whole[q]


def join_stage(own, got, axis, stage, width, last, after):
    lines = own.shape[1]
    return pl.pallas_call(
        functools.partial(join_kernel, axis, stage, width, last),
        in_specs=[IN_VMEM] * (1 + len(got)) + [ANYWHERE] * len(after),
        out_shape=[shape_of(3 if last else 7, lines, LANES)] + [shape_of(3, lines, LANES)] * width,
        compiler_params=params(),
    )(own, *got, *after)


def gather_line(view, axis, widest=1, meanwhile=()):
    stages = stages_of(axis)
    links, stage = [], 0
    while stage < stages - 1:
        width = min(widest, stages - 1 - stage)
        got = [swap(view, axis, flip << stage) for flip in range(1, 1 << width)]
        last = stage + width == stages - 1
        view, *ties = join_stage(view, got, axis, stage, width, last, meanwhile)
        links += ties
        stage += width
        meanwhile = ()
    return view, swap(view, axis, 1 << stage), links


def top_flux(axis, stages, own, got):
    right = on_right(axis, stages - 1)
    face = own[2] + got[2]
    jump = jnp.where(right, own[1] - got[1], got[1] - own[1])
    return jump * face * inverse(1.0 + face * (own[0] + got[0]))


def block_ends(axis, stages, links):
    shape = links[0].shape[1:] if links else None
    right = on_right(axis, stages - 1)
    zero = jnp.zeros(shape, F32)
    low, high = zero, zero
    unit_low = zero + jnp.where(right, -1.0, 0.0)
    unit_high = zero + jnp.where(right, 0.0, 1.0)
    for stage in range(stages - 2, -1, -1):
        tie = links[stage]
        right = on_right(axis, stage)
        flux = between(tie[0], tie[1], tie[2], low, high)
        unit = between(0.0, tie[1], tie[2], unit_low, unit_high)
        low, high = jnp.where(right, -flux, low), jnp.where(right, high, flux)
        unit_low, unit_high = jnp.where(right, -unit, unit_low), jnp.where(right, unit_high, unit)
    return (low, high), (unit_low, unit_high)


def natural(index, parts):
    span = SUBLANES * parts
    local = index % span
    return index - local + local % SUBLANES * parts + local // SUBLANES


def turn_matrix(shape, from_natural, parts):
    row = lax.broadcasted_iota(jnp.int32, shape, 0)
    column = lax.broadcasted_iota(jnp.int32, shape, 1) % LANES
    hit = natural(row, parts) == column if from_natural else row == natural(column, parts)
    return jnp.where(hit, 1.0, 0.0).astype(jnp.bfloat16)


def turned(matrix, field):
    high = field.astype(jnp.bfloat16)
    low = (field - high.astype(F32)).astype(jnp.bfloat16)
    both = jnp.concatenate([high, low], 1)
    return lax.dot_general(
        matrix, both, (((1,), (1,)), ((), ())), preferred_element_type=F32
    )


def y_factor_kernel(c_ref, after, w_ref, i_ref, p_ref, inner, outer, view, to_y, to_x, c_s, q_s, r_s):
    chunks, sheets, rows, _ = c_ref.shape
    each = LANES // rows
    pairs = sheets // each
    x_steps = rows // SUBLANES
    steps = LANES // SUBLANES
    to_y[...] = turn_matrix(to_y.shape, True, steps)
    to_x[...] = turn_matrix(to_x.shape, False, x_steps)
    for m in range(pairs):
        for y in range(chunks):
            block = jnp.concatenate(
                [
                    c_ref[y, m * each + i, pl.ds(k, SUBLANES, stride=x_steps), :]
                    for i in range(each)
                    for k in range(x_steps)
                ],
                0,
            )
            c_s[m, part_of(y), :] = block.T

    members = [(y, m) for y in range(chunks) for m in range(pairs)]
    lines = len(members)

    def cond(k):
        return jnp.stack([c_s[m, pl.ds(y * LANES + k, SUBLANES, stride=steps), :] for y, m in members], 0)

    def keep(k, w, inv, p):
        w_ref[k] = w
        i_ref[k] = inv
        p_ref[k] = p

    block = factor(cond, steps, keep)
    for n, q in enumerate(COEFS):
        for i in range(lines):
            q_s[n, i * SUBLANES : (i + 1) * SUBLANES, :] = block[q][i]
    segments = [
        {q: q_s[n, pl.ds(s, lines, stride=SUBLANES), :] for n, q in enumerate(COEFS)}
        for s in range(SUBLANES)
    ]
    whole, levels = tree(segments, join_coefs)
    for (offset, _), level in zip(node_offsets(SUBLANES), levels):
        for n, values in enumerate(level):
            for i in range(3):
                inner[offset + n, i] = values[i]
    for n, q in enumerate(COEFS):
        r_s[n] = whole[q]
    parts = [
        {q: r_s[n, y * pairs : (y + 1) * pairs, :] for n, q in enumerate(COEFS)} for y in range(chunks)
    ]
    whole, levels = tree(parts, join_coefs)
    for (offset, _), level in zip(node_offsets(chunks), levels):
        for n, values in enumerate(level):
            for i in range(3):
                outer[offset + n, i] = values[i]
    for n, q in enumerate(COEFS):
        view[n] = whole[q]


def y_factor(c, after):
    chunks, sheets, rows, _ = c.shape
    pairs = sheets * rows // LANES
    lines = chunks * pairs
    stored = shape_of(LANES // SUBLANES, lines, SUBLANES, LANES)
    matrix = jax.ShapeDtypeStruct((LANES, 2 * LANES), jnp.bfloat16)
    return pl.pallas_call(
        y_factor_kernel,
        in_specs=[IN_VMEM, ANYWHERE],
        out_shape=[
            stored,
            stored,
            stored,
            shape_of(SUBLANES - 1, 3, lines, LANES),
            shape_of(chunks - 1, 3, pairs, LANES),
            shape_of(len(COEFS), pairs, LANES),
            matrix,
            matrix,
        ],
        scratch_shapes=[
            pltpu.VMEM((pairs, chunks * LANES, LANES), F32),
            pltpu.VMEM((len(COEFS), lines * SUBLANES, LANES), F32),
            pltpu.VMEM((len(COEFS), lines, LANES), F32),
        ],
        compiler_params=params(),
        cost_estimate=pl.CostEstimate(flops=20 * c.size, bytes_accessed=16 * c.size, transcendentals=0),
    )(c, after)


def z_factor_kernel(c_ref, after, w_ref, i_ref):
    sheets = c_ref.shape[1]
    ground = 1.0
    for z in range(sheets - 1):
        face = c_ref[:, z] + c_ref[:, z + 1]
        inv = inverse(ground + face)
        w = face * inv
        i_ref[z] = inv
        w_ref[z] = w
        ground = 1.0 + w * ground
    i_ref[sheets - 1] = inverse(ground)


def z_factor(c, after):
    chunks, sheets, rows, _ = c.shape
    return pl.pallas_call(
        z_factor_kernel,
        in_specs=[IN_VMEM, ANYWHERE],
        out_shape=[
            shape_of(sheets - 1, chunks, rows, LANES),
            shape_of(sheets, chunks, rows, LANES),
        ],
        compiler_params=params(),
        cost_estimate=pl.CostEstimate(flops=10 * c.size, bytes_accessed=12 * c.size, transcendentals=0),
    )(c, after)


def join_tree(items, links, own):
    for offset, count in node_offsets(len(items)):
        joined = []
        for n in range(count):
            tie = tuple(links[offset + n, i] for i in range(3))
            both, flux = join_targets(items[2 * n], items[2 * n + 1], tie)
            own[offset + n] = flux
            joined.append(both)
        items = joined
    return items[0]


def tree_ends(leaves, links, own, low, high):
    levels = [
        [(own(offset + n), links[offset + n, 1], links[offset + n, 2]) for n in range(count)]
        for offset, count in node_offsets(leaves)
    ]
    return descend(levels, low, high)


def nothing(node):
    return 0.0


def y_prepare_kernel(stages, *refs):
    ties = refs[: stages - 1]
    xw, xh, xm, xp, x_links, x_own, t_ref, to_y = refs[stages - 1 : stages + 7]
    base, response, f_s, g_s = refs[stages + 7 :]
    x_steps, lines = xw.shape[:2]
    chunks = base.shape[0]
    sheets = lines // chunks
    rows = x_steps * SUBLANES

    ends, units = block_ends("gx", stages, ties)
    for n, (own, (low, high)) in enumerate(((lambda i: x_own[i], ends), (nothing, units))):
        for s, pair in enumerate(tree_ends(SUBLANES, x_links, own, low, high)):
            for i in range(2):
                f_s[n, i, pl.ds(s, lines, stride=SUBLANES), :] = pair[i]
    first = 0
    for n, members in enumerate(line_groups(chunks, sheets)):
        at = slice(first, first + len(members))
        h_ref_of, h_at = (xh, at) if n == 0 else (xm, slice(first - 2 * sheets, at.stop - 2 * sheets))
        (low, value), (unit_low, unit) = (
            [
                jnp.stack(
                    [f_s[q, i, j * SUBLANES : (j + 1) * SUBLANES, :] for j in range(at.start, at.stop)], 0
                )
                for i in range(2)
            ]
            for q in range(2)
        )
        for k in range(x_steps - 1, -1, -1):
            w, p = xw[k, at], xp[k, at]
            value = w * value + (h_ref_of[k, h_at] + p * low)
            unit = w * unit + p * unit_low
            field = value - t_ref[k, at]
            for j, (y, z) in enumerate(members):
                place = z * rows + k * SUBLANES
                g_s[0, y, place : place + SUBLANES, :] = field[j]
                g_s[1, y, place : place + SUBLANES, :] = unit[j]
        first = at.stop

    for y in range(chunks):
        base[y] = turned(to_y[...], g_s[0, y])
        response[y] = turned(to_y[...], g_s[1, y])


def y_prepare(ties, xw, xh, xm, xp, x_links, x_own, t, to_y, chunks):
    x_steps, lines = xw.shape[:2]
    width = lines // chunks * x_steps * SUBLANES
    field = shape_of(chunks, LANES, width)
    return pl.pallas_call(
        functools.partial(y_prepare_kernel, len(ties) + 1),
        out_shape=[field, field],
        scratch_shapes=[
            pltpu.VMEM((2, 2, lines * SUBLANES, LANES), F32),
            pltpu.VMEM((2, chunks, width, LANES), F32),
        ],
        compiler_params=params(),
        cost_estimate=pl.CostEstimate(flops=8 * t.size, bytes_accessed=16 * t.size, transcendentals=0),
    )(*ties, xw, xh, xm, xp, x_links, x_own, t, to_y)


def y_target_kernel(stages, own, got, base, response, yw, yi, yp, inner, outer, view, to_y, *refs):
    h_ref, inner_own, outer_own, send, q_s, r_s = refs
    chunks, _, width = base.shape
    pairs = width // LANES
    sheets = own.shape[1] // chunks
    rows = width // sheets
    steps = yw.shape[0]

    flux = top_flux("gx", stages, own, got)
    line_of = {member: n for n, member in enumerate(sum(line_groups(chunks, sheets), []))}
    fields = []
    for y in range(chunks):
        spread = jnp.concatenate(
            [
                jnp.broadcast_to(flux[line_of[y, z] : line_of[y, z] + 1, :], (rows, LANES))
                for z in range(sheets)
            ],
            0,
        )
        fields.append(base[y] + response[y] * turned(to_y[...], spread))

    def target(k):
        at = slice(k * SUBLANES, (k + 1) * SUBLANES)
        return jnp.stack(
            [fields[y][at, m * LANES : (m + 1) * LANES] for y in range(chunks) for m in range(pairs)], 0
        )

    def keep(k, h):
        h_ref[k] = h

    ends = eliminate(target, steps, lambda k: yw[k], lambda k: yi[k], lambda k: yp[k], keep)
    for q in range(2):
        for i in range(chunks * pairs):
            q_s[q, i * SUBLANES : (i + 1) * SUBLANES, :] = ends[q][i]
    items = [
        tuple(q_s[q, pl.ds(s, chunks * pairs, stride=SUBLANES), :] for q in range(2))
        for s in range(SUBLANES)
    ]
    r_s[0], r_s[1] = join_tree(items, inner, inner_own)
    items = [tuple(r_s[q, y * pairs : (y + 1) * pairs, :] for q in range(2)) for y in range(chunks)]
    for n, q in enumerate(COEFS):
        send[q] = view[n]
    send[FIRST], send[LAST] = join_tree(items, outer, outer_own)


def y_target(own, got, base, response, yw, yi, yp, inner, outer, view, to_y):
    y_lines = yw.shape[1]
    pairs = view.shape[1]
    chunks = y_lines // pairs
    return pl.pallas_call(
        functools.partial(y_target_kernel, stages_of("gx")),
        out_shape=[
            shape_of(*yw.shape),
            shape_of(SUBLANES - 1, y_lines, LANES),
            shape_of(chunks - 1, pairs, LANES),
            shape_of(7, pairs, LANES),
        ],
        scratch_shapes=[
            pltpu.VMEM((2, y_lines * SUBLANES, LANES), F32),
            pltpu.VMEM((2, y_lines, LANES), F32),
        ],
        compiler_params=params(),
    )(own, got, base, response, yw, yi, yp, inner, outer, view, to_y)


def z_solve(zw, zi, field, at, keep):
    sheets = zi.shape[0]
    rhs, kept = None, []
    for z in range(sheets):
        rhs = field(z) if z == 0 else field(z) + zw[z - 1, at] * rhs
        kept.append(rhs * zi[z, at])
    value = kept[-1]
    keep(sheets - 1, value)
    for z in range(sheets - 2, -1, -1):
        value = zw[z, at] * value + kept[z]
        keep(z, value)


def finish_prepare_kernel(stages, *refs):
    ties = refs[: stages - 1]
    yw, yh, yp, inner, inner_own, outer, outer_own, zw, zi, t_ref, to_x = refs[stages - 1 : stages + 10]
    base, response, r_s, e_s, u_s = refs[stages + 10 :]
    chunks, sheets, rows, _ = base.shape
    each = LANES // rows
    pairs = sheets // each
    steps = yw.shape[0]
    lines = chunks * pairs

    ends, units = block_ends("gy", stages, ties)
    both = (
        (lambda i: outer_own[i], lambda i: inner_own[i], ends),
        (nothing, nothing, units),
    )
    for n, (upper, lower, (low, high)) in enumerate(both):
        for y, pair in enumerate(tree_ends(chunks, outer, upper, low, high)):
            for i in range(2):
                r_s[n, i, y * pairs : (y + 1) * pairs, :] = pair[i]
        for s, pair in enumerate(tree_ends(SUBLANES, inner, lower, r_s[n, 0], r_s[n, 1])):
            for i in range(2):
                e_s[n, i, pl.ds(s, lines, stride=SUBLANES), :] = pair[i]
    (low, value), (unit_low, unit) = (
        [
            jnp.stack([e_s[q, i, n * SUBLANES : (n + 1) * SUBLANES, :] for n in range(lines)], 0)
            for i in range(2)
        ]
        for q in range(2)
    )
    for k in range(steps - 1, -1, -1):
        w, p = yw[k], yp[k]
        value = w * value + (yh[k] + p * low)
        unit = w * unit + p * unit_low
        for y in range(chunks):
            for m in range(pairs):
                place = pl.ds(y * LANES + k, SUBLANES, stride=steps)
                u_s[0, m, place, :] = value[y * pairs + m]
                u_s[1, m, place, :] = unit[y * pairs + m]

    for y in range(chunks):
        part = part_of(y)
        fields = [turned(to_x[...], u_s[0, m, part, :]) for m in range(pairs)]

        def field(z):
            at = z % each * rows
            return fields[z // each][at : at + rows, :]

        def keep(z, value):
            base[y, z] = t_ref[z, :, part] + value

        z_solve(zw, zi, field, y, keep)
        for m in range(pairs):
            units = turned(to_x[...], u_s[1, m, part, :])
            for i in range(each):
                response[y, m * each + i] = units[i * rows : (i + 1) * rows, :]


def finish_prepare(ties, yw, yh, yp, inner, inner_own, outer, outer_own, zw, zi, t, to_x):
    sheets, rows, columns = t.shape
    chunks = columns // LANES
    pairs = sheets * rows // LANES
    lines = chunks * pairs
    field = shape_of(chunks, sheets, rows, LANES)
    return pl.pallas_call(
        functools.partial(finish_prepare_kernel, len(ties) + 1),
        out_shape=[field, field],
        scratch_shapes=[
            pltpu.VMEM((2, 2, lines, LANES), F32),
            pltpu.VMEM((2, 2, lines * SUBLANES, LANES), F32),
            pltpu.VMEM((2, pairs, columns, LANES), F32),
        ],
        compiler_params=params(),
        cost_estimate=pl.CostEstimate(flops=12 * t.size, bytes_accessed=20 * t.size, transcendentals=0),
    )(*ties, yw, yh, yp, inner, inner_own, outer, outer_own, zw, zi, t, to_x)


def finish_kernel(stages, own, got, base, response, zw, zi, to_x, out, o_s, sems):
    chunks, sheets, rows, _ = base.shape
    each = LANES // rows
    pairs = sheets // each
    copies, _, wide = o_s.shape

    flux = top_flux("gy", stages, own, got)
    spread = [
        turned(to_x[...], jnp.broadcast_to(flux[m : m + 1, :], (LANES, LANES))) for m in range(pairs)
    ]
    started = []
    for n in range(copies):
        for y in range(n * chunks // copies, (n + 1) * chunks // copies):
            part = part_of(y - n * chunks // copies)

            def field(z):
                at = z % each * rows
                return response[y, z] * spread[z // each][at : at + rows, :]

            def keep(z, value):
                o_s[n, z * rows : (z + 1) * rows, part] = base[y, z] + value

            z_solve(zw, zi, field, y, keep)
        copy = pltpu.make_async_copy(o_s.at[n], out.at[:, pl.ds(n * wide, wide)], sems.at[n])
        copy.start()
        started.append(copy)
    for copy in started:
        copy.wait()


def finish(own, got, base, response, zw, zi, to_x):
    chunks, sheets, rows, _ = base.shape
    copies = chunks
    return pl.pallas_call(
        functools.partial(finish_kernel, stages_of("gy")),
        out_shape=shape_of(sheets * rows, chunks * LANES),
        out_specs=ANYWHERE,
        scratch_shapes=[
            pltpu.VMEM((copies, sheets * rows, chunks * LANES // copies), F32),
            pltpu.SemaphoreType.DMA((copies,)),
        ],
        compiler_params=params(),
    )(own, got, base, response, zw, zi, to_x).reshape(sheets, rows, chunks * LANES)


def per_device(temperature, base, locations, energy):
    columns = temperature.shape[2]
    gy = lax.axis_size("gy")
    t, b, loc, heat, packed = load(temperature, base, locations[None], energy[None])
    near = swap(packed, "gy", 1)
    far = lax.ppermute(packed, "gy", [(i, ((i + 1) % gy ^ 1) - 1 if i else gy - 1) for i in range(gy)])
    c, total, xw, xi, xp, x_links, x_view, xm, ends, t_steps = x_factor(loc, heat, t, b, columns * gy, packed)
    xh, x_own, view = x_target(packed, t, total, near, far, xw, xi, xp, x_links, x_view, ends)
    yw, yi, yp, inner, outer, y_view, to_y, to_x = y_factor(c, x_view)
    zw, zi = z_factor(c, view)
    own, got, ties = gather_line(view, "gx", 2, (y_view, zw))
    base, response = y_prepare(
        ties, xw, xh, xm, xp, x_links, x_own, t_steps, to_y, columns // LANES
    )
    yh, inner_own, outer_own, view = y_target(
        own, got, base, response, yw, yi, yp, inner, outer, y_view, to_y
    )
    own, got, ties = gather_line(view, "gy")
    base, response = finish_prepare(
        ties, yw, yh, yp, inner, inner_own, outer, outer_own, zw, zi, t, to_x
    )
    return finish(own, got, base, response, zw, zi, to_x)


def solution(mesh):
    in_specs = (P(None, "gx", "gy"), P(None, "gx", "gy"), P(), P())
    out_specs = P(None, "gx", "gy")
    return jax.shard_map(
        per_device, mesh=mesh, in_specs=in_specs, out_specs=out_specs, check_vma=False
    )
```

```python
import functools

import jax
import jax.numpy as jnp
from jax import lax
from jax.experimental import pallas as pl
from jax.experimental.pallas import tpu as pltpu
from jax.sharding import PartitionSpec as P

RATE = 2000.0
THERMAL_GROWTH = 0.8
LANES = 128
SUBLANES = 8
F32 = jnp.float32
MIB = 1024 * 1024
ANYWHERE = pl.BlockSpec(memory_space=pl.ANY)
IN_HBM = pl.BlockSpec(memory_space=pltpu.HBM)
IN_VMEM = pl.BlockSpec(memory_space=pltpu.VMEM)

R00, R0L, RLL, FIRST, LAST, C0, CL = range(7)
COEFS = (R00, R0L, RLL, C0, CL)


def params(limit=40):
    return pltpu.CompilerParams(vmem_limit_bytes=limit * MIB)


def shape_of(*sizes):
    return jax.ShapeDtypeStruct(sizes, F32)


def half_conduct(base, temperature):
    return base * (0.5 * RATE + (0.5 * RATE * THERMAL_GROWTH) * temperature)


def inverse(x):
    guess = pl.reciprocal(x, approx=True)
    return guess * (2.0 - x * guess)


def join_coefs(a, b):
    face = a[CL] + b[C0]
    inv = face * inverse(1.0 + face * (a[RLL] + b[R00]))
    left = a[R0L] * inv
    right = b[R0L] * inv
    joined = {
        R00: a[R00] - left * a[R0L],
        R0L: left * b[R0L],
        RLL: b[RLL] - right * b[R0L],
        C0: a[C0],
        CL: b[CL],
    }
    return joined, (inv, right, left)


def join_targets(a, b, links):
    inv, right, left = links
    jump = b[0] - a[1]
    return (a[0] + left * jump, b[1] - right * jump), jump * inv


def between(own, right, left, low, high):
    return own + right * high - left * low


def tree(items, join):
    levels = []
    while len(items) > 1:
        pairs = [join(items[i], items[i + 1]) for i in range(0, len(items), 2)]
        items = [p[0] for p in pairs]
        levels.append([p[1] for p in pairs])
    return items[0], levels


def descend(levels, low, high):
    ends = [(low, high)]
    for level in reversed(levels):
        below = []
        for (lo, hi), (own, right, left) in zip(ends, level):
            flux = between(own, right, left, lo, hi)
            below += [(lo, flux), (-flux, hi)]
        ends = below
    return ends


def node_offsets(leaves):
    offsets, at, count = [], 0, leaves // 2
    while count:
        offsets.append((at, count))
        at += count
        count //= 2
    return offsets


def factor(cond, steps, keep):
    here = cond(0)
    c_first = here
    one = jnp.ones_like(here)
    ground, path, first_first = one, one, None
    for k in range(steps - 1):
        following = cond(k + 1)
        face = here + following
        inv = inverse(ground + face)
        w = face * inv
        p = path * inv
        keep(k, w, inv, p)
        step = path * p
        first_first = step if first_first is None else first_first + step
        path = path * w
        ground = 1.0 + w * ground
        here = following
    inv = inverse(ground)
    p = path * inv
    keep(steps - 1, inv, inv, p)
    return {R00: first_first + path * p, R0L: p, RLL: inv, C0: c_first, CL: here}


def eliminate(target, steps, w, inv, p, keep):
    rhs = target(0)
    first = None
    for k in range(steps):
        h = rhs * inv(k)
        keep(k, h)
        step = rhs * p(k)
        first = step if first is None else first + step
        if k < steps - 1:
            rhs = target(k + 1) + w(k) * rhs
    return first, h


def is_odd(axis):
    return lax.axis_index(axis) % 2 == 1


def fold(cells, used):
    total = cells[:SUBLANES]
    lane = lax.broadcasted_iota(jnp.int32, total.shape, 1)
    for n in range(1, cells.shape[0] // SUBLANES):
        part = pltpu.roll(cells[n * SUBLANES : (n + 1) * SUBLANES], n * used, 1)
        total = jnp.where(lane // used == n, part, total)
    return total


def unfold(cells, used, rows):
    parts = [cells] + [
        pltpu.roll(cells, LANES - n * used, 1) for n in range(1, rows // SUBLANES)
    ]
    return jnp.concatenate(parts, 0)


def load_kernel(t_hbm, b_hbm, loc_hbm, energy_hbm, t_out, b_out, loc, energy, packed, sems):
    sheets, rows, columns = t_hbm.shape
    parts = [(0, LANES), (columns - LANES, LANES), (LANES, columns - 2 * LANES)]
    copies = []
    for n, (start, size) in enumerate(parts):
        part = pl.ds(start, size)
        for i, (src, dst) in enumerate(((t_hbm, t_out), (b_hbm, b_out))):
            copies.append(
                pltpu.make_async_copy(src.at[:, :, part], dst.at[:, :, part], sems.at[i, n])
            )
    copies.append(pltpu.make_async_copy(loc_hbm, loc, sems.at[2, 0]))
    copies.append(pltpu.make_async_copy(energy_hbm, energy, sems.at[2, 1]))
    for copy in copies:
        copy.start()
    lane = lax.broadcasted_iota(jnp.int32, (rows, LANES), 1)
    total = jnp.zeros((rows, LANES), F32)
    for side, source in enumerate((0, LANES - 1)):
        for copy in copies[2 * side : 2 * side + 2]:
            copy.wait()
        part = slice(parts[side][0], parts[side][0] + LANES)
        for z in range(sheets):
            t = t_out[z, :, part]
            c = half_conduct(b_out[z, :, part], t)
            place = 2 * sheets * side + z
            total = jnp.where(lane == place, t[:, source : source + 1], total)
            total = jnp.where(lane == place + sheets, c[:, source : source + 1], total)
    packed[...] = fold(total, 4 * sheets)
    for copy in copies[4:]:
        copy.wait()


def load(temperature, base, locations, energy):
    sheets, rows, columns = temperature.shape
    assert rows // SUBLANES * 4 * sheets <= LANES and columns > 2 * LANES
    operands = (temperature, base, locations, energy)
    return pl.pallas_call(
        load_kernel,
        in_specs=[IN_HBM] * 4,
        out_shape=[pltpu.VMEM(v.shape, v.dtype) for v in operands]
        + [pltpu.VMEM((SUBLANES, LANES), F32)],
        scratch_shapes=[pltpu.SemaphoreType.DMA((3, 3))],
        compiler_params=params(),
    )(*[pltpu.with_memory_space_constraint(v, pltpu.HBM) for v in operands])


def source_plane(loc, energy, rows, columns, plate):
    place = loc[...]
    count = place.shape[1]
    local_x = place // plate - lax.axis_index("gx") * rows
    local_y = place % plate - lax.axis_index("gy") * columns
    in_x = lax.broadcasted_iota(jnp.int32, (rows, count), 0) == local_x
    in_y = lax.broadcasted_iota(jnp.int32, (columns, count), 0) == local_y
    by_y = jnp.where(in_y, 1.0, 0.0).astype(jnp.bfloat16)
    left = energy[...]
    plane = None
    for _ in range(3):
        part = left.astype(jnp.bfloat16).astype(F32)
        left = left - part
        term = lax.dot_general(
            jnp.where(in_x, part, 0.0).astype(jnp.bfloat16),
            by_y,
            (((1,), (1,)), ((), ())),
            preferred_element_type=F32,
        )
        plane = term if plane is None else plane + term
    return plane


def part_of(y):
    return slice(y * LANES, (y + 1) * LANES)


def line_groups(chunks, sheets):
    order = [0, chunks - 1] + list(range(1, chunks - 1))
    return [[(y, z) for y in order[i : i + 2] for z in range(sheets)] for i in range(0, chunks, 2)]


def x_eliminate(field, members, first_line, w_ref, i_ref, p_ref, h_ref, h_line, q_s):
    steps = w_ref.shape[0]
    at = slice(first_line, first_line + len(members))
    kept_at = slice(h_line, h_line + len(members))

    def target(k):
        return jnp.stack([field(y, z)[pl.ds(k, SUBLANES, stride=steps), :] for y, z in members], 0)

    def keep(k, h):
        h_ref[k, kept_at] = h

    ends = eliminate(
        target, steps, lambda k: w_ref[k, at], lambda k: i_ref[k, at], lambda k: p_ref[k, at], keep
    )
    for q in range(2):
        for i in range(len(members)):
            first = (first_line + i) * SUBLANES
            q_s[q, first : first + SUBLANES, :] = ends[q][i]


def x_factor_kernel(plate, loc, energy, t_ref, b_ref, after, *refs):
    c_ref, total_ref, w_ref, i_ref, p_ref, links, view, h_ref, ends_ref, t_out, q_s, t_s = refs
    chunks, sheets, rows, _ = c_ref.shape
    lines = chunks * sheets
    steps = rows // SUBLANES
    plane = source_plane(loc, energy, rows, chunks * LANES, plate)

    lane = lax.broadcasted_iota(jnp.int32, (SUBLANES, LANES), 1)
    is_first, is_last = lane == 0, lane == LANES - 1
    for r in range(steps):
        at = slice(r * SUBLANES, (r + 1) * SUBLANES)
        before_t, before_c = None, None
        for z in range(sheets):
            ts = [t_ref[z, at, part_of(y)] for y in range(chunks)]
            cs = [half_conduct(b_ref[z, at, part_of(y)], ts[y]) for y in range(chunks)]
            t_turned = [pltpu.roll(v, LANES - 1, 1) for v in ts]
            c_turned = [pltpu.roll(v, LANES - 1, 1) for v in cs]
            flux = []
            for y in range(chunks):
                if y < chunks - 1:
                    t_next = jnp.where(is_last, t_turned[y + 1], t_turned[y])
                    c_next = jnp.where(is_last, c_turned[y + 1], c_turned[y])
                    flux.append((cs[y] + c_next) * (t_next - ts[y]))
                else:
                    inside = (cs[y] + c_turned[y]) * (t_turned[y] - ts[y])
                    flux.append(jnp.where(is_last, 0.0, inside))
            turned = [pltpu.roll(v, 1, 1) for v in flux]
            for y in range(chunks):
                from_low = jnp.where(is_first, turned[y - 1] if y else 0.0, turned[y])
                total = ts[y] + (flux[y] - from_low)
                if z == 0:
                    total = total + plane[at, part_of(y)]
                else:
                    across = (before_c[y] + cs[y]) * (ts[y] - before_t[y])
                    total = total - across
                    total_ref[y, z - 1, at, :] += across
                total_ref[y, z, at, :] = total
                c_ref[y, z, at, :] = cs[y]
                t_s[y, z, at, :] = ts[y]
            before_t, before_c = ts, cs

    at = 0
    for n, members in enumerate(line_groups(chunks, sheets)):

        def cond(k):
            return jnp.stack([c_ref[y, z, pl.ds(k, SUBLANES, stride=steps), :] for y, z in members], 0)

        def keep(k, w, inv, p):
            w_ref[k, at : at + len(members)] = w
            i_ref[k, at : at + len(members)] = inv
            p_ref[k, at : at + len(members)] = p

        block = factor(cond, steps, keep)
        for i, q in enumerate(COEFS):
            for j in range(len(members)):
                first = (at + j) * SUBLANES
                q_s[i, first : first + SUBLANES, :] = block[q][j]
        if n > 0:
            x_eliminate(
                lambda y, z: total_ref.at[y, z], members, at, w_ref, i_ref, p_ref, h_ref,
                at - 2 * sheets, ends_ref,
            )
        for k in range(steps):
            for i, (y, z) in enumerate(members):
                t_out[k, at + i] = t_s[y, z, pl.ds(k, SUBLANES, stride=steps), :]
        at += len(members)

    segments = [
        {q: q_s[n, pl.ds(s, lines, stride=SUBLANES), :] for n, q in enumerate(COEFS)}
        for s in range(SUBLANES)
    ]
    whole, levels = tree(segments, join_coefs)
    for (offset, _), level in zip(node_offsets(SUBLANES), levels):
        for n, values in enumerate(level):
            for i in range(3):
                links[offset + n, i] = values[i]
    for n, q in enumerate(COEFS):
        view[n] = whole[q]


def x_factor(loc, energy, t, b, plate, after):
    sheets, rows, columns = t.shape
    chunks = columns // LANES
    lines = chunks * sheets
    steps = rows // SUBLANES
    field = shape_of(chunks, sheets, rows, LANES)
    stored = shape_of(steps, lines, SUBLANES, LANES)
    return pl.pallas_call(
        functools.partial(x_factor_kernel, plate),
        in_specs=[IN_VMEM] * 4 + [ANYWHERE],
        out_shape=[
            field,
            field,
            stored,
            stored,
            stored,
            shape_of(SUBLANES - 1, 3, lines, LANES),
            shape_of(len(COEFS), lines, LANES),
            shape_of(steps, max(1, lines - 2 * sheets), SUBLANES, LANES),
            shape_of(2, lines * SUBLANES, LANES),
            stored,
        ],
        scratch_shapes=[
            pltpu.VMEM((len(COEFS), lines * SUBLANES, LANES), F32),
            pltpu.VMEM((chunks, sheets, rows, LANES), F32),
        ],
        compiler_params=params(),
        cost_estimate=pl.CostEstimate(flops=40 * t.size, bytes_accessed=28 * t.size, transcendentals=0),
    )(loc, energy, t, b, after)


def x_target_kernel(own_cells, t_ref, total_ref, near_ref, far_ref, *refs):
    w_ref, i_ref, p_ref, links, view, ends_ref, h_ref, own, send, e_s, q_s = refs
    chunks, sheets, rows, _ = total_ref.shape
    lines = chunks * sheets

    lane = lax.broadcasted_iota(jnp.int32, (rows, LANES), 1)
    side = 2 * sheets
    place = lax.axis_index("gy")
    inner = (place > 0) & (place < lax.axis_size("gy") - 1)
    near, far = near_ref[...], jnp.where(inner, far_ref[...], 0.0)
    before = unfold(jnp.where(is_odd("gy"), near, far), 2 * side, rows)
    after = unfold(jnp.where(is_odd("gy"), far, near), 2 * side, rows)
    beyond = jnp.where(lane < side, pltpu.roll(before, LANES - side, 1), pltpu.roll(after, side, 1))
    mine = unfold(own_cells[...], 2 * side, rows)
    face = jnp.where(beyond > 0.0, mine + beyond, 0.0)
    flux = pltpu.roll(face, LANES - sheets, 1) * (beyond - mine)
    for n, (y, edge) in enumerate(((0, 0), (chunks - 1, LANES - 1))):
        for z in range(sheets):
            at = n * side + z
            e_s[n, z] = total_ref[y, z] + jnp.where(lane == edge, flux[:, at : at + 1], 0.0)

    members = line_groups(chunks, sheets)[0]
    x_eliminate(
        lambda y, z: e_s.at[0 if y == 0 else 1, z], members, 0, w_ref, i_ref, p_ref, h_ref, 0, q_s
    )
    split = len(members)
    items = [
        tuple(
            jnp.concatenate(
                [
                    q_s[q, pl.ds(s, split, stride=SUBLANES), :],
                    ends_ref[q, pl.ds(split * SUBLANES + s, lines - split, stride=SUBLANES), :],
                ],
                0,
            )
            for q in range(2)
        )
        for s in range(SUBLANES)
    ]
    for offset, count in node_offsets(SUBLANES):
        joined = []
        for n in range(count):
            ties = tuple(links[offset + n, i] for i in range(3))
            both, flux = join_targets(items[2 * n], items[2 * n + 1], ties)
            own[offset + n] = flux
            joined.append(both)
        items = joined
    for n, q in enumerate(COEFS):
        send[q] = view[n]
    send[FIRST], send[LAST] = items[0]


def x_target(own_cells, t, total, near, far, w, inv, p, links, view, ends):
    chunks, sheets, rows, _ = total.shape
    lines = chunks * sheets
    steps = rows // SUBLANES
    return pl.pallas_call(
        x_target_kernel,
        out_shape=[
            shape_of(steps, 2 * sheets, SUBLANES, LANES),
            shape_of(SUBLANES - 1, lines, LANES),
            shape_of(7, lines, LANES),
        ],
        scratch_shapes=[
            pltpu.VMEM((2, sheets, rows, LANES), F32),
            pltpu.VMEM((2, 2 * sheets * SUBLANES, LANES), F32),
        ],
        compiler_params=params(),
    )(own_cells, t, total, near, far, w, inv, p, links, view, ends)


def stages_of(axis):
    return lax.axis_size(axis).bit_length() - 1


def swap(value, axis, flip):
    count = lax.axis_size(axis)
    return lax.ppermute(value, axis, [(i, i ^ flip) for i in range(count)])


def on_right(axis, stage):
    return (lax.axis_index(axis) >> stage) % 2 == 1


def toward(right, block):
    return (
        jnp.where(right, block[R00], block[RLL]),
        jnp.where(right, block[FIRST], block[LAST]),
        jnp.where(right, block[C0], block[CL]),
    )


def join(a, b):
    joined, ties = join_coefs(a, b)
    (joined[FIRST], joined[LAST]), flux = join_targets((a[FIRST], a[LAST]), (b[FIRST], b[LAST]), ties)
    return joined, (flux, ties[1], ties[2])


def ordered(right, own, other):
    first = [jnp.where(right, theirs, mine) for mine, theirs in zip(own, other)]
    second = [jnp.where(right, mine, theirs) for mine, theirs in zip(own, other)]
    return first, second


def join_kernel(axis, stage, width, last, *refs):
    count = 1 << width
    blocks = [[refs[i][q] for q in range(7)] for i in range(count)]
    send = refs[-1 - width]
    links = refs[-width:]
    for bit in range(width):
        right = on_right(axis, stage + bit)
        for i in range(count):
            if not i >> bit & 1:
                j = i | 1 << bit
                blocks[i], blocks[j] = ordered(right, blocks[i], blocks[j])
    for bit in range(width):
        pairs = [join(blocks[i], blocks[i + 1]) for i in range(0, len(blocks), 2)]
        blocks = [p[0] for p in pairs]
        ties = [p[1] for p in pairs]
        for upper in range(bit + 1, width):
            right = on_right(axis, stage + upper)
            ties = [
                tuple(jnp.where(right, v, u) for u, v in zip(ties[i], ties[i + 1]))
                for i in range(0, len(ties), 2)
            ]
        for i in range(3):
            links[bit][i] = ties[0][i]
    (whole,) = blocks
    if last:
        for n, value in enumerate(toward(on_right(axis, stage + width), whole)):
            send[n] = value
    else:
        for q in range(7):
            send[q] = whole[q]


def join_stage(own, got, axis, stage, width, last, after):
    lines = own.shape[1]
    return pl.pallas_call(
        functools.partial(join_kernel, axis, stage, width, last),
        in_specs=[IN_VMEM] * (1 + len(got)) + [ANYWHERE] * len(after),
        out_shape=[shape_of(3 if last else 7, lines, LANES)] + [shape_of(3, lines, LANES)] * width,
        compiler_params=params(),
    )(own, *got, *after)


def gather_line(view, axis, widest=1, meanwhile=(), cross=False):
    stages = stages_of(axis)
    links, stage = [], 0
    while stage < stages - 1:
        width = min(widest, stages - 1 - stage)
        got = [swap(view, axis, flip << stage) for flip in range(1, 1 << width)]
        last = stage + width == stages - 1
        view, *ties = join_stage(view, got, axis, stage, width, last, meanwhile)
        links += ties
        stage += width
        meanwhile = ()
    return view, swap(view, axis, 1 << stage | (cross and stage > 0)), links


def top_flux(axis, stages, own, got):
    right = on_right(axis, stages - 1)
    face = own[2] + got[2]
    jump = jnp.where(right, own[1] - got[1], got[1] - own[1])
    return jump * face * inverse(1.0 + face * (own[0] + got[0]))


def block_ends(axis, stages, links):
    shape = links[0].shape[1:] if links else None
    right = on_right(axis, stages - 1)
    zero = jnp.zeros(shape, F32)
    low, high = zero, zero
    unit_low = zero + jnp.where(right, -1.0, 0.0)
    unit_high = zero + jnp.where(right, 0.0, 1.0)
    for stage in range(stages - 2, -1, -1):
        tie = links[stage]
        right = on_right(axis, stage)
        flux = between(tie[0], tie[1], tie[2], low, high)
        unit = between(0.0, tie[1], tie[2], unit_low, unit_high)
        low, high = jnp.where(right, -flux, low), jnp.where(right, high, flux)
        unit_low, unit_high = jnp.where(right, -unit, unit_low), jnp.where(right, unit_high, unit)
    return (low, high), (unit_low, unit_high)


def natural(index, parts):
    span = SUBLANES * parts
    local = index % span
    return index - local + local % SUBLANES * parts + local // SUBLANES


def turn_matrix(shape, from_natural, parts):
    row = lax.broadcasted_iota(jnp.int32, shape, 0)
    column = lax.broadcasted_iota(jnp.int32, shape, 1) % LANES
    hit = natural(row, parts) == column if from_natural else row == natural(column, parts)
    return jnp.where(hit, 1.0, 0.0).astype(jnp.bfloat16)


def turned(matrix, field):
    high = field.astype(jnp.bfloat16)
    low = (field - high.astype(F32)).astype(jnp.bfloat16)
    both = jnp.concatenate([high, low], 1)
    return lax.dot_general(
        matrix, both, (((1,), (1,)), ((), ())), preferred_element_type=F32
    )


def y_factor_kernel(c_ref, after, w_ref, i_ref, p_ref, inner, outer, view, to_y, to_x, c_s, q_s, r_s):
    chunks, sheets, rows, _ = c_ref.shape
    each = LANES // rows
    pairs = sheets // each
    x_steps = rows // SUBLANES
    steps = LANES // SUBLANES
    to_y[...] = turn_matrix(to_y.shape, True, steps)
    to_x[...] = turn_matrix(to_x.shape, False, x_steps)
    for m in range(pairs):
        for y in range(chunks):
            block = jnp.concatenate(
                [
                    c_ref[y, m * each + i, pl.ds(k, SUBLANES, stride=x_steps), :]
                    for i in range(each)
                    for k in range(x_steps)
                ],
                0,
            )
            c_s[m, part_of(y), :] = block.T

    members = [(y, m) for y in range(chunks) for m in range(pairs)]
    lines = len(members)

    def cond(k):
        return jnp.stack([c_s[m, pl.ds(y * LANES + k, SUBLANES, stride=steps), :] for y, m in members], 0)

    def keep(k, w, inv, p):
        w_ref[k] = w
        i_ref[k] = inv
        p_ref[k] = p

    block = factor(cond, steps, keep)
    for n, q in enumerate(COEFS):
        for i in range(lines):
            q_s[n, i * SUBLANES : (i + 1) * SUBLANES, :] = block[q][i]
    segments = [
        {q: q_s[n, pl.ds(s, lines, stride=SUBLANES), :] for n, q in enumerate(COEFS)}
        for s in range(SUBLANES)
    ]
    whole, levels = tree(segments, join_coefs)
    for (offset, _), level in zip(node_offsets(SUBLANES), levels):
        for n, values in enumerate(level):
            for i in range(3):
                inner[offset + n, i] = values[i]
    for n, q in enumerate(COEFS):
        r_s[n] = whole[q]
    parts = [
        {q: r_s[n, y * pairs : (y + 1) * pairs, :] for n, q in enumerate(COEFS)} for y in range(chunks)
    ]
    whole, levels = tree(parts, join_coefs)
    for (offset, _), level in zip(node_offsets(chunks), levels):
        for n, values in enumerate(level):
            for i in range(3):
                outer[offset + n, i] = values[i]
    for n, q in enumerate(COEFS):
        view[n] = whole[q]


def y_factor(c, after):
    chunks, sheets, rows, _ = c.shape
    pairs = sheets * rows // LANES
    lines = chunks * pairs
    stored = shape_of(LANES // SUBLANES, lines, SUBLANES, LANES)
    matrix = jax.ShapeDtypeStruct((LANES, 2 * LANES), jnp.bfloat16)
    return pl.pallas_call(
        y_factor_kernel,
        in_specs=[IN_VMEM, ANYWHERE],
        out_shape=[
            stored,
            stored,
            stored,
            shape_of(SUBLANES - 1, 3, lines, LANES),
            shape_of(chunks - 1, 3, pairs, LANES),
            shape_of(len(COEFS), pairs, LANES),
            matrix,
            matrix,
        ],
        scratch_shapes=[
            pltpu.VMEM((pairs, chunks * LANES, LANES), F32),
            pltpu.VMEM((len(COEFS), lines * SUBLANES, LANES), F32),
            pltpu.VMEM((len(COEFS), lines, LANES), F32),
        ],
        compiler_params=params(),
        cost_estimate=pl.CostEstimate(flops=20 * c.size, bytes_accessed=16 * c.size, transcendentals=0),
    )(c, after)


def z_factor_kernel(c_ref, after, w_ref, i_ref):
    sheets = c_ref.shape[1]
    ground = 1.0
    for z in range(sheets - 1):
        face = c_ref[:, z] + c_ref[:, z + 1]
        inv = inverse(ground + face)
        w = face * inv
        i_ref[z] = inv
        w_ref[z] = w
        ground = 1.0 + w * ground
    i_ref[sheets - 1] = inverse(ground)


def z_factor(c, after):
    chunks, sheets, rows, _ = c.shape
    return pl.pallas_call(
        z_factor_kernel,
        in_specs=[IN_VMEM, ANYWHERE],
        out_shape=[
            shape_of(sheets - 1, chunks, rows, LANES),
            shape_of(sheets, chunks, rows, LANES),
        ],
        compiler_params=params(),
        cost_estimate=pl.CostEstimate(flops=10 * c.size, bytes_accessed=12 * c.size, transcendentals=0),
    )(c, after)


def join_tree(items, links, own):
    for offset, count in node_offsets(len(items)):
        joined = []
        for n in range(count):
            tie = tuple(links[offset + n, i] for i in range(3))
            both, flux = join_targets(items[2 * n], items[2 * n + 1], tie)
            own[offset + n] = flux
            joined.append(both)
        items = joined
    return items[0]


def tree_ends(leaves, links, own, low, high):
    levels = [
        [(own(offset + n), links[offset + n, 1], links[offset + n, 2]) for n in range(count)]
        for offset, count in node_offsets(leaves)
    ]
    return descend(levels, low, high)


def nothing(node):
    return 0.0


def y_prepare_kernel(stages, *refs):
    ties = refs[: stages - 1]
    xw, xh, xm, xp, x_links, x_own, t_ref, to_y = refs[stages - 1 : stages + 7]
    base, response, f_s, g_s = refs[stages + 7 :]
    x_steps, lines = xw.shape[:2]
    chunks = base.shape[0]
    sheets = lines // chunks
    rows = x_steps * SUBLANES

    ends, units = block_ends("gx", stages, ties)
    for n, (own, (low, high)) in enumerate(((lambda i: x_own[i], ends), (nothing, units))):
        for s, pair in enumerate(tree_ends(SUBLANES, x_links, own, low, high)):
            for i in range(2):
                f_s[n, i, pl.ds(s, lines, stride=SUBLANES), :] = pair[i]
    first = 0
    for n, members in enumerate(line_groups(chunks, sheets)):
        at = slice(first, first + len(members))
        h_ref_of, h_at = (xh, at) if n == 0 else (xm, slice(first - 2 * sheets, at.stop - 2 * sheets))
        (low, value), (unit_low, unit) = (
            [
                jnp.stack(
                    [f_s[q, i, j * SUBLANES : (j + 1) * SUBLANES, :] for j in range(at.start, at.stop)], 0
                )
                for i in range(2)
            ]
            for q in range(2)
        )
        for k in range(x_steps - 1, -1, -1):
            w, p = xw[k, at], xp[k, at]
            value = w * value + (h_ref_of[k, h_at] + p * low)
            unit = w * unit + p * unit_low
            field = value - t_ref[k, at]
            for j, (y, z) in enumerate(members):
                place = z * rows + k * SUBLANES
                g_s[0, y, place : place + SUBLANES, :] = field[j]
                g_s[1, y, place : place + SUBLANES, :] = unit[j]
        first = at.stop

    for y in range(chunks):
        base[y] = turned(to_y[...], g_s[0, y])
        response[y] = turned(to_y[...], g_s[1, y])


def y_prepare(ties, xw, xh, xm, xp, x_links, x_own, t, to_y, chunks):
    x_steps, lines = xw.shape[:2]
    width = lines // chunks * x_steps * SUBLANES
    field = shape_of(chunks, LANES, width)
    return pl.pallas_call(
        functools.partial(y_prepare_kernel, len(ties) + 1),
        out_shape=[field, field],
        scratch_shapes=[
            pltpu.VMEM((2, 2, lines * SUBLANES, LANES), F32),
            pltpu.VMEM((2, chunks, width, LANES), F32),
        ],
        compiler_params=params(),
        cost_estimate=pl.CostEstimate(flops=8 * t.size, bytes_accessed=16 * t.size, transcendentals=0),
    )(*ties, xw, xh, xm, xp, x_links, x_own, t, to_y)


def y_target_kernel(stages, own, got, base, response, yw, yi, yp, inner, outer, view, to_y, *refs):
    h_ref, inner_own, outer_own, send, q_s, r_s = refs
    chunks, _, width = base.shape
    pairs = width // LANES
    sheets = own.shape[1] // chunks
    rows = width // sheets
    steps = yw.shape[0]

    flux = top_flux("gx", stages, own, got)
    line_of = {member: n for n, member in enumerate(sum(line_groups(chunks, sheets), []))}
    fields = []
    for y in range(chunks):
        spread = jnp.concatenate(
            [
                jnp.broadcast_to(flux[line_of[y, z] : line_of[y, z] + 1, :], (rows, LANES))
                for z in range(sheets)
            ],
            0,
        )
        fields.append(base[y] + response[y] * turned(to_y[...], spread))

    def target(k):
        at = slice(k * SUBLANES, (k + 1) * SUBLANES)
        return jnp.stack(
            [fields[y][at, m * LANES : (m + 1) * LANES] for y in range(chunks) for m in range(pairs)], 0
        )

    def keep(k, h):
        h_ref[k] = h

    ends = eliminate(target, steps, lambda k: yw[k], lambda k: yi[k], lambda k: yp[k], keep)
    for q in range(2):
        for i in range(chunks * pairs):
            q_s[q, i * SUBLANES : (i + 1) * SUBLANES, :] = ends[q][i]
    items = [
        tuple(q_s[q, pl.ds(s, chunks * pairs, stride=SUBLANES), :] for q in range(2))
        for s in range(SUBLANES)
    ]
    r_s[0], r_s[1] = join_tree(items, inner, inner_own)
    items = [tuple(r_s[q, y * pairs : (y + 1) * pairs, :] for q in range(2)) for y in range(chunks)]
    for n, q in enumerate(COEFS):
        send[q] = view[n]
    send[FIRST], send[LAST] = join_tree(items, outer, outer_own)


def y_target(own, got, base, response, yw, yi, yp, inner, outer, view, to_y):
    y_lines = yw.shape[1]
    pairs = view.shape[1]
    chunks = y_lines // pairs
    return pl.pallas_call(
        functools.partial(y_target_kernel, stages_of("gx")),
        out_shape=[
            shape_of(*yw.shape),
            shape_of(SUBLANES - 1, y_lines, LANES),
            shape_of(chunks - 1, pairs, LANES),
            shape_of(7, pairs, LANES),
        ],
        scratch_shapes=[
            pltpu.VMEM((2, y_lines * SUBLANES, LANES), F32),
            pltpu.VMEM((2, y_lines, LANES), F32),
        ],
        compiler_params=params(),
    )(own, got, base, response, yw, yi, yp, inner, outer, view, to_y)


def z_solve(zw, zi, field, at, keep):
    sheets = zi.shape[0]
    rhs, kept = None, []
    for z in range(sheets):
        rhs = field(z) if z == 0 else field(z) + zw[z - 1, at] * rhs
        kept.append(rhs * zi[z, at])
    value = kept[-1]
    keep(sheets - 1, value)
    for z in range(sheets - 2, -1, -1):
        value = zw[z, at] * value + kept[z]
        keep(z, value)


def finish_prepare_kernel(stages, *refs):
    ties = refs[: stages - 1]
    yw, yh, yp, inner, inner_own, outer, outer_own, zw, zi, t_ref, to_x = refs[stages - 1 : stages + 10]
    base, response, r_s, e_s, u_s = refs[stages + 10 :]
    chunks, sheets, rows, _ = base.shape
    each = LANES // rows
    pairs = sheets // each
    steps = yw.shape[0]
    lines = chunks * pairs

    ends, units = block_ends("gy", stages, ties)
    both = (
        (lambda i: outer_own[i], lambda i: inner_own[i], ends),
        (nothing, nothing, units),
    )
    for n, (upper, lower, (low, high)) in enumerate(both):
        for y, pair in enumerate(tree_ends(chunks, outer, upper, low, high)):
            for i in range(2):
                r_s[n, i, y * pairs : (y + 1) * pairs, :] = pair[i]
        for s, pair in enumerate(tree_ends(SUBLANES, inner, lower, r_s[n, 0], r_s[n, 1])):
            for i in range(2):
                e_s[n, i, pl.ds(s, lines, stride=SUBLANES), :] = pair[i]
    (low, value), (unit_low, unit) = (
        [
            jnp.stack([e_s[q, i, n * SUBLANES : (n + 1) * SUBLANES, :] for n in range(lines)], 0)
            for i in range(2)
        ]
        for q in range(2)
    )
    for k in range(steps - 1, -1, -1):
        w, p = yw[k], yp[k]
        value = w * value + (yh[k] + p * low)
        unit = w * unit + p * unit_low
        for y in range(chunks):
            for m in range(pairs):
                place = pl.ds(y * LANES + k, SUBLANES, stride=steps)
                u_s[0, m, place, :] = value[y * pairs + m]
                u_s[1, m, place, :] = unit[y * pairs + m]

    for y in range(chunks):
        part = part_of(y)
        fields = [turned(to_x[...], u_s[0, m, part, :]) for m in range(pairs)]

        def field(z):
            at = z % each * rows
            return fields[z // each][at : at + rows, :]

        def keep(z, value):
            base[y, z] = t_ref[z, :, part] + value

        z_solve(zw, zi, field, y, keep)
        for m in range(pairs):
            units = turned(to_x[...], u_s[1, m, part, :])
            for i in range(each):
                response[y, m * each + i] = units[i * rows : (i + 1) * rows, :]


def finish_prepare(ties, yw, yh, yp, inner, inner_own, outer, outer_own, zw, zi, t, to_x):
    sheets, rows, columns = t.shape
    chunks = columns // LANES
    pairs = sheets * rows // LANES
    lines = chunks * pairs
    field = shape_of(chunks, sheets, rows, LANES)
    return pl.pallas_call(
        functools.partial(finish_prepare_kernel, len(ties) + 1),
        out_shape=[field, field],
        scratch_shapes=[
            pltpu.VMEM((2, 2, lines, LANES), F32),
            pltpu.VMEM((2, 2, lines * SUBLANES, LANES), F32),
            pltpu.VMEM((2, pairs, columns, LANES), F32),
        ],
        compiler_params=params(),
        cost_estimate=pl.CostEstimate(flops=12 * t.size, bytes_accessed=20 * t.size, transcendentals=0),
    )(*ties, yw, yh, yp, inner, inner_own, outer, outer_own, zw, zi, t, to_x)


def finish_kernel(stages, own, got, base, response, zw, zi, to_x, out, o_s, sems):
    chunks, sheets, rows, _ = base.shape
    each = LANES // rows
    pairs = sheets // each
    copies, _, wide = o_s.shape

    flux = top_flux("gy", stages, own, got)
    spread = [
        turned(to_x[...], jnp.broadcast_to(flux[m : m + 1, :], (LANES, LANES))) for m in range(pairs)
    ]
    started = []
    for n in range(copies):
        for y in range(n * chunks // copies, (n + 1) * chunks // copies):
            part = part_of(y - n * chunks // copies)

            def field(z):
                at = z % each * rows
                return response[y, z] * spread[z // each][at : at + rows, :]

            def keep(z, value):
                o_s[n, z * rows : (z + 1) * rows, part] = base[y, z] + value

            z_solve(zw, zi, field, y, keep)
        copy = pltpu.make_async_copy(o_s.at[n], out.at[:, pl.ds(n * wide, wide)], sems.at[n])
        copy.start()
        started.append(copy)
    for copy in started:
        copy.wait()


def finish(own, got, base, response, zw, zi, to_x):
    chunks, sheets, rows, _ = base.shape
    copies = chunks
    return pl.pallas_call(
        functools.partial(finish_kernel, stages_of("gy")),
        out_shape=shape_of(sheets * rows, chunks * LANES),
        out_specs=ANYWHERE,
        scratch_shapes=[
            pltpu.VMEM((copies, sheets * rows, chunks * LANES // copies), F32),
            pltpu.SemaphoreType.DMA((copies,)),
        ],
        compiler_params=params(),
    )(own, got, base, response, zw, zi, to_x).reshape(sheets, rows, chunks * LANES)


def per_device(temperature, base, locations, energy):
    columns = temperature.shape[2]
    gy = lax.axis_size("gy")
    t, b, loc, heat, packed = load(temperature, base, locations[None], energy[None])
    near = swap(packed, "gy", 1)
    far = lax.ppermute(packed, "gy", [(i, ((i + 1) % gy ^ 1) - 1 if i else gy - 1) for i in range(gy)])
    c, total, xw, xi, xp, x_links, x_view, xm, ends, t_steps = x_factor(loc, heat, t, b, columns * gy, packed)
    xh, x_own, view = x_target(packed, t, total, near, far, xw, xi, xp, x_links, x_view, ends)
    yw, yi, yp, inner, outer, y_view, to_y, to_x = y_factor(c, x_view)
    zw, zi = z_factor(c, view)
    own, got, ties = gather_line(view, "gx", 2, (y_view, zw))
    base, response = y_prepare(
        ties, xw, xh, xm, xp, x_links, x_own, t_steps, to_y, columns // LANES
    )
    yh, inner_own, outer_own, view = y_target(
        own, got, base, response, yw, yi, yp, inner, outer, y_view, to_y
    )
    own, got, ties = gather_line(view, "gy", cross=True)
    base, response = finish_prepare(
        ties, yw, yh, yp, inner, inner_own, outer, outer_own, zw, zi, t, to_x
    )
    return finish(own, got, base, response, zw, zi, to_x)


def solution(mesh):
    in_specs = (P(None, "gx", "gy"), P(None, "gx", "gy"), P(), P())
    out_specs = P(None, "gx", "gy")
    return jax.shard_map(
        per_device, mesh=mesh, in_specs=in_specs, out_specs=out_specs, check_vma=False
    )
```

```python
import functools

import jax
import jax.numpy as jnp
from jax import lax
from jax.experimental import pallas as pl
from jax.experimental.pallas import tpu as pltpu
from jax.sharding import PartitionSpec as P

RATE = 2000.0
THERMAL_GROWTH = 0.8
LANES = 128
SUBLANES = 8
F32 = jnp.float32
MIB = 1024 * 1024
ANYWHERE = pl.BlockSpec(memory_space=pl.ANY)
IN_HBM = pl.BlockSpec(memory_space=pltpu.HBM)
IN_VMEM = pl.BlockSpec(memory_space=pltpu.VMEM)

R00, R0L, RLL, FIRST, LAST, C0, CL = range(7)
COEFS = (R00, R0L, RLL, C0, CL)


def params(limit=40):
    return pltpu.CompilerParams(vmem_limit_bytes=limit * MIB)


def shape_of(*sizes):
    return jax.ShapeDtypeStruct(sizes, F32)


def half_conduct(base, temperature):
    return base * (0.5 * RATE + (0.5 * RATE * THERMAL_GROWTH) * temperature)


def inverse(x):
    guess = pl.reciprocal(x, approx=True)
    return guess * (2.0 - x * guess)


def join_coefs(a, b):
    face = a[CL] + b[C0]
    inv = face * inverse(1.0 + face * (a[RLL] + b[R00]))
    left = a[R0L] * inv
    right = b[R0L] * inv
    joined = {
        R00: a[R00] - left * a[R0L],
        R0L: left * b[R0L],
        RLL: b[RLL] - right * b[R0L],
        C0: a[C0],
        CL: b[CL],
    }
    return joined, (inv, right, left)


def join_targets(a, b, links):
    inv, right, left = links
    jump = b[0] - a[1]
    return (a[0] + left * jump, b[1] - right * jump), jump * inv


def between(own, right, left, low, high):
    return own + right * high - left * low


def tree(items, join):
    levels = []
    while len(items) > 1:
        pairs = [join(items[i], items[i + 1]) for i in range(0, len(items), 2)]
        items = [p[0] for p in pairs]
        levels.append([p[1] for p in pairs])
    return items[0], levels


def descend(levels, low, high):
    ends = [(low, high)]
    for level in reversed(levels):
        below = []
        for (lo, hi), (own, right, left) in zip(ends, level):
            flux = between(own, right, left, lo, hi)
            below += [(lo, flux), (-flux, hi)]
        ends = below
    return ends


def node_offsets(leaves):
    offsets, at, count = [], 0, leaves // 2
    while count:
        offsets.append((at, count))
        at += count
        count //= 2
    return offsets


def factor(cond, steps, keep):
    here = cond(0)
    c_first = here
    one = jnp.ones_like(here)
    ground, path, first_first = one, one, None
    for k in range(steps - 1):
        following = cond(k + 1)
        face = here + following
        inv = inverse(ground + face)
        w = face * inv
        p = path * inv
        keep(k, w, inv, p)
        step = path * p
        first_first = step if first_first is None else first_first + step
        path = path * w
        ground = 1.0 + w * ground
        here = following
    inv = inverse(ground)
    p = path * inv
    keep(steps - 1, inv, inv, p)
    return {R00: first_first + path * p, R0L: p, RLL: inv, C0: c_first, CL: here}


def eliminate(target, steps, w, inv, p, keep):
    rhs = target(0)
    first = None
    for k in range(steps):
        h = rhs * inv(k)
        keep(k, h)
        step = rhs * p(k)
        first = step if first is None else first + step
        if k < steps - 1:
            rhs = target(k + 1) + w(k) * rhs
    return first, h


def is_odd(axis):
    return lax.axis_index(axis) % 2 == 1


def fold(cells, used):
    steps = cells.shape[0] // SUBLANES
    total = cells[pl.ds(0, SUBLANES, stride=steps), :]
    lane = lax.broadcasted_iota(jnp.int32, total.shape, 1)
    for k in range(1, steps):
        part = pltpu.roll(cells[pl.ds(k, SUBLANES, stride=steps), :], k * used, 1)
        total = jnp.where(lane // used == k, part, total)
    return total


def load_kernel(t_hbm, b_hbm, loc_hbm, energy_hbm, t_out, b_out, loc, energy, packed, swapped, cells, sems):
    sheets, rows, columns = t_hbm.shape
    parts = [(0, LANES), (columns - LANES, LANES), (LANES, columns - 2 * LANES)]
    copies = []
    for n, (start, size) in enumerate(parts):
        part = pl.ds(start, size)
        for i, (src, dst) in enumerate(((t_hbm, t_out), (b_hbm, b_out))):
            copies.append(
                pltpu.make_async_copy(src.at[:, :, part], dst.at[:, :, part], sems.at[i, n])
            )
    copies.append(pltpu.make_async_copy(loc_hbm, loc, sems.at[2, 0]))
    copies.append(pltpu.make_async_copy(energy_hbm, energy, sems.at[2, 1]))
    for copy in copies:
        copy.start()
    lane = lax.broadcasted_iota(jnp.int32, (rows, LANES), 1)
    edge_t = jnp.zeros((rows, LANES), F32)
    edge_c = edge_t
    for side, source in enumerate((0, LANES - 1)):
        for copy in copies[2 * side : 2 * side + 2]:
            copy.wait()
        part = slice(parts[side][0], parts[side][0] + LANES)
        for z in range(sheets):
            t = t_out[z, :, part]
            c = half_conduct(b_out[z, :, part], t)
            place = lane == sheets * side + z
            edge_t = jnp.where(place, t[:, source : source + 1], edge_t)
            edge_c = jnp.where(place, c[:, source : source + 1], edge_c)
    cells[0], cells[1] = edge_t, edge_c
    in_low = lax.broadcasted_iota(jnp.int32, (SUBLANES, LANES), 1) % (2 * sheets) < sheets
    for i in range(2):
        at = slice(i * SUBLANES, (i + 1) * SUBLANES)
        folded = fold(cells.at[i], 2 * sheets)
        packed[at, :] = folded
        swapped[at, :] = jnp.where(
            in_low, pltpu.roll(folded, LANES - sheets, 1), pltpu.roll(folded, sheets, 1)
        )
    for copy in copies[4:]:
        copy.wait()


def load(temperature, base, locations, energy):
    sheets, rows, columns = temperature.shape
    assert rows // SUBLANES * 2 * sheets <= LANES and columns > 2 * LANES
    operands = (temperature, base, locations, energy)
    return pl.pallas_call(
        load_kernel,
        in_specs=[IN_HBM] * 4,
        out_shape=[pltpu.VMEM(v.shape, v.dtype) for v in operands]
        + [pltpu.VMEM((2 * SUBLANES, LANES), F32)] * 2,
        scratch_shapes=[pltpu.VMEM((2, rows, LANES), F32), pltpu.SemaphoreType.DMA((3, 3))],
        compiler_params=params(),
    )(*[pltpu.with_memory_space_constraint(v, pltpu.HBM) for v in operands])


def source_plane(loc, energy, rows, columns, plate):
    place = loc[...]
    count = place.shape[1]
    local_x = place // plate - lax.axis_index("gx") * rows
    local_y = place % plate - lax.axis_index("gy") * columns
    in_x = lax.broadcasted_iota(jnp.int32, (rows, count), 0) == local_x
    in_y = lax.broadcasted_iota(jnp.int32, (columns, count), 0) == local_y
    by_y = jnp.where(in_y, 1.0, 0.0).astype(jnp.bfloat16)
    left = energy[...]
    plane = None
    for _ in range(3):
        part = left.astype(jnp.bfloat16).astype(F32)
        left = left - part
        term = lax.dot_general(
            jnp.where(in_x, part, 0.0).astype(jnp.bfloat16),
            by_y,
            (((1,), (1,)), ((), ())),
            preferred_element_type=F32,
        )
        plane = term if plane is None else plane + term
    return plane


def part_of(y):
    return slice(y * LANES, (y + 1) * LANES)


def line_groups(chunks, sheets):
    order = [0, chunks - 1] + list(range(1, chunks - 1))
    return [[(y, z) for y in order[i : i + 2] for z in range(sheets)] for i in range(0, chunks, 2)]


def x_eliminate(cells, members, first_line, w_ref, i_ref, p_ref, h_ref, h_line, q_s):
    steps = w_ref.shape[0]
    at = slice(first_line, first_line + len(members))
    kept_at = slice(h_line, h_line + len(members))

    def target(k):
        return jnp.stack([cells(y, z, k) for y, z in members], 0)

    def keep(k, h):
        h_ref[k, kept_at] = h

    ends = eliminate(
        target, steps, lambda k: w_ref[k, at], lambda k: i_ref[k, at], lambda k: p_ref[k, at], keep
    )
    for q in range(2):
        for i in range(len(members)):
            first = (first_line + i) * SUBLANES
            q_s[q, first : first + SUBLANES, :] = ends[q][i]


def x_factor_kernel(plate, loc, energy, t_ref, b_ref, after, *refs):
    c_ref, total_ref, w_ref, i_ref, p_ref, links, view, h_ref, ends_ref, t_out, q_s, t_s = refs
    chunks, sheets, rows, _ = c_ref.shape
    lines = chunks * sheets
    steps = rows // SUBLANES
    plane = source_plane(loc, energy, rows, chunks * LANES, plate)

    lane = lax.broadcasted_iota(jnp.int32, (SUBLANES, LANES), 1)
    is_first, is_last = lane == 0, lane == LANES - 1
    for r in range(steps):
        at = slice(r * SUBLANES, (r + 1) * SUBLANES)
        before_t, before_c = None, None
        for z in range(sheets):
            ts = [t_ref[z, at, part_of(y)] for y in range(chunks)]
            cs = [half_conduct(b_ref[z, at, part_of(y)], ts[y]) for y in range(chunks)]
            t_turned = [pltpu.roll(v, LANES - 1, 1) for v in ts]
            c_turned = [pltpu.roll(v, LANES - 1, 1) for v in cs]
            flux = []
            for y in range(chunks):
                if y < chunks - 1:
                    t_next = jnp.where(is_last, t_turned[y + 1], t_turned[y])
                    c_next = jnp.where(is_last, c_turned[y + 1], c_turned[y])
                    flux.append((cs[y] + c_next) * (t_next - ts[y]))
                else:
                    inside = (cs[y] + c_turned[y]) * (t_turned[y] - ts[y])
                    flux.append(jnp.where(is_last, 0.0, inside))
            turned = [pltpu.roll(v, 1, 1) for v in flux]
            for y in range(chunks):
                from_low = jnp.where(is_first, turned[y - 1] if y else 0.0, turned[y])
                total = ts[y] + (flux[y] - from_low)
                if z == 0:
                    total = total + plane[at, part_of(y)]
                else:
                    across = (before_c[y] + cs[y]) * (ts[y] - before_t[y])
                    total = total - across
                    total_ref[y, z - 1, at, :] += across
                total_ref[y, z, at, :] = total
                c_ref[y, z, at, :] = cs[y]
                t_s[y, z, at, :] = ts[y]
            before_t, before_c = ts, cs

    at = 0
    for n, members in enumerate(line_groups(chunks, sheets)):

        def cond(k):
            return jnp.stack([c_ref[y, z, pl.ds(k, SUBLANES, stride=steps), :] for y, z in members], 0)

        def keep(k, w, inv, p):
            w_ref[k, at : at + len(members)] = w
            i_ref[k, at : at + len(members)] = inv
            p_ref[k, at : at + len(members)] = p

        block = factor(cond, steps, keep)
        for i, q in enumerate(COEFS):
            for j in range(len(members)):
                first = (at + j) * SUBLANES
                q_s[i, first : first + SUBLANES, :] = block[q][j]
        if n > 0:
            x_eliminate(
                lambda y, z, k: total_ref[y, z, pl.ds(k, SUBLANES, stride=steps), :],
                members, at, w_ref, i_ref, p_ref, h_ref, at - 2 * sheets, ends_ref,
            )
        for k in range(steps):
            for i, (y, z) in enumerate(members):
                t_out[k, at + i] = t_s[y, z, pl.ds(k, SUBLANES, stride=steps), :]
        at += len(members)

    segments = [
        {q: q_s[n, pl.ds(s, lines, stride=SUBLANES), :] for n, q in enumerate(COEFS)}
        for s in range(SUBLANES)
    ]
    whole, levels = tree(segments, join_coefs)
    for (offset, _), level in zip(node_offsets(SUBLANES), levels):
        for n, values in enumerate(level):
            for i in range(3):
                links[offset + n, i] = values[i]
    for n, q in enumerate(COEFS):
        view[n] = whole[q]


def x_factor(loc, energy, t, b, plate, after):
    sheets, rows, columns = t.shape
    chunks = columns // LANES
    lines = chunks * sheets
    steps = rows // SUBLANES
    field = shape_of(chunks, sheets, rows, LANES)
    stored = shape_of(steps, lines, SUBLANES, LANES)
    return pl.pallas_call(
        functools.partial(x_factor_kernel, plate),
        in_specs=[IN_VMEM] * 4 + [ANYWHERE],
        out_shape=[
            field,
            field,
            stored,
            stored,
            stored,
            shape_of(SUBLANES - 1, 3, lines, LANES),
            shape_of(len(COEFS), lines, LANES),
            shape_of(steps, max(1, lines - 2 * sheets), SUBLANES, LANES),
            shape_of(2, lines * SUBLANES, LANES),
            stored,
        ],
        scratch_shapes=[
            pltpu.VMEM((len(COEFS), lines * SUBLANES, LANES), F32),
            pltpu.VMEM((chunks, sheets, rows, LANES), F32),
        ],
        compiler_params=params(),
        cost_estimate=pl.CostEstimate(flops=40 * t.size, bytes_accessed=28 * t.size, transcendentals=0),
    )(loc, energy, t, b, after)


def x_target_kernel(own_cells, total_ref, near, far, *refs):
    w_ref, i_ref, p_ref, links, view, ends_ref, h_ref, own, send, q_s = refs
    chunks, sheets, rows, _ = total_ref.shape
    lines = chunks * sheets
    steps = rows // SUBLANES

    place = lax.axis_index("gy")
    inner = (place > 0) & (place < lax.axis_size("gy") - 1)
    lane = lax.broadcasted_iota(jnp.int32, (SUBLANES, LANES), 1)
    side = 2 * sheets
    is_near = (lane % side >= sheets).astype(jnp.int32) == place % 2
    t, c = (
        jnp.where(is_near, near[at, :], jnp.where(inner, far[at, :], 0.0))
        for at in (slice(0, SUBLANES), slice(SUBLANES, 2 * SUBLANES))
    )
    face = jnp.where(c > 0.0, own_cells[SUBLANES:, :] + c, 0.0)
    flux = face * (t - own_cells[:SUBLANES, :])

    def cells(y, z, k):
        at = k * side + (sheets + z if y == 0 else z)
        edge = 0 if y == 0 else LANES - 1
        inflow = jnp.where(lane == edge, flux[:, at : at + 1], 0.0)
        return total_ref[y, z, pl.ds(k, SUBLANES, stride=steps), :] + inflow

    members = line_groups(chunks, sheets)[0]
    x_eliminate(cells, members, 0, w_ref, i_ref, p_ref, h_ref, 0, q_s)
    split = len(members)
    items = [
        tuple(
            jnp.concatenate(
                [
                    q_s[q, pl.ds(s, split, stride=SUBLANES), :],
                    ends_ref[q, pl.ds(split * SUBLANES + s, lines - split, stride=SUBLANES), :],
                ],
                0,
            )
            for q in range(2)
        )
        for s in range(SUBLANES)
    ]
    for offset, count in node_offsets(SUBLANES):
        joined = []
        for n in range(count):
            ties = tuple(links[offset + n, i] for i in range(3))
            both, flux = join_targets(items[2 * n], items[2 * n + 1], ties)
            own[offset + n] = flux
            joined.append(both)
        items = joined
    for n, q in enumerate(COEFS):
        send[q] = view[n]
    send[FIRST], send[LAST] = items[0]


def x_target(own_cells, total, near, far, w, inv, p, links, view, ends):
    chunks, sheets, rows, _ = total.shape
    lines = chunks * sheets
    steps = rows // SUBLANES
    return pl.pallas_call(
        x_target_kernel,
        out_shape=[
            shape_of(steps, 2 * sheets, SUBLANES, LANES),
            shape_of(SUBLANES - 1, lines, LANES),
            shape_of(7, lines, LANES),
        ],
        scratch_shapes=[
            pltpu.VMEM((2, 2 * sheets * SUBLANES, LANES), F32),
        ],
        compiler_params=params(),
    )(own_cells, total, near, far, w, inv, p, links, view, ends)


def stages_of(axis):
    return lax.axis_size(axis).bit_length() - 1


def swap(value, axis, flip):
    count = lax.axis_size(axis)
    return lax.ppermute(value, axis, [(i, i ^ flip) for i in range(count)])


def on_right(axis, stage):
    return (lax.axis_index(axis) >> stage) % 2 == 1


def toward(right, block):
    return (
        jnp.where(right, block[R00], block[RLL]),
        jnp.where(right, block[FIRST], block[LAST]),
        jnp.where(right, block[C0], block[CL]),
    )


def join(a, b):
    joined, ties = join_coefs(a, b)
    (joined[FIRST], joined[LAST]), flux = join_targets((a[FIRST], a[LAST]), (b[FIRST], b[LAST]), ties)
    return joined, (flux, ties[1], ties[2])


def ordered(right, own, other):
    first = [jnp.where(right, theirs, mine) for mine, theirs in zip(own, other)]
    second = [jnp.where(right, mine, theirs) for mine, theirs in zip(own, other)]
    return first, second


def join_kernel(axis, stage, width, last, *refs):
    count = 1 << width
    blocks = [[refs[i][q] for q in range(7)] for i in range(count)]
    send = refs[-1 - width]
    links = refs[-width:]
    for bit in range(width):
        right = on_right(axis, stage + bit)
        for i in range(count):
            if not i >> bit & 1:
                j = i | 1 << bit
                blocks[i], blocks[j] = ordered(right, blocks[i], blocks[j])
    for bit in range(width):
        pairs = [join(blocks[i], blocks[i + 1]) for i in range(0, len(blocks), 2)]
        blocks = [p[0] for p in pairs]
        ties = [p[1] for p in pairs]
        for upper in range(bit + 1, width):
            right = on_right(axis, stage + upper)
            ties = [
                tuple(jnp.where(right, v, u) for u, v in zip(ties[i], ties[i + 1]))
                for i in range(0, len(ties), 2)
            ]
        for i in range(3):
            links[bit][i] = ties[0][i]
    (whole,) = blocks
    if last:
        for n, value in enumerate(toward(on_right(axis, stage + width), whole)):
            send[n] = value
    else:
        for q in range(7):
            send[q] = whole[q]


def join_stage(own, got, axis, stage, width, last, after):
    lines = own.shape[1]
    return pl.pallas_call(
        functools.partial(join_kernel, axis, stage, width, last),
        in_specs=[IN_VMEM] * (1 + len(got)) + [ANYWHERE] * len(after),
        out_shape=[shape_of(3 if last else 7, lines, LANES)] + [shape_of(3, lines, LANES)] * width,
        compiler_params=params(),
    )(own, *got, *after)


def gather_line(view, axis, widest=1, meanwhile=(), cross=False):
    stages = stages_of(axis)
    links, stage = [], 0
    while stage < stages - 1:
        width = min(widest, stages - 1 - stage)
        got = [swap(view, axis, flip << stage) for flip in range(1, 1 << width)]
        last = stage + width == stages - 1
        view, *ties = join_stage(view, got, axis, stage, width, last, meanwhile)
        links += ties
        stage += width
        meanwhile = ()
    return view, swap(view, axis, 1 << stage | (cross and stage > 0)), links


def top_flux(axis, stages, own, got):
    right = on_right(axis, stages - 1)
    face = own[2] + got[2]
    jump = jnp.where(right, own[1] - got[1], got[1] - own[1])
    return jump * face * inverse(1.0 + face * (own[0] + got[0]))


def block_ends(axis, stages, links):
    shape = links[0].shape[1:] if links else None
    right = on_right(axis, stages - 1)
    zero = jnp.zeros(shape, F32)
    low, high = zero, zero
    unit_low = zero + jnp.where(right, -1.0, 0.0)
    unit_high = zero + jnp.where(right, 0.0, 1.0)
    for stage in range(stages - 2, -1, -1):
        tie = links[stage]
        right = on_right(axis, stage)
        flux = between(tie[0], tie[1], tie[2], low, high)
        unit = between(0.0, tie[1], tie[2], unit_low, unit_high)
        low, high = jnp.where(right, -flux, low), jnp.where(right, high, flux)
        unit_low, unit_high = jnp.where(right, -unit, unit_low), jnp.where(right, unit_high, unit)
    return (low, high), (unit_low, unit_high)


def natural(index, parts):
    span = SUBLANES * parts
    local = index % span
    return index - local + local % SUBLANES * parts + local // SUBLANES


def turn_matrix(shape, from_natural, parts):
    row = lax.broadcasted_iota(jnp.int32, shape, 0)
    column = lax.broadcasted_iota(jnp.int32, shape, 1) % LANES
    hit = natural(row, parts) == column if from_natural else row == natural(column, parts)
    return jnp.where(hit, 1.0, 0.0).astype(jnp.bfloat16)


def turned(matrix, field):
    high = field.astype(jnp.bfloat16)
    low = (field - high.astype(F32)).astype(jnp.bfloat16)
    both = jnp.concatenate([high, low], 1)
    return lax.dot_general(
        matrix, both, (((1,), (1,)), ((), ())), preferred_element_type=F32
    )


def y_factor_kernel(c_ref, after, w_ref, i_ref, p_ref, inner, outer, view, to_y, to_x, c_s, q_s, r_s):
    chunks, sheets, rows, _ = c_ref.shape
    each = LANES // rows
    pairs = sheets // each
    x_steps = rows // SUBLANES
    steps = LANES // SUBLANES
    to_y[...] = turn_matrix(to_y.shape, True, steps)
    to_x[...] = turn_matrix(to_x.shape, False, x_steps)
    for m in range(pairs):
        for y in range(chunks):
            block = jnp.concatenate(
                [
                    c_ref[y, m * each + i, pl.ds(k, SUBLANES, stride=x_steps), :]
                    for i in range(each)
                    for k in range(x_steps)
                ],
                0,
            )
            c_s[m, part_of(y), :] = block.T

    members = [(y, m) for y in range(chunks) for m in range(pairs)]
    lines = len(members)

    def cond(k):
        return jnp.stack([c_s[m, pl.ds(y * LANES + k, SUBLANES, stride=steps), :] for y, m in members], 0)

    def keep(k, w, inv, p):
        w_ref[k] = w
        i_ref[k] = inv
        p_ref[k] = p

    block = factor(cond, steps, keep)
    for n, q in enumerate(COEFS):
        for i in range(lines):
            q_s[n, i * SUBLANES : (i + 1) * SUBLANES, :] = block[q][i]
    segments = [
        {q: q_s[n, pl.ds(s, lines, stride=SUBLANES), :] for n, q in enumerate(COEFS)}
        for s in range(SUBLANES)
    ]
    whole, levels = tree(segments, join_coefs)
    for (offset, _), level in zip(node_offsets(SUBLANES), levels):
        for n, values in enumerate(level):
            for i in range(3):
                inner[offset + n, i] = values[i]
    for n, q in enumerate(COEFS):
        r_s[n] = whole[q]
    parts = [
        {q: r_s[n, y * pairs : (y + 1) * pairs, :] for n, q in enumerate(COEFS)} for y in range(chunks)
    ]
    whole, levels = tree(parts, join_coefs)
    for (offset, _), level in zip(node_offsets(chunks), levels):
        for n, values in enumerate(level):
            for i in range(3):
                outer[offset + n, i] = values[i]
    for n, q in enumerate(COEFS):
        view[n] = whole[q]


def y_factor(c, after):
    chunks, sheets, rows, _ = c.shape
    pairs = sheets * rows // LANES
    lines = chunks * pairs
    stored = shape_of(LANES // SUBLANES, lines, SUBLANES, LANES)
    matrix = jax.ShapeDtypeStruct((LANES, 2 * LANES), jnp.bfloat16)
    return pl.pallas_call(
        y_factor_kernel,
        in_specs=[IN_VMEM, ANYWHERE],
        out_shape=[
            stored,
            stored,
            stored,
            shape_of(SUBLANES - 1, 3, lines, LANES),
            shape_of(chunks - 1, 3, pairs, LANES),
            shape_of(len(COEFS), pairs, LANES),
            matrix,
            matrix,
        ],
        scratch_shapes=[
            pltpu.VMEM((pairs, chunks * LANES, LANES), F32),
            pltpu.VMEM((len(COEFS), lines * SUBLANES, LANES), F32),
            pltpu.VMEM((len(COEFS), lines, LANES), F32),
        ],
        compiler_params=params(),
        cost_estimate=pl.CostEstimate(flops=20 * c.size, bytes_accessed=16 * c.size, transcendentals=0),
    )(c, after)


def z_factor_kernel(c_ref, after, w_ref, i_ref):
    sheets = c_ref.shape[1]
    ground = 1.0
    for z in range(sheets - 1):
        face = c_ref[:, z] + c_ref[:, z + 1]
        inv = inverse(ground + face)
        w = face * inv
        i_ref[z] = inv
        w_ref[z] = w
        ground = 1.0 + w * ground
    i_ref[sheets - 1] = inverse(ground)


def z_factor(c, after):
    chunks, sheets, rows, _ = c.shape
    return pl.pallas_call(
        z_factor_kernel,
        in_specs=[IN_VMEM, ANYWHERE],
        out_shape=[
            shape_of(sheets - 1, chunks, rows, LANES),
            shape_of(sheets, chunks, rows, LANES),
        ],
        compiler_params=params(),
        cost_estimate=pl.CostEstimate(flops=10 * c.size, bytes_accessed=12 * c.size, transcendentals=0),
    )(c, after)


def join_tree(items, links, own):
    for offset, count in node_offsets(len(items)):
        joined = []
        for n in range(count):
            tie = tuple(links[offset + n, i] for i in range(3))
            both, flux = join_targets(items[2 * n], items[2 * n + 1], tie)
            own[offset + n] = flux
            joined.append(both)
        items = joined
    return items[0]


def tree_ends(leaves, links, own, low, high):
    levels = [
        [(own(offset + n), links[offset + n, 1], links[offset + n, 2]) for n in range(count)]
        for offset, count in node_offsets(leaves)
    ]
    return descend(levels, low, high)


def nothing(node):
    return 0.0


def y_prepare_kernel(stages, *refs):
    ties = refs[: stages - 1]
    xw, xh, xm, xp, x_links, x_own, t_ref, to_y = refs[stages - 1 : stages + 7]
    base, response, f_s, g_s = refs[stages + 7 :]
    x_steps, lines = xw.shape[:2]
    chunks = base.shape[0]
    sheets = lines // chunks
    rows = x_steps * SUBLANES

    ends, units = block_ends("gx", stages, ties)
    for n, (own, (low, high)) in enumerate(((lambda i: x_own[i], ends), (nothing, units))):
        for s, pair in enumerate(tree_ends(SUBLANES, x_links, own, low, high)):
            for i in range(2):
                f_s[n, i, pl.ds(s, lines, stride=SUBLANES), :] = pair[i]
    first = 0
    for n, members in enumerate(line_groups(chunks, sheets)):
        at = slice(first, first + len(members))
        h_ref_of, h_at = (xh, at) if n == 0 else (xm, slice(first - 2 * sheets, at.stop - 2 * sheets))
        (low, value), (unit_low, unit) = (
            [
                jnp.stack(
                    [f_s[q, i, j * SUBLANES : (j + 1) * SUBLANES, :] for j in range(at.start, at.stop)], 0
                )
                for i in range(2)
            ]
            for q in range(2)
        )
        for k in range(x_steps - 1, -1, -1):
            w, p = xw[k, at], xp[k, at]
            value = w * value + (h_ref_of[k, h_at] + p * low)
            unit = w * unit + p * unit_low
            field = value - t_ref[k, at]
            for j, (y, z) in enumerate(members):
                place = z * rows + k * SUBLANES
                g_s[0, y, place : place + SUBLANES, :] = field[j]
                g_s[1, y, place : place + SUBLANES, :] = unit[j]
        first = at.stop

    for y in range(chunks):
        base[y] = turned(to_y[...], g_s[0, y])
        response[y] = turned(to_y[...], g_s[1, y])


def y_prepare(ties, xw, xh, xm, xp, x_links, x_own, t, to_y, chunks):
    x_steps, lines = xw.shape[:2]
    width = lines // chunks * x_steps * SUBLANES
    field = shape_of(chunks, LANES, width)
    return pl.pallas_call(
        functools.partial(y_prepare_kernel, len(ties) + 1),
        out_shape=[field, field],
        scratch_shapes=[
            pltpu.VMEM((2, 2, lines * SUBLANES, LANES), F32),
            pltpu.VMEM((2, chunks, width, LANES), F32),
        ],
        compiler_params=params(),
        cost_estimate=pl.CostEstimate(flops=8 * t.size, bytes_accessed=16 * t.size, transcendentals=0),
    )(*ties, xw, xh, xm, xp, x_links, x_own, t, to_y)


def y_target_kernel(stages, own, got, base, response, yw, yi, yp, inner, outer, view, to_y, *refs):
    h_ref, inner_own, outer_own, send, q_s, r_s = refs
    chunks, _, width = base.shape
    pairs = width // LANES
    sheets = own.shape[1] // chunks
    rows = width // sheets
    steps = yw.shape[0]

    flux = top_flux("gx", stages, own, got)
    line_of = {member: n for n, member in enumerate(sum(line_groups(chunks, sheets), []))}
    fields = []
    for y in range(chunks):
        spread = jnp.concatenate(
            [
                jnp.broadcast_to(flux[line_of[y, z] : line_of[y, z] + 1, :], (rows, LANES))
                for z in range(sheets)
            ],
            0,
        )
        fields.append(base[y] + response[y] * turned(to_y[...], spread))

    def target(k):
        at = slice(k * SUBLANES, (k + 1) * SUBLANES)
        return jnp.stack(
            [fields[y][at, m * LANES : (m + 1) * LANES] for y in range(chunks) for m in range(pairs)], 0
        )

    def keep(k, h):
        h_ref[k] = h

    ends = eliminate(target, steps, lambda k: yw[k], lambda k: yi[k], lambda k: yp[k], keep)
    for q in range(2):
        for i in range(chunks * pairs):
            q_s[q, i * SUBLANES : (i + 1) * SUBLANES, :] = ends[q][i]
    items = [
        tuple(q_s[q, pl.ds(s, chunks * pairs, stride=SUBLANES), :] for q in range(2))
        for s in range(SUBLANES)
    ]
    r_s[0], r_s[1] = join_tree(items, inner, inner_own)
    items = [tuple(r_s[q, y * pairs : (y + 1) * pairs, :] for q in range(2)) for y in range(chunks)]
    for n, q in enumerate(COEFS):
        send[q] = view[n]
    send[FIRST], send[LAST] = join_tree(items, outer, outer_own)


def y_target(own, got, base, response, yw, yi, yp, inner, outer, view, to_y):
    y_lines = yw.shape[1]
    pairs = view.shape[1]
    chunks = y_lines // pairs
    return pl.pallas_call(
        functools.partial(y_target_kernel, stages_of("gx")),
        out_shape=[
            shape_of(*yw.shape),
            shape_of(SUBLANES - 1, y_lines, LANES),
            shape_of(chunks - 1, pairs, LANES),
            shape_of(7, pairs, LANES),
        ],
        scratch_shapes=[
            pltpu.VMEM((2, y_lines * SUBLANES, LANES), F32),
            pltpu.VMEM((2, y_lines, LANES), F32),
        ],
        compiler_params=params(),
    )(own, got, base, response, yw, yi, yp, inner, outer, view, to_y)


def z_solve(zw, zi, field, at, keep):
    sheets = zi.shape[0]
    rhs, kept = None, []
    for z in range(sheets):
        rhs = field(z) if z == 0 else field(z) + zw[z - 1, at] * rhs
        kept.append(rhs * zi[z, at])
    value = kept[-1]
    keep(sheets - 1, value)
    for z in range(sheets - 2, -1, -1):
        value = zw[z, at] * value + kept[z]
        keep(z, value)


def finish_prepare_kernel(stages, *refs):
    ties = refs[: stages - 1]
    yw, yh, yp, inner, inner_own, outer, outer_own, zw, zi, t_ref, to_x = refs[stages - 1 : stages + 10]
    base, response, r_s, e_s, u_s = refs[stages + 10 :]
    chunks, sheets, rows, _ = base.shape
    each = LANES // rows
    pairs = sheets // each
    steps = yw.shape[0]
    lines = chunks * pairs

    ends, units = block_ends("gy", stages, ties)
    both = (
        (lambda i: outer_own[i], lambda i: inner_own[i], ends),
        (nothing, nothing, units),
    )
    for n, (upper, lower, (low, high)) in enumerate(both):
        for y, pair in enumerate(tree_ends(chunks, outer, upper, low, high)):
            for i in range(2):
                r_s[n, i, y * pairs : (y + 1) * pairs, :] = pair[i]
        for s, pair in enumerate(tree_ends(SUBLANES, inner, lower, r_s[n, 0], r_s[n, 1])):
            for i in range(2):
                e_s[n, i, pl.ds(s, lines, stride=SUBLANES), :] = pair[i]
    (low, value), (unit_low, unit) = (
        [
            jnp.stack([e_s[q, i, n * SUBLANES : (n + 1) * SUBLANES, :] for n in range(lines)], 0)
            for i in range(2)
        ]
        for q in range(2)
    )
    for k in range(steps - 1, -1, -1):
        w, p = yw[k], yp[k]
        value = w * value + (yh[k] + p * low)
        unit = w * unit + p * unit_low
        for y in range(chunks):
            for m in range(pairs):
                place = pl.ds(y * LANES + k, SUBLANES, stride=steps)
                u_s[0, m, place, :] = value[y * pairs + m]
                u_s[1, m, place, :] = unit[y * pairs + m]

    for y in range(chunks):
        part = part_of(y)
        fields = [turned(to_x[...], u_s[0, m, part, :]) for m in range(pairs)]

        def field(z):
            at = z % each * rows
            return fields[z // each][at : at + rows, :]

        def keep(z, value):
            base[y, z] = t_ref[z, :, part] + value

        z_solve(zw, zi, field, y, keep)
        for m in range(pairs):
            units = turned(to_x[...], u_s[1, m, part, :])
            for i in range(each):
                response[y, m * each + i] = units[i * rows : (i + 1) * rows, :]


def finish_prepare(ties, yw, yh, yp, inner, inner_own, outer, outer_own, zw, zi, t, to_x):
    sheets, rows, columns = t.shape
    chunks = columns // LANES
    pairs = sheets * rows // LANES
    lines = chunks * pairs
    field = shape_of(chunks, sheets, rows, LANES)
    return pl.pallas_call(
        functools.partial(finish_prepare_kernel, len(ties) + 1),
        out_shape=[field, field],
        scratch_shapes=[
            pltpu.VMEM((2, 2, lines, LANES), F32),
            pltpu.VMEM((2, 2, lines * SUBLANES, LANES), F32),
            pltpu.VMEM((2, pairs, columns, LANES), F32),
        ],
        compiler_params=params(),
        cost_estimate=pl.CostEstimate(flops=12 * t.size, bytes_accessed=20 * t.size, transcendentals=0),
    )(*ties, yw, yh, yp, inner, inner_own, outer, outer_own, zw, zi, t, to_x)


def finish_kernel(stages, own, got, base, response, zw, zi, to_x, out, o_s, sems):
    chunks, sheets, rows, _ = base.shape
    each = LANES // rows
    pairs = sheets // each
    copies, _, wide = o_s.shape

    flux = top_flux("gy", stages, own, got)
    spread = [
        turned(to_x[...], jnp.broadcast_to(flux[m : m + 1, :], (LANES, LANES))) for m in range(pairs)
    ]
    started = []
    for n in range(copies):
        for y in range(n * chunks // copies, (n + 1) * chunks // copies):
            part = part_of(y - n * chunks // copies)

            def field(z):
                at = z % each * rows
                return response[y, z] * spread[z // each][at : at + rows, :]

            def keep(z, value):
                o_s[n, z * rows : (z + 1) * rows, part] = base[y, z] + value

            z_solve(zw, zi, field, y, keep)
        copy = pltpu.make_async_copy(o_s.at[n], out.at[:, pl.ds(n * wide, wide)], sems.at[n])
        copy.start()
        started.append(copy)
    for copy in started:
        copy.wait()


def finish(own, got, base, response, zw, zi, to_x):
    chunks, sheets, rows, _ = base.shape
    copies = chunks
    return pl.pallas_call(
        functools.partial(finish_kernel, stages_of("gy")),
        out_shape=shape_of(sheets * rows, chunks * LANES),
        out_specs=ANYWHERE,
        scratch_shapes=[
            pltpu.VMEM((copies, sheets * rows, chunks * LANES // copies), F32),
            pltpu.SemaphoreType.DMA((copies,)),
        ],
        compiler_params=params(),
    )(own, got, base, response, zw, zi, to_x).reshape(sheets, rows, chunks * LANES)


def per_device(temperature, base, locations, energy):
    columns = temperature.shape[2]
    gy = lax.axis_size("gy")
    t, b, loc, heat, packed, swapped = load(temperature, base, locations[None], energy[None])
    near = swap(packed, "gy", 1)
    far = lax.ppermute(packed, "gy", [(i, ((i + 1) % gy ^ 1) - 1 if i else gy - 1) for i in range(gy)])
    c, total, xw, xi, xp, x_links, x_view, xm, ends, t_steps = x_factor(loc, heat, t, b, columns * gy, packed)
    xh, x_own, view = x_target(swapped, total, near, far, xw, xi, xp, x_links, x_view, ends)
    yw, yi, yp, inner, outer, y_view, to_y, to_x = y_factor(c, x_view)
    zw, zi = z_factor(c, view)
    own, got, ties = gather_line(view, "gx", 2, (y_view, zw))
    base, response = y_prepare(
        ties, xw, xh, xm, xp, x_links, x_own, t_steps, to_y, columns // LANES
    )
    yh, inner_own, outer_own, view = y_target(
        own, got, base, response, yw, yi, yp, inner, outer, y_view, to_y
    )
    own, got, ties = gather_line(view, "gy", cross=True)
    base, response = finish_prepare(
        ties, yw, yh, yp, inner, inner_own, outer, outer_own, zw, zi, t, to_x
    )
    return finish(own, got, base, response, zw, zi, to_x)


def solution(mesh):
    in_specs = (P(None, "gx", "gy"), P(None, "gx", "gy"), P(), P())
    out_specs = P(None, "gx", "gy")
    return jax.shard_map(
        per_device, mesh=mesh, in_specs=in_specs, out_specs=out_specs, check_vma=False
    )
```

```python
import functools

import jax
import jax.numpy as jnp
from jax import lax
from jax.experimental import pallas as pl
from jax.experimental.pallas import tpu as pltpu
from jax.sharding import PartitionSpec as P

RATE = 2000.0
THERMAL_GROWTH = 0.8
LANES = 128
SUBLANES = 8
F32 = jnp.float32
MIB = 1024 * 1024
ANYWHERE = pl.BlockSpec(memory_space=pl.ANY)
IN_HBM = pl.BlockSpec(memory_space=pltpu.HBM)
IN_VMEM = pl.BlockSpec(memory_space=pltpu.VMEM)

R00, R0L, RLL, FIRST, LAST, C0, CL = range(7)
COEFS = (R00, R0L, RLL, C0, CL)


def params(limit=40):
    return pltpu.CompilerParams(vmem_limit_bytes=limit * MIB)


def shape_of(*sizes):
    return jax.ShapeDtypeStruct(sizes, F32)


def half_conduct(base, temperature):
    return base * (0.5 * RATE + (0.5 * RATE * THERMAL_GROWTH) * temperature)


def inverse(x):
    guess = pl.reciprocal(x, approx=True)
    return guess * (2.0 - x * guess)


def join_coefs(a, b):
    face = a[CL] + b[C0]
    inv = face * inverse(1.0 + face * (a[RLL] + b[R00]))
    left = a[R0L] * inv
    right = b[R0L] * inv
    joined = {
        R00: a[R00] - left * a[R0L],
        R0L: left * b[R0L],
        RLL: b[RLL] - right * b[R0L],
        C0: a[C0],
        CL: b[CL],
    }
    return joined, (inv, right, left)


def join_targets(a, b, links):
    inv, right, left = links
    jump = b[0] - a[1]
    return (a[0] + left * jump, b[1] - right * jump), jump * inv


def between(own, right, left, low, high):
    return own + right * high - left * low


def tree(items, join):
    levels = []
    while len(items) > 1:
        pairs = [join(items[i], items[i + 1]) for i in range(0, len(items), 2)]
        items = [p[0] for p in pairs]
        levels.append([p[1] for p in pairs])
    return items[0], levels


def descend(levels, low, high):
    ends = [(low, high)]
    for level in reversed(levels):
        below = []
        for (lo, hi), (own, right, left) in zip(ends, level):
            flux = between(own, right, left, lo, hi)
            below += [(lo, flux), (-flux, hi)]
        ends = below
    return ends


def node_offsets(leaves):
    offsets, at, count = [], 0, leaves // 2
    while count:
        offsets.append((at, count))
        at += count
        count //= 2
    return offsets


def factor(cond, steps, keep):
    here = cond(0)
    c_first = here
    one = jnp.ones_like(here)
    ground, path, first_first = one, one, None
    for k in range(steps - 1):
        following = cond(k + 1)
        face = here + following
        inv = inverse(ground + face)
        w = face * inv
        p = path * inv
        keep(k, w, inv, p)
        step = path * p
        first_first = step if first_first is None else first_first + step
        path = path * w
        ground = 1.0 + w * ground
        here = following
    inv = inverse(ground)
    p = path * inv
    keep(steps - 1, inv, inv, p)
    return {R00: first_first + path * p, R0L: p, RLL: inv, C0: c_first, CL: here}


def eliminate(target, steps, w, inv, p, keep):
    rhs = target(0)
    first = None
    for k in range(steps):
        h = rhs * inv(k)
        keep(k, h)
        step = rhs * p(k)
        first = step if first is None else first + step
        if k < steps - 1:
            rhs = target(k + 1) + w(k) * rhs
    return first, h


def is_odd(axis):
    return lax.axis_index(axis) % 2 == 1


def fold(cells, used):
    steps = cells.shape[0] // SUBLANES
    total = cells[pl.ds(0, SUBLANES, stride=steps), :]
    lane = lax.broadcasted_iota(jnp.int32, total.shape, 1)
    for k in range(1, steps):
        part = pltpu.roll(cells[pl.ds(k, SUBLANES, stride=steps), :], k * used, 1)
        total = jnp.where(lane // used == k, part, total)
    return total


def load_kernel(t_hbm, b_hbm, loc_hbm, energy_hbm, t_out, b_out, loc, energy, packed, cells, sems):
    sheets, rows, columns = t_hbm.shape
    parts = [(0, LANES), (columns - LANES, LANES), (LANES, columns - 2 * LANES)]
    copies = []
    for n, (start, size) in enumerate(parts):
        part = pl.ds(start, size)
        for i, (src, dst) in enumerate(((t_hbm, t_out), (b_hbm, b_out))):
            copies.append(
                pltpu.make_async_copy(src.at[:, :, part], dst.at[:, :, part], sems.at[i, n])
            )
    copies.append(pltpu.make_async_copy(loc_hbm, loc, sems.at[2, 0]))
    copies.append(pltpu.make_async_copy(energy_hbm, energy, sems.at[2, 1]))
    for copy in copies:
        copy.start()
    lane = lax.broadcasted_iota(jnp.int32, (rows, LANES), 1)
    edge_t = jnp.zeros((rows, LANES), F32)
    edge_c = edge_t
    for side, source in enumerate((0, LANES - 1)):
        for copy in copies[2 * side : 2 * side + 2]:
            copy.wait()
        part = slice(parts[side][0], parts[side][0] + LANES)
        for z in range(sheets):
            t = t_out[z, :, part]
            c = half_conduct(b_out[z, :, part], t)
            place = lane == sheets * side + z
            edge_t = jnp.where(place, t[:, source : source + 1], edge_t)
            edge_c = jnp.where(place, c[:, source : source + 1], edge_c)
    cells[0], cells[1] = edge_t, edge_c
    for i in range(2):
        packed[i * SUBLANES : (i + 1) * SUBLANES, :] = fold(cells.at[i], 2 * sheets)
    for copy in copies[4:]:
        copy.wait()


def load(temperature, base, locations, energy):
    sheets, rows, columns = temperature.shape
    assert rows // SUBLANES * 2 * sheets <= LANES and columns > 2 * LANES
    operands = (temperature, base, locations, energy)
    return pl.pallas_call(
        load_kernel,
        in_specs=[IN_HBM] * 4,
        out_shape=[pltpu.VMEM(v.shape, v.dtype) for v in operands]
        + [pltpu.VMEM((2 * SUBLANES, LANES), F32)],
        scratch_shapes=[pltpu.VMEM((2, rows, LANES), F32), pltpu.SemaphoreType.DMA((3, 3))],
        compiler_params=params(),
    )(*[pltpu.with_memory_space_constraint(v, pltpu.HBM) for v in operands])


def source_plane(loc, energy, rows, columns, plate):
    place = loc[...]
    count = place.shape[1]
    local_x = place // plate - lax.axis_index("gx") * rows
    local_y = place % plate - lax.axis_index("gy") * columns
    in_x = lax.broadcasted_iota(jnp.int32, (rows, count), 0) == local_x
    in_y = lax.broadcasted_iota(jnp.int32, (columns, count), 0) == local_y
    by_y = jnp.where(in_y, 1.0, 0.0).astype(jnp.bfloat16)
    left = energy[...]
    plane = None
    for _ in range(3):
        part = left.astype(jnp.bfloat16).astype(F32)
        left = left - part
        term = lax.dot_general(
            jnp.where(in_x, part, 0.0).astype(jnp.bfloat16),
            by_y,
            (((1,), (1,)), ((), ())),
            preferred_element_type=F32,
        )
        plane = term if plane is None else plane + term
    return plane


def part_of(y):
    return slice(y * LANES, (y + 1) * LANES)


def line_groups(chunks, sheets):
    order = [0, chunks - 1] + list(range(1, chunks - 1))
    return [[(y, z) for y in order[i : i + 2] for z in range(sheets)] for i in range(0, chunks, 2)]


def x_eliminate(cells, members, first_line, w_ref, i_ref, p_ref, h_ref, h_line, q_s):
    steps = w_ref.shape[0]
    at = slice(first_line, first_line + len(members))
    kept_at = slice(h_line, h_line + len(members))

    def target(k):
        return jnp.stack([cells(y, z, k) for y, z in members], 0)

    def keep(k, h):
        h_ref[k, kept_at] = h

    ends = eliminate(
        target, steps, lambda k: w_ref[k, at], lambda k: i_ref[k, at], lambda k: p_ref[k, at], keep
    )
    for q in range(2):
        for i in range(len(members)):
            first = (first_line + i) * SUBLANES
            q_s[q, first : first + SUBLANES, :] = ends[q][i]


def x_factor_kernel(plate, loc, energy, t_ref, b_ref, own_cells, *refs):
    c_ref, total_ref, w_ref, i_ref, p_ref, links, view, h_ref, ends_ref, t_out, swapped, q_s, t_s = refs
    chunks, sheets, rows, _ = c_ref.shape
    lines = chunks * sheets
    steps = rows // SUBLANES
    plane = source_plane(loc, energy, rows, chunks * LANES, plate)
    mine = own_cells[...]
    in_low = lax.broadcasted_iota(jnp.int32, mine.shape, 1) % (2 * sheets) < sheets
    swapped[...] = jnp.where(
        in_low, pltpu.roll(mine, LANES - sheets, 1), pltpu.roll(mine, sheets, 1)
    )

    lane = lax.broadcasted_iota(jnp.int32, (SUBLANES, LANES), 1)
    is_first, is_last = lane == 0, lane == LANES - 1
    for r in range(steps):
        at = slice(r * SUBLANES, (r + 1) * SUBLANES)
        before_t, before_c = None, None
        for z in range(sheets):
            ts = [t_ref[z, at, part_of(y)] for y in range(chunks)]
            cs = [half_conduct(b_ref[z, at, part_of(y)], ts[y]) for y in range(chunks)]
            t_turned = [pltpu.roll(v, LANES - 1, 1) for v in ts]
            c_turned = [pltpu.roll(v, LANES - 1, 1) for v in cs]
            flux = []
            for y in range(chunks):
                if y < chunks - 1:
                    t_next = jnp.where(is_last, t_turned[y + 1], t_turned[y])
                    c_next = jnp.where(is_last, c_turned[y + 1], c_turned[y])
                    flux.append((cs[y] + c_next) * (t_next - ts[y]))
                else:
                    inside = (cs[y] + c_turned[y]) * (t_turned[y] - ts[y])
                    flux.append(jnp.where(is_last, 0.0, inside))
            turned = [pltpu.roll(v, 1, 1) for v in flux]
            for y in range(chunks):
                from_low = jnp.where(is_first, turned[y - 1] if y else 0.0, turned[y])
                total = ts[y] + (flux[y] - from_low)
                if z == 0:
                    total = total + plane[at, part_of(y)]
                else:
                    across = (before_c[y] + cs[y]) * (ts[y] - before_t[y])
                    total = total - across
                    total_ref[y, z - 1, at, :] += across
                total_ref[y, z, at, :] = total
                c_ref[y, z, at, :] = cs[y]
                t_s[y, z, at, :] = ts[y]
            before_t, before_c = ts, cs

    at = 0
    for n, members in enumerate(line_groups(chunks, sheets)):

        def cond(k):
            return jnp.stack([c_ref[y, z, pl.ds(k, SUBLANES, stride=steps), :] for y, z in members], 0)

        def keep(k, w, inv, p):
            w_ref[k, at : at + len(members)] = w
            i_ref[k, at : at + len(members)] = inv
            p_ref[k, at : at + len(members)] = p

        block = factor(cond, steps, keep)
        for i, q in enumerate(COEFS):
            for j in range(len(members)):
                first = (at + j) * SUBLANES
                q_s[i, first : first + SUBLANES, :] = block[q][j]
        if n > 0:
            x_eliminate(
                lambda y, z, k: total_ref[y, z, pl.ds(k, SUBLANES, stride=steps), :],
                members, at, w_ref, i_ref, p_ref, h_ref, at - 2 * sheets, ends_ref,
            )
        for k in range(steps):
            for i, (y, z) in enumerate(members):
                t_out[k, at + i] = t_s[y, z, pl.ds(k, SUBLANES, stride=steps), :]
        at += len(members)

    segments = [
        {q: q_s[n, pl.ds(s, lines, stride=SUBLANES), :] for n, q in enumerate(COEFS)}
        for s in range(SUBLANES)
    ]
    whole, levels = tree(segments, join_coefs)
    for (offset, _), level in zip(node_offsets(SUBLANES), levels):
        for n, values in enumerate(level):
            for i in range(3):
                links[offset + n, i] = values[i]
    for n, q in enumerate(COEFS):
        view[n] = whole[q]


def x_factor(loc, energy, t, b, plate, own_cells):
    sheets, rows, columns = t.shape
    chunks = columns // LANES
    lines = chunks * sheets
    steps = rows // SUBLANES
    field = shape_of(chunks, sheets, rows, LANES)
    stored = shape_of(steps, lines, SUBLANES, LANES)
    return pl.pallas_call(
        functools.partial(x_factor_kernel, plate),
        in_specs=[IN_VMEM] * 5,
        out_shape=[
            field,
            field,
            stored,
            stored,
            stored,
            shape_of(SUBLANES - 1, 3, lines, LANES),
            shape_of(len(COEFS), lines, LANES),
            shape_of(steps, max(1, lines - 2 * sheets), SUBLANES, LANES),
            shape_of(2, lines * SUBLANES, LANES),
            stored,
            shape_of(*own_cells.shape),
        ],
        scratch_shapes=[
            pltpu.VMEM((len(COEFS), lines * SUBLANES, LANES), F32),
            pltpu.VMEM((chunks, sheets, rows, LANES), F32),
        ],
        compiler_params=params(),
        cost_estimate=pl.CostEstimate(flops=40 * t.size, bytes_accessed=28 * t.size, transcendentals=0),
    )(loc, energy, t, b, own_cells)


def x_target_kernel(own_cells, total_ref, near, far, *refs):
    w_ref, i_ref, p_ref, links, view, ends_ref, h_ref, own, send, q_s = refs
    chunks, sheets, rows, _ = total_ref.shape
    lines = chunks * sheets
    steps = rows // SUBLANES

    place = lax.axis_index("gy")
    inner = (place > 0) & (place < lax.axis_size("gy") - 1)
    lane = lax.broadcasted_iota(jnp.int32, (SUBLANES, LANES), 1)
    side = 2 * sheets
    is_near = (lane % side >= sheets).astype(jnp.int32) == place % 2
    t, c = (
        jnp.where(is_near, near[at, :], jnp.where(inner, far[at, :], 0.0))
        for at in (slice(0, SUBLANES), slice(SUBLANES, 2 * SUBLANES))
    )
    face = jnp.where(c > 0.0, own_cells[SUBLANES:, :] + c, 0.0)
    flux = face * (t - own_cells[:SUBLANES, :])

    def cells(y, z, k):
        at = k * side + (sheets + z if y == 0 else z)
        edge = 0 if y == 0 else LANES - 1
        inflow = jnp.where(lane == edge, flux[:, at : at + 1], 0.0)
        return total_ref[y, z, pl.ds(k, SUBLANES, stride=steps), :] + inflow

    members = line_groups(chunks, sheets)[0]
    x_eliminate(cells, members, 0, w_ref, i_ref, p_ref, h_ref, 0, q_s)
    split = len(members)
    items = [
        tuple(
            jnp.concatenate(
                [
                    q_s[q, pl.ds(s, split, stride=SUBLANES), :],
                    ends_ref[q, pl.ds(split * SUBLANES + s, lines - split, stride=SUBLANES), :],
                ],
                0,
            )
            for q in range(2)
        )
        for s in range(SUBLANES)
    ]
    for offset, count in node_offsets(SUBLANES):
        joined = []
        for n in range(count):
            ties = tuple(links[offset + n, i] for i in range(3))
            both, flux = join_targets(items[2 * n], items[2 * n + 1], ties)
            own[offset + n] = flux
            joined.append(both)
        items = joined
    for n, q in enumerate(COEFS):
        send[q] = view[n]
    send[FIRST], send[LAST] = items[0]


def x_target(own_cells, total, near, far, w, inv, p, links, view, ends):
    chunks, sheets, rows, _ = total.shape
    lines = chunks * sheets
    steps = rows // SUBLANES
    return pl.pallas_call(
        x_target_kernel,
        out_shape=[
            shape_of(steps, 2 * sheets, SUBLANES, LANES),
            shape_of(SUBLANES - 1, lines, LANES),
            shape_of(7, lines, LANES),
        ],
        scratch_shapes=[
            pltpu.VMEM((2, 2 * sheets * SUBLANES, LANES), F32),
        ],
        compiler_params=params(),
    )(own_cells, total, near, far, w, inv, p, links, view, ends)


def stages_of(axis):
    return lax.axis_size(axis).bit_length() - 1


def swap(value, axis, flip):
    count = lax.axis_size(axis)
    return lax.ppermute(value, axis, [(i, i ^ flip) for i in range(count)])


def on_right(axis, stage):
    return (lax.axis_index(axis) >> stage) % 2 == 1


def toward(right, block):
    return (
        jnp.where(right, block[R00], block[RLL]),
        jnp.where(right, block[FIRST], block[LAST]),
        jnp.where(right, block[C0], block[CL]),
    )


def join(a, b):
    joined, ties = join_coefs(a, b)
    (joined[FIRST], joined[LAST]), flux = join_targets((a[FIRST], a[LAST]), (b[FIRST], b[LAST]), ties)
    return joined, (flux, ties[1], ties[2])


def ordered(right, own, other):
    first = [jnp.where(right, theirs, mine) for mine, theirs in zip(own, other)]
    second = [jnp.where(right, mine, theirs) for mine, theirs in zip(own, other)]
    return first, second


def join_kernel(axis, stage, width, last, *refs):
    count = 1 << width
    blocks = [[refs[i][q] for q in range(7)] for i in range(count)]
    send = refs[-1 - width]
    links = refs[-width:]
    for bit in range(width):
        right = on_right(axis, stage + bit)
        for i in range(count):
            if not i >> bit & 1:
                j = i | 1 << bit
                blocks[i], blocks[j] = ordered(right, blocks[i], blocks[j])
    for bit in range(width):
        pairs = [join(blocks[i], blocks[i + 1]) for i in range(0, len(blocks), 2)]
        blocks = [p[0] for p in pairs]
        ties = [p[1] for p in pairs]
        for upper in range(bit + 1, width):
            right = on_right(axis, stage + upper)
            ties = [
                tuple(jnp.where(right, v, u) for u, v in zip(ties[i], ties[i + 1]))
                for i in range(0, len(ties), 2)
            ]
        for i in range(3):
            links[bit][i] = ties[0][i]
    (whole,) = blocks
    if last:
        for n, value in enumerate(toward(on_right(axis, stage + width), whole)):
            send[n] = value
    else:
        for q in range(7):
            send[q] = whole[q]


def join_stage(own, got, axis, stage, width, last, after):
    lines = own.shape[1]
    return pl.pallas_call(
        functools.partial(join_kernel, axis, stage, width, last),
        in_specs=[IN_VMEM] * (1 + len(got)) + [ANYWHERE] * len(after),
        out_shape=[shape_of(3 if last else 7, lines, LANES)] + [shape_of(3, lines, LANES)] * width,
        compiler_params=params(),
    )(own, *got, *after)


def gather_line(view, axis, widest=1, meanwhile=(), cross=False):
    stages = stages_of(axis)
    links, stage = [], 0
    while stage < stages - 1:
        width = min(widest, stages - 1 - stage)
        got = [swap(view, axis, flip << stage) for flip in range(1, 1 << width)]
        last = stage + width == stages - 1
        view, *ties = join_stage(view, got, axis, stage, width, last, meanwhile)
        links += ties
        stage += width
        meanwhile = ()
    return view, swap(view, axis, 1 << stage | (cross and stage > 0)), links


def top_flux(axis, stages, own, got):
    right = on_right(axis, stages - 1)
    face = own[2] + got[2]
    jump = jnp.where(right, own[1] - got[1], got[1] - own[1])
    return jump * face * inverse(1.0 + face * (own[0] + got[0]))


def block_ends(axis, stages, links):
    shape = links[0].shape[1:] if links else None
    right = on_right(axis, stages - 1)
    zero = jnp.zeros(shape, F32)
    low, high = zero, zero
    unit_low = zero + jnp.where(right, -1.0, 0.0)
    unit_high = zero + jnp.where(right, 0.0, 1.0)
    for stage in range(stages - 2, -1, -1):
        tie = links[stage]
        right = on_right(axis, stage)
        flux = between(tie[0], tie[1], tie[2], low, high)
        unit = between(0.0, tie[1], tie[2], unit_low, unit_high)
        low, high = jnp.where(right, -flux, low), jnp.where(right, high, flux)
        unit_low, unit_high = jnp.where(right, -unit, unit_low), jnp.where(right, unit_high, unit)
    return (low, high), (unit_low, unit_high)


def natural(index, parts):
    span = SUBLANES * parts
    local = index % span
    return index - local + local % SUBLANES * parts + local // SUBLANES


def turn_matrix(shape, from_natural, parts):
    row = lax.broadcasted_iota(jnp.int32, shape, 0)
    column = lax.broadcasted_iota(jnp.int32, shape, 1) % LANES
    hit = natural(row, parts) == column if from_natural else row == natural(column, parts)
    return jnp.where(hit, 1.0, 0.0).astype(jnp.bfloat16)


def turned(matrix, field, rows=None):
    high = field.astype(jnp.bfloat16).astype(F32)
    both = jnp.concatenate([high, field - high], 1)
    if rows:
        both = jnp.concatenate(
            [jnp.broadcast_to(both[n : n + 1, :], (rows, 2 * LANES)) for n in range(field.shape[0])], 0
        )
    both = both.astype(jnp.bfloat16)
    return lax.dot_general(
        matrix, both, (((1,), (1,)), ((), ())), preferred_element_type=F32
    )


def y_factor_kernel(c_ref, after, w_ref, i_ref, p_ref, inner, outer, view, to_y, to_x, unit_low, unit_high, c_s, q_s, r_s):
    chunks, sheets, rows, _ = c_ref.shape
    each = LANES // rows
    pairs = sheets // each
    x_steps = rows // SUBLANES
    steps = LANES // SUBLANES
    to_y[...] = turn_matrix(to_y.shape, True, steps)
    to_x[...] = turn_matrix(to_x.shape, False, x_steps)
    for m in range(pairs):
        for y in range(chunks):
            block = jnp.concatenate(
                [
                    c_ref[y, m * each + i, pl.ds(k, SUBLANES, stride=x_steps), :]
                    for i in range(each)
                    for k in range(x_steps)
                ],
                0,
            )
            c_s[m, part_of(y), :] = block.T

    members = [(y, m) for y in range(chunks) for m in range(pairs)]
    lines = len(members)

    def cond(k):
        return jnp.stack([c_s[m, pl.ds(y * LANES + k, SUBLANES, stride=steps), :] for y, m in members], 0)

    def keep(k, w, inv, p):
        w_ref[k] = w
        i_ref[k] = inv
        p_ref[k] = p

    block = factor(cond, steps, keep)
    for n, q in enumerate(COEFS):
        for i in range(lines):
            q_s[n, i * SUBLANES : (i + 1) * SUBLANES, :] = block[q][i]
    segments = [
        {q: q_s[n, pl.ds(s, lines, stride=SUBLANES), :] for n, q in enumerate(COEFS)}
        for s in range(SUBLANES)
    ]
    whole, levels = tree(segments, join_coefs)
    for (offset, _), level in zip(node_offsets(SUBLANES), levels):
        for n, values in enumerate(level):
            for i in range(3):
                inner[offset + n, i] = values[i]
    for n, q in enumerate(COEFS):
        r_s[n] = whole[q]
    parts = [
        {q: r_s[n, y * pairs : (y + 1) * pairs, :] for n, q in enumerate(COEFS)} for y in range(chunks)
    ]
    whole, levels = tree(parts, join_coefs)
    for (offset, _), level in zip(node_offsets(chunks), levels):
        for n, values in enumerate(level):
            for i in range(3):
                outer[offset + n, i] = values[i]
    for n, q in enumerate(COEFS):
        view[n] = whole[q]

    one = jnp.ones((pairs, LANES), F32)
    for n, (low, high, field) in enumerate(((one, 0.0 * one, unit_low), (0.0 * one, one, unit_high))):
        for y, pair in enumerate(tree_ends(chunks, outer, nothing, low, high)):
            for i in range(2):
                r_s[2 * n + i, y * pairs : (y + 1) * pairs, :] = pair[i]
        for s, pair in enumerate(tree_ends(SUBLANES, inner, nothing, r_s[2 * n], r_s[2 * n + 1])):
            for i in range(2):
                q_s[2 * n + i, pl.ds(s, lines, stride=SUBLANES), :] = pair[i]
        low, value = (
            jnp.stack(
                [q_s[2 * n + i, j * SUBLANES : (j + 1) * SUBLANES, :] for j in range(lines)], 0
            )
            for i in range(2)
        )
        for k in range(steps - 1, -1, -1):
            value = w_ref[k] * value + p_ref[k] * low
            for j, (y, m) in enumerate(members):
                field[y, k * SUBLANES : (k + 1) * SUBLANES, part_of(m)] = value[j]


def y_factor(c, after):
    chunks, sheets, rows, _ = c.shape
    pairs = sheets * rows // LANES
    lines = chunks * pairs
    stored = shape_of(LANES // SUBLANES, lines, SUBLANES, LANES)
    matrix = jax.ShapeDtypeStruct((LANES, 2 * LANES), jnp.bfloat16)
    return pl.pallas_call(
        y_factor_kernel,
        in_specs=[IN_VMEM, ANYWHERE],
        out_shape=[
            stored,
            stored,
            stored,
            shape_of(SUBLANES - 1, 3, lines, LANES),
            shape_of(chunks - 1, 3, pairs, LANES),
            shape_of(len(COEFS), pairs, LANES),
            matrix,
            matrix,
            shape_of(chunks, LANES, pairs * LANES),
            shape_of(chunks, LANES, pairs * LANES),
        ],
        scratch_shapes=[
            pltpu.VMEM((pairs, chunks * LANES, LANES), F32),
            pltpu.VMEM((len(COEFS), lines * SUBLANES, LANES), F32),
            pltpu.VMEM((len(COEFS), lines, LANES), F32),
        ],
        compiler_params=params(),
        cost_estimate=pl.CostEstimate(flops=20 * c.size, bytes_accessed=16 * c.size, transcendentals=0),
    )(c, after)


def z_factor_kernel(c_ref, after, w_ref, i_ref):
    sheets = c_ref.shape[1]
    ground = 1.0
    for z in range(sheets - 1):
        face = c_ref[:, z] + c_ref[:, z + 1]
        inv = inverse(ground + face)
        w = face * inv
        i_ref[z] = inv
        w_ref[z] = w
        ground = 1.0 + w * ground
    i_ref[sheets - 1] = inverse(ground)


def z_factor(c, after):
    chunks, sheets, rows, _ = c.shape
    return pl.pallas_call(
        z_factor_kernel,
        in_specs=[IN_VMEM, ANYWHERE],
        out_shape=[
            shape_of(sheets - 1, chunks, rows, LANES),
            shape_of(sheets, chunks, rows, LANES),
        ],
        compiler_params=params(),
        cost_estimate=pl.CostEstimate(flops=10 * c.size, bytes_accessed=12 * c.size, transcendentals=0),
    )(c, after)


def join_tree(items, links, own):
    for offset, count in node_offsets(len(items)):
        joined = []
        for n in range(count):
            tie = tuple(links[offset + n, i] for i in range(3))
            both, flux = join_targets(items[2 * n], items[2 * n + 1], tie)
            own[offset + n] = flux
            joined.append(both)
        items = joined
    return items[0]


def tree_ends(leaves, links, own, low, high):
    levels = [
        [(own(offset + n), links[offset + n, 1], links[offset + n, 2]) for n in range(count)]
        for offset, count in node_offsets(leaves)
    ]
    return descend(levels, low, high)


def nothing(node):
    return 0.0


def y_prepare_kernel(stages, *refs):
    ties = refs[: stages - 1]
    xw, xh, xm, xp, x_links, x_own, t_ref, to_y, y_low, y_high = refs[stages - 1 : stages + 9]
    base, response, to_first, to_last, fixed, f_s, g_s = refs[stages + 9 :]
    x_steps, lines = xw.shape[:2]
    chunks = base.shape[0]
    sheets = lines // chunks
    rows = x_steps * SUBLANES

    ends, units = block_ends("gx", stages, ties)
    for n, (own, (low, high)) in enumerate(((lambda i: x_own[i], ends), (nothing, units))):
        for s, pair in enumerate(tree_ends(SUBLANES, x_links, own, low, high)):
            for i in range(2):
                f_s[n, i, pl.ds(s, lines, stride=SUBLANES), :] = pair[i]
    first = 0
    for n, members in enumerate(line_groups(chunks, sheets)):
        at = slice(first, first + len(members))
        h_ref_of, h_at = (xh, at) if n == 0 else (xm, slice(first - 2 * sheets, at.stop - 2 * sheets))
        (low, value), (unit_low, unit) = (
            [
                jnp.stack(
                    [f_s[q, i, j * SUBLANES : (j + 1) * SUBLANES, :] for j in range(at.start, at.stop)], 0
                )
                for i in range(2)
            ]
            for q in range(2)
        )
        for k in range(x_steps - 1, -1, -1):
            w, p = xw[k, at], xp[k, at]
            value = w * value + (h_ref_of[k, h_at] + p * low)
            unit = w * unit + p * unit_low
            field = value - t_ref[k, at]
            for j, (y, z) in enumerate(members):
                place = z * rows + k * SUBLANES
                g_s[0, y, place : place + SUBLANES, :] = field[j]
                g_s[1, y, place : place + SUBLANES, :] = unit[j]
        first = at.stop

    totals = [None, None]
    for y in range(chunks):
        field = turned(to_y[...], g_s[0, y])
        answer = turned(to_y[...], g_s[1, y])
        base[y] = field
        response[y] = answer
        for i, (unit, weight) in enumerate(((y_low, to_first), (y_high, to_last))):
            weight[y] = unit[y] * answer
            part = unit[y] * field
            totals[i] = part if y == 0 else totals[i] + part
    for i in range(2):
        put_sums(fixed.at[i], totals[i])


def put_sums(out, field):
    total = jnp.sum(field, 0, keepdims=True)
    for m in range(out.shape[0]):
        out[m : m + 1, :] = total[:, part_of(m)]


def y_prepare(ties, xw, xh, xm, xp, x_links, x_own, t, to_y, unit_low, unit_high):
    chunks = unit_low.shape[0]
    x_steps, lines = xw.shape[:2]
    width = lines // chunks * x_steps * SUBLANES
    field = shape_of(chunks, LANES, width)
    return pl.pallas_call(
        functools.partial(y_prepare_kernel, len(ties) + 1),
        out_shape=[field] * 4 + [shape_of(2, width // LANES, LANES)],
        scratch_shapes=[
            pltpu.VMEM((2, 2, lines * SUBLANES, LANES), F32),
            pltpu.VMEM((2, chunks, width, LANES), F32),
        ],
        compiler_params=params(),
        cost_estimate=pl.CostEstimate(flops=8 * t.size, bytes_accessed=16 * t.size, transcendentals=0),
    )(*ties, xw, xh, xm, xp, x_links, x_own, t, to_y, unit_low, unit_high)


def y_target_kernel(stages, own, got, to_first, to_last, fixed, view, to_y, spread, send, r_s):
    chunks, _, width = to_first.shape
    sheets = own.shape[1] // chunks
    rows = width // sheets

    flux = top_flux("gx", stages, own, got)
    line_of = {member: n for n, member in enumerate(sum(line_groups(chunks, sheets), []))}
    totals = [None, None]
    for y in range(chunks):
        own_flux = jnp.concatenate([flux[line_of[y, z] : line_of[y, z] + 1, :] for z in range(sheets)], 0)
        wide = turned(to_y[...], own_flux, rows)
        spread[y] = wide
        for i, weight in enumerate((to_first, to_last)):
            part = weight[y] * wide
            totals[i] = part if y == 0 else totals[i] + part
    for n, q in enumerate(COEFS):
        send[q] = view[n]
    for i, q in enumerate((FIRST, LAST)):
        put_sums(r_s.at[i], totals[i])
        send[q] = fixed[i] + r_s[i]


def y_target(own, got, to_first, to_last, fixed, view, to_y):
    pairs = view.shape[1]
    return pl.pallas_call(
        functools.partial(y_target_kernel, stages_of("gx")),
        out_shape=[shape_of(*to_first.shape), shape_of(7, pairs, LANES)],
        scratch_shapes=[pltpu.VMEM((2, pairs, LANES), F32)],
        compiler_params=params(),
    )(own, got, to_first, to_last, fixed, view, to_y)


def y_eliminate_kernel(base, response, spread, yw, yi, yp, inner, outer, after, *refs):
    h_ref, inner_own, outer_own, q_s, r_s = refs
    chunks, _, width = base.shape
    pairs = width // LANES
    steps = yw.shape[0]
    members = [(y, m) for y in range(chunks) for m in range(pairs)]

    def target(k):
        at = slice(k * SUBLANES, (k + 1) * SUBLANES)
        return jnp.stack(
            [
                base[y, at, part_of(m)] + response[y, at, part_of(m)] * spread[y, at, part_of(m)]
                for y, m in members
            ],
            0,
        )

    def keep(k, h):
        h_ref[k] = h

    ends = eliminate(target, steps, lambda k: yw[k], lambda k: yi[k], lambda k: yp[k], keep)
    for q in range(2):
        for i in range(len(members)):
            q_s[q, i * SUBLANES : (i + 1) * SUBLANES, :] = ends[q][i]
    items = [
        tuple(q_s[q, pl.ds(s, len(members), stride=SUBLANES), :] for q in range(2))
        for s in range(SUBLANES)
    ]
    r_s[0], r_s[1] = join_tree(items, inner, inner_own)
    items = [tuple(r_s[q, y * pairs : (y + 1) * pairs, :] for q in range(2)) for y in range(chunks)]
    join_tree(items, outer, outer_own)


def y_eliminate(base, response, spread, yw, yi, yp, inner, outer, after):
    y_lines = yw.shape[1]
    pairs = outer.shape[2]
    chunks = y_lines // pairs
    return pl.pallas_call(
        y_eliminate_kernel,
        in_specs=[IN_VMEM] * 8 + [ANYWHERE],
        out_shape=[
            shape_of(*yw.shape),
            shape_of(SUBLANES - 1, y_lines, LANES),
            shape_of(chunks - 1, pairs, LANES),
        ],
        scratch_shapes=[
            pltpu.VMEM((2, y_lines * SUBLANES, LANES), F32),
            pltpu.VMEM((2, y_lines, LANES), F32),
        ],
        compiler_params=params(),
        cost_estimate=pl.CostEstimate(flops=8 * base.size, bytes_accessed=16 * base.size, transcendentals=0),
    )(base, response, spread, yw, yi, yp, inner, outer, after)


def z_solve(zw, zi, field, at, keep):
    sheets = zi.shape[0]
    rhs, kept = None, []
    for z in range(sheets):
        rhs = field(z) if z == 0 else field(z) + zw[z - 1, at] * rhs
        kept.append(rhs * zi[z, at])
    value = kept[-1]
    keep(sheets - 1, value)
    for z in range(sheets - 2, -1, -1):
        value = zw[z, at] * value + kept[z]
        keep(z, value)


def finish_prepare_kernel(stages, *refs):
    ties = refs[: stages - 1]
    yw, yh, yp, inner, inner_own, outer, outer_own, zw, zi, t_ref, to_x = refs[stages - 1 : stages + 10]
    base, response, r_s, e_s, u_s = refs[stages + 10 :]
    chunks, sheets, rows, _ = base.shape
    each = LANES // rows
    pairs = sheets // each
    steps = yw.shape[0]
    lines = chunks * pairs

    ends, units = block_ends("gy", stages, ties)
    both = (
        (lambda i: outer_own[i], lambda i: inner_own[i], ends),
        (nothing, nothing, units),
    )
    for n, (upper, lower, (low, high)) in enumerate(both):
        for y, pair in enumerate(tree_ends(chunks, outer, upper, low, high)):
            for i in range(2):
                r_s[n, i, y * pairs : (y + 1) * pairs, :] = pair[i]
        for s, pair in enumerate(tree_ends(SUBLANES, inner, lower, r_s[n, 0], r_s[n, 1])):
            for i in range(2):
                e_s[n, i, pl.ds(s, lines, stride=SUBLANES), :] = pair[i]
    (low, value), (unit_low, unit) = (
        [
            jnp.stack([e_s[q, i, n * SUBLANES : (n + 1) * SUBLANES, :] for n in range(lines)], 0)
            for i in range(2)
        ]
        for q in range(2)
    )
    for k in range(steps - 1, -1, -1):
        w, p = yw[k], yp[k]
        value = w * value + (yh[k] + p * low)
        unit = w * unit + p * unit_low
        for y in range(chunks):
            for m in range(pairs):
                place = pl.ds(y * LANES + k, SUBLANES, stride=steps)
                u_s[0, m, place, :] = value[y * pairs + m]
                u_s[1, m, place, :] = unit[y * pairs + m]

    for y in range(chunks):
        part = part_of(y)
        fields = [turned(to_x[...], u_s[0, m, part, :]) for m in range(pairs)]

        def field(z):
            at = z % each * rows
            return fields[z // each][at : at + rows, :]

        def keep(z, value):
            base[y, z] = t_ref[z, :, part] + value

        z_solve(zw, zi, field, y, keep)
        for m in range(pairs):
            units = turned(to_x[...], u_s[1, m, part, :])
            for i in range(each):
                response[y, m * each + i] = units[i * rows : (i + 1) * rows, :]


def finish_prepare(ties, yw, yh, yp, inner, inner_own, outer, outer_own, zw, zi, t, to_x):
    sheets, rows, columns = t.shape
    chunks = columns // LANES
    pairs = sheets * rows // LANES
    lines = chunks * pairs
    field = shape_of(chunks, sheets, rows, LANES)
    return pl.pallas_call(
        functools.partial(finish_prepare_kernel, len(ties) + 1),
        out_shape=[field, field],
        scratch_shapes=[
            pltpu.VMEM((2, 2, lines, LANES), F32),
            pltpu.VMEM((2, 2, lines * SUBLANES, LANES), F32),
            pltpu.VMEM((2, pairs, columns, LANES), F32),
        ],
        compiler_params=params(),
        cost_estimate=pl.CostEstimate(flops=12 * t.size, bytes_accessed=20 * t.size, transcendentals=0),
    )(*ties, yw, yh, yp, inner, inner_own, outer, outer_own, zw, zi, t, to_x)


def finish_kernel(stages, own, got, base, response, zw, zi, to_x, out, o_s, sems):
    chunks, sheets, rows, _ = base.shape
    each = LANES // rows
    pairs = sheets // each
    copies, _, wide = o_s.shape

    flux = top_flux("gy", stages, own, got)
    spread = [
        turned(to_x[...], flux[m : m + 1, :], LANES) for m in range(pairs)
    ]
    started = []
    for n in range(copies):
        for y in range(n * chunks // copies, (n + 1) * chunks // copies):
            part = part_of(y - n * chunks // copies)

            def field(z):
                at = z % each * rows
                return response[y, z] * spread[z // each][at : at + rows, :]

            def keep(z, value):
                o_s[n, z * rows : (z + 1) * rows, part] = base[y, z] + value

            z_solve(zw, zi, field, y, keep)
        copy = pltpu.make_async_copy(o_s.at[n], out.at[:, pl.ds(n * wide, wide)], sems.at[n])
        copy.start()
        started.append(copy)
    for copy in started:
        copy.wait()


def finish(own, got, base, response, zw, zi, to_x):
    chunks, sheets, rows, _ = base.shape
    copies = chunks
    return pl.pallas_call(
        functools.partial(finish_kernel, stages_of("gy")),
        out_shape=shape_of(sheets * rows, chunks * LANES),
        out_specs=ANYWHERE,
        scratch_shapes=[
            pltpu.VMEM((copies, sheets * rows, chunks * LANES // copies), F32),
            pltpu.SemaphoreType.DMA((copies,)),
        ],
        compiler_params=params(),
    )(own, got, base, response, zw, zi, to_x).reshape(sheets, rows, chunks * LANES)


def per_device(temperature, base, locations, energy):
    columns = temperature.shape[2]
    gy = lax.axis_size("gy")
    t, b, loc, heat, packed = load(temperature, base, locations[None], energy[None])
    near = swap(packed, "gy", 1)
    far = lax.ppermute(packed, "gy", [(i, ((i + 1) % gy ^ 1) - 1 if i else gy - 1) for i in range(gy)])
    c, total, xw, xi, xp, x_links, x_view, xm, ends, t_steps, swapped = x_factor(loc, heat, t, b, columns * gy, packed)
    xh, x_own, view = x_target(swapped, total, near, far, xw, xi, xp, x_links, x_view, ends)
    yw, yi, yp, inner, outer, y_view, to_y, to_x, unit_low, unit_high = y_factor(c, x_view)
    zw, zi = z_factor(c, view)
    own, got, ties = gather_line(view, "gx", 2, (y_view, zw))
    base, response, to_first, to_last, fixed = y_prepare(
        ties, xw, xh, xm, xp, x_links, x_own, t_steps, to_y, unit_low, unit_high
    )
    spread, view = y_target(own, got, to_first, to_last, fixed, y_view, to_y)
    yh, inner_own, outer_own = y_eliminate(base, response, spread, yw, yi, yp, inner, outer, view)
    own, got, ties = gather_line(view, "gy", meanwhile=(yh,), cross=True)
    base, response = finish_prepare(
        ties, yw, yh, yp, inner, inner_own, outer, outer_own, zw, zi, t, to_x
    )
    return finish(own, got, base, response, zw, zi, to_x)


def solution(mesh):
    in_specs = (P(None, "gx", "gy"), P(None, "gx", "gy"), P(), P())
    out_specs = P(None, "gx", "gy")
    return jax.shard_map(
        per_device, mesh=mesh, in_specs=in_specs, out_specs=out_specs, check_vma=False
    )
```

```python
import functools

import jax
import jax.numpy as jnp
from jax import lax
from jax.experimental import pallas as pl
from jax.experimental.pallas import tpu as pltpu
from jax.sharding import PartitionSpec as P

RATE = 2000.0
THERMAL_GROWTH = 0.8
LANES = 128
SUBLANES = 8
F32 = jnp.float32
MIB = 1024 * 1024
ORDER = (2, 1, 3)
ANYWHERE = pl.BlockSpec(memory_space=pl.ANY)
IN_HBM = pl.BlockSpec(memory_space=pltpu.HBM)
IN_VMEM = pl.BlockSpec(memory_space=pltpu.VMEM)

R00, R0L, RLL, FIRST, LAST, C0, CL = range(7)
COEFS = (R00, R0L, RLL, C0, CL)


def params(limit=40):
    return pltpu.CompilerParams(vmem_limit_bytes=limit * MIB)


def shape_of(*sizes):
    return jax.ShapeDtypeStruct(sizes, F32)


def half_conduct(base, temperature):
    return base * (0.5 * RATE + (0.5 * RATE * THERMAL_GROWTH) * temperature)


def inverse(x):
    guess = pl.reciprocal(x, approx=True)
    return guess * (2.0 - x * guess)


def join_coefs(a, b):
    face = a[CL] + b[C0]
    inv = face * inverse(1.0 + face * (a[RLL] + b[R00]))
    left = a[R0L] * inv
    right = b[R0L] * inv
    joined = {
        R00: a[R00] - left * a[R0L],
        R0L: left * b[R0L],
        RLL: b[RLL] - right * b[R0L],
        C0: a[C0],
        CL: b[CL],
    }
    return joined, (inv, right, left)


def join_targets(a, b, links):
    inv, right, left = links
    jump = b[0] - a[1]
    return (a[0] + left * jump, b[1] - right * jump), jump * inv


def between(own, right, left, low, high):
    return own + right * high - left * low


def tree(items, join):
    levels = []
    while len(items) > 1:
        pairs = [join(items[i], items[i + 1]) for i in range(0, len(items), 2)]
        items = [p[0] for p in pairs]
        levels.append([p[1] for p in pairs])
    return items[0], levels


def descend(levels, low, high):
    ends = [(low, high)]
    for level in reversed(levels):
        below = []
        for (lo, hi), (own, right, left) in zip(ends, level):
            flux = between(own, right, left, lo, hi)
            below += [(lo, flux), (-flux, hi)]
        ends = below
    return ends


def node_offsets(leaves):
    offsets, at, count = [], 0, leaves // 2
    while count:
        offsets.append((at, count))
        at += count
        count //= 2
    return offsets


def factor(cond, steps, keep):
    here = cond(0)
    c_first = here
    one = jnp.ones_like(here)
    ground, path, first_first = one, one, None
    for k in range(steps - 1):
        following = cond(k + 1)
        face = here + following
        inv = inverse(ground + face)
        w = face * inv
        p = path * inv
        keep(k, w, inv, p)
        step = path * p
        first_first = step if first_first is None else first_first + step
        path = path * w
        ground = 1.0 + w * ground
        here = following
    inv = inverse(ground)
    p = path * inv
    keep(steps - 1, inv, inv, p)
    return {R00: first_first + path * p, R0L: p, RLL: inv, C0: c_first, CL: here}


def eliminate(target, steps, w, inv, p, keep):
    rhs = target(0)
    first = None
    for k in range(steps):
        h = rhs * inv(k)
        keep(k, h)
        step = rhs * p(k)
        first = step if first is None else first + step
        if k < steps - 1:
            rhs = target(k + 1) + w(k) * rhs
    return first, h


def is_odd(axis):
    return lax.axis_index(axis) % 2 == 1


def fold(cells, used):
    steps = cells.shape[0] // SUBLANES
    total = cells[pl.ds(0, SUBLANES, stride=steps), :]
    lane = lax.broadcasted_iota(jnp.int32, total.shape, 1)
    for k in range(1, steps):
        part = pltpu.roll(cells[pl.ds(k, SUBLANES, stride=steps), :], k * used, 1)
        total = jnp.where(lane // used == k, part, total)
    return total


def load_kernel(t_hbm, b_hbm, loc_hbm, energy_hbm, t_out, b_out, loc, energy, packed, cells, sems):
    sheets, rows, columns = t_hbm.shape
    parts = [(0, LANES), (columns - LANES, LANES), (LANES, columns - 2 * LANES)]
    copies = []
    for n, (start, size) in enumerate(parts):
        part = pl.ds(start, size)
        for i, (src, dst) in enumerate(((t_hbm, t_out), (b_hbm, b_out))):
            copies.append(
                pltpu.make_async_copy(src.at[:, :, part], dst.at[:, :, part], sems.at[i, n])
            )
    copies.append(pltpu.make_async_copy(loc_hbm, loc, sems.at[2, 0]))
    copies.append(pltpu.make_async_copy(energy_hbm, energy, sems.at[2, 1]))
    for copy in copies:
        copy.start()
    lane = lax.broadcasted_iota(jnp.int32, (rows, LANES), 1)
    edge_t = jnp.zeros((rows, LANES), F32)
    edge_c = edge_t
    for side, source in enumerate((0, LANES - 1)):
        for copy in copies[2 * side : 2 * side + 2]:
            copy.wait()
        part = slice(parts[side][0], parts[side][0] + LANES)
        for z in range(sheets):
            t = t_out[z, :, part]
            c = half_conduct(b_out[z, :, part], t)
            place = lane == sheets * side + z
            edge_t = jnp.where(place, t[:, source : source + 1], edge_t)
            edge_c = jnp.where(place, c[:, source : source + 1], edge_c)
    cells[0], cells[1] = edge_t, edge_c
    for i in range(2):
        packed[i * SUBLANES : (i + 1) * SUBLANES, :] = fold(cells.at[i], 2 * sheets)
    for copy in copies[4:]:
        copy.wait()


def load(temperature, base, locations, energy):
    sheets, rows, columns = temperature.shape
    assert rows // SUBLANES * 2 * sheets <= LANES and columns > 2 * LANES
    operands = (temperature, base, locations, energy)
    return pl.pallas_call(
        load_kernel,
        in_specs=[IN_HBM] * 4,
        out_shape=[pltpu.VMEM(v.shape, v.dtype) for v in operands]
        + [pltpu.VMEM((2 * SUBLANES, LANES), F32)],
        scratch_shapes=[pltpu.VMEM((2, rows, LANES), F32), pltpu.SemaphoreType.DMA((3, 3))],
        compiler_params=params(),
    )(*[pltpu.with_memory_space_constraint(v, pltpu.HBM) for v in operands])


def source_plane(loc, energy, rows, columns, plate):
    place = loc[...]
    count = place.shape[1]
    local_x = place // plate - lax.axis_index("gx") * rows
    local_y = place % plate - lax.axis_index("gy") * columns
    in_x = lax.broadcasted_iota(jnp.int32, (rows, count), 0) == local_x
    in_y = lax.broadcasted_iota(jnp.int32, (columns, count), 0) == local_y
    by_y = jnp.where(in_y, 1.0, 0.0).astype(jnp.bfloat16)
    left = energy[...]
    plane = None
    for _ in range(3):
        part = left.astype(jnp.bfloat16).astype(F32)
        left = left - part
        term = lax.dot_general(
            jnp.where(in_x, part, 0.0).astype(jnp.bfloat16),
            by_y,
            (((1,), (1,)), ((), ())),
            preferred_element_type=F32,
        )
        plane = term if plane is None else plane + term
    return plane


def part_of(y):
    return slice(y * LANES, (y + 1) * LANES)


def line_groups(chunks, sheets):
    order = [0, chunks - 1] + list(range(1, chunks - 1))
    return [[(y, z) for y in order[i : i + 2] for z in range(sheets)] for i in range(0, chunks, 2)]


def x_eliminate(cells, members, first_line, w_ref, i_ref, p_ref, h_ref, h_line, q_s):
    steps = w_ref.shape[0]
    at = slice(first_line, first_line + len(members))
    kept_at = slice(h_line, h_line + len(members))

    def target(k):
        return jnp.stack([cells(y, z, k) for y, z in members], 0)

    def keep(k, h):
        h_ref[k, kept_at] = h

    ends = eliminate(
        target, steps, lambda k: w_ref[k, at], lambda k: i_ref[k, at], lambda k: p_ref[k, at], keep
    )
    for q in range(2):
        for i in range(len(members)):
            first = (first_line + i) * SUBLANES
            q_s[q, first : first + SUBLANES, :] = ends[q][i]


def x_factor_kernel(plate, loc, energy, t_ref, b_ref, own_cells, *refs):
    c_ref, total_ref, w_ref, i_ref, p_ref, links, view, h_ref, ends_ref, t_out, swapped, q_s, t_s = refs
    chunks, sheets, rows, _ = c_ref.shape
    lines = chunks * sheets
    steps = rows // SUBLANES
    plane = source_plane(loc, energy, rows, chunks * LANES, plate)
    mine = own_cells[...]
    in_low = lax.broadcasted_iota(jnp.int32, mine.shape, 1) % (2 * sheets) < sheets
    swapped[...] = jnp.where(
        in_low, pltpu.roll(mine, LANES - sheets, 1), pltpu.roll(mine, sheets, 1)
    )

    lane = lax.broadcasted_iota(jnp.int32, (SUBLANES, LANES), 1)
    is_first, is_last = lane == 0, lane == LANES - 1
    for r in range(steps):
        at = slice(r * SUBLANES, (r + 1) * SUBLANES)
        before_t, before_c = None, None
        for z in range(sheets):
            ts = [t_ref[z, at, part_of(y)] for y in range(chunks)]
            cs = [half_conduct(b_ref[z, at, part_of(y)], ts[y]) for y in range(chunks)]
            t_turned = [pltpu.roll(v, LANES - 1, 1) for v in ts]
            c_turned = [pltpu.roll(v, LANES - 1, 1) for v in cs]
            flux = []
            for y in range(chunks):
                if y < chunks - 1:
                    t_next = jnp.where(is_last, t_turned[y + 1], t_turned[y])
                    c_next = jnp.where(is_last, c_turned[y + 1], c_turned[y])
                    flux.append((cs[y] + c_next) * (t_next - ts[y]))
                else:
                    inside = (cs[y] + c_turned[y]) * (t_turned[y] - ts[y])
                    flux.append(jnp.where(is_last, 0.0, inside))
            turned = [pltpu.roll(v, 1, 1) for v in flux]
            for y in range(chunks):
                from_low = jnp.where(is_first, turned[y - 1] if y else 0.0, turned[y])
                total = ts[y] + (flux[y] - from_low)
                if z == 0:
                    total = total + plane[at, part_of(y)]
                else:
                    across = (before_c[y] + cs[y]) * (ts[y] - before_t[y])
                    total = total - across
                    total_ref[y, z - 1, at, :] += across
                total_ref[y, z, at, :] = total
                c_ref[y, z, at, :] = cs[y]
                t_s[y, z, at, :] = ts[y]
            before_t, before_c = ts, cs

    at = 0
    for n, members in enumerate(line_groups(chunks, sheets)):

        def cond(k):
            return jnp.stack([c_ref[y, z, pl.ds(k, SUBLANES, stride=steps), :] for y, z in members], 0)

        def keep(k, w, inv, p):
            w_ref[k, at : at + len(members)] = w
            i_ref[k, at : at + len(members)] = inv
            p_ref[k, at : at + len(members)] = p

        block = factor(cond, steps, keep)
        for i, q in enumerate(COEFS):
            for j in range(len(members)):
                first = (at + j) * SUBLANES
                q_s[i, first : first + SUBLANES, :] = block[q][j]
        if n > 0:
            x_eliminate(
                lambda y, z, k: total_ref[y, z, pl.ds(k, SUBLANES, stride=steps), :],
                members, at, w_ref, i_ref, p_ref, h_ref, at - 2 * sheets, ends_ref,
            )
        for k in range(steps):
            for i, (y, z) in enumerate(members):
                t_out[k, at + i] = t_s[y, z, pl.ds(k, SUBLANES, stride=steps), :]
        at += len(members)

    segments = [
        {q: q_s[n, pl.ds(s, lines, stride=SUBLANES), :] for n, q in enumerate(COEFS)}
        for s in range(SUBLANES)
    ]
    whole, levels = tree(segments, join_coefs)
    for (offset, _), level in zip(node_offsets(SUBLANES), levels):
        for n, values in enumerate(level):
            for i in range(3):
                links[offset + n, i] = values[i]
    for n, q in enumerate(COEFS):
        view[n] = whole[q]


def x_factor(loc, energy, t, b, plate, own_cells):
    sheets, rows, columns = t.shape
    chunks = columns // LANES
    lines = chunks * sheets
    steps = rows // SUBLANES
    field = shape_of(chunks, sheets, rows, LANES)
    stored = shape_of(steps, lines, SUBLANES, LANES)
    return pl.pallas_call(
        functools.partial(x_factor_kernel, plate),
        in_specs=[IN_VMEM] * 5,
        out_shape=[
            field,
            field,
            stored,
            stored,
            stored,
            shape_of(SUBLANES - 1, 3, lines, LANES),
            shape_of(len(COEFS), lines, LANES),
            shape_of(steps, max(1, lines - 2 * sheets), SUBLANES, LANES),
            shape_of(2, lines * SUBLANES, LANES),
            stored,
            shape_of(*own_cells.shape),
        ],
        scratch_shapes=[
            pltpu.VMEM((len(COEFS), lines * SUBLANES, LANES), F32),
            pltpu.VMEM((chunks, sheets, rows, LANES), F32),
        ],
        compiler_params=params(),
        cost_estimate=pl.CostEstimate(flops=40 * t.size, bytes_accessed=28 * t.size, transcendentals=0),
    )(loc, energy, t, b, own_cells)


def x_target_kernel(own_cells, total_ref, near, far, *refs):
    w_ref, i_ref, p_ref, links, view, ends_ref, h_ref, own, send, q_s = refs
    chunks, sheets, rows, _ = total_ref.shape
    lines = chunks * sheets
    steps = rows // SUBLANES

    place = lax.axis_index("gy")
    inner = (place > 0) & (place < lax.axis_size("gy") - 1)
    lane = lax.broadcasted_iota(jnp.int32, (SUBLANES, LANES), 1)
    side = 2 * sheets
    is_near = (lane % side >= sheets).astype(jnp.int32) == place % 2
    t, c = (
        jnp.where(is_near, near[at, :], jnp.where(inner, far[at, :], 0.0))
        for at in (slice(0, SUBLANES), slice(SUBLANES, 2 * SUBLANES))
    )
    face = jnp.where(c > 0.0, own_cells[SUBLANES:, :] + c, 0.0)
    flux = face * (t - own_cells[:SUBLANES, :])

    def cells(y, z, k):
        at = k * side + (sheets + z if y == 0 else z)
        edge = 0 if y == 0 else LANES - 1
        inflow = jnp.where(lane == edge, flux[:, at : at + 1], 0.0)
        return total_ref[y, z, pl.ds(k, SUBLANES, stride=steps), :] + inflow

    members = line_groups(chunks, sheets)[0]
    x_eliminate(cells, members, 0, w_ref, i_ref, p_ref, h_ref, 0, q_s)
    split = len(members)
    items = [
        tuple(
            jnp.concatenate(
                [
                    q_s[q, pl.ds(s, split, stride=SUBLANES), :],
                    ends_ref[q, pl.ds(split * SUBLANES + s, lines - split, stride=SUBLANES), :],
                ],
                0,
            )
            for q in range(2)
        )
        for s in range(SUBLANES)
    ]
    for offset, count in node_offsets(SUBLANES):
        joined = []
        for n in range(count):
            ties = tuple(links[offset + n, i] for i in range(3))
            both, flux = join_targets(items[2 * n], items[2 * n + 1], ties)
            own[offset + n] = flux
            joined.append(both)
        items = joined
    for n, q in enumerate(COEFS):
        send[q] = view[n]
    send[FIRST], send[LAST] = items[0]


def x_target(own_cells, total, near, far, w, inv, p, links, view, ends):
    chunks, sheets, rows, _ = total.shape
    lines = chunks * sheets
    steps = rows // SUBLANES
    return pl.pallas_call(
        x_target_kernel,
        out_shape=[
            shape_of(steps, 2 * sheets, SUBLANES, LANES),
            shape_of(SUBLANES - 1, lines, LANES),
            shape_of(7, lines, LANES),
        ],
        scratch_shapes=[
            pltpu.VMEM((2, 2 * sheets * SUBLANES, LANES), F32),
        ],
        compiler_params=params(),
    )(own_cells, total, near, far, w, inv, p, links, view, ends)


def stages_of(axis):
    return lax.axis_size(axis).bit_length() - 1


def swap(value, axis, flip):
    count = lax.axis_size(axis)
    return lax.ppermute(value, axis, [(i, i ^ flip) for i in range(count)])


def on_right(axis, stage):
    return (lax.axis_index(axis) >> stage) % 2 == 1


def toward(right, block):
    return (
        jnp.where(right, block[R00], block[RLL]),
        jnp.where(right, block[FIRST], block[LAST]),
        jnp.where(right, block[C0], block[CL]),
    )


def join(a, b):
    joined, ties = join_coefs(a, b)
    (joined[FIRST], joined[LAST]), flux = join_targets((a[FIRST], a[LAST]), (b[FIRST], b[LAST]), ties)
    return joined, (flux, ties[1], ties[2])


def ordered(right, own, other):
    first = [jnp.where(right, theirs, mine) for mine, theirs in zip(own, other)]
    second = [jnp.where(right, mine, theirs) for mine, theirs in zip(own, other)]
    return first, second


def flips_of(width):
    return ORDER if width == 2 else range(1, 1 << width)


def join_kernel(axis, stage, width, last, *refs):
    count = 1 << width
    at = {flip: 1 + n for n, flip in enumerate(flips_of(width))}
    blocks = [[refs[at.get(i, 0)][q] for q in range(7)] for i in range(count)]
    send = refs[-1 - width]
    links = refs[-width:]
    for bit in range(width):
        right = on_right(axis, stage + bit)
        for i in range(count):
            if not i >> bit & 1:
                j = i | 1 << bit
                blocks[i], blocks[j] = ordered(right, blocks[i], blocks[j])
    for bit in range(width):
        pairs = [join(blocks[i], blocks[i + 1]) for i in range(0, len(blocks), 2)]
        blocks = [p[0] for p in pairs]
        ties = [p[1] for p in pairs]
        for upper in range(bit + 1, width):
            right = on_right(axis, stage + upper)
            ties = [
                tuple(jnp.where(right, v, u) for u, v in zip(ties[i], ties[i + 1]))
                for i in range(0, len(ties), 2)
            ]
        for i in range(3):
            links[bit][i] = ties[0][i]
    (whole,) = blocks
    if last:
        for n, value in enumerate(toward(on_right(axis, stage + width), whole)):
            send[n] = value
    else:
        for q in range(7):
            send[q] = whole[q]


def join_stage(own, got, axis, stage, width, last, after):
    lines = own.shape[1]
    return pl.pallas_call(
        functools.partial(join_kernel, axis, stage, width, last),
        in_specs=[IN_VMEM] * (1 + len(got)) + [ANYWHERE] * len(after),
        out_shape=[shape_of(3 if last else 7, lines, LANES)] + [shape_of(3, lines, LANES)] * width,
        compiler_params=params(),
    )(own, *got, *after)


def gather_line(view, axis, widest=1, meanwhile=(), cross=False):
    stages = stages_of(axis)
    links, stage = [], 0
    while stage < stages - 1:
        width = min(widest, stages - 1 - stage)
        got = [swap(view, axis, flip << stage) for flip in flips_of(width)]
        last = stage + width == stages - 1
        view, *ties = join_stage(view, got, axis, stage, width, last, meanwhile)
        links += ties
        stage += width
        meanwhile = ()
    return view, swap(view, axis, 1 << stage | (cross and stage > 0)), links


def top_flux(axis, stages, own, got):
    right = on_right(axis, stages - 1)
    face = own[2] + got[2]
    jump = jnp.where(right, own[1] - got[1], got[1] - own[1])
    return jump * face * inverse(1.0 + face * (own[0] + got[0]))


def block_ends(axis, stages, links):
    shape = links[0].shape[1:] if links else None
    right = on_right(axis, stages - 1)
    zero = jnp.zeros(shape, F32)
    low, high = zero, zero
    unit_low = zero + jnp.where(right, -1.0, 0.0)
    unit_high = zero + jnp.where(right, 0.0, 1.0)
    for stage in range(stages - 2, -1, -1):
        tie = links[stage]
        right = on_right(axis, stage)
        flux = between(tie[0], tie[1], tie[2], low, high)
        unit = between(0.0, tie[1], tie[2], unit_low, unit_high)
        low, high = jnp.where(right, -flux, low), jnp.where(right, high, flux)
        unit_low, unit_high = jnp.where(right, -unit, unit_low), jnp.where(right, unit_high, unit)
    return (low, high), (unit_low, unit_high)


def natural(index, parts):
    span = SUBLANES * parts
    local = index % span
    return index - local + local % SUBLANES * parts + local // SUBLANES


def turn_matrix(shape, from_natural, parts):
    row = lax.broadcasted_iota(jnp.int32, shape, 0)
    column = lax.broadcasted_iota(jnp.int32, shape, 1) % LANES
    hit = natural(row, parts) == column if from_natural else row == natural(column, parts)
    return jnp.where(hit, 1.0, 0.0).astype(jnp.bfloat16)


def turned(matrix, field, rows=None):
    high = field.astype(jnp.bfloat16).astype(F32)
    both = jnp.concatenate([high, field - high], 1)
    if rows:
        both = jnp.concatenate(
            [jnp.broadcast_to(both[n : n + 1, :], (rows, 2 * LANES)) for n in range(field.shape[0])], 0
        )
    both = both.astype(jnp.bfloat16)
    return lax.dot_general(
        matrix, both, (((1,), (1,)), ((), ())), preferred_element_type=F32
    )


def y_factor_kernel(c_ref, after, w_ref, i_ref, p_ref, inner, outer, view, to_y, to_x, unit_low, unit_high, c_s, q_s, r_s):
    chunks, sheets, rows, _ = c_ref.shape
    each = LANES // rows
    pairs = sheets // each
    x_steps = rows // SUBLANES
    steps = LANES // SUBLANES
    to_y[...] = turn_matrix(to_y.shape, True, steps)
    to_x[...] = turn_matrix(to_x.shape, False, x_steps)
    for m in range(pairs):
        for y in range(chunks):
            block = jnp.concatenate(
                [
                    c_ref[y, m * each + i, pl.ds(k, SUBLANES, stride=x_steps), :]
                    for i in range(each)
                    for k in range(x_steps)
                ],
                0,
            )
            c_s[m, part_of(y), :] = block.T

    members = [(y, m) for y in range(chunks) for m in range(pairs)]
    lines = len(members)

    def cond(k):
        return jnp.stack([c_s[m, pl.ds(y * LANES + k, SUBLANES, stride=steps), :] for y, m in members], 0)

    def keep(k, w, inv, p):
        w_ref[k] = w
        i_ref[k] = inv
        p_ref[k] = p

    block = factor(cond, steps, keep)
    for n, q in enumerate(COEFS):
        for i in range(lines):
            q_s[n, i * SUBLANES : (i + 1) * SUBLANES, :] = block[q][i]
    segments = [
        {q: q_s[n, pl.ds(s, lines, stride=SUBLANES), :] for n, q in enumerate(COEFS)}
        for s in range(SUBLANES)
    ]
    whole, levels = tree(segments, join_coefs)
    for (offset, _), level in zip(node_offsets(SUBLANES), levels):
        for n, values in enumerate(level):
            for i in range(3):
                inner[offset + n, i] = values[i]
    for n, q in enumerate(COEFS):
        r_s[n] = whole[q]
    parts = [
        {q: r_s[n, y * pairs : (y + 1) * pairs, :] for n, q in enumerate(COEFS)} for y in range(chunks)
    ]
    whole, levels = tree(parts, join_coefs)
    for (offset, _), level in zip(node_offsets(chunks), levels):
        for n, values in enumerate(level):
            for i in range(3):
                outer[offset + n, i] = values[i]
    for n, q in enumerate(COEFS):
        view[n] = whole[q]

    one = jnp.ones((pairs, LANES), F32)
    for n, (low, high, field) in enumerate(((one, 0.0 * one, unit_low), (0.0 * one, one, unit_high))):
        for y, pair in enumerate(tree_ends(chunks, outer, nothing, low, high)):
            for i in range(2):
                r_s[2 * n + i, y * pairs : (y + 1) * pairs, :] = pair[i]
        for s, pair in enumerate(tree_ends(SUBLANES, inner, nothing, r_s[2 * n], r_s[2 * n + 1])):
            for i in range(2):
                q_s[2 * n + i, pl.ds(s, lines, stride=SUBLANES), :] = pair[i]
        low, value = (
            jnp.stack(
                [q_s[2 * n + i, j * SUBLANES : (j + 1) * SUBLANES, :] for j in range(lines)], 0
            )
            for i in range(2)
        )
        for k in range(steps - 1, -1, -1):
            value = w_ref[k] * value + p_ref[k] * low
            for j, (y, m) in enumerate(members):
                field[y, k * SUBLANES : (k + 1) * SUBLANES, part_of(m)] = value[j]


def y_factor(c, after):
    chunks, sheets, rows, _ = c.shape
    pairs = sheets * rows // LANES
    lines = chunks * pairs
    stored = shape_of(LANES // SUBLANES, lines, SUBLANES, LANES)
    matrix = jax.ShapeDtypeStruct((LANES, 2 * LANES), jnp.bfloat16)
    return pl.pallas_call(
        y_factor_kernel,
        in_specs=[IN_VMEM, ANYWHERE],
        out_shape=[
            stored,
            stored,
            stored,
            shape_of(SUBLANES - 1, 3, lines, LANES),
            shape_of(chunks - 1, 3, pairs, LANES),
            shape_of(len(COEFS), pairs, LANES),
            matrix,
            matrix,
            shape_of(chunks, LANES, pairs * LANES),
            shape_of(chunks, LANES, pairs * LANES),
        ],
        scratch_shapes=[
            pltpu.VMEM((pairs, chunks * LANES, LANES), F32),
            pltpu.VMEM((len(COEFS), lines * SUBLANES, LANES), F32),
            pltpu.VMEM((len(COEFS), lines, LANES), F32),
        ],
        compiler_params=params(),
        cost_estimate=pl.CostEstimate(flops=20 * c.size, bytes_accessed=16 * c.size, transcendentals=0),
    )(c, after)


def z_factor_kernel(c_ref, after, w_ref, i_ref):
    sheets = c_ref.shape[1]
    ground = 1.0
    for z in range(sheets - 1):
        face = c_ref[:, z] + c_ref[:, z + 1]
        inv = inverse(ground + face)
        w = face * inv
        i_ref[z] = inv
        w_ref[z] = w
        ground = 1.0 + w * ground
    i_ref[sheets - 1] = inverse(ground)


def z_factor(c, after):
    chunks, sheets, rows, _ = c.shape
    return pl.pallas_call(
        z_factor_kernel,
        in_specs=[IN_VMEM, ANYWHERE],
        out_shape=[
            shape_of(sheets - 1, chunks, rows, LANES),
            shape_of(sheets, chunks, rows, LANES),
        ],
        compiler_params=params(),
        cost_estimate=pl.CostEstimate(flops=10 * c.size, bytes_accessed=12 * c.size, transcendentals=0),
    )(c, after)


def join_tree(items, links, own):
    for offset, count in node_offsets(len(items)):
        joined = []
        for n in range(count):
            tie = tuple(links[offset + n, i] for i in range(3))
            both, flux = join_targets(items[2 * n], items[2 * n + 1], tie)
            own[offset + n] = flux
            joined.append(both)
        items = joined
    return items[0]


def tree_ends(leaves, links, own, low, high):
    levels = [
        [(own(offset + n), links[offset + n, 1], links[offset + n, 2]) for n in range(count)]
        for offset, count in node_offsets(leaves)
    ]
    return descend(levels, low, high)


def nothing(node):
    return 0.0


def y_prepare_kernel(stages, *refs):
    ties = refs[: stages - 1]
    xw, xh, xm, xp, x_links, x_own, t_ref, to_y, y_low, y_high = refs[stages - 1 : stages + 9]
    base, response, to_first, to_last, fixed, f_s, g_s = refs[stages + 9 :]
    x_steps, lines = xw.shape[:2]
    chunks = base.shape[0]
    sheets = lines // chunks
    rows = x_steps * SUBLANES

    ends, units = block_ends("gx", stages, ties)
    for n, (own, (low, high)) in enumerate(((lambda i: x_own[i], ends), (nothing, units))):
        for s, pair in enumerate(tree_ends(SUBLANES, x_links, own, low, high)):
            for i in range(2):
                f_s[n, i, pl.ds(s, lines, stride=SUBLANES), :] = pair[i]
    first = 0
    for n, members in enumerate(line_groups(chunks, sheets)):
        at = slice(first, first + len(members))
        h_ref_of, h_at = (xh, at) if n == 0 else (xm, slice(first - 2 * sheets, at.stop - 2 * sheets))
        (low, value), (unit_low, unit) = (
            [
                jnp.stack(
                    [f_s[q, i, j * SUBLANES : (j + 1) * SUBLANES, :] for j in range(at.start, at.stop)], 0
                )
                for i in range(2)
            ]
            for q in range(2)
        )
        for k in range(x_steps - 1, -1, -1):
            w, p = xw[k, at], xp[k, at]
            value = w * value + (h_ref_of[k, h_at] + p * low)
            unit = w * unit + p * unit_low
            field = value - t_ref[k, at]
            for j, (y, z) in enumerate(members):
                place = z * rows + k * SUBLANES
                g_s[0, y, place : place + SUBLANES, :] = field[j]
                g_s[1, y, place : place + SUBLANES, :] = unit[j]
        first = at.stop

    totals = [None, None]
    for y in range(chunks):
        field = turned(to_y[...], g_s[0, y])
        answer = turned(to_y[...], g_s[1, y])
        base[y] = field
        response[y] = answer
        for i, (unit, weight) in enumerate(((y_low, to_first), (y_high, to_last))):
            weight[y] = unit[y] * answer
            part = unit[y] * field
            totals[i] = part if y == 0 else totals[i] + part
    for i in range(2):
        put_sums(fixed.at[i], totals[i])


def put_sums(out, field):
    total = jnp.sum(field, 0, keepdims=True)
    for m in range(out.shape[0]):
        out[m : m + 1, :] = total[:, part_of(m)]


def y_prepare(ties, xw, xh, xm, xp, x_links, x_own, t, to_y, unit_low, unit_high):
    chunks = unit_low.shape[0]
    x_steps, lines = xw.shape[:2]
    width = lines // chunks * x_steps * SUBLANES
    field = shape_of(chunks, LANES, width)
    return pl.pallas_call(
        functools.partial(y_prepare_kernel, len(ties) + 1),
        out_shape=[field] * 4 + [shape_of(2, width // LANES, LANES)],
        scratch_shapes=[
            pltpu.VMEM((2, 2, lines * SUBLANES, LANES), F32),
            pltpu.VMEM((2, chunks, width, LANES), F32),
        ],
        compiler_params=params(),
        cost_estimate=pl.CostEstimate(flops=8 * t.size, bytes_accessed=16 * t.size, transcendentals=0),
    )(*ties, xw, xh, xm, xp, x_links, x_own, t, to_y, unit_low, unit_high)


def y_target_kernel(stages, own, got, to_first, to_last, fixed, view, to_y, spread, send, r_s):
    chunks, _, width = to_first.shape
    sheets = own.shape[1] // chunks
    rows = width // sheets

    flux = top_flux("gx", stages, own, got)
    line_of = {member: n for n, member in enumerate(sum(line_groups(chunks, sheets), []))}
    totals = [None, None]
    for y in range(chunks):
        own_flux = jnp.concatenate([flux[line_of[y, z] : line_of[y, z] + 1, :] for z in range(sheets)], 0)
        wide = turned(to_y[...], own_flux, rows)
        spread[y] = wide
        for i, weight in enumerate((to_first, to_last)):
            part = weight[y] * wide
            totals[i] = part if y == 0 else totals[i] + part
    for n, q in enumerate(COEFS):
        send[q] = view[n]
    for i, q in enumerate((FIRST, LAST)):
        put_sums(r_s.at[i], totals[i])
        send[q] = fixed[i] + r_s[i]


def y_target(own, got, to_first, to_last, fixed, view, to_y):
    pairs = view.shape[1]
    return pl.pallas_call(
        functools.partial(y_target_kernel, stages_of("gx")),
        out_shape=[shape_of(*to_first.shape), shape_of(7, pairs, LANES)],
        scratch_shapes=[pltpu.VMEM((2, pairs, LANES), F32)],
        compiler_params=params(),
    )(own, got, to_first, to_last, fixed, view, to_y)


def y_eliminate_kernel(base, response, spread, yw, yi, yp, inner, outer, after, *refs):
    h_ref, inner_own, outer_own, q_s, r_s = refs
    chunks, _, width = base.shape
    pairs = width // LANES
    steps = yw.shape[0]
    members = [(y, m) for y in range(chunks) for m in range(pairs)]

    def target(k):
        at = slice(k * SUBLANES, (k + 1) * SUBLANES)
        return jnp.stack(
            [
                base[y, at, part_of(m)] + response[y, at, part_of(m)] * spread[y, at, part_of(m)]
                for y, m in members
            ],
            0,
        )

    def keep(k, h):
        h_ref[k] = h

    ends = eliminate(target, steps, lambda k: yw[k], lambda k: yi[k], lambda k: yp[k], keep)
    for q in range(2):
        for i in range(len(members)):
            q_s[q, i * SUBLANES : (i + 1) * SUBLANES, :] = ends[q][i]
    items = [
        tuple(q_s[q, pl.ds(s, len(members), stride=SUBLANES), :] for q in range(2))
        for s in range(SUBLANES)
    ]
    r_s[0], r_s[1] = join_tree(items, inner, inner_own)
    items = [tuple(r_s[q, y * pairs : (y + 1) * pairs, :] for q in range(2)) for y in range(chunks)]
    join_tree(items, outer, outer_own)


def y_eliminate(base, response, spread, yw, yi, yp, inner, outer, after):
    y_lines = yw.shape[1]
    pairs = outer.shape[2]
    chunks = y_lines // pairs
    return pl.pallas_call(
        y_eliminate_kernel,
        in_specs=[IN_VMEM] * 8 + [ANYWHERE],
        out_shape=[
            shape_of(*yw.shape),
            shape_of(SUBLANES - 1, y_lines, LANES),
            shape_of(chunks - 1, pairs, LANES),
        ],
        scratch_shapes=[
            pltpu.VMEM((2, y_lines * SUBLANES, LANES), F32),
            pltpu.VMEM((2, y_lines, LANES), F32),
        ],
        compiler_params=params(),
        cost_estimate=pl.CostEstimate(flops=8 * base.size, bytes_accessed=16 * base.size, transcendentals=0),
    )(base, response, spread, yw, yi, yp, inner, outer, after)


def z_solve(zw, zi, field, at, keep):
    sheets = zi.shape[0]
    rhs, kept = None, []
    for z in range(sheets):
        rhs = field(z) if z == 0 else field(z) + zw[z - 1, at] * rhs
        kept.append(rhs * zi[z, at])
    value = kept[-1]
    keep(sheets - 1, value)
    for z in range(sheets - 2, -1, -1):
        value = zw[z, at] * value + kept[z]
        keep(z, value)


def finish_prepare_kernel(stages, *refs):
    ties = refs[: stages - 1]
    yw, yh, yp, inner, inner_own, outer, outer_own, zw, zi, t_ref, to_x = refs[stages - 1 : stages + 10]
    base, response, r_s, e_s, u_s = refs[stages + 10 :]
    chunks, sheets, rows, _ = base.shape
    each = LANES // rows
    pairs = sheets // each
    steps = yw.shape[0]
    lines = chunks * pairs

    ends, units = block_ends("gy", stages, ties)
    both = (
        (lambda i: outer_own[i], lambda i: inner_own[i], ends),
        (nothing, nothing, units),
    )
    for n, (upper, lower, (low, high)) in enumerate(both):
        for y, pair in enumerate(tree_ends(chunks, outer, upper, low, high)):
            for i in range(2):
                r_s[n, i, y * pairs : (y + 1) * pairs, :] = pair[i]
        for s, pair in enumerate(tree_ends(SUBLANES, inner, lower, r_s[n, 0], r_s[n, 1])):
            for i in range(2):
                e_s[n, i, pl.ds(s, lines, stride=SUBLANES), :] = pair[i]
    (low, value), (unit_low, unit) = (
        [
            jnp.stack([e_s[q, i, n * SUBLANES : (n + 1) * SUBLANES, :] for n in range(lines)], 0)
            for i in range(2)
        ]
        for q in range(2)
    )
    for k in range(steps - 1, -1, -1):
        w, p = yw[k], yp[k]
        value = w * value + (yh[k] + p * low)
        unit = w * unit + p * unit_low
        for y in range(chunks):
            for m in range(pairs):
                place = pl.ds(y * LANES + k, SUBLANES, stride=steps)
                u_s[0, m, place, :] = value[y * pairs + m]
                u_s[1, m, place, :] = unit[y * pairs + m]

    for y in range(chunks):
        part = part_of(y)
        fields = [turned(to_x[...], u_s[0, m, part, :]) for m in range(pairs)]

        def field(z):
            at = z % each * rows
            return fields[z // each][at : at + rows, :]

        def keep(z, value):
            base[y, z] = t_ref[z, :, part] + value

        z_solve(zw, zi, field, y, keep)
        for m in range(pairs):
            units = turned(to_x[...], u_s[1, m, part, :])
            for i in range(each):
                response[y, m * each + i] = units[i * rows : (i + 1) * rows, :]


def finish_prepare(ties, yw, yh, yp, inner, inner_own, outer, outer_own, zw, zi, t, to_x):
    sheets, rows, columns = t.shape
    chunks = columns // LANES
    pairs = sheets * rows // LANES
    lines = chunks * pairs
    field = shape_of(chunks, sheets, rows, LANES)
    return pl.pallas_call(
        functools.partial(finish_prepare_kernel, len(ties) + 1),
        out_shape=[field, field],
        scratch_shapes=[
            pltpu.VMEM((2, 2, lines, LANES), F32),
            pltpu.VMEM((2, 2, lines * SUBLANES, LANES), F32),
            pltpu.VMEM((2, pairs, columns, LANES), F32),
        ],
        compiler_params=params(),
        cost_estimate=pl.CostEstimate(flops=12 * t.size, bytes_accessed=20 * t.size, transcendentals=0),
    )(*ties, yw, yh, yp, inner, inner_own, outer, outer_own, zw, zi, t, to_x)


def finish_kernel(stages, own, got, base, response, zw, zi, to_x, out, o_s, sems):
    chunks, sheets, rows, _ = base.shape
    each = LANES // rows
    pairs = sheets // each
    copies, _, wide = o_s.shape

    flux = top_flux("gy", stages, own, got)
    spread = [
        turned(to_x[...], flux[m : m + 1, :], LANES) for m in range(pairs)
    ]
    started = []
    for n in range(copies):
        for y in range(n * chunks // copies, (n + 1) * chunks // copies):
            part = part_of(y - n * chunks // copies)

            def field(z):
                at = z % each * rows
                return response[y, z] * spread[z // each][at : at + rows, :]

            def keep(z, value):
                o_s[n, z * rows : (z + 1) * rows, part] = base[y, z] + value

            z_solve(zw, zi, field, y, keep)
        copy = pltpu.make_async_copy(o_s.at[n], out.at[:, pl.ds(n * wide, wide)], sems.at[n])
        copy.start()
        started.append(copy)
    for copy in started:
        copy.wait()


def finish(own, got, base, response, zw, zi, to_x):
    chunks, sheets, rows, _ = base.shape
    copies = chunks
    return pl.pallas_call(
        functools.partial(finish_kernel, stages_of("gy")),
        out_shape=shape_of(sheets * rows, chunks * LANES),
        out_specs=ANYWHERE,
        scratch_shapes=[
            pltpu.VMEM((copies, sheets * rows, chunks * LANES // copies), F32),
            pltpu.SemaphoreType.DMA((copies,)),
        ],
        compiler_params=params(),
    )(own, got, base, response, zw, zi, to_x).reshape(sheets, rows, chunks * LANES)


def per_device(temperature, base, locations, energy):
    columns = temperature.shape[2]
    gy = lax.axis_size("gy")
    t, b, loc, heat, packed = load(temperature, base, locations[None], energy[None])
    near = swap(packed, "gy", 1)
    far = lax.ppermute(packed, "gy", [(i, ((i + 1) % gy ^ 1) - 1 if i else gy - 1) for i in range(gy)])
    c, total, xw, xi, xp, x_links, x_view, xm, ends, t_steps, swapped = x_factor(loc, heat, t, b, columns * gy, packed)
    xh, x_own, view = x_target(swapped, total, near, far, xw, xi, xp, x_links, x_view, ends)
    yw, yi, yp, inner, outer, y_view, to_y, to_x, unit_low, unit_high = y_factor(c, x_view)
    zw, zi = z_factor(c, view)
    own, got, ties = gather_line(view, "gx", 2, (y_view, zw))
    base, response, to_first, to_last, fixed = y_prepare(
        ties, xw, xh, xm, xp, x_links, x_own, t_steps, to_y, unit_low, unit_high
    )
    spread, view = y_target(own, got, to_first, to_last, fixed, y_view, to_y)
    yh, inner_own, outer_own = y_eliminate(base, response, spread, yw, yi, yp, inner, outer, view)
    own, got, ties = gather_line(view, "gy", meanwhile=(yh,), cross=True)
    base, response = finish_prepare(
        ties, yw, yh, yp, inner, inner_own, outer, outer_own, zw, zi, t, to_x
    )
    return finish(own, got, base, response, zw, zi, to_x)


def solution(mesh):
    in_specs = (P(None, "gx", "gy"), P(None, "gx", "gy"), P(), P())
    out_specs = P(None, "gx", "gy")
    return jax.shard_map(
        per_device, mesh=mesh, in_specs=in_specs, out_specs=out_specs, check_vma=False
    )
```

```python
import functools

import jax
import jax.numpy as jnp
from jax import lax
from jax.experimental import pallas as pl
from jax.experimental.pallas import tpu as pltpu
from jax.sharding import PartitionSpec as P

RATE = 2000.0
THERMAL_GROWTH = 0.8
LANES = 128
SUBLANES = 8
F32 = jnp.float32
MIB = 1024 * 1024
OUT_COPIES = 4
ANYWHERE = pl.BlockSpec(memory_space=pl.ANY)
IN_HBM = pl.BlockSpec(memory_space=pltpu.HBM)
IN_VMEM = pl.BlockSpec(memory_space=pltpu.VMEM)

R00, R0L, RLL, FIRST, LAST, C0, CL = range(7)
COEFS = (R00, R0L, RLL, C0, CL)


def params(limit=40):
    return pltpu.CompilerParams(vmem_limit_bytes=limit * MIB)


def shape_of(*sizes):
    return jax.ShapeDtypeStruct(sizes, F32)


def half_conduct(base, temperature):
    return base * (0.5 * RATE + (0.5 * RATE * THERMAL_GROWTH) * temperature)


def inverse(x):
    guess = pl.reciprocal(x, approx=True)
    return guess * (2.0 - x * guess)


def join_coefs(a, b):
    face = a[CL] + b[C0]
    inv = face * inverse(1.0 + face * (a[RLL] + b[R00]))
    left = a[R0L] * inv
    right = b[R0L] * inv
    joined = {
        R00: a[R00] - left * a[R0L],
        R0L: left * b[R0L],
        RLL: b[RLL] - right * b[R0L],
        C0: a[C0],
        CL: b[CL],
    }
    return joined, (inv, right, left)


def join_targets(a, b, links):
    inv, right, left = links
    jump = b[0] - a[1]
    return (a[0] + left * jump, b[1] - right * jump), jump * inv


def between(own, right, left, low, high):
    return own + right * high - left * low


def tree(items, join):
    levels = []
    while len(items) > 1:
        pairs = [join(items[i], items[i + 1]) for i in range(0, len(items), 2)]
        items = [p[0] for p in pairs]
        levels.append([p[1] for p in pairs])
    return items[0], levels


def descend(levels, low, high):
    ends = [(low, high)]
    for level in reversed(levels):
        below = []
        for (lo, hi), (own, right, left) in zip(ends, level):
            flux = between(own, right, left, lo, hi)
            below += [(lo, flux), (-flux, hi)]
        ends = below
    return ends


def node_offsets(leaves):
    offsets, at, count = [], 0, leaves // 2
    while count:
        offsets.append((at, count))
        at += count
        count //= 2
    return offsets


def factor(cond, steps, keep):
    here = cond(0)
    c_first = here
    one = jnp.ones_like(here)
    ground, path, first_first = one, one, None
    for k in range(steps - 1):
        following = cond(k + 1)
        face = here + following
        inv = inverse(ground + face)
        w = face * inv
        p = path * inv
        keep(k, w, inv, p)
        step = path * p
        first_first = step if first_first is None else first_first + step
        path = path * w
        ground = 1.0 + w * ground
        here = following
    inv = inverse(ground)
    p = path * inv
    keep(steps - 1, inv, inv, p)
    return {R00: first_first + path * p, R0L: p, RLL: inv, C0: c_first, CL: here}


def eliminate(target, steps, w, inv, p, keep):
    rhs = target(0)
    first = None
    for k in range(steps):
        h = rhs * inv(k)
        keep(k, h)
        step = rhs * p(k)
        first = step if first is None else first + step
        if k < steps - 1:
            rhs = target(k + 1) + w(k) * rhs
    return first, h


def is_odd(axis):
    return lax.axis_index(axis) % 2 == 1


def fold(cells, used):
    steps = cells.shape[0] // SUBLANES
    total = cells[pl.ds(0, SUBLANES, stride=steps), :]
    lane = lax.broadcasted_iota(jnp.int32, total.shape, 1)
    for k in range(1, steps):
        part = pltpu.roll(cells[pl.ds(k, SUBLANES, stride=steps), :], k * used, 1)
        total = jnp.where(lane // used == k, part, total)
    return total


def load_kernel(t_hbm, b_hbm, loc_hbm, energy_hbm, t_out, b_out, loc, energy, packed, cells, sems):
    sheets, rows, columns = t_hbm.shape
    halves = 2
    copies = []
    for n in range(halves):
        part = pl.ds(n * sheets // halves, sheets // halves)
        for i, (src, dst) in enumerate(((t_hbm, t_out), (b_hbm, b_out))):
            copies.append(pltpu.make_async_copy(src.at[part], dst.at[part], sems.at[i, n]))
    copies.append(pltpu.make_async_copy(loc_hbm, loc, sems.at[2, 0]))
    copies.append(pltpu.make_async_copy(energy_hbm, energy, sems.at[2, 1]))
    for copy in copies:
        copy.start()
    lane = lax.broadcasted_iota(jnp.int32, (rows, LANES), 1)
    edge_t = jnp.zeros((rows, LANES), F32)
    edge_c = edge_t
    for n in range(halves):
        for copy in copies[2 * n : 2 * n + 2]:
            copy.wait()
        for z in range(n * sheets // halves, (n + 1) * sheets // halves):
            for side, part in enumerate((slice(0, LANES), slice(columns - LANES, columns))):
                source = 0 if side == 0 else LANES - 1
                t = t_out[z, :, part]
                c = half_conduct(b_out[z, :, part], t)
                place = lane == sheets * side + z
                edge_t = jnp.where(place, t[:, source : source + 1], edge_t)
                edge_c = jnp.where(place, c[:, source : source + 1], edge_c)
    cells[0], cells[1] = edge_t, edge_c
    for i in range(2):
        packed[i * SUBLANES : (i + 1) * SUBLANES, :] = fold(cells.at[i], 2 * sheets)
    for copy in copies[2 * halves :]:
        copy.wait()


def load(temperature, base, locations, energy):
    sheets, rows, columns = temperature.shape
    assert rows // SUBLANES * 2 * sheets <= LANES and columns > 2 * LANES
    operands = (temperature, base, locations, energy)
    return pl.pallas_call(
        load_kernel,
        in_specs=[IN_HBM] * 4,
        out_shape=[pltpu.VMEM(v.shape, v.dtype) for v in operands]
        + [pltpu.VMEM((2 * SUBLANES, LANES), F32)],
        scratch_shapes=[pltpu.VMEM((2, rows, LANES), F32), pltpu.SemaphoreType.DMA((3, 3))],
        compiler_params=params(),
    )(*[pltpu.with_memory_space_constraint(v, pltpu.HBM) for v in operands])


def source_plane(loc, energy, rows, columns, plate):
    place = loc[...]
    count = place.shape[1]
    local_x = place // plate - lax.axis_index("gx") * rows
    local_y = place % plate - lax.axis_index("gy") * columns
    in_x = lax.broadcasted_iota(jnp.int32, (rows, count), 0) == local_x
    in_y = lax.broadcasted_iota(jnp.int32, (columns, count), 0) == local_y
    by_y = jnp.where(in_y, 1.0, 0.0).astype(jnp.bfloat16)
    left = energy[...]
    plane = None
    for _ in range(3):
        part = left.astype(jnp.bfloat16).astype(F32)
        left = left - part
        term = lax.dot_general(
            jnp.where(in_x, part, 0.0).astype(jnp.bfloat16),
            by_y,
            (((1,), (1,)), ((), ())),
            preferred_element_type=F32,
        )
        plane = term if plane is None else plane + term
    return plane


def part_of(y):
    return slice(y * LANES, (y + 1) * LANES)


def line_groups(chunks, sheets):
    order = [0, chunks - 1] + list(range(1, chunks - 1))
    return [[(y, z) for y in order[i : i + 2] for z in range(sheets)] for i in range(0, chunks, 2)]


def x_eliminate(cells, members, first_line, w_ref, i_ref, p_ref, h_ref, h_line, q_s):
    steps = w_ref.shape[0]
    at = slice(first_line, first_line + len(members))
    kept_at = slice(h_line, h_line + len(members))

    def target(k):
        return jnp.stack([cells(y, z, k) for y, z in members], 0)

    def keep(k, h):
        h_ref[k, kept_at] = h

    ends = eliminate(
        target, steps, lambda k: w_ref[k, at], lambda k: i_ref[k, at], lambda k: p_ref[k, at], keep
    )
    for q in range(2):
        for i in range(len(members)):
            first = (first_line + i) * SUBLANES
            q_s[q, first : first + SUBLANES, :] = ends[q][i]


def x_factor_kernel(plate, loc, energy, t_ref, b_ref, own_cells, *refs):
    c_ref, total_ref, w_ref, i_ref, p_ref, links, view, h_ref, ends_ref, t_out, swapped, q_s, t_s = refs
    chunks, sheets, rows, _ = c_ref.shape
    lines = chunks * sheets
    steps = rows // SUBLANES
    plane = source_plane(loc, energy, rows, chunks * LANES, plate)
    mine = own_cells[...]
    in_low = lax.broadcasted_iota(jnp.int32, mine.shape, 1) % (2 * sheets) < sheets
    swapped[...] = jnp.where(
        in_low, pltpu.roll(mine, LANES - sheets, 1), pltpu.roll(mine, sheets, 1)
    )

    lane = lax.broadcasted_iota(jnp.int32, (SUBLANES, LANES), 1)
    is_first, is_last = lane == 0, lane == LANES - 1
    for r in range(steps):
        at = slice(r * SUBLANES, (r + 1) * SUBLANES)
        before_t, before_c = None, None
        for z in range(sheets):
            ts = [t_ref[z, at, part_of(y)] for y in range(chunks)]
            cs = [half_conduct(b_ref[z, at, part_of(y)], ts[y]) for y in range(chunks)]
            t_turned = [pltpu.roll(v, LANES - 1, 1) for v in ts]
            c_turned = [pltpu.roll(v, LANES - 1, 1) for v in cs]
            flux = []
            for y in range(chunks):
                if y < chunks - 1:
                    t_next = jnp.where(is_last, t_turned[y + 1], t_turned[y])
                    c_next = jnp.where(is_last, c_turned[y + 1], c_turned[y])
                    flux.append((cs[y] + c_next) * (t_next - ts[y]))
                else:
                    inside = (cs[y] + c_turned[y]) * (t_turned[y] - ts[y])
                    flux.append(jnp.where(is_last, 0.0, inside))
            turned = [pltpu.roll(v, 1, 1) for v in flux]
            for y in range(chunks):
                from_low = jnp.where(is_first, turned[y - 1] if y else 0.0, turned[y])
                total = ts[y] + (flux[y] - from_low)
                if z == 0:
                    total = total + plane[at, part_of(y)]
                else:
                    across = (before_c[y] + cs[y]) * (ts[y] - before_t[y])
                    total = total - across
                    total_ref[y, z - 1, at, :] += across
                total_ref[y, z, at, :] = total
                c_ref[y, z, at, :] = cs[y]
                t_s[y, z, at, :] = ts[y]
            before_t, before_c = ts, cs

    at = 0
    for n, members in enumerate(line_groups(chunks, sheets)):

        def cond(k):
            return jnp.stack([c_ref[y, z, pl.ds(k, SUBLANES, stride=steps), :] for y, z in members], 0)

        def keep(k, w, inv, p):
            w_ref[k, at : at + len(members)] = w
            i_ref[k, at : at + len(members)] = inv
            p_ref[k, at : at + len(members)] = p

        block = factor(cond, steps, keep)
        for i, q in enumerate(COEFS):
            for j in range(len(members)):
                first = (at + j) * SUBLANES
                q_s[i, first : first + SUBLANES, :] = block[q][j]
        if n > 0:
            x_eliminate(
                lambda y, z, k: total_ref[y, z, pl.ds(k, SUBLANES, stride=steps), :],
                members, at, w_ref, i_ref, p_ref, h_ref, at - 2 * sheets, ends_ref,
            )
        for k in range(steps):
            for i, (y, z) in enumerate(members):
                t_out[k, at + i] = t_s[y, z, pl.ds(k, SUBLANES, stride=steps), :]
        at += len(members)

    segments = [
        {q: q_s[n, pl.ds(s, lines, stride=SUBLANES), :] for n, q in enumerate(COEFS)}
        for s in range(SUBLANES)
    ]
    whole, levels = tree(segments, join_coefs)
    for (offset, _), level in zip(node_offsets(SUBLANES), levels):
        for n, values in enumerate(level):
            for i in range(3):
                links[offset + n, i] = values[i]
    for n, q in enumerate(COEFS):
        view[n] = whole[q]


def x_factor(loc, energy, t, b, plate, own_cells):
    sheets, rows, columns = t.shape
    chunks = columns // LANES
    lines = chunks * sheets
    steps = rows // SUBLANES
    field = shape_of(chunks, sheets, rows, LANES)
    stored = shape_of(steps, lines, SUBLANES, LANES)
    return pl.pallas_call(
        functools.partial(x_factor_kernel, plate),
        in_specs=[IN_VMEM] * 5,
        out_shape=[
            field,
            field,
            stored,
            stored,
            stored,
            shape_of(SUBLANES - 1, 3, lines, LANES),
            shape_of(len(COEFS), lines, LANES),
            shape_of(steps, max(1, lines - 2 * sheets), SUBLANES, LANES),
            shape_of(2, lines * SUBLANES, LANES),
            stored,
            shape_of(*own_cells.shape),
        ],
        scratch_shapes=[
            pltpu.VMEM((len(COEFS), lines * SUBLANES, LANES), F32),
            pltpu.VMEM((chunks, sheets, rows, LANES), F32),
        ],
        compiler_params=params(),
        cost_estimate=pl.CostEstimate(flops=40 * t.size, bytes_accessed=28 * t.size, transcendentals=0),
    )(loc, energy, t, b, own_cells)


def x_target_kernel(own_cells, total_ref, near, far, *refs):
    w_ref, i_ref, p_ref, links, view, ends_ref, h_ref, own, send, q_s = refs
    chunks, sheets, rows, _ = total_ref.shape
    lines = chunks * sheets
    steps = rows // SUBLANES

    place = lax.axis_index("gy")
    inner = (place > 0) & (place < lax.axis_size("gy") - 1)
    lane = lax.broadcasted_iota(jnp.int32, (SUBLANES, LANES), 1)
    side = 2 * sheets
    is_near = (lane % side >= sheets).astype(jnp.int32) == place % 2
    t, c = (
        jnp.where(is_near, near[at, :], jnp.where(inner, far[at, :], 0.0))
        for at in (slice(0, SUBLANES), slice(SUBLANES, 2 * SUBLANES))
    )
    face = jnp.where(c > 0.0, own_cells[SUBLANES:, :] + c, 0.0)
    flux = face * (t - own_cells[:SUBLANES, :])

    def cells(y, z, k):
        at = k * side + (sheets + z if y == 0 else z)
        edge = 0 if y == 0 else LANES - 1
        inflow = jnp.where(lane == edge, flux[:, at : at + 1], 0.0)
        return total_ref[y, z, pl.ds(k, SUBLANES, stride=steps), :] + inflow

    members = line_groups(chunks, sheets)[0]
    x_eliminate(cells, members, 0, w_ref, i_ref, p_ref, h_ref, 0, q_s)
    split = len(members)
    items = [
        tuple(
            jnp.concatenate(
                [
                    q_s[q, pl.ds(s, split, stride=SUBLANES), :],
                    ends_ref[q, pl.ds(split * SUBLANES + s, lines - split, stride=SUBLANES), :],
                ],
                0,
            )
            for q in range(2)
        )
        for s in range(SUBLANES)
    ]
    for offset, count in node_offsets(SUBLANES):
        joined = []
        for n in range(count):
            ties = tuple(links[offset + n, i] for i in range(3))
            both, flux = join_targets(items[2 * n], items[2 * n + 1], ties)
            own[offset + n] = flux
            joined.append(both)
        items = joined
    for n, q in enumerate(COEFS):
        send[q] = view[n]
    send[FIRST], send[LAST] = items[0]


def x_target(own_cells, total, near, far, w, inv, p, links, view, ends):
    chunks, sheets, rows, _ = total.shape
    lines = chunks * sheets
    steps = rows // SUBLANES
    return pl.pallas_call(
        x_target_kernel,
        out_shape=[
            shape_of(steps, 2 * sheets, SUBLANES, LANES),
            shape_of(SUBLANES - 1, lines, LANES),
            shape_of(7, lines, LANES),
        ],
        scratch_shapes=[
            pltpu.VMEM((2, 2 * sheets * SUBLANES, LANES), F32),
        ],
        compiler_params=params(),
    )(own_cells, total, near, far, w, inv, p, links, view, ends)


def stages_of(axis):
    return lax.axis_size(axis).bit_length() - 1


def swap(value, axis, flip):
    count = lax.axis_size(axis)
    return lax.ppermute(value, axis, [(i, i ^ flip) for i in range(count)])


def on_right(axis, stage):
    return (lax.axis_index(axis) >> stage) % 2 == 1


def toward(right, block):
    return (
        jnp.where(right, block[R00], block[RLL]),
        jnp.where(right, block[FIRST], block[LAST]),
        jnp.where(right, block[C0], block[CL]),
    )


def join(a, b):
    joined, ties = join_coefs(a, b)
    (joined[FIRST], joined[LAST]), flux = join_targets((a[FIRST], a[LAST]), (b[FIRST], b[LAST]), ties)
    return joined, (flux, ties[1], ties[2])


def ordered(right, own, other):
    first = [jnp.where(right, theirs, mine) for mine, theirs in zip(own, other)]
    second = [jnp.where(right, mine, theirs) for mine, theirs in zip(own, other)]
    return first, second


def join_kernel(axis, stage, width, last, *refs):
    count = 1 << width
    blocks = [[refs[i][q] for q in range(7)] for i in range(count)]
    send = refs[-1 - width]
    links = refs[-width:]
    for bit in range(width):
        right = on_right(axis, stage + bit)
        for i in range(count):
            if not i >> bit & 1:
                j = i | 1 << bit
                blocks[i], blocks[j] = ordered(right, blocks[i], blocks[j])
    for bit in range(width):
        pairs = [join(blocks[i], blocks[i + 1]) for i in range(0, len(blocks), 2)]
        blocks = [p[0] for p in pairs]
        ties = [p[1] for p in pairs]
        for upper in range(bit + 1, width):
            right = on_right(axis, stage + upper)
            ties = [
                tuple(jnp.where(right, v, u) for u, v in zip(ties[i], ties[i + 1]))
                for i in range(0, len(ties), 2)
            ]
        for i in range(3):
            links[bit][i] = ties[0][i]
    (whole,) = blocks
    if last:
        for n, value in enumerate(toward(on_right(axis, stage + width), whole)):
            send[n] = value
    else:
        for q in range(7):
            send[q] = whole[q]


def join_stage(own, got, axis, stage, width, last, after):
    lines = own.shape[1]
    return pl.pallas_call(
        functools.partial(join_kernel, axis, stage, width, last),
        in_specs=[IN_VMEM] * (1 + len(got)) + [ANYWHERE] * len(after),
        out_shape=[shape_of(3 if last else 7, lines, LANES)] + [shape_of(3, lines, LANES)] * width,
        compiler_params=params(),
    )(own, *got, *after)


def gather_line(view, axis, widest=1, meanwhile=(), cross=False):
    stages = stages_of(axis)
    links, stage = [], 0
    while stage < stages - 1:
        width = min(widest, stages - 1 - stage)
        got = [swap(view, axis, flip << stage) for flip in range(1, 1 << width)]
        last = stage + width == stages - 1
        view, *ties = join_stage(view, got, axis, stage, width, last, meanwhile)
        links += ties
        stage += width
        meanwhile = ()
    return view, swap(view, axis, 1 << stage | (cross and stage > 0)), links


def top_flux(axis, stages, own, got):
    right = on_right(axis, stages - 1)
    face = own[2] + got[2]
    jump = jnp.where(right, own[1] - got[1], got[1] - own[1])
    return jump * face * inverse(1.0 + face * (own[0] + got[0]))


def block_ends(axis, stages, links):
    shape = links[0].shape[1:] if links else None
    right = on_right(axis, stages - 1)
    zero = jnp.zeros(shape, F32)
    low, high = zero, zero
    unit_low = zero + jnp.where(right, -1.0, 0.0)
    unit_high = zero + jnp.where(right, 0.0, 1.0)
    for stage in range(stages - 2, -1, -1):
        tie = links[stage]
        right = on_right(axis, stage)
        flux = between(tie[0], tie[1], tie[2], low, high)
        unit = between(0.0, tie[1], tie[2], unit_low, unit_high)
        low, high = jnp.where(right, -flux, low), jnp.where(right, high, flux)
        unit_low, unit_high = jnp.where(right, -unit, unit_low), jnp.where(right, unit_high, unit)
    return (low, high), (unit_low, unit_high)


def natural(index, parts):
    span = SUBLANES * parts
    local = index % span
    return index - local + local % SUBLANES * parts + local // SUBLANES


def turn_matrix(shape, from_natural, parts):
    row = lax.broadcasted_iota(jnp.int32, shape, 0)
    column = lax.broadcasted_iota(jnp.int32, shape, 1) % LANES
    hit = natural(row, parts) == column if from_natural else row == natural(column, parts)
    return jnp.where(hit, 1.0, 0.0).astype(jnp.bfloat16)


def turned(matrix, field, rows=None):
    high = field.astype(jnp.bfloat16).astype(F32)
    both = jnp.concatenate([high, field - high], 1)
    if rows:
        both = jnp.concatenate(
            [jnp.broadcast_to(both[n : n + 1, :], (rows, 2 * LANES)) for n in range(field.shape[0])], 0
        )
    both = both.astype(jnp.bfloat16)
    return lax.dot_general(
        matrix, both, (((1,), (1,)), ((), ())), preferred_element_type=F32
    )


def y_factor_kernel(c_ref, after, w_ref, i_ref, p_ref, inner, outer, view, to_y, to_x, unit_low, unit_high, c_s, q_s, r_s):
    chunks, sheets, rows, _ = c_ref.shape
    each = LANES // rows
    pairs = sheets // each
    x_steps = rows // SUBLANES
    steps = LANES // SUBLANES
    to_y[...] = turn_matrix(to_y.shape, True, steps)
    to_x[...] = turn_matrix(to_x.shape, False, x_steps)
    for m in range(pairs):
        for y in range(chunks):
            block = jnp.concatenate(
                [
                    c_ref[y, m * each + i, pl.ds(k, SUBLANES, stride=x_steps), :]
                    for i in range(each)
                    for k in range(x_steps)
                ],
                0,
            )
            c_s[m, part_of(y), :] = block.T

    members = [(y, m) for y in range(chunks) for m in range(pairs)]
    lines = len(members)

    def cond(k):
        return jnp.stack([c_s[m, pl.ds(y * LANES + k, SUBLANES, stride=steps), :] for y, m in members], 0)

    def keep(k, w, inv, p):
        w_ref[k] = w
        i_ref[k] = inv
        p_ref[k] = p

    block = factor(cond, steps, keep)
    for n, q in enumerate(COEFS):
        for i in range(lines):
            q_s[n, i * SUBLANES : (i + 1) * SUBLANES, :] = block[q][i]
    segments = [
        {q: q_s[n, pl.ds(s, lines, stride=SUBLANES), :] for n, q in enumerate(COEFS)}
        for s in range(SUBLANES)
    ]
    whole, levels = tree(segments, join_coefs)
    for (offset, _), level in zip(node_offsets(SUBLANES), levels):
        for n, values in enumerate(level):
            for i in range(3):
                inner[offset + n, i] = values[i]
    for n, q in enumerate(COEFS):
        r_s[n] = whole[q]
    parts = [
        {q: r_s[n, y * pairs : (y + 1) * pairs, :] for n, q in enumerate(COEFS)} for y in range(chunks)
    ]
    whole, levels = tree(parts, join_coefs)
    for (offset, _), level in zip(node_offsets(chunks), levels):
        for n, values in enumerate(level):
            for i in range(3):
                outer[offset + n, i] = values[i]
    for n, q in enumerate(COEFS):
        view[n] = whole[q]

    one = jnp.ones((pairs, LANES), F32)
    for n, (low, high, field) in enumerate(((one, 0.0 * one, unit_low), (0.0 * one, one, unit_high))):
        for y, pair in enumerate(tree_ends(chunks, outer, nothing, low, high)):
            for i in range(2):
                r_s[2 * n + i, y * pairs : (y + 1) * pairs, :] = pair[i]
        for s, pair in enumerate(tree_ends(SUBLANES, inner, nothing, r_s[2 * n], r_s[2 * n + 1])):
            for i in range(2):
                q_s[2 * n + i, pl.ds(s, lines, stride=SUBLANES), :] = pair[i]
        low, value = (
            jnp.stack(
                [q_s[2 * n + i, j * SUBLANES : (j + 1) * SUBLANES, :] for j in range(lines)], 0
            )
            for i in range(2)
        )
        for k in range(steps - 1, -1, -1):
            value = w_ref[k] * value + p_ref[k] * low
            for j, (y, m) in enumerate(members):
                field[y, k * SUBLANES : (k + 1) * SUBLANES, part_of(m)] = value[j]


def y_factor(c, after):
    chunks, sheets, rows, _ = c.shape
    pairs = sheets * rows // LANES
    lines = chunks * pairs
    stored = shape_of(LANES // SUBLANES, lines, SUBLANES, LANES)
    matrix = jax.ShapeDtypeStruct((LANES, 2 * LANES), jnp.bfloat16)
    return pl.pallas_call(
        y_factor_kernel,
        in_specs=[IN_VMEM, ANYWHERE],
        out_shape=[
            stored,
            stored,
            stored,
            shape_of(SUBLANES - 1, 3, lines, LANES),
            shape_of(chunks - 1, 3, pairs, LANES),
            shape_of(len(COEFS), pairs, LANES),
            matrix,
            matrix,
            shape_of(chunks, LANES, pairs * LANES),
            shape_of(chunks, LANES, pairs * LANES),
        ],
        scratch_shapes=[
            pltpu.VMEM((pairs, chunks * LANES, LANES), F32),
            pltpu.VMEM((len(COEFS), lines * SUBLANES, LANES), F32),
            pltpu.VMEM((len(COEFS), lines, LANES), F32),
        ],
        compiler_params=params(),
        cost_estimate=pl.CostEstimate(flops=20 * c.size, bytes_accessed=16 * c.size, transcendentals=0),
    )(c, after)


def z_factor_kernel(c_ref, after, w_ref, i_ref):
    sheets = c_ref.shape[1]
    ground = 1.0
    for z in range(sheets - 1):
        face = c_ref[:, z] + c_ref[:, z + 1]
        inv = inverse(ground + face)
        w = face * inv
        i_ref[z] = inv
        w_ref[z] = w
        ground = 1.0 + w * ground
    i_ref[sheets - 1] = inverse(ground)


def z_factor(c, after):
    chunks, sheets, rows, _ = c.shape
    return pl.pallas_call(
        z_factor_kernel,
        in_specs=[IN_VMEM, ANYWHERE],
        out_shape=[
            shape_of(sheets - 1, chunks, rows, LANES),
            shape_of(sheets, chunks, rows, LANES),
        ],
        compiler_params=params(),
        cost_estimate=pl.CostEstimate(flops=10 * c.size, bytes_accessed=12 * c.size, transcendentals=0),
    )(c, after)


def join_tree(items, links, own):
    for offset, count in node_offsets(len(items)):
        joined = []
        for n in range(count):
            tie = tuple(links[offset + n, i] for i in range(3))
            both, flux = join_targets(items[2 * n], items[2 * n + 1], tie)
            own[offset + n] = flux
            joined.append(both)
        items = joined
    return items[0]


def tree_ends(leaves, links, own, low, high):
    levels = [
        [(own(offset + n), links[offset + n, 1], links[offset + n, 2]) for n in range(count)]
        for offset, count in node_offsets(leaves)
    ]
    return descend(levels, low, high)


def nothing(node):
    return 0.0


def y_prepare_kernel(stages, *refs):
    ties = refs[: stages - 1]
    xw, xh, xm, xp, x_links, x_own, t_ref, to_y, y_low, y_high = refs[stages - 1 : stages + 9]
    base, response, to_first, to_last, fixed, f_s, g_s = refs[stages + 9 :]
    x_steps, lines = xw.shape[:2]
    chunks = base.shape[0]
    sheets = lines // chunks
    rows = x_steps * SUBLANES

    ends, units = block_ends("gx", stages, ties)
    for n, (own, (low, high)) in enumerate(((lambda i: x_own[i], ends), (nothing, units))):
        for s, pair in enumerate(tree_ends(SUBLANES, x_links, own, low, high)):
            for i in range(2):
                f_s[n, i, pl.ds(s, lines, stride=SUBLANES), :] = pair[i]
    first = 0
    for n, members in enumerate(line_groups(chunks, sheets)):
        at = slice(first, first + len(members))
        h_ref_of, h_at = (xh, at) if n == 0 else (xm, slice(first - 2 * sheets, at.stop - 2 * sheets))
        (low, value), (unit_low, unit) = (
            [
                jnp.stack(
                    [f_s[q, i, j * SUBLANES : (j + 1) * SUBLANES, :] for j in range(at.start, at.stop)], 0
                )
                for i in range(2)
            ]
            for q in range(2)
        )
        for k in range(x_steps - 1, -1, -1):
            w, p = xw[k, at], xp[k, at]
            value = w * value + (h_ref_of[k, h_at] + p * low)
            unit = w * unit + p * unit_low
            field = value - t_ref[k, at]
            for j, (y, z) in enumerate(members):
                place = z * rows + k * SUBLANES
                g_s[0, y, place : place + SUBLANES, :] = field[j]
                g_s[1, y, place : place + SUBLANES, :] = unit[j]
        first = at.stop

    totals = [None, None]
    for y in range(chunks):
        field = turned(to_y[...], g_s[0, y])
        answer = turned(to_y[...], g_s[1, y])
        base[y] = field
        response[y] = answer
        for i, (unit, weight) in enumerate(((y_low, to_first), (y_high, to_last))):
            weight[y] = unit[y] * answer
            part = unit[y] * field
            totals[i] = part if y == 0 else totals[i] + part
    for i in range(2):
        put_sums(fixed.at[i], totals[i])


def put_sums(out, field):
    total = jnp.sum(field, 0, keepdims=True)
    for m in range(out.shape[0]):
        out[m : m + 1, :] = total[:, part_of(m)]


def y_prepare(ties, xw, xh, xm, xp, x_links, x_own, t, to_y, unit_low, unit_high):
    chunks = unit_low.shape[0]
    x_steps, lines = xw.shape[:2]
    width = lines // chunks * x_steps * SUBLANES
    field = shape_of(chunks, LANES, width)
    return pl.pallas_call(
        functools.partial(y_prepare_kernel, len(ties) + 1),
        out_shape=[field] * 4 + [shape_of(2, width // LANES, LANES)],
        scratch_shapes=[
            pltpu.VMEM((2, 2, lines * SUBLANES, LANES), F32),
            pltpu.VMEM((2, chunks, width, LANES), F32),
        ],
        compiler_params=params(),
        cost_estimate=pl.CostEstimate(flops=8 * t.size, bytes_accessed=16 * t.size, transcendentals=0),
    )(*ties, xw, xh, xm, xp, x_links, x_own, t, to_y, unit_low, unit_high)


def y_target_kernel(stages, own, got, to_first, to_last, fixed, view, to_y, spread, send, r_s):
    chunks, _, width = to_first.shape
    sheets = own.shape[1] // chunks
    rows = width // sheets

    flux = top_flux("gx", stages, own, got)
    line_of = {member: n for n, member in enumerate(sum(line_groups(chunks, sheets), []))}
    totals = [None, None]
    for y in range(chunks):
        own_flux = jnp.concatenate([flux[line_of[y, z] : line_of[y, z] + 1, :] for z in range(sheets)], 0)
        wide = turned(to_y[...], own_flux, rows)
        spread[y] = wide
        for i, weight in enumerate((to_first, to_last)):
            part = weight[y] * wide
            totals[i] = part if y == 0 else totals[i] + part
    for n, q in enumerate(COEFS):
        send[q] = view[n]
    for i, q in enumerate((FIRST, LAST)):
        put_sums(r_s.at[i], totals[i])
        send[q] = fixed[i] + r_s[i]


def y_target(own, got, to_first, to_last, fixed, view, to_y):
    pairs = view.shape[1]
    return pl.pallas_call(
        functools.partial(y_target_kernel, stages_of("gx")),
        out_shape=[shape_of(*to_first.shape), shape_of(7, pairs, LANES)],
        scratch_shapes=[pltpu.VMEM((2, pairs, LANES), F32)],
        compiler_params=params(),
    )(own, got, to_first, to_last, fixed, view, to_y)


def y_eliminate_kernel(base, response, spread, yw, yi, yp, inner, outer, after, *refs):
    h_ref, inner_own, outer_own, q_s, r_s = refs
    chunks, _, width = base.shape
    pairs = width // LANES
    steps = yw.shape[0]
    members = [(y, m) for y in range(chunks) for m in range(pairs)]

    def target(k):
        at = slice(k * SUBLANES, (k + 1) * SUBLANES)
        return jnp.stack(
            [
                base[y, at, part_of(m)] + response[y, at, part_of(m)] * spread[y, at, part_of(m)]
                for y, m in members
            ],
            0,
        )

    def keep(k, h):
        h_ref[k] = h

    ends = eliminate(target, steps, lambda k: yw[k], lambda k: yi[k], lambda k: yp[k], keep)
    for q in range(2):
        for i in range(len(members)):
            q_s[q, i * SUBLANES : (i + 1) * SUBLANES, :] = ends[q][i]
    items = [
        tuple(q_s[q, pl.ds(s, len(members), stride=SUBLANES), :] for q in range(2))
        for s in range(SUBLANES)
    ]
    r_s[0], r_s[1] = join_tree(items, inner, inner_own)
    items = [tuple(r_s[q, y * pairs : (y + 1) * pairs, :] for q in range(2)) for y in range(chunks)]
    join_tree(items, outer, outer_own)


def y_eliminate(base, response, spread, yw, yi, yp, inner, outer, after):
    y_lines = yw.shape[1]
    pairs = outer.shape[2]
    chunks = y_lines // pairs
    return pl.pallas_call(
        y_eliminate_kernel,
        in_specs=[IN_VMEM] * 8 + [ANYWHERE],
        out_shape=[
            shape_of(*yw.shape),
            shape_of(SUBLANES - 1, y_lines, LANES),
            shape_of(chunks - 1, pairs, LANES),
        ],
        scratch_shapes=[
            pltpu.VMEM((2, y_lines * SUBLANES, LANES), F32),
            pltpu.VMEM((2, y_lines, LANES), F32),
        ],
        compiler_params=params(),
        cost_estimate=pl.CostEstimate(flops=8 * base.size, bytes_accessed=16 * base.size, transcendentals=0),
    )(base, response, spread, yw, yi, yp, inner, outer, after)


def z_solve(zw, zi, field, at, keep):
    sheets = zi.shape[0]
    rhs, kept = None, []
    for z in range(sheets):
        rhs = field(z) if z == 0 else field(z) + zw[(z - 1, *at)] * rhs
        kept.append(rhs * zi[(z, *at)])
    value = kept[-1]
    keep(sheets - 1, value)
    for z in range(sheets - 2, -1, -1):
        value = zw[(z, *at)] * value + kept[z]
        keep(z, value)


def finish_prepare_kernel(stages, *refs):
    ties = refs[: stages - 1]
    yw, yh, yp, inner, inner_own, outer, outer_own, zw, zi, t_ref, to_x = refs[stages - 1 : stages + 10]
    base, response, r_s, e_s, u_s = refs[stages + 10 :]
    chunks, sheets, rows, _ = base.shape
    each = LANES // rows
    pairs = sheets // each
    steps = yw.shape[0]
    lines = chunks * pairs

    ends, units = block_ends("gy", stages, ties)
    both = (
        (lambda i: outer_own[i], lambda i: inner_own[i], ends),
        (nothing, nothing, units),
    )
    for n, (upper, lower, (low, high)) in enumerate(both):
        for y, pair in enumerate(tree_ends(chunks, outer, upper, low, high)):
            for i in range(2):
                r_s[n, i, y * pairs : (y + 1) * pairs, :] = pair[i]
        for s, pair in enumerate(tree_ends(SUBLANES, inner, lower, r_s[n, 0], r_s[n, 1])):
            for i in range(2):
                e_s[n, i, pl.ds(s, lines, stride=SUBLANES), :] = pair[i]
    (low, value), (unit_low, unit) = (
        [
            jnp.stack([e_s[q, i, n * SUBLANES : (n + 1) * SUBLANES, :] for n in range(lines)], 0)
            for i in range(2)
        ]
        for q in range(2)
    )
    for k in range(steps - 1, -1, -1):
        w, p = yw[k], yp[k]
        value = w * value + (yh[k] + p * low)
        unit = w * unit + p * unit_low
        for y in range(chunks):
            for m in range(pairs):
                place = pl.ds(y * LANES + k, SUBLANES, stride=steps)
                u_s[0, m, place, :] = value[y * pairs + m]
                u_s[1, m, place, :] = unit[y * pairs + m]

    for y in range(chunks):
        part = part_of(y)
        fields = [turned(to_x[...], u_s[0, m, part, :]) for m in range(pairs)]

        def field(z):
            at = z % each * rows
            return fields[z // each][at : at + rows, :]

        def keep(z, value):
            base[y, z] = t_ref[z, :, part] + value

        z_solve(zw, zi, field, (y,), keep)
        for m in range(pairs):
            units = turned(to_x[...], u_s[1, m, part, :])
            for i in range(each):
                response[y, m * each + i] = units[i * rows : (i + 1) * rows, :]


def finish_prepare(ties, yw, yh, yp, inner, inner_own, outer, outer_own, zw, zi, t, to_x):
    sheets, rows, columns = t.shape
    chunks = columns // LANES
    pairs = sheets * rows // LANES
    lines = chunks * pairs
    field = shape_of(chunks, sheets, rows, LANES)
    return pl.pallas_call(
        functools.partial(finish_prepare_kernel, len(ties) + 1),
        out_shape=[field, field],
        scratch_shapes=[
            pltpu.VMEM((2, 2, lines, LANES), F32),
            pltpu.VMEM((2, 2, lines * SUBLANES, LANES), F32),
            pltpu.VMEM((2, pairs, columns, LANES), F32),
        ],
        compiler_params=params(),
        cost_estimate=pl.CostEstimate(flops=12 * t.size, bytes_accessed=20 * t.size, transcendentals=0),
    )(*ties, yw, yh, yp, inner, inner_own, outer, outer_own, zw, zi, t, to_x)


def finish_kernel(stages, own, got, base, response, zw, zi, to_x, out, o_s, sems):
    chunks, sheets, rows, _ = base.shape
    each = LANES // rows
    pairs = sheets // each
    flux = top_flux("gy", stages, own, got)
    spread = [
        turned(to_x[...], flux[m : m + 1, :], LANES) for m in range(pairs)
    ]
    started = []
    block = rows // OUT_COPIES
    for n in range(OUT_COPIES):
        strip = slice(n * block, (n + 1) * block)
        for y in range(chunks):

            def field(z):
                at = z % each * rows + strip.start
                return response[y, z, strip, :] * spread[z // each][at : at + block, :]

            def keep(z, value):
                o_s[z, strip, part_of(y)] = base[y, z, strip, :] + value

            z_solve(zw, zi, field, (y, strip), keep)
        at = pl.ds(strip.start, block)
        copy = pltpu.make_async_copy(o_s.at[:, at, :], out.at[:, at, :], sems.at[n])
        copy.start()
        started.append(copy)
    for copy in started:
        copy.wait()


def finish(own, got, base, response, zw, zi, to_x):
    chunks, sheets, rows, _ = base.shape
    shape = (sheets, rows, chunks * LANES)
    return pl.pallas_call(
        functools.partial(finish_kernel, stages_of("gy")),
        out_shape=shape_of(*shape),
        out_specs=ANYWHERE,
        scratch_shapes=[pltpu.VMEM(shape, F32), pltpu.SemaphoreType.DMA((OUT_COPIES,))],
        compiler_params=params(),
    )(own, got, base, response, zw, zi, to_x)


def per_device(temperature, base, locations, energy):
    columns = temperature.shape[2]
    gy = lax.axis_size("gy")
    t, b, loc, heat, packed = load(temperature, base, locations[None], energy[None])
    near = swap(packed, "gy", 1)
    far = lax.ppermute(packed, "gy", [(i, ((i + 1) % gy ^ 1) - 1 if i else gy - 1) for i in range(gy)])
    c, total, xw, xi, xp, x_links, x_view, xm, ends, t_steps, swapped = x_factor(loc, heat, t, b, columns * gy, packed)
    xh, x_own, view = x_target(swapped, total, near, far, xw, xi, xp, x_links, x_view, ends)
    yw, yi, yp, inner, outer, y_view, to_y, to_x, unit_low, unit_high = y_factor(c, x_view)
    zw, zi = z_factor(c, view)
    own, got, ties = gather_line(view, "gx", 2, (y_view, zw))
    base, response, to_first, to_last, fixed = y_prepare(
        ties, xw, xh, xm, xp, x_links, x_own, t_steps, to_y, unit_low, unit_high
    )
    spread, view = y_target(own, got, to_first, to_last, fixed, y_view, to_y)
    yh, inner_own, outer_own = y_eliminate(base, response, spread, yw, yi, yp, inner, outer, view)
    own, got, ties = gather_line(view, "gy", meanwhile=(yh,), cross=True)
    base, response = finish_prepare(
        ties, yw, yh, yp, inner, inner_own, outer, outer_own, zw, zi, t, to_x
    )
    return finish(own, got, base, response, zw, zi, to_x)


def solution(mesh):
    in_specs = (P(None, "gx", "gy"), P(None, "gx", "gy"), P(), P())
    out_specs = P(None, "gx", "gy")
    return jax.shard_map(
        per_device, mesh=mesh, in_specs=in_specs, out_specs=out_specs, check_vma=False
    )
```

```python
import functools

import jax
import jax.numpy as jnp
from jax import lax
from jax.experimental import pallas as pl
from jax.experimental.pallas import tpu as pltpu
from jax.sharding import PartitionSpec as P

RATE = 2000.0
THERMAL_GROWTH = 0.8
LANES = 128
SUBLANES = 8
F32 = jnp.float32
MIB = 1024 * 1024
OUT_COPIES = 4
ANYWHERE = pl.BlockSpec(memory_space=pl.ANY)
IN_HBM = pl.BlockSpec(memory_space=pltpu.HBM)
IN_VMEM = pl.BlockSpec(memory_space=pltpu.VMEM)

R00, R0L, RLL, FIRST, LAST, C0, CL = range(7)
COEFS = (R00, R0L, RLL, C0, CL)


def params(limit=40):
    return pltpu.CompilerParams(vmem_limit_bytes=limit * MIB)


def shape_of(*sizes):
    return jax.ShapeDtypeStruct(sizes, F32)


def half_conduct(base, temperature):
    return base * (0.5 * RATE + (0.5 * RATE * THERMAL_GROWTH) * temperature)


def inverse(x):
    guess = pl.reciprocal(x, approx=True)
    return guess * (2.0 - x * guess)


def join_coefs(a, b):
    face = a[CL] + b[C0]
    inv = face * inverse(1.0 + face * (a[RLL] + b[R00]))
    left = a[R0L] * inv
    right = b[R0L] * inv
    joined = {
        R00: a[R00] - left * a[R0L],
        R0L: left * b[R0L],
        RLL: b[RLL] - right * b[R0L],
        C0: a[C0],
        CL: b[CL],
    }
    return joined, (inv, right, left)


def join_targets(a, b, links):
    inv, right, left = links
    jump = b[0] - a[1]
    return (a[0] + left * jump, b[1] - right * jump), jump * inv


def between(own, right, left, low, high):
    return own + right * high - left * low


def tree(items, join):
    levels = []
    while len(items) > 1:
        pairs = [join(items[i], items[i + 1]) for i in range(0, len(items), 2)]
        items = [p[0] for p in pairs]
        levels.append([p[1] for p in pairs])
    return items[0], levels


def descend(levels, low, high):
    ends = [(low, high)]
    for level in reversed(levels):
        below = []
        for (lo, hi), (own, right, left) in zip(ends, level):
            flux = between(own, right, left, lo, hi)
            below += [(lo, flux), (-flux, hi)]
        ends = below
    return ends


def node_offsets(leaves):
    offsets, at, count = [], 0, leaves // 2
    while count:
        offsets.append((at, count))
        at += count
        count //= 2
    return offsets


def factor(cond, steps, keep):
    here = cond(0)
    c_first = here
    one = jnp.ones_like(here)
    ground, path, first_first = one, one, None
    for k in range(steps - 1):
        following = cond(k + 1)
        face = here + following
        inv = inverse(ground + face)
        w = face * inv
        p = path * inv
        keep(k, w, inv, p)
        step = path * p
        first_first = step if first_first is None else first_first + step
        path = path * w
        ground = 1.0 + w * ground
        here = following
    inv = inverse(ground)
    p = path * inv
    keep(steps - 1, inv, inv, p)
    return {R00: first_first + path * p, R0L: p, RLL: inv, C0: c_first, CL: here}


def eliminate(target, steps, w, inv, p, keep):
    rhs = target(0)
    first = None
    for k in range(steps):
        h = rhs * inv(k)
        keep(k, h)
        step = rhs * p(k)
        first = step if first is None else first + step
        if k < steps - 1:
            rhs = target(k + 1) + w(k) * rhs
    return first, h


def is_odd(axis):
    return lax.axis_index(axis) % 2 == 1


def fold(cells, used):
    steps = cells.shape[0] // SUBLANES
    total = cells[pl.ds(0, SUBLANES, stride=steps), :]
    lane = lax.broadcasted_iota(jnp.int32, total.shape, 1)
    for k in range(1, steps):
        part = pltpu.roll(cells[pl.ds(k, SUBLANES, stride=steps), :], k * used, 1)
        total = jnp.where(lane // used == k, part, total)
    return total


def load_kernel(t_hbm, b_hbm, loc_hbm, energy_hbm, t_out, b_out, loc, energy, packed, cells, sems):
    sheets, rows, columns = t_hbm.shape
    copies = []
    for n, start in enumerate((0, columns - LANES)):
        part = pl.ds(start, LANES)
        for i, (src, dst) in enumerate(((t_hbm, t_out), (b_hbm, b_out))):
            copies.append(pltpu.make_async_copy(src.at[:, :, part], dst.at[n], sems.at[i, n]))
    copies.append(pltpu.make_async_copy(loc_hbm, loc, sems.at[2, 0]))
    copies.append(pltpu.make_async_copy(energy_hbm, energy, sems.at[2, 1]))
    for copy in copies:
        copy.start()
    lane = lax.broadcasted_iota(jnp.int32, (rows, LANES), 1)
    edge_t = jnp.zeros((rows, LANES), F32)
    edge_c = edge_t
    for side, source in enumerate((0, LANES - 1)):
        for copy in copies[2 * side : 2 * side + 2]:
            copy.wait()
        for z in range(sheets):
            t = t_out[side, z]
            c = half_conduct(b_out[side, z], t)
            place = lane == sheets * side + z
            edge_t = jnp.where(place, t[:, source : source + 1], edge_t)
            edge_c = jnp.where(place, c[:, source : source + 1], edge_c)
    cells[0], cells[1] = edge_t, edge_c
    for i in range(2):
        packed[i * SUBLANES : (i + 1) * SUBLANES, :] = fold(cells.at[i], 2 * sheets)
    for copy in copies[4:]:
        copy.wait()


def load(temperature, base, locations, energy):
    sheets, rows, columns = temperature.shape
    assert rows // SUBLANES * 2 * sheets <= LANES and columns > 2 * LANES
    operands = (temperature, base, locations, energy)
    return pl.pallas_call(
        load_kernel,
        in_specs=[IN_HBM] * 4,
        out_shape=[pltpu.VMEM((2, sheets, rows, LANES), F32)] * 2
        + [pltpu.VMEM(v.shape, v.dtype) for v in operands[2:]]
        + [pltpu.VMEM((2 * SUBLANES, LANES), F32)],
        scratch_shapes=[pltpu.VMEM((2, rows, LANES), F32), pltpu.SemaphoreType.DMA((3, 2))],
        compiler_params=params(),
    )(*[pltpu.with_memory_space_constraint(v, pltpu.HBM) for v in operands])


def source_plane(loc, energy, rows, columns, plate):
    place = loc[...]
    count = place.shape[1]
    local_x = place // plate - lax.axis_index("gx") * rows
    local_y = place % plate - lax.axis_index("gy") * columns
    in_x = lax.broadcasted_iota(jnp.int32, (rows, count), 0) == local_x
    in_y = lax.broadcasted_iota(jnp.int32, (columns, count), 0) == local_y
    by_y = jnp.where(in_y, 1.0, 0.0).astype(jnp.bfloat16)
    left = energy[...]
    plane = None
    for _ in range(3):
        part = left.astype(jnp.bfloat16).astype(F32)
        left = left - part
        term = lax.dot_general(
            jnp.where(in_x, part, 0.0).astype(jnp.bfloat16),
            by_y,
            (((1,), (1,)), ((), ())),
            preferred_element_type=F32,
        )
        plane = term if plane is None else plane + term
    return plane


def part_of(y):
    return slice(y * LANES, (y + 1) * LANES)


def line_groups(chunks, sheets):
    order = [0, chunks - 1] + list(range(1, chunks - 1))
    return [[(y, z) for y in order[i : i + 2] for z in range(sheets)] for i in range(0, chunks, 2)]


def x_eliminate(cells, members, first_line, w_ref, i_ref, p_ref, h_ref, h_line, q_s):
    steps = w_ref.shape[0]
    at = slice(first_line, first_line + len(members))
    kept_at = slice(h_line, h_line + len(members))

    def target(k):
        return jnp.stack([cells(y, z, k) for y, z in members], 0)

    def keep(k, h):
        h_ref[k, kept_at] = h

    ends = eliminate(
        target, steps, lambda k: w_ref[k, at], lambda k: i_ref[k, at], lambda k: p_ref[k, at], keep
    )
    for q in range(2):
        for i in range(len(members)):
            first = (first_line + i) * SUBLANES
            q_s[q, first : first + SUBLANES, :] = ends[q][i]


def x_factor_kernel(plate, loc, energy, t_edge, b_edge, own_cells, t_hbm, b_hbm, *refs):
    c_ref, total_ref, w_ref, i_ref, p_ref, links, view, h_ref, ends_ref, t_out, swapped, t_s, q_s, t_m, b_m, sems = refs
    chunks, sheets, rows, _ = c_ref.shape
    lines = chunks * sheets
    steps = rows // SUBLANES
    middle = pl.ds(LANES, (chunks - 2) * LANES)
    copies = [
        pltpu.make_async_copy(src.at[:, :, middle], dst, sems.at[i])
        for i, (src, dst) in enumerate(((t_hbm, t_m), (b_hbm, b_m)))
    ]
    for copy in copies:
        copy.start()
    plane = source_plane(loc, energy, rows, chunks * LANES, plate)
    mine = own_cells[...]
    in_low = lax.broadcasted_iota(jnp.int32, mine.shape, 1) % (2 * sheets) < sheets
    swapped[...] = jnp.where(
        in_low, pltpu.roll(mine, LANES - sheets, 1), pltpu.roll(mine, sheets, 1)
    )

    def factor_group(members, at):
        def cond(k):
            return jnp.stack([c_ref[y, z, pl.ds(k, SUBLANES, stride=steps), :] for y, z in members], 0)

        def keep(k, w, inv, p):
            w_ref[k, at : at + len(members)] = w
            i_ref[k, at : at + len(members)] = inv
            p_ref[k, at : at + len(members)] = p

        block = factor(cond, steps, keep)
        for i, q in enumerate(COEFS):
            for j in range(len(members)):
                first = (at + j) * SUBLANES
                q_s[i, first : first + SUBLANES, :] = block[q][j]

    groups = line_groups(chunks, sheets)
    for y, side in ((0, 0), (chunks - 1, 1)):
        for z in range(sheets):
            t_s[y, z] = t_edge[side, z]
            c_ref[y, z] = half_conduct(b_edge[side, z], t_edge[side, z])
    factor_group(groups[0], 0)
    for copy in copies:
        copy.wait()

    lane = lax.broadcasted_iota(jnp.int32, (SUBLANES, LANES), 1)
    is_first, is_last = lane == 0, lane == LANES - 1
    for r in range(steps):
        at = slice(r * SUBLANES, (r + 1) * SUBLANES)
        before_t, before_c = None, None
        for z in range(sheets):
            ts, cs = [], []
            for y in range(chunks):
                if y in (0, chunks - 1):
                    ts.append(t_s[y, z, at, :])
                    cs.append(c_ref[y, z, at, :])
                else:
                    ts.append(t_m[z, at, part_of(y - 1)])
                    cs.append(half_conduct(b_m[z, at, part_of(y - 1)], ts[y]))
                    t_s[y, z, at, :] = ts[y]
                    c_ref[y, z, at, :] = cs[y]
            t_turned = [pltpu.roll(v, LANES - 1, 1) for v in ts]
            c_turned = [pltpu.roll(v, LANES - 1, 1) for v in cs]
            flux = []
            for y in range(chunks):
                if y < chunks - 1:
                    t_next = jnp.where(is_last, t_turned[y + 1], t_turned[y])
                    c_next = jnp.where(is_last, c_turned[y + 1], c_turned[y])
                    flux.append((cs[y] + c_next) * (t_next - ts[y]))
                else:
                    inside = (cs[y] + c_turned[y]) * (t_turned[y] - ts[y])
                    flux.append(jnp.where(is_last, 0.0, inside))
            turned = [pltpu.roll(v, 1, 1) for v in flux]
            for y in range(chunks):
                from_low = jnp.where(is_first, turned[y - 1] if y else 0.0, turned[y])
                total = ts[y] + (flux[y] - from_low)
                if z == 0:
                    total = total + plane[at, part_of(y)]
                else:
                    across = (before_c[y] + cs[y]) * (ts[y] - before_t[y])
                    total = total - across
                    total_ref[y, z - 1, at, :] += across
                total_ref[y, z, at, :] = total
            before_t, before_c = ts, cs

    at = 0
    for n, members in enumerate(groups):
        if n > 0:
            factor_group(members, at)
            x_eliminate(
                lambda y, z, k: total_ref[y, z, pl.ds(k, SUBLANES, stride=steps), :],
                members, at, w_ref, i_ref, p_ref, h_ref, at - 2 * sheets, ends_ref,
            )
        for k in range(steps):
            for i, (y, z) in enumerate(members):
                t_out[k, at + i] = t_s[y, z, pl.ds(k, SUBLANES, stride=steps), :]
        at += len(members)

    segments = [
        {q: q_s[n, pl.ds(s, lines, stride=SUBLANES), :] for n, q in enumerate(COEFS)}
        for s in range(SUBLANES)
    ]
    whole, levels = tree(segments, join_coefs)
    for (offset, _), level in zip(node_offsets(SUBLANES), levels):
        for n, values in enumerate(level):
            for i in range(3):
                links[offset + n, i] = values[i]
    for n, q in enumerate(COEFS):
        view[n] = whole[q]


def x_factor(loc, energy, t_edge, b_edge, temperature, base, plate, own_cells):
    sheets, rows, columns = temperature.shape
    chunks = columns // LANES
    lines = chunks * sheets
    steps = rows // SUBLANES
    field = shape_of(chunks, sheets, rows, LANES)
    stored = shape_of(steps, lines, SUBLANES, LANES)
    return pl.pallas_call(
        functools.partial(x_factor_kernel, plate),
        in_specs=[IN_VMEM] * 5 + [IN_HBM] * 2,
        out_shape=[
            field,
            field,
            stored,
            stored,
            stored,
            shape_of(SUBLANES - 1, 3, lines, LANES),
            shape_of(len(COEFS), lines, LANES),
            shape_of(steps, max(1, lines - 2 * sheets), SUBLANES, LANES),
            shape_of(2, lines * SUBLANES, LANES),
            stored,
            shape_of(*own_cells.shape),
            field,
        ],
        scratch_shapes=[
            pltpu.VMEM((len(COEFS), lines * SUBLANES, LANES), F32),
            pltpu.VMEM((sheets, rows, columns - 2 * LANES), F32),
            pltpu.VMEM((sheets, rows, columns - 2 * LANES), F32),
            pltpu.SemaphoreType.DMA((2,)),
        ],
        compiler_params=params(),
        cost_estimate=pl.CostEstimate(
            flops=40 * temperature.size, bytes_accessed=28 * temperature.size, transcendentals=0
        ),
    )(
        loc, energy, t_edge, b_edge, own_cells,
        *[pltpu.with_memory_space_constraint(v, pltpu.HBM) for v in (temperature, base)],
    )


def x_target_kernel(own_cells, total_ref, near, far, *refs):
    w_ref, i_ref, p_ref, links, view, ends_ref, h_ref, own, send, q_s = refs
    chunks, sheets, rows, _ = total_ref.shape
    lines = chunks * sheets
    steps = rows // SUBLANES

    place = lax.axis_index("gy")
    inner = (place > 0) & (place < lax.axis_size("gy") - 1)
    lane = lax.broadcasted_iota(jnp.int32, (SUBLANES, LANES), 1)
    side = 2 * sheets
    is_near = (lane % side >= sheets).astype(jnp.int32) == place % 2
    t, c = (
        jnp.where(is_near, near[at, :], jnp.where(inner, far[at, :], 0.0))
        for at in (slice(0, SUBLANES), slice(SUBLANES, 2 * SUBLANES))
    )
    face = jnp.where(c > 0.0, own_cells[SUBLANES:, :] + c, 0.0)
    flux = face * (t - own_cells[:SUBLANES, :])

    def cells(y, z, k):
        at = k * side + (sheets + z if y == 0 else z)
        edge = 0 if y == 0 else LANES - 1
        inflow = jnp.where(lane == edge, flux[:, at : at + 1], 0.0)
        return total_ref[y, z, pl.ds(k, SUBLANES, stride=steps), :] + inflow

    members = line_groups(chunks, sheets)[0]
    x_eliminate(cells, members, 0, w_ref, i_ref, p_ref, h_ref, 0, q_s)
    split = len(members)
    items = [
        tuple(
            jnp.concatenate(
                [
                    q_s[q, pl.ds(s, split, stride=SUBLANES), :],
                    ends_ref[q, pl.ds(split * SUBLANES + s, lines - split, stride=SUBLANES), :],
                ],
                0,
            )
            for q in range(2)
        )
        for s in range(SUBLANES)
    ]
    for offset, count in node_offsets(SUBLANES):
        joined = []
        for n in range(count):
            ties = tuple(links[offset + n, i] for i in range(3))
            both, flux = join_targets(items[2 * n], items[2 * n + 1], ties)
            own[offset + n] = flux
            joined.append(both)
        items = joined
    for n, q in enumerate(COEFS):
        send[q] = view[n]
    send[FIRST], send[LAST] = items[0]


def x_target(own_cells, total, near, far, w, inv, p, links, view, ends):
    chunks, sheets, rows, _ = total.shape
    lines = chunks * sheets
    steps = rows // SUBLANES
    return pl.pallas_call(
        x_target_kernel,
        out_shape=[
            shape_of(steps, 2 * sheets, SUBLANES, LANES),
            shape_of(SUBLANES - 1, lines, LANES),
            shape_of(7, lines, LANES),
        ],
        scratch_shapes=[
            pltpu.VMEM((2, 2 * sheets * SUBLANES, LANES), F32),
        ],
        compiler_params=params(),
    )(own_cells, total, near, far, w, inv, p, links, view, ends)


def stages_of(axis):
    return lax.axis_size(axis).bit_length() - 1


def swap(value, axis, flip):
    count = lax.axis_size(axis)
    return lax.ppermute(value, axis, [(i, i ^ flip) for i in range(count)])


def on_right(axis, stage):
    return (lax.axis_index(axis) >> stage) % 2 == 1


def toward(right, block):
    return (
        jnp.where(right, block[R00], block[RLL]),
        jnp.where(right, block[FIRST], block[LAST]),
        jnp.where(right, block[C0], block[CL]),
    )


def join(a, b):
    joined, ties = join_coefs(a, b)
    (joined[FIRST], joined[LAST]), flux = join_targets((a[FIRST], a[LAST]), (b[FIRST], b[LAST]), ties)
    return joined, (flux, ties[1], ties[2])


def ordered(right, own, other):
    first = [jnp.where(right, theirs, mine) for mine, theirs in zip(own, other)]
    second = [jnp.where(right, mine, theirs) for mine, theirs in zip(own, other)]
    return first, second


def join_kernel(axis, stage, width, last, *refs):
    count = 1 << width
    blocks = [[refs[i][q] for q in range(7)] for i in range(count)]
    send = refs[-1 - width]
    links = refs[-width:]
    for bit in range(width):
        right = on_right(axis, stage + bit)
        for i in range(count):
            if not i >> bit & 1:
                j = i | 1 << bit
                blocks[i], blocks[j] = ordered(right, blocks[i], blocks[j])
    for bit in range(width):
        pairs = [join(blocks[i], blocks[i + 1]) for i in range(0, len(blocks), 2)]
        blocks = [p[0] for p in pairs]
        ties = [p[1] for p in pairs]
        for upper in range(bit + 1, width):
            right = on_right(axis, stage + upper)
            ties = [
                tuple(jnp.where(right, v, u) for u, v in zip(ties[i], ties[i + 1]))
                for i in range(0, len(ties), 2)
            ]
        for i in range(3):
            links[bit][i] = ties[0][i]
    (whole,) = blocks
    if last:
        for n, value in enumerate(toward(on_right(axis, stage + width), whole)):
            send[n] = value
    else:
        for q in range(7):
            send[q] = whole[q]


def join_stage(own, got, axis, stage, width, last, after):
    lines = own.shape[1]
    return pl.pallas_call(
        functools.partial(join_kernel, axis, stage, width, last),
        in_specs=[IN_VMEM] * (1 + len(got)) + [ANYWHERE] * len(after),
        out_shape=[shape_of(3 if last else 7, lines, LANES)] + [shape_of(3, lines, LANES)] * width,
        compiler_params=params(),
    )(own, *got, *after)


def gather_line(view, axis, widest=1, meanwhile=(), cross=False):
    stages = stages_of(axis)
    links, stage = [], 0
    while stage < stages - 1:
        width = min(widest, stages - 1 - stage)
        got = [swap(view, axis, flip << stage) for flip in range(1, 1 << width)]
        last = stage + width == stages - 1
        view, *ties = join_stage(view, got, axis, stage, width, last, meanwhile)
        links += ties
        stage += width
        meanwhile = ()
    return view, swap(view, axis, 1 << stage | (cross and stage > 0)), links


def top_flux(axis, stages, own, got):
    right = on_right(axis, stages - 1)
    face = own[2] + got[2]
    jump = jnp.where(right, own[1] - got[1], got[1] - own[1])
    return jump * face * inverse(1.0 + face * (own[0] + got[0]))


def block_ends(axis, stages, links):
    shape = links[0].shape[1:] if links else None
    right = on_right(axis, stages - 1)
    zero = jnp.zeros(shape, F32)
    low, high = zero, zero
    unit_low = zero + jnp.where(right, -1.0, 0.0)
    unit_high = zero + jnp.where(right, 0.0, 1.0)
    for stage in range(stages - 2, -1, -1):
        tie = links[stage]
        right = on_right(axis, stage)
        flux = between(tie[0], tie[1], tie[2], low, high)
        unit = between(0.0, tie[1], tie[2], unit_low, unit_high)
        low, high = jnp.where(right, -flux, low), jnp.where(right, high, flux)
        unit_low, unit_high = jnp.where(right, -unit, unit_low), jnp.where(right, unit_high, unit)
    return (low, high), (unit_low, unit_high)


def natural(index, parts):
    span = SUBLANES * parts
    local = index % span
    return index - local + local % SUBLANES * parts + local // SUBLANES


def turn_matrix(shape, from_natural, parts):
    row = lax.broadcasted_iota(jnp.int32, shape, 0)
    column = lax.broadcasted_iota(jnp.int32, shape, 1) % LANES
    hit = natural(row, parts) == column if from_natural else row == natural(column, parts)
    return jnp.where(hit, 1.0, 0.0).astype(jnp.bfloat16)


def turned(matrix, field, rows=None):
    high = field.astype(jnp.bfloat16).astype(F32)
    both = jnp.concatenate([high, field - high], 1)
    if rows:
        both = jnp.concatenate(
            [jnp.broadcast_to(both[n : n + 1, :], (rows, 2 * LANES)) for n in range(field.shape[0])], 0
        )
    both = both.astype(jnp.bfloat16)
    return lax.dot_general(
        matrix, both, (((1,), (1,)), ((), ())), preferred_element_type=F32
    )


def y_factor_kernel(c_ref, after, w_ref, i_ref, p_ref, inner, outer, view, to_y, to_x, unit_low, unit_high, c_s, q_s, r_s):
    chunks, sheets, rows, _ = c_ref.shape
    each = LANES // rows
    pairs = sheets // each
    x_steps = rows // SUBLANES
    steps = LANES // SUBLANES
    to_y[...] = turn_matrix(to_y.shape, True, steps)
    to_x[...] = turn_matrix(to_x.shape, False, x_steps)
    for m in range(pairs):
        for y in range(chunks):
            block = jnp.concatenate(
                [
                    c_ref[y, m * each + i, pl.ds(k, SUBLANES, stride=x_steps), :]
                    for i in range(each)
                    for k in range(x_steps)
                ],
                0,
            )
            c_s[m, part_of(y), :] = block.T

    members = [(y, m) for y in range(chunks) for m in range(pairs)]
    lines = len(members)

    def cond(k):
        return jnp.stack([c_s[m, pl.ds(y * LANES + k, SUBLANES, stride=steps), :] for y, m in members], 0)

    def keep(k, w, inv, p):
        w_ref[k] = w
        i_ref[k] = inv
        p_ref[k] = p

    block = factor(cond, steps, keep)
    for n, q in enumerate(COEFS):
        for i in range(lines):
            q_s[n, i * SUBLANES : (i + 1) * SUBLANES, :] = block[q][i]
    segments = [
        {q: q_s[n, pl.ds(s, lines, stride=SUBLANES), :] for n, q in enumerate(COEFS)}
        for s in range(SUBLANES)
    ]
    whole, levels = tree(segments, join_coefs)
    for (offset, _), level in zip(node_offsets(SUBLANES), levels):
        for n, values in enumerate(level):
            for i in range(3):
                inner[offset + n, i] = values[i]
    for n, q in enumerate(COEFS):
        r_s[n] = whole[q]
    parts = [
        {q: r_s[n, y * pairs : (y + 1) * pairs, :] for n, q in enumerate(COEFS)} for y in range(chunks)
    ]
    whole, levels = tree(parts, join_coefs)
    for (offset, _), level in zip(node_offsets(chunks), levels):
        for n, values in enumerate(level):
            for i in range(3):
                outer[offset + n, i] = values[i]
    for n, q in enumerate(COEFS):
        view[n] = whole[q]

    one = jnp.ones((pairs, LANES), F32)
    for n, (low, high, field) in enumerate(((one, 0.0 * one, unit_low), (0.0 * one, one, unit_high))):
        for y, pair in enumerate(tree_ends(chunks, outer, nothing, low, high)):
            for i in range(2):
                r_s[2 * n + i, y * pairs : (y + 1) * pairs, :] = pair[i]
        for s, pair in enumerate(tree_ends(SUBLANES, inner, nothing, r_s[2 * n], r_s[2 * n + 1])):
            for i in range(2):
                q_s[2 * n + i, pl.ds(s, lines, stride=SUBLANES), :] = pair[i]
        low, value = (
            jnp.stack(
                [q_s[2 * n + i, j * SUBLANES : (j + 1) * SUBLANES, :] for j in range(lines)], 0
            )
            for i in range(2)
        )
        for k in range(steps - 1, -1, -1):
            value = w_ref[k] * value + p_ref[k] * low
            for j, (y, m) in enumerate(members):
                field[y, k * SUBLANES : (k + 1) * SUBLANES, part_of(m)] = value[j]


def y_factor(c, after):
    chunks, sheets, rows, _ = c.shape
    pairs = sheets * rows // LANES
    lines = chunks * pairs
    stored = shape_of(LANES // SUBLANES, lines, SUBLANES, LANES)
    matrix = jax.ShapeDtypeStruct((LANES, 2 * LANES), jnp.bfloat16)
    return pl.pallas_call(
        y_factor_kernel,
        in_specs=[IN_VMEM, ANYWHERE],
        out_shape=[
            stored,
            stored,
            stored,
            shape_of(SUBLANES - 1, 3, lines, LANES),
            shape_of(chunks - 1, 3, pairs, LANES),
            shape_of(len(COEFS), pairs, LANES),
            matrix,
            matrix,
            shape_of(chunks, LANES, pairs * LANES),
            shape_of(chunks, LANES, pairs * LANES),
        ],
        scratch_shapes=[
            pltpu.VMEM((pairs, chunks * LANES, LANES), F32),
            pltpu.VMEM((len(COEFS), lines * SUBLANES, LANES), F32),
            pltpu.VMEM((len(COEFS), lines, LANES), F32),
        ],
        compiler_params=params(),
        cost_estimate=pl.CostEstimate(flops=20 * c.size, bytes_accessed=16 * c.size, transcendentals=0),
    )(c, after)


def z_factor_kernel(c_ref, after, w_ref, i_ref):
    sheets = c_ref.shape[1]
    ground = 1.0
    for z in range(sheets - 1):
        face = c_ref[:, z] + c_ref[:, z + 1]
        inv = inverse(ground + face)
        w = face * inv
        i_ref[z] = inv
        w_ref[z] = w
        ground = 1.0 + w * ground
    i_ref[sheets - 1] = inverse(ground)


def z_factor(c, after):
    chunks, sheets, rows, _ = c.shape
    return pl.pallas_call(
        z_factor_kernel,
        in_specs=[IN_VMEM, ANYWHERE],
        out_shape=[
            shape_of(sheets - 1, chunks, rows, LANES),
            shape_of(sheets, chunks, rows, LANES),
        ],
        compiler_params=params(),
        cost_estimate=pl.CostEstimate(flops=10 * c.size, bytes_accessed=12 * c.size, transcendentals=0),
    )(c, after)


def join_tree(items, links, own):
    for offset, count in node_offsets(len(items)):
        joined = []
        for n in range(count):
            tie = tuple(links[offset + n, i] for i in range(3))
            both, flux = join_targets(items[2 * n], items[2 * n + 1], tie)
            own[offset + n] = flux
            joined.append(both)
        items = joined
    return items[0]


def tree_ends(leaves, links, own, low, high):
    levels = [
        [(own(offset + n), links[offset + n, 1], links[offset + n, 2]) for n in range(count)]
        for offset, count in node_offsets(leaves)
    ]
    return descend(levels, low, high)


def nothing(node):
    return 0.0


def y_prepare_kernel(stages, *refs):
    ties = refs[: stages - 1]
    xw, xh, xm, xp, x_links, x_own, t_ref, to_y, y_low, y_high = refs[stages - 1 : stages + 9]
    base, response, to_first, to_last, fixed, f_s, g_s = refs[stages + 9 :]
    x_steps, lines = xw.shape[:2]
    chunks = base.shape[0]
    sheets = lines // chunks
    rows = x_steps * SUBLANES

    ends, units = block_ends("gx", stages, ties)
    for n, (own, (low, high)) in enumerate(((lambda i: x_own[i], ends), (nothing, units))):
        for s, pair in enumerate(tree_ends(SUBLANES, x_links, own, low, high)):
            for i in range(2):
                f_s[n, i, pl.ds(s, lines, stride=SUBLANES), :] = pair[i]
    first = 0
    for n, members in enumerate(line_groups(chunks, sheets)):
        at = slice(first, first + len(members))
        h_ref_of, h_at = (xh, at) if n == 0 else (xm, slice(first - 2 * sheets, at.stop - 2 * sheets))
        (low, value), (unit_low, unit) = (
            [
                jnp.stack(
                    [f_s[q, i, j * SUBLANES : (j + 1) * SUBLANES, :] for j in range(at.start, at.stop)], 0
                )
                for i in range(2)
            ]
            for q in range(2)
        )
        for k in range(x_steps - 1, -1, -1):
            w, p = xw[k, at], xp[k, at]
            value = w * value + (h_ref_of[k, h_at] + p * low)
            unit = w * unit + p * unit_low
            field = value - t_ref[k, at]
            for j, (y, z) in enumerate(members):
                place = z * rows + k * SUBLANES
                g_s[0, y, place : place + SUBLANES, :] = field[j]
                g_s[1, y, place : place + SUBLANES, :] = unit[j]
        first = at.stop

    totals = [None, None]
    for y in range(chunks):
        field = turned(to_y[...], g_s[0, y])
        answer = turned(to_y[...], g_s[1, y])
        base[y] = field
        response[y] = answer
        for i, (unit, weight) in enumerate(((y_low, to_first), (y_high, to_last))):
            weight[y] = unit[y] * answer
            part = unit[y] * field
            totals[i] = part if y == 0 else totals[i] + part
    for i in range(2):
        put_sums(fixed.at[i], totals[i])


def put_sums(out, field):
    total = jnp.sum(field, 0, keepdims=True)
    for m in range(out.shape[0]):
        out[m : m + 1, :] = total[:, part_of(m)]


def y_prepare(ties, xw, xh, xm, xp, x_links, x_own, t, to_y, unit_low, unit_high):
    chunks = unit_low.shape[0]
    x_steps, lines = xw.shape[:2]
    width = lines // chunks * x_steps * SUBLANES
    field = shape_of(chunks, LANES, width)
    return pl.pallas_call(
        functools.partial(y_prepare_kernel, len(ties) + 1),
        out_shape=[field] * 4 + [shape_of(2, width // LANES, LANES)],
        scratch_shapes=[
            pltpu.VMEM((2, 2, lines * SUBLANES, LANES), F32),
            pltpu.VMEM((2, chunks, width, LANES), F32),
        ],
        compiler_params=params(),
        cost_estimate=pl.CostEstimate(flops=8 * t.size, bytes_accessed=16 * t.size, transcendentals=0),
    )(*ties, xw, xh, xm, xp, x_links, x_own, t, to_y, unit_low, unit_high)


def y_target_kernel(stages, own, got, to_first, to_last, fixed, view, to_y, spread, send, r_s):
    chunks, _, width = to_first.shape
    sheets = own.shape[1] // chunks
    rows = width // sheets

    flux = top_flux("gx", stages, own, got)
    line_of = {member: n for n, member in enumerate(sum(line_groups(chunks, sheets), []))}
    totals = [None, None]
    for y in range(chunks):
        own_flux = jnp.concatenate([flux[line_of[y, z] : line_of[y, z] + 1, :] for z in range(sheets)], 0)
        wide = turned(to_y[...], own_flux, rows)
        spread[y] = wide
        for i, weight in enumerate((to_first, to_last)):
            part = weight[y] * wide
            totals[i] = part if y == 0 else totals[i] + part
    for n, q in enumerate(COEFS):
        send[q] = view[n]
    for i, q in enumerate((FIRST, LAST)):
        put_sums(r_s.at[i], totals[i])
        send[q] = fixed[i] + r_s[i]


def y_target(own, got, to_first, to_last, fixed, view, to_y):
    pairs = view.shape[1]
    return pl.pallas_call(
        functools.partial(y_target_kernel, stages_of("gx")),
        out_shape=[shape_of(*to_first.shape), shape_of(7, pairs, LANES)],
        scratch_shapes=[pltpu.VMEM((2, pairs, LANES), F32)],
        compiler_params=params(),
    )(own, got, to_first, to_last, fixed, view, to_y)


def y_eliminate_kernel(base, response, spread, yw, yi, yp, inner, outer, after, *refs):
    h_ref, inner_own, outer_own, q_s, r_s = refs
    chunks, _, width = base.shape
    pairs = width // LANES
    steps = yw.shape[0]
    members = [(y, m) for y in range(chunks) for m in range(pairs)]

    def target(k):
        at = slice(k * SUBLANES, (k + 1) * SUBLANES)
        return jnp.stack(
            [
                base[y, at, part_of(m)] + response[y, at, part_of(m)] * spread[y, at, part_of(m)]
                for y, m in members
            ],
            0,
        )

    def keep(k, h):
        h_ref[k] = h

    ends = eliminate(target, steps, lambda k: yw[k], lambda k: yi[k], lambda k: yp[k], keep)
    for q in range(2):
        for i in range(len(members)):
            q_s[q, i * SUBLANES : (i + 1) * SUBLANES, :] = ends[q][i]
    items = [
        tuple(q_s[q, pl.ds(s, len(members), stride=SUBLANES), :] for q in range(2))
        for s in range(SUBLANES)
    ]
    r_s[0], r_s[1] = join_tree(items, inner, inner_own)
    items = [tuple(r_s[q, y * pairs : (y + 1) * pairs, :] for q in range(2)) for y in range(chunks)]
    join_tree(items, outer, outer_own)


def y_eliminate(base, response, spread, yw, yi, yp, inner, outer, after):
    y_lines = yw.shape[1]
    pairs = outer.shape[2]
    chunks = y_lines // pairs
    return pl.pallas_call(
        y_eliminate_kernel,
        in_specs=[IN_VMEM] * 8 + [ANYWHERE],
        out_shape=[
            shape_of(*yw.shape),
            shape_of(SUBLANES - 1, y_lines, LANES),
            shape_of(chunks - 1, pairs, LANES),
        ],
        scratch_shapes=[
            pltpu.VMEM((2, y_lines * SUBLANES, LANES), F32),
            pltpu.VMEM((2, y_lines, LANES), F32),
        ],
        compiler_params=params(),
        cost_estimate=pl.CostEstimate(flops=8 * base.size, bytes_accessed=16 * base.size, transcendentals=0),
    )(base, response, spread, yw, yi, yp, inner, outer, after)


def z_solve(zw, zi, field, at, keep):
    sheets = zi.shape[0]
    rhs, kept = None, []
    for z in range(sheets):
        rhs = field(z) if z == 0 else field(z) + zw[(z - 1, *at)] * rhs
        kept.append(rhs * zi[(z, *at)])
    value = kept[-1]
    keep(sheets - 1, value)
    for z in range(sheets - 2, -1, -1):
        value = zw[(z, *at)] * value + kept[z]
        keep(z, value)


def finish_prepare_kernel(stages, *refs):
    ties = refs[: stages - 1]
    yw, yh, yp, inner, inner_own, outer, outer_own, zw, zi, t_ref, to_x = refs[stages - 1 : stages + 10]
    base, response, r_s, e_s, u_s = refs[stages + 10 :]
    chunks, sheets, rows, _ = base.shape
    each = LANES // rows
    pairs = sheets // each
    steps = yw.shape[0]
    lines = chunks * pairs

    ends, units = block_ends("gy", stages, ties)
    both = (
        (lambda i: outer_own[i], lambda i: inner_own[i], ends),
        (nothing, nothing, units),
    )
    for n, (upper, lower, (low, high)) in enumerate(both):
        for y, pair in enumerate(tree_ends(chunks, outer, upper, low, high)):
            for i in range(2):
                r_s[n, i, y * pairs : (y + 1) * pairs, :] = pair[i]
        for s, pair in enumerate(tree_ends(SUBLANES, inner, lower, r_s[n, 0], r_s[n, 1])):
            for i in range(2):
                e_s[n, i, pl.ds(s, lines, stride=SUBLANES), :] = pair[i]
    (low, value), (unit_low, unit) = (
        [
            jnp.stack([e_s[q, i, n * SUBLANES : (n + 1) * SUBLANES, :] for n in range(lines)], 0)
            for i in range(2)
        ]
        for q in range(2)
    )
    for k in range(steps - 1, -1, -1):
        w, p = yw[k], yp[k]
        value = w * value + (yh[k] + p * low)
        unit = w * unit + p * unit_low
        for y in range(chunks):
            for m in range(pairs):
                place = pl.ds(y * LANES + k, SUBLANES, stride=steps)
                u_s[0, m, place, :] = value[y * pairs + m]
                u_s[1, m, place, :] = unit[y * pairs + m]

    for y in range(chunks):
        part = part_of(y)
        fields = [turned(to_x[...], u_s[0, m, part, :]) for m in range(pairs)]

        def field(z):
            at = z % each * rows
            return fields[z // each][at : at + rows, :]

        def keep(z, value):
            base[y, z] = t_ref[y, z] + value

        z_solve(zw, zi, field, (y,), keep)
        for m in range(pairs):
            units = turned(to_x[...], u_s[1, m, part, :])
            for i in range(each):
                response[y, m * each + i] = units[i * rows : (i + 1) * rows, :]


def finish_prepare(ties, yw, yh, yp, inner, inner_own, outer, outer_own, zw, zi, t, to_x):
    chunks, sheets, rows, _ = t.shape
    pairs = sheets * rows // LANES
    lines = chunks * pairs
    field = shape_of(chunks, sheets, rows, LANES)
    return pl.pallas_call(
        functools.partial(finish_prepare_kernel, len(ties) + 1),
        out_shape=[field, field],
        scratch_shapes=[
            pltpu.VMEM((2, 2, lines, LANES), F32),
            pltpu.VMEM((2, 2, lines * SUBLANES, LANES), F32),
            pltpu.VMEM((2, pairs, chunks * LANES, LANES), F32),
        ],
        compiler_params=params(),
        cost_estimate=pl.CostEstimate(flops=12 * t.size, bytes_accessed=20 * t.size, transcendentals=0),
    )(*ties, yw, yh, yp, inner, inner_own, outer, outer_own, zw, zi, t, to_x)


def finish_kernel(stages, own, got, base, response, zw, zi, to_x, out, o_s, sems):
    chunks, sheets, rows, _ = base.shape
    each = LANES // rows
    pairs = sheets // each
    flux = top_flux("gy", stages, own, got)
    spread = [
        turned(to_x[...], flux[m : m + 1, :], LANES) for m in range(pairs)
    ]
    started = []
    block = rows // OUT_COPIES
    for n in range(OUT_COPIES):
        strip = slice(n * block, (n + 1) * block)
        for y in range(chunks):

            def field(z):
                at = z % each * rows + strip.start
                return response[y, z, strip, :] * spread[z // each][at : at + block, :]

            def keep(z, value):
                o_s[z, strip, part_of(y)] = base[y, z, strip, :] + value

            z_solve(zw, zi, field, (y, strip), keep)
        at = pl.ds(strip.start, block)
        copy = pltpu.make_async_copy(o_s.at[:, at, :], out.at[:, at, :], sems.at[n])
        copy.start()
        started.append(copy)
    for copy in started:
        copy.wait()


def finish(own, got, base, response, zw, zi, to_x):
    chunks, sheets, rows, _ = base.shape
    shape = (sheets, rows, chunks * LANES)
    return pl.pallas_call(
        functools.partial(finish_kernel, stages_of("gy")),
        out_shape=shape_of(*shape),
        out_specs=ANYWHERE,
        scratch_shapes=[pltpu.VMEM(shape, F32), pltpu.SemaphoreType.DMA((OUT_COPIES,))],
        compiler_params=params(),
    )(own, got, base, response, zw, zi, to_x)


def per_device(temperature, base, locations, energy):
    columns = temperature.shape[2]
    gy = lax.axis_size("gy")
    t_edge, b_edge, loc, heat, packed = load(temperature, base, locations[None], energy[None])
    near = swap(packed, "gy", 1)
    far = lax.ppermute(packed, "gy", [(i, ((i + 1) % gy ^ 1) - 1 if i else gy - 1) for i in range(gy)])
    c, total, xw, xi, xp, x_links, x_view, xm, ends, t_steps, swapped, t = x_factor(
        loc, heat, t_edge, b_edge, temperature, base, columns * gy, packed
    )
    xh, x_own, view = x_target(swapped, total, near, far, xw, xi, xp, x_links, x_view, ends)
    yw, yi, yp, inner, outer, y_view, to_y, to_x, unit_low, unit_high = y_factor(c, x_view)
    zw, zi = z_factor(c, view)
    own, got, ties = gather_line(view, "gx", 2, (y_view, zw))
    base, response, to_first, to_last, fixed = y_prepare(
        ties, xw, xh, xm, xp, x_links, x_own, t_steps, to_y, unit_low, unit_high
    )
    spread, view = y_target(own, got, to_first, to_last, fixed, y_view, to_y)
    yh, inner_own, outer_own = y_eliminate(base, response, spread, yw, yi, yp, inner, outer, view)
    own, got, ties = gather_line(view, "gy", meanwhile=(yh,), cross=True)
    base, response = finish_prepare(
        ties, yw, yh, yp, inner, inner_own, outer, outer_own, zw, zi, t, to_x
    )
    return finish(own, got, base, response, zw, zi, to_x)


def solution(mesh):
    in_specs = (P(None, "gx", "gy"), P(None, "gx", "gy"), P(), P())
    out_specs = P(None, "gx", "gy")
    return jax.shard_map(
        per_device, mesh=mesh, in_specs=in_specs, out_specs=out_specs, check_vma=False
    )
```

```python
import functools

import jax
import jax.numpy as jnp
from jax import lax
from jax.experimental import pallas as pl
from jax.experimental.pallas import tpu as pltpu
from jax.sharding import PartitionSpec as P

RATE = 2000.0
THERMAL_GROWTH = 0.8
LANES = 128
SUBLANES = 8
F32 = jnp.float32
MIB = 1024 * 1024
OUT_COPIES = 4
ANYWHERE = pl.BlockSpec(memory_space=pl.ANY)
IN_HBM = pl.BlockSpec(memory_space=pltpu.HBM)
IN_VMEM = pl.BlockSpec(memory_space=pltpu.VMEM)

R00, R0L, RLL, FIRST, LAST, C0, CL = range(7)
COEFS = (R00, R0L, RLL, C0, CL)


def params(limit=40):
    return pltpu.CompilerParams(vmem_limit_bytes=limit * MIB)


def shape_of(*sizes):
    return jax.ShapeDtypeStruct(sizes, F32)


def half_conduct(base, temperature):
    return base * (0.5 * RATE + (0.5 * RATE * THERMAL_GROWTH) * temperature)


def inverse(x):
    guess = pl.reciprocal(x, approx=True)
    return guess * (2.0 - x * guess)


def join_coefs(a, b):
    face = a[CL] + b[C0]
    inv = face * inverse(1.0 + face * (a[RLL] + b[R00]))
    left = a[R0L] * inv
    right = b[R0L] * inv
    joined = {
        R00: a[R00] - left * a[R0L],
        R0L: left * b[R0L],
        RLL: b[RLL] - right * b[R0L],
        C0: a[C0],
        CL: b[CL],
    }
    return joined, (inv, right, left)


def join_targets(a, b, links):
    inv, right, left = links
    jump = b[0] - a[1]
    return (a[0] + left * jump, b[1] - right * jump), jump * inv


def between(own, right, left, low, high):
    return own + right * high - left * low


def tree(items, join):
    levels = []
    while len(items) > 1:
        pairs = [join(items[i], items[i + 1]) for i in range(0, len(items), 2)]
        items = [p[0] for p in pairs]
        levels.append([p[1] for p in pairs])
    return items[0], levels


def descend(levels, low, high):
    ends = [(low, high)]
    for level in reversed(levels):
        below = []
        for (lo, hi), (own, right, left) in zip(ends, level):
            flux = between(own, right, left, lo, hi)
            below += [(lo, flux), (-flux, hi)]
        ends = below
    return ends


def node_offsets(leaves):
    offsets, at, count = [], 0, leaves // 2
    while count:
        offsets.append((at, count))
        at += count
        count //= 2
    return offsets


def factor(cond, steps, keep):
    here = cond(0)
    c_first = here
    one = jnp.ones_like(here)
    ground, path, first_first = one, one, None
    for k in range(steps - 1):
        following = cond(k + 1)
        face = here + following
        inv = inverse(ground + face)
        w = face * inv
        p = path * inv
        keep(k, w, inv, p)
        step = path * p
        first_first = step if first_first is None else first_first + step
        path = path * w
        ground = 1.0 + w * ground
        here = following
    inv = inverse(ground)
    p = path * inv
    keep(steps - 1, inv, inv, p)
    return {R00: first_first + path * p, R0L: p, RLL: inv, C0: c_first, CL: here}


def eliminate(target, steps, w, inv, p, keep):
    rhs = target(0)
    first = None
    for k in range(steps):
        h = rhs * inv(k)
        keep(k, h)
        step = rhs * p(k)
        first = step if first is None else first + step
        if k < steps - 1:
            rhs = target(k + 1) + w(k) * rhs
    return first, h


def is_odd(axis):
    return lax.axis_index(axis) % 2 == 1


def fold(cells, used):
    steps = cells.shape[0] // SUBLANES
    total = cells[pl.ds(0, SUBLANES, stride=steps), :]
    lane = lax.broadcasted_iota(jnp.int32, total.shape, 1)
    for k in range(1, steps):
        part = pltpu.roll(cells[pl.ds(k, SUBLANES, stride=steps), :], k * used, 1)
        total = jnp.where(lane // used == k, part, total)
    return total


def load_kernel(t_hbm, b_hbm, t_out, b_out, packed, cells, sems):
    sheets, rows, columns = t_hbm.shape
    parts = [(0, LANES), (columns - LANES, LANES), (LANES, columns - 2 * LANES)]
    copies = []
    for n, (start, size) in enumerate(parts):
        part = pl.ds(start, size)
        for i, (src, dst) in enumerate(((t_hbm, t_out), (b_hbm, b_out))):
            copies.append(
                pltpu.make_async_copy(src.at[:, :, part], dst.at[:, :, part], sems.at[i, n])
            )
    for copy in copies:
        copy.start()
    lane = lax.broadcasted_iota(jnp.int32, (rows, LANES), 1)
    edge_t = jnp.zeros((rows, LANES), F32)
    edge_c = edge_t
    for side, source in enumerate((0, LANES - 1)):
        for copy in copies[2 * side : 2 * side + 2]:
            copy.wait()
        part = slice(parts[side][0], parts[side][0] + LANES)
        for z in range(sheets):
            t = t_out[z, :, part]
            c = half_conduct(b_out[z, :, part], t)
            place = lane == sheets * side + z
            edge_t = jnp.where(place, t[:, source : source + 1], edge_t)
            edge_c = jnp.where(place, c[:, source : source + 1], edge_c)
    cells[0], cells[1] = edge_t, edge_c
    for i in range(2):
        packed[i * SUBLANES : (i + 1) * SUBLANES, :] = fold(cells.at[i], 2 * sheets)
    for copy in copies[4:]:
        copy.wait()


def load(temperature, base):
    sheets, rows, columns = temperature.shape
    assert rows // SUBLANES * 2 * sheets <= LANES and columns > 2 * LANES
    operands = (temperature, base)
    return pl.pallas_call(
        load_kernel,
        in_specs=[IN_HBM] * 2,
        out_shape=[pltpu.VMEM(v.shape, v.dtype) for v in operands]
        + [pltpu.VMEM((2 * SUBLANES, LANES), F32)],
        scratch_shapes=[pltpu.VMEM((2, rows, LANES), F32), pltpu.SemaphoreType.DMA((2, 3))],
        compiler_params=params(),
    )(*[pltpu.with_memory_space_constraint(v, pltpu.HBM) for v in operands])


def source_plane(loc, energy, rows, columns, plate):
    place = loc[...]
    count = place.shape[1]
    local_x = place // plate - lax.axis_index("gx") * rows
    local_y = place % plate - lax.axis_index("gy") * columns
    in_x = lax.broadcasted_iota(jnp.int32, (rows, count), 0) == local_x
    in_y = lax.broadcasted_iota(jnp.int32, (columns, count), 0) == local_y
    by_y = jnp.where(in_y, 1.0, 0.0).astype(jnp.bfloat16)
    left = energy[...]
    plane = None
    for _ in range(3):
        part = left.astype(jnp.bfloat16).astype(F32)
        left = left - part
        term = lax.dot_general(
            jnp.where(in_x, part, 0.0).astype(jnp.bfloat16),
            by_y,
            (((1,), (1,)), ((), ())),
            preferred_element_type=F32,
        )
        plane = term if plane is None else plane + term
    return plane


def part_of(y):
    return slice(y * LANES, (y + 1) * LANES)


def line_groups(chunks, sheets):
    order = [0, chunks - 1] + list(range(1, chunks - 1))
    return [[(y, z) for y in order[i : i + 2] for z in range(sheets)] for i in range(0, chunks, 2)]


def x_eliminate(cells, members, first_line, w_ref, i_ref, p_ref, h_ref, h_line, q_s):
    steps = w_ref.shape[0]
    at = slice(first_line, first_line + len(members))
    kept_at = slice(h_line, h_line + len(members))

    def target(k):
        return jnp.stack([cells(y, z, k) for y, z in members], 0)

    def keep(k, h):
        h_ref[k, kept_at] = h

    ends = eliminate(
        target, steps, lambda k: w_ref[k, at], lambda k: i_ref[k, at], lambda k: p_ref[k, at], keep
    )
    for q in range(2):
        for i in range(len(members)):
            first = (first_line + i) * SUBLANES
            q_s[q, first : first + SUBLANES, :] = ends[q][i]


def x_factor_kernel(plate, loc_hbm, energy_hbm, t_ref, b_ref, own_cells, *refs):
    c_ref, total_ref, w_ref, i_ref, p_ref, links, view, h_ref, ends_ref, t_out, swapped, q_s, t_s, loc, energy, sems = refs
    chunks, sheets, rows, _ = c_ref.shape
    lines = chunks * sheets
    steps = rows // SUBLANES
    copies = [
        pltpu.make_async_copy(src, dst, sems.at[i])
        for i, (src, dst) in enumerate(((loc_hbm, loc), (energy_hbm, energy)))
    ]
    for copy in copies:
        copy.start()
    mine = own_cells[...]
    in_low = lax.broadcasted_iota(jnp.int32, mine.shape, 1) % (2 * sheets) < sheets
    swapped[...] = jnp.where(
        in_low, pltpu.roll(mine, LANES - sheets, 1), pltpu.roll(mine, sheets, 1)
    )

    lane = lax.broadcasted_iota(jnp.int32, (SUBLANES, LANES), 1)
    is_first, is_last = lane == 0, lane == LANES - 1
    for r in range(steps):
        at = slice(r * SUBLANES, (r + 1) * SUBLANES)
        before_t, before_c = None, None
        for z in range(sheets):
            ts = [t_ref[z, at, part_of(y)] for y in range(chunks)]
            cs = [half_conduct(b_ref[z, at, part_of(y)], ts[y]) for y in range(chunks)]
            t_turned = [pltpu.roll(v, LANES - 1, 1) for v in ts]
            c_turned = [pltpu.roll(v, LANES - 1, 1) for v in cs]
            flux = []
            for y in range(chunks):
                if y < chunks - 1:
                    t_next = jnp.where(is_last, t_turned[y + 1], t_turned[y])
                    c_next = jnp.where(is_last, c_turned[y + 1], c_turned[y])
                    flux.append((cs[y] + c_next) * (t_next - ts[y]))
                else:
                    inside = (cs[y] + c_turned[y]) * (t_turned[y] - ts[y])
                    flux.append(jnp.where(is_last, 0.0, inside))
            turned = [pltpu.roll(v, 1, 1) for v in flux]
            for y in range(chunks):
                from_low = jnp.where(is_first, turned[y - 1] if y else 0.0, turned[y])
                total = ts[y] + (flux[y] - from_low)
                if z > 0:
                    across = (before_c[y] + cs[y]) * (ts[y] - before_t[y])
                    total = total - across
                    total_ref[y, z - 1, at, :] += across
                total_ref[y, z, at, :] = total
                c_ref[y, z, at, :] = cs[y]
                t_s[y, z, at, :] = ts[y]
            before_t, before_c = ts, cs

    for copy in copies:
        copy.wait()
    plane = source_plane(loc, energy, rows, chunks * LANES, plate)
    for y in range(chunks):
        total_ref[y, 0] += plane[:, part_of(y)]

    at = 0
    for n, members in enumerate(line_groups(chunks, sheets)):

        def cond(k):
            return jnp.stack([c_ref[y, z, pl.ds(k, SUBLANES, stride=steps), :] for y, z in members], 0)

        def keep(k, w, inv, p):
            w_ref[k, at : at + len(members)] = w
            i_ref[k, at : at + len(members)] = inv
            p_ref[k, at : at + len(members)] = p

        block = factor(cond, steps, keep)
        for i, q in enumerate(COEFS):
            for j in range(len(members)):
                first = (at + j) * SUBLANES
                q_s[i, first : first + SUBLANES, :] = block[q][j]
        if n > 0:
            x_eliminate(
                lambda y, z, k: total_ref[y, z, pl.ds(k, SUBLANES, stride=steps), :],
                members, at, w_ref, i_ref, p_ref, h_ref, at - 2 * sheets, ends_ref,
            )
        for k in range(steps):
            for i, (y, z) in enumerate(members):
                t_out[k, at + i] = t_s[y, z, pl.ds(k, SUBLANES, stride=steps), :]
        at += len(members)

    segments = [
        {q: q_s[n, pl.ds(s, lines, stride=SUBLANES), :] for n, q in enumerate(COEFS)}
        for s in range(SUBLANES)
    ]
    whole, levels = tree(segments, join_coefs)
    for (offset, _), level in zip(node_offsets(SUBLANES), levels):
        for n, values in enumerate(level):
            for i in range(3):
                links[offset + n, i] = values[i]
    for n, q in enumerate(COEFS):
        view[n] = whole[q]


def x_factor(loc, energy, t, b, plate, own_cells):
    sheets, rows, columns = t.shape
    chunks = columns // LANES
    lines = chunks * sheets
    steps = rows // SUBLANES
    field = shape_of(chunks, sheets, rows, LANES)
    stored = shape_of(steps, lines, SUBLANES, LANES)
    return pl.pallas_call(
        functools.partial(x_factor_kernel, plate),
        in_specs=[IN_HBM] * 2 + [IN_VMEM] * 3,
        out_shape=[
            field,
            field,
            stored,
            stored,
            stored,
            shape_of(SUBLANES - 1, 3, lines, LANES),
            shape_of(len(COEFS), lines, LANES),
            shape_of(steps, max(1, lines - 2 * sheets), SUBLANES, LANES),
            shape_of(2, lines * SUBLANES, LANES),
            stored,
            shape_of(*own_cells.shape),
        ],
        scratch_shapes=[
            pltpu.VMEM((len(COEFS), lines * SUBLANES, LANES), F32),
            pltpu.VMEM((chunks, sheets, rows, LANES), F32),
            pltpu.VMEM(loc.shape, loc.dtype),
            pltpu.VMEM(energy.shape, energy.dtype),
            pltpu.SemaphoreType.DMA((2,)),
        ],
        compiler_params=params(),
        cost_estimate=pl.CostEstimate(flops=40 * t.size, bytes_accessed=28 * t.size, transcendentals=0),
    )(*[pltpu.with_memory_space_constraint(v, pltpu.HBM) for v in (loc, energy)], t, b, own_cells)


def x_target_kernel(own_cells, total_ref, near, far, *refs):
    w_ref, i_ref, p_ref, links, view, ends_ref, h_ref, own, send, q_s = refs
    chunks, sheets, rows, _ = total_ref.shape
    lines = chunks * sheets
    steps = rows // SUBLANES

    place = lax.axis_index("gy")
    inner = (place > 0) & (place < lax.axis_size("gy") - 1)
    lane = lax.broadcasted_iota(jnp.int32, (SUBLANES, LANES), 1)
    side = 2 * sheets
    is_near = (lane % side >= sheets).astype(jnp.int32) == place % 2
    t, c = (
        jnp.where(is_near, near[at, :], jnp.where(inner, far[at, :], 0.0))
        for at in (slice(0, SUBLANES), slice(SUBLANES, 2 * SUBLANES))
    )
    face = jnp.where(c > 0.0, own_cells[SUBLANES:, :] + c, 0.0)
    flux = face * (t - own_cells[:SUBLANES, :])

    def cells(y, z, k):
        at = k * side + (sheets + z if y == 0 else z)
        edge = 0 if y == 0 else LANES - 1
        inflow = jnp.where(lane == edge, flux[:, at : at + 1], 0.0)
        return total_ref[y, z, pl.ds(k, SUBLANES, stride=steps), :] + inflow

    members = line_groups(chunks, sheets)[0]
    x_eliminate(cells, members, 0, w_ref, i_ref, p_ref, h_ref, 0, q_s)
    split = len(members)
    items = [
        tuple(
            jnp.concatenate(
                [
                    q_s[q, pl.ds(s, split, stride=SUBLANES), :],
                    ends_ref[q, pl.ds(split * SUBLANES + s, lines - split, stride=SUBLANES), :],
                ],
                0,
            )
            for q in range(2)
        )
        for s in range(SUBLANES)
    ]
    for offset, count in node_offsets(SUBLANES):
        joined = []
        for n in range(count):
            ties = tuple(links[offset + n, i] for i in range(3))
            both, flux = join_targets(items[2 * n], items[2 * n + 1], ties)
            own[offset + n] = flux
            joined.append(both)
        items = joined
    for n, q in enumerate(COEFS):
        send[q] = view[n]
    send[FIRST], send[LAST] = items[0]


def x_target(own_cells, total, near, far, w, inv, p, links, view, ends):
    chunks, sheets, rows, _ = total.shape
    lines = chunks * sheets
    steps = rows // SUBLANES
    return pl.pallas_call(
        x_target_kernel,
        out_shape=[
            shape_of(steps, 2 * sheets, SUBLANES, LANES),
            shape_of(SUBLANES - 1, lines, LANES),
            shape_of(7, lines, LANES),
        ],
        scratch_shapes=[
            pltpu.VMEM((2, 2 * sheets * SUBLANES, LANES), F32),
        ],
        compiler_params=params(),
    )(own_cells, total, near, far, w, inv, p, links, view, ends)


def stages_of(axis):
    return lax.axis_size(axis).bit_length() - 1


def swap(value, axis, flip):
    count = lax.axis_size(axis)
    return lax.ppermute(value, axis, [(i, i ^ flip) for i in range(count)])


def on_right(axis, stage):
    return (lax.axis_index(axis) >> stage) % 2 == 1


def toward(right, block):
    return (
        jnp.where(right, block[R00], block[RLL]),
        jnp.where(right, block[FIRST], block[LAST]),
        jnp.where(right, block[C0], block[CL]),
    )


def join(a, b):
    joined, ties = join_coefs(a, b)
    (joined[FIRST], joined[LAST]), flux = join_targets((a[FIRST], a[LAST]), (b[FIRST], b[LAST]), ties)
    return joined, (flux, ties[1], ties[2])


def ordered(right, own, other):
    first = [jnp.where(right, theirs, mine) for mine, theirs in zip(own, other)]
    second = [jnp.where(right, mine, theirs) for mine, theirs in zip(own, other)]
    return first, second


def join_kernel(axis, stage, width, last, *refs):
    count = 1 << width
    blocks = [[refs[i][q] for q in range(7)] for i in range(count)]
    send = refs[-1 - width]
    links = refs[-width:]
    for bit in range(width):
        right = on_right(axis, stage + bit)
        for i in range(count):
            if not i >> bit & 1:
                j = i | 1 << bit
                blocks[i], blocks[j] = ordered(right, blocks[i], blocks[j])
    for bit in range(width):
        pairs = [join(blocks[i], blocks[i + 1]) for i in range(0, len(blocks), 2)]
        blocks = [p[0] for p in pairs]
        ties = [p[1] for p in pairs]
        for upper in range(bit + 1, width):
            right = on_right(axis, stage + upper)
            ties = [
                tuple(jnp.where(right, v, u) for u, v in zip(ties[i], ties[i + 1]))
                for i in range(0, len(ties), 2)
            ]
        for i in range(3):
            links[bit][i] = ties[0][i]
    (whole,) = blocks
    if last:
        for n, value in enumerate(toward(on_right(axis, stage + width), whole)):
            send[n] = value
    else:
        for q in range(7):
            send[q] = whole[q]


def join_stage(own, got, axis, stage, width, last, after):
    lines = own.shape[1]
    return pl.pallas_call(
        functools.partial(join_kernel, axis, stage, width, last),
        in_specs=[IN_VMEM] * (1 + len(got)) + [ANYWHERE] * len(after),
        out_shape=[shape_of(3 if last else 7, lines, LANES)] + [shape_of(3, lines, LANES)] * width,
        compiler_params=params(),
    )(own, *got, *after)


def gather_line(view, axis, widest=1, meanwhile=(), cross=False):
    stages = stages_of(axis)
    links, stage = [], 0
    while stage < stages - 1:
        width = min(widest, stages - 1 - stage)
        got = [swap(view, axis, flip << stage) for flip in range(1, 1 << width)]
        last = stage + width == stages - 1
        view, *ties = join_stage(view, got, axis, stage, width, last, meanwhile)
        links += ties
        stage += width
        meanwhile = ()
    return view, swap(view, axis, 1 << stage | (cross and stage > 0)), links


def top_flux(axis, stages, own, got):
    right = on_right(axis, stages - 1)
    face = own[2] + got[2]
    jump = jnp.where(right, own[1] - got[1], got[1] - own[1])
    return jump * face * inverse(1.0 + face * (own[0] + got[0]))


def block_ends(axis, stages, links):
    shape = links[0].shape[1:] if links else None
    right = on_right(axis, stages - 1)
    zero = jnp.zeros(shape, F32)
    low, high = zero, zero
    unit_low = zero + jnp.where(right, -1.0, 0.0)
    unit_high = zero + jnp.where(right, 0.0, 1.0)
    for stage in range(stages - 2, -1, -1):
        tie = links[stage]
        right = on_right(axis, stage)
        flux = between(tie[0], tie[1], tie[2], low, high)
        unit = between(0.0, tie[1], tie[2], unit_low, unit_high)
        low, high = jnp.where(right, -flux, low), jnp.where(right, high, flux)
        unit_low, unit_high = jnp.where(right, -unit, unit_low), jnp.where(right, unit_high, unit)
    return (low, high), (unit_low, unit_high)


def natural(index, parts):
    span = SUBLANES * parts
    local = index % span
    return index - local + local % SUBLANES * parts + local // SUBLANES


def turn_matrix(shape, from_natural, parts):
    row = lax.broadcasted_iota(jnp.int32, shape, 0)
    column = lax.broadcasted_iota(jnp.int32, shape, 1) % LANES
    hit = natural(row, parts) == column if from_natural else row == natural(column, parts)
    return jnp.where(hit, 1.0, 0.0).astype(jnp.bfloat16)


def turned(matrix, field, rows=None):
    high = field.astype(jnp.bfloat16).astype(F32)
    both = jnp.concatenate([high, field - high], 1)
    if rows:
        both = jnp.concatenate(
            [jnp.broadcast_to(both[n : n + 1, :], (rows, 2 * LANES)) for n in range(field.shape[0])], 0
        )
    both = both.astype(jnp.bfloat16)
    return lax.dot_general(
        matrix, both, (((1,), (1,)), ((), ())), preferred_element_type=F32
    )


def y_factor_kernel(c_ref, after, w_ref, i_ref, p_ref, inner, outer, view, to_y, to_x, unit_low, unit_high, c_s, q_s, r_s):
    chunks, sheets, rows, _ = c_ref.shape
    each = LANES // rows
    pairs = sheets // each
    x_steps = rows // SUBLANES
    steps = LANES // SUBLANES
    to_y[...] = turn_matrix(to_y.shape, True, steps)
    to_x[...] = turn_matrix(to_x.shape, False, x_steps)
    for m in range(pairs):
        for y in range(chunks):
            block = jnp.concatenate(
                [
                    c_ref[y, m * each + i, pl.ds(k, SUBLANES, stride=x_steps), :]
                    for i in range(each)
                    for k in range(x_steps)
                ],
                0,
            )
            c_s[m, part_of(y), :] = block.T

    members = [(y, m) for y in range(chunks) for m in range(pairs)]
    lines = len(members)

    def cond(k):
        return jnp.stack([c_s[m, pl.ds(y * LANES + k, SUBLANES, stride=steps), :] for y, m in members], 0)

    def keep(k, w, inv, p):
        w_ref[k] = w
        i_ref[k] = inv
        p_ref[k] = p

    block = factor(cond, steps, keep)
    for n, q in enumerate(COEFS):
        for i in range(lines):
            q_s[n, i * SUBLANES : (i + 1) * SUBLANES, :] = block[q][i]
    segments = [
        {q: q_s[n, pl.ds(s, lines, stride=SUBLANES), :] for n, q in enumerate(COEFS)}
        for s in range(SUBLANES)
    ]
    whole, levels = tree(segments, join_coefs)
    for (offset, _), level in zip(node_offsets(SUBLANES), levels):
        for n, values in enumerate(level):
            for i in range(3):
                inner[offset + n, i] = values[i]
    for n, q in enumerate(COEFS):
        r_s[n] = whole[q]
    parts = [
        {q: r_s[n, y * pairs : (y + 1) * pairs, :] for n, q in enumerate(COEFS)} for y in range(chunks)
    ]
    whole, levels = tree(parts, join_coefs)
    for (offset, _), level in zip(node_offsets(chunks), levels):
        for n, values in enumerate(level):
            for i in range(3):
                outer[offset + n, i] = values[i]
    for n, q in enumerate(COEFS):
        view[n] = whole[q]

    one = jnp.ones((pairs, LANES), F32)
    for n, (low, high, field) in enumerate(((one, 0.0 * one, unit_low), (0.0 * one, one, unit_high))):
        for y, pair in enumerate(tree_ends(chunks, outer, nothing, low, high)):
            for i in range(2):
                r_s[2 * n + i, y * pairs : (y + 1) * pairs, :] = pair[i]
        for s, pair in enumerate(tree_ends(SUBLANES, inner, nothing, r_s[2 * n], r_s[2 * n + 1])):
            for i in range(2):
                q_s[2 * n + i, pl.ds(s, lines, stride=SUBLANES), :] = pair[i]
        low, value = (
            jnp.stack(
                [q_s[2 * n + i, j * SUBLANES : (j + 1) * SUBLANES, :] for j in range(lines)], 0
            )
            for i in range(2)
        )
        for k in range(steps - 1, -1, -1):
            value = w_ref[k] * value + p_ref[k] * low
            for j, (y, m) in enumerate(members):
                field[y, k * SUBLANES : (k + 1) * SUBLANES, part_of(m)] = value[j]


def y_factor(c, after):
    chunks, sheets, rows, _ = c.shape
    pairs = sheets * rows // LANES
    lines = chunks * pairs
    stored = shape_of(LANES // SUBLANES, lines, SUBLANES, LANES)
    matrix = jax.ShapeDtypeStruct((LANES, 2 * LANES), jnp.bfloat16)
    return pl.pallas_call(
        y_factor_kernel,
        in_specs=[IN_VMEM, ANYWHERE],
        out_shape=[
            stored,
            stored,
            stored,
            shape_of(SUBLANES - 1, 3, lines, LANES),
            shape_of(chunks - 1, 3, pairs, LANES),
            shape_of(len(COEFS), pairs, LANES),
            matrix,
            matrix,
            shape_of(chunks, LANES, pairs * LANES),
            shape_of(chunks, LANES, pairs * LANES),
        ],
        scratch_shapes=[
            pltpu.VMEM((pairs, chunks * LANES, LANES), F32),
            pltpu.VMEM((len(COEFS), lines * SUBLANES, LANES), F32),
            pltpu.VMEM((len(COEFS), lines, LANES), F32),
        ],
        compiler_params=params(),
        cost_estimate=pl.CostEstimate(flops=20 * c.size, bytes_accessed=16 * c.size, transcendentals=0),
    )(c, after)


def z_factor_kernel(c_ref, after, w_ref, i_ref):
    sheets = c_ref.shape[1]
    ground = 1.0
    for z in range(sheets - 1):
        face = c_ref[:, z] + c_ref[:, z + 1]
        inv = inverse(ground + face)
        w = face * inv
        i_ref[z] = inv
        w_ref[z] = w
        ground = 1.0 + w * ground
    i_ref[sheets - 1] = inverse(ground)


def z_factor(c, after):
    chunks, sheets, rows, _ = c.shape
    return pl.pallas_call(
        z_factor_kernel,
        in_specs=[IN_VMEM, ANYWHERE],
        out_shape=[
            shape_of(sheets - 1, chunks, rows, LANES),
            shape_of(sheets, chunks, rows, LANES),
        ],
        compiler_params=params(),
        cost_estimate=pl.CostEstimate(flops=10 * c.size, bytes_accessed=12 * c.size, transcendentals=0),
    )(c, after)


def join_tree(items, links, own):
    for offset, count in node_offsets(len(items)):
        joined = []
        for n in range(count):
            tie = tuple(links[offset + n, i] for i in range(3))
            both, flux = join_targets(items[2 * n], items[2 * n + 1], tie)
            own[offset + n] = flux
            joined.append(both)
        items = joined
    return items[0]


def tree_ends(leaves, links, own, low, high):
    levels = [
        [(own(offset + n), links[offset + n, 1], links[offset + n, 2]) for n in range(count)]
        for offset, count in node_offsets(leaves)
    ]
    return descend(levels, low, high)


def nothing(node):
    return 0.0


def y_prepare_kernel(stages, *refs):
    ties = refs[: stages - 1]
    xw, xh, xm, xp, x_links, x_own, t_ref, to_y, y_low, y_high = refs[stages - 1 : stages + 9]
    base, response, to_first, to_last, fixed, f_s, g_s = refs[stages + 9 :]
    x_steps, lines = xw.shape[:2]
    chunks = base.shape[0]
    sheets = lines // chunks
    rows = x_steps * SUBLANES

    ends, units = block_ends("gx", stages, ties)
    for n, (own, (low, high)) in enumerate(((lambda i: x_own[i], ends), (nothing, units))):
        for s, pair in enumerate(tree_ends(SUBLANES, x_links, own, low, high)):
            for i in range(2):
                f_s[n, i, pl.ds(s, lines, stride=SUBLANES), :] = pair[i]
    first = 0
    for n, members in enumerate(line_groups(chunks, sheets)):
        at = slice(first, first + len(members))
        h_ref_of, h_at = (xh, at) if n == 0 else (xm, slice(first - 2 * sheets, at.stop - 2 * sheets))
        (low, value), (unit_low, unit) = (
            [
                jnp.stack(
                    [f_s[q, i, j * SUBLANES : (j + 1) * SUBLANES, :] for j in range(at.start, at.stop)], 0
                )
                for i in range(2)
            ]
            for q in range(2)
        )
        for k in range(x_steps - 1, -1, -1):
            w, p = xw[k, at], xp[k, at]
            value = w * value + (h_ref_of[k, h_at] + p * low)
            unit = w * unit + p * unit_low
            field = value - t_ref[k, at]
            for j, (y, z) in enumerate(members):
                place = z * rows + k * SUBLANES
                g_s[0, y, place : place + SUBLANES, :] = field[j]
                g_s[1, y, place : place + SUBLANES, :] = unit[j]
        first = at.stop

    totals = [None, None]
    for y in range(chunks):
        field = turned(to_y[...], g_s[0, y])
        answer = turned(to_y[...], g_s[1, y])
        base[y] = field
        response[y] = answer
        for i, (unit, weight) in enumerate(((y_low, to_first), (y_high, to_last))):
            weight[y] = unit[y] * answer
            part = unit[y] * field
            totals[i] = part if y == 0 else totals[i] + part
    for i in range(2):
        put_sums(fixed.at[i], totals[i])


def put_sums(out, field):
    total = jnp.sum(field, 0, keepdims=True)
    for m in range(out.shape[0]):
        out[m : m + 1, :] = total[:, part_of(m)]


def y_prepare(ties, xw, xh, xm, xp, x_links, x_own, t, to_y, unit_low, unit_high):
    chunks = unit_low.shape[0]
    x_steps, lines = xw.shape[:2]
    width = lines // chunks * x_steps * SUBLANES
    field = shape_of(chunks, LANES, width)
    return pl.pallas_call(
        functools.partial(y_prepare_kernel, len(ties) + 1),
        out_shape=[field] * 4 + [shape_of(2, width // LANES, LANES)],
        scratch_shapes=[
            pltpu.VMEM((2, 2, lines * SUBLANES, LANES), F32),
            pltpu.VMEM((2, chunks, width, LANES), F32),
        ],
        compiler_params=params(),
        cost_estimate=pl.CostEstimate(flops=8 * t.size, bytes_accessed=16 * t.size, transcendentals=0),
    )(*ties, xw, xh, xm, xp, x_links, x_own, t, to_y, unit_low, unit_high)


def y_target_kernel(stages, own, got, to_first, to_last, fixed, view, to_y, spread, send, r_s):
    chunks, _, width = to_first.shape
    sheets = own.shape[1] // chunks
    rows = width // sheets

    flux = top_flux("gx", stages, own, got)
    line_of = {member: n for n, member in enumerate(sum(line_groups(chunks, sheets), []))}
    totals = [None, None]
    for y in range(chunks):
        own_flux = jnp.concatenate([flux[line_of[y, z] : line_of[y, z] + 1, :] for z in range(sheets)], 0)
        wide = turned(to_y[...], own_flux, rows)
        spread[y] = wide
        for i, weight in enumerate((to_first, to_last)):
            part = weight[y] * wide
            totals[i] = part if y == 0 else totals[i] + part
    for n, q in enumerate(COEFS):
        send[q] = view[n]
    for i, q in enumerate((FIRST, LAST)):
        put_sums(r_s.at[i], totals[i])
        send[q] = fixed[i] + r_s[i]


def y_target(own, got, to_first, to_last, fixed, view, to_y):
    pairs = view.shape[1]
    return pl.pallas_call(
        functools.partial(y_target_kernel, stages_of("gx")),
        out_shape=[shape_of(*to_first.shape), shape_of(7, pairs, LANES)],
        scratch_shapes=[pltpu.VMEM((2, pairs, LANES), F32)],
        compiler_params=params(),
    )(own, got, to_first, to_last, fixed, view, to_y)


def y_eliminate_kernel(base, response, spread, yw, yi, yp, inner, outer, after, *refs):
    h_ref, inner_own, outer_own, q_s, r_s = refs
    chunks, _, width = base.shape
    pairs = width // LANES
    steps = yw.shape[0]
    members = [(y, m) for y in range(chunks) for m in range(pairs)]

    def target(k):
        at = slice(k * SUBLANES, (k + 1) * SUBLANES)
        return jnp.stack(
            [
                base[y, at, part_of(m)] + response[y, at, part_of(m)] * spread[y, at, part_of(m)]
                for y, m in members
            ],
            0,
        )

    def keep(k, h):
        h_ref[k] = h

    ends = eliminate(target, steps, lambda k: yw[k], lambda k: yi[k], lambda k: yp[k], keep)
    for q in range(2):
        for i in range(len(members)):
            q_s[q, i * SUBLANES : (i + 1) * SUBLANES, :] = ends[q][i]
    items = [
        tuple(q_s[q, pl.ds(s, len(members), stride=SUBLANES), :] for q in range(2))
        for s in range(SUBLANES)
    ]
    r_s[0], r_s[1] = join_tree(items, inner, inner_own)
    items = [tuple(r_s[q, y * pairs : (y + 1) * pairs, :] for q in range(2)) for y in range(chunks)]
    join_tree(items, outer, outer_own)


def y_eliminate(base, response, spread, yw, yi, yp, inner, outer, after):
    y_lines = yw.shape[1]
    pairs = outer.shape[2]
    chunks = y_lines // pairs
    return pl.pallas_call(
        y_eliminate_kernel,
        in_specs=[IN_VMEM] * 8 + [ANYWHERE],
        out_shape=[
            shape_of(*yw.shape),
            shape_of(SUBLANES - 1, y_lines, LANES),
            shape_of(chunks - 1, pairs, LANES),
        ],
        scratch_shapes=[
            pltpu.VMEM((2, y_lines * SUBLANES, LANES), F32),
            pltpu.VMEM((2, y_lines, LANES), F32),
        ],
        compiler_params=params(),
        cost_estimate=pl.CostEstimate(flops=8 * base.size, bytes_accessed=16 * base.size, transcendentals=0),
    )(base, response, spread, yw, yi, yp, inner, outer, after)


def z_solve(zw, zi, field, at, keep):
    sheets = zi.shape[0]
    rhs, kept = None, []
    for z in range(sheets):
        rhs = field(z) if z == 0 else field(z) + zw[(z - 1, *at)] * rhs
        kept.append(rhs * zi[(z, *at)])
    value = kept[-1]
    keep(sheets - 1, value)
    for z in range(sheets - 2, -1, -1):
        value = zw[(z, *at)] * value + kept[z]
        keep(z, value)


def finish_prepare_kernel(stages, *refs):
    ties = refs[: stages - 1]
    yw, yh, yp, inner, inner_own, outer, outer_own, zw, zi, t_ref, to_x = refs[stages - 1 : stages + 10]
    base, response, r_s, e_s, u_s = refs[stages + 10 :]
    chunks, sheets, rows, _ = base.shape
    each = LANES // rows
    pairs = sheets // each
    steps = yw.shape[0]
    lines = chunks * pairs

    ends, units = block_ends("gy", stages, ties)
    both = (
        (lambda i: outer_own[i], lambda i: inner_own[i], ends),
        (nothing, nothing, units),
    )
    for n, (upper, lower, (low, high)) in enumerate(both):
        for y, pair in enumerate(tree_ends(chunks, outer, upper, low, high)):
            for i in range(2):
                r_s[n, i, y * pairs : (y + 1) * pairs, :] = pair[i]
        for s, pair in enumerate(tree_ends(SUBLANES, inner, lower, r_s[n, 0], r_s[n, 1])):
            for i in range(2):
                e_s[n, i, pl.ds(s, lines, stride=SUBLANES), :] = pair[i]
    (low, value), (unit_low, unit) = (
        [
            jnp.stack([e_s[q, i, n * SUBLANES : (n + 1) * SUBLANES, :] for n in range(lines)], 0)
            for i in range(2)
        ]
        for q in range(2)
    )
    for k in range(steps - 1, -1, -1):
        w, p = yw[k], yp[k]
        value = w * value + (yh[k] + p * low)
        unit = w * unit + p * unit_low
        for y in range(chunks):
            for m in range(pairs):
                place = pl.ds(y * LANES + k, SUBLANES, stride=steps)
                u_s[0, m, place, :] = value[y * pairs + m]
                u_s[1, m, place, :] = unit[y * pairs + m]

    for y in range(chunks):
        part = part_of(y)
        fields = [turned(to_x[...], u_s[0, m, part, :]) for m in range(pairs)]

        def field(z):
            at = z % each * rows
            return fields[z // each][at : at + rows, :]

        def keep(z, value):
            base[y, z] = t_ref[z, :, part] + value

        z_solve(zw, zi, field, (y,), keep)
        for m in range(pairs):
            units = turned(to_x[...], u_s[1, m, part, :])
            for i in range(each):
                response[y, m * each + i] = units[i * rows : (i + 1) * rows, :]


def finish_prepare(ties, yw, yh, yp, inner, inner_own, outer, outer_own, zw, zi, t, to_x):
    sheets, rows, columns = t.shape
    chunks = columns // LANES
    pairs = sheets * rows // LANES
    lines = chunks * pairs
    field = shape_of(chunks, sheets, rows, LANES)
    return pl.pallas_call(
        functools.partial(finish_prepare_kernel, len(ties) + 1),
        out_shape=[field, field],
        scratch_shapes=[
            pltpu.VMEM((2, 2, lines, LANES), F32),
            pltpu.VMEM((2, 2, lines * SUBLANES, LANES), F32),
            pltpu.VMEM((2, pairs, columns, LANES), F32),
        ],
        compiler_params=params(),
        cost_estimate=pl.CostEstimate(flops=12 * t.size, bytes_accessed=20 * t.size, transcendentals=0),
    )(*ties, yw, yh, yp, inner, inner_own, outer, outer_own, zw, zi, t, to_x)


def finish_kernel(stages, own, got, base, response, zw, zi, to_x, out, o_s, sems):
    chunks, sheets, rows, _ = base.shape
    each = LANES // rows
    pairs = sheets // each
    flux = top_flux("gy", stages, own, got)
    spread = [
        turned(to_x[...], flux[m : m + 1, :], LANES) for m in range(pairs)
    ]
    started = []
    block = rows // OUT_COPIES
    for n in range(OUT_COPIES):
        strip = slice(n * block, (n + 1) * block)
        for y in range(chunks):

            def field(z):
                at = z % each * rows + strip.start
                return response[y, z, strip, :] * spread[z // each][at : at + block, :]

            def keep(z, value):
                o_s[z, strip, part_of(y)] = base[y, z, strip, :] + value

            z_solve(zw, zi, field, (y, strip), keep)
        at = pl.ds(strip.start, block)
        copy = pltpu.make_async_copy(o_s.at[:, at, :], out.at[:, at, :], sems.at[n])
        copy.start()
        started.append(copy)
    for copy in started:
        copy.wait()


def finish(own, got, base, response, zw, zi, to_x):
    chunks, sheets, rows, _ = base.shape
    shape = (sheets, rows, chunks * LANES)
    return pl.pallas_call(
        functools.partial(finish_kernel, stages_of("gy")),
        out_shape=shape_of(*shape),
        out_specs=ANYWHERE,
        scratch_shapes=[pltpu.VMEM(shape, F32), pltpu.SemaphoreType.DMA((OUT_COPIES,))],
        compiler_params=params(),
    )(own, got, base, response, zw, zi, to_x)


def per_device(temperature, base, locations, energy):
    columns = temperature.shape[2]
    gy = lax.axis_size("gy")
    t, b, packed = load(temperature, base)
    near = swap(packed, "gy", 1)
    far = lax.ppermute(packed, "gy", [(i, ((i + 1) % gy ^ 1) - 1 if i else gy - 1) for i in range(gy)])
    c, total, xw, xi, xp, x_links, x_view, xm, ends, t_steps, swapped = x_factor(
        locations[None], energy[None], t, b, columns * gy, packed
    )
    xh, x_own, view = x_target(swapped, total, near, far, xw, xi, xp, x_links, x_view, ends)
    yw, yi, yp, inner, outer, y_view, to_y, to_x, unit_low, unit_high = y_factor(c, x_view)
    zw, zi = z_factor(c, view)
    own, got, ties = gather_line(view, "gx", 2, (y_view, zw))
    base, response, to_first, to_last, fixed = y_prepare(
        ties, xw, xh, xm, xp, x_links, x_own, t_steps, to_y, unit_low, unit_high
    )
    spread, view = y_target(own, got, to_first, to_last, fixed, y_view, to_y)
    yh, inner_own, outer_own = y_eliminate(base, response, spread, yw, yi, yp, inner, outer, view)
    own, got, ties = gather_line(view, "gy", meanwhile=(yh,), cross=True)
    base, response = finish_prepare(
        ties, yw, yh, yp, inner, inner_own, outer, outer_own, zw, zi, t, to_x
    )
    return finish(own, got, base, response, zw, zi, to_x)


def solution(mesh):
    in_specs = (P(None, "gx", "gy"), P(None, "gx", "gy"), P(), P())
    out_specs = P(None, "gx", "gy")
    return jax.shard_map(
        per_device, mesh=mesh, in_specs=in_specs, out_specs=out_specs, check_vma=False
    )
```

```python
import functools

import jax
import jax.numpy as jnp
from jax import lax
from jax.experimental import pallas as pl
from jax.experimental.pallas import tpu as pltpu
from jax.sharding import PartitionSpec as P

RATE = 2000.0
THERMAL_GROWTH = 0.8
LANES = 128
SUBLANES = 8
F32 = jnp.float32
MIB = 1024 * 1024
OUT_COPIES = 4
ANYWHERE = pl.BlockSpec(memory_space=pl.ANY)
IN_HBM = pl.BlockSpec(memory_space=pltpu.HBM)
IN_VMEM = pl.BlockSpec(memory_space=pltpu.VMEM)

R00, R0L, RLL, FIRST, LAST, C0, CL = range(7)
COEFS = (R00, R0L, RLL, C0, CL)


def params(limit=40):
    return pltpu.CompilerParams(vmem_limit_bytes=limit * MIB)


def shape_of(*sizes):
    return jax.ShapeDtypeStruct(sizes, F32)


def half_conduct(base, temperature):
    return base * (0.5 * RATE + (0.5 * RATE * THERMAL_GROWTH) * temperature)


def inverse(x):
    guess = pl.reciprocal(x, approx=True)
    return guess * (2.0 - x * guess)


def join_coefs(a, b):
    face = a[CL] + b[C0]
    inv = face * inverse(1.0 + face * (a[RLL] + b[R00]))
    left = a[R0L] * inv
    right = b[R0L] * inv
    joined = {
        R00: a[R00] - left * a[R0L],
        R0L: left * b[R0L],
        RLL: b[RLL] - right * b[R0L],
        C0: a[C0],
        CL: b[CL],
    }
    return joined, (inv, right, left)


def join_targets(a, b, links):
    inv, right, left = links
    jump = b[0] - a[1]
    return (a[0] + left * jump, b[1] - right * jump), jump * inv


def between(own, right, left, low, high):
    return own + right * high - left * low


def tree(items, join):
    levels = []
    while len(items) > 1:
        pairs = [join(items[i], items[i + 1]) for i in range(0, len(items), 2)]
        items = [p[0] for p in pairs]
        levels.append([p[1] for p in pairs])
    return items[0], levels


def descend(levels, low, high):
    ends = [(low, high)]
    for level in reversed(levels):
        below = []
        for (lo, hi), (own, right, left) in zip(ends, level):
            flux = between(own, right, left, lo, hi)
            below += [(lo, flux), (-flux, hi)]
        ends = below
    return ends


def node_offsets(leaves):
    offsets, at, count = [], 0, leaves // 2
    while count:
        offsets.append((at, count))
        at += count
        count //= 2
    return offsets


def factor(cond, steps, keep):
    here = cond(0)
    c_first = here
    one = jnp.ones_like(here)
    ground, path, first_first = one, one, None
    for k in range(steps - 1):
        following = cond(k + 1)
        face = here + following
        inv = inverse(ground + face)
        w = face * inv
        p = path * inv
        keep(k, w, inv, p)
        step = path * p
        first_first = step if first_first is None else first_first + step
        path = path * w
        ground = 1.0 + w * ground
        here = following
    inv = inverse(ground)
    p = path * inv
    keep(steps - 1, inv, inv, p)
    return {R00: first_first + path * p, R0L: p, RLL: inv, C0: c_first, CL: here}


def eliminate(target, steps, w, inv, p, keep):
    rhs = target(0)
    first = None
    for k in range(steps):
        h = rhs * inv(k)
        keep(k, h)
        step = rhs * p(k)
        first = step if first is None else first + step
        if k < steps - 1:
            rhs = target(k + 1) + w(k) * rhs
    return first, h


def is_odd(axis):
    return lax.axis_index(axis) % 2 == 1


def fold(cells, used):
    steps = cells.shape[0] // SUBLANES
    total = cells[pl.ds(0, SUBLANES, stride=steps), :]
    lane = lax.broadcasted_iota(jnp.int32, total.shape, 1)
    for k in range(1, steps):
        part = pltpu.roll(cells[pl.ds(k, SUBLANES, stride=steps), :], k * used, 1)
        total = jnp.where(lane // used == k, part, total)
    return total


def load_kernel(t_hbm, b_hbm, loc_hbm, energy_hbm, t_out, b_out, loc, energy, packed, cells, sems):
    sheets, rows, columns = t_hbm.shape
    parts = [(0, LANES), (columns - LANES, LANES), (LANES, columns - 2 * LANES)]
    copies = []
    for n, (start, size) in enumerate(parts):
        part = pl.ds(start, size)
        for i, (src, dst) in enumerate(((t_hbm, t_out), (b_hbm, b_out))):
            copies.append(
                pltpu.make_async_copy(src.at[:, :, part], dst.at[:, :, part], sems.at[i, n])
            )
    copies.append(pltpu.make_async_copy(loc_hbm, loc, sems.at[2, 0]))
    copies.append(pltpu.make_async_copy(energy_hbm, energy, sems.at[2, 1]))
    for copy in copies:
        copy.start()
    lane = lax.broadcasted_iota(jnp.int32, (rows, LANES), 1)
    edge_t = jnp.zeros((rows, LANES), F32)
    edge_c = edge_t
    for side, source in enumerate((0, LANES - 1)):
        for copy in copies[2 * side : 2 * side + 2]:
            copy.wait()
        part = slice(parts[side][0], parts[side][0] + LANES)
        for z in range(sheets):
            t = t_out[z, :, part]
            c = half_conduct(b_out[z, :, part], t)
            place = lane == sheets * side + z
            edge_t = jnp.where(place, t[:, source : source + 1], edge_t)
            edge_c = jnp.where(place, c[:, source : source + 1], edge_c)
    cells[0], cells[1] = edge_t, edge_c
    for i in range(2):
        packed[i * SUBLANES : (i + 1) * SUBLANES, :] = fold(cells.at[i], 2 * sheets)
    for copy in copies[4:]:
        copy.wait()


def load(temperature, base, locations, energy):
    sheets, rows, columns = temperature.shape
    assert rows // SUBLANES * 2 * sheets <= LANES and columns > 2 * LANES
    operands = (temperature, base, locations, energy)
    return pl.pallas_call(
        load_kernel,
        in_specs=[IN_HBM] * 4,
        out_shape=[pltpu.VMEM(v.shape, v.dtype) for v in operands]
        + [pltpu.VMEM((2 * SUBLANES, LANES), F32)],
        scratch_shapes=[pltpu.VMEM((2, rows, LANES), F32), pltpu.SemaphoreType.DMA((3, 3))],
        compiler_params=params(),
    )(*[pltpu.with_memory_space_constraint(v, pltpu.HBM) for v in operands])


def source_plane(loc, energy, rows, columns, plate):
    place = loc[...]
    count = place.shape[1]
    local_x = place // plate - lax.axis_index("gx") * rows
    local_y = place % plate - lax.axis_index("gy") * columns
    in_x = lax.broadcasted_iota(jnp.int32, (rows, count), 0) == local_x
    in_y = lax.broadcasted_iota(jnp.int32, (columns, count), 0) == local_y
    by_y = jnp.where(in_y, 1.0, 0.0).astype(jnp.bfloat16)
    left = energy[...]
    plane = None
    for _ in range(3):
        part = left.astype(jnp.bfloat16).astype(F32)
        left = left - part
        term = lax.dot_general(
            jnp.where(in_x, part, 0.0).astype(jnp.bfloat16),
            by_y,
            (((1,), (1,)), ((), ())),
            preferred_element_type=F32,
        )
        plane = term if plane is None else plane + term
    return plane


def part_of(y):
    return slice(y * LANES, (y + 1) * LANES)


def line_groups(chunks, sheets):
    order = [0, chunks - 1] + list(range(1, chunks - 1))
    return [[(y, z) for y in order[i : i + 2] for z in range(sheets)] for i in range(0, chunks, 2)]


def x_eliminate(cells, members, first_line, w_ref, i_ref, p_ref, h_ref, h_line, q_s):
    steps = w_ref.shape[0]
    at = slice(first_line, first_line + len(members))
    kept_at = slice(h_line, h_line + len(members))

    def target(k):
        return jnp.stack([cells(y, z, k) for y, z in members], 0)

    def keep(k, h):
        h_ref[k, kept_at] = h

    ends = eliminate(
        target, steps, lambda k: w_ref[k, at], lambda k: i_ref[k, at], lambda k: p_ref[k, at], keep
    )
    for q in range(2):
        for i in range(len(members)):
            first = (first_line + i) * SUBLANES
            q_s[q, first : first + SUBLANES, :] = ends[q][i]


def x_factor_kernel(plate, loc, energy, t_ref, b_ref, own_cells, *refs):
    c_ref, total_ref, w_ref, i_ref, p_ref, links, view, h_ref, ends_ref, t_out, swapped, q_s, t_s = refs
    chunks, sheets, rows, _ = c_ref.shape
    lines = chunks * sheets
    steps = rows // SUBLANES
    plane = source_plane(loc, energy, rows, chunks * LANES, plate)
    mine = own_cells[...]
    in_low = lax.broadcasted_iota(jnp.int32, mine.shape, 1) % (2 * sheets) < sheets
    swapped[...] = jnp.where(
        in_low, pltpu.roll(mine, LANES - sheets, 1), pltpu.roll(mine, sheets, 1)
    )

    lane = lax.broadcasted_iota(jnp.int32, (SUBLANES, LANES), 1)
    is_first, is_last = lane == 0, lane == LANES - 1
    for r in range(steps):
        at = slice(r * SUBLANES, (r + 1) * SUBLANES)
        before_t, before_c = None, None
        for z in range(sheets):
            ts = [t_ref[z, at, part_of(y)] for y in range(chunks)]
            cs = [half_conduct(b_ref[z, at, part_of(y)], ts[y]) for y in range(chunks)]
            t_turned = [pltpu.roll(v, LANES - 1, 1) for v in ts]
            c_turned = [pltpu.roll(v, LANES - 1, 1) for v in cs]
            flux = []
            for y in range(chunks):
                if y < chunks - 1:
                    t_next = jnp.where(is_last, t_turned[y + 1], t_turned[y])
                    c_next = jnp.where(is_last, c_turned[y + 1], c_turned[y])
                    flux.append((cs[y] + c_next) * (t_next - ts[y]))
                else:
                    inside = (cs[y] + c_turned[y]) * (t_turned[y] - ts[y])
                    flux.append(jnp.where(is_last, 0.0, inside))
            turned = [pltpu.roll(v, 1, 1) for v in flux]
            for y in range(chunks):
                from_low = jnp.where(is_first, turned[y - 1] if y else 0.0, turned[y])
                total = ts[y] + (flux[y] - from_low)
                if z == 0:
                    total = total + plane[at, part_of(y)]
                else:
                    across = (before_c[y] + cs[y]) * (ts[y] - before_t[y])
                    total = total - across
                    total_ref[y, z - 1, at, :] += across
                total_ref[y, z, at, :] = total
                c_ref[y, z, at, :] = cs[y]
                t_s[y, z, at, :] = ts[y]
            before_t, before_c = ts, cs

    at = 0
    for n, members in enumerate(line_groups(chunks, sheets)):

        def cond(k):
            return jnp.stack([c_ref[y, z, pl.ds(k, SUBLANES, stride=steps), :] for y, z in members], 0)

        def keep(k, w, inv, p):
            w_ref[k, at : at + len(members)] = w
            i_ref[k, at : at + len(members)] = inv
            p_ref[k, at : at + len(members)] = p

        block = factor(cond, steps, keep)
        for i, q in enumerate(COEFS):
            for j in range(len(members)):
                first = (at + j) * SUBLANES
                q_s[i, first : first + SUBLANES, :] = block[q][j]
        if n > 0:
            x_eliminate(
                lambda y, z, k: total_ref[y, z, pl.ds(k, SUBLANES, stride=steps), :],
                members, at, w_ref, i_ref, p_ref, h_ref, at - 2 * sheets, ends_ref,
            )
        for k in range(steps):
            for i, (y, z) in enumerate(members):
                t_out[k, at + i] = t_s[y, z, pl.ds(k, SUBLANES, stride=steps), :]
        at += len(members)

    segments = [
        {q: q_s[n, pl.ds(s, lines, stride=SUBLANES), :] for n, q in enumerate(COEFS)}
        for s in range(SUBLANES)
    ]
    whole, levels = tree(segments, join_coefs)
    for (offset, _), level in zip(node_offsets(SUBLANES), levels):
        for n, values in enumerate(level):
            for i in range(3):
                links[offset + n, i] = values[i]
    for n, q in enumerate(COEFS):
        view[n] = whole[q]


def x_factor(loc, energy, t, b, plate, own_cells):
    sheets, rows, columns = t.shape
    chunks = columns // LANES
    lines = chunks * sheets
    steps = rows // SUBLANES
    field = shape_of(chunks, sheets, rows, LANES)
    stored = shape_of(steps, lines, SUBLANES, LANES)
    return pl.pallas_call(
        functools.partial(x_factor_kernel, plate),
        in_specs=[IN_VMEM] * 5,
        out_shape=[
            field,
            field,
            stored,
            stored,
            stored,
            shape_of(SUBLANES - 1, 3, lines, LANES),
            shape_of(len(COEFS), lines, LANES),
            shape_of(steps, max(1, lines - 2 * sheets), SUBLANES, LANES),
            shape_of(2, lines * SUBLANES, LANES),
            stored,
            shape_of(*own_cells.shape),
        ],
        scratch_shapes=[
            pltpu.VMEM((len(COEFS), lines * SUBLANES, LANES), F32),
            pltpu.VMEM((chunks, sheets, rows, LANES), F32),
        ],
        compiler_params=params(),
        cost_estimate=pl.CostEstimate(flops=40 * t.size, bytes_accessed=28 * t.size, transcendentals=0),
    )(loc, energy, t, b, own_cells)


def x_target_kernel(own_cells, total_ref, near, far, *refs):
    w_ref, i_ref, p_ref, links, view, ends_ref, h_ref, own, send, q_s = refs
    chunks, sheets, rows, _ = total_ref.shape
    lines = chunks * sheets
    steps = rows // SUBLANES

    place = lax.axis_index("gy")
    inner = (place > 0) & (place < lax.axis_size("gy") - 1)
    lane = lax.broadcasted_iota(jnp.int32, (SUBLANES, LANES), 1)
    side = 2 * sheets
    is_near = (lane % side >= sheets).astype(jnp.int32) == place % 2
    t, c = (
        jnp.where(is_near, near[at, :], jnp.where(inner, far[at, :], 0.0))
        for at in (slice(0, SUBLANES), slice(SUBLANES, 2 * SUBLANES))
    )
    face = jnp.where(c > 0.0, own_cells[SUBLANES:, :] + c, 0.0)
    flux = face * (t - own_cells[:SUBLANES, :])

    def cells(y, z, k):
        at = k * side + (sheets + z if y == 0 else z)
        edge = 0 if y == 0 else LANES - 1
        inflow = jnp.where(lane == edge, flux[:, at : at + 1], 0.0)
        return total_ref[y, z, pl.ds(k, SUBLANES, stride=steps), :] + inflow

    members = line_groups(chunks, sheets)[0]
    x_eliminate(cells, members, 0, w_ref, i_ref, p_ref, h_ref, 0, q_s)
    split = len(members)
    items = [
        tuple(
            jnp.concatenate(
                [
                    q_s[q, pl.ds(s, split, stride=SUBLANES), :],
                    ends_ref[q, pl.ds(split * SUBLANES + s, lines - split, stride=SUBLANES), :],
                ],
                0,
            )
            for q in range(2)
        )
        for s in range(SUBLANES)
    ]
    for offset, count in node_offsets(SUBLANES):
        joined = []
        for n in range(count):
            ties = tuple(links[offset + n, i] for i in range(3))
            both, flux = join_targets(items[2 * n], items[2 * n + 1], ties)
            own[offset + n] = flux
            joined.append(both)
        items = joined
    for n, q in enumerate(COEFS):
        send[q] = view[n]
    send[FIRST], send[LAST] = items[0]


def x_target(own_cells, total, near, far, w, inv, p, links, view, ends):
    chunks, sheets, rows, _ = total.shape
    lines = chunks * sheets
    steps = rows // SUBLANES
    return pl.pallas_call(
        x_target_kernel,
        out_shape=[
            shape_of(steps, 2 * sheets, SUBLANES, LANES),
            shape_of(SUBLANES - 1, lines, LANES),
            shape_of(7, lines, LANES),
        ],
        scratch_shapes=[
            pltpu.VMEM((2, 2 * sheets * SUBLANES, LANES), F32),
        ],
        compiler_params=params(),
    )(own_cells, total, near, far, w, inv, p, links, view, ends)


def stages_of(axis):
    return lax.axis_size(axis).bit_length() - 1


def swap(value, axis, flip):
    count = lax.axis_size(axis)
    return lax.ppermute(value, axis, [(i, i ^ flip) for i in range(count)])


def on_right(axis, stage):
    return (lax.axis_index(axis) >> stage) % 2 == 1


def toward(right, block):
    return (
        jnp.where(right, block[R00], block[RLL]),
        jnp.where(right, block[FIRST], block[LAST]),
        jnp.where(right, block[C0], block[CL]),
    )


def join(a, b):
    joined, ties = join_coefs(a, b)
    (joined[FIRST], joined[LAST]), flux = join_targets((a[FIRST], a[LAST]), (b[FIRST], b[LAST]), ties)
    return joined, (flux, ties[1], ties[2])


def ordered(right, own, other):
    first = [jnp.where(right, theirs, mine) for mine, theirs in zip(own, other)]
    second = [jnp.where(right, mine, theirs) for mine, theirs in zip(own, other)]
    return first, second


def join_kernel(axis, stage, width, last, *refs):
    count = 1 << width
    blocks = [[refs[i][q] for q in range(7)] for i in range(count)]
    send = refs[-1 - width]
    links = refs[-width:]
    for bit in range(width):
        right = on_right(axis, stage + bit)
        for i in range(count):
            if not i >> bit & 1:
                j = i | 1 << bit
                blocks[i], blocks[j] = ordered(right, blocks[i], blocks[j])
    for bit in range(width):
        pairs = [join(blocks[i], blocks[i + 1]) for i in range(0, len(blocks), 2)]
        blocks = [p[0] for p in pairs]
        ties = [p[1] for p in pairs]
        for upper in range(bit + 1, width):
            right = on_right(axis, stage + upper)
            ties = [
                tuple(jnp.where(right, v, u) for u, v in zip(ties[i], ties[i + 1]))
                for i in range(0, len(ties), 2)
            ]
        for i in range(3):
            links[bit][i] = ties[0][i]
    (whole,) = blocks
    if last:
        for n, value in enumerate(toward(on_right(axis, stage + width), whole)):
            send[n] = value
    else:
        for q in range(7):
            send[q] = whole[q]


def join_stage(own, got, axis, stage, width, last, after):
    lines = own.shape[1]
    return pl.pallas_call(
        functools.partial(join_kernel, axis, stage, width, last),
        in_specs=[IN_VMEM] * (1 + len(got)) + [ANYWHERE] * len(after),
        out_shape=[shape_of(3 if last else 7, lines, LANES)] + [shape_of(3, lines, LANES)] * width,
        compiler_params=params(),
    )(own, *got, *after)


def gather_line(view, axis, widest=1, meanwhile=(), cross=False):
    stages = stages_of(axis)
    links, stage = [], 0
    while stage < stages - 1:
        width = min(widest, stages - 1 - stage)
        got = [swap(view, axis, flip << stage) for flip in range(1, 1 << width)]
        last = stage + width == stages - 1
        view, *ties = join_stage(view, got, axis, stage, width, last, meanwhile)
        links += ties
        stage += width
        meanwhile = ()
    return view, swap(view, axis, 1 << stage | (cross and stage > 0)), links


def top_flux(axis, stages, own, got):
    right = on_right(axis, stages - 1)
    face = own[2] + got[2]
    jump = jnp.where(right, own[1] - got[1], got[1] - own[1])
    return jump * face * inverse(1.0 + face * (own[0] + got[0]))


def block_ends(axis, stages, links):
    shape = links[0].shape[1:] if links else None
    right = on_right(axis, stages - 1)
    zero = jnp.zeros(shape, F32)
    low, high = zero, zero
    unit_low = zero + jnp.where(right, -1.0, 0.0)
    unit_high = zero + jnp.where(right, 0.0, 1.0)
    for stage in range(stages - 2, -1, -1):
        tie = links[stage]
        right = on_right(axis, stage)
        flux = between(tie[0], tie[1], tie[2], low, high)
        unit = between(0.0, tie[1], tie[2], unit_low, unit_high)
        low, high = jnp.where(right, -flux, low), jnp.where(right, high, flux)
        unit_low, unit_high = jnp.where(right, -unit, unit_low), jnp.where(right, unit_high, unit)
    return (low, high), (unit_low, unit_high)


def natural(index, parts):
    span = SUBLANES * parts
    local = index % span
    return index - local + local % SUBLANES * parts + local // SUBLANES


def turn_matrix(shape, from_natural, parts):
    row = lax.broadcasted_iota(jnp.int32, shape, 0)
    column = lax.broadcasted_iota(jnp.int32, shape, 1) % LANES
    hit = natural(row, parts) == column if from_natural else row == natural(column, parts)
    return jnp.where(hit, 1.0, 0.0).astype(jnp.bfloat16)


def turned(matrix, field, rows=None):
    high = field.astype(jnp.bfloat16).astype(F32)
    both = jnp.concatenate([high, field - high], 1)
    if rows:
        both = jnp.concatenate(
            [jnp.broadcast_to(both[n : n + 1, :], (rows, 2 * LANES)) for n in range(field.shape[0])], 0
        )
    both = both.astype(jnp.bfloat16)
    return lax.dot_general(
        matrix, both, (((1,), (1,)), ((), ())), preferred_element_type=F32
    )


def y_factor_kernel(c_ref, after, w_ref, i_ref, p_ref, inner, outer, view, to_y, to_x, unit_low, unit_high, c_s, q_s, r_s):
    chunks, sheets, rows, _ = c_ref.shape
    each = LANES // rows
    pairs = sheets // each
    x_steps = rows // SUBLANES
    steps = LANES // SUBLANES
    to_y[...] = turn_matrix(to_y.shape, True, steps)
    to_x[...] = turn_matrix(to_x.shape, False, x_steps)
    for m in range(pairs):
        for y in range(chunks):
            block = jnp.concatenate(
                [
                    c_ref[y, m * each + i, pl.ds(k, SUBLANES, stride=x_steps), :]
                    for i in range(each)
                    for k in range(x_steps)
                ],
                0,
            )
            c_s[m, part_of(y), :] = block.T

    members = [(y, m) for y in range(chunks) for m in range(pairs)]
    lines = len(members)

    def cond(k):
        return jnp.stack([c_s[m, pl.ds(y * LANES + k, SUBLANES, stride=steps), :] for y, m in members], 0)

    def keep(k, w, inv, p):
        w_ref[k] = w
        i_ref[k] = inv
        p_ref[k] = p

    block = factor(cond, steps, keep)
    for n, q in enumerate(COEFS):
        for i in range(lines):
            q_s[n, i * SUBLANES : (i + 1) * SUBLANES, :] = block[q][i]
    segments = [
        {q: q_s[n, pl.ds(s, lines, stride=SUBLANES), :] for n, q in enumerate(COEFS)}
        for s in range(SUBLANES)
    ]
    whole, levels = tree(segments, join_coefs)
    for (offset, _), level in zip(node_offsets(SUBLANES), levels):
        for n, values in enumerate(level):
            for i in range(3):
                inner[offset + n, i] = values[i]
    for n, q in enumerate(COEFS):
        r_s[n] = whole[q]
    parts = [
        {q: r_s[n, y * pairs : (y + 1) * pairs, :] for n, q in enumerate(COEFS)} for y in range(chunks)
    ]
    whole, levels = tree(parts, join_coefs)
    for (offset, _), level in zip(node_offsets(chunks), levels):
        for n, values in enumerate(level):
            for i in range(3):
                outer[offset + n, i] = values[i]
    for n, q in enumerate(COEFS):
        view[n] = whole[q]

    one = jnp.ones((pairs, LANES), F32)
    for n, (low, high, field) in enumerate(((one, 0.0 * one, unit_low), (0.0 * one, one, unit_high))):
        for y, pair in enumerate(tree_ends(chunks, outer, nothing, low, high)):
            for i in range(2):
                r_s[2 * n + i, y * pairs : (y + 1) * pairs, :] = pair[i]
        for s, pair in enumerate(tree_ends(SUBLANES, inner, nothing, r_s[2 * n], r_s[2 * n + 1])):
            for i in range(2):
                q_s[2 * n + i, pl.ds(s, lines, stride=SUBLANES), :] = pair[i]
        low, value = (
            jnp.stack(
                [q_s[2 * n + i, j * SUBLANES : (j + 1) * SUBLANES, :] for j in range(lines)], 0
            )
            for i in range(2)
        )
        for k in range(steps - 1, -1, -1):
            value = w_ref[k] * value + p_ref[k] * low
            for j, (y, m) in enumerate(members):
                field[y, k * SUBLANES : (k + 1) * SUBLANES, part_of(m)] = value[j]


def y_factor(c, after):
    chunks, sheets, rows, _ = c.shape
    pairs = sheets * rows // LANES
    lines = chunks * pairs
    stored = shape_of(LANES // SUBLANES, lines, SUBLANES, LANES)
    matrix = jax.ShapeDtypeStruct((LANES, 2 * LANES), jnp.bfloat16)
    return pl.pallas_call(
        y_factor_kernel,
        in_specs=[IN_VMEM, ANYWHERE],
        out_shape=[
            stored,
            stored,
            stored,
            shape_of(SUBLANES - 1, 3, lines, LANES),
            shape_of(chunks - 1, 3, pairs, LANES),
            shape_of(len(COEFS), pairs, LANES),
            matrix,
            matrix,
            shape_of(chunks, LANES, pairs * LANES),
            shape_of(chunks, LANES, pairs * LANES),
        ],
        scratch_shapes=[
            pltpu.VMEM((pairs, chunks * LANES, LANES), F32),
            pltpu.VMEM((len(COEFS), lines * SUBLANES, LANES), F32),
            pltpu.VMEM((len(COEFS), lines, LANES), F32),
        ],
        compiler_params=params(),
        cost_estimate=pl.CostEstimate(flops=20 * c.size, bytes_accessed=16 * c.size, transcendentals=0),
    )(c, after)


def z_factor_kernel(c_ref, after, w_ref, i_ref):
    sheets = c_ref.shape[1]
    ground = 1.0
    for z in range(sheets - 1):
        face = c_ref[:, z] + c_ref[:, z + 1]
        inv = inverse(ground + face)
        w = face * inv
        i_ref[z] = inv
        w_ref[z] = w
        ground = 1.0 + w * ground
    i_ref[sheets - 1] = inverse(ground)


def z_factor(c, after):
    chunks, sheets, rows, _ = c.shape
    return pl.pallas_call(
        z_factor_kernel,
        in_specs=[IN_VMEM, ANYWHERE],
        out_shape=[
            shape_of(sheets - 1, chunks, rows, LANES),
            shape_of(sheets, chunks, rows, LANES),
        ],
        compiler_params=params(),
        cost_estimate=pl.CostEstimate(flops=10 * c.size, bytes_accessed=12 * c.size, transcendentals=0),
    )(c, after)


def join_tree(items, links, own):
    for offset, count in node_offsets(len(items)):
        joined = []
        for n in range(count):
            tie = tuple(links[offset + n, i] for i in range(3))
            both, flux = join_targets(items[2 * n], items[2 * n + 1], tie)
            own[offset + n] = flux
            joined.append(both)
        items = joined
    return items[0]


def tree_ends(leaves, links, own, low, high):
    levels = [
        [(own(offset + n), links[offset + n, 1], links[offset + n, 2]) for n in range(count)]
        for offset, count in node_offsets(leaves)
    ]
    return descend(levels, low, high)


def nothing(node):
    return 0.0


def y_prepare_kernel(stages, *refs):
    ties = refs[: stages - 1]
    xw, xh, xm, xp, x_links, x_own, t_ref, to_y, y_low, y_high = refs[stages - 1 : stages + 9]
    base, response, to_first, to_last, fixed, f_s, g_s = refs[stages + 9 :]
    x_steps, lines = xw.shape[:2]
    chunks = base.shape[0]
    sheets = lines // chunks
    rows = x_steps * SUBLANES

    ends, units = block_ends("gx", stages, ties)
    for n, (own, (low, high)) in enumerate(((lambda i: x_own[i], ends), (nothing, units))):
        for s, pair in enumerate(tree_ends(SUBLANES, x_links, own, low, high)):
            for i in range(2):
                f_s[n, i, pl.ds(s, lines, stride=SUBLANES), :] = pair[i]
    first = 0
    for n, members in enumerate(line_groups(chunks, sheets)):
        at = slice(first, first + len(members))
        h_ref_of, h_at = (xh, at) if n == 0 else (xm, slice(first - 2 * sheets, at.stop - 2 * sheets))
        (low, value), (unit_low, unit) = (
            [
                jnp.stack(
                    [f_s[q, i, j * SUBLANES : (j + 1) * SUBLANES, :] for j in range(at.start, at.stop)], 0
                )
                for i in range(2)
            ]
            for q in range(2)
        )
        for k in range(x_steps - 1, -1, -1):
            w, p = xw[k, at], xp[k, at]
            value = w * value + (h_ref_of[k, h_at] + p * low)
            unit = w * unit + p * unit_low
            field = value - t_ref[k, at]
            for j, (y, z) in enumerate(members):
                place = z * rows + k * SUBLANES
                g_s[0, y, place : place + SUBLANES, :] = field[j]
                g_s[1, y, place : place + SUBLANES, :] = unit[j]
        first = at.stop

    totals = [None, None]
    for y in range(chunks):
        field = turned(to_y[...], g_s[0, y])
        answer = turned(to_y[...], g_s[1, y])
        base[y] = field
        response[y] = answer
        for i, (unit, weight) in enumerate(((y_low, to_first), (y_high, to_last))):
            weight[y] = unit[y] * answer
            part = unit[y] * field
            totals[i] = part if y == 0 else totals[i] + part
    for i in range(2):
        put_sums(fixed.at[i], totals[i])


def put_sums(out, field):
    total = jnp.sum(field, 0, keepdims=True)
    for m in range(out.shape[0]):
        out[m : m + 1, :] = total[:, part_of(m)]


def y_prepare(ties, xw, xh, xm, xp, x_links, x_own, t, to_y, unit_low, unit_high):
    chunks = unit_low.shape[0]
    x_steps, lines = xw.shape[:2]
    width = lines // chunks * x_steps * SUBLANES
    field = shape_of(chunks, LANES, width)
    return pl.pallas_call(
        functools.partial(y_prepare_kernel, len(ties) + 1),
        out_shape=[field] * 4 + [shape_of(2, width // LANES, LANES)],
        scratch_shapes=[
            pltpu.VMEM((2, 2, lines * SUBLANES, LANES), F32),
            pltpu.VMEM((2, chunks, width, LANES), F32),
        ],
        compiler_params=params(),
        cost_estimate=pl.CostEstimate(flops=8 * t.size, bytes_accessed=16 * t.size, transcendentals=0),
    )(*ties, xw, xh, xm, xp, x_links, x_own, t, to_y, unit_low, unit_high)


def y_target_kernel(stages, own, got, to_first, to_last, fixed, view, to_y, spread, send, r_s):
    chunks, _, width = to_first.shape
    sheets = own.shape[1] // chunks
    rows = width // sheets

    flux = top_flux("gx", stages, own, got)
    line_of = {member: n for n, member in enumerate(sum(line_groups(chunks, sheets), []))}
    totals = [None, None]
    for y in range(chunks):
        own_flux = jnp.concatenate([flux[line_of[y, z] : line_of[y, z] + 1, :] for z in range(sheets)], 0)
        wide = turned(to_y[...], own_flux, rows)
        spread[y] = wide
        for i, weight in enumerate((to_first, to_last)):
            part = weight[y] * wide
            totals[i] = part if y == 0 else totals[i] + part
    for n, q in enumerate(COEFS):
        send[q] = view[n]
    for i, q in enumerate((FIRST, LAST)):
        put_sums(r_s.at[i], totals[i])
        send[q] = fixed[i] + r_s[i]


def y_target(own, got, to_first, to_last, fixed, view, to_y):
    pairs = view.shape[1]
    return pl.pallas_call(
        functools.partial(y_target_kernel, stages_of("gx")),
        out_shape=[shape_of(*to_first.shape), shape_of(7, pairs, LANES)],
        scratch_shapes=[pltpu.VMEM((2, pairs, LANES), F32)],
        compiler_params=params(),
    )(own, got, to_first, to_last, fixed, view, to_y)


def y_eliminate_kernel(base, response, spread, yw, yi, yp, inner, outer, after, *refs):
    h_ref, inner_own, outer_own, q_s, r_s = refs
    chunks, _, width = base.shape
    pairs = width // LANES
    steps = yw.shape[0]
    members = [(y, m) for y in range(chunks) for m in range(pairs)]

    def target(k):
        at = slice(k * SUBLANES, (k + 1) * SUBLANES)
        return jnp.stack(
            [
                base[y, at, part_of(m)] + response[y, at, part_of(m)] * spread[y, at, part_of(m)]
                for y, m in members
            ],
            0,
        )

    def keep(k, h):
        h_ref[k] = h

    ends = eliminate(target, steps, lambda k: yw[k], lambda k: yi[k], lambda k: yp[k], keep)
    for q in range(2):
        for i in range(len(members)):
            q_s[q, i * SUBLANES : (i + 1) * SUBLANES, :] = ends[q][i]
    items = [
        tuple(q_s[q, pl.ds(s, len(members), stride=SUBLANES), :] for q in range(2))
        for s in range(SUBLANES)
    ]
    r_s[0], r_s[1] = join_tree(items, inner, inner_own)
    items = [tuple(r_s[q, y * pairs : (y + 1) * pairs, :] for q in range(2)) for y in range(chunks)]
    join_tree(items, outer, outer_own)


def y_eliminate(base, response, spread, yw, yi, yp, inner, outer, after):
    y_lines = yw.shape[1]
    pairs = outer.shape[2]
    chunks = y_lines // pairs
    return pl.pallas_call(
        y_eliminate_kernel,
        in_specs=[IN_VMEM] * 8 + [ANYWHERE],
        out_shape=[
            shape_of(*yw.shape),
            shape_of(SUBLANES - 1, y_lines, LANES),
            shape_of(chunks - 1, pairs, LANES),
        ],
        scratch_shapes=[
            pltpu.VMEM((2, y_lines * SUBLANES, LANES), F32),
            pltpu.VMEM((2, y_lines, LANES), F32),
        ],
        compiler_params=params(),
        cost_estimate=pl.CostEstimate(flops=8 * base.size, bytes_accessed=16 * base.size, transcendentals=0),
    )(base, response, spread, yw, yi, yp, inner, outer, after)


def z_solve(zw, zi, field, at, keep):
    sheets = zi.shape[0]
    rhs, kept = None, []
    for z in range(sheets):
        rhs = field(z) if z == 0 else field(z) + zw[(z - 1, *at)] * rhs
        kept.append(rhs * zi[(z, *at)])
    value = kept[-1]
    keep(sheets - 1, value)
    for z in range(sheets - 2, -1, -1):
        value = zw[(z, *at)] * value + kept[z]
        keep(z, value)


def finish_prepare_kernel(stages, *refs):
    ties = refs[: stages - 1]
    yw, yh, yp, inner, inner_own, outer, outer_own, zw, zi, t_ref, to_x = refs[stages - 1 : stages + 10]
    base, response, r_s, e_s, u_s = refs[stages + 10 :]
    chunks, sheets, rows, _ = base.shape
    each = LANES // rows
    pairs = sheets // each
    steps = yw.shape[0]
    lines = chunks * pairs

    ends, units = block_ends("gy", stages, ties)
    both = (
        (lambda i: outer_own[i], lambda i: inner_own[i], ends),
        (nothing, nothing, units),
    )
    for n, (upper, lower, (low, high)) in enumerate(both):
        for y, pair in enumerate(tree_ends(chunks, outer, upper, low, high)):
            for i in range(2):
                r_s[n, i, y * pairs : (y + 1) * pairs, :] = pair[i]
        for s, pair in enumerate(tree_ends(SUBLANES, inner, lower, r_s[n, 0], r_s[n, 1])):
            for i in range(2):
                e_s[n, i, pl.ds(s, lines, stride=SUBLANES), :] = pair[i]
    (low, value), (unit_low, unit) = (
        [
            jnp.stack([e_s[q, i, n * SUBLANES : (n + 1) * SUBLANES, :] for n in range(lines)], 0)
            for i in range(2)
        ]
        for q in range(2)
    )
    for k in range(steps - 1, -1, -1):
        w, p = yw[k], yp[k]
        value = w * value + (yh[k] + p * low)
        unit = w * unit + p * unit_low
        for y in range(chunks):
            for m in range(pairs):
                place = pl.ds(y * LANES + k, SUBLANES, stride=steps)
                u_s[0, m, place, :] = value[y * pairs + m]
                u_s[1, m, place, :] = unit[y * pairs + m]

    for y in range(chunks):
        part = part_of(y)
        fields = [turned(to_x[...], u_s[0, m, part, :]) for m in range(pairs)]

        def field(z):
            at = z % each * rows
            return fields[z // each][at : at + rows, :]

        def keep(z, value):
            base[y, z] = t_ref[z, :, part] + value

        z_solve(zw, zi, field, (y,), keep)
        for m in range(pairs):
            units = turned(to_x[...], u_s[1, m, part, :])
            for i in range(each):
                response[y, m * each + i] = units[i * rows : (i + 1) * rows, :]


def finish_prepare(ties, yw, yh, yp, inner, inner_own, outer, outer_own, zw, zi, t, to_x):
    sheets, rows, columns = t.shape
    chunks = columns // LANES
    pairs = sheets * rows // LANES
    lines = chunks * pairs
    field = shape_of(chunks, sheets, rows, LANES)
    return pl.pallas_call(
        functools.partial(finish_prepare_kernel, len(ties) + 1),
        out_shape=[field, field],
        scratch_shapes=[
            pltpu.VMEM((2, 2, lines, LANES), F32),
            pltpu.VMEM((2, 2, lines * SUBLANES, LANES), F32),
            pltpu.VMEM((2, pairs, columns, LANES), F32),
        ],
        compiler_params=params(),
        cost_estimate=pl.CostEstimate(flops=12 * t.size, bytes_accessed=20 * t.size, transcendentals=0),
    )(*ties, yw, yh, yp, inner, inner_own, outer, outer_own, zw, zi, t, to_x)


def finish_kernel(stages, own, got, base, response, zw, zi, to_x, out, o_s, sems):
    chunks, sheets, rows, _ = base.shape
    each = LANES // rows
    pairs = sheets // each
    flux = top_flux("gy", stages, own, got)
    spread = [
        turned(to_x[...], flux[m : m + 1, :], LANES) for m in range(pairs)
    ]
    started = []
    block = rows // OUT_COPIES
    for n in range(OUT_COPIES):
        strip = slice(n * block, (n + 1) * block)
        for y in range(chunks):

            def field(z):
                at = z % each * rows + strip.start
                return response[y, z, strip, :] * spread[z // each][at : at + block, :]

            def keep(z, value):
                o_s[z, strip, part_of(y)] = base[y, z, strip, :] + value

            z_solve(zw, zi, field, (y, strip), keep)
        at = pl.ds(strip.start, block)
        copy = pltpu.make_async_copy(o_s.at[:, at, :], out.at[:, at, :], sems.at[n])
        copy.start()
        started.append(copy)
    for copy in started:
        copy.wait()


def finish(own, got, base, response, zw, zi, to_x):
    chunks, sheets, rows, _ = base.shape
    shape = (sheets, rows, chunks * LANES)
    return pl.pallas_call(
        functools.partial(finish_kernel, stages_of("gy")),
        out_shape=shape_of(*shape),
        out_specs=ANYWHERE,
        scratch_shapes=[pltpu.VMEM(shape, F32), pltpu.SemaphoreType.DMA((OUT_COPIES,))],
        compiler_params=params(),
    )(own, got, base, response, zw, zi, to_x)


def per_device(temperature, base, locations, energy):
    columns = temperature.shape[2]
    gy = lax.axis_size("gy")
    t, b, loc, heat, packed = load(temperature, base, locations[None], energy[None])
    near = swap(packed, "gy", 1)
    far = lax.ppermute(packed, "gy", [(i, ((i + 1) % gy ^ 1) - 1 if i else gy - 1) for i in range(gy)])
    c, total, xw, xi, xp, x_links, x_view, xm, ends, t_steps, swapped = x_factor(loc, heat, t, b, columns * gy, packed)
    xh, x_own, view = x_target(swapped, total, near, far, xw, xi, xp, x_links, x_view, ends)
    yw, yi, yp, inner, outer, y_view, to_y, to_x, unit_low, unit_high = y_factor(c, x_view)
    zw, zi = z_factor(c, view)
    own, got, ties = gather_line(view, "gx", 2, (y_view, zw))
    base, response, to_first, to_last, fixed = y_prepare(
        ties, xw, xh, xm, xp, x_links, x_own, t_steps, to_y, unit_low, unit_high
    )
    spread, view = y_target(own, got, to_first, to_last, fixed, y_view, to_y)
    yh, inner_own, outer_own = y_eliminate(base, response, spread, yw, yi, yp, inner, outer, view)
    own, got, ties = gather_line(view, "gy", meanwhile=(yh,), cross=True)
    base, response = finish_prepare(
        ties, yw, yh, yp, inner, inner_own, outer, outer_own, zw, zi, t, to_x
    )
    return finish(own, got, base, response, zw, zi, to_x)


def solution(mesh):
    in_specs = (P(None, "gx", "gy"), P(None, "gx", "gy"), P(), P())
    out_specs = P(None, "gx", "gy")
    return jax.shard_map(
        per_device, mesh=mesh, in_specs=in_specs, out_specs=out_specs, check_vma=False
    )
```

```python
import functools

import jax
import jax.numpy as jnp
from jax import lax
from jax.experimental import pallas as pl
from jax.experimental.pallas import tpu as pltpu
from jax.sharding import PartitionSpec as P

RATE = 2000.0
THERMAL_GROWTH = 0.8
LANES = 128
SUBLANES = 8
F32 = jnp.float32
MIB = 1024 * 1024
OUT_COPIES = 4
ANYWHERE = pl.BlockSpec(memory_space=pl.ANY)
IN_HBM = pl.BlockSpec(memory_space=pltpu.HBM)
IN_VMEM = pl.BlockSpec(memory_space=pltpu.VMEM)

R00, R0L, RLL, FIRST, LAST, C0, CL = range(7)
COEFS = (R00, R0L, RLL, C0, CL)


def params(limit=40):
    return pltpu.CompilerParams(vmem_limit_bytes=limit * MIB)


def shape_of(*sizes):
    return jax.ShapeDtypeStruct(sizes, F32)


def half_conduct(base, temperature):
    return base * (0.5 * RATE + (0.5 * RATE * THERMAL_GROWTH) * temperature)


def inverse(x):
    guess = pl.reciprocal(x, approx=True)
    return guess * (2.0 - x * guess)


def join_coefs(a, b):
    face = a[CL] + b[C0]
    inv = face * inverse(1.0 + face * (a[RLL] + b[R00]))
    left = a[R0L] * inv
    right = b[R0L] * inv
    joined = {
        R00: a[R00] - left * a[R0L],
        R0L: left * b[R0L],
        RLL: b[RLL] - right * b[R0L],
        C0: a[C0],
        CL: b[CL],
    }
    return joined, (inv, right, left)


def join_targets(a, b, links):
    inv, right, left = links
    jump = b[0] - a[1]
    return (a[0] + left * jump, b[1] - right * jump), jump * inv


def between(own, right, left, low, high):
    return own + right * high - left * low


def tree(items, join):
    levels = []
    while len(items) > 1:
        pairs = [join(items[i], items[i + 1]) for i in range(0, len(items), 2)]
        items = [p[0] for p in pairs]
        levels.append([p[1] for p in pairs])
    return items[0], levels


def descend(levels, low, high):
    ends = [(low, high)]
    for level in reversed(levels):
        below = []
        for (lo, hi), (own, right, left) in zip(ends, level):
            flux = between(own, right, left, lo, hi)
            below += [(lo, flux), (-flux, hi)]
        ends = below
    return ends


def node_offsets(leaves):
    offsets, at, count = [], 0, leaves // 2
    while count:
        offsets.append((at, count))
        at += count
        count //= 2
    return offsets


def factor(cond, steps, keep):
    here = cond(0)
    c_first = here
    one = jnp.ones_like(here)
    ground, path, first_first = one, one, None
    for k in range(steps - 1):
        following = cond(k + 1)
        face = here + following
        inv = inverse(ground + face)
        w = face * inv
        p = path * inv
        keep(k, w, inv, p)
        step = path * p
        first_first = step if first_first is None else first_first + step
        path = path * w
        ground = 1.0 + w * ground
        here = following
    inv = inverse(ground)
    p = path * inv
    keep(steps - 1, inv, inv, p)
    return {R00: first_first + path * p, R0L: p, RLL: inv, C0: c_first, CL: here}


def eliminate(target, steps, w, inv, p, keep):
    rhs = target(0)
    first = None
    for k in range(steps):
        h = rhs * inv(k)
        keep(k, h)
        step = rhs * p(k)
        first = step if first is None else first + step
        if k < steps - 1:
            rhs = target(k + 1) + w(k) * rhs
    return first, h


def is_odd(axis):
    return lax.axis_index(axis) % 2 == 1


def fold(cells, used):
    steps = cells.shape[0] // SUBLANES
    total = cells[pl.ds(0, SUBLANES, stride=steps), :]
    lane = lax.broadcasted_iota(jnp.int32, total.shape, 1)
    for k in range(1, steps):
        part = pltpu.roll(cells[pl.ds(k, SUBLANES, stride=steps), :], k * used, 1)
        total = jnp.where(lane // used == k, part, total)
    return total


def load_kernel(t_hbm, b_hbm, loc_hbm, energy_hbm, t_out, b_out, loc, energy, packed, cells, sems):
    sheets, rows, columns = t_hbm.shape
    parts = [(0, LANES), (columns - LANES, LANES), (LANES, columns - 2 * LANES)]
    copies = []
    for n, (start, size) in enumerate(parts):
        part = pl.ds(start, size)
        for i, (src, dst) in enumerate(((t_hbm, t_out), (b_hbm, b_out))):
            copies.append(
                pltpu.make_async_copy(src.at[:, :, part], dst.at[:, :, part], sems.at[i, n])
            )
    copies.append(pltpu.make_async_copy(loc_hbm, loc, sems.at[2, 0]))
    copies.append(pltpu.make_async_copy(energy_hbm, energy, sems.at[2, 1]))
    for copy in copies:
        copy.start()
    lane = lax.broadcasted_iota(jnp.int32, (rows, LANES), 1)
    edge_t = jnp.zeros((rows, LANES), F32)
    edge_c = edge_t
    for side, source in enumerate((0, LANES - 1)):
        for copy in copies[2 * side : 2 * side + 2]:
            copy.wait()
        part = slice(parts[side][0], parts[side][0] + LANES)
        for z in range(sheets):
            t = t_out[z, :, part]
            c = half_conduct(b_out[z, :, part], t)
            place = lane == sheets * side + z
            edge_t = jnp.where(place, t[:, source : source + 1], edge_t)
            edge_c = jnp.where(place, c[:, source : source + 1], edge_c)
    cells[0], cells[1] = edge_t, edge_c
    for i in range(2):
        packed[i * SUBLANES : (i + 1) * SUBLANES, :] = fold(cells.at[i], 2 * sheets)
    for copy in copies[4:]:
        copy.wait()


def load(temperature, base, locations, energy):
    sheets, rows, columns = temperature.shape
    assert rows // SUBLANES * 2 * sheets <= LANES and columns > 2 * LANES
    operands = (temperature, base, locations, energy)
    return pl.pallas_call(
        load_kernel,
        in_specs=[IN_HBM] * 4,
        out_shape=[pltpu.VMEM(v.shape, v.dtype) for v in operands]
        + [pltpu.VMEM((2 * SUBLANES, LANES), F32)],
        scratch_shapes=[pltpu.VMEM((2, rows, LANES), F32), pltpu.SemaphoreType.DMA((3, 3))],
        compiler_params=params(),
    )(*[pltpu.with_memory_space_constraint(v, pltpu.HBM) for v in operands])


def source_plane(loc, energy, rows, columns, plate):
    place = loc[...]
    count = place.shape[1]
    local_x = place // plate - lax.axis_index("gx") * rows
    local_y = place % plate - lax.axis_index("gy") * columns
    in_x = lax.broadcasted_iota(jnp.int32, (rows, count), 0) == local_x
    in_y = lax.broadcasted_iota(jnp.int32, (columns, count), 0) == local_y
    by_y = jnp.where(in_y, 1.0, 0.0).astype(jnp.bfloat16)
    left = energy[...]
    plane = None
    for _ in range(3):
        part = left.astype(jnp.bfloat16).astype(F32)
        left = left - part
        term = lax.dot_general(
            jnp.where(in_x, part, 0.0).astype(jnp.bfloat16),
            by_y,
            (((1,), (1,)), ((), ())),
            preferred_element_type=F32,
        )
        plane = term if plane is None else plane + term
    return plane


def part_of(y):
    return slice(y * LANES, (y + 1) * LANES)


def line_groups(chunks, sheets):
    order = [0, chunks - 1] + list(range(1, chunks - 1))
    return [[(y, z) for y in order[i : i + 2] for z in range(sheets)] for i in range(0, chunks, 2)]


def x_eliminate(cells, members, first_line, w_ref, i_ref, p_ref, h_ref, h_line, q_s):
    steps = w_ref.shape[0]
    at = slice(first_line, first_line + len(members))
    kept_at = slice(h_line, h_line + len(members))

    def target(k):
        return jnp.stack([cells(y, z, k) for y, z in members], 0)

    def keep(k, h):
        h_ref[k, kept_at] = h

    ends = eliminate(
        target, steps, lambda k: w_ref[k, at], lambda k: i_ref[k, at], lambda k: p_ref[k, at], keep
    )
    for q in range(2):
        for i in range(len(members)):
            first = (first_line + i) * SUBLANES
            q_s[q, first : first + SUBLANES, :] = ends[q][i]


def x_factor_kernel(plate, loc, energy, t_ref, b_ref, own_cells, *refs):
    c_ref, total_ref, w_ref, i_ref, p_ref, links, view, h_ref, ends_ref, t_out, swapped, q_s, t_s = refs
    chunks, sheets, rows, _ = c_ref.shape
    lines = chunks * sheets
    steps = rows // SUBLANES
    plane = source_plane(loc, energy, rows, chunks * LANES, plate)
    mine = own_cells[...]
    in_low = lax.broadcasted_iota(jnp.int32, mine.shape, 1) % (2 * sheets) < sheets
    swapped[...] = jnp.where(
        in_low, pltpu.roll(mine, LANES - sheets, 1), pltpu.roll(mine, sheets, 1)
    )

    lane = lax.broadcasted_iota(jnp.int32, (SUBLANES, LANES), 1)
    is_first, is_last = lane == 0, lane == LANES - 1
    for r in range(steps):
        at = slice(r * SUBLANES, (r + 1) * SUBLANES)
        before_t, before_c = None, None
        for z in range(sheets):
            ts = [t_ref[z, at, part_of(y)] for y in range(chunks)]
            cs = [half_conduct(b_ref[z, at, part_of(y)], ts[y]) for y in range(chunks)]
            t_turned = [pltpu.roll(v, LANES - 1, 1) for v in ts]
            c_turned = [pltpu.roll(v, LANES - 1, 1) for v in cs]
            flux = []
            for y in range(chunks):
                if y < chunks - 1:
                    t_next = jnp.where(is_last, t_turned[y + 1], t_turned[y])
                    c_next = jnp.where(is_last, c_turned[y + 1], c_turned[y])
                    flux.append((cs[y] + c_next) * (t_next - ts[y]))
                else:
                    inside = (cs[y] + c_turned[y]) * (t_turned[y] - ts[y])
                    flux.append(jnp.where(is_last, 0.0, inside))
            turned = [pltpu.roll(v, 1, 1) for v in flux]
            for y in range(chunks):
                from_low = jnp.where(is_first, turned[y - 1] if y else 0.0, turned[y])
                total = ts[y] + (flux[y] - from_low)
                if z == 0:
                    total = total + plane[at, part_of(y)]
                else:
                    across = (before_c[y] + cs[y]) * (ts[y] - before_t[y])
                    total = total - across
                    total_ref[y, z - 1, at, :] += across
                total_ref[y, z, at, :] = total
                c_ref[y, z, at, :] = cs[y]
                t_s[y, z, at, :] = ts[y]
            before_t, before_c = ts, cs

    at = 0
    for n, members in enumerate(line_groups(chunks, sheets)):

        def cond(k):
            return jnp.stack([c_ref[y, z, pl.ds(k, SUBLANES, stride=steps), :] for y, z in members], 0)

        def keep(k, w, inv, p):
            w_ref[k, at : at + len(members)] = w
            i_ref[k, at : at + len(members)] = inv
            p_ref[k, at : at + len(members)] = p

        block = factor(cond, steps, keep)
        for i, q in enumerate(COEFS):
            for j in range(len(members)):
                first = (at + j) * SUBLANES
                q_s[i, first : first + SUBLANES, :] = block[q][j]
        if n > 0:
            x_eliminate(
                lambda y, z, k: total_ref[y, z, pl.ds(k, SUBLANES, stride=steps), :],
                members, at, w_ref, i_ref, p_ref, h_ref, at - 2 * sheets, ends_ref,
            )
        for k in range(steps):
            for i, (y, z) in enumerate(members):
                t_out[k, at + i] = t_s[y, z, pl.ds(k, SUBLANES, stride=steps), :]
        at += len(members)

    segments = [
        {q: q_s[n, pl.ds(s, lines, stride=SUBLANES), :] for n, q in enumerate(COEFS)}
        for s in range(SUBLANES)
    ]
    whole, levels = tree(segments, join_coefs)
    for (offset, _), level in zip(node_offsets(SUBLANES), levels):
        for n, values in enumerate(level):
            for i in range(3):
                links[offset + n, i] = values[i]
    for n, q in enumerate(COEFS):
        view[n] = whole[q]


def x_factor(loc, energy, t, b, plate, own_cells):
    sheets, rows, columns = t.shape
    chunks = columns // LANES
    lines = chunks * sheets
    steps = rows // SUBLANES
    field = shape_of(chunks, sheets, rows, LANES)
    stored = shape_of(steps, lines, SUBLANES, LANES)
    return pl.pallas_call(
        functools.partial(x_factor_kernel, plate),
        in_specs=[IN_VMEM] * 5,
        out_shape=[
            field,
            field,
            stored,
            stored,
            stored,
            shape_of(SUBLANES - 1, 3, lines, LANES),
            shape_of(len(COEFS), lines, LANES),
            shape_of(steps, max(1, lines - 2 * sheets), SUBLANES, LANES),
            shape_of(2, lines * SUBLANES, LANES),
            stored,
            shape_of(*own_cells.shape),
        ],
        scratch_shapes=[
            pltpu.VMEM((len(COEFS), lines * SUBLANES, LANES), F32),
            pltpu.VMEM((chunks, sheets, rows, LANES), F32),
        ],
        compiler_params=params(),
        cost_estimate=pl.CostEstimate(flops=40 * t.size, bytes_accessed=28 * t.size, transcendentals=0),
    )(loc, energy, t, b, own_cells)


def x_target_kernel(own_cells, total_ref, near, far, *refs):
    w_ref, i_ref, p_ref, links, view, ends_ref, h_ref, own, send, q_s = refs
    chunks, sheets, rows, _ = total_ref.shape
    lines = chunks * sheets
    steps = rows // SUBLANES

    place = lax.axis_index("gy")
    inner = (place > 0) & (place < lax.axis_size("gy") - 1)
    lane = lax.broadcasted_iota(jnp.int32, (SUBLANES, LANES), 1)
    side = 2 * sheets
    is_near = (lane % side >= sheets).astype(jnp.int32) == place % 2
    t, c = (
        jnp.where(is_near, near[at, :], jnp.where(inner, far[at, :], 0.0))
        for at in (slice(0, SUBLANES), slice(SUBLANES, 2 * SUBLANES))
    )
    face = jnp.where(c > 0.0, own_cells[SUBLANES:, :] + c, 0.0)
    flux = face * (t - own_cells[:SUBLANES, :])

    def cells(y, z, k):
        at = k * side + (sheets + z if y == 0 else z)
        edge = 0 if y == 0 else LANES - 1
        inflow = jnp.where(lane == edge, flux[:, at : at + 1], 0.0)
        return total_ref[y, z, pl.ds(k, SUBLANES, stride=steps), :] + inflow

    members = line_groups(chunks, sheets)[0]
    x_eliminate(cells, members, 0, w_ref, i_ref, p_ref, h_ref, 0, q_s)
    split = len(members)
    items = [
        tuple(
            jnp.concatenate(
                [
                    q_s[q, pl.ds(s, split, stride=SUBLANES), :],
                    ends_ref[q, pl.ds(split * SUBLANES + s, lines - split, stride=SUBLANES), :],
                ],
                0,
            )
            for q in range(2)
        )
        for s in range(SUBLANES)
    ]
    for offset, count in node_offsets(SUBLANES):
        joined = []
        for n in range(count):
            ties = tuple(links[offset + n, i] for i in range(3))
            both, flux = join_targets(items[2 * n], items[2 * n + 1], ties)
            own[offset + n] = flux
            joined.append(both)
        items = joined
    for n, q in enumerate(COEFS):
        send[q] = view[n]
    send[FIRST], send[LAST] = items[0]


def x_target(own_cells, total, near, far, w, inv, p, links, view, ends):
    chunks, sheets, rows, _ = total.shape
    lines = chunks * sheets
    steps = rows // SUBLANES
    return pl.pallas_call(
        x_target_kernel,
        out_shape=[
            shape_of(steps, 2 * sheets, SUBLANES, LANES),
            shape_of(SUBLANES - 1, lines, LANES),
            shape_of(7, lines, LANES),
        ],
        scratch_shapes=[
            pltpu.VMEM((2, 2 * sheets * SUBLANES, LANES), F32),
        ],
        compiler_params=params(),
    )(own_cells, total, near, far, w, inv, p, links, view, ends)


def stages_of(axis):
    return lax.axis_size(axis).bit_length() - 1


def swap(value, axis, flip):
    count = lax.axis_size(axis)
    return lax.ppermute(value, axis, [(i, i ^ flip) for i in range(count)])


def on_right(axis, stage):
    return (lax.axis_index(axis) >> stage) % 2 == 1


def toward(right, block):
    return (
        jnp.where(right, block[R00], block[RLL]),
        jnp.where(right, block[FIRST], block[LAST]),
        jnp.where(right, block[C0], block[CL]),
    )


def join(a, b):
    joined, ties = join_coefs(a, b)
    (joined[FIRST], joined[LAST]), flux = join_targets((a[FIRST], a[LAST]), (b[FIRST], b[LAST]), ties)
    return joined, (flux, ties[1], ties[2])


def ordered(right, own, other):
    first = [jnp.where(right, theirs, mine) for mine, theirs in zip(own, other)]
    second = [jnp.where(right, mine, theirs) for mine, theirs in zip(own, other)]
    return first, second


def join_kernel(axis, stage, width, last, *refs):
    count = 1 << width
    blocks = [[refs[i][q] for q in range(7)] for i in range(count)]
    send = refs[-1 - width]
    links = refs[-width:]
    for bit in range(width):
        right = on_right(axis, stage + bit)
        for i in range(count):
            if not i >> bit & 1:
                j = i | 1 << bit
                blocks[i], blocks[j] = ordered(right, blocks[i], blocks[j])
    for bit in range(width):
        pairs = [join(blocks[i], blocks[i + 1]) for i in range(0, len(blocks), 2)]
        blocks = [p[0] for p in pairs]
        ties = [p[1] for p in pairs]
        for upper in range(bit + 1, width):
            right = on_right(axis, stage + upper)
            ties = [
                tuple(jnp.where(right, v, u) for u, v in zip(ties[i], ties[i + 1]))
                for i in range(0, len(ties), 2)
            ]
        for i in range(3):
            links[bit][i] = ties[0][i]
    (whole,) = blocks
    if last:
        for n, value in enumerate(toward(on_right(axis, stage + width), whole)):
            send[n] = value
    else:
        for q in range(7):
            send[q] = whole[q]


def join_stage(own, got, axis, stage, width, last, after):
    lines = own.shape[1]
    return pl.pallas_call(
        functools.partial(join_kernel, axis, stage, width, last),
        in_specs=[IN_VMEM] * (1 + len(got)) + [ANYWHERE] * len(after),
        out_shape=[shape_of(3 if last else 7, lines, LANES)] + [shape_of(3, lines, LANES)] * width,
        compiler_params=params(),
    )(own, *got, *after)


def gather_line(view, axis, widest=1, meanwhile=(), cross=False):
    stages = stages_of(axis)
    links, stage = [], 0
    while stage < stages - 1:
        width = min(widest, stages - 1 - stage)
        got = [swap(view, axis, flip << stage) for flip in range(1, 1 << width)]
        last = stage + width == stages - 1
        view, *ties = join_stage(view, got, axis, stage, width, last, meanwhile)
        links += ties
        stage += width
        meanwhile = ()
    return view, swap(view, axis, 1 << stage | (cross and stage > 0)), links


def top_flux(axis, stages, own, got):
    right = on_right(axis, stages - 1)
    face = own[2] + got[2]
    jump = jnp.where(right, own[1] - got[1], got[1] - own[1])
    return jump * face * inverse(1.0 + face * (own[0] + got[0]))


def block_ends(axis, stages, links):
    shape = links[0].shape[1:] if links else None
    right = on_right(axis, stages - 1)
    zero = jnp.zeros(shape, F32)
    low, high = zero, zero
    unit_low = zero + jnp.where(right, -1.0, 0.0)
    unit_high = zero + jnp.where(right, 0.0, 1.0)
    for stage in range(stages - 2, -1, -1):
        tie = links[stage]
        right = on_right(axis, stage)
        flux = between(tie[0], tie[1], tie[2], low, high)
        unit = between(0.0, tie[1], tie[2], unit_low, unit_high)
        low, high = jnp.where(right, -flux, low), jnp.where(right, high, flux)
        unit_low, unit_high = jnp.where(right, -unit, unit_low), jnp.where(right, unit_high, unit)
    return (low, high), (unit_low, unit_high)


def natural(index, parts):
    span = SUBLANES * parts
    local = index % span
    return index - local + local % SUBLANES * parts + local // SUBLANES


def turn_matrix(shape, from_natural, parts):
    row = lax.broadcasted_iota(jnp.int32, shape, 0)
    column = lax.broadcasted_iota(jnp.int32, shape, 1) % LANES
    hit = natural(row, parts) == column if from_natural else row == natural(column, parts)
    return jnp.where(hit, 1.0, 0.0).astype(jnp.bfloat16)


def turned(matrix, field, rows=None):
    high = field.astype(jnp.bfloat16).astype(F32)
    both = jnp.concatenate([high, field - high], 1)
    if rows:
        both = jnp.concatenate(
            [jnp.broadcast_to(both[n : n + 1, :], (rows, 2 * LANES)) for n in range(field.shape[0])], 0
        )
    both = both.astype(jnp.bfloat16)
    return lax.dot_general(
        matrix, both, (((1,), (1,)), ((), ())), preferred_element_type=F32
    )


def y_factor_kernel(c_ref, after, w_ref, i_ref, p_ref, inner, outer, view, to_y, to_x, unit_low, unit_high, c_s, q_s, r_s):
    chunks, sheets, rows, _ = c_ref.shape
    each = LANES // rows
    pairs = sheets // each
    x_steps = rows // SUBLANES
    steps = LANES // SUBLANES
    to_y[...] = turn_matrix(to_y.shape, True, steps)
    to_x[...] = turn_matrix(to_x.shape, False, x_steps)
    for m in range(pairs):
        for y in range(chunks):
            block = jnp.concatenate(
                [
                    c_ref[y, m * each + i, pl.ds(k, SUBLANES, stride=x_steps), :]
                    for i in range(each)
                    for k in range(x_steps)
                ],
                0,
            )
            c_s[m, part_of(y), :] = block.T

    members = [(y, m) for y in range(chunks) for m in range(pairs)]
    lines = len(members)

    def cond(k):
        return jnp.stack([c_s[m, pl.ds(y * LANES + k, SUBLANES, stride=steps), :] for y, m in members], 0)

    def keep(k, w, inv, p):
        w_ref[k] = w
        i_ref[k] = inv
        p_ref[k] = p

    block = factor(cond, steps, keep)
    for n, q in enumerate(COEFS):
        for i in range(lines):
            q_s[n, i * SUBLANES : (i + 1) * SUBLANES, :] = block[q][i]
    segments = [
        {q: q_s[n, pl.ds(s, lines, stride=SUBLANES), :] for n, q in enumerate(COEFS)}
        for s in range(SUBLANES)
    ]
    whole, levels = tree(segments, join_coefs)
    for (offset, _), level in zip(node_offsets(SUBLANES), levels):
        for n, values in enumerate(level):
            for i in range(3):
                inner[offset + n, i] = values[i]
    for n, q in enumerate(COEFS):
        r_s[n] = whole[q]
    parts = [
        {q: r_s[n, y * pairs : (y + 1) * pairs, :] for n, q in enumerate(COEFS)} for y in range(chunks)
    ]
    whole, levels = tree(parts, join_coefs)
    for (offset, _), level in zip(node_offsets(chunks), levels):
        for n, values in enumerate(level):
            for i in range(3):
                outer[offset + n, i] = values[i]
    for n, q in enumerate(COEFS):
        view[n] = whole[q]

    same = turn_matrix(to_y.shape, True, 1)
    one = jnp.ones((pairs, LANES), F32)
    for n, (low, high, field) in enumerate(((one, 0.0 * one, unit_low), (0.0 * one, one, unit_high))):
        for y, pair in enumerate(tree_ends(chunks, outer, nothing, low, high)):
            for i in range(2):
                r_s[2 * n + i, y * pairs : (y + 1) * pairs, :] = pair[i]
        for s, pair in enumerate(tree_ends(SUBLANES, inner, nothing, r_s[2 * n], r_s[2 * n + 1])):
            for i in range(2):
                q_s[2 * n + i, pl.ds(s, lines, stride=SUBLANES), :] = pair[i]
        low, value = (
            jnp.stack(
                [q_s[2 * n + i, j * SUBLANES : (j + 1) * SUBLANES, :] for j in range(lines)], 0
            )
            for i in range(2)
        )
        for k in range(steps - 1, -1, -1):
            value = w_ref[k] * value + p_ref[k] * low
            for j, (y, m) in enumerate(members):
                c_s[m, pl.ds(y * LANES + k, SUBLANES, stride=steps), :] = value[j]
        for y, m in members:
            field[y, part_of(m), :] = turned(same, c_s[m, part_of(y), :])


def y_factor(c, after):
    chunks, sheets, rows, _ = c.shape
    pairs = sheets * rows // LANES
    lines = chunks * pairs
    stored = shape_of(LANES // SUBLANES, lines, SUBLANES, LANES)
    matrix = jax.ShapeDtypeStruct((LANES, 2 * LANES), jnp.bfloat16)
    return pl.pallas_call(
        y_factor_kernel,
        in_specs=[IN_VMEM, ANYWHERE],
        out_shape=[
            stored,
            stored,
            stored,
            shape_of(SUBLANES - 1, 3, lines, LANES),
            shape_of(chunks - 1, 3, pairs, LANES),
            shape_of(len(COEFS), pairs, LANES),
            matrix,
            matrix,
            shape_of(chunks, pairs * LANES, LANES),
            shape_of(chunks, pairs * LANES, LANES),
        ],
        scratch_shapes=[
            pltpu.VMEM((pairs, chunks * LANES, LANES), F32),
            pltpu.VMEM((len(COEFS), lines * SUBLANES, LANES), F32),
            pltpu.VMEM((len(COEFS), lines, LANES), F32),
        ],
        compiler_params=params(),
        cost_estimate=pl.CostEstimate(flops=20 * c.size, bytes_accessed=16 * c.size, transcendentals=0),
    )(c, after)


def z_factor_kernel(c_ref, after, w_ref, i_ref):
    sheets = c_ref.shape[1]
    ground = 1.0
    for z in range(sheets - 1):
        face = c_ref[:, z] + c_ref[:, z + 1]
        inv = inverse(ground + face)
        w = face * inv
        i_ref[z] = inv
        w_ref[z] = w
        ground = 1.0 + w * ground
    i_ref[sheets - 1] = inverse(ground)


def z_factor(c, after):
    chunks, sheets, rows, _ = c.shape
    return pl.pallas_call(
        z_factor_kernel,
        in_specs=[IN_VMEM, ANYWHERE],
        out_shape=[
            shape_of(sheets - 1, chunks, rows, LANES),
            shape_of(sheets, chunks, rows, LANES),
        ],
        compiler_params=params(),
        cost_estimate=pl.CostEstimate(flops=10 * c.size, bytes_accessed=12 * c.size, transcendentals=0),
    )(c, after)


def join_tree(items, links, own):
    for offset, count in node_offsets(len(items)):
        joined = []
        for n in range(count):
            tie = tuple(links[offset + n, i] for i in range(3))
            both, flux = join_targets(items[2 * n], items[2 * n + 1], tie)
            own[offset + n] = flux
            joined.append(both)
        items = joined
    return items[0]


def tree_ends(leaves, links, own, low, high):
    levels = [
        [(own(offset + n), links[offset + n, 1], links[offset + n, 2]) for n in range(count)]
        for offset, count in node_offsets(leaves)
    ]
    return descend(levels, low, high)


def nothing(node):
    return 0.0


def y_prepare_kernel(stages, *refs):
    ties = refs[: stages - 1]
    xw, xh, xm, xp, x_links, x_own, t_ref, to_y, y_low, y_high = refs[stages - 1 : stages + 9]
    base, response, to_first, to_last, fixed, f_s, g_s = refs[stages + 9 :]
    x_steps, lines = xw.shape[:2]
    chunks = base.shape[0]
    sheets = lines // chunks
    rows = x_steps * SUBLANES

    ends, units = block_ends("gx", stages, ties)
    for n, (own, (low, high)) in enumerate(((lambda i: x_own[i], ends), (nothing, units))):
        for s, pair in enumerate(tree_ends(SUBLANES, x_links, own, low, high)):
            for i in range(2):
                f_s[n, i, pl.ds(s, lines, stride=SUBLANES), :] = pair[i]
    first = 0
    for n, members in enumerate(line_groups(chunks, sheets)):
        at = slice(first, first + len(members))
        h_ref_of, h_at = (xh, at) if n == 0 else (xm, slice(first - 2 * sheets, at.stop - 2 * sheets))
        (low, value), (unit_low, unit) = (
            [
                jnp.stack(
                    [f_s[q, i, j * SUBLANES : (j + 1) * SUBLANES, :] for j in range(at.start, at.stop)], 0
                )
                for i in range(2)
            ]
            for q in range(2)
        )
        for k in range(x_steps - 1, -1, -1):
            w, p = xw[k, at], xp[k, at]
            value = w * value + (h_ref_of[k, h_at] + p * low)
            unit = w * unit + p * unit_low
            field = value - t_ref[k, at]
            for j, (y, z) in enumerate(members):
                place = z * rows + k * SUBLANES
                g_s[0, y, place : place + SUBLANES, :] = field[j]
                g_s[1, y, place : place + SUBLANES, :] = unit[j]
        first = at.stop

    totals = [None, None]
    for y in range(chunks):
        base[y] = turned(to_y[...], g_s[0, y])
        response[y] = turned(to_y[...], g_s[1, y])
        for i, (unit, weight) in enumerate(((y_low, to_first), (y_high, to_last))):
            weight[y] = unit[y] * g_s[1, y]
            part = unit[y] * g_s[0, y]
            totals[i] = part if y == 0 else totals[i] + part
    for i in range(2):
        put_sums(fixed.at[i], totals[i])


def put_sums(out, field):
    ones = jnp.ones((2 * SUBLANES, 2 * LANES), jnp.bfloat16)
    total = turned(ones, field)
    for m in range(out.shape[0]):
        out[m : m + 1, :] = total[:1, part_of(m)]


def y_prepare(ties, xw, xh, xm, xp, x_links, x_own, t, to_y, unit_low, unit_high):
    chunks = unit_low.shape[0]
    x_steps, lines = xw.shape[:2]
    width = lines // chunks * x_steps * SUBLANES
    field, weight = shape_of(chunks, LANES, width), shape_of(chunks, width, LANES)
    return pl.pallas_call(
        functools.partial(y_prepare_kernel, len(ties) + 1),
        out_shape=[field] * 2 + [weight] * 2 + [shape_of(2, width // LANES, LANES)],
        scratch_shapes=[
            pltpu.VMEM((2, 2, lines * SUBLANES, LANES), F32),
            pltpu.VMEM((2, chunks, width, LANES), F32),
        ],
        compiler_params=params(),
        cost_estimate=pl.CostEstimate(flops=8 * t.size, bytes_accessed=16 * t.size, transcendentals=0),
    )(*ties, xw, xh, xm, xp, x_links, x_own, t, to_y, unit_low, unit_high)


def sheet_rows(values, y, chunks, sheets):
    line_of = {member: n for n, member in enumerate(sum(line_groups(chunks, sheets), []))}
    return [values[line_of[y, z] : line_of[y, z] + 1, :] for z in range(sheets)]


def y_target_kernel(stages, own, got, to_first, to_last, fixed, view, flux_ref, send, r_s):
    chunks, width, _ = to_first.shape
    sheets = own.shape[1] // chunks
    rows = width // sheets

    flux = top_flux("gx", stages, own, got)
    flux_ref[...] = flux
    totals = [[None] * sheets, [None] * sheets]
    for y in range(chunks):
        for z, row in enumerate(sheet_rows(flux, y, chunks, sheets)):
            for total, weight in zip(totals, (to_first, to_last)):
                part = weight[y, z * rows : (z + 1) * rows, :] * row
                total[z] = part if y == 0 else total[z] + part
    for n, q in enumerate(COEFS):
        send[q] = view[n]
    for i, q in enumerate((FIRST, LAST)):
        put_sums(r_s.at[i], jnp.concatenate(totals[i], 0))
        send[q] = fixed[i] + r_s[i]


def y_target(own, got, to_first, to_last, fixed, view):
    pairs = view.shape[1]
    return pl.pallas_call(
        functools.partial(y_target_kernel, stages_of("gx")),
        out_shape=[shape_of(*own.shape[1:]), shape_of(7, pairs, LANES)],
        scratch_shapes=[pltpu.VMEM((2, pairs, LANES), F32)],
        compiler_params=params(),
    )(own, got, to_first, to_last, fixed, view)


def y_eliminate_kernel(base, response, flux, to_y, yw, yi, yp, inner, outer, after, *refs):
    h_ref, inner_own, outer_own, q_s, r_s = refs
    chunks, _, width = base.shape
    pairs = width // LANES
    sheets = flux.shape[0] // chunks
    steps = yw.shape[0]
    members = [(y, m) for y in range(chunks) for m in range(pairs)]
    fields = []
    for y in range(chunks):
        by_sheet = jnp.concatenate(sheet_rows(flux[...], y, chunks, sheets), 0)
        fields.append(base[y] + response[y] * turned(to_y[...], by_sheet, width // sheets))

    def target(k):
        at = slice(k * SUBLANES, (k + 1) * SUBLANES)
        return jnp.stack([fields[y][at, part_of(m)] for y, m in members], 0)

    def keep(k, h):
        h_ref[k] = h

    ends = eliminate(target, steps, lambda k: yw[k], lambda k: yi[k], lambda k: yp[k], keep)
    for q in range(2):
        for i in range(len(members)):
            q_s[q, i * SUBLANES : (i + 1) * SUBLANES, :] = ends[q][i]
    items = [
        tuple(q_s[q, pl.ds(s, len(members), stride=SUBLANES), :] for q in range(2))
        for s in range(SUBLANES)
    ]
    r_s[0], r_s[1] = join_tree(items, inner, inner_own)
    items = [tuple(r_s[q, y * pairs : (y + 1) * pairs, :] for q in range(2)) for y in range(chunks)]
    join_tree(items, outer, outer_own)


def y_eliminate(base, response, flux, to_y, yw, yi, yp, inner, outer, after):
    y_lines = yw.shape[1]
    pairs = outer.shape[2]
    chunks = y_lines // pairs
    return pl.pallas_call(
        y_eliminate_kernel,
        in_specs=[IN_VMEM] * 9 + [ANYWHERE],
        out_shape=[
            shape_of(*yw.shape),
            shape_of(SUBLANES - 1, y_lines, LANES),
            shape_of(chunks - 1, pairs, LANES),
        ],
        scratch_shapes=[
            pltpu.VMEM((2, y_lines * SUBLANES, LANES), F32),
            pltpu.VMEM((2, y_lines, LANES), F32),
        ],
        compiler_params=params(),
        cost_estimate=pl.CostEstimate(flops=8 * base.size, bytes_accessed=16 * base.size, transcendentals=0),
    )(base, response, flux, to_y, yw, yi, yp, inner, outer, after)


def z_solve(zw, zi, field, at, keep):
    sheets = zi.shape[0]
    rhs, kept = None, []
    for z in range(sheets):
        rhs = field(z) if z == 0 else field(z) + zw[(z - 1, *at)] * rhs
        kept.append(rhs * zi[(z, *at)])
    value = kept[-1]
    keep(sheets - 1, value)
    for z in range(sheets - 2, -1, -1):
        value = zw[(z, *at)] * value + kept[z]
        keep(z, value)


def finish_prepare_kernel(stages, *refs):
    ties = refs[: stages - 1]
    yw, yh, yp, inner, inner_own, outer, outer_own, zw, zi, t_ref, to_x = refs[stages - 1 : stages + 10]
    base, response, r_s, e_s, u_s = refs[stages + 10 :]
    chunks, sheets, rows, _ = base.shape
    each = LANES // rows
    pairs = sheets // each
    steps = yw.shape[0]
    lines = chunks * pairs

    ends, units = block_ends("gy", stages, ties)
    both = (
        (lambda i: outer_own[i], lambda i: inner_own[i], ends),
        (nothing, nothing, units),
    )
    for n, (upper, lower, (low, high)) in enumerate(both):
        for y, pair in enumerate(tree_ends(chunks, outer, upper, low, high)):
            for i in range(2):
                r_s[n, i, y * pairs : (y + 1) * pairs, :] = pair[i]
        for s, pair in enumerate(tree_ends(SUBLANES, inner, lower, r_s[n, 0], r_s[n, 1])):
            for i in range(2):
                e_s[n, i, pl.ds(s, lines, stride=SUBLANES), :] = pair[i]
    (low, value), (unit_low, unit) = (
        [
            jnp.stack([e_s[q, i, n * SUBLANES : (n + 1) * SUBLANES, :] for n in range(lines)], 0)
            for i in range(2)
        ]
        for q in range(2)
    )
    for k in range(steps - 1, -1, -1):
        w, p = yw[k], yp[k]
        value = w * value + (yh[k] + p * low)
        unit = w * unit + p * unit_low
        for y in range(chunks):
            for m in range(pairs):
                place = pl.ds(y * LANES + k, SUBLANES, stride=steps)
                u_s[0, m, place, :] = value[y * pairs + m]
                u_s[1, m, place, :] = unit[y * pairs + m]

    for y in range(chunks):
        part = part_of(y)
        fields = [turned(to_x[...], u_s[0, m, part, :]) for m in range(pairs)]

        def field(z):
            at = z % each * rows
            return fields[z // each][at : at + rows, :]

        def keep(z, value):
            base[y, z] = t_ref[z, :, part] + value

        z_solve(zw, zi, field, (y,), keep)
        for m in range(pairs):
            units = turned(to_x[...], u_s[1, m, part, :])
            for i in range(each):
                response[y, m * each + i] = units[i * rows : (i + 1) * rows, :]


def finish_prepare(ties, yw, yh, yp, inner, inner_own, outer, outer_own, zw, zi, t, to_x):
    sheets, rows, columns = t.shape
    chunks = columns // LANES
    pairs = sheets * rows // LANES
    lines = chunks * pairs
    field = shape_of(chunks, sheets, rows, LANES)
    return pl.pallas_call(
        functools.partial(finish_prepare_kernel, len(ties) + 1),
        out_shape=[field, field],
        scratch_shapes=[
            pltpu.VMEM((2, 2, lines, LANES), F32),
            pltpu.VMEM((2, 2, lines * SUBLANES, LANES), F32),
            pltpu.VMEM((2, pairs, columns, LANES), F32),
        ],
        compiler_params=params(),
        cost_estimate=pl.CostEstimate(flops=12 * t.size, bytes_accessed=20 * t.size, transcendentals=0),
    )(*ties, yw, yh, yp, inner, inner_own, outer, outer_own, zw, zi, t, to_x)


def finish_kernel(stages, own, got, base, response, zw, zi, to_x, out, o_s, sems):
    chunks, sheets, rows, _ = base.shape
    each = LANES // rows
    pairs = sheets // each
    flux = top_flux("gy", stages, own, got)
    spread = [
        turned(to_x[...], flux[m : m + 1, :], LANES) for m in range(pairs)
    ]
    started = []
    block = rows // OUT_COPIES
    for n in range(OUT_COPIES):
        strip = slice(n * block, (n + 1) * block)
        for y in range(chunks):

            def field(z):
                at = z % each * rows + strip.start
                return response[y, z, strip, :] * spread[z // each][at : at + block, :]

            def keep(z, value):
                o_s[z, strip, part_of(y)] = base[y, z, strip, :] + value

            z_solve(zw, zi, field, (y, strip), keep)
        at = pl.ds(strip.start, block)
        copy = pltpu.make_async_copy(o_s.at[:, at, :], out.at[:, at, :], sems.at[n])
        copy.start()
        started.append(copy)
    for copy in started:
        copy.wait()


def finish(own, got, base, response, zw, zi, to_x):
    chunks, sheets, rows, _ = base.shape
    shape = (sheets, rows, chunks * LANES)
    return pl.pallas_call(
        functools.partial(finish_kernel, stages_of("gy")),
        out_shape=shape_of(*shape),
        out_specs=ANYWHERE,
        scratch_shapes=[pltpu.VMEM(shape, F32), pltpu.SemaphoreType.DMA((OUT_COPIES,))],
        compiler_params=params(),
    )(own, got, base, response, zw, zi, to_x)


def per_device(temperature, base, locations, energy):
    columns = temperature.shape[2]
    gy = lax.axis_size("gy")
    t, b, loc, heat, packed = load(temperature, base, locations[None], energy[None])
    near = swap(packed, "gy", 1)
    far = lax.ppermute(packed, "gy", [(i, ((i + 1) % gy ^ 1) - 1 if i else gy - 1) for i in range(gy)])
    c, total, xw, xi, xp, x_links, x_view, xm, ends, t_steps, swapped = x_factor(loc, heat, t, b, columns * gy, packed)
    xh, x_own, view = x_target(swapped, total, near, far, xw, xi, xp, x_links, x_view, ends)
    yw, yi, yp, inner, outer, y_view, to_y, to_x, unit_low, unit_high = y_factor(c, x_view)
    zw, zi = z_factor(c, view)
    own, got, ties = gather_line(view, "gx", 2, (y_view, zw))
    base, response, to_first, to_last, fixed = y_prepare(
        ties, xw, xh, xm, xp, x_links, x_own, t_steps, to_y, unit_low, unit_high
    )
    flux, view = y_target(own, got, to_first, to_last, fixed, y_view)
    yh, inner_own, outer_own = y_eliminate(
        base, response, flux, to_y, yw, yi, yp, inner, outer, view
    )
    own, got, ties = gather_line(view, "gy", meanwhile=(yh,), cross=True)
    base, response = finish_prepare(
        ties, yw, yh, yp, inner, inner_own, outer, outer_own, zw, zi, t, to_x
    )
    return finish(own, got, base, response, zw, zi, to_x)


def solution(mesh):
    in_specs = (P(None, "gx", "gy"), P(None, "gx", "gy"), P(), P())
    out_specs = P(None, "gx", "gy")
    return jax.shard_map(
        per_device, mesh=mesh, in_specs=in_specs, out_specs=out_specs, check_vma=False
    )
```

```python
import functools

import jax
import jax.numpy as jnp
from jax import lax
from jax.experimental import pallas as pl
from jax.experimental.pallas import tpu as pltpu
from jax.sharding import PartitionSpec as P

RATE = 2000.0
THERMAL_GROWTH = 0.8
LANES = 128
SUBLANES = 8
F32 = jnp.float32
MIB = 1024 * 1024
OUT_COPIES = 2
ANYWHERE = pl.BlockSpec(memory_space=pl.ANY)
IN_HBM = pl.BlockSpec(memory_space=pltpu.HBM)
IN_VMEM = pl.BlockSpec(memory_space=pltpu.VMEM)

R00, R0L, RLL, FIRST, LAST, C0, CL = range(7)
COEFS = (R00, R0L, RLL, C0, CL)


def params(limit=40):
    return pltpu.CompilerParams(vmem_limit_bytes=limit * MIB)


def shape_of(*sizes):
    return jax.ShapeDtypeStruct(sizes, F32)


def half_conduct(base, temperature):
    return base * (0.5 * RATE + (0.5 * RATE * THERMAL_GROWTH) * temperature)


def inverse(x):
    guess = pl.reciprocal(x, approx=True)
    return guess * (2.0 - x * guess)


def join_coefs(a, b):
    face = a[CL] + b[C0]
    inv = face * inverse(1.0 + face * (a[RLL] + b[R00]))
    left = a[R0L] * inv
    right = b[R0L] * inv
    joined = {
        R00: a[R00] - left * a[R0L],
        R0L: left * b[R0L],
        RLL: b[RLL] - right * b[R0L],
        C0: a[C0],
        CL: b[CL],
    }
    return joined, (inv, right, left)


def join_targets(a, b, links):
    inv, right, left = links
    jump = b[0] - a[1]
    return (a[0] + left * jump, b[1] - right * jump), jump * inv


def between(own, right, left, low, high):
    return own + right * high - left * low


def tree(items, join):
    levels = []
    while len(items) > 1:
        pairs = [join(items[i], items[i + 1]) for i in range(0, len(items), 2)]
        items = [p[0] for p in pairs]
        levels.append([p[1] for p in pairs])
    return items[0], levels


def descend(levels, low, high):
    ends = [(low, high)]
    for level in reversed(levels):
        below = []
        for (lo, hi), (own, right, left) in zip(ends, level):
            flux = between(own, right, left, lo, hi)
            below += [(lo, flux), (-flux, hi)]
        ends = below
    return ends


def node_offsets(leaves):
    offsets, at, count = [], 0, leaves // 2
    while count:
        offsets.append((at, count))
        at += count
        count //= 2
    return offsets


def factor(cond, steps, keep):
    here = cond(0)
    c_first = here
    one = jnp.ones_like(here)
    ground, path, first_first = one, one, None
    for k in range(steps - 1):
        following = cond(k + 1)
        face = here + following
        inv = inverse(ground + face)
        w = face * inv
        p = path * inv
        keep(k, w, inv, p)
        step = path * p
        first_first = step if first_first is None else first_first + step
        path = path * w
        ground = 1.0 + w * ground
        here = following
    inv = inverse(ground)
    p = path * inv
    keep(steps - 1, inv, inv, p)
    return {R00: first_first + path * p, R0L: p, RLL: inv, C0: c_first, CL: here}


def eliminate(target, steps, w, inv, p, keep):
    rhs = target(0)
    first = None
    for k in range(steps):
        h = rhs * inv(k)
        keep(k, h)
        step = rhs * p(k)
        first = step if first is None else first + step
        if k < steps - 1:
            rhs = target(k + 1) + w(k) * rhs
    return first, h


def is_odd(axis):
    return lax.axis_index(axis) % 2 == 1


def fold(cells, used):
    steps = cells.shape[0] // SUBLANES
    total = cells[pl.ds(0, SUBLANES, stride=steps), :]
    lane = lax.broadcasted_iota(jnp.int32, total.shape, 1)
    for k in range(1, steps):
        part = pltpu.roll(cells[pl.ds(k, SUBLANES, stride=steps), :], k * used, 1)
        total = jnp.where(lane // used == k, part, total)
    return total


def load_kernel(t_hbm, b_hbm, loc_hbm, energy_hbm, t_out, b_out, loc, energy, packed, cells, sems):
    sheets, rows, columns = t_hbm.shape
    parts = [(0, LANES), (columns - LANES, LANES), (LANES, columns - 2 * LANES)]
    copies = []
    for n, (start, size) in enumerate(parts):
        part = pl.ds(start, size)
        for i, (src, dst) in enumerate(((t_hbm, t_out), (b_hbm, b_out))):
            copies.append(
                pltpu.make_async_copy(src.at[:, :, part], dst.at[:, :, part], sems.at[i, n])
            )
    copies.append(pltpu.make_async_copy(loc_hbm, loc, sems.at[2, 0]))
    copies.append(pltpu.make_async_copy(energy_hbm, energy, sems.at[2, 1]))
    for copy in copies:
        copy.start()
    lane = lax.broadcasted_iota(jnp.int32, (rows, LANES), 1)
    edge_t = jnp.zeros((rows, LANES), F32)
    edge_c = edge_t
    for side, source in enumerate((0, LANES - 1)):
        for copy in copies[2 * side : 2 * side + 2]:
            copy.wait()
        part = slice(parts[side][0], parts[side][0] + LANES)
        for z in range(sheets):
            t = t_out[z, :, part]
            c = half_conduct(b_out[z, :, part], t)
            place = lane == sheets * side + z
            edge_t = jnp.where(place, t[:, source : source + 1], edge_t)
            edge_c = jnp.where(place, c[:, source : source + 1], edge_c)
    cells[0], cells[1] = edge_t, edge_c
    for i in range(2):
        packed[i * SUBLANES : (i + 1) * SUBLANES, :] = fold(cells.at[i], 2 * sheets)
    for copy in copies[4:]:
        copy.wait()


def load(temperature, base, locations, energy):
    sheets, rows, columns = temperature.shape
    assert rows // SUBLANES * 2 * sheets <= LANES and columns > 2 * LANES
    operands = (temperature, base, locations, energy)
    return pl.pallas_call(
        load_kernel,
        in_specs=[IN_HBM] * 4,
        out_shape=[pltpu.VMEM(v.shape, v.dtype) for v in operands]
        + [pltpu.VMEM((2 * SUBLANES, LANES), F32)],
        scratch_shapes=[pltpu.VMEM((2, rows, LANES), F32), pltpu.SemaphoreType.DMA((3, 3))],
        compiler_params=params(),
    )(*[pltpu.with_memory_space_constraint(v, pltpu.HBM) for v in operands])


def source_plane(loc, energy, rows, columns, plate):
    place = loc[...]
    count = place.shape[1]
    local_x = place // plate - lax.axis_index("gx") * rows
    local_y = place % plate - lax.axis_index("gy") * columns
    in_x = lax.broadcasted_iota(jnp.int32, (rows, count), 0) == local_x
    in_y = lax.broadcasted_iota(jnp.int32, (columns, count), 0) == local_y
    by_y = jnp.where(in_y, 1.0, 0.0).astype(jnp.bfloat16)
    left = energy[...]
    plane = None
    for _ in range(3):
        part = left.astype(jnp.bfloat16).astype(F32)
        left = left - part
        term = lax.dot_general(
            jnp.where(in_x, part, 0.0).astype(jnp.bfloat16),
            by_y,
            (((1,), (1,)), ((), ())),
            preferred_element_type=F32,
        )
        plane = term if plane is None else plane + term
    return plane


def part_of(y):
    return slice(y * LANES, (y + 1) * LANES)


def line_groups(chunks, sheets):
    order = [0, chunks - 1] + list(range(1, chunks - 1))
    return [[(y, z) for y in order[i : i + 2] for z in range(sheets)] for i in range(0, chunks, 2)]


def x_eliminate(cells, members, first_line, w_ref, i_ref, p_ref, h_ref, h_line, q_s):
    steps = w_ref.shape[0]
    at = slice(first_line, first_line + len(members))
    kept_at = slice(h_line, h_line + len(members))

    def target(k):
        return jnp.stack([cells(y, z, k) for y, z in members], 0)

    def keep(k, h):
        h_ref[k, kept_at] = h

    ends = eliminate(
        target, steps, lambda k: w_ref[k, at], lambda k: i_ref[k, at], lambda k: p_ref[k, at], keep
    )
    for q in range(2):
        for i in range(len(members)):
            first = (first_line + i) * SUBLANES
            q_s[q, first : first + SUBLANES, :] = ends[q][i]


def x_factor_kernel(plate, loc, energy, t_ref, b_ref, own_cells, *refs):
    c_ref, total_ref, w_ref, i_ref, p_ref, links, view, h_ref, ends_ref, t_out, swapped, q_s, t_s = refs
    chunks, sheets, rows, _ = c_ref.shape
    lines = chunks * sheets
    steps = rows // SUBLANES
    plane = source_plane(loc, energy, rows, chunks * LANES, plate)
    mine = own_cells[...]
    in_low = lax.broadcasted_iota(jnp.int32, mine.shape, 1) % (2 * sheets) < sheets
    swapped[...] = jnp.where(
        in_low, pltpu.roll(mine, LANES - sheets, 1), pltpu.roll(mine, sheets, 1)
    )

    lane = lax.broadcasted_iota(jnp.int32, (SUBLANES, LANES), 1)
    is_first, is_last = lane == 0, lane == LANES - 1
    for r in range(steps):
        at = slice(r * SUBLANES, (r + 1) * SUBLANES)
        before_t, before_c = None, None
        for z in range(sheets):
            ts = [t_ref[z, at, part_of(y)] for y in range(chunks)]
            cs = [half_conduct(b_ref[z, at, part_of(y)], ts[y]) for y in range(chunks)]
            t_turned = [pltpu.roll(v, LANES - 1, 1) for v in ts]
            c_turned = [pltpu.roll(v, LANES - 1, 1) for v in cs]
            flux = []
            for y in range(chunks):
                if y < chunks - 1:
                    t_next = jnp.where(is_last, t_turned[y + 1], t_turned[y])
                    c_next = jnp.where(is_last, c_turned[y + 1], c_turned[y])
                    flux.append((cs[y] + c_next) * (t_next - ts[y]))
                else:
                    inside = (cs[y] + c_turned[y]) * (t_turned[y] - ts[y])
                    flux.append(jnp.where(is_last, 0.0, inside))
            turned = [pltpu.roll(v, 1, 1) for v in flux]
            for y in range(chunks):
                from_low = jnp.where(is_first, turned[y - 1] if y else 0.0, turned[y])
                total = ts[y] + (flux[y] - from_low)
                if z == 0:
                    total = total + plane[at, part_of(y)]
                else:
                    across = (before_c[y] + cs[y]) * (ts[y] - before_t[y])
                    total = total - across
                    total_ref[y, z - 1, at, :] += across
                total_ref[y, z, at, :] = total
                c_ref[y, z, at, :] = cs[y]
                t_s[y, z, at, :] = ts[y]
            before_t, before_c = ts, cs

    at = 0
    for n, members in enumerate(line_groups(chunks, sheets)):

        def cond(k):
            return jnp.stack([c_ref[y, z, pl.ds(k, SUBLANES, stride=steps), :] for y, z in members], 0)

        def keep(k, w, inv, p):
            w_ref[k, at : at + len(members)] = w
            i_ref[k, at : at + len(members)] = inv
            p_ref[k, at : at + len(members)] = p

        block = factor(cond, steps, keep)
        for i, q in enumerate(COEFS):
            for j in range(len(members)):
                first = (at + j) * SUBLANES
                q_s[i, first : first + SUBLANES, :] = block[q][j]
        if n > 0:
            x_eliminate(
                lambda y, z, k: total_ref[y, z, pl.ds(k, SUBLANES, stride=steps), :],
                members, at, w_ref, i_ref, p_ref, h_ref, at - 2 * sheets, ends_ref,
            )
        for k in range(steps):
            for i, (y, z) in enumerate(members):
                t_out[k, at + i] = t_s[y, z, pl.ds(k, SUBLANES, stride=steps), :]
        at += len(members)

    segments = [
        {q: q_s[n, pl.ds(s, lines, stride=SUBLANES), :] for n, q in enumerate(COEFS)}
        for s in range(SUBLANES)
    ]
    whole, levels = tree(segments, join_coefs)
    for (offset, _), level in zip(node_offsets(SUBLANES), levels):
        for n, values in enumerate(level):
            for i in range(3):
                links[offset + n, i] = values[i]
    for n, q in enumerate(COEFS):
        view[n] = whole[q]


def x_factor(loc, energy, t, b, plate, own_cells):
    sheets, rows, columns = t.shape
    chunks = columns // LANES
    lines = chunks * sheets
    steps = rows // SUBLANES
    field = shape_of(chunks, sheets, rows, LANES)
    stored = shape_of(steps, lines, SUBLANES, LANES)
    return pl.pallas_call(
        functools.partial(x_factor_kernel, plate),
        in_specs=[IN_VMEM] * 5,
        out_shape=[
            field,
            field,
            stored,
            stored,
            stored,
            shape_of(SUBLANES - 1, 3, lines, LANES),
            shape_of(len(COEFS), lines, LANES),
            shape_of(steps, max(1, lines - 2 * sheets), SUBLANES, LANES),
            shape_of(2, lines * SUBLANES, LANES),
            stored,
            shape_of(*own_cells.shape),
        ],
        scratch_shapes=[
            pltpu.VMEM((len(COEFS), lines * SUBLANES, LANES), F32),
            pltpu.VMEM((chunks, sheets, rows, LANES), F32),
        ],
        compiler_params=params(),
        cost_estimate=pl.CostEstimate(flops=40 * t.size, bytes_accessed=28 * t.size, transcendentals=0),
    )(loc, energy, t, b, own_cells)


def x_target_kernel(own_cells, total_ref, near, far, *refs):
    w_ref, i_ref, p_ref, links, view, ends_ref, h_ref, own, send, q_s = refs
    chunks, sheets, rows, _ = total_ref.shape
    lines = chunks * sheets
    steps = rows // SUBLANES

    place = lax.axis_index("gy")
    inner = (place > 0) & (place < lax.axis_size("gy") - 1)
    lane = lax.broadcasted_iota(jnp.int32, (SUBLANES, LANES), 1)
    side = 2 * sheets
    is_near = (lane % side >= sheets).astype(jnp.int32) == place % 2
    t, c = (
        jnp.where(is_near, near[at, :], jnp.where(inner, far[at, :], 0.0))
        for at in (slice(0, SUBLANES), slice(SUBLANES, 2 * SUBLANES))
    )
    face = jnp.where(c > 0.0, own_cells[SUBLANES:, :] + c, 0.0)
    flux = face * (t - own_cells[:SUBLANES, :])

    def cells(y, z, k):
        at = k * side + (sheets + z if y == 0 else z)
        edge = 0 if y == 0 else LANES - 1
        inflow = jnp.where(lane == edge, flux[:, at : at + 1], 0.0)
        return total_ref[y, z, pl.ds(k, SUBLANES, stride=steps), :] + inflow

    members = line_groups(chunks, sheets)[0]
    x_eliminate(cells, members, 0, w_ref, i_ref, p_ref, h_ref, 0, q_s)
    split = len(members)
    items = [
        tuple(
            jnp.concatenate(
                [
                    q_s[q, pl.ds(s, split, stride=SUBLANES), :],
                    ends_ref[q, pl.ds(split * SUBLANES + s, lines - split, stride=SUBLANES), :],
                ],
                0,
            )
            for q in range(2)
        )
        for s in range(SUBLANES)
    ]
    for offset, count in node_offsets(SUBLANES):
        joined = []
        for n in range(count):
            ties = tuple(links[offset + n, i] for i in range(3))
            both, flux = join_targets(items[2 * n], items[2 * n + 1], ties)
            own[offset + n] = flux
            joined.append(both)
        items = joined
    for n, q in enumerate(COEFS):
        send[q] = view[n]
    send[FIRST], send[LAST] = items[0]


def x_target(own_cells, total, near, far, w, inv, p, links, view, ends):
    chunks, sheets, rows, _ = total.shape
    lines = chunks * sheets
    steps = rows // SUBLANES
    return pl.pallas_call(
        x_target_kernel,
        out_shape=[
            shape_of(steps, 2 * sheets, SUBLANES, LANES),
            shape_of(SUBLANES - 1, lines, LANES),
            shape_of(7, lines, LANES),
        ],
        scratch_shapes=[
            pltpu.VMEM((2, 2 * sheets * SUBLANES, LANES), F32),
        ],
        compiler_params=params(),
    )(own_cells, total, near, far, w, inv, p, links, view, ends)


def stages_of(axis):
    return lax.axis_size(axis).bit_length() - 1


def swap(value, axis, flip):
    count = lax.axis_size(axis)
    return lax.ppermute(value, axis, [(i, i ^ flip) for i in range(count)])


def on_right(axis, stage):
    return (lax.axis_index(axis) >> stage) % 2 == 1


def toward(right, block):
    return (
        jnp.where(right, block[R00], block[RLL]),
        jnp.where(right, block[FIRST], block[LAST]),
        jnp.where(right, block[C0], block[CL]),
    )


def join(a, b):
    joined, ties = join_coefs(a, b)
    (joined[FIRST], joined[LAST]), flux = join_targets((a[FIRST], a[LAST]), (b[FIRST], b[LAST]), ties)
    return joined, (flux, ties[1], ties[2])


def ordered(right, own, other):
    first = [jnp.where(right, theirs, mine) for mine, theirs in zip(own, other)]
    second = [jnp.where(right, mine, theirs) for mine, theirs in zip(own, other)]
    return first, second


def join_kernel(axis, stage, width, last, *refs):
    count = 1 << width
    blocks = [[refs[i][q] for q in range(7)] for i in range(count)]
    send = refs[-1 - width]
    links = refs[-width:]
    for bit in range(width):
        right = on_right(axis, stage + bit)
        for i in range(count):
            if not i >> bit & 1:
                j = i | 1 << bit
                blocks[i], blocks[j] = ordered(right, blocks[i], blocks[j])
    for bit in range(width):
        pairs = [join(blocks[i], blocks[i + 1]) for i in range(0, len(blocks), 2)]
        blocks = [p[0] for p in pairs]
        ties = [p[1] for p in pairs]
        for upper in range(bit + 1, width):
            right = on_right(axis, stage + upper)
            ties = [
                tuple(jnp.where(right, v, u) for u, v in zip(ties[i], ties[i + 1]))
                for i in range(0, len(ties), 2)
            ]
        for i in range(3):
            links[bit][i] = ties[0][i]
    (whole,) = blocks
    if last:
        for n, value in enumerate(toward(on_right(axis, stage + width), whole)):
            send[n] = value
    else:
        for q in range(7):
            send[q] = whole[q]


def join_stage(own, got, axis, stage, width, last, after):
    lines = own.shape[1]
    return pl.pallas_call(
        functools.partial(join_kernel, axis, stage, width, last),
        in_specs=[IN_VMEM] * (1 + len(got)) + [ANYWHERE] * len(after),
        out_shape=[shape_of(3 if last else 7, lines, LANES)] + [shape_of(3, lines, LANES)] * width,
        compiler_params=params(),
    )(own, *got, *after)


def gather_line(view, axis, widest=1, meanwhile=(), cross=False):
    stages = stages_of(axis)
    links, stage = [], 0
    while stage < stages - 1:
        width = min(widest, stages - 1 - stage)
        got = [swap(view, axis, flip << stage) for flip in range(1, 1 << width)]
        last = stage + width == stages - 1
        view, *ties = join_stage(view, got, axis, stage, width, last, meanwhile)
        links += ties
        stage += width
        meanwhile = ()
    return view, swap(view, axis, 1 << stage | (cross and stage > 0)), links


def top_flux(axis, stages, own, got):
    right = on_right(axis, stages - 1)
    face = own[2] + got[2]
    jump = jnp.where(right, own[1] - got[1], got[1] - own[1])
    return jump * face * inverse(1.0 + face * (own[0] + got[0]))


def block_ends(axis, stages, links):
    shape = links[0].shape[1:] if links else None
    right = on_right(axis, stages - 1)
    zero = jnp.zeros(shape, F32)
    low, high = zero, zero
    unit_low = zero + jnp.where(right, -1.0, 0.0)
    unit_high = zero + jnp.where(right, 0.0, 1.0)
    for stage in range(stages - 2, -1, -1):
        tie = links[stage]
        right = on_right(axis, stage)
        flux = between(tie[0], tie[1], tie[2], low, high)
        unit = between(0.0, tie[1], tie[2], unit_low, unit_high)
        low, high = jnp.where(right, -flux, low), jnp.where(right, high, flux)
        unit_low, unit_high = jnp.where(right, -unit, unit_low), jnp.where(right, unit_high, unit)
    return (low, high), (unit_low, unit_high)


def natural(index, parts):
    span = SUBLANES * parts
    local = index % span
    return index - local + local % SUBLANES * parts + local // SUBLANES


def turn_matrix(shape, from_natural, parts):
    row = lax.broadcasted_iota(jnp.int32, shape, 0)
    column = lax.broadcasted_iota(jnp.int32, shape, 1) % LANES
    hit = natural(row, parts) == column if from_natural else row == natural(column, parts)
    return jnp.where(hit, 1.0, 0.0).astype(jnp.bfloat16)


def turned(matrix, field, rows=None):
    high = field.astype(jnp.bfloat16).astype(F32)
    both = jnp.concatenate([high, field - high], 1)
    if rows:
        both = jnp.concatenate(
            [jnp.broadcast_to(both[n : n + 1, :], (rows, 2 * LANES)) for n in range(field.shape[0])], 0
        )
    both = both.astype(jnp.bfloat16)
    return lax.dot_general(
        matrix, both, (((1,), (1,)), ((), ())), preferred_element_type=F32
    )


def y_factor_kernel(c_ref, after, w_ref, i_ref, p_ref, inner, outer, view, to_y, to_x, unit_low, unit_high, c_s, q_s, r_s):
    chunks, sheets, rows, _ = c_ref.shape
    each = LANES // rows
    pairs = sheets // each
    x_steps = rows // SUBLANES
    steps = LANES // SUBLANES
    to_y[...] = turn_matrix(to_y.shape, True, steps)
    to_x[...] = turn_matrix(to_x.shape, False, x_steps)
    for m in range(pairs):
        for y in range(chunks):
            block = jnp.concatenate(
                [
                    c_ref[y, m * each + i, pl.ds(k, SUBLANES, stride=x_steps), :]
                    for i in range(each)
                    for k in range(x_steps)
                ],
                0,
            )
            c_s[m, part_of(y), :] = block.T

    members = [(y, m) for y in range(chunks) for m in range(pairs)]
    lines = len(members)

    def cond(k):
        return jnp.stack([c_s[m, pl.ds(y * LANES + k, SUBLANES, stride=steps), :] for y, m in members], 0)

    def keep(k, w, inv, p):
        w_ref[k] = w
        i_ref[k] = inv
        p_ref[k] = p

    block = factor(cond, steps, keep)
    for n, q in enumerate(COEFS):
        for i in range(lines):
            q_s[n, i * SUBLANES : (i + 1) * SUBLANES, :] = block[q][i]
    segments = [
        {q: q_s[n, pl.ds(s, lines, stride=SUBLANES), :] for n, q in enumerate(COEFS)}
        for s in range(SUBLANES)
    ]
    whole, levels = tree(segments, join_coefs)
    for (offset, _), level in zip(node_offsets(SUBLANES), levels):
        for n, values in enumerate(level):
            for i in range(3):
                inner[offset + n, i] = values[i]
    for n, q in enumerate(COEFS):
        r_s[n] = whole[q]
    parts = [
        {q: r_s[n, y * pairs : (y + 1) * pairs, :] for n, q in enumerate(COEFS)} for y in range(chunks)
    ]
    whole, levels = tree(parts, join_coefs)
    for (offset, _), level in zip(node_offsets(chunks), levels):
        for n, values in enumerate(level):
            for i in range(3):
                outer[offset + n, i] = values[i]
    for n, q in enumerate(COEFS):
        view[n] = whole[q]

    same = turn_matrix(to_y.shape, True, 1)
    one = jnp.ones((pairs, LANES), F32)
    for n, (low, high, field) in enumerate(((one, 0.0 * one, unit_low), (0.0 * one, one, unit_high))):
        for y, pair in enumerate(tree_ends(chunks, outer, nothing, low, high)):
            for i in range(2):
                r_s[2 * n + i, y * pairs : (y + 1) * pairs, :] = pair[i]
        for s, pair in enumerate(tree_ends(SUBLANES, inner, nothing, r_s[2 * n], r_s[2 * n + 1])):
            for i in range(2):
                q_s[2 * n + i, pl.ds(s, lines, stride=SUBLANES), :] = pair[i]
        low, value = (
            jnp.stack(
                [q_s[2 * n + i, j * SUBLANES : (j + 1) * SUBLANES, :] for j in range(lines)], 0
            )
            for i in range(2)
        )
        for k in range(steps - 1, -1, -1):
            value = w_ref[k] * value + p_ref[k] * low
            for j, (y, m) in enumerate(members):
                c_s[m, pl.ds(y * LANES + k, SUBLANES, stride=steps), :] = value[j]
        for y, m in members:
            field[y, part_of(m), :] = turned(same, c_s[m, part_of(y), :])


def y_factor(c, after):
    chunks, sheets, rows, _ = c.shape
    pairs = sheets * rows // LANES
    lines = chunks * pairs
    stored = shape_of(LANES // SUBLANES, lines, SUBLANES, LANES)
    matrix = jax.ShapeDtypeStruct((LANES, 2 * LANES), jnp.bfloat16)
    return pl.pallas_call(
        y_factor_kernel,
        in_specs=[IN_VMEM, ANYWHERE],
        out_shape=[
            stored,
            stored,
            stored,
            shape_of(SUBLANES - 1, 3, lines, LANES),
            shape_of(chunks - 1, 3, pairs, LANES),
            shape_of(len(COEFS), pairs, LANES),
            matrix,
            matrix,
            shape_of(chunks, pairs * LANES, LANES),
            shape_of(chunks, pairs * LANES, LANES),
        ],
        scratch_shapes=[
            pltpu.VMEM((pairs, chunks * LANES, LANES), F32),
            pltpu.VMEM((len(COEFS), lines * SUBLANES, LANES), F32),
            pltpu.VMEM((len(COEFS), lines, LANES), F32),
        ],
        compiler_params=params(),
        cost_estimate=pl.CostEstimate(flops=20 * c.size, bytes_accessed=16 * c.size, transcendentals=0),
    )(c, after)


def z_factor_kernel(c_ref, after, w_ref, i_ref):
    sheets = c_ref.shape[1]
    ground = 1.0
    for z in range(sheets - 1):
        face = c_ref[:, z] + c_ref[:, z + 1]
        inv = inverse(ground + face)
        w = face * inv
        i_ref[z] = inv
        w_ref[z] = w
        ground = 1.0 + w * ground
    i_ref[sheets - 1] = inverse(ground)


def z_factor(c, after):
    chunks, sheets, rows, _ = c.shape
    return pl.pallas_call(
        z_factor_kernel,
        in_specs=[IN_VMEM, ANYWHERE],
        out_shape=[
            shape_of(sheets - 1, chunks, rows, LANES),
            shape_of(sheets, chunks, rows, LANES),
        ],
        compiler_params=params(),
        cost_estimate=pl.CostEstimate(flops=10 * c.size, bytes_accessed=12 * c.size, transcendentals=0),
    )(c, after)


def join_tree(items, links, own):
    for offset, count in node_offsets(len(items)):
        joined = []
        for n in range(count):
            tie = tuple(links[offset + n, i] for i in range(3))
            both, flux = join_targets(items[2 * n], items[2 * n + 1], tie)
            own[offset + n] = flux
            joined.append(both)
        items = joined
    return items[0]


def tree_ends(leaves, links, own, low, high):
    levels = [
        [(own(offset + n), links[offset + n, 1], links[offset + n, 2]) for n in range(count)]
        for offset, count in node_offsets(leaves)
    ]
    return descend(levels, low, high)


def nothing(node):
    return 0.0


def y_prepare_kernel(stages, *refs):
    ties = refs[: stages - 1]
    xw, xh, xm, xp, x_links, x_own, t_ref, to_y, y_low, y_high = refs[stages - 1 : stages + 9]
    base, response, to_first, to_last, fixed, f_s, g_s = refs[stages + 9 :]
    x_steps, lines = xw.shape[:2]
    chunks = base.shape[0]
    sheets = lines // chunks
    rows = x_steps * SUBLANES

    ends, units = block_ends("gx", stages, ties)
    for n, (own, (low, high)) in enumerate(((lambda i: x_own[i], ends), (nothing, units))):
        for s, pair in enumerate(tree_ends(SUBLANES, x_links, own, low, high)):
            for i in range(2):
                f_s[n, i, pl.ds(s, lines, stride=SUBLANES), :] = pair[i]
    first = 0
    for n, members in enumerate(line_groups(chunks, sheets)):
        at = slice(first, first + len(members))
        h_ref_of, h_at = (xh, at) if n == 0 else (xm, slice(first - 2 * sheets, at.stop - 2 * sheets))
        (low, value), (unit_low, unit) = (
            [
                jnp.stack(
                    [f_s[q, i, j * SUBLANES : (j + 1) * SUBLANES, :] for j in range(at.start, at.stop)], 0
                )
                for i in range(2)
            ]
            for q in range(2)
        )
        for k in range(x_steps - 1, -1, -1):
            w, p = xw[k, at], xp[k, at]
            value = w * value + (h_ref_of[k, h_at] + p * low)
            unit = w * unit + p * unit_low
            field = value - t_ref[k, at]
            for j, (y, z) in enumerate(members):
                place = z * rows + k * SUBLANES
                g_s[0, y, place : place + SUBLANES, :] = field[j]
                g_s[1, y, place : place + SUBLANES, :] = unit[j]
        first = at.stop

    totals = [None, None]
    for y in range(chunks):
        base[y] = turned(to_y[...], g_s[0, y])
        response[y] = turned(to_y[...], g_s[1, y])
        for i, (unit, weight) in enumerate(((y_low, to_first), (y_high, to_last))):
            weight[y] = unit[y] * g_s[1, y]
            part = unit[y] * g_s[0, y]
            totals[i] = part if y == 0 else totals[i] + part
    for i in range(2):
        put_sums(fixed.at[i], totals[i])


def put_sums(out, field):
    ones = jnp.ones((2 * SUBLANES, 2 * LANES), jnp.bfloat16)
    total = turned(ones, field)
    for m in range(out.shape[0]):
        out[m : m + 1, :] = total[:1, part_of(m)]


def y_prepare(ties, xw, xh, xm, xp, x_links, x_own, t, to_y, unit_low, unit_high):
    chunks = unit_low.shape[0]
    x_steps, lines = xw.shape[:2]
    width = lines // chunks * x_steps * SUBLANES
    field, weight = shape_of(chunks, LANES, width), shape_of(chunks, width, LANES)
    return pl.pallas_call(
        functools.partial(y_prepare_kernel, len(ties) + 1),
        out_shape=[field] * 2 + [weight] * 2 + [shape_of(2, width // LANES, LANES)],
        scratch_shapes=[
            pltpu.VMEM((2, 2, lines * SUBLANES, LANES), F32),
            pltpu.VMEM((2, chunks, width, LANES), F32),
        ],
        compiler_params=params(),
        cost_estimate=pl.CostEstimate(flops=8 * t.size, bytes_accessed=16 * t.size, transcendentals=0),
    )(*ties, xw, xh, xm, xp, x_links, x_own, t, to_y, unit_low, unit_high)


def sheet_rows(values, y, chunks, sheets):
    line_of = {member: n for n, member in enumerate(sum(line_groups(chunks, sheets), []))}
    return [values[line_of[y, z] : line_of[y, z] + 1, :] for z in range(sheets)]


def y_target_kernel(stages, own, got, to_first, to_last, fixed, view, flux_ref, send, r_s):
    chunks, width, _ = to_first.shape
    sheets = own.shape[1] // chunks
    rows = width // sheets

    flux = top_flux("gx", stages, own, got)
    flux_ref[...] = flux
    totals = [[None] * sheets, [None] * sheets]
    for y in range(chunks):
        for z, row in enumerate(sheet_rows(flux, y, chunks, sheets)):
            for total, weight in zip(totals, (to_first, to_last)):
                part = weight[y, z * rows : (z + 1) * rows, :] * row
                total[z] = part if y == 0 else total[z] + part
    for n, q in enumerate(COEFS):
        send[q] = view[n]
    for i, q in enumerate((FIRST, LAST)):
        put_sums(r_s.at[i], jnp.concatenate(totals[i], 0))
        send[q] = fixed[i] + r_s[i]


def y_target(own, got, to_first, to_last, fixed, view):
    pairs = view.shape[1]
    return pl.pallas_call(
        functools.partial(y_target_kernel, stages_of("gx")),
        out_shape=[shape_of(*own.shape[1:]), shape_of(7, pairs, LANES)],
        scratch_shapes=[pltpu.VMEM((2, pairs, LANES), F32)],
        compiler_params=params(),
    )(own, got, to_first, to_last, fixed, view)


def y_eliminate_kernel(base, response, flux, to_y, yw, yi, yp, inner, outer, after, *refs):
    h_ref, inner_own, outer_own, q_s, r_s = refs
    chunks, _, width = base.shape
    pairs = width // LANES
    sheets = flux.shape[0] // chunks
    steps = yw.shape[0]
    members = [(y, m) for y in range(chunks) for m in range(pairs)]
    fields = []
    for y in range(chunks):
        by_sheet = jnp.concatenate(sheet_rows(flux[...], y, chunks, sheets), 0)
        fields.append(base[y] + response[y] * turned(to_y[...], by_sheet, width // sheets))

    def target(k):
        at = slice(k * SUBLANES, (k + 1) * SUBLANES)
        return jnp.stack([fields[y][at, part_of(m)] for y, m in members], 0)

    def keep(k, h):
        h_ref[k] = h

    ends = eliminate(target, steps, lambda k: yw[k], lambda k: yi[k], lambda k: yp[k], keep)
    for q in range(2):
        for i in range(len(members)):
            q_s[q, i * SUBLANES : (i + 1) * SUBLANES, :] = ends[q][i]
    items = [
        tuple(q_s[q, pl.ds(s, len(members), stride=SUBLANES), :] for q in range(2))
        for s in range(SUBLANES)
    ]
    r_s[0], r_s[1] = join_tree(items, inner, inner_own)
    items = [tuple(r_s[q, y * pairs : (y + 1) * pairs, :] for q in range(2)) for y in range(chunks)]
    join_tree(items, outer, outer_own)


def y_eliminate(base, response, flux, to_y, yw, yi, yp, inner, outer, after):
    y_lines = yw.shape[1]
    pairs = outer.shape[2]
    chunks = y_lines // pairs
    return pl.pallas_call(
        y_eliminate_kernel,
        in_specs=[IN_VMEM] * 9 + [ANYWHERE],
        out_shape=[
            shape_of(*yw.shape),
            shape_of(SUBLANES - 1, y_lines, LANES),
            shape_of(chunks - 1, pairs, LANES),
        ],
        scratch_shapes=[
            pltpu.VMEM((2, y_lines * SUBLANES, LANES), F32),
            pltpu.VMEM((2, y_lines, LANES), F32),
        ],
        compiler_params=params(),
        cost_estimate=pl.CostEstimate(flops=8 * base.size, bytes_accessed=16 * base.size, transcendentals=0),
    )(base, response, flux, to_y, yw, yi, yp, inner, outer, after)


def z_solve(zw, zi, field, at, keep):
    sheets = zi.shape[0]
    rhs, kept = None, []
    for z in range(sheets):
        rhs = field(z) if z == 0 else field(z) + zw[(z - 1, *at)] * rhs
        kept.append(rhs * zi[(z, *at)])
    value = kept[-1]
    keep(sheets - 1, value)
    for z in range(sheets - 2, -1, -1):
        value = zw[(z, *at)] * value + kept[z]
        keep(z, value)


def finish_prepare_kernel(stages, *refs):
    ties = refs[: stages - 1]
    yw, yh, yp, inner, inner_own, outer, outer_own, zw, zi, t_ref, to_x = refs[stages - 1 : stages + 10]
    base, response, r_s, e_s, u_s = refs[stages + 10 :]
    chunks, sheets, rows, _ = base.shape
    each = LANES // rows
    pairs = sheets // each
    steps = yw.shape[0]
    lines = chunks * pairs

    ends, units = block_ends("gy", stages, ties)
    both = (
        (lambda i: outer_own[i], lambda i: inner_own[i], ends),
        (nothing, nothing, units),
    )
    for n, (upper, lower, (low, high)) in enumerate(both):
        for y, pair in enumerate(tree_ends(chunks, outer, upper, low, high)):
            for i in range(2):
                r_s[n, i, y * pairs : (y + 1) * pairs, :] = pair[i]
        for s, pair in enumerate(tree_ends(SUBLANES, inner, lower, r_s[n, 0], r_s[n, 1])):
            for i in range(2):
                e_s[n, i, pl.ds(s, lines, stride=SUBLANES), :] = pair[i]
    (low, value), (unit_low, unit) = (
        [
            jnp.stack([e_s[q, i, n * SUBLANES : (n + 1) * SUBLANES, :] for n in range(lines)], 0)
            for i in range(2)
        ]
        for q in range(2)
    )
    for k in range(steps - 1, -1, -1):
        w, p = yw[k], yp[k]
        value = w * value + (yh[k] + p * low)
        unit = w * unit + p * unit_low
        for y in range(chunks):
            for m in range(pairs):
                place = pl.ds(y * LANES + k, SUBLANES, stride=steps)
                u_s[0, m, place, :] = value[y * pairs + m]
                u_s[1, m, place, :] = unit[y * pairs + m]

    for y in range(chunks):
        part = part_of(y)
        fields = [turned(to_x[...], u_s[0, m, part, :]) for m in range(pairs)]

        def field(z):
            at = z % each * rows
            return fields[z // each][at : at + rows, :]

        def keep(z, value):
            base[y, z] = t_ref[z, :, part] + value

        z_solve(zw, zi, field, (y,), keep)
        for m in range(pairs):
            units = turned(to_x[...], u_s[1, m, part, :])
            for i in range(each):
                response[y, m * each + i] = units[i * rows : (i + 1) * rows, :]


def finish_prepare(ties, yw, yh, yp, inner, inner_own, outer, outer_own, zw, zi, t, to_x):
    sheets, rows, columns = t.shape
    chunks = columns // LANES
    pairs = sheets * rows // LANES
    lines = chunks * pairs
    field = shape_of(chunks, sheets, rows, LANES)
    return pl.pallas_call(
        functools.partial(finish_prepare_kernel, len(ties) + 1),
        out_shape=[field, field],
        scratch_shapes=[
            pltpu.VMEM((2, 2, lines, LANES), F32),
            pltpu.VMEM((2, 2, lines * SUBLANES, LANES), F32),
            pltpu.VMEM((2, pairs, columns, LANES), F32),
        ],
        compiler_params=params(),
        cost_estimate=pl.CostEstimate(flops=12 * t.size, bytes_accessed=20 * t.size, transcendentals=0),
    )(*ties, yw, yh, yp, inner, inner_own, outer, outer_own, zw, zi, t, to_x)


def finish_kernel(stages, own, got, base, response, zw, zi, to_x, out, o_s, sems):
    chunks, sheets, rows, _ = base.shape
    each = LANES // rows
    pairs = sheets // each
    flux = top_flux("gy", stages, own, got)
    spread = [
        turned(to_x[...], flux[m : m + 1, :], LANES) for m in range(pairs)
    ]
    started = []
    block = rows // OUT_COPIES
    for n in range(OUT_COPIES):
        strip = slice(n * block, (n + 1) * block)
        for y in range(chunks):

            def field(z):
                at = z % each * rows + strip.start
                return response[y, z, strip, :] * spread[z // each][at : at + block, :]

            def keep(z, value):
                o_s[z, strip, part_of(y)] = base[y, z, strip, :] + value

            z_solve(zw, zi, field, (y, strip), keep)
        at = pl.ds(strip.start, block)
        copy = pltpu.make_async_copy(o_s.at[:, at, :], out.at[:, at, :], sems.at[n])
        copy.start()
        started.append(copy)
    for copy in started:
        copy.wait()


def finish(own, got, base, response, zw, zi, to_x):
    chunks, sheets, rows, _ = base.shape
    shape = (sheets, rows, chunks * LANES)
    return pl.pallas_call(
        functools.partial(finish_kernel, stages_of("gy")),
        out_shape=shape_of(*shape),
        out_specs=ANYWHERE,
        scratch_shapes=[pltpu.VMEM(shape, F32), pltpu.SemaphoreType.DMA((OUT_COPIES,))],
        compiler_params=params(),
    )(own, got, base, response, zw, zi, to_x)


def per_device(temperature, base, locations, energy):
    columns = temperature.shape[2]
    gy = lax.axis_size("gy")
    t, b, loc, heat, packed = load(temperature, base, locations[None], energy[None])
    near = swap(packed, "gy", 1)
    far = lax.ppermute(packed, "gy", [(i, ((i + 1) % gy ^ 1) - 1 if i else gy - 1) for i in range(gy)])
    c, total, xw, xi, xp, x_links, x_view, xm, ends, t_steps, swapped = x_factor(loc, heat, t, b, columns * gy, packed)
    xh, x_own, view = x_target(swapped, total, near, far, xw, xi, xp, x_links, x_view, ends)
    yw, yi, yp, inner, outer, y_view, to_y, to_x, unit_low, unit_high = y_factor(c, x_view)
    zw, zi = z_factor(c, view)
    own, got, ties = gather_line(view, "gx", 2, (y_view, zw))
    base, response, to_first, to_last, fixed = y_prepare(
        ties, xw, xh, xm, xp, x_links, x_own, t_steps, to_y, unit_low, unit_high
    )
    flux, view = y_target(own, got, to_first, to_last, fixed, y_view)
    yh, inner_own, outer_own = y_eliminate(
        base, response, flux, to_y, yw, yi, yp, inner, outer, view
    )
    own, got, ties = gather_line(view, "gy", meanwhile=(yh,), cross=True)
    base, response = finish_prepare(
        ties, yw, yh, yp, inner, inner_own, outer, outer_own, zw, zi, t, to_x
    )
    return finish(own, got, base, response, zw, zi, to_x)


def solution(mesh):
    in_specs = (P(None, "gx", "gy"), P(None, "gx", "gy"), P(), P())
    out_specs = P(None, "gx", "gy")
    return jax.shard_map(
        per_device, mesh=mesh, in_specs=in_specs, out_specs=out_specs, check_vma=False
    )
```

```python
import functools

import jax
import jax.numpy as jnp
from jax import lax
from jax.experimental import pallas as pl
from jax.experimental.pallas import tpu as pltpu
from jax.sharding import PartitionSpec as P

RATE = 2000.0
THERMAL_GROWTH = 0.8
LANES = 128
SUBLANES = 8
F32 = jnp.float32
MIB = 1024 * 1024
OUT_COPIES = 4
ANYWHERE = pl.BlockSpec(memory_space=pl.ANY)
IN_HBM = pl.BlockSpec(memory_space=pltpu.HBM)
IN_VMEM = pl.BlockSpec(memory_space=pltpu.VMEM)

R00, R0L, RLL, FIRST, LAST, C0, CL = range(7)
COEFS = (R00, R0L, RLL, C0, CL)


def params(limit=40):
    return pltpu.CompilerParams(vmem_limit_bytes=limit * MIB)


def shape_of(*sizes):
    return jax.ShapeDtypeStruct(sizes, F32)


def half_conduct(base, temperature):
    return base * (0.5 * RATE + (0.5 * RATE * THERMAL_GROWTH) * temperature)


def inverse(x):
    guess = pl.reciprocal(x, approx=True)
    return guess * (2.0 - x * guess)


def join_coefs(a, b):
    face = a[CL] + b[C0]
    inv = face * inverse(1.0 + face * (a[RLL] + b[R00]))
    left = a[R0L] * inv
    right = b[R0L] * inv
    joined = {
        R00: a[R00] - left * a[R0L],
        R0L: left * b[R0L],
        RLL: b[RLL] - right * b[R0L],
        C0: a[C0],
        CL: b[CL],
    }
    return joined, (inv, right, left)


def join_targets(a, b, links):
    inv, right, left = links
    jump = b[0] - a[1]
    return (a[0] + left * jump, b[1] - right * jump), jump * inv


def between(own, right, left, low, high):
    return own + right * high - left * low


def tree(items, join):
    levels = []
    while len(items) > 1:
        pairs = [join(items[i], items[i + 1]) for i in range(0, len(items), 2)]
        items = [p[0] for p in pairs]
        levels.append([p[1] for p in pairs])
    return items[0], levels


def descend(levels, low, high):
    ends = [(low, high)]
    for level in reversed(levels):
        below = []
        for (lo, hi), (own, right, left) in zip(ends, level):
            flux = between(own, right, left, lo, hi)
            below += [(lo, flux), (-flux, hi)]
        ends = below
    return ends


def node_offsets(leaves):
    offsets, at, count = [], 0, leaves // 2
    while count:
        offsets.append((at, count))
        at += count
        count //= 2
    return offsets


def factor(cond, steps, keep):
    here = cond(0)
    c_first = here
    one = jnp.ones_like(here)
    ground, path, first_first = one, one, None
    for k in range(steps - 1):
        following = cond(k + 1)
        face = here + following
        inv = inverse(ground + face)
        w = face * inv
        p = path * inv
        keep(k, w, inv, p)
        step = path * p
        first_first = step if first_first is None else first_first + step
        path = path * w
        ground = 1.0 + w * ground
        here = following
    inv = inverse(ground)
    p = path * inv
    keep(steps - 1, inv, inv, p)
    return {R00: first_first + path * p, R0L: p, RLL: inv, C0: c_first, CL: here}


def eliminate(target, steps, w, inv, p, keep):
    rhs = target(0)
    first = None
    for k in range(steps):
        h = rhs * inv(k)
        keep(k, h)
        step = rhs * p(k)
        first = step if first is None else first + step
        if k < steps - 1:
            rhs = target(k + 1) + w(k) * rhs
    return first, h


def is_odd(axis):
    return lax.axis_index(axis) % 2 == 1


def fold(cells, used):
    steps = cells.shape[0] // SUBLANES
    total = cells[pl.ds(0, SUBLANES, stride=steps), :]
    lane = lax.broadcasted_iota(jnp.int32, total.shape, 1)
    for k in range(1, steps):
        part = pltpu.roll(cells[pl.ds(k, SUBLANES, stride=steps), :], k * used, 1)
        total = jnp.where(lane // used == k, part, total)
    return total


def load_kernel(t_hbm, b_hbm, loc_hbm, energy_hbm, t_out, b_out, loc, energy, packed, cells, sems):
    sheets, rows, columns = t_hbm.shape
    parts = [(0, LANES), (columns - LANES, LANES), (LANES, columns - 2 * LANES)]
    copies = []
    for n, (start, size) in enumerate(parts):
        part = pl.ds(start, size)
        for i, (src, dst) in enumerate(((t_hbm, t_out), (b_hbm, b_out))):
            copies.append(
                pltpu.make_async_copy(src.at[:, :, part], dst.at[:, :, part], sems.at[i, n])
            )
    copies.append(pltpu.make_async_copy(loc_hbm, loc, sems.at[2, 0]))
    copies.append(pltpu.make_async_copy(energy_hbm, energy, sems.at[2, 1]))
    for copy in copies:
        copy.start()
    lane = lax.broadcasted_iota(jnp.int32, (rows, LANES), 1)
    edge_t = jnp.zeros((rows, LANES), F32)
    edge_c = edge_t
    for side, source in enumerate((0, LANES - 1)):
        for copy in copies[2 * side : 2 * side + 2]:
            copy.wait()
        part = slice(parts[side][0], parts[side][0] + LANES)
        for z in range(sheets):
            t = t_out[z, :, part]
            c = half_conduct(b_out[z, :, part], t)
            place = lane == sheets * side + z
            edge_t = jnp.where(place, t[:, source : source + 1], edge_t)
            edge_c = jnp.where(place, c[:, source : source + 1], edge_c)
    cells[0], cells[1] = edge_t, edge_c
    for i in range(2):
        packed[i * SUBLANES : (i + 1) * SUBLANES, :] = fold(cells.at[i], 2 * sheets)
    for copy in copies[4:]:
        copy.wait()


def load(temperature, base, locations, energy):
    sheets, rows, columns = temperature.shape
    assert rows // SUBLANES * 2 * sheets <= LANES and columns > 2 * LANES
    operands = (temperature, base, locations, energy)
    return pl.pallas_call(
        load_kernel,
        in_specs=[IN_HBM] * 4,
        out_shape=[pltpu.VMEM(v.shape, v.dtype) for v in operands]
        + [pltpu.VMEM((2 * SUBLANES, LANES), F32)],
        scratch_shapes=[pltpu.VMEM((2, rows, LANES), F32), pltpu.SemaphoreType.DMA((3, 3))],
        compiler_params=params(),
    )(*[pltpu.with_memory_space_constraint(v, pltpu.HBM) for v in operands])


def source_plane(loc, energy, rows, columns, plate):
    place = loc[...]
    count = place.shape[1]
    local_x = place // plate - lax.axis_index("gx") * rows
    local_y = place % plate - lax.axis_index("gy") * columns
    in_x = lax.broadcasted_iota(jnp.int32, (rows, count), 0) == local_x
    in_y = lax.broadcasted_iota(jnp.int32, (columns, count), 0) == local_y
    by_y = jnp.where(in_y, 1.0, 0.0).astype(jnp.bfloat16)
    left = energy[...]
    plane = None
    for _ in range(3):
        part = left.astype(jnp.bfloat16).astype(F32)
        left = left - part
        term = lax.dot_general(
            jnp.where(in_x, part, 0.0).astype(jnp.bfloat16),
            by_y,
            (((1,), (1,)), ((), ())),
            preferred_element_type=F32,
        )
        plane = term if plane is None else plane + term
    return plane


def part_of(y):
    return slice(y * LANES, (y + 1) * LANES)


def line_groups(chunks, sheets):
    order = [0, chunks - 1] + list(range(1, chunks - 1))
    return [[(y, z) for y in order[i : i + 2] for z in range(sheets)] for i in range(0, chunks, 2)]


def x_eliminate(cells, members, first_line, w_ref, i_ref, p_ref, h_ref, h_line, q_s):
    steps = w_ref.shape[0]
    at = slice(first_line, first_line + len(members))
    kept_at = slice(h_line, h_line + len(members))

    def target(k):
        return jnp.stack([cells(y, z, k) for y, z in members], 0)

    def keep(k, h):
        h_ref[k, kept_at] = h

    ends = eliminate(
        target, steps, lambda k: w_ref[k, at], lambda k: i_ref[k, at], lambda k: p_ref[k, at], keep
    )
    for q in range(2):
        for i in range(len(members)):
            first = (first_line + i) * SUBLANES
            q_s[q, first : first + SUBLANES, :] = ends[q][i]


def x_factor_kernel(plate, loc, energy, t_ref, b_ref, own_cells, *refs):
    c_ref, total_ref, w_ref, i_ref, p_ref, links, view, h_ref, ends_ref, t_out, swapped, q_s, t_s = refs
    chunks, sheets, rows, _ = c_ref.shape
    lines = chunks * sheets
    steps = rows // SUBLANES
    plane = source_plane(loc, energy, rows, chunks * LANES, plate)
    mine = own_cells[...]
    in_low = lax.broadcasted_iota(jnp.int32, mine.shape, 1) % (2 * sheets) < sheets
    swapped[...] = jnp.where(
        in_low, pltpu.roll(mine, LANES - sheets, 1), pltpu.roll(mine, sheets, 1)
    )

    lane = lax.broadcasted_iota(jnp.int32, (SUBLANES, LANES), 1)
    is_first, is_last = lane == 0, lane == LANES - 1
    for r in range(steps):
        at = slice(r * SUBLANES, (r + 1) * SUBLANES)
        before_t, before_c = None, None
        for z in range(sheets):
            ts = [t_ref[z, at, part_of(y)] for y in range(chunks)]
            cs = [half_conduct(b_ref[z, at, part_of(y)], ts[y]) for y in range(chunks)]
            t_turned = [pltpu.roll(v, LANES - 1, 1) for v in ts]
            c_turned = [pltpu.roll(v, LANES - 1, 1) for v in cs]
            flux = []
            for y in range(chunks):
                if y < chunks - 1:
                    t_next = jnp.where(is_last, t_turned[y + 1], t_turned[y])
                    c_next = jnp.where(is_last, c_turned[y + 1], c_turned[y])
                    flux.append((cs[y] + c_next) * (t_next - ts[y]))
                else:
                    inside = (cs[y] + c_turned[y]) * (t_turned[y] - ts[y])
                    flux.append(jnp.where(is_last, 0.0, inside))
            turned = [pltpu.roll(v, 1, 1) for v in flux]
            for y in range(chunks):
                from_low = jnp.where(is_first, turned[y - 1] if y else 0.0, turned[y])
                total = ts[y] + (flux[y] - from_low)
                if z == 0:
                    total = total + plane[at, part_of(y)]
                else:
                    across = (before_c[y] + cs[y]) * (ts[y] - before_t[y])
                    total = total - across
                    total_ref[y, z - 1, at, :] += across
                total_ref[y, z, at, :] = total
                c_ref[y, z, at, :] = cs[y]
                t_s[y, z, at, :] = ts[y]
            before_t, before_c = ts, cs

    at = 0
    for n, members in enumerate(line_groups(chunks, sheets)):

        def cond(k):
            return jnp.stack([c_ref[y, z, pl.ds(k, SUBLANES, stride=steps), :] for y, z in members], 0)

        def keep(k, w, inv, p):
            w_ref[k, at : at + len(members)] = w
            i_ref[k, at : at + len(members)] = inv
            p_ref[k, at : at + len(members)] = p

        block = factor(cond, steps, keep)
        for i, q in enumerate(COEFS):
            for j in range(len(members)):
                first = (at + j) * SUBLANES
                q_s[i, first : first + SUBLANES, :] = block[q][j]
        if n > 0:
            x_eliminate(
                lambda y, z, k: total_ref[y, z, pl.ds(k, SUBLANES, stride=steps), :],
                members, at, w_ref, i_ref, p_ref, h_ref, at - 2 * sheets, ends_ref,
            )
        for k in range(steps):
            for i, (y, z) in enumerate(members):
                t_out[k, at + i] = t_s[y, z, pl.ds(k, SUBLANES, stride=steps), :]
        at += len(members)

    segments = [
        {q: q_s[n, pl.ds(s, lines, stride=SUBLANES), :] for n, q in enumerate(COEFS)}
        for s in range(SUBLANES)
    ]
    whole, levels = tree(segments, join_coefs)
    for (offset, _), level in zip(node_offsets(SUBLANES), levels):
        for n, values in enumerate(level):
            for i in range(3):
                links[offset + n, i] = values[i]
    for n, q in enumerate(COEFS):
        view[n] = whole[q]


def x_factor(loc, energy, t, b, plate, own_cells):
    sheets, rows, columns = t.shape
    chunks = columns // LANES
    lines = chunks * sheets
    steps = rows // SUBLANES
    field = shape_of(chunks, sheets, rows, LANES)
    stored = shape_of(steps, lines, SUBLANES, LANES)
    return pl.pallas_call(
        functools.partial(x_factor_kernel, plate),
        in_specs=[IN_VMEM] * 5,
        out_shape=[
            field,
            field,
            stored,
            stored,
            stored,
            shape_of(SUBLANES - 1, 3, lines, LANES),
            shape_of(len(COEFS), lines, LANES),
            shape_of(steps, max(1, lines - 2 * sheets), SUBLANES, LANES),
            shape_of(2, lines * SUBLANES, LANES),
            stored,
            shape_of(*own_cells.shape),
        ],
        scratch_shapes=[
            pltpu.VMEM((len(COEFS), lines * SUBLANES, LANES), F32),
            pltpu.VMEM((chunks, sheets, rows, LANES), F32),
        ],
        compiler_params=params(),
        cost_estimate=pl.CostEstimate(flops=40 * t.size, bytes_accessed=28 * t.size, transcendentals=0),
    )(loc, energy, t, b, own_cells)


def x_target_kernel(own_cells, total_ref, near, far, *refs):
    w_ref, i_ref, p_ref, links, view, ends_ref, h_ref, own, send, q_s = refs
    chunks, sheets, rows, _ = total_ref.shape
    lines = chunks * sheets
    steps = rows // SUBLANES

    place = lax.axis_index("gy")
    inner = (place > 0) & (place < lax.axis_size("gy") - 1)
    lane = lax.broadcasted_iota(jnp.int32, (SUBLANES, LANES), 1)
    side = 2 * sheets
    is_near = (lane % side >= sheets).astype(jnp.int32) == place % 2
    t, c = (
        jnp.where(is_near, near[at, :], jnp.where(inner, far[at, :], 0.0))
        for at in (slice(0, SUBLANES), slice(SUBLANES, 2 * SUBLANES))
    )
    face = jnp.where(c > 0.0, own_cells[SUBLANES:, :] + c, 0.0)
    flux = face * (t - own_cells[:SUBLANES, :])

    def cells(y, z, k):
        at = k * side + (sheets + z if y == 0 else z)
        edge = 0 if y == 0 else LANES - 1
        inflow = jnp.where(lane == edge, flux[:, at : at + 1], 0.0)
        return total_ref[y, z, pl.ds(k, SUBLANES, stride=steps), :] + inflow

    members = line_groups(chunks, sheets)[0]
    x_eliminate(cells, members, 0, w_ref, i_ref, p_ref, h_ref, 0, q_s)
    split = len(members)
    items = [
        tuple(
            jnp.concatenate(
                [
                    q_s[q, pl.ds(s, split, stride=SUBLANES), :],
                    ends_ref[q, pl.ds(split * SUBLANES + s, lines - split, stride=SUBLANES), :],
                ],
                0,
            )
            for q in range(2)
        )
        for s in range(SUBLANES)
    ]
    for offset, count in node_offsets(SUBLANES):
        joined = []
        for n in range(count):
            ties = tuple(links[offset + n, i] for i in range(3))
            both, flux = join_targets(items[2 * n], items[2 * n + 1], ties)
            own[offset + n] = flux
            joined.append(both)
        items = joined
    for n, q in enumerate(COEFS):
        send[q] = view[n]
    send[FIRST], send[LAST] = items[0]


def x_target(own_cells, total, near, far, w, inv, p, links, view, ends):
    chunks, sheets, rows, _ = total.shape
    lines = chunks * sheets
    steps = rows // SUBLANES
    return pl.pallas_call(
        x_target_kernel,
        out_shape=[
            shape_of(steps, 2 * sheets, SUBLANES, LANES),
            shape_of(SUBLANES - 1, lines, LANES),
            shape_of(7, lines, LANES),
        ],
        scratch_shapes=[
            pltpu.VMEM((2, 2 * sheets * SUBLANES, LANES), F32),
        ],
        compiler_params=params(),
    )(own_cells, total, near, far, w, inv, p, links, view, ends)


def stages_of(axis):
    return lax.axis_size(axis).bit_length() - 1


def swap(value, axis, flip):
    count = lax.axis_size(axis)
    return lax.ppermute(value, axis, [(i, i ^ flip) for i in range(count)])


def on_right(axis, stage):
    return (lax.axis_index(axis) >> stage) % 2 == 1


def toward(right, block):
    return (
        jnp.where(right, block[R00], block[RLL]),
        jnp.where(right, block[FIRST], block[LAST]),
        jnp.where(right, block[C0], block[CL]),
    )


def join(a, b):
    joined, ties = join_coefs(a, b)
    (joined[FIRST], joined[LAST]), flux = join_targets((a[FIRST], a[LAST]), (b[FIRST], b[LAST]), ties)
    return joined, (flux, ties[1], ties[2])


def ordered(right, own, other):
    first = [jnp.where(right, theirs, mine) for mine, theirs in zip(own, other)]
    second = [jnp.where(right, mine, theirs) for mine, theirs in zip(own, other)]
    return first, second


def join_kernel(axis, stage, width, last, *refs):
    count = 1 << width
    blocks = [[refs[i][q] for q in range(7)] for i in range(count)]
    send = refs[-1 - width]
    links = refs[-width:]
    for bit in range(width):
        right = on_right(axis, stage + bit)
        for i in range(count):
            if not i >> bit & 1:
                j = i | 1 << bit
                blocks[i], blocks[j] = ordered(right, blocks[i], blocks[j])
    for bit in range(width):
        pairs = [join(blocks[i], blocks[i + 1]) for i in range(0, len(blocks), 2)]
        blocks = [p[0] for p in pairs]
        ties = [p[1] for p in pairs]
        for upper in range(bit + 1, width):
            right = on_right(axis, stage + upper)
            ties = [
                tuple(jnp.where(right, v, u) for u, v in zip(ties[i], ties[i + 1]))
                for i in range(0, len(ties), 2)
            ]
        for i in range(3):
            links[bit][i] = ties[0][i]
    (whole,) = blocks
    if last:
        for n, value in enumerate(toward(on_right(axis, stage + width), whole)):
            send[n] = value
    else:
        for q in range(7):
            send[q] = whole[q]


def join_stage(own, got, axis, stage, width, last, after):
    lines = own.shape[1]
    return pl.pallas_call(
        functools.partial(join_kernel, axis, stage, width, last),
        in_specs=[IN_VMEM] * (1 + len(got)) + [ANYWHERE] * len(after),
        out_shape=[shape_of(3 if last else 7, lines, LANES)] + [shape_of(3, lines, LANES)] * width,
        compiler_params=params(),
    )(own, *got, *after)


def gather_line(view, axis, widest=1, meanwhile=(), cross=False):
    stages = stages_of(axis)
    links, stage = [], 0
    while stage < stages - 1:
        width = min(widest, stages - 1 - stage)
        got = [swap(view, axis, flip << stage) for flip in range(1, 1 << width)]
        last = stage + width == stages - 1
        view, *ties = join_stage(view, got, axis, stage, width, last, meanwhile)
        links += ties
        stage += width
        meanwhile = ()
    return view, swap(view, axis, 1 << stage | (cross and stage > 0)), links


def top_flux(axis, stages, own, got):
    right = on_right(axis, stages - 1)
    face = own[2] + got[2]
    jump = jnp.where(right, own[1] - got[1], got[1] - own[1])
    return jump * face * inverse(1.0 + face * (own[0] + got[0]))


def block_ends(axis, stages, links):
    shape = links[0].shape[1:] if links else None
    right = on_right(axis, stages - 1)
    zero = jnp.zeros(shape, F32)
    low, high = zero, zero
    unit_low = zero + jnp.where(right, -1.0, 0.0)
    unit_high = zero + jnp.where(right, 0.0, 1.0)
    for stage in range(stages - 2, -1, -1):
        tie = links[stage]
        right = on_right(axis, stage)
        flux = between(tie[0], tie[1], tie[2], low, high)
        unit = between(0.0, tie[1], tie[2], unit_low, unit_high)
        low, high = jnp.where(right, -flux, low), jnp.where(right, high, flux)
        unit_low, unit_high = jnp.where(right, -unit, unit_low), jnp.where(right, unit_high, unit)
    return (low, high), (unit_low, unit_high)


def natural(index, parts):
    span = SUBLANES * parts
    local = index % span
    return index - local + local % SUBLANES * parts + local // SUBLANES


def turn_matrix(shape, from_natural, parts):
    row = lax.broadcasted_iota(jnp.int32, shape, 0)
    column = lax.broadcasted_iota(jnp.int32, shape, 1) % LANES
    hit = natural(row, parts) == column if from_natural else row == natural(column, parts)
    return jnp.where(hit, 1.0, 0.0).astype(jnp.bfloat16)


def turned(matrix, field, rows=None):
    high = field.astype(jnp.bfloat16).astype(F32)
    both = jnp.concatenate([high, field - high], 1)
    if rows:
        both = jnp.concatenate(
            [jnp.broadcast_to(both[n : n + 1, :], (rows, 2 * LANES)) for n in range(field.shape[0])], 0
        )
    both = both.astype(jnp.bfloat16)
    return lax.dot_general(
        matrix, both, (((1,), (1,)), ((), ())), preferred_element_type=F32
    )


def y_factor_kernel(c_ref, after, w_ref, i_ref, p_ref, inner, outer, view, to_y, to_x, unit_low, unit_high, c_s, q_s, r_s):
    chunks, sheets, rows, _ = c_ref.shape
    each = LANES // rows
    pairs = sheets // each
    x_steps = rows // SUBLANES
    steps = LANES // SUBLANES
    to_y[...] = turn_matrix(to_y.shape, True, steps)
    to_x[...] = turn_matrix(to_x.shape, False, x_steps)
    for m in range(pairs):
        for y in range(chunks):
            block = jnp.concatenate(
                [
                    c_ref[y, m * each + i, pl.ds(k, SUBLANES, stride=x_steps), :]
                    for i in range(each)
                    for k in range(x_steps)
                ],
                0,
            )
            c_s[m, part_of(y), :] = block.T

    members = [(y, m) for y in range(chunks) for m in range(pairs)]
    lines = len(members)

    def cond(k):
        return jnp.stack([c_s[m, pl.ds(y * LANES + k, SUBLANES, stride=steps), :] for y, m in members], 0)

    def keep(k, w, inv, p):
        w_ref[k] = w
        i_ref[k] = inv
        p_ref[k] = p

    block = factor(cond, steps, keep)
    for n, q in enumerate(COEFS):
        for i in range(lines):
            q_s[n, i * SUBLANES : (i + 1) * SUBLANES, :] = block[q][i]
    segments = [
        {q: q_s[n, pl.ds(s, lines, stride=SUBLANES), :] for n, q in enumerate(COEFS)}
        for s in range(SUBLANES)
    ]
    whole, levels = tree(segments, join_coefs)
    for (offset, _), level in zip(node_offsets(SUBLANES), levels):
        for n, values in enumerate(level):
            for i in range(3):
                inner[offset + n, i] = values[i]
    for n, q in enumerate(COEFS):
        r_s[n] = whole[q]
    parts = [
        {q: r_s[n, y * pairs : (y + 1) * pairs, :] for n, q in enumerate(COEFS)} for y in range(chunks)
    ]
    whole, levels = tree(parts, join_coefs)
    for (offset, _), level in zip(node_offsets(chunks), levels):
        for n, values in enumerate(level):
            for i in range(3):
                outer[offset + n, i] = values[i]
    for n, q in enumerate(COEFS):
        view[n] = whole[q]

    same = turn_matrix(to_y.shape, True, 1)
    one = jnp.ones((pairs, LANES), F32)
    for n, (low, high, field) in enumerate(((one, 0.0 * one, unit_low), (0.0 * one, one, unit_high))):
        for y, pair in enumerate(tree_ends(chunks, outer, nothing, low, high)):
            for i in range(2):
                r_s[2 * n + i, y * pairs : (y + 1) * pairs, :] = pair[i]
        for s, pair in enumerate(tree_ends(SUBLANES, inner, nothing, r_s[2 * n], r_s[2 * n + 1])):
            for i in range(2):
                q_s[2 * n + i, pl.ds(s, lines, stride=SUBLANES), :] = pair[i]
        low, value = (
            jnp.stack(
                [q_s[2 * n + i, j * SUBLANES : (j + 1) * SUBLANES, :] for j in range(lines)], 0
            )
            for i in range(2)
        )
        for k in range(steps - 1, -1, -1):
            value = w_ref[k] * value + p_ref[k] * low
            for j, (y, m) in enumerate(members):
                c_s[m, pl.ds(y * LANES + k, SUBLANES, stride=steps), :] = value[j]
        for y, m in members:
            field[y, part_of(m), :] = turned(same, c_s[m, part_of(y), :])


def y_factor(c, after):
    chunks, sheets, rows, _ = c.shape
    pairs = sheets * rows // LANES
    lines = chunks * pairs
    stored = shape_of(LANES // SUBLANES, lines, SUBLANES, LANES)
    matrix = jax.ShapeDtypeStruct((LANES, 2 * LANES), jnp.bfloat16)
    return pl.pallas_call(
        y_factor_kernel,
        in_specs=[IN_VMEM, ANYWHERE],
        out_shape=[
            stored,
            stored,
            stored,
            shape_of(SUBLANES - 1, 3, lines, LANES),
            shape_of(chunks - 1, 3, pairs, LANES),
            shape_of(len(COEFS), pairs, LANES),
            matrix,
            matrix,
            shape_of(chunks, pairs * LANES, LANES),
            shape_of(chunks, pairs * LANES, LANES),
        ],
        scratch_shapes=[
            pltpu.VMEM((pairs, chunks * LANES, LANES), F32),
            pltpu.VMEM((len(COEFS), lines * SUBLANES, LANES), F32),
            pltpu.VMEM((len(COEFS), lines, LANES), F32),
        ],
        compiler_params=params(),
        cost_estimate=pl.CostEstimate(flops=20 * c.size, bytes_accessed=16 * c.size, transcendentals=0),
    )(c, after)


def z_factor_kernel(c_ref, after, w_ref, i_ref):
    sheets = c_ref.shape[1]
    ground = 1.0
    for z in range(sheets - 1):
        face = c_ref[:, z] + c_ref[:, z + 1]
        inv = inverse(ground + face)
        w = face * inv
        i_ref[z] = inv
        w_ref[z] = w
        ground = 1.0 + w * ground
    i_ref[sheets - 1] = inverse(ground)


def z_factor(c, after):
    chunks, sheets, rows, _ = c.shape
    return pl.pallas_call(
        z_factor_kernel,
        in_specs=[IN_VMEM, ANYWHERE],
        out_shape=[
            shape_of(sheets - 1, chunks, rows, LANES),
            shape_of(sheets, chunks, rows, LANES),
        ],
        compiler_params=params(),
        cost_estimate=pl.CostEstimate(flops=10 * c.size, bytes_accessed=12 * c.size, transcendentals=0),
    )(c, after)


def join_tree(items, links, own):
    for offset, count in node_offsets(len(items)):
        joined = []
        for n in range(count):
            tie = tuple(links[offset + n, i] for i in range(3))
            both, flux = join_targets(items[2 * n], items[2 * n + 1], tie)
            own[offset + n] = flux
            joined.append(both)
        items = joined
    return items[0]


def tree_ends(leaves, links, own, low, high):
    levels = [
        [(own(offset + n), links[offset + n, 1], links[offset + n, 2]) for n in range(count)]
        for offset, count in node_offsets(leaves)
    ]
    return descend(levels, low, high)


def nothing(node):
    return 0.0


def y_prepare_kernel(stages, *refs):
    ties = refs[: stages - 1]
    xw, xh, xm, xp, x_links, x_own, t_ref, to_y, y_low, y_high = refs[stages - 1 : stages + 9]
    base, response, to_first, to_last, fixed, f_s, g_s = refs[stages + 9 :]
    x_steps, lines = xw.shape[:2]
    chunks = base.shape[0]
    sheets = lines // chunks
    rows = x_steps * SUBLANES

    ends, units = block_ends("gx", stages, ties)
    for n, (own, (low, high)) in enumerate(((lambda i: x_own[i], ends), (nothing, units))):
        for s, pair in enumerate(tree_ends(SUBLANES, x_links, own, low, high)):
            for i in range(2):
                f_s[n, i, pl.ds(s, lines, stride=SUBLANES), :] = pair[i]
    first = 0
    for n, members in enumerate(line_groups(chunks, sheets)):
        at = slice(first, first + len(members))
        h_ref_of, h_at = (xh, at) if n == 0 else (xm, slice(first - 2 * sheets, at.stop - 2 * sheets))
        (low, value), (unit_low, unit) = (
            [
                jnp.stack(
                    [f_s[q, i, j * SUBLANES : (j + 1) * SUBLANES, :] for j in range(at.start, at.stop)], 0
                )
                for i in range(2)
            ]
            for q in range(2)
        )
        for k in range(x_steps - 1, -1, -1):
            w, p = xw[k, at], xp[k, at]
            value = w * value + (h_ref_of[k, h_at] + p * low)
            unit = w * unit + p * unit_low
            field = value - t_ref[k, at]
            for j, (y, z) in enumerate(members):
                place = z * rows + k * SUBLANES
                g_s[0, y, place : place + SUBLANES, :] = field[j]
                g_s[1, y, place : place + SUBLANES, :] = unit[j]
        first = at.stop

    totals = [None, None]
    for y in range(chunks):
        base[y] = turned(to_y[...], g_s[0, y])
        response[y] = turned(to_y[...], g_s[1, y])
        for i, (unit, weight) in enumerate(((y_low, to_first), (y_high, to_last))):
            weight[y] = unit[y] * g_s[1, y]
            part = unit[y] * g_s[0, y]
            totals[i] = part if y == 0 else totals[i] + part
    for i in range(2):
        put_sums(fixed.at[i], totals[i])


def put_sums(out, field):
    ones = jnp.ones((2 * SUBLANES, 2 * LANES), jnp.bfloat16)
    total = turned(ones, field)
    for m in range(out.shape[0]):
        out[m : m + 1, :] = total[:1, part_of(m)]


def y_prepare(ties, xw, xh, xm, xp, x_links, x_own, t, to_y, unit_low, unit_high):
    chunks = unit_low.shape[0]
    x_steps, lines = xw.shape[:2]
    width = lines // chunks * x_steps * SUBLANES
    field, weight = shape_of(chunks, LANES, width), shape_of(chunks, width, LANES)
    return pl.pallas_call(
        functools.partial(y_prepare_kernel, len(ties) + 1),
        out_shape=[field] * 2 + [weight] * 2 + [shape_of(2, width // LANES, LANES)],
        scratch_shapes=[
            pltpu.VMEM((2, 2, lines * SUBLANES, LANES), F32),
            pltpu.VMEM((2, chunks, width, LANES), F32),
        ],
        compiler_params=params(),
        cost_estimate=pl.CostEstimate(flops=8 * t.size, bytes_accessed=16 * t.size, transcendentals=0),
    )(*ties, xw, xh, xm, xp, x_links, x_own, t, to_y, unit_low, unit_high)


def sheet_rows(values, y, chunks, sheets):
    line_of = {member: n for n, member in enumerate(sum(line_groups(chunks, sheets), []))}
    return [values[line_of[y, z] : line_of[y, z] + 1, :] for z in range(sheets)]


def y_target_kernel(stages, own, got, to_first, to_last, fixed, view, flux_ref, send, r_s):
    chunks, width, _ = to_first.shape
    sheets = own.shape[1] // chunks
    rows = width // sheets

    flux = top_flux("gx", stages, own, got)
    flux_ref[...] = flux
    totals = [[None] * sheets, [None] * sheets]
    for y in range(chunks):
        for z, row in enumerate(sheet_rows(flux, y, chunks, sheets)):
            for total, weight in zip(totals, (to_first, to_last)):
                part = weight[y, z * rows : (z + 1) * rows, :] * row
                total[z] = part if y == 0 else total[z] + part
    for n, q in enumerate(COEFS):
        send[q] = view[n]
    for i, q in enumerate((FIRST, LAST)):
        put_sums(r_s.at[i], jnp.concatenate(totals[i], 0))
        send[q] = fixed[i] + r_s[i]


def y_target(own, got, to_first, to_last, fixed, view):
    pairs = view.shape[1]
    return pl.pallas_call(
        functools.partial(y_target_kernel, stages_of("gx")),
        out_shape=[shape_of(*own.shape[1:]), shape_of(7, pairs, LANES)],
        scratch_shapes=[pltpu.VMEM((2, pairs, LANES), F32)],
        compiler_params=params(),
    )(own, got, to_first, to_last, fixed, view)


def y_eliminate_kernel(base, response, flux, to_y, yw, yi, yp, inner, outer, after, *refs):
    h_ref, inner_own, outer_own, q_s, r_s = refs
    chunks, _, width = base.shape
    pairs = width // LANES
    sheets = flux.shape[0] // chunks
    steps = yw.shape[0]
    members = [(y, m) for y in range(chunks) for m in range(pairs)]
    fields = []
    for y in range(chunks):
        by_sheet = jnp.concatenate(sheet_rows(flux[...], y, chunks, sheets), 0)
        fields.append(base[y] + response[y] * turned(to_y[...], by_sheet, width // sheets))

    def target(k):
        at = slice(k * SUBLANES, (k + 1) * SUBLANES)
        return jnp.stack([fields[y][at, part_of(m)] for y, m in members], 0)

    def keep(k, h):
        h_ref[k] = h

    ends = eliminate(target, steps, lambda k: yw[k], lambda k: yi[k], lambda k: yp[k], keep)
    for q in range(2):
        for i in range(len(members)):
            q_s[q, i * SUBLANES : (i + 1) * SUBLANES, :] = ends[q][i]
    items = [
        tuple(q_s[q, pl.ds(s, len(members), stride=SUBLANES), :] for q in range(2))
        for s in range(SUBLANES)
    ]
    r_s[0], r_s[1] = join_tree(items, inner, inner_own)
    items = [tuple(r_s[q, y * pairs : (y + 1) * pairs, :] for q in range(2)) for y in range(chunks)]
    join_tree(items, outer, outer_own)


def y_eliminate(base, response, flux, to_y, yw, yi, yp, inner, outer, after):
    y_lines = yw.shape[1]
    pairs = outer.shape[2]
    chunks = y_lines // pairs
    return pl.pallas_call(
        y_eliminate_kernel,
        in_specs=[IN_VMEM] * 9 + [ANYWHERE],
        out_shape=[
            shape_of(*yw.shape),
            shape_of(SUBLANES - 1, y_lines, LANES),
            shape_of(chunks - 1, pairs, LANES),
        ],
        scratch_shapes=[
            pltpu.VMEM((2, y_lines * SUBLANES, LANES), F32),
            pltpu.VMEM((2, y_lines, LANES), F32),
        ],
        compiler_params=params(),
        cost_estimate=pl.CostEstimate(flops=8 * base.size, bytes_accessed=16 * base.size, transcendentals=0),
    )(base, response, flux, to_y, yw, yi, yp, inner, outer, after)


def z_solve(zw, zi, field, at, keep):
    sheets = zi.shape[0]
    rhs, kept = None, []
    for z in range(sheets):
        rhs = field(z) if z == 0 else field(z) + zw[(z - 1, *at)] * rhs
        kept.append(rhs * zi[(z, *at)])
    value = kept[-1]
    keep(sheets - 1, value)
    for z in range(sheets - 2, -1, -1):
        value = zw[(z, *at)] * value + kept[z]
        keep(z, value)


def finish_prepare_kernel(stages, *refs):
    ties = refs[: stages - 1]
    yw, yh, yp, inner, inner_own, outer, outer_own, zw, zi, t_ref, to_x = refs[stages - 1 : stages + 10]
    base, response, r_s, e_s, u_s = refs[stages + 10 :]
    chunks, sheets, rows, _ = base.shape
    each = LANES // rows
    pairs = sheets // each
    steps = yw.shape[0]
    lines = chunks * pairs

    ends, units = block_ends("gy", stages, ties)
    both = (
        (lambda i: outer_own[i], lambda i: inner_own[i], ends),
        (nothing, nothing, units),
    )
    for n, (upper, lower, (low, high)) in enumerate(both):
        for y, pair in enumerate(tree_ends(chunks, outer, upper, low, high)):
            for i in range(2):
                r_s[n, i, y * pairs : (y + 1) * pairs, :] = pair[i]
        for s, pair in enumerate(tree_ends(SUBLANES, inner, lower, r_s[n, 0], r_s[n, 1])):
            for i in range(2):
                e_s[n, i, pl.ds(s, lines, stride=SUBLANES), :] = pair[i]
    (low, value), (unit_low, unit) = (
        [
            jnp.stack([e_s[q, i, n * SUBLANES : (n + 1) * SUBLANES, :] for n in range(lines)], 0)
            for i in range(2)
        ]
        for q in range(2)
    )
    for k in range(steps - 1, -1, -1):
        w, p = yw[k], yp[k]
        value = w * value + (yh[k] + p * low)
        unit = w * unit + p * unit_low
        for y in range(chunks):
            for m in range(pairs):
                place = pl.ds(y * LANES + k, SUBLANES, stride=steps)
                u_s[0, m, place, :] = value[y * pairs + m]
                u_s[1, m, place, :] = unit[y * pairs + m]

    for y in range(chunks):
        part = part_of(y)
        fields = [turned(to_x[...], u_s[0, m, part, :]) for m in range(pairs)]

        def field(z):
            at = z % each * rows
            return fields[z // each][at : at + rows, :]

        def keep(z, value):
            base[y, z] = t_ref[z, :, part] + value

        z_solve(zw, zi, field, (y,), keep)
        for m in range(pairs):
            units = turned(to_x[...], u_s[1, m, part, :])
            for i in range(each):
                response[y, m * each + i] = units[i * rows : (i + 1) * rows, :]


def finish_prepare(ties, yw, yh, yp, inner, inner_own, outer, outer_own, zw, zi, t, to_x):
    sheets, rows, columns = t.shape
    chunks = columns // LANES
    pairs = sheets * rows // LANES
    lines = chunks * pairs
    field = shape_of(chunks, sheets, rows, LANES)
    return pl.pallas_call(
        functools.partial(finish_prepare_kernel, len(ties) + 1),
        out_shape=[field, field],
        scratch_shapes=[
            pltpu.VMEM((2, 2, lines, LANES), F32),
            pltpu.VMEM((2, 2, lines * SUBLANES, LANES), F32),
            pltpu.VMEM((2, pairs, columns, LANES), F32),
        ],
        compiler_params=params(),
        cost_estimate=pl.CostEstimate(flops=12 * t.size, bytes_accessed=20 * t.size, transcendentals=0),
    )(*ties, yw, yh, yp, inner, inner_own, outer, outer_own, zw, zi, t, to_x)


def finish_kernel(stages, own, got, base, response, zw, zi, to_x, out, o_s, sems):
    chunks, sheets, rows, _ = base.shape
    each = LANES // rows
    pairs = sheets // each
    flux = top_flux("gy", stages, own, got)
    wide = turned(to_x[...], flux, LANES)
    spread = [wide[:, part_of(m)] for m in range(pairs)]
    started = []
    block = rows // OUT_COPIES
    for n in range(OUT_COPIES):
        strip = slice(n * block, (n + 1) * block)
        for y in range(chunks):

            def field(z):
                at = z % each * rows + strip.start
                return response[y, z, strip, :] * spread[z // each][at : at + block, :]

            def keep(z, value):
                o_s[z, strip, part_of(y)] = base[y, z, strip, :] + value

            z_solve(zw, zi, field, (y, strip), keep)
        at = pl.ds(strip.start, block)
        copy = pltpu.make_async_copy(o_s.at[:, at, :], out.at[:, at, :], sems.at[n])
        copy.start()
        started.append(copy)
    for copy in started:
        copy.wait()


def finish(own, got, base, response, zw, zi, to_x):
    chunks, sheets, rows, _ = base.shape
    shape = (sheets, rows, chunks * LANES)
    return pl.pallas_call(
        functools.partial(finish_kernel, stages_of("gy")),
        out_shape=shape_of(*shape),
        out_specs=ANYWHERE,
        scratch_shapes=[pltpu.VMEM(shape, F32), pltpu.SemaphoreType.DMA((OUT_COPIES,))],
        compiler_params=params(),
    )(own, got, base, response, zw, zi, to_x)


def per_device(temperature, base, locations, energy):
    columns = temperature.shape[2]
    gy = lax.axis_size("gy")
    t, b, loc, heat, packed = load(temperature, base, locations[None], energy[None])
    near = swap(packed, "gy", 1)
    far = lax.ppermute(packed, "gy", [(i, ((i + 1) % gy ^ 1) - 1 if i else gy - 1) for i in range(gy)])
    c, total, xw, xi, xp, x_links, x_view, xm, ends, t_steps, swapped = x_factor(loc, heat, t, b, columns * gy, packed)
    xh, x_own, view = x_target(swapped, total, near, far, xw, xi, xp, x_links, x_view, ends)
    yw, yi, yp, inner, outer, y_view, to_y, to_x, unit_low, unit_high = y_factor(c, x_view)
    zw, zi = z_factor(c, view)
    own, got, ties = gather_line(view, "gx", 2, (y_view, zw))
    base, response, to_first, to_last, fixed = y_prepare(
        ties, xw, xh, xm, xp, x_links, x_own, t_steps, to_y, unit_low, unit_high
    )
    flux, view = y_target(own, got, to_first, to_last, fixed, y_view)
    yh, inner_own, outer_own = y_eliminate(
        base, response, flux, to_y, yw, yi, yp, inner, outer, view
    )
    own, got, ties = gather_line(view, "gy", meanwhile=(yh,), cross=True)
    base, response = finish_prepare(
        ties, yw, yh, yp, inner, inner_own, outer, outer_own, zw, zi, t, to_x
    )
    return finish(own, got, base, response, zw, zi, to_x)


def solution(mesh):
    in_specs = (P(None, "gx", "gy"), P(None, "gx", "gy"), P(), P())
    out_specs = P(None, "gx", "gy")
    return jax.shard_map(
        per_device, mesh=mesh, in_specs=in_specs, out_specs=out_specs, check_vma=False
    )
```

```python
import functools

import jax
import jax.numpy as jnp
from jax import lax
from jax.experimental import pallas as pl
from jax.experimental.pallas import tpu as pltpu
from jax.sharding import PartitionSpec as P

RATE = 2000.0
THERMAL_GROWTH = 0.8
LANES = 128
SUBLANES = 8
F32 = jnp.float32
MIB = 1024 * 1024
OUT_COPIES = 4
ANYWHERE = pl.BlockSpec(memory_space=pl.ANY)
IN_HBM = pl.BlockSpec(memory_space=pltpu.HBM)
IN_VMEM = pl.BlockSpec(memory_space=pltpu.VMEM)

R00, R0L, RLL, FIRST, LAST, C0, CL = range(7)
COEFS = (R00, R0L, RLL, C0, CL)


def params(limit=40):
    return pltpu.CompilerParams(vmem_limit_bytes=limit * MIB)


def shape_of(*sizes):
    return jax.ShapeDtypeStruct(sizes, F32)


def half_conduct(base, temperature):
    return base * (0.5 * RATE + (0.5 * RATE * THERMAL_GROWTH) * temperature)


def inverse(x):
    guess = pl.reciprocal(x, approx=True)
    return guess * (2.0 - x * guess)


def join_coefs(a, b):
    face = a[CL] + b[C0]
    inv = face * inverse(1.0 + face * (a[RLL] + b[R00]))
    left = a[R0L] * inv
    right = b[R0L] * inv
    joined = {
        R00: a[R00] - left * a[R0L],
        R0L: left * b[R0L],
        RLL: b[RLL] - right * b[R0L],
        C0: a[C0],
        CL: b[CL],
    }
    return joined, (inv, right, left)


def join_targets(a, b, links):
    inv, right, left = links
    jump = b[0] - a[1]
    return (a[0] + left * jump, b[1] - right * jump), jump * inv


def between(own, right, left, low, high):
    return own + right * high - left * low


def tree(items, join):
    levels = []
    while len(items) > 1:
        pairs = [join(items[i], items[i + 1]) for i in range(0, len(items), 2)]
        items = [p[0] for p in pairs]
        levels.append([p[1] for p in pairs])
    return items[0], levels


def descend(levels, low, high):
    ends = [(low, high)]
    for level in reversed(levels):
        below = []
        for (lo, hi), (own, right, left) in zip(ends, level):
            flux = between(own, right, left, lo, hi)
            below += [(lo, flux), (-flux, hi)]
        ends = below
    return ends


def node_offsets(leaves):
    offsets, at, count = [], 0, leaves // 2
    while count:
        offsets.append((at, count))
        at += count
        count //= 2
    return offsets


def factor(cond, steps, keep):
    here = cond(0)
    c_first = here
    one = jnp.ones_like(here)
    ground, path, first_first = one, one, None
    for k in range(steps - 1):
        following = cond(k + 1)
        face = here + following
        inv = inverse(ground + face)
        w = face * inv
        p = path * inv
        keep(k, w, inv, p)
        step = path * p
        first_first = step if first_first is None else first_first + step
        path = path * w
        ground = 1.0 + w * ground
        here = following
    inv = inverse(ground)
    p = path * inv
    keep(steps - 1, inv, inv, p)
    return {R00: first_first + path * p, R0L: p, RLL: inv, C0: c_first, CL: here}


def eliminate(target, steps, w, inv, p, keep):
    rhs = target(0)
    first = None
    for k in range(steps):
        h = rhs * inv(k)
        keep(k, h)
        step = rhs * p(k)
        first = step if first is None else first + step
        if k < steps - 1:
            rhs = target(k + 1) + w(k) * rhs
    return first, h


def is_odd(axis):
    return lax.axis_index(axis) % 2 == 1


def fold(cells, used):
    steps = cells.shape[0] // SUBLANES
    total = cells[pl.ds(0, SUBLANES, stride=steps), :]
    lane = lax.broadcasted_iota(jnp.int32, total.shape, 1)
    for k in range(1, steps):
        part = pltpu.roll(cells[pl.ds(k, SUBLANES, stride=steps), :], k * used, 1)
        total = jnp.where(lane // used == k, part, total)
    return total


def load_kernel(t_hbm, b_hbm, loc_hbm, energy_hbm, t_out, b_out, loc, energy, packed, cells, sems):
    sheets, rows, columns = t_hbm.shape
    parts = [(0, LANES), (columns - LANES, LANES), (LANES, columns - 2 * LANES)]
    copies = []
    for n, (start, size) in enumerate(parts):
        part = pl.ds(start, size)
        for i, (src, dst) in enumerate(((t_hbm, t_out), (b_hbm, b_out))):
            copies.append(
                pltpu.make_async_copy(src.at[:, :, part], dst.at[:, :, part], sems.at[i, n])
            )
    copies.append(pltpu.make_async_copy(loc_hbm, loc, sems.at[2, 0]))
    copies.append(pltpu.make_async_copy(energy_hbm, energy, sems.at[2, 1]))
    for copy in copies:
        copy.start()
    lane = lax.broadcasted_iota(jnp.int32, (rows, LANES), 1)
    edge_t = jnp.zeros((rows, LANES), F32)
    edge_c = edge_t
    for side, source in enumerate((0, LANES - 1)):
        for copy in copies[2 * side : 2 * side + 2]:
            copy.wait()
        part = slice(parts[side][0], parts[side][0] + LANES)
        for z in range(sheets):
            t = t_out[z, :, part]
            c = half_conduct(b_out[z, :, part], t)
            place = lane == sheets * side + z
            edge_t = jnp.where(place, t[:, source : source + 1], edge_t)
            edge_c = jnp.where(place, c[:, source : source + 1], edge_c)
    cells[0], cells[1] = edge_t, edge_c
    for i in range(2):
        packed[i * SUBLANES : (i + 1) * SUBLANES, :] = fold(cells.at[i], 2 * sheets)
    for copy in copies[4:]:
        copy.wait()


def load(temperature, base, locations, energy):
    sheets, rows, columns = temperature.shape
    assert rows // SUBLANES * 2 * sheets <= LANES and columns > 2 * LANES
    operands = (temperature, base, locations, energy)
    return pl.pallas_call(
        load_kernel,
        in_specs=[IN_HBM] * 4,
        out_shape=[pltpu.VMEM(v.shape, v.dtype) for v in operands]
        + [pltpu.VMEM((2 * SUBLANES, LANES), F32)],
        scratch_shapes=[pltpu.VMEM((2, rows, LANES), F32), pltpu.SemaphoreType.DMA((3, 3))],
        compiler_params=params(),
    )(*[pltpu.with_memory_space_constraint(v, pltpu.HBM) for v in operands])


def source_plane(loc, energy, rows, columns, plate):
    place = loc[...]
    count = place.shape[1]
    local_x = place // plate - lax.axis_index("gx") * rows
    local_y = place % plate - lax.axis_index("gy") * columns
    in_x = lax.broadcasted_iota(jnp.int32, (rows, count), 0) == local_x
    in_y = lax.broadcasted_iota(jnp.int32, (columns, count), 0) == local_y
    by_y = jnp.where(in_y, 1.0, 0.0).astype(jnp.bfloat16)
    left = energy[...]
    plane = None
    for _ in range(3):
        part = left.astype(jnp.bfloat16).astype(F32)
        left = left - part
        term = lax.dot_general(
            jnp.where(in_x, part, 0.0).astype(jnp.bfloat16),
            by_y,
            (((1,), (1,)), ((), ())),
            preferred_element_type=F32,
        )
        plane = term if plane is None else plane + term
    return plane


def part_of(y):
    return slice(y * LANES, (y + 1) * LANES)


def line_groups(chunks, sheets):
    order = [0, chunks - 1] + list(range(1, chunks - 1))
    return [[(y, z) for y in order[i : i + 2] for z in range(sheets)] for i in range(0, chunks, 2)]


def x_eliminate(cells, members, first_line, w_ref, i_ref, p_ref, h_ref, h_line, q_s):
    steps = w_ref.shape[0]
    at = slice(first_line, first_line + len(members))
    kept_at = slice(h_line, h_line + len(members))

    def target(k):
        return jnp.stack([cells(y, z, k) for y, z in members], 0)

    def keep(k, h):
        h_ref[k, kept_at] = h

    ends = eliminate(
        target, steps, lambda k: w_ref[k, at], lambda k: i_ref[k, at], lambda k: p_ref[k, at], keep
    )
    for q in range(2):
        for i in range(len(members)):
            first = (first_line + i) * SUBLANES
            q_s[q, first : first + SUBLANES, :] = ends[q][i]


def x_factor_kernel(plate, loc, energy, t_ref, b_ref, own_cells, *refs):
    c_ref, total_ref, w_ref, i_ref, p_ref, links, view, h_ref, ends_ref, t_out, swapped, q_s, t_s = refs
    chunks, sheets, rows, _ = c_ref.shape
    lines = chunks * sheets
    steps = rows // SUBLANES
    plane = source_plane(loc, energy, rows, chunks * LANES, plate)
    mine = own_cells[...]
    in_low = lax.broadcasted_iota(jnp.int32, mine.shape, 1) % (2 * sheets) < sheets
    swapped[...] = jnp.where(
        in_low, pltpu.roll(mine, LANES - sheets, 1), pltpu.roll(mine, sheets, 1)
    )

    lane = lax.broadcasted_iota(jnp.int32, (SUBLANES, LANES), 1)
    is_first, is_last = lane == 0, lane == LANES - 1
    for r in range(steps):
        at = slice(r * SUBLANES, (r + 1) * SUBLANES)
        before_t, before_c = None, None
        for z in range(sheets):
            ts = [t_ref[z, at, part_of(y)] for y in range(chunks)]
            cs = [half_conduct(b_ref[z, at, part_of(y)], ts[y]) for y in range(chunks)]
            t_turned = [pltpu.roll(v, LANES - 1, 1) for v in ts]
            c_turned = [pltpu.roll(v, LANES - 1, 1) for v in cs]
            flux = []
            for y in range(chunks):
                if y < chunks - 1:
                    t_next = jnp.where(is_last, t_turned[y + 1], t_turned[y])
                    c_next = jnp.where(is_last, c_turned[y + 1], c_turned[y])
                    flux.append((cs[y] + c_next) * (t_next - ts[y]))
                else:
                    inside = (cs[y] + c_turned[y]) * (t_turned[y] - ts[y])
                    flux.append(jnp.where(is_last, 0.0, inside))
            turned = [pltpu.roll(v, 1, 1) for v in flux]
            for y in range(chunks):
                from_low = jnp.where(is_first, turned[y - 1] if y else 0.0, turned[y])
                total = ts[y] + (flux[y] - from_low)
                if z == 0:
                    total = total + plane[at, part_of(y)]
                else:
                    across = (before_c[y] + cs[y]) * (ts[y] - before_t[y])
                    total = total - across
                    total_ref[y, z - 1, at, :] += across
                total_ref[y, z, at, :] = total
                c_ref[y, z, at, :] = cs[y]
                t_s[y, z, at, :] = ts[y]
            before_t, before_c = ts, cs

    at = 0
    for n, members in enumerate(line_groups(chunks, sheets)):

        def cond(k):
            return jnp.stack([c_ref[y, z, pl.ds(k, SUBLANES, stride=steps), :] for y, z in members], 0)

        def keep(k, w, inv, p):
            w_ref[k, at : at + len(members)] = w
            i_ref[k, at : at + len(members)] = inv
            p_ref[k, at : at + len(members)] = p

        block = factor(cond, steps, keep)
        for i, q in enumerate(COEFS):
            for j in range(len(members)):
                first = (at + j) * SUBLANES
                q_s[i, first : first + SUBLANES, :] = block[q][j]
        if n > 0:
            x_eliminate(
                lambda y, z, k: total_ref[y, z, pl.ds(k, SUBLANES, stride=steps), :],
                members, at, w_ref, i_ref, p_ref, h_ref, at - 2 * sheets, ends_ref,
            )
        for k in range(steps):
            for i, (y, z) in enumerate(members):
                t_out[k, at + i] = t_s[y, z, pl.ds(k, SUBLANES, stride=steps), :]
        at += len(members)

    segments = [
        {q: q_s[n, pl.ds(s, lines, stride=SUBLANES), :] for n, q in enumerate(COEFS)}
        for s in range(SUBLANES)
    ]
    whole, levels = tree(segments, join_coefs)
    for (offset, _), level in zip(node_offsets(SUBLANES), levels):
        for n, values in enumerate(level):
            for i in range(3):
                links[offset + n, i] = values[i]
    for n, q in enumerate(COEFS):
        view[n] = whole[q]


def x_factor(loc, energy, t, b, plate, own_cells):
    sheets, rows, columns = t.shape
    chunks = columns // LANES
    lines = chunks * sheets
    steps = rows // SUBLANES
    field = shape_of(chunks, sheets, rows, LANES)
    stored = shape_of(steps, lines, SUBLANES, LANES)
    return pl.pallas_call(
        functools.partial(x_factor_kernel, plate),
        in_specs=[IN_VMEM] * 5,
        out_shape=[
            field,
            field,
            stored,
            stored,
            stored,
            shape_of(SUBLANES - 1, 3, lines, LANES),
            shape_of(len(COEFS), lines, LANES),
            shape_of(steps, max(1, lines - 2 * sheets), SUBLANES, LANES),
            shape_of(2, lines * SUBLANES, LANES),
            stored,
            shape_of(*own_cells.shape),
        ],
        scratch_shapes=[
            pltpu.VMEM((len(COEFS), lines * SUBLANES, LANES), F32),
            pltpu.VMEM((chunks, sheets, rows, LANES), F32),
        ],
        compiler_params=params(),
        cost_estimate=pl.CostEstimate(flops=40 * t.size, bytes_accessed=28 * t.size, transcendentals=0),
    )(loc, energy, t, b, own_cells)


def x_target_kernel(own_cells, total_ref, near, far, *refs):
    w_ref, i_ref, p_ref, links, view, ends_ref, h_ref, own, send, q_s = refs
    chunks, sheets, rows, _ = total_ref.shape
    lines = chunks * sheets
    steps = rows // SUBLANES

    place = lax.axis_index("gy")
    inner = (place > 0) & (place < lax.axis_size("gy") - 1)
    lane = lax.broadcasted_iota(jnp.int32, (SUBLANES, LANES), 1)
    side = 2 * sheets
    is_near = (lane % side >= sheets).astype(jnp.int32) == place % 2
    t, c = (
        jnp.where(is_near, near[at, :], jnp.where(inner, far[at, :], 0.0))
        for at in (slice(0, SUBLANES), slice(SUBLANES, 2 * SUBLANES))
    )
    face = jnp.where(c > 0.0, own_cells[SUBLANES:, :] + c, 0.0)
    flux = face * (t - own_cells[:SUBLANES, :])

    def cells(y, z, k):
        at = k * side + (sheets + z if y == 0 else z)
        edge = 0 if y == 0 else LANES - 1
        inflow = jnp.where(lane == edge, flux[:, at : at + 1], 0.0)
        return total_ref[y, z, pl.ds(k, SUBLANES, stride=steps), :] + inflow

    members = line_groups(chunks, sheets)[0]
    x_eliminate(cells, members, 0, w_ref, i_ref, p_ref, h_ref, 0, q_s)
    split = len(members)
    items = [
        tuple(
            jnp.concatenate(
                [
                    q_s[q, pl.ds(s, split, stride=SUBLANES), :],
                    ends_ref[q, pl.ds(split * SUBLANES + s, lines - split, stride=SUBLANES), :],
                ],
                0,
            )
            for q in range(2)
        )
        for s in range(SUBLANES)
    ]
    for offset, count in node_offsets(SUBLANES):
        joined = []
        for n in range(count):
            ties = tuple(links[offset + n, i] for i in range(3))
            both, flux = join_targets(items[2 * n], items[2 * n + 1], ties)
            own[offset + n] = flux
            joined.append(both)
        items = joined
    for n, q in enumerate(COEFS):
        send[q] = view[n]
    send[FIRST], send[LAST] = items[0]


def x_target(own_cells, total, near, far, w, inv, p, links, view, ends):
    chunks, sheets, rows, _ = total.shape
    lines = chunks * sheets
    steps = rows // SUBLANES
    return pl.pallas_call(
        x_target_kernel,
        out_shape=[
            shape_of(steps, 2 * sheets, SUBLANES, LANES),
            shape_of(SUBLANES - 1, lines, LANES),
            shape_of(7, lines, LANES),
        ],
        scratch_shapes=[
            pltpu.VMEM((2, 2 * sheets * SUBLANES, LANES), F32),
        ],
        compiler_params=params(),
    )(own_cells, total, near, far, w, inv, p, links, view, ends)


def stages_of(axis):
    return lax.axis_size(axis).bit_length() - 1


def swap(value, axis, flip):
    count = lax.axis_size(axis)
    return lax.ppermute(value, axis, [(i, i ^ flip) for i in range(count)])


def on_right(axis, stage):
    return (lax.axis_index(axis) >> stage) % 2 == 1


def toward(right, block):
    return (
        jnp.where(right, block[R00], block[RLL]),
        jnp.where(right, block[FIRST], block[LAST]),
        jnp.where(right, block[C0], block[CL]),
    )


def join(a, b):
    joined, ties = join_coefs(a, b)
    (joined[FIRST], joined[LAST]), flux = join_targets((a[FIRST], a[LAST]), (b[FIRST], b[LAST]), ties)
    return joined, (flux, ties[1], ties[2])


def ordered(right, own, other):
    first = [jnp.where(right, theirs, mine) for mine, theirs in zip(own, other)]
    second = [jnp.where(right, mine, theirs) for mine, theirs in zip(own, other)]
    return first, second


def flips_of(width):
    return (1, 3, 2) if width == 2 else range(1, 1 << width)


def join_kernel(axis, stage, width, last, *refs):
    count = 1 << width
    at = {flip: 1 + n for n, flip in enumerate(flips_of(width))}
    blocks = [[refs[at.get(i, 0)][q] for q in range(7)] for i in range(count)]
    send = refs[-1 - width]
    links = refs[-width:]
    for bit in range(width):
        right = on_right(axis, stage + bit)
        for i in range(count):
            if not i >> bit & 1:
                j = i | 1 << bit
                blocks[i], blocks[j] = ordered(right, blocks[i], blocks[j])
    for bit in range(width):
        pairs = [join(blocks[i], blocks[i + 1]) for i in range(0, len(blocks), 2)]
        blocks = [p[0] for p in pairs]
        ties = [p[1] for p in pairs]
        for upper in range(bit + 1, width):
            right = on_right(axis, stage + upper)
            ties = [
                tuple(jnp.where(right, v, u) for u, v in zip(ties[i], ties[i + 1]))
                for i in range(0, len(ties), 2)
            ]
        for i in range(3):
            links[bit][i] = ties[0][i]
    (whole,) = blocks
    if last:
        for n, value in enumerate(toward(on_right(axis, stage + width), whole)):
            send[n] = value
    else:
        for q in range(7):
            send[q] = whole[q]


def join_stage(own, got, axis, stage, width, last, after):
    lines = own.shape[1]
    return pl.pallas_call(
        functools.partial(join_kernel, axis, stage, width, last),
        in_specs=[IN_VMEM] * (1 + len(got)) + [ANYWHERE] * len(after),
        out_shape=[shape_of(3 if last else 7, lines, LANES)] + [shape_of(3, lines, LANES)] * width,
        compiler_params=params(),
    )(own, *got, *after)


def gather_line(view, axis, widest=1, meanwhile=(), cross=False):
    stages = stages_of(axis)
    links, stage = [], 0
    while stage < stages - 1:
        width = min(widest, stages - 1 - stage)
        got = [swap(view, axis, flip << stage) for flip in flips_of(width)]
        last = stage + width == stages - 1
        view, *ties = join_stage(view, got, axis, stage, width, last, meanwhile)
        links += ties
        stage += width
        meanwhile = ()
    return view, swap(view, axis, 1 << stage | (cross and stage > 0)), links


def top_flux(axis, stages, own, got):
    right = on_right(axis, stages - 1)
    face = own[2] + got[2]
    jump = jnp.where(right, own[1] - got[1], got[1] - own[1])
    return jump * face * inverse(1.0 + face * (own[0] + got[0]))


def block_ends(axis, stages, links):
    shape = links[0].shape[1:] if links else None
    right = on_right(axis, stages - 1)
    zero = jnp.zeros(shape, F32)
    low, high = zero, zero
    unit_low = zero + jnp.where(right, -1.0, 0.0)
    unit_high = zero + jnp.where(right, 0.0, 1.0)
    for stage in range(stages - 2, -1, -1):
        tie = links[stage]
        right = on_right(axis, stage)
        flux = between(tie[0], tie[1], tie[2], low, high)
        unit = between(0.0, tie[1], tie[2], unit_low, unit_high)
        low, high = jnp.where(right, -flux, low), jnp.where(right, high, flux)
        unit_low, unit_high = jnp.where(right, -unit, unit_low), jnp.where(right, unit_high, unit)
    return (low, high), (unit_low, unit_high)


def natural(index, parts):
    span = SUBLANES * parts
    local = index % span
    return index - local + local % SUBLANES * parts + local // SUBLANES


def turn_matrix(shape, from_natural, parts):
    row = lax.broadcasted_iota(jnp.int32, shape, 0)
    column = lax.broadcasted_iota(jnp.int32, shape, 1) % LANES
    hit = natural(row, parts) == column if from_natural else row == natural(column, parts)
    return jnp.where(hit, 1.0, 0.0).astype(jnp.bfloat16)


def turned(matrix, field, rows=None):
    high = field.astype(jnp.bfloat16).astype(F32)
    both = jnp.concatenate([high, field - high], 1)
    if rows:
        both = jnp.concatenate(
            [jnp.broadcast_to(both[n : n + 1, :], (rows, 2 * LANES)) for n in range(field.shape[0])], 0
        )
    both = both.astype(jnp.bfloat16)
    return lax.dot_general(
        matrix, both, (((1,), (1,)), ((), ())), preferred_element_type=F32
    )


def y_factor_kernel(c_ref, after, w_ref, i_ref, p_ref, inner, outer, view, to_y, to_x, unit_low, unit_high, c_s, q_s, r_s):
    chunks, sheets, rows, _ = c_ref.shape
    each = LANES // rows
    pairs = sheets // each
    x_steps = rows // SUBLANES
    steps = LANES // SUBLANES
    to_y[...] = turn_matrix(to_y.shape, True, steps)
    to_x[...] = turn_matrix(to_x.shape, False, x_steps)
    for m in range(pairs):
        for y in range(chunks):
            block = jnp.concatenate(
                [
                    c_ref[y, m * each + i, pl.ds(k, SUBLANES, stride=x_steps), :]
                    for i in range(each)
                    for k in range(x_steps)
                ],
                0,
            )
            c_s[m, part_of(y), :] = block.T

    members = [(y, m) for y in range(chunks) for m in range(pairs)]
    lines = len(members)

    def cond(k):
        return jnp.stack([c_s[m, pl.ds(y * LANES + k, SUBLANES, stride=steps), :] for y, m in members], 0)

    def keep(k, w, inv, p):
        w_ref[k] = w
        i_ref[k] = inv
        p_ref[k] = p

    block = factor(cond, steps, keep)
    for n, q in enumerate(COEFS):
        for i in range(lines):
            q_s[n, i * SUBLANES : (i + 1) * SUBLANES, :] = block[q][i]
    segments = [
        {q: q_s[n, pl.ds(s, lines, stride=SUBLANES), :] for n, q in enumerate(COEFS)}
        for s in range(SUBLANES)
    ]
    whole, levels = tree(segments, join_coefs)
    for (offset, _), level in zip(node_offsets(SUBLANES), levels):
        for n, values in enumerate(level):
            for i in range(3):
                inner[offset + n, i] = values[i]
    for n, q in enumerate(COEFS):
        r_s[n] = whole[q]
    parts = [
        {q: r_s[n, y * pairs : (y + 1) * pairs, :] for n, q in enumerate(COEFS)} for y in range(chunks)
    ]
    whole, levels = tree(parts, join_coefs)
    for (offset, _), level in zip(node_offsets(chunks), levels):
        for n, values in enumerate(level):
            for i in range(3):
                outer[offset + n, i] = values[i]
    for n, q in enumerate(COEFS):
        view[n] = whole[q]

    same = turn_matrix(to_y.shape, True, 1)
    one = jnp.ones((pairs, LANES), F32)
    for n, (low, high, field) in enumerate(((one, 0.0 * one, unit_low), (0.0 * one, one, unit_high))):
        for y, pair in enumerate(tree_ends(chunks, outer, nothing, low, high)):
            for i in range(2):
                r_s[2 * n + i, y * pairs : (y + 1) * pairs, :] = pair[i]
        for s, pair in enumerate(tree_ends(SUBLANES, inner, nothing, r_s[2 * n], r_s[2 * n + 1])):
            for i in range(2):
                q_s[2 * n + i, pl.ds(s, lines, stride=SUBLANES), :] = pair[i]
        low, value = (
            jnp.stack(
                [q_s[2 * n + i, j * SUBLANES : (j + 1) * SUBLANES, :] for j in range(lines)], 0
            )
            for i in range(2)
        )
        for k in range(steps - 1, -1, -1):
            value = w_ref[k] * value + p_ref[k] * low
            for j, (y, m) in enumerate(members):
                c_s[m, pl.ds(y * LANES + k, SUBLANES, stride=steps), :] = value[j]
        for y, m in members:
            field[y, part_of(m), :] = turned(same, c_s[m, part_of(y), :])


def y_factor(c, after):
    chunks, sheets, rows, _ = c.shape
    pairs = sheets * rows // LANES
    lines = chunks * pairs
    stored = shape_of(LANES // SUBLANES, lines, SUBLANES, LANES)
    matrix = jax.ShapeDtypeStruct((LANES, 2 * LANES), jnp.bfloat16)
    return pl.pallas_call(
        y_factor_kernel,
        in_specs=[IN_VMEM, ANYWHERE],
        out_shape=[
            stored,
            stored,
            stored,
            shape_of(SUBLANES - 1, 3, lines, LANES),
            shape_of(chunks - 1, 3, pairs, LANES),
            shape_of(len(COEFS), pairs, LANES),
            matrix,
            matrix,
            shape_of(chunks, pairs * LANES, LANES),
            shape_of(chunks, pairs * LANES, LANES),
        ],
        scratch_shapes=[
            pltpu.VMEM((pairs, chunks * LANES, LANES), F32),
            pltpu.VMEM((len(COEFS), lines * SUBLANES, LANES), F32),
            pltpu.VMEM((len(COEFS), lines, LANES), F32),
        ],
        compiler_params=params(),
        cost_estimate=pl.CostEstimate(flops=20 * c.size, bytes_accessed=16 * c.size, transcendentals=0),
    )(c, after)


def z_factor_kernel(c_ref, after, w_ref, i_ref):
    sheets = c_ref.shape[1]
    ground = 1.0
    for z in range(sheets - 1):
        face = c_ref[:, z] + c_ref[:, z + 1]
        inv = inverse(ground + face)
        w = face * inv
        i_ref[z] = inv
        w_ref[z] = w
        ground = 1.0 + w * ground
    i_ref[sheets - 1] = inverse(ground)


def z_factor(c, after):
    chunks, sheets, rows, _ = c.shape
    return pl.pallas_call(
        z_factor_kernel,
        in_specs=[IN_VMEM, ANYWHERE],
        out_shape=[
            shape_of(sheets - 1, chunks, rows, LANES),
            shape_of(sheets, chunks, rows, LANES),
        ],
        compiler_params=params(),
        cost_estimate=pl.CostEstimate(flops=10 * c.size, bytes_accessed=12 * c.size, transcendentals=0),
    )(c, after)


def join_tree(items, links, own):
    for offset, count in node_offsets(len(items)):
        joined = []
        for n in range(count):
            tie = tuple(links[offset + n, i] for i in range(3))
            both, flux = join_targets(items[2 * n], items[2 * n + 1], tie)
            own[offset + n] = flux
            joined.append(both)
        items = joined
    return items[0]


def tree_ends(leaves, links, own, low, high):
    levels = [
        [(own(offset + n), links[offset + n, 1], links[offset + n, 2]) for n in range(count)]
        for offset, count in node_offsets(leaves)
    ]
    return descend(levels, low, high)


def nothing(node):
    return 0.0


def y_prepare_kernel(stages, *refs):
    ties = refs[: stages - 1]
    xw, xh, xm, xp, x_links, x_own, t_ref, to_y, y_low, y_high = refs[stages - 1 : stages + 9]
    base, response, to_first, to_last, fixed, f_s, g_s = refs[stages + 9 :]
    x_steps, lines = xw.shape[:2]
    chunks = base.shape[0]
    sheets = lines // chunks
    rows = x_steps * SUBLANES

    ends, units = block_ends("gx", stages, ties)
    for n, (own, (low, high)) in enumerate(((lambda i: x_own[i], ends), (nothing, units))):
        for s, pair in enumerate(tree_ends(SUBLANES, x_links, own, low, high)):
            for i in range(2):
                f_s[n, i, pl.ds(s, lines, stride=SUBLANES), :] = pair[i]
    first = 0
    for n, members in enumerate(line_groups(chunks, sheets)):
        at = slice(first, first + len(members))
        h_ref_of, h_at = (xh, at) if n == 0 else (xm, slice(first - 2 * sheets, at.stop - 2 * sheets))
        (low, value), (unit_low, unit) = (
            [
                jnp.stack(
                    [f_s[q, i, j * SUBLANES : (j + 1) * SUBLANES, :] for j in range(at.start, at.stop)], 0
                )
                for i in range(2)
            ]
            for q in range(2)
        )
        for k in range(x_steps - 1, -1, -1):
            w, p = xw[k, at], xp[k, at]
            value = w * value + (h_ref_of[k, h_at] + p * low)
            unit = w * unit + p * unit_low
            field = value - t_ref[k, at]
            for j, (y, z) in enumerate(members):
                place = z * rows + k * SUBLANES
                g_s[0, y, place : place + SUBLANES, :] = field[j]
                g_s[1, y, place : place + SUBLANES, :] = unit[j]
        first = at.stop

    totals = [None, None]
    for y in range(chunks):
        base[y] = turned(to_y[...], g_s[0, y])
        response[y] = turned(to_y[...], g_s[1, y])
        for i, (unit, weight) in enumerate(((y_low, to_first), (y_high, to_last))):
            weight[y] = unit[y] * g_s[1, y]
            part = unit[y] * g_s[0, y]
            totals[i] = part if y == 0 else totals[i] + part
    for i in range(2):
        put_sums(fixed.at[i], totals[i])


def put_sums(out, field):
    ones = jnp.ones((2 * SUBLANES, 2 * LANES), jnp.bfloat16)
    total = turned(ones, field)
    for m in range(out.shape[0]):
        out[m : m + 1, :] = total[:1, part_of(m)]


def y_prepare(ties, xw, xh, xm, xp, x_links, x_own, t, to_y, unit_low, unit_high):
    chunks = unit_low.shape[0]
    x_steps, lines = xw.shape[:2]
    width = lines // chunks * x_steps * SUBLANES
    field, weight = shape_of(chunks, LANES, width), shape_of(chunks, width, LANES)
    return pl.pallas_call(
        functools.partial(y_prepare_kernel, len(ties) + 1),
        out_shape=[field] * 2 + [weight] * 2 + [shape_of(2, width // LANES, LANES)],
        scratch_shapes=[
            pltpu.VMEM((2, 2, lines * SUBLANES, LANES), F32),
            pltpu.VMEM((2, chunks, width, LANES), F32),
        ],
        compiler_params=params(),
        cost_estimate=pl.CostEstimate(flops=8 * t.size, bytes_accessed=16 * t.size, transcendentals=0),
    )(*ties, xw, xh, xm, xp, x_links, x_own, t, to_y, unit_low, unit_high)


def sheet_rows(values, y, chunks, sheets):
    line_of = {member: n for n, member in enumerate(sum(line_groups(chunks, sheets), []))}
    return [values[line_of[y, z] : line_of[y, z] + 1, :] for z in range(sheets)]


def y_target_kernel(stages, own, got, to_first, to_last, fixed, view, flux_ref, send, r_s):
    chunks, width, _ = to_first.shape
    sheets = own.shape[1] // chunks
    rows = width // sheets

    flux = top_flux("gx", stages, own, got)
    flux_ref[...] = flux
    totals = [[None] * sheets, [None] * sheets]
    for y in range(chunks):
        for z, row in enumerate(sheet_rows(flux, y, chunks, sheets)):
            for total, weight in zip(totals, (to_first, to_last)):
                part = weight[y, z * rows : (z + 1) * rows, :] * row
                total[z] = part if y == 0 else total[z] + part
    for n, q in enumerate(COEFS):
        send[q] = view[n]
    for i, q in enumerate((FIRST, LAST)):
        put_sums(r_s.at[i], jnp.concatenate(totals[i], 0))
        send[q] = fixed[i] + r_s[i]


def y_target(own, got, to_first, to_last, fixed, view):
    pairs = view.shape[1]
    return pl.pallas_call(
        functools.partial(y_target_kernel, stages_of("gx")),
        out_shape=[shape_of(*own.shape[1:]), shape_of(7, pairs, LANES)],
        scratch_shapes=[pltpu.VMEM((2, pairs, LANES), F32)],
        compiler_params=params(),
    )(own, got, to_first, to_last, fixed, view)


def y_eliminate_kernel(base, response, flux, to_y, yw, yi, yp, inner, outer, after, *refs):
    h_ref, inner_own, outer_own, q_s, r_s = refs
    chunks, _, width = base.shape
    pairs = width // LANES
    sheets = flux.shape[0] // chunks
    steps = yw.shape[0]
    members = [(y, m) for y in range(chunks) for m in range(pairs)]
    fields = []
    for y in range(chunks):
        by_sheet = jnp.concatenate(sheet_rows(flux[...], y, chunks, sheets), 0)
        fields.append(base[y] + response[y] * turned(to_y[...], by_sheet, width // sheets))

    def target(k):
        at = slice(k * SUBLANES, (k + 1) * SUBLANES)
        return jnp.stack([fields[y][at, part_of(m)] for y, m in members], 0)

    def keep(k, h):
        h_ref[k] = h

    ends = eliminate(target, steps, lambda k: yw[k], lambda k: yi[k], lambda k: yp[k], keep)
    for q in range(2):
        for i in range(len(members)):
            q_s[q, i * SUBLANES : (i + 1) * SUBLANES, :] = ends[q][i]
    items = [
        tuple(q_s[q, pl.ds(s, len(members), stride=SUBLANES), :] for q in range(2))
        for s in range(SUBLANES)
    ]
    r_s[0], r_s[1] = join_tree(items, inner, inner_own)
    items = [tuple(r_s[q, y * pairs : (y + 1) * pairs, :] for q in range(2)) for y in range(chunks)]
    join_tree(items, outer, outer_own)


def y_eliminate(base, response, flux, to_y, yw, yi, yp, inner, outer, after):
    y_lines = yw.shape[1]
    pairs = outer.shape[2]
    chunks = y_lines // pairs
    return pl.pallas_call(
        y_eliminate_kernel,
        in_specs=[IN_VMEM] * 9 + [ANYWHERE],
        out_shape=[
            shape_of(*yw.shape),
            shape_of(SUBLANES - 1, y_lines, LANES),
            shape_of(chunks - 1, pairs, LANES),
        ],
        scratch_shapes=[
            pltpu.VMEM((2, y_lines * SUBLANES, LANES), F32),
            pltpu.VMEM((2, y_lines, LANES), F32),
        ],
        compiler_params=params(),
        cost_estimate=pl.CostEstimate(flops=8 * base.size, bytes_accessed=16 * base.size, transcendentals=0),
    )(base, response, flux, to_y, yw, yi, yp, inner, outer, after)


def z_solve(zw, zi, field, at, keep):
    sheets = zi.shape[0]
    rhs, kept = None, []
    for z in range(sheets):
        rhs = field(z) if z == 0 else field(z) + zw[(z - 1, *at)] * rhs
        kept.append(rhs * zi[(z, *at)])
    value = kept[-1]
    keep(sheets - 1, value)
    for z in range(sheets - 2, -1, -1):
        value = zw[(z, *at)] * value + kept[z]
        keep(z, value)


def finish_prepare_kernel(stages, *refs):
    ties = refs[: stages - 1]
    yw, yh, yp, inner, inner_own, outer, outer_own, zw, zi, t_ref, to_x = refs[stages - 1 : stages + 10]
    base, response, r_s, e_s, u_s = refs[stages + 10 :]
    chunks, sheets, rows, _ = base.shape
    each = LANES // rows
    pairs = sheets // each
    steps = yw.shape[0]
    lines = chunks * pairs

    ends, units = block_ends("gy", stages, ties)
    both = (
        (lambda i: outer_own[i], lambda i: inner_own[i], ends),
        (nothing, nothing, units),
    )
    for n, (upper, lower, (low, high)) in enumerate(both):
        for y, pair in enumerate(tree_ends(chunks, outer, upper, low, high)):
            for i in range(2):
                r_s[n, i, y * pairs : (y + 1) * pairs, :] = pair[i]
        for s, pair in enumerate(tree_ends(SUBLANES, inner, lower, r_s[n, 0], r_s[n, 1])):
            for i in range(2):
                e_s[n, i, pl.ds(s, lines, stride=SUBLANES), :] = pair[i]
    (low, value), (unit_low, unit) = (
        [
            jnp.stack([e_s[q, i, n * SUBLANES : (n + 1) * SUBLANES, :] for n in range(lines)], 0)
            for i in range(2)
        ]
        for q in range(2)
    )
    for k in range(steps - 1, -1, -1):
        w, p = yw[k], yp[k]
        value = w * value + (yh[k] + p * low)
        unit = w * unit + p * unit_low
        for y in range(chunks):
            for m in range(pairs):
                place = pl.ds(y * LANES + k, SUBLANES, stride=steps)
                u_s[0, m, place, :] = value[y * pairs + m]
                u_s[1, m, place, :] = unit[y * pairs + m]

    for y in range(chunks):
        part = part_of(y)
        fields = [turned(to_x[...], u_s[0, m, part, :]) for m in range(pairs)]

        def field(z):
            at = z % each * rows
            return fields[z // each][at : at + rows, :]

        def keep(z, value):
            base[y, z] = t_ref[z, :, part] + value

        z_solve(zw, zi, field, (y,), keep)
        for m in range(pairs):
            units = turned(to_x[...], u_s[1, m, part, :])
            for i in range(each):
                response[y, m * each + i] = units[i * rows : (i + 1) * rows, :]


def finish_prepare(ties, yw, yh, yp, inner, inner_own, outer, outer_own, zw, zi, t, to_x):
    sheets, rows, columns = t.shape
    chunks = columns // LANES
    pairs = sheets * rows // LANES
    lines = chunks * pairs
    field = shape_of(chunks, sheets, rows, LANES)
    return pl.pallas_call(
        functools.partial(finish_prepare_kernel, len(ties) + 1),
        out_shape=[field, field],
        scratch_shapes=[
            pltpu.VMEM((2, 2, lines, LANES), F32),
            pltpu.VMEM((2, 2, lines * SUBLANES, LANES), F32),
            pltpu.VMEM((2, pairs, columns, LANES), F32),
        ],
        compiler_params=params(),
        cost_estimate=pl.CostEstimate(flops=12 * t.size, bytes_accessed=20 * t.size, transcendentals=0),
    )(*ties, yw, yh, yp, inner, inner_own, outer, outer_own, zw, zi, t, to_x)


def finish_kernel(stages, own, got, base, response, zw, zi, to_x, out, o_s, sems):
    chunks, sheets, rows, _ = base.shape
    each = LANES // rows
    pairs = sheets // each
    flux = top_flux("gy", stages, own, got)
    wide = turned(to_x[...], flux, LANES)
    spread = [wide[:, part_of(m)] for m in range(pairs)]
    started = []
    block = rows // OUT_COPIES
    for n in range(OUT_COPIES):
        strip = slice(n * block, (n + 1) * block)
        for y in range(chunks):

            def field(z):
                at = z % each * rows + strip.start
                return response[y, z, strip, :] * spread[z // each][at : at + block, :]

            def keep(z, value):
                o_s[z, strip, part_of(y)] = base[y, z, strip, :] + value

            z_solve(zw, zi, field, (y, strip), keep)
        at = pl.ds(strip.start, block)
        copy = pltpu.make_async_copy(o_s.at[:, at, :], out.at[:, at, :], sems.at[n])
        copy.start()
        started.append(copy)
    for copy in started:
        copy.wait()


def finish(own, got, base, response, zw, zi, to_x):
    chunks, sheets, rows, _ = base.shape
    shape = (sheets, rows, chunks * LANES)
    return pl.pallas_call(
        functools.partial(finish_kernel, stages_of("gy")),
        out_shape=shape_of(*shape),
        out_specs=ANYWHERE,
        scratch_shapes=[pltpu.VMEM(shape, F32), pltpu.SemaphoreType.DMA((OUT_COPIES,))],
        compiler_params=params(),
    )(own, got, base, response, zw, zi, to_x)


def per_device(temperature, base, locations, energy):
    columns = temperature.shape[2]
    gy = lax.axis_size("gy")
    t, b, loc, heat, packed = load(temperature, base, locations[None], energy[None])
    near = swap(packed, "gy", 1)
    far = lax.ppermute(packed, "gy", [(i, ((i + 1) % gy ^ 1) - 1 if i else gy - 1) for i in range(gy)])
    c, total, xw, xi, xp, x_links, x_view, xm, ends, t_steps, swapped = x_factor(loc, heat, t, b, columns * gy, packed)
    xh, x_own, view = x_target(swapped, total, near, far, xw, xi, xp, x_links, x_view, ends)
    yw, yi, yp, inner, outer, y_view, to_y, to_x, unit_low, unit_high = y_factor(c, x_view)
    zw, zi = z_factor(c, view)
    own, got, ties = gather_line(view, "gx", 2, (y_view, zw))
    base, response, to_first, to_last, fixed = y_prepare(
        ties, xw, xh, xm, xp, x_links, x_own, t_steps, to_y, unit_low, unit_high
    )
    flux, view = y_target(own, got, to_first, to_last, fixed, y_view)
    yh, inner_own, outer_own = y_eliminate(
        base, response, flux, to_y, yw, yi, yp, inner, outer, view
    )
    own, got, ties = gather_line(view, "gy", meanwhile=(yh,), cross=True)
    base, response = finish_prepare(
        ties, yw, yh, yp, inner, inner_own, outer, outer_own, zw, zi, t, to_x
    )
    return finish(own, got, base, response, zw, zi, to_x)


def solution(mesh):
    in_specs = (P(None, "gx", "gy"), P(None, "gx", "gy"), P(), P())
    out_specs = P(None, "gx", "gy")
    return jax.shard_map(
        per_device, mesh=mesh, in_specs=in_specs, out_specs=out_specs, check_vma=False
    )
```

```python
import functools

import jax
import jax.numpy as jnp
from jax import lax
from jax.experimental import pallas as pl
from jax.experimental.pallas import tpu as pltpu
from jax.sharding import PartitionSpec as P

RATE = 2000.0
THERMAL_GROWTH = 0.8
LANES = 128
SUBLANES = 8
F32 = jnp.float32
MIB = 1024 * 1024
OUT_COPIES = 4
ANYWHERE = pl.BlockSpec(memory_space=pl.ANY)
IN_HBM = pl.BlockSpec(memory_space=pltpu.HBM)
IN_VMEM = pl.BlockSpec(memory_space=pltpu.VMEM)

R00, R0L, RLL, FIRST, LAST, C0, CL = range(7)
COEFS = (R00, R0L, RLL, C0, CL)


def params(limit=40):
    return pltpu.CompilerParams(vmem_limit_bytes=limit * MIB)


def shape_of(*sizes):
    return jax.ShapeDtypeStruct(sizes, F32)


def half_conduct(base, temperature):
    return base * (0.5 * RATE + (0.5 * RATE * THERMAL_GROWTH) * temperature)


def inverse(x):
    guess = pl.reciprocal(x, approx=True)
    return guess * (2.0 - x * guess)


def join_coefs(a, b):
    face = a[CL] + b[C0]
    inv = face * inverse(1.0 + face * (a[RLL] + b[R00]))
    left = a[R0L] * inv
    right = b[R0L] * inv
    joined = {
        R00: a[R00] - left * a[R0L],
        R0L: left * b[R0L],
        RLL: b[RLL] - right * b[R0L],
        C0: a[C0],
        CL: b[CL],
    }
    return joined, (inv, right, left)


def join_targets(a, b, links):
    inv, right, left = links
    jump = b[0] - a[1]
    return (a[0] + left * jump, b[1] - right * jump), jump * inv


def between(own, right, left, low, high):
    return own + right * high - left * low


def tree(items, join):
    levels = []
    while len(items) > 1:
        pairs = [join(items[i], items[i + 1]) for i in range(0, len(items), 2)]
        items = [p[0] for p in pairs]
        levels.append([p[1] for p in pairs])
    return items[0], levels


def descend(levels, low, high):
    ends = [(low, high)]
    for level in reversed(levels):
        below = []
        for (lo, hi), (own, right, left) in zip(ends, level):
            flux = between(own, right, left, lo, hi)
            below += [(lo, flux), (-flux, hi)]
        ends = below
    return ends


def node_offsets(leaves):
    offsets, at, count = [], 0, leaves // 2
    while count:
        offsets.append((at, count))
        at += count
        count //= 2
    return offsets


def factor(cond, steps, keep):
    here = cond(0)
    c_first = here
    one = jnp.ones_like(here)
    ground, path, first_first = one, one, None
    for k in range(steps - 1):
        following = cond(k + 1)
        face = here + following
        inv = inverse(ground + face)
        w = face * inv
        p = path * inv
        keep(k, w, inv, p)
        step = path * p
        first_first = step if first_first is None else first_first + step
        path = path * w
        ground = 1.0 + w * ground
        here = following
    inv = inverse(ground)
    p = path * inv
    keep(steps - 1, inv, inv, p)
    return {R00: first_first + path * p, R0L: p, RLL: inv, C0: c_first, CL: here}


def eliminate(target, steps, w, inv, p, keep):
    rhs = target(0)
    first = None
    for k in range(steps):
        h = rhs * inv(k)
        keep(k, h)
        step = rhs * p(k)
        first = step if first is None else first + step
        if k < steps - 1:
            rhs = target(k + 1) + w(k) * rhs
    return first, h


def is_odd(axis):
    return lax.axis_index(axis) % 2 == 1


def fold(cells, used):
    steps = cells.shape[0] // SUBLANES
    total = cells[pl.ds(0, SUBLANES, stride=steps), :]
    lane = lax.broadcasted_iota(jnp.int32, total.shape, 1)
    for k in range(1, steps):
        part = pltpu.roll(cells[pl.ds(k, SUBLANES, stride=steps), :], k * used, 1)
        total = jnp.where(lane // used == k, part, total)
    return total


def load_kernel(t_hbm, b_hbm, loc_hbm, energy_hbm, t_out, b_out, loc, energy, packed, cells, sems):
    sheets, rows, columns = t_hbm.shape
    parts = [(0, LANES), (columns - LANES, LANES), (LANES, columns - 2 * LANES)]
    copies = []
    for n, (start, size) in enumerate(parts):
        part = pl.ds(start, size)
        for i, (src, dst) in enumerate(((t_hbm, t_out), (b_hbm, b_out))):
            copies.append(
                pltpu.make_async_copy(src.at[:, :, part], dst.at[:, :, part], sems.at[i, n])
            )
    copies.append(pltpu.make_async_copy(loc_hbm, loc, sems.at[2, 0]))
    copies.append(pltpu.make_async_copy(energy_hbm, energy, sems.at[2, 1]))
    for copy in copies:
        copy.start()
    lane = lax.broadcasted_iota(jnp.int32, (rows, LANES), 1)
    edge_t = jnp.zeros((rows, LANES), F32)
    edge_c = edge_t
    for side, source in enumerate((0, LANES - 1)):
        for copy in copies[2 * side : 2 * side + 2]:
            copy.wait()
        part = slice(parts[side][0], parts[side][0] + LANES)
        for z in range(sheets):
            t = t_out[z, :, part]
            c = half_conduct(b_out[z, :, part], t)
            place = lane == sheets * side + z
            edge_t = jnp.where(place, t[:, source : source + 1], edge_t)
            edge_c = jnp.where(place, c[:, source : source + 1], edge_c)
    cells[0], cells[1] = edge_t, edge_c
    for i in range(2):
        packed[i * SUBLANES : (i + 1) * SUBLANES, :] = fold(cells.at[i], 2 * sheets)
    for copy in copies[4:]:
        copy.wait()


def load(temperature, base, locations, energy):
    sheets, rows, columns = temperature.shape
    assert rows // SUBLANES * 2 * sheets <= LANES and columns > 2 * LANES
    operands = (temperature, base, locations, energy)
    return pl.pallas_call(
        load_kernel,
        in_specs=[IN_HBM] * 4,
        out_shape=[pltpu.VMEM(v.shape, v.dtype) for v in operands]
        + [pltpu.VMEM((2 * SUBLANES, LANES), F32)],
        scratch_shapes=[pltpu.VMEM((2, rows, LANES), F32), pltpu.SemaphoreType.DMA((3, 3))],
        compiler_params=params(),
    )(*[pltpu.with_memory_space_constraint(v, pltpu.HBM) for v in operands])


def source_plane(loc, energy, rows, columns, plate):
    place = loc[...]
    count = place.shape[1]
    local_x = place // plate - lax.axis_index("gx") * rows
    local_y = place % plate - lax.axis_index("gy") * columns
    in_x = lax.broadcasted_iota(jnp.int32, (rows, count), 0) == local_x
    in_y = lax.broadcasted_iota(jnp.int32, (columns, count), 0) == local_y
    by_y = jnp.where(in_y, 1.0, 0.0).astype(jnp.bfloat16)
    left = energy[...]
    plane = None
    for _ in range(3):
        part = left.astype(jnp.bfloat16).astype(F32)
        left = left - part
        term = lax.dot_general(
            jnp.where(in_x, part, 0.0).astype(jnp.bfloat16),
            by_y,
            (((1,), (1,)), ((), ())),
            preferred_element_type=F32,
        )
        plane = term if plane is None else plane + term
    return plane


def part_of(y):
    return slice(y * LANES, (y + 1) * LANES)


def line_groups(chunks, sheets):
    order = [0, chunks - 1] + list(range(1, chunks - 1))
    return [[(y, z) for y in order[i : i + 2] for z in range(sheets)] for i in range(0, chunks, 2)]


def x_eliminate(cells, members, first_line, w_ref, i_ref, p_ref, h_ref, h_line, q_s):
    steps = w_ref.shape[0]
    at = slice(first_line, first_line + len(members))
    kept_at = slice(h_line, h_line + len(members))

    def target(k):
        return jnp.stack([cells(y, z, k) for y, z in members], 0)

    def keep(k, h):
        h_ref[k, kept_at] = h

    ends = eliminate(
        target, steps, lambda k: w_ref[k, at], lambda k: i_ref[k, at], lambda k: p_ref[k, at], keep
    )
    for q in range(2):
        for i in range(len(members)):
            first = (first_line + i) * SUBLANES
            q_s[q, first : first + SUBLANES, :] = ends[q][i]


def x_factor_kernel(plate, loc, energy, t_ref, b_ref, own_cells, *refs):
    c_ref, total_ref, w_ref, i_ref, p_ref, links, view, h_ref, ends_ref, t_out, swapped, q_s, t_s = refs
    chunks, sheets, rows, _ = c_ref.shape
    lines = chunks * sheets
    steps = rows // SUBLANES
    plane = source_plane(loc, energy, rows, chunks * LANES, plate)
    mine = own_cells[...]
    in_low = lax.broadcasted_iota(jnp.int32, mine.shape, 1) % (2 * sheets) < sheets
    swapped[...] = jnp.where(
        in_low, pltpu.roll(mine, LANES - sheets, 1), pltpu.roll(mine, sheets, 1)
    )

    lane = lax.broadcasted_iota(jnp.int32, (SUBLANES, LANES), 1)
    is_first, is_last = lane == 0, lane == LANES - 1
    for r in range(steps):
        at = slice(r * SUBLANES, (r + 1) * SUBLANES)
        before_t, before_c = None, None
        for z in range(sheets):
            ts = [t_ref[z, at, part_of(y)] for y in range(chunks)]
            cs = [half_conduct(b_ref[z, at, part_of(y)], ts[y]) for y in range(chunks)]
            t_turned = [pltpu.roll(v, LANES - 1, 1) for v in ts]
            c_turned = [pltpu.roll(v, LANES - 1, 1) for v in cs]
            flux = []
            for y in range(chunks):
                if y < chunks - 1:
                    t_next = jnp.where(is_last, t_turned[y + 1], t_turned[y])
                    c_next = jnp.where(is_last, c_turned[y + 1], c_turned[y])
                    flux.append((cs[y] + c_next) * (t_next - ts[y]))
                else:
                    inside = (cs[y] + c_turned[y]) * (t_turned[y] - ts[y])
                    flux.append(jnp.where(is_last, 0.0, inside))
            turned = [pltpu.roll(v, 1, 1) for v in flux]
            for y in range(chunks):
                from_low = jnp.where(is_first, turned[y - 1] if y else 0.0, turned[y])
                total = ts[y] + (flux[y] - from_low)
                if z == 0:
                    total = total + plane[at, part_of(y)]
                else:
                    across = (before_c[y] + cs[y]) * (ts[y] - before_t[y])
                    total = total - across
                    total_ref[y, z - 1, at, :] += across
                total_ref[y, z, at, :] = total
                c_ref[y, z, at, :] = cs[y]
                t_s[y, z, at, :] = ts[y]
            before_t, before_c = ts, cs

    at = 0
    for n, members in enumerate(line_groups(chunks, sheets)):

        def cond(k):
            return jnp.stack([c_ref[y, z, pl.ds(k, SUBLANES, stride=steps), :] for y, z in members], 0)

        def keep(k, w, inv, p):
            w_ref[k, at : at + len(members)] = w
            i_ref[k, at : at + len(members)] = inv
            p_ref[k, at : at + len(members)] = p

        block = factor(cond, steps, keep)
        for i, q in enumerate(COEFS):
            for j in range(len(members)):
                first = (at + j) * SUBLANES
                q_s[i, first : first + SUBLANES, :] = block[q][j]
        if n > 0:
            x_eliminate(
                lambda y, z, k: total_ref[y, z, pl.ds(k, SUBLANES, stride=steps), :],
                members, at, w_ref, i_ref, p_ref, h_ref, at - 2 * sheets, ends_ref,
            )
        for k in range(steps):
            for i, (y, z) in enumerate(members):
                t_out[k, at + i] = t_s[y, z, pl.ds(k, SUBLANES, stride=steps), :]
        at += len(members)

    segments = [
        {q: q_s[n, pl.ds(s, lines, stride=SUBLANES), :] for n, q in enumerate(COEFS)}
        for s in range(SUBLANES)
    ]
    whole, levels = tree(segments, join_coefs)
    for (offset, _), level in zip(node_offsets(SUBLANES), levels):
        for n, values in enumerate(level):
            for i in range(3):
                links[offset + n, i] = values[i]
    for n, q in enumerate(COEFS):
        view[n] = whole[q]


def x_factor(loc, energy, t, b, plate, own_cells):
    sheets, rows, columns = t.shape
    chunks = columns // LANES
    lines = chunks * sheets
    steps = rows // SUBLANES
    field = shape_of(chunks, sheets, rows, LANES)
    stored = shape_of(steps, lines, SUBLANES, LANES)
    return pl.pallas_call(
        functools.partial(x_factor_kernel, plate),
        in_specs=[IN_VMEM] * 5,
        out_shape=[
            field,
            field,
            stored,
            stored,
            stored,
            shape_of(SUBLANES - 1, 3, lines, LANES),
            shape_of(len(COEFS), lines, LANES),
            shape_of(steps, max(1, lines - 2 * sheets), SUBLANES, LANES),
            shape_of(2, lines * SUBLANES, LANES),
            stored,
            shape_of(*own_cells.shape),
        ],
        scratch_shapes=[
            pltpu.VMEM((len(COEFS), lines * SUBLANES, LANES), F32),
            pltpu.VMEM((chunks, sheets, rows, LANES), F32),
        ],
        compiler_params=params(),
        cost_estimate=pl.CostEstimate(flops=40 * t.size, bytes_accessed=28 * t.size, transcendentals=0),
    )(loc, energy, t, b, own_cells)


def x_target_kernel(own_cells, total_ref, near, far, *refs):
    w_ref, i_ref, p_ref, links, view, ends_ref, h_ref, own, send, q_s = refs
    chunks, sheets, rows, _ = total_ref.shape
    lines = chunks * sheets
    steps = rows // SUBLANES

    place = lax.axis_index("gy")
    inner = (place > 0) & (place < lax.axis_size("gy") - 1)
    lane = lax.broadcasted_iota(jnp.int32, (SUBLANES, LANES), 1)
    side = 2 * sheets
    is_near = (lane % side >= sheets).astype(jnp.int32) == place % 2
    t, c = (
        jnp.where(is_near, near[at, :], jnp.where(inner, far[at, :], 0.0))
        for at in (slice(0, SUBLANES), slice(SUBLANES, 2 * SUBLANES))
    )
    face = jnp.where(c > 0.0, own_cells[SUBLANES:, :] + c, 0.0)
    flux = face * (t - own_cells[:SUBLANES, :])

    def cells(y, z, k):
        at = k * side + (sheets + z if y == 0 else z)
        edge = 0 if y == 0 else LANES - 1
        inflow = jnp.where(lane == edge, flux[:, at : at + 1], 0.0)
        return total_ref[y, z, pl.ds(k, SUBLANES, stride=steps), :] + inflow

    members = line_groups(chunks, sheets)[0]
    x_eliminate(cells, members, 0, w_ref, i_ref, p_ref, h_ref, 0, q_s)
    split = len(members)
    items = [
        tuple(
            jnp.concatenate(
                [
                    q_s[q, pl.ds(s, split, stride=SUBLANES), :],
                    ends_ref[q, pl.ds(split * SUBLANES + s, lines - split, stride=SUBLANES), :],
                ],
                0,
            )
            for q in range(2)
        )
        for s in range(SUBLANES)
    ]
    for offset, count in node_offsets(SUBLANES):
        joined = []
        for n in range(count):
            ties = tuple(links[offset + n, i] for i in range(3))
            both, flux = join_targets(items[2 * n], items[2 * n + 1], ties)
            own[offset + n] = flux
            joined.append(both)
        items = joined
    for n, q in enumerate(COEFS):
        send[q] = view[n]
    send[FIRST], send[LAST] = items[0]


def x_target(own_cells, total, near, far, w, inv, p, links, view, ends):
    chunks, sheets, rows, _ = total.shape
    lines = chunks * sheets
    steps = rows // SUBLANES
    return pl.pallas_call(
        x_target_kernel,
        out_shape=[
            shape_of(steps, 2 * sheets, SUBLANES, LANES),
            shape_of(SUBLANES - 1, lines, LANES),
            shape_of(7, lines, LANES),
        ],
        scratch_shapes=[
            pltpu.VMEM((2, 2 * sheets * SUBLANES, LANES), F32),
        ],
        compiler_params=params(),
    )(own_cells, total, near, far, w, inv, p, links, view, ends)


def stages_of(axis):
    return lax.axis_size(axis).bit_length() - 1


def swap(value, axis, flip):
    count = lax.axis_size(axis)
    return lax.ppermute(value, axis, [(i, i ^ flip) for i in range(count)])


def on_right(axis, stage):
    return (lax.axis_index(axis) >> stage) % 2 == 1


def toward(right, block):
    return (
        jnp.where(right, block[R00], block[RLL]),
        jnp.where(right, block[FIRST], block[LAST]),
        jnp.where(right, block[C0], block[CL]),
    )


def join(a, b):
    joined, ties = join_coefs(a, b)
    (joined[FIRST], joined[LAST]), flux = join_targets((a[FIRST], a[LAST]), (b[FIRST], b[LAST]), ties)
    return joined, (flux, ties[1], ties[2])


def ordered(right, own, other):
    first = [jnp.where(right, theirs, mine) for mine, theirs in zip(own, other)]
    second = [jnp.where(right, mine, theirs) for mine, theirs in zip(own, other)]
    return first, second


def join_kernel(axis, stage, width, last, *refs):
    count = 1 << width
    blocks = [[refs[i][q] for q in range(7)] for i in range(count)]
    send = refs[-1 - width]
    links = refs[-width:]
    for bit in range(width):
        right = on_right(axis, stage + bit)
        for i in range(count):
            if not i >> bit & 1:
                j = i | 1 << bit
                blocks[i], blocks[j] = ordered(right, blocks[i], blocks[j])
    for bit in range(width):
        pairs = [join(blocks[i], blocks[i + 1]) for i in range(0, len(blocks), 2)]
        blocks = [p[0] for p in pairs]
        ties = [p[1] for p in pairs]
        for upper in range(bit + 1, width):
            right = on_right(axis, stage + upper)
            ties = [
                tuple(jnp.where(right, v, u) for u, v in zip(ties[i], ties[i + 1]))
                for i in range(0, len(ties), 2)
            ]
        for i in range(3):
            links[bit][i] = ties[0][i]
    (whole,) = blocks
    if last:
        for n, value in enumerate(toward(on_right(axis, stage + width), whole)):
            send[n] = value
    else:
        for q in range(7):
            send[q] = whole[q]


def join_stage(own, got, axis, stage, width, last, after):
    lines = own.shape[1]
    return pl.pallas_call(
        functools.partial(join_kernel, axis, stage, width, last),
        in_specs=[IN_VMEM] * (1 + len(got)) + [ANYWHERE] * len(after),
        out_shape=[shape_of(3 if last else 7, lines, LANES)] + [shape_of(3, lines, LANES)] * width,
        compiler_params=params(),
    )(own, *got, *after)


def gather_line(view, axis, widest=1, meanwhile=(), cross=False):
    stages = stages_of(axis)
    links, stage = [], 0
    while stage < stages - 1:
        width = min(widest, stages - 1 - stage)
        got = [swap(view, axis, flip << stage) for flip in range(1, 1 << width)]
        last = stage + width == stages - 1
        view, *ties = join_stage(view, got, axis, stage, width, last, meanwhile)
        links += ties
        stage += width
        meanwhile = ()
    return view, swap(view, axis, 1 << stage | (cross and stage > 0)), links


def top_flux(axis, stages, own, got):
    right = on_right(axis, stages - 1)
    face = own[2] + got[2]
    jump = jnp.where(right, own[1] - got[1], got[1] - own[1])
    return jump * face * inverse(1.0 + face * (own[0] + got[0]))


def block_ends(axis, stages, links):
    shape = links[0].shape[1:] if links else None
    right = on_right(axis, stages - 1)
    zero = jnp.zeros(shape, F32)
    low, high = zero, zero
    unit_low = zero + jnp.where(right, -1.0, 0.0)
    unit_high = zero + jnp.where(right, 0.0, 1.0)
    for stage in range(stages - 2, -1, -1):
        tie = links[stage]
        right = on_right(axis, stage)
        flux = between(tie[0], tie[1], tie[2], low, high)
        unit = between(0.0, tie[1], tie[2], unit_low, unit_high)
        low, high = jnp.where(right, -flux, low), jnp.where(right, high, flux)
        unit_low, unit_high = jnp.where(right, -unit, unit_low), jnp.where(right, unit_high, unit)
    return (low, high), (unit_low, unit_high)


def natural(index, parts):
    span = SUBLANES * parts
    local = index % span
    return index - local + local % SUBLANES * parts + local // SUBLANES


def turn_matrix(shape, from_natural, parts):
    row = lax.broadcasted_iota(jnp.int32, shape, 0)
    column = lax.broadcasted_iota(jnp.int32, shape, 1) % LANES
    hit = natural(row, parts) == column if from_natural else row == natural(column, parts)
    return jnp.where(hit, 1.0, 0.0).astype(jnp.bfloat16)


def turned(matrix, field, rows=None):
    high = field.astype(jnp.bfloat16).astype(F32)
    both = jnp.concatenate([high, field - high], 1)
    if rows:
        both = jnp.concatenate(
            [jnp.broadcast_to(both[n : n + 1, :], (rows, 2 * LANES)) for n in range(field.shape[0])], 0
        )
    both = both.astype(jnp.bfloat16)
    return lax.dot_general(
        matrix, both, (((1,), (1,)), ((), ())), preferred_element_type=F32
    )


def y_factor_kernel(c_ref, after, w_ref, i_ref, p_ref, inner, outer, view, to_y, to_x, unit_low, unit_high, c_s, q_s, r_s):
    chunks, sheets, rows, _ = c_ref.shape
    each = LANES // rows
    pairs = sheets // each
    x_steps = rows // SUBLANES
    steps = LANES // SUBLANES
    to_y[...] = turn_matrix(to_y.shape, True, steps)
    to_x[...] = turn_matrix(to_x.shape, False, x_steps)
    for m in range(pairs):
        for y in range(chunks):
            block = jnp.concatenate(
                [
                    c_ref[y, m * each + i, pl.ds(k, SUBLANES, stride=x_steps), :]
                    for i in range(each)
                    for k in range(x_steps)
                ],
                0,
            )
            c_s[m, part_of(y), :] = block.T

    members = [(y, m) for y in range(chunks) for m in range(pairs)]
    lines = len(members)

    def cond(k):
        return jnp.stack([c_s[m, pl.ds(y * LANES + k, SUBLANES, stride=steps), :] for y, m in members], 0)

    def keep(k, w, inv, p):
        w_ref[k] = w
        i_ref[k] = inv
        p_ref[k] = p

    block = factor(cond, steps, keep)
    for n, q in enumerate(COEFS):
        for i in range(lines):
            q_s[n, i * SUBLANES : (i + 1) * SUBLANES, :] = block[q][i]
    segments = [
        {q: q_s[n, pl.ds(s, lines, stride=SUBLANES), :] for n, q in enumerate(COEFS)}
        for s in range(SUBLANES)
    ]
    whole, levels = tree(segments, join_coefs)
    for (offset, _), level in zip(node_offsets(SUBLANES), levels):
        for n, values in enumerate(level):
            for i in range(3):
                inner[offset + n, i] = values[i]
    for n, q in enumerate(COEFS):
        r_s[n] = whole[q]
    parts = [
        {q: r_s[n, y * pairs : (y + 1) * pairs, :] for n, q in enumerate(COEFS)} for y in range(chunks)
    ]
    whole, levels = tree(parts, join_coefs)
    for (offset, _), level in zip(node_offsets(chunks), levels):
        for n, values in enumerate(level):
            for i in range(3):
                outer[offset + n, i] = values[i]
    for n, q in enumerate(COEFS):
        view[n] = whole[q]

    same = turn_matrix(to_y.shape, True, 1)
    one = jnp.ones((pairs, LANES), F32)
    for n, (low, high, field) in enumerate(((one, 0.0 * one, unit_low), (0.0 * one, one, unit_high))):
        for y, pair in enumerate(tree_ends(chunks, outer, nothing, low, high)):
            for i in range(2):
                r_s[2 * n + i, y * pairs : (y + 1) * pairs, :] = pair[i]
        for s, pair in enumerate(tree_ends(SUBLANES, inner, nothing, r_s[2 * n], r_s[2 * n + 1])):
            for i in range(2):
                q_s[2 * n + i, pl.ds(s, lines, stride=SUBLANES), :] = pair[i]
        low, value = (
            jnp.stack(
                [q_s[2 * n + i, j * SUBLANES : (j + 1) * SUBLANES, :] for j in range(lines)], 0
            )
            for i in range(2)
        )
        for k in range(steps - 1, -1, -1):
            value = w_ref[k] * value + p_ref[k] * low
            for j, (y, m) in enumerate(members):
                c_s[m, pl.ds(y * LANES + k, SUBLANES, stride=steps), :] = value[j]
        for y, m in members:
            field[y, part_of(m), :] = turned(same, c_s[m, part_of(y), :])


def y_factor(c, after):
    chunks, sheets, rows, _ = c.shape
    pairs = sheets * rows // LANES
    lines = chunks * pairs
    stored = shape_of(LANES // SUBLANES, lines, SUBLANES, LANES)
    matrix = jax.ShapeDtypeStruct((LANES, 2 * LANES), jnp.bfloat16)
    return pl.pallas_call(
        y_factor_kernel,
        in_specs=[IN_VMEM, ANYWHERE],
        out_shape=[
            stored,
            stored,
            stored,
            shape_of(SUBLANES - 1, 3, lines, LANES),
            shape_of(chunks - 1, 3, pairs, LANES),
            shape_of(len(COEFS), pairs, LANES),
            matrix,
            matrix,
            shape_of(chunks, pairs * LANES, LANES),
            shape_of(chunks, pairs * LANES, LANES),
        ],
        scratch_shapes=[
            pltpu.VMEM((pairs, chunks * LANES, LANES), F32),
            pltpu.VMEM((len(COEFS), lines * SUBLANES, LANES), F32),
            pltpu.VMEM((len(COEFS), lines, LANES), F32),
        ],
        compiler_params=params(),
        cost_estimate=pl.CostEstimate(flops=20 * c.size, bytes_accessed=16 * c.size, transcendentals=0),
    )(c, after)


def z_factor_kernel(c_ref, after, w_ref, i_ref):
    sheets = c_ref.shape[1]
    ground = 1.0
    for z in range(sheets - 1):
        face = c_ref[:, z] + c_ref[:, z + 1]
        inv = inverse(ground + face)
        w = face * inv
        i_ref[z] = inv
        w_ref[z] = w
        ground = 1.0 + w * ground
    i_ref[sheets - 1] = inverse(ground)


def z_factor(c, after):
    chunks, sheets, rows, _ = c.shape
    return pl.pallas_call(
        z_factor_kernel,
        in_specs=[IN_VMEM, ANYWHERE],
        out_shape=[
            shape_of(sheets - 1, chunks, rows, LANES),
            shape_of(sheets, chunks, rows, LANES),
        ],
        compiler_params=params(),
        cost_estimate=pl.CostEstimate(flops=10 * c.size, bytes_accessed=12 * c.size, transcendentals=0),
    )(c, after)


def join_tree(items, links, own):
    for offset, count in node_offsets(len(items)):
        joined = []
        for n in range(count):
            tie = tuple(links[offset + n, i] for i in range(3))
            both, flux = join_targets(items[2 * n], items[2 * n + 1], tie)
            own[offset + n] = flux
            joined.append(both)
        items = joined
    return items[0]


def tree_ends(leaves, links, own, low, high):
    levels = [
        [(own(offset + n), links[offset + n, 1], links[offset + n, 2]) for n in range(count)]
        for offset, count in node_offsets(leaves)
    ]
    return descend(levels, low, high)


def nothing(node):
    return 0.0


def y_prepare_kernel(stages, *refs):
    ties = refs[: stages - 1]
    xw, xh, xm, xp, x_links, x_own, t_ref, to_y, y_low, y_high = refs[stages - 1 : stages + 9]
    base, response, to_first, to_last, fixed, f_s, g_s = refs[stages + 9 :]
    x_steps, lines = xw.shape[:2]
    chunks = base.shape[0]
    sheets = lines // chunks
    rows = x_steps * SUBLANES

    ends, units = block_ends("gx", stages, ties)
    for n, (own, (low, high)) in enumerate(((lambda i: x_own[i], ends), (nothing, units))):
        for s, pair in enumerate(tree_ends(SUBLANES, x_links, own, low, high)):
            for i in range(2):
                f_s[n, i, pl.ds(s, lines, stride=SUBLANES), :] = pair[i]
    first = 0
    for n, members in enumerate(line_groups(chunks, sheets)):
        at = slice(first, first + len(members))
        h_ref_of, h_at = (xh, at) if n == 0 else (xm, slice(first - 2 * sheets, at.stop - 2 * sheets))
        (low, value), (unit_low, unit) = (
            [
                jnp.stack(
                    [f_s[q, i, j * SUBLANES : (j + 1) * SUBLANES, :] for j in range(at.start, at.stop)], 0
                )
                for i in range(2)
            ]
            for q in range(2)
        )
        for k in range(x_steps - 1, -1, -1):
            w, p = xw[k, at], xp[k, at]
            value = w * value + (h_ref_of[k, h_at] + p * low)
            unit = w * unit + p * unit_low
            field = value - t_ref[k, at]
            for j, (y, z) in enumerate(members):
                place = z * rows + k * SUBLANES
                g_s[0, y, place : place + SUBLANES, :] = field[j]
                g_s[1, y, place : place + SUBLANES, :] = unit[j]
        first = at.stop

    totals = [None, None]
    for y in range(chunks):
        base[y] = turned(to_y[...], g_s[0, y])
        response[y] = turned(to_y[...], g_s[1, y])
        for i, (unit, weight) in enumerate(((y_low, to_first), (y_high, to_last))):
            weight[y] = unit[y] * g_s[1, y]
            part = unit[y] * g_s[0, y]
            totals[i] = part if y == 0 else totals[i] + part
    for i in range(2):
        put_sums(fixed.at[i], totals[i])


def put_sums(out, field):
    ones = jnp.ones((2 * SUBLANES, 2 * LANES), jnp.bfloat16)
    total = turned(ones, field)
    for m in range(out.shape[0]):
        out[m : m + 1, :] = total[:1, part_of(m)]


def y_prepare(ties, xw, xh, xm, xp, x_links, x_own, t, to_y, unit_low, unit_high):
    chunks = unit_low.shape[0]
    x_steps, lines = xw.shape[:2]
    width = lines // chunks * x_steps * SUBLANES
    field, weight = shape_of(chunks, LANES, width), shape_of(chunks, width, LANES)
    return pl.pallas_call(
        functools.partial(y_prepare_kernel, len(ties) + 1),
        out_shape=[field] * 2 + [weight] * 2 + [shape_of(2, width // LANES, LANES)],
        scratch_shapes=[
            pltpu.VMEM((2, 2, lines * SUBLANES, LANES), F32),
            pltpu.VMEM((2, chunks, width, LANES), F32),
        ],
        compiler_params=params(),
        cost_estimate=pl.CostEstimate(flops=8 * t.size, bytes_accessed=16 * t.size, transcendentals=0),
    )(*ties, xw, xh, xm, xp, x_links, x_own, t, to_y, unit_low, unit_high)


def sheet_rows(values, y, chunks, sheets):
    line_of = {member: n for n, member in enumerate(sum(line_groups(chunks, sheets), []))}
    return [values[line_of[y, z] : line_of[y, z] + 1, :] for z in range(sheets)]


def y_target_kernel(stages, own, got, to_first, to_last, fixed, view, flux_ref, send, r_s):
    chunks, width, _ = to_first.shape
    sheets = own.shape[1] // chunks
    rows = width // sheets

    flux = top_flux("gx", stages, own, got)
    flux_ref[...] = flux
    totals = [[None] * sheets, [None] * sheets]
    for y in range(chunks):
        for z, row in enumerate(sheet_rows(flux, y, chunks, sheets)):
            for total, weight in zip(totals, (to_first, to_last)):
                part = weight[y, z * rows : (z + 1) * rows, :] * row
                total[z] = part if y == 0 else total[z] + part
    for n, q in enumerate(COEFS):
        send[q] = view[n]
    put_sums(r_s, jnp.concatenate(totals[0] + totals[1], 0))
    pairs = view.shape[1]
    for i, q in enumerate((FIRST, LAST)):
        send[q] = fixed[i] + r_s[i * pairs : (i + 1) * pairs, :]


def y_target(own, got, to_first, to_last, fixed, view):
    pairs = view.shape[1]
    return pl.pallas_call(
        functools.partial(y_target_kernel, stages_of("gx")),
        out_shape=[shape_of(*own.shape[1:]), shape_of(7, pairs, LANES)],
        scratch_shapes=[pltpu.VMEM((2 * pairs, LANES), F32)],
        compiler_params=params(),
    )(own, got, to_first, to_last, fixed, view)


def y_eliminate_kernel(base, response, flux, to_y, yw, yi, yp, inner, outer, after, *refs):
    h_ref, inner_own, outer_own, q_s, r_s = refs
    chunks, _, width = base.shape
    pairs = width // LANES
    sheets = flux.shape[0] // chunks
    steps = yw.shape[0]
    members = [(y, m) for y in range(chunks) for m in range(pairs)]
    fields = []
    for y in range(chunks):
        by_sheet = jnp.concatenate(sheet_rows(flux[...], y, chunks, sheets), 0)
        fields.append(base[y] + response[y] * turned(to_y[...], by_sheet, width // sheets))

    def target(k):
        at = slice(k * SUBLANES, (k + 1) * SUBLANES)
        return jnp.stack([fields[y][at, part_of(m)] for y, m in members], 0)

    def keep(k, h):
        h_ref[k] = h

    ends = eliminate(target, steps, lambda k: yw[k], lambda k: yi[k], lambda k: yp[k], keep)
    for q in range(2):
        for i in range(len(members)):
            q_s[q, i * SUBLANES : (i + 1) * SUBLANES, :] = ends[q][i]
    items = [
        tuple(q_s[q, pl.ds(s, len(members), stride=SUBLANES), :] for q in range(2))
        for s in range(SUBLANES)
    ]
    r_s[0], r_s[1] = join_tree(items, inner, inner_own)
    items = [tuple(r_s[q, y * pairs : (y + 1) * pairs, :] for q in range(2)) for y in range(chunks)]
    join_tree(items, outer, outer_own)


def y_eliminate(base, response, flux, to_y, yw, yi, yp, inner, outer, after):
    y_lines = yw.shape[1]
    pairs = outer.shape[2]
    chunks = y_lines // pairs
    return pl.pallas_call(
        y_eliminate_kernel,
        in_specs=[IN_VMEM] * 9 + [ANYWHERE],
        out_shape=[
            shape_of(*yw.shape),
            shape_of(SUBLANES - 1, y_lines, LANES),
            shape_of(chunks - 1, pairs, LANES),
        ],
        scratch_shapes=[
            pltpu.VMEM((2, y_lines * SUBLANES, LANES), F32),
            pltpu.VMEM((2, y_lines, LANES), F32),
        ],
        compiler_params=params(),
        cost_estimate=pl.CostEstimate(flops=8 * base.size, bytes_accessed=16 * base.size, transcendentals=0),
    )(base, response, flux, to_y, yw, yi, yp, inner, outer, after)


def z_solve(zw, zi, field, at, keep):
    sheets = zi.shape[0]
    rhs, kept = None, []
    for z in range(sheets):
        rhs = field(z) if z == 0 else field(z) + zw[(z - 1, *at)] * rhs
        kept.append(rhs * zi[(z, *at)])
    value = kept[-1]
    keep(sheets - 1, value)
    for z in range(sheets - 2, -1, -1):
        value = zw[(z, *at)] * value + kept[z]
        keep(z, value)


def finish_prepare_kernel(stages, *refs):
    ties = refs[: stages - 1]
    yw, yh, yp, inner, inner_own, outer, outer_own, zw, zi, t_ref, to_x = refs[stages - 1 : stages + 10]
    base, response, r_s, e_s, u_s = refs[stages + 10 :]
    chunks, sheets, rows, _ = base.shape
    each = LANES // rows
    pairs = sheets // each
    steps = yw.shape[0]
    lines = chunks * pairs

    ends, units = block_ends("gy", stages, ties)
    both = (
        (lambda i: outer_own[i], lambda i: inner_own[i], ends),
        (nothing, nothing, units),
    )
    for n, (upper, lower, (low, high)) in enumerate(both):
        for y, pair in enumerate(tree_ends(chunks, outer, upper, low, high)):
            for i in range(2):
                r_s[n, i, y * pairs : (y + 1) * pairs, :] = pair[i]
        for s, pair in enumerate(tree_ends(SUBLANES, inner, lower, r_s[n, 0], r_s[n, 1])):
            for i in range(2):
                e_s[n, i, pl.ds(s, lines, stride=SUBLANES), :] = pair[i]
    (low, value), (unit_low, unit) = (
        [
            jnp.stack([e_s[q, i, n * SUBLANES : (n + 1) * SUBLANES, :] for n in range(lines)], 0)
            for i in range(2)
        ]
        for q in range(2)
    )
    for k in range(steps - 1, -1, -1):
        w, p = yw[k], yp[k]
        value = w * value + (yh[k] + p * low)
        unit = w * unit + p * unit_low
        for y in range(chunks):
            for m in range(pairs):
                place = pl.ds(y * LANES + k, SUBLANES, stride=steps)
                u_s[0, m, place, :] = value[y * pairs + m]
                u_s[1, m, place, :] = unit[y * pairs + m]

    for y in range(chunks):
        part = part_of(y)
        fields = [turned(to_x[...], u_s[0, m, part, :]) for m in range(pairs)]

        def field(z):
            at = z % each * rows
            return fields[z // each][at : at + rows, :]

        def keep(z, value):
            base[y, z] = t_ref[z, :, part] + value

        z_solve(zw, zi, field, (y,), keep)
        for m in range(pairs):
            units = turned(to_x[...], u_s[1, m, part, :])
            for i in range(each):
                response[y, m * each + i] = units[i * rows : (i + 1) * rows, :]


def finish_prepare(ties, yw, yh, yp, inner, inner_own, outer, outer_own, zw, zi, t, to_x):
    sheets, rows, columns = t.shape
    chunks = columns // LANES
    pairs = sheets * rows // LANES
    lines = chunks * pairs
    field = shape_of(chunks, sheets, rows, LANES)
    return pl.pallas_call(
        functools.partial(finish_prepare_kernel, len(ties) + 1),
        out_shape=[field, field],
        scratch_shapes=[
            pltpu.VMEM((2, 2, lines, LANES), F32),
            pltpu.VMEM((2, 2, lines * SUBLANES, LANES), F32),
            pltpu.VMEM((2, pairs, columns, LANES), F32),
        ],
        compiler_params=params(),
        cost_estimate=pl.CostEstimate(flops=12 * t.size, bytes_accessed=20 * t.size, transcendentals=0),
    )(*ties, yw, yh, yp, inner, inner_own, outer, outer_own, zw, zi, t, to_x)


def finish_kernel(stages, own, got, base, response, zw, zi, to_x, out, o_s, sems):
    chunks, sheets, rows, _ = base.shape
    each = LANES // rows
    pairs = sheets // each
    flux = top_flux("gy", stages, own, got)
    wide = turned(to_x[...], flux, LANES)
    spread = [wide[:, part_of(m)] for m in range(pairs)]
    started = []
    block = rows // OUT_COPIES
    for n in range(OUT_COPIES):
        strip = slice(n * block, (n + 1) * block)
        for y in range(chunks):

            def field(z):
                at = z % each * rows + strip.start
                return response[y, z, strip, :] * spread[z // each][at : at + block, :]

            def keep(z, value):
                o_s[z, strip, part_of(y)] = base[y, z, strip, :] + value

            z_solve(zw, zi, field, (y, strip), keep)
        at = pl.ds(strip.start, block)
        copy = pltpu.make_async_copy(o_s.at[:, at, :], out.at[:, at, :], sems.at[n])
        copy.start()
        started.append(copy)
    for copy in started:
        copy.wait()


def finish(own, got, base, response, zw, zi, to_x):
    chunks, sheets, rows, _ = base.shape
    shape = (sheets, rows, chunks * LANES)
    return pl.pallas_call(
        functools.partial(finish_kernel, stages_of("gy")),
        out_shape=shape_of(*shape),
        out_specs=ANYWHERE,
        scratch_shapes=[pltpu.VMEM(shape, F32), pltpu.SemaphoreType.DMA((OUT_COPIES,))],
        compiler_params=params(),
    )(own, got, base, response, zw, zi, to_x)


def per_device(temperature, base, locations, energy):
    columns = temperature.shape[2]
    gy = lax.axis_size("gy")
    t, b, loc, heat, packed = load(temperature, base, locations[None], energy[None])
    near = swap(packed, "gy", 1)
    far = lax.ppermute(packed, "gy", [(i, ((i + 1) % gy ^ 1) - 1 if i else gy - 1) for i in range(gy)])
    c, total, xw, xi, xp, x_links, x_view, xm, ends, t_steps, swapped = x_factor(loc, heat, t, b, columns * gy, packed)
    xh, x_own, view = x_target(swapped, total, near, far, xw, xi, xp, x_links, x_view, ends)
    yw, yi, yp, inner, outer, y_view, to_y, to_x, unit_low, unit_high = y_factor(c, x_view)
    zw, zi = z_factor(c, view)
    own, got, ties = gather_line(view, "gx", 2, (y_view, zw))
    base, response, to_first, to_last, fixed = y_prepare(
        ties, xw, xh, xm, xp, x_links, x_own, t_steps, to_y, unit_low, unit_high
    )
    flux, view = y_target(own, got, to_first, to_last, fixed, y_view)
    yh, inner_own, outer_own = y_eliminate(
        base, response, flux, to_y, yw, yi, yp, inner, outer, view
    )
    own, got, ties = gather_line(view, "gy", meanwhile=(yh,), cross=True)
    base, response = finish_prepare(
        ties, yw, yh, yp, inner, inner_own, outer, outer_own, zw, zi, t, to_x
    )
    return finish(own, got, base, response, zw, zi, to_x)


def solution(mesh):
    in_specs = (P(None, "gx", "gy"), P(None, "gx", "gy"), P(), P())
    out_specs = P(None, "gx", "gy")
    return jax.shard_map(
        per_device, mesh=mesh, in_specs=in_specs, out_specs=out_specs, check_vma=False
    )
```
